32 devices in a mesh: dp: 8 (over y, x, core), mp: 4 (over z).
Axes of the slice: x: 2, y: 2, z: 4, core: 2. Of those that a mesh axis runs over, the one named last changes fastest.
Arguments:
- hr_in: bfloat16 [8, 48, 48, 1536], P('dp', 'mp'), may hold values from -6 to 6
- low_in: bfloat16 [8, 576, 1024], P('dp', 'mp'), may hold values from -6 to 6
- valid: int32 [8, 48, 48], P('dp', 'mp'), may hold values from 0 to 1, as said below
- conv_w: bfloat16 [7, 7, 1536], replicated, may hold values from -0.875 to 0.875
- hr_gain: bfloat16 [1536], replicated, may hold values from 0.099609375 to 1.8984375
- cn_up: bfloat16 [1536, 6144], P(None, 'mp'), may hold values from -0.15625 to 0.15625
- cn_down: bfloat16 [6144, 1536], P('mp'), may hold values from -0.078125 to 0.078125
- ad_gate: bfloat16 [1024, 1024], P(None, 'mp'), may hold values from -0.1875 to 0.1875
- ad_high: bfloat16 [1536, 1024], P(None, 'mp'), may hold values from -0.15625 to 0.15625
- ad_out: bfloat16 [1024, 1024], P('mp'), may hold values from -0.1875 to 0.1875
- ln1_gain: bfloat16 [1024], replicated, may hold values from 0.099609375 to 1.8984375
- w_qkv: bfloat16 [3, 1024, 1024], P(None, None, 'mp'), may hold values from -0.1875 to 0.1875
- w_proj: bfloat16 [1024, 1024], P('mp'), may hold values from -0.75 to 0.75
- ln2_gain: bfloat16 [1024], replicated, may hold values from 0.099609375 to 1.8984375
- w_up: bfloat16 [1024, 4096], P(None, 'mp'), may hold values from -0.1875 to 0.1875
- w_down: bfloat16 [4096, 1024], P('mp'), may hold values from -0.09375 to 0.09375
- cot_low: bfloat16 [8, 576, 1024], P('dp', 'mp'), may hold values from -6 to 6
- cot_hr: bfloat16 [8, 48, 48, 1536], P('dp', 'mp'), may hold values from -6 to 6
Outputs:
- low_out: float32 [8, 576, 1024], P('dp', 'mp')
- hr_out: float32 [8, 48, 48, 1536], P('dp', 'mp')
- d_low_in: float32 [8, 576, 1024], P('dp', 'mp')
- d_hr_in: float32 [8, 48, 48, 1536], P('dp', 'mp')
- g_conv: float32 [7, 7, 1536], replicated
- g_hr_gain: float32 [1536], replicated
- g_cn_up: float32 [1536, 6144], P('dp', 'mp')
- g_cn_down: float32 [6144, 1536], P('mp', 'dp')
- g_ad_gate: float32 [1024, 1024], P('dp', 'mp')
- g_ad_high: float32 [1536, 1024], P('dp', 'mp')
- g_ad_out: float32 [1024, 1024], P('mp', 'dp')
- g_ln1: float32 [1024], replicated
- g_qkv: float32 [3, 1024, 1024], P(None, 'dp', 'mp')
- g_proj: float32 [1024, 1024], P('mp', 'dp')
- g_ln2: float32 [1024], replicated
- g_up: float32 [1024, 4096], P('dp', 'mp')
- g_down: float32 [4096, 1024], P('mp', 'dp')
The draws below stay inside these ranges and needn't reach their ends.
Inputs may be any that keep to these rules, and one draw needn't show every extreme that they name: `valid`: for each item the cells of rows below s and columns below w are 1 and the others 0, with s one half, two thirds or all of 48 and w from s // 2 to s; in every aligned block of 2 items one item has s = 48.
All inputs are finite; a program needn't handle non-finite values.
Results may differ from the reference program's by a relative error of at most 0.034.
Values may be sent and summed in bfloat16 or wider, within the bound.
A program may use at most 256 MiB of HBM per device.

```python
import jax
import jax.numpy as jnp
from jax import lax

D = 1024
HEADS = 16
HEAD = 64
FF = 4096
C = 1536
CH = 6144
GRID = 48
ITEMS_DEV = 1
ITEMS = 8
LOW = 24
TOK = 576


def draw_valid(key, part):
    key = jax.random.fold_in(key, 11)
    key_size, key_full, key_width = jax.random.split(key, 3)
    block_len = max(ITEMS_DEV, 2)
    picks = jax.random.randint(key_size, (ITEMS,), 0, 3)
    heights = jnp.where(picks == 0, GRID // 2, jnp.where(picks == 1, 2 * GRID // 3, GRID))
    chosen = jax.random.randint(key_full, (ITEMS // block_len,), 0, block_len)
    is_full = jnp.arange(ITEMS) % block_len == jnp.repeat(chosen, block_len)
    heights = jnp.where(is_full, GRID, heights).astype(jnp.int32)
    spread_w = jax.random.randint(key_width, (ITEMS,), 0, 4 * GRID)
    widths = heights // 2 + spread_w % (heights - heights // 2 + 1)
    cells = jnp.arange(GRID)
    inside = (cells[None, :, None] < heights[:, None, None]) & (cells[None, None, :] < widths[:, None, None])
    return inside.astype(jnp.int32)


def levels(stream_key, extent, cuts, least, top_value):
    level, own = 1.0, jax.random.fold_in(stream_key, 6)
    for dim, blocks in cuts:
        steps = jnp.exp(jax.random.uniform(jax.random.fold_in(own, dim), (blocks,), jnp.float32, least / len(cuts), top_value / len(cuts)))
        level = level * jnp.repeat(steps, extent[dim] // blocks).reshape([-1 if axis == dim else 1 for axis in range(len(extent))])
    return level


def noise(rng, extent, width, bound, cuts=(), held_as=jnp.bfloat16):
    level = levels(rng, extent, cuts, -0.22, 0.18) if cuts else 1.0
    drawn = jax.random.normal(rng, extent, jnp.float32) * width * level
    return jnp.minimum(jnp.maximum(drawn, -bound), bound).astype(held_as)


def setup_inputs(seed: int = 0) -> dict:
    seeds = jax.random.split(jax.random.key(seed), 19)
    return {
        "hr_in": noise(seeds[0], (ITEMS, GRID, GRID, C), 1.0, 6.0, ((0, 8), (1, 4))),
        "low_in": noise(seeds[1], (ITEMS, TOK, D), 1.0, 6.0, ((0, 8), (1, 4))),
        "valid": draw_valid(jax.random.fold_in(seeds[18], 71), 0),
        "conv_w": noise(seeds[3], (7, 7, C), 49 ** -0.5, 0.875),
        "hr_gain": jnp.clip(1.0 + 0.18 * jax.random.normal(seeds[4], (C,), jnp.float32), 0.099609375, 1.8984375).astype(jnp.bfloat16),
        "cn_up": noise(seeds[5], (C, CH), C ** -0.5, 0.15625, ((1, 4),)),
        "cn_down": noise(seeds[6], (CH, C), CH ** -0.5, 0.078125, ((0, 4),)),
        "ad_gate": noise(seeds[7], (D, D), D ** -0.5, 0.1875, ((1, 4),)),
        "ad_high": noise(seeds[8], (C, D), C ** -0.5, 0.15625, ((1, 4),)),
        "ad_out": noise(seeds[9], (D, D), D ** -0.5, 0.1875, ((0, 4),)),
        "ln1_gain": jnp.clip(1.0 + 0.18 * jax.random.normal(seeds[10], (D,), jnp.float32), 0.099609375, 1.8984375).astype(jnp.bfloat16),
        "w_qkv": noise(seeds[11], (3, D, D), D ** -0.5, 0.1875, ((2, 4),)),
        "w_proj": noise(seeds[12], (D, D), (D // 16) ** -0.5, 0.75, ((0, 4),)),
        "ln2_gain": jnp.clip(1.0 + 0.18 * jax.random.normal(seeds[13], (D,), jnp.float32), 0.099609375, 1.8984375).astype(jnp.bfloat16),
        "w_up": noise(seeds[14], (D, FF), D ** -0.5, 0.1875, ((1, 4),)),
        "w_down": noise(seeds[15], (FF, D), FF ** -0.5, 0.09375, ((0, 4),)),
        "cot_low": noise(seeds[16], (ITEMS, TOK, D), 1.0, 6.0, ((0, 8), (1, 4))),
        "cot_hr": noise(seeds[17], (ITEMS, GRID, GRID, C), 1.0, 6.0, ((0, 8), (1, 4))),
    }


@jax.custom_vjp
def low(v):
    return lax.optimization_barrier(v.astype(jnp.bfloat16)).astype(jnp.float32)

@jax.custom_vjp
def low_back(v):
    return v

def low_keep(v):
    return (low(v), None)

def low_pass(kept, grad):
    return (grad,)

def back_keep(v):
    return (v, None)

def back_low(kept, grad):
    return (low(grad),)
low.defvjp(low_keep, low_pass)
low_back.defvjp(back_keep, back_low)

def layer_norm(values, gain):
    centre = lax.optimization_barrier(jnp.mean(values, -1, keepdims=True))
    centred = values - centre
    variance = lax.optimization_barrier(jnp.mean(centred * centred, -1, keepdims=True))
    return centred * lax.rsqrt(variance + 1e-06) * gain

def matmul(left, right):
    return jnp.dot(left, right, precision=lax.Precision.HIGHEST, preferred_element_type=jnp.float32)

def one_item(weights, hr_item, low_item, mask_item):
    conv_kernel, hr_gain, cn_up, cn_down, ad_gate, ad_high, ad_out, ln1_gain, w_qkv, w_proj, ln2_gain, w_up, w_down = weights
    cell_mask = mask_item[..., None]
    masked = hr_item * cell_mask
    framed = jnp.pad(masked, ((3, 3), (3, 3), (0, 0)))
    conv_out = jnp.zeros((GRID, GRID, C), jnp.float32)
    for row_off in range(7):
        for col_off in range(7):
            conv_out = conv_out + framed[row_off:row_off + GRID, col_off:col_off + GRID] * conv_kernel[row_off, col_off]
    conv_out = conv_out * cell_mask
    normed = low(layer_norm(conv_out, hr_gain)).reshape(GRID * GRID, C)
    hidden_pre = low_back(matmul(normed, cn_up))
    hidden_act = low(jax.nn.gelu(hidden_pre))
    branch = low_back(matmul(hidden_act, cn_down)).reshape(GRID, GRID, C)
    hr_out = (masked + branch) * cell_mask
    block_sum = hr_out.reshape(LOW, 2, LOW, 2, C).sum(axis=(1, 3))
    counts = mask_item.reshape(LOW, 2, LOW, 2).sum(axis=(1, 3))
    pooled = low((block_sum / jnp.maximum(counts, 1.0)[..., None]).reshape(TOK, C))
    gate_pre = low_back(matmul(low_item, ad_gate))
    high_pre = low_back(matmul(pooled, ad_high))
    merging = low(high_pre * jax.nn.sigmoid(gate_pre))
    merged_rows = low_item + low_back(matmul(merging, ad_out))
    first_norm = low(layer_norm(merged_rows, ln1_gain))
    stacked = jnp.einsum('td,kdh->kth', first_norm, w_qkv, precision=lax.Precision.HIGHEST)
    stacked = low(low_back(stacked)).reshape(3, TOK, HEADS, HEAD)
    scores = jnp.einsum('qne,kne->nqk', stacked[0], stacked[1], precision=lax.Precision.HIGHEST)
    scores = low_back(scores * HEAD ** (-0.5))
    attn_probs = low(jax.nn.softmax(scores, axis=-1))
    attended = jnp.einsum('nqk,kne->qne', attn_probs, stacked[2], precision=lax.Precision.HIGHEST)
    attended = low(low_back(attended)).reshape(TOK, D)
    residual = merged_rows + low_back(matmul(attended, w_proj))
    second_norm = low(layer_norm(residual, ln2_gain))
    up_act = low(jax.nn.gelu(low_back(matmul(second_norm, w_up))))
    return (residual + low_back(matmul(up_act, w_down)), hr_out)

def reference(hr_in, low_in, valid, conv_w, hr_gain, cn_up, cn_down, ad_gate, ad_high, ad_out, ln1_gain, w_qkv, w_proj, ln2_gain, w_up, w_down, cot_low, cot_hr):
    weights = tuple((w.astype(jnp.float32) for w in (conv_w, hr_gain, cn_up, cn_down, ad_gate, ad_high, ad_out, ln1_gain, w_qkv, w_proj, ln2_gain, w_up, w_down)))
    mask_all = valid.astype(jnp.float32)

    def forward(weight_set, hr_all, low_all):

        def per_item(pieces):
            return one_item(weight_set, pieces[0], pieces[1], pieces[2])
        return lax.map(jax.checkpoint(per_item), (hr_all, low_all, mask_all))
    outputs, pull = jax.vjp(forward, weights, hr_in.astype(jnp.float32), low_in.astype(jnp.float32))
    grads, d_hr, d_low = pull((cot_low.astype(jnp.float32), cot_hr.astype(jnp.float32)))
    return (outputs[0], outputs[1], d_low, d_hr, grads[0], grads[1], grads[2], grads[3], grads[4], grads[5], grads[6], grads[7], grads[8], grads[9], grads[10], grads[11], grads[12])
```

```python
import jax
import jax.numpy as jnp
from jax import lax
from jax.experimental import pallas as pl
from jax.experimental.pallas import tpu as pltpu
from jax.sharding import PartitionSpec as P

HEAD = 64
LANES = 128
EDGE = 8
CHUNKS = 6
TILE = 512
MIB = 1024 * 1024
MESH = pl.DeviceIdType.MESH
BF = jnp.bfloat16
F32 = jnp.float32

def gelu_parts(x):
    c = 0.7978845608028654
    x2 = x * x
    t = jnp.tanh(c * x * (1.0 + 0.044715 * x2))
    half = 0.5 * (1.0 + t)
    slope = half + 0.5 * x * (1.0 - t * t) * (c * (1.0 + 3 * 0.044715 * x2))
    return x * half, slope


def gelu(x):
    c = 0.7978845608028654
    t = jnp.tanh(c * x * (1.0 + 0.044715 * (x * x)))
    return 0.5 * x * (1.0 + t)


def chain_exchange(n, chunks, lag, own_hbm, gathered, partial, travel, compute, result_hbm,
                   sems, prepare, arrived):
    ag_send, ag_recv, rs_send, rs_recv, local_sem = sems
    d = lax.axis_index("mp")
    has_left, has_right = d > 0, d < n - 1

    barrier = pltpu.get_barrier_semaphore()

    @pl.when(has_left)
    def _():
        pl.semaphore_signal(barrier, inc=1, device_id={"mp": d - 1}, device_id_type=MESH)

    @pl.when(has_right)
    def _():
        pl.semaphore_signal(barrier, inc=1, device_id={"mp": d + 1}, device_id_type=MESH)

    load = pltpu.make_async_copy(own_hbm, gathered.at[d], local_sem)
    load.start()

    pl.semaphore_wait(barrier, has_left.astype(jnp.int32) + has_right.astype(jnp.int32))
    load.wait()

    def ag(way, s, j):
        return pltpu.make_async_remote_copy(
            src_ref=gathered.at[s, j], dst_ref=gathered.at[s, j],
            send_sem=ag_send.at[way, s, j], recv_sem=ag_recv.at[s, j],
            device_id={"mp": d + 1 - 2 * way}, device_id_type=MESH)

    def rs(way, s, j):
        there = d + 1 - 2 * way
        slot = jnp.where((s == there) & (way == 0), n, s)
        return pltpu.make_async_remote_copy(
            src_ref=travel.at[s, j], dst_ref=travel.at[slot, j],
            send_sem=rs_send.at[s, j], recv_sem=rs_recv.at[slot, j],
            device_id={"mp": there}, device_id_type=MESH)

    def rs_wait(slot, j):
        pltpu.make_async_copy(travel.at[slot, j], travel.at[slot, j], rs_recv.at[slot, j]).wait()

    def first(j, _):
        @pl.when(has_right)
        def _():
            ag(0, d, j).start()

        @pl.when(has_left)
        def _():
            ag(1, d, j).start()
        return 0
    lax.fori_loop(0, chunks, first, 0)

    def step(g, _):
        k, j = g // chunks, lax.rem(g, chunks)

        @pl.when(g < n * chunks)
        def _():
            def side(way, _):
                s = d - k + 2 * k * way
                ok = (s >= 0) & (s < n) & ((k > 0) | (way == 0))

                @pl.when(ok)
                def _():
                    prepare(s, j)

                    @pl.when(k > 0)
                    def _():
                        pltpu.make_async_copy(gathered.at[s, j], gathered.at[s, j], ag_recv.at[s, j]).wait()

                        @pl.when((way == 0) & has_right)
                        def _():
                            ag(0, s, j).start()

                        @pl.when((way == 1) & has_left)
                        def _():
                            ag(1, s, j).start()
                    arrived(s, j)
                    compute(s, j)
                return 0
            lax.fori_loop(0, 2, side, 0)

        q = g - (n - 1 - d) * lag
        ql = jnp.clip(q, 0, n * chunks - 1)
        s, jj = n - 1 - ql // chunks, lax.rem(ql, chunks)

        @pl.when((q >= 0) & (q < n * chunks) & (s <= d) & (has_right | (s < d)))
        def _():
            @pl.when(has_right)
            def _():
                rs_wait(s, jj)

                @pl.when(s < d)
                def _():
                    travel[s, jj] = (partial[s, jj].astype(F32) + travel[s, jj].astype(F32)).astype(BF)

                @pl.when(s == d)
                def _():
                    partial[s, jj] = (partial[s, jj].astype(F32) + travel[s, jj].astype(F32)).astype(partial.dtype)

            @pl.when(d == n - 1)
            def _():
                travel[s, jj] = partial[s, jj].astype(BF)

            @pl.when(s < d)
            def _():
                rs(1, s, jj).start()

        q2 = g - d * lag
        qr = jnp.clip(q2, 0, n * chunks - 1)
        s2, j2 = qr // chunks, lax.rem(qr, chunks)

        @pl.when((q2 >= 0) & (q2 < n * chunks) & (s2 >= d) & (has_left | (s2 > d)))
        def _():
            @pl.when(has_left)
            def _():
                slot = jnp.where(s2 == d, n, s2)
                rs_wait(slot, j2)

                @pl.when(s2 > d)
                def _():
                    travel[s2, j2] = (partial[s2, j2].astype(F32) + travel[s2, j2].astype(F32)).astype(BF)

                @pl.when(s2 == d)
                def _():
                    partial[s2, j2] = (partial[s2, j2].astype(F32) + travel[n, j2].astype(F32)).astype(partial.dtype)

            @pl.when(d == 0)
            def _():
                travel[s2, j2] = partial[s2, j2].astype(BF)

            @pl.when(s2 > d)
            def _():
                rs(0, s2, j2).start()
        return 0

    lax.fori_loop(0, n * chunks + (n - 1) * lag, step, 0)

    store = pltpu.make_async_copy(partial.at[d], result_hbm, local_sem)
    store.start()

    def drain(i, _):
        s, j = i // chunks, lax.rem(i, chunks)

        @pl.when(has_right & (s <= d))
        def _():
            ag(0, s, j).wait_send()

        @pl.when(has_left & (s >= d))
        def _():
            ag(1, s, j).wait_send()

        @pl.when(s < d)
        def _():
            rs(1, s, j).wait_send()

        @pl.when(s > d)
        def _():
            rs(0, s, j).wait_send()
        return 0
    lax.fori_loop(0, n * chunks, drain, 0)
    store.wait()


def chain_sems(n, chunks):
    dma = pltpu.SemaphoreType.DMA
    return [dma((2, n, chunks)), dma((n, chunks)), dma((n, chunks)), dma((n + 1, chunks)), dma]


def chunk_buffers(n, rows, c, kept):
    return [
        pltpu.VMEM((n, CHUNKS, rows, c), BF),
        pltpu.VMEM((n, CHUNKS, rows, c), kept),
        pltpu.VMEM((n + 1, CHUNKS, rows, c), BF),
    ]


def columns(i):
    return pl.ds(pl.multiple_of(i * TILE, TILE), TILE)


def drain_copies(n, copy):
    def one(i, _):
        copy(i // CHUNKS, lax.rem(i, CHUNKS)).wait()
        return 0

    lax.fori_loop(0, n * CHUNKS, one, 0)


def big_forward(x, w_up, w_down, n):
    t, c = x.shape
    h = w_up.shape[1]
    rows = t // CHUNKS

    def kernel(
        x_ref, wu, wd, out, x_all, act_all, slope_all,
        gathered, partial, travel, act, slope, copied, stored, *sems
    ):
        def x_copy(s, j):
            return pltpu.make_async_copy(gathered.at[s, j], x_all.at[s, j], copied.at[s, j])

        def prepare(s, j):
            pass

        def arrived(s, j):
            x_copy(s, j).start()

        def compute(s, j):
            block = gathered.at[s, j]

            def up(i, _):
                pre = jnp.dot(block[...], wu[:, columns(i)], preferred_element_type=F32)
                value, rate = gelu_parts(pre)
                act[:, columns(i)] = value.astype(BF)
                slope[:, columns(i)] = rate.astype(BF)
                return 0

            lax.fori_loop(0, h // TILE, up, 0)
            keep_act = pltpu.make_async_copy(act, act_all.at[s, j], stored.at[0])
            keep_slope = pltpu.make_async_copy(slope, slope_all.at[s, j], stored.at[1])
            keep_act.start()
            keep_slope.start()

            def down(i, _):
                partial[s, j, :, columns(i)] = jnp.dot(
                    act[...], wd[:, columns(i)], preferred_element_type=F32
                )
                return 0

            lax.fori_loop(0, c // TILE, down, 0)
            keep_act.wait()
            keep_slope.wait()

        chain_exchange(
            n, CHUNKS, 1, x_ref, gathered, partial, travel, compute, out, sems, prepare, arrived
        )
        drain_copies(n, x_copy)

    whole = pl.BlockSpec(memory_space=pl.ANY)
    local = pl.BlockSpec(memory_space=pltpu.VMEM)
    out, x_all, act_all, slope_all = pl.pallas_call(
        kernel,
        out_shape=(
            jax.ShapeDtypeStruct((CHUNKS, rows, c), F32),
            jax.ShapeDtypeStruct((n, CHUNKS, rows, c), BF),
            jax.ShapeDtypeStruct((n, CHUNKS, rows, h), BF),
            jax.ShapeDtypeStruct((n, CHUNKS, rows, h), BF),
        ),
        in_specs=[whole, local, local],
        out_specs=(whole,) * 4,
        scratch_shapes=chunk_buffers(n, rows, c, F32)
        + [pltpu.VMEM((rows, h), BF)] * 2
        + [pltpu.SemaphoreType.DMA((n, CHUNKS)), pltpu.SemaphoreType.DMA((2,))]
        + chain_sems(n, CHUNKS),
        compiler_params=pltpu.CompilerParams(
            collective_id=0, has_side_effects=True, vmem_limit_bytes=60 * MIB
        ),
        cost_estimate=pl.CostEstimate(
            flops=4 * n * t * c * h, bytes_accessed=8 * n * t * c, transcendentals=n * t * h
        ),
    )(x.reshape(CHUNKS, rows, c), w_up, w_down)
    return (
        out.reshape(t, c),
        x_all.reshape(n * t, c),
        act_all.reshape(n * t, h),
        slope_all.reshape(n * t, h),
    )


def big_backward(d, slope_all, w_up, w_down, n):
    t, c = d.shape
    h = w_up.shape[1]
    rows = t // CHUNKS

    def kernel(
        d_ref, slopes, wu, wd, out, d_all, h_all,
        gathered, partial, travel, slope, grad, copied, stored, *sems
    ):
        def d_copy(s, j):
            return pltpu.make_async_copy(gathered.at[s, j], d_all.at[s, j], copied.at[s, j])

        def slope_copy(s, j):
            return pltpu.make_async_copy(slopes.at[s, j], slope, stored.at[0])

        def prepare(s, j):
            slope_copy(s, j).start()

        def arrived(s, j):
            d_copy(s, j).start()

        def compute(s, j):
            block = gathered.at[s, j]
            slope_copy(s, j).wait()

            def up(i, _):
                back = lax.dot_general(
                    block[...], wd[columns(i), :], (((1,), (1,)), ((), ())), preferred_element_type=F32
                )
                grad[:, columns(i)] = (back * slope[:, columns(i)].astype(F32)).astype(BF)
                return 0

            lax.fori_loop(0, h // TILE, up, 0)
            keep = pltpu.make_async_copy(grad, h_all.at[s, j], stored.at[1])
            keep.start()

            def down(i, _):
                partial[s, j, :, columns(i)] = lax.dot_general(
                    grad[...], wu[columns(i), :], (((1,), (1,)), ((), ())), preferred_element_type=F32
                )
                return 0

            lax.fori_loop(0, c // TILE, down, 0)
            keep.wait()

        chain_exchange(
            n, CHUNKS, 1, d_ref, gathered, partial, travel, compute, out, sems, prepare, arrived
        )
        drain_copies(n, d_copy)

    whole = pl.BlockSpec(memory_space=pl.ANY)
    local = pl.BlockSpec(memory_space=pltpu.VMEM)
    out, d_all, h_all = pl.pallas_call(
        kernel,
        out_shape=(
            jax.ShapeDtypeStruct((CHUNKS, rows, c), F32),
            jax.ShapeDtypeStruct((n, CHUNKS, rows, c), BF),
            jax.ShapeDtypeStruct((n, CHUNKS, rows, h), BF),
        ),
        in_specs=[whole, whole, local, local],
        out_specs=(whole,) * 3,
        scratch_shapes=chunk_buffers(n, rows, c, F32)
        + [pltpu.VMEM((rows, h), BF)] * 2
        + [pltpu.SemaphoreType.DMA((n, CHUNKS)), pltpu.SemaphoreType.DMA((2,))]
        + chain_sems(n, CHUNKS),
        compiler_params=pltpu.CompilerParams(
            collective_id=1, has_side_effects=True, vmem_limit_bytes=60 * MIB
        ),
        cost_estimate=pl.CostEstimate(
            flops=4 * n * t * c * h, bytes_accessed=8 * n * t * c, transcendentals=0
        ),
    )(d.reshape(CHUNKS, rows, c), slope_all.reshape(n, CHUNKS, rows, h), w_up, w_down)
    return out.reshape(t, c), d_all.reshape(n * t, c), h_all.reshape(n * t, h)


def frame(dst, src):
    rows, cols, _ = src.shape
    dst[:, :EDGE] = jnp.zeros((rows, EDGE, LANES), F32)
    dst[:, EDGE + cols:] = jnp.zeros((rows, EDGE, LANES), F32)
    dst[:, EDGE:EDGE + cols] = src[...].astype(F32)


def correlate(out, framed, taps, size, flip, group):
    rows, cols, _ = out.shape
    reach = size // 2
    def some(r, _):
        acc = jnp.zeros((group, cols, LANES), F32)
        for a in range(size):
            for b in range(size):
                tap = (size - 1 - a) * size + size - 1 - b if flip else a * size + b
                acc = acc + framed[pl.ds(r * group + a, group), pl.ds(EDGE - reach + b, cols), :] * taps[tap]
        out[pl.ds(r * group, group)] = acc
        return 0
    lax.fori_loop(0, rows // group, some, 0)


def conv_forward(x, w, size, group=2):
    high, cols, c = x.shape
    rows = high - size + 1
    def kernel(x_ref, w_ref, out, framed):
        frame(framed, x_ref)
        correlate(out, framed, w_ref, size, False, group)
    return pl.pallas_call(
        kernel, grid=(c // LANES,),
        out_shape=jax.ShapeDtypeStruct((rows, cols, c), F32),
        in_specs=[pl.BlockSpec((high, cols, LANES), lambda i: (0, 0, i)), pl.BlockSpec((size * size, 1, LANES), lambda i: (0, 0, i))],
        out_specs=pl.BlockSpec((rows, cols, LANES), lambda i: (0, 0, i)),
        scratch_shapes=[pltpu.VMEM((high, cols + 2 * EDGE, LANES), F32)],
        compiler_params=pltpu.CompilerParams(vmem_limit_bytes=32 << 20),
    )(x, w)


def conv_backward(d, x, w, size, group=2, bgroup=2):
    high, cols, c = x.shape
    rows = high - size + 1
    reach = size // 2
    def kernel(d_ref, x_ref, w_ref, out, g, dframed, xframed):
        frame(dframed, d_ref)
        frame(xframed, x_ref)
        correlate(out, dframed, w_ref, size, True, group)
        for a in range(size):
            def some(r, accs):
                dv = dframed[pl.ds(reach + r * bgroup, bgroup), EDGE:EDGE + cols]
                new = []
                for b in range(size):
                    prod = dv * xframed[pl.ds(r * bgroup + a, bgroup), pl.ds(EDGE - reach + b, cols), :]
                    new.append(accs[b] + jnp.sum(prod.reshape(-1, 8, LANES), axis=0))
                return tuple(new)
            accs = lax.fori_loop(0, rows // bgroup, some, tuple(jnp.zeros((8, LANES), F32) for _ in range(size)))
            for b in range(size):
                g[a * size + b] = jnp.sum(accs[b], axis=0, keepdims=True)
    return pl.pallas_call(
        kernel, grid=(c // LANES,),
        out_shape=(jax.ShapeDtypeStruct((rows, cols, c), F32), jax.ShapeDtypeStruct((size * size, 1, c), F32)),
        in_specs=[pl.BlockSpec((high, cols, LANES), lambda i: (0, 0, i))] * 2 + [pl.BlockSpec((size * size, 1, LANES), lambda i: (0, 0, i))],
        out_specs=(pl.BlockSpec((rows, cols, LANES), lambda i: (0, 0, i)), pl.BlockSpec((size * size, 1, LANES), lambda i: (0, 0, i))),
        scratch_shapes=[pltpu.VMEM((high, cols + 2 * EDGE, LANES), F32)] * 2,
        compiler_params=pltpu.CompilerParams(vmem_limit_bytes=32 << 20),
    )(d, x, w)


def for_sending(value):
    return jax.tree.map(lambda a: a.astype(jnp.bfloat16) if a.dtype == jnp.float32 else a, value)


def extended(value, sides, width):
    for axis, dim in sides:
        devices, length = (lax.axis_size(axis), value.shape[dim])
        up = [(i, (i + 1) % devices) for i in range(devices - 1)]
        down = [(j, i) for i, j in up]
        last = lax.slice_in_dim(value, length - width, length, axis=dim)
        first = lax.slice_in_dim(value, 0, width, axis=dim)
        before = lax.ppermute(last, axis, up)
        after = lax.ppermute(first, axis, down)
        value = jnp.concatenate([before, value, after], axis=dim)
    return value


def layer_norm(values, gain):
    centre = jnp.mean(values, -1, keepdims=True)
    centred = values - centre
    variance = jnp.mean(centred * centred, -1, keepdims=True)
    return centred * lax.rsqrt(variance + 1e-06) * gain


def spread(values):
    return jax.tree.map(
        lambda part, own: part.astype(own.dtype),
        lax.all_gather(for_sending(values), "mp", axis=1, tiled=True),
        values,
    )


def collect(values):
    return jax.tree.map(
        lambda part: part.astype(jnp.float32),
        lax.psum_scatter(for_sending(values), "mp", scatter_dimension=1, tiled=True),
    )


def per_device(
    hr_in,
    low_in,
    valid,
    conv_w,
    hr_gain,
    cn_up,
    cn_down,
    ad_gate,
    ad_high,
    ad_out,
    ln1_gain,
    w_qkv,
    w_proj,
    ln2_gain,
    w_up,
    w_down,
    cot_low,
    cot_hr,
):
    item_count, row_count, col_count, chan_count = hr_in.shape
    plane_mask = valid.astype(jnp.float32)
    cell_mask = plane_mask[..., None]
    masked = hr_in * valid.astype(jnp.bfloat16)[..., None]
    bordered = extended(masked, (("mp", 1),), 3)
    size = conv_w.shape[0]
    taps = conv_w.astype(F32).reshape(size * size, 1, chan_count)
    conv_out = conv_forward(bordered[0], taps, size)[None]
    conv_out = conv_out * cell_mask
    hr_gainf = hr_gain.astype(jnp.float32)
    normed = layer_norm(conv_out, hr_gainf).astype(jnp.bfloat16)
    shards = lax.axis_size("mp")
    branch, normed_all, hidden_act, hidden_slope = big_forward(
        normed.reshape(row_count * col_count, chan_count), cn_up, cn_down, shards
    )
    branch = branch.reshape(hr_in.shape)
    hr_out = (masked.astype(jnp.float32) + branch) * cell_mask
    half_rows, half_cols = (row_count // 2, col_count // 2)
    block_sum = hr_out.reshape(item_count, half_rows, 2, half_cols, 2, chan_count).sum(axis=(2, 4))
    counts = plane_mask.reshape(item_count, half_rows, 2, half_cols, 2).sum(axis=(2, 4))
    divisor = jnp.maximum(counts, 1.0)[..., None]
    pooled = (
        (block_sum / divisor)
        .astype(jnp.bfloat16)
        .reshape(item_count, half_rows * half_cols, chan_count)
    )
    low_all, pooled_all = spread((low_in, pooled))
    gate_pre = jnp.einsum("itd,dh->ith", low_all, ad_gate, preferred_element_type=jnp.float32)
    high_pre = jnp.einsum("itc,ch->ith", pooled_all, ad_high, preferred_element_type=jnp.float32)
    gate_vals = jax.nn.sigmoid(gate_pre)
    merging = (high_pre * gate_vals).astype(jnp.bfloat16)
    merged_rows = low_in.astype(jnp.float32) + collect(
        jnp.einsum("ith,hd->itd", merging, ad_out, preferred_element_type=jnp.float32)
    )
    ln1f = ln1_gain.astype(jnp.float32)
    first_norm = layer_norm(merged_rows, ln1f).astype(jnp.bfloat16)
    first_all = spread(first_norm)
    token_count = first_all.shape[1]
    heads_local = w_qkv.shape[2] // HEAD
    stacked = jnp.einsum(
        "itd,kdh->kith", first_all, w_qkv, preferred_element_type=jnp.float32
    ).astype(jnp.bfloat16)
    stacked = stacked.reshape(3, item_count, token_count, heads_local, HEAD)
    query_heads, key_heads, value_heads = (stacked[0], stacked[1], stacked[2])
    score_scale = HEAD ** (-0.5)
    scores = (
        jnp.einsum("iqne,ikne->inqk", query_heads, key_heads, preferred_element_type=jnp.float32)
        * score_scale
    )
    row_max = jnp.max(scores, -1, keepdims=True)
    log_total = jnp.log(jnp.sum(jnp.exp(scores - row_max), -1, keepdims=True)) + row_max
    attn_probs = jnp.exp(scores - log_total).astype(jnp.bfloat16)
    attended = jnp.einsum(
        "inqk,ikne->iqne", attn_probs, value_heads, preferred_element_type=jnp.float32
    )
    attended = attended.astype(jnp.bfloat16).reshape(item_count, token_count, heads_local * HEAD)
    residual = merged_rows + collect(
        jnp.einsum("itm,md->itd", attended, w_proj, preferred_element_type=jnp.float32)
    )
    ln2f = ln2_gain.astype(jnp.float32)
    second_norm = layer_norm(residual, ln2f).astype(jnp.bfloat16)
    second_all = spread(second_norm)
    up_pre = jnp.einsum("itd,df->itf", second_all, w_up, preferred_element_type=jnp.float32)
    up_act = jax.nn.gelu(up_pre).astype(jnp.bfloat16)
    low_out = residual + collect(
        jnp.einsum("itf,fd->itd", up_act, w_down, preferred_element_type=jnp.float32)
    )
    d_out_all = spread(cot_low)
    g_down = jnp.einsum("itf,itd->fd", up_act, d_out_all, preferred_element_type=jnp.float32)
    d_upact = jnp.einsum("itd,fd->itf", d_out_all, w_down, preferred_element_type=jnp.float32)
    d_uppre = jax.vjp(jax.nn.gelu, up_pre)[1](d_upact)[0].astype(jnp.bfloat16)
    g_up = jnp.einsum("itd,itf->df", second_all, d_uppre, preferred_element_type=jnp.float32)
    d_second = collect(jnp.einsum("itf,df->itd", d_uppre, w_up, preferred_element_type=jnp.float32))
    d_res_norm, g_ln2 = jax.vjp(layer_norm, residual, ln2f)[1](d_second)
    d_res = cot_low.astype(jnp.float32) + d_res_norm
    d_attn_all = spread(d_res.astype(jnp.bfloat16))
    g_proj = jnp.einsum("itm,itd->md", attended, d_attn_all, preferred_element_type=jnp.float32)
    d_att = jnp.einsum(
        "itd,md->itm", d_attn_all, w_proj, preferred_element_type=jnp.float32
    ).astype(jnp.bfloat16)
    d_att = d_att.reshape(item_count, token_count, heads_local, HEAD)
    scores_again = (
        jnp.einsum("iqne,ikne->inqk", query_heads, key_heads, preferred_element_type=jnp.float32)
        * score_scale
    )
    probs_full = jnp.exp(scores_again - log_total)
    d_value = jnp.einsum(
        "inqk,iqne->ikne",
        probs_full.astype(jnp.bfloat16),
        d_att,
        preferred_element_type=jnp.float32,
    ).astype(jnp.bfloat16)
    d_probs = jnp.einsum("iqne,ikne->inqk", d_att, value_heads, preferred_element_type=jnp.float32)
    d_scores = (probs_full * (d_probs - jnp.sum(d_probs * probs_full, -1, keepdims=True))).astype(
        jnp.bfloat16
    )
    d_query = (
        jnp.einsum("inqk,ikne->iqne", d_scores, key_heads, preferred_element_type=jnp.float32)
        * score_scale
    ).astype(jnp.bfloat16)
    d_key = (
        jnp.einsum("inqk,iqne->ikne", d_scores, query_heads, preferred_element_type=jnp.float32)
        * score_scale
    ).astype(jnp.bfloat16)
    d_stacked = jnp.stack([d_query, d_key, d_value]).reshape(
        3, item_count, token_count, heads_local * HEAD
    )
    g_qkv = jnp.einsum("itd,kith->kdh", first_all, d_stacked, preferred_element_type=jnp.float32)
    d_first = collect(
        jnp.einsum("kith,kdh->itd", d_stacked, w_qkv, preferred_element_type=jnp.float32)
    )
    d_merged_norm, g_ln1 = jax.vjp(layer_norm, merged_rows, ln1f)[1](d_first)
    d_merged = d_res + d_merged_norm
    d_merging_all = spread(d_merged.astype(jnp.bfloat16))
    g_ad_out = jnp.einsum("ith,itd->hd", merging, d_merging_all, preferred_element_type=jnp.float32)
    d_merging = jnp.einsum("itd,hd->ith", d_merging_all, ad_out, preferred_element_type=jnp.float32)
    d_high = (d_merging * gate_vals).astype(jnp.bfloat16)
    d_gate = (d_merging * high_pre * gate_vals * (1.0 - gate_vals)).astype(jnp.bfloat16)
    g_ad_high = jnp.einsum("itc,ith->ch", pooled_all, d_high, preferred_element_type=jnp.float32)
    g_ad_gate = jnp.einsum("itd,ith->dh", low_all, d_gate, preferred_element_type=jnp.float32)
    d_pooled, d_low = collect(
        (
            jnp.einsum("ith,ch->itc", d_high, ad_high, preferred_element_type=jnp.float32),
            jnp.einsum("ith,dh->itd", d_gate, ad_gate, preferred_element_type=jnp.float32),
        )
    )
    d_low_in = d_merged + d_low
    d_block = d_pooled.reshape(item_count, half_rows, half_cols, chan_count) / divisor
    d_block = d_block.reshape(item_count, half_rows, 1, half_cols, 1, chan_count)
    d_map = cot_hr.astype(jnp.float32) + jnp.broadcast_to(
        d_block, (item_count, half_rows, 2, half_cols, 2, chan_count)
    ).reshape(hr_in.shape)
    d_branch = d_map * cell_mask
    d_normed, d_branch_all, d_hidden = big_backward(
        d_branch.astype(BF).reshape(row_count * col_count, chan_count),
        hidden_slope, cn_up, cn_down, shards,
    )
    d_normed = d_normed.reshape(hr_in.shape)
    g_cn_down = jnp.einsum("th,tc->hc", hidden_act, d_branch_all, preferred_element_type=F32).astype(BF)
    g_cn_up = jnp.einsum("tc,th->ch", normed_all, d_hidden, preferred_element_type=F32).astype(BF)
    d_conv, g_hr_gain = jax.vjp(layer_norm, conv_out, hr_gainf)[1](d_normed)
    d_conv = d_conv * cell_mask
    d_bordered = extended(d_conv.astype(BF), (("mp", 1),), 3)
    d_conv_in, g_conv = conv_backward(d_bordered[0], bordered[0], taps, size)
    g_conv = g_conv.reshape(conv_w.shape)
    d_hr_in = (d_branch + d_conv_in) * cell_mask
    small = (g_conv, g_hr_gain, g_ln1, g_ln2)
    packed = jnp.concatenate([g.reshape(-1) for g in small])
    packed = lax.psum(lax.psum(packed, "mp"), "dp")
    parts, at = [], 0
    for g in small:
        parts.append(packed[at : at + g.size].reshape(g.shape))
        at += g.size
    g_conv, g_hr_gain, g_ln1, g_ln2 = parts
    g_cn_up, g_ad_gate, g_ad_high, g_up = (
        lax.psum_scatter(g_cn_up.astype(BF), "dp", scatter_dimension=0, tiled=True).astype(F32),
        lax.psum_scatter(g_ad_gate.astype(BF), "dp", scatter_dimension=0, tiled=True).astype(F32),
        lax.psum_scatter(g_ad_high.astype(BF), "dp", scatter_dimension=0, tiled=True).astype(F32),
        lax.psum_scatter(g_up.astype(BF), "dp", scatter_dimension=0, tiled=True).astype(F32),
    )
    g_cn_down, g_ad_out, g_qkv, g_proj, g_down = (
        lax.psum_scatter(g_cn_down.astype(BF), "dp", scatter_dimension=1, tiled=True).astype(F32),
        lax.psum_scatter(g_ad_out.astype(BF), "dp", scatter_dimension=1, tiled=True).astype(F32),
        lax.psum_scatter(g_qkv.astype(BF), "dp", scatter_dimension=1, tiled=True).astype(F32),
        lax.psum_scatter(g_proj.astype(BF), "dp", scatter_dimension=1, tiled=True).astype(F32),
        lax.psum_scatter(g_down.astype(BF), "dp", scatter_dimension=1, tiled=True).astype(F32),
    )
    return (
        low_out,
        hr_out,
        d_low_in,
        d_hr_in,
        g_conv,
        g_hr_gain,
        g_cn_up,
        g_cn_down,
        g_ad_gate,
        g_ad_high,
        g_ad_out,
        g_ln1,
        g_qkv,
        g_proj,
        g_ln2,
        g_up,
        g_down,
    )


def solution(mesh):
    return jax.shard_map(
        per_device,
        mesh=mesh,
        in_specs=(
            P("dp", "mp", None, None),
            P("dp", "mp", None),
            P("dp", "mp", None),
            P(),
            P(),
            P(None, "mp"),
            P("mp", None),
            P(None, "mp"),
            P(None, "mp"),
            P("mp", None),
            P(),
            P(None, None, "mp"),
            P("mp", None),
            P(),
            P(None, "mp"),
            P("mp", None),
            P("dp", "mp", None),
            P("dp", "mp", None, None),
        ),
        out_specs=(
            P("dp", "mp", None),
            P("dp", "mp", None, None),
            P("dp", "mp", None),
            P("dp", "mp", None, None),
            P(),
            P(),
            P("dp", "mp"),
            P("mp", "dp"),
            P("dp", "mp"),
            P("dp", "mp"),
            P("mp", "dp"),
            P(),
            P(None, "dp", "mp"),
            P("mp", "dp"),
            P(),
            P("dp", "mp"),
            P("mp", "dp"),
        ),
        check_vma=False,
    )
```

```python
import jax
import jax.numpy as jnp
from jax import lax
from jax.experimental import pallas as pl
from jax.experimental.pallas import tpu as pltpu
from jax.sharding import PartitionSpec as P

HEAD = 64
LANES = 128
EDGE = 8
CHUNKS = 6
TILE = 512
MIB = 1024 * 1024
MESH = pl.DeviceIdType.MESH
BF = jnp.bfloat16
F32 = jnp.float32

def gelu_parts(x):
    c = 0.7978845608028654
    x2 = x * x
    t = jnp.tanh(c * x * (1.0 + 0.044715 * x2))
    half = 0.5 * (1.0 + t)
    slope = half + 0.5 * x * (1.0 - t * t) * (c * (1.0 + 3 * 0.044715 * x2))
    return x * half, slope


def gelu(x):
    c = 0.7978845608028654
    t = jnp.tanh(c * x * (1.0 + 0.044715 * (x * x)))
    return 0.5 * x * (1.0 + t)


def dp_bit(position):
    return lax.rem(lax.axis_index("dp") // 2**position, 2)


def dp_mate(position):
    return lax.axis_index("dp") + 2**position * (1 - 2 * dp_bit(position))


class Halving:
    def __init__(self, bits, lasts, shape, block):
        self.lasts, self.shape, self.block = lasts, shape, block
        left = list(bits)
        self.bits = [left.pop(0 if last else -1) for last in lasts]

    def split(self, count, p):
        if count == 1:
            return (1, 1)
        return (count // 2, 2) if self.lasts[p] else (2, count // 2)

    def buffers(self):
        count, rows, cols = self.shape
        got, held = [], []
        for p in range(len(self.bits)):
            count //= 2
            got.append(jax.ShapeDtypeStruct((count, rows, cols), BF))
            held.append(jax.ShapeDtypeStruct(self.split(count, p + 1) + (rows, cols), BF))
        return got + held

    def semaphores(self):
        return [pltpu.SemaphoreType.DMA((len(self.bits),))] * 2

    def bind(self, first, buffers, send, recv):
        steps = len(self.bits)
        self.now = [first] + list(buffers[steps:])
        self.got, self.send, self.recv = buffers[:steps], send, recv

    def part(self, p, mine):
        bit = dp_bit(self.bits[p])
        index = bit if mine else 1 - bit
        return self.now[p].at[:, index] if self.lasts[p] else self.now[p].at[index]

    def copy(self, p):
        return pltpu.make_async_remote_copy(
            src_ref=self.part(p, False), dst_ref=self.got[p], send_sem=self.send.at[p], recv_sem=self.recv.at[p],
            device_id={"dp": dp_mate(self.bits[p])}, device_id_type=MESH,
        )

    def start(self, p):
        self.copy(p).start()

    def finish(self, p):
        self.copy(p).wait()
        count, rows, cols = self.got[p].shape
        ways = self.split(count, p + 1)

        def add(a, b, out):
            out[...] = (a[...].astype(F32) + b[...].astype(F32)).astype(BF).reshape(out.shape)

        flat = pl.BlockSpec((1, rows, self.block), lambda k, c: (k, 0, c))
        paired = pl.BlockSpec((1, 1, rows, self.block), lambda k, c: (k // ways[1], lax.rem(k, ways[1]), 0, c))
        pltpu.emit_pipeline(add, grid=(count, cols // self.block), in_specs=[flat, flat], out_specs=[paired])(
            self.part(p, True), self.got[p], self.now[p + 1]
        )


def chain_exchange(n, chunks, lag, own_hbm, gathered, partial, travel, compute, result_hbm,
                   sems, prepare, arrived, mates=(), begin=None, turn=None):
    ag_send, ag_recv, rs_send, rs_recv, local_sem = sems
    d = lax.axis_index("mp")
    has_left, has_right = d > 0, d < n - 1

    barrier = pltpu.get_barrier_semaphore()

    @pl.when(has_left)
    def _():
        pl.semaphore_signal(barrier, inc=1, device_id={"mp": d - 1}, device_id_type=MESH)

    @pl.when(has_right)
    def _():
        pl.semaphore_signal(barrier, inc=1, device_id={"mp": d + 1}, device_id_type=MESH)

    for mate in mates:
        pl.semaphore_signal(barrier, inc=1, device_id={"dp": mate}, device_id_type=MESH)

    load = pltpu.make_async_copy(own_hbm, gathered.at[d], local_sem)
    load.start()

    pl.semaphore_wait(barrier, has_left.astype(jnp.int32) + has_right.astype(jnp.int32) + len(mates))
    if begin is not None:
        begin()
    load.wait()

    def ag(way, s, j):
        return pltpu.make_async_remote_copy(
            src_ref=gathered.at[s, j], dst_ref=gathered.at[s, j],
            send_sem=ag_send.at[way, s, j], recv_sem=ag_recv.at[s, j],
            device_id={"mp": d + 1 - 2 * way}, device_id_type=MESH)

    def rs(way, s, j):
        there = d + 1 - 2 * way
        slot = jnp.where((s == there) & (way == 0), n, s)
        return pltpu.make_async_remote_copy(
            src_ref=travel.at[s, j], dst_ref=travel.at[slot, j],
            send_sem=rs_send.at[s, j], recv_sem=rs_recv.at[slot, j],
            device_id={"mp": there}, device_id_type=MESH)

    def rs_wait(slot, j):
        pltpu.make_async_copy(travel.at[slot, j], travel.at[slot, j], rs_recv.at[slot, j]).wait()

    def first(j, _):
        @pl.when(has_right)
        def _():
            ag(0, d, j).start()

        @pl.when(has_left)
        def _():
            ag(1, d, j).start()
        return 0
    lax.fori_loop(0, chunks, first, 0)

    def step(g, _):
        k, j = g // chunks, lax.rem(g, chunks)
        if turn is not None:
            turn(g)

        @pl.when(g < n * chunks)
        def _():
            def side(way, _):
                s = d - k + 2 * k * way
                ok = (s >= 0) & (s < n) & ((k > 0) | (way == 0))

                @pl.when(ok)
                def _():
                    prepare(s, j)

                    @pl.when(k > 0)
                    def _():
                        pltpu.make_async_copy(gathered.at[s, j], gathered.at[s, j], ag_recv.at[s, j]).wait()

                        @pl.when((way == 0) & has_right)
                        def _():
                            ag(0, s, j).start()

                        @pl.when((way == 1) & has_left)
                        def _():
                            ag(1, s, j).start()
                    arrived(s, j)
                    compute(s, j)
                return 0
            lax.fori_loop(0, 2, side, 0)

        q = g - (n - 1 - d) * lag
        ql = jnp.clip(q, 0, n * chunks - 1)
        s, jj = n - 1 - ql // chunks, lax.rem(ql, chunks)

        @pl.when((q >= 0) & (q < n * chunks) & (s <= d) & (has_right | (s < d)))
        def _():
            @pl.when(has_right)
            def _():
                rs_wait(s, jj)

                @pl.when(s < d)
                def _():
                    travel[s, jj] = (partial[s, jj].astype(F32) + travel[s, jj].astype(F32)).astype(BF)

                @pl.when(s == d)
                def _():
                    partial[s, jj] = (partial[s, jj].astype(F32) + travel[s, jj].astype(F32)).astype(partial.dtype)

            @pl.when(d == n - 1)
            def _():
                travel[s, jj] = partial[s, jj].astype(BF)

            @pl.when(s < d)
            def _():
                rs(1, s, jj).start()

        q2 = g - d * lag
        qr = jnp.clip(q2, 0, n * chunks - 1)
        s2, j2 = qr // chunks, lax.rem(qr, chunks)

        @pl.when((q2 >= 0) & (q2 < n * chunks) & (s2 >= d) & (has_left | (s2 > d)))
        def _():
            @pl.when(has_left)
            def _():
                slot = jnp.where(s2 == d, n, s2)
                rs_wait(slot, j2)

                @pl.when(s2 > d)
                def _():
                    travel[s2, j2] = (partial[s2, j2].astype(F32) + travel[s2, j2].astype(F32)).astype(BF)

                @pl.when(s2 == d)
                def _():
                    partial[s2, j2] = (partial[s2, j2].astype(F32) + travel[n, j2].astype(F32)).astype(partial.dtype)

            @pl.when(d == 0)
            def _():
                travel[s2, j2] = partial[s2, j2].astype(BF)

            @pl.when(s2 > d)
            def _():
                rs(0, s2, j2).start()
        return 0

    lax.fori_loop(0, n * chunks + (n - 1) * lag, step, 0)

    store = pltpu.make_async_copy(partial.at[d], result_hbm, local_sem)
    store.start()

    def drain(i, _):
        s, j = i // chunks, lax.rem(i, chunks)

        @pl.when(has_right & (s <= d))
        def _():
            ag(0, s, j).wait_send()

        @pl.when(has_left & (s >= d))
        def _():
            ag(1, s, j).wait_send()

        @pl.when(s < d)
        def _():
            rs(1, s, j).wait_send()

        @pl.when(s > d)
        def _():
            rs(0, s, j).wait_send()
        return 0
    lax.fori_loop(0, n * chunks, drain, 0)
    store.wait()


def chain_sems(n, chunks):
    dma = pltpu.SemaphoreType.DMA
    return [dma((2, n, chunks)), dma((n, chunks)), dma((n, chunks)), dma((n + 1, chunks)), dma]


def chunk_buffers(n, rows, c, kept):
    return [
        pltpu.VMEM((n, CHUNKS, rows, c), BF),
        pltpu.VMEM((n, CHUNKS, rows, c), kept),
        pltpu.VMEM((n + 1, CHUNKS, rows, c), BF),
    ]


def columns(i):
    return pl.ds(pl.multiple_of(i * TILE, TILE), TILE)


def drain_copies(n, copy):
    def one(i, _):
        copy(i // CHUNKS, lax.rem(i, CHUNKS)).wait()
        return 0

    lax.fori_loop(0, n * CHUNKS, one, 0)


def big_forward(x, w_up, w_down, n):
    t, c = x.shape
    h = w_up.shape[1]
    rows = t // CHUNKS

    def kernel(
        x_ref, wu, wd, out, x_all, act_all, slope_all,
        gathered, partial, travel, act, slope, copied, stored, *sems
    ):
        def x_copy(s, j):
            return pltpu.make_async_copy(gathered.at[s, j], x_all.at[s, j], copied.at[s, j])

        def prepare(s, j):
            pass

        def arrived(s, j):
            x_copy(s, j).start()

        def compute(s, j):
            block = gathered.at[s, j]

            def up(i, _):
                pre = jnp.dot(block[...], wu[:, columns(i)], preferred_element_type=F32)
                value, rate = gelu_parts(pre)
                act[:, columns(i)] = value.astype(BF)
                slope[:, columns(i)] = rate.astype(BF)
                return 0

            lax.fori_loop(0, h // TILE, up, 0)
            keep_act = pltpu.make_async_copy(act, act_all.at[s, j], stored.at[0])
            keep_slope = pltpu.make_async_copy(slope, slope_all.at[s, j], stored.at[1])
            keep_act.start()
            keep_slope.start()

            def down(i, _):
                partial[s, j, :, columns(i)] = jnp.dot(
                    act[...], wd[:, columns(i)], preferred_element_type=F32
                )
                return 0

            lax.fori_loop(0, c // TILE, down, 0)
            keep_act.wait()
            keep_slope.wait()

        chain_exchange(
            n, CHUNKS, 1, x_ref, gathered, partial, travel, compute, out, sems, prepare, arrived
        )
        drain_copies(n, x_copy)

    whole = pl.BlockSpec(memory_space=pl.ANY)
    local = pl.BlockSpec(memory_space=pltpu.VMEM)
    out, x_all, act_all, slope_all = pl.pallas_call(
        kernel,
        out_shape=(
            jax.ShapeDtypeStruct((CHUNKS, rows, c), F32),
            jax.ShapeDtypeStruct((n, CHUNKS, rows, c), BF),
            jax.ShapeDtypeStruct((n, CHUNKS, rows, h), BF),
            jax.ShapeDtypeStruct((n, CHUNKS, rows, h), BF),
        ),
        in_specs=[whole, local, local],
        out_specs=(whole,) * 4,
        scratch_shapes=chunk_buffers(n, rows, c, F32)
        + [pltpu.VMEM((rows, h), BF)] * 2
        + [pltpu.SemaphoreType.DMA((n, CHUNKS)), pltpu.SemaphoreType.DMA((2,))]
        + chain_sems(n, CHUNKS),
        compiler_params=pltpu.CompilerParams(
            collective_id=0, has_side_effects=True, vmem_limit_bytes=60 * MIB
        ),
        cost_estimate=pl.CostEstimate(
            flops=4 * n * t * c * h, bytes_accessed=8 * n * t * c, transcendentals=n * t * h
        ),
    )(x.reshape(CHUNKS, rows, c), w_up, w_down)
    return (
        out.reshape(t, c),
        x_all.reshape(n * t, c),
        act_all.reshape(n * t, h),
        slope_all.reshape(n * t, h),
    )


def big_backward(d, slope_all, w_up, w_down, grads, n, devices):
    t, c = d.shape
    h = w_up.shape[1]
    rows = t // CHUNKS
    pairs, g_rows, g_cols = grads.shape
    bits = range(1, devices.bit_length() - 1)
    split = g_cols // 2
    steps = len(bits)
    plans = [Halving(bits, [last] * steps, (pairs, g_rows, split), min(split, 1024)) for last in (True, False)]

    def kernel(d_ref, slopes, wu, wd, g_first, g_second, out, d_all, h_all, *rest):
        extra, rest = rest[: 4 * steps], rest[4 * steps :]
        gathered, partial, travel, slope, grad, copied, stored, send0, recv0, send1, recv1 = rest[:11]
        sems = rest[11:]
        plans[0].bind(g_first.at[:, :, :, pl.ds(0, split)], extra[: 2 * steps], send0, recv0)
        plans[1].bind(g_second.at[:, :, :, pl.ds(split, split)], extra[2 * steps :], send1, recv1)

        def begin():
            for plan in plans:
                plan.start(0)

        def pass_on(p):
            for plan in plans:
                plan.finish(p)
            if p + 1 < steps:
                for plan in plans:
                    plan.start(p + 1)

        total = n * CHUNKS + n - 1
        due = [total * (2 ** steps - 2 ** (steps - 1 - p)) * 8 // (10 * (2 ** steps - 1)) for p in range(steps)]

        def turn(g):
            for p in range(steps - 1):
                pl.when(g == due[p])(lambda p=p: pass_on(p))

        def d_copy(s, j):
            return pltpu.make_async_copy(gathered.at[s, j], d_all.at[s, j], copied.at[s, j])

        def slope_copy(s, j):
            return pltpu.make_async_copy(slopes.at[s, j], slope, stored.at[0])

        def prepare(s, j):
            slope_copy(s, j).start()

        def arrived(s, j):
            d_copy(s, j).start()

        def compute(s, j):
            block = gathered.at[s, j]
            slope_copy(s, j).wait()

            def up(i, _):
                back = lax.dot_general(
                    block[...], wd[columns(i), :], (((1,), (1,)), ((), ())), preferred_element_type=F32
                )
                grad[:, columns(i)] = (back * slope[:, columns(i)].astype(F32)).astype(BF)
                return 0

            lax.fori_loop(0, h // TILE, up, 0)
            keep = pltpu.make_async_copy(grad, h_all.at[s, j], stored.at[1])
            keep.start()

            def down(i, _):
                partial[s, j, :, columns(i)] = lax.dot_general(
                    grad[...], wu[columns(i), :], (((1,), (1,)), ((), ())), preferred_element_type=F32
                )
                return 0

            lax.fori_loop(0, c // TILE, down, 0)
            keep.wait()

        chain_exchange(
            n, CHUNKS, 1, d_ref, gathered, partial, travel, compute, out, sems, prepare, arrived,
            [dp_mate(b) for b in bits], begin, turn
        )
        pass_on(steps - 1)
        drain_copies(n, d_copy)

    whole = pl.BlockSpec(memory_space=pl.ANY)
    local = pl.BlockSpec(memory_space=pltpu.VMEM)
    out, d_all, h_all, *extra = pl.pallas_call(
        kernel,
        out_shape=(
            jax.ShapeDtypeStruct((CHUNKS, rows, c), F32),
            jax.ShapeDtypeStruct((n, CHUNKS, rows, c), BF),
            jax.ShapeDtypeStruct((n, CHUNKS, rows, h), BF),
            *plans[0].buffers(),
            *plans[1].buffers(),
        ),
        in_specs=[whole, whole, local, local, whole, whole],
        out_specs=(whole,) * (3 + 4 * steps),
        scratch_shapes=chunk_buffers(n, rows, c, F32)
        + [pltpu.VMEM((rows, h), BF)] * 2
        + [pltpu.SemaphoreType.DMA((n, CHUNKS)), pltpu.SemaphoreType.DMA((2,))]
        + plans[0].semaphores() + plans[1].semaphores()
        + chain_sems(n, CHUNKS),
        compiler_params=pltpu.CompilerParams(
            collective_id=1, has_side_effects=True, vmem_limit_bytes=60 * MIB
        ),
        cost_estimate=pl.CostEstimate(
            flops=4 * n * t * c * h, bytes_accessed=8 * n * t * c, transcendentals=0
        ),
    )(
        d.reshape(CHUNKS, rows, c), slope_all.reshape(n, CHUNKS, rows, h), w_up, w_down,
        grads.reshape(pairs // 2, 2, g_rows, g_cols), grads.reshape(2, pairs // 2, g_rows, g_cols),
    )
    sums = [extra[2 * steps - 1].reshape(g_rows, split), extra[4 * steps - 1].reshape(g_rows, split)]
    return out.reshape(t, c), d_all.reshape(n * t, c), h_all.reshape(n * t, h), sums


def frame(dst, src):
    rows, cols, _ = src.shape
    dst[:, :EDGE] = jnp.zeros((rows, EDGE, LANES), F32)
    dst[:, EDGE + cols:] = jnp.zeros((rows, EDGE, LANES), F32)
    dst[:, EDGE:EDGE + cols] = src[...].astype(F32)


def correlate(out, framed, taps, size, flip, group):
    rows, cols, _ = out.shape
    reach = size // 2
    def some(r, _):
        acc = jnp.zeros((group, cols, LANES), F32)
        for a in range(size):
            for b in range(size):
                tap = (size - 1 - a) * size + size - 1 - b if flip else a * size + b
                acc = acc + framed[pl.ds(r * group + a, group), pl.ds(EDGE - reach + b, cols), :] * taps[tap]
        out[pl.ds(r * group, group)] = acc
        return 0
    lax.fori_loop(0, rows // group, some, 0)


def conv_forward(x, w, size, group=2):
    high, cols, c = x.shape
    rows = high - size + 1
    def kernel(x_ref, w_ref, out, framed):
        frame(framed, x_ref)
        correlate(out, framed, w_ref, size, False, group)
    return pl.pallas_call(
        kernel, grid=(c // LANES,),
        out_shape=jax.ShapeDtypeStruct((rows, cols, c), F32),
        in_specs=[pl.BlockSpec((high, cols, LANES), lambda i: (0, 0, i)), pl.BlockSpec((size * size, 1, LANES), lambda i: (0, 0, i))],
        out_specs=pl.BlockSpec((rows, cols, LANES), lambda i: (0, 0, i)),
        scratch_shapes=[pltpu.VMEM((high, cols + 2 * EDGE, LANES), F32)],
        compiler_params=pltpu.CompilerParams(vmem_limit_bytes=32 << 20),
    )(x, w)


def conv_backward(d, x, w, size, grads, devices, group=4, bgroup=4):
    high, cols, c = x.shape
    rows = high - size + 1
    reach = size // 2
    steps = devices.bit_length() - 1
    shape = grads[0].shape
    plans = [Halving(range(steps), [True] + [last] * (steps - 1), shape, shape[2]) for last in (True, False)]
    blocks = c // LANES
    due = [blocks * (p + 1) // (steps + 1) for p in range(steps)]

    def kernel(d_ref, x_ref, w_ref, g0, g1, out, g, *rest):
        extra, rest = rest[: 4 * steps], rest[4 * steps :]
        dframed, xframed, *sems = rest
        plans[0].bind(g0, extra[: 2 * steps], sems[0], sems[1])
        plans[1].bind(g1, extra[2 * steps :], sems[2], sems[3])
        i = pl.program_id(0)

        @pl.when(i == 0)
        def _():
            barrier = pltpu.get_barrier_semaphore()
            for b in range(steps):
                pl.semaphore_signal(barrier, inc=1, device_id={"dp": dp_mate(b)}, device_id_type=MESH)
            pl.semaphore_wait(barrier, steps)
            for plan in plans:
                plan.start(0)

        for p in range(steps - 1):
            @pl.when(i == due[p])
            def _():
                for plan in plans:
                    plan.finish(p)
                for plan in plans:
                    plan.start(p + 1)

        frame(dframed, d_ref)
        frame(xframed, x_ref)
        correlate(out, dframed, w_ref, size, True, group)
        for a in range(size):
            def some(r, accs):
                dv = dframed[pl.ds(reach + r * bgroup, bgroup), EDGE : EDGE + cols]
                new = []
                for b in range(size):
                    prod = dv * xframed[pl.ds(r * bgroup + a, bgroup), pl.ds(EDGE - reach + b, cols), :]
                    new.append(accs[b] + jnp.sum(prod.reshape(-1, 8, LANES), axis=0))
                return tuple(new)

            accs = lax.fori_loop(
                0, rows // bgroup, some, tuple(jnp.zeros((8, LANES), F32) for _ in range(size))
            )
            for b in range(size):
                g[a * size + b] = jnp.sum(accs[b], axis=0, keepdims=True)

        @pl.when(i == blocks - 1)
        def _():
            for plan in plans:
                plan.finish(steps - 1)

    whole = pl.BlockSpec(memory_space=pl.ANY)
    d_in, g, *extra = pl.pallas_call(
        kernel,
        grid=(blocks,),
        out_shape=(
            jax.ShapeDtypeStruct((rows, cols, c), F32),
            jax.ShapeDtypeStruct((size * size, 1, c), F32),
            *plans[0].buffers(),
            *plans[1].buffers(),
        ),
        in_specs=[pl.BlockSpec((high, cols, LANES), lambda i: (0, 0, i))] * 2
        + [pl.BlockSpec((size * size, 1, LANES), lambda i: (0, 0, i)), whole, whole],
        out_specs=(
            pl.BlockSpec((rows, cols, LANES), lambda i: (0, 0, i)),
            pl.BlockSpec((size * size, 1, LANES), lambda i: (0, 0, i)),
        )
        + (whole,) * (4 * steps),
        scratch_shapes=[pltpu.VMEM((high, cols + 2 * EDGE, LANES), F32)] * 2
        + plans[0].semaphores() + plans[1].semaphores(),
        compiler_params=pltpu.CompilerParams(
            collective_id=3, has_side_effects=True, vmem_limit_bytes=40 * MIB
        ),
    )(
        d, x, w, grads[0].reshape((shape[0] // 2, 2) + shape[1:]), grads[1].reshape((shape[0] // 2, 2) + shape[1:])
    )
    return d_in, g, [extra[2 * steps - 1].reshape(shape[1:]), extra[4 * steps - 1].reshape(shape[1:])]


GATE, OUT, HIGH_A, HIGH_B, QUERY, KEY, VALUE, PROJ = range(8)
L_LOW, L_DF, L_POOL_A, L_POOL_B, L_FIRST, L_DA, L_SECOND, L_COT = range(8)
R_DGATE, R_MERGE, R_DHIGH, R_DQ, R_DK, R_DV, R_ATT, R_DUP, R_ACT = range(9)


def nn(a, b):
    return jnp.dot(a, b, preferred_element_type=F32)


def nt(a, b):
    return lax.dot_general(a, b, (((1,), (1,)), ((), ())), preferred_element_type=F32)


def tn(a, b):
    return lax.dot_general(a, b, (((0,), (0,)), ((), ())), preferred_element_type=F32)


def normalise(x, gain):
    centred = x - jnp.mean(x, -1, keepdims=True)
    rate = lax.rsqrt(jnp.mean(centred * centred, -1, keepdims=True) + 1e-06)
    return centred * rate * gain


def normalise_back(x, gain, d):
    centred = x - jnp.mean(x, -1, keepdims=True)
    rate = lax.rsqrt(jnp.mean(centred * centred, -1, keepdims=True) + 1e-06)
    hat = centred * rate
    dg = d * gain
    back = rate * (dg - jnp.mean(dg, -1, keepdims=True) - hat * jnp.mean(dg * hat, -1, keepdims=True))
    return back, jnp.sum(d * hat, axis=0, keepdims=True)


def low_stage(low, pool_a, pool_b, cot, gain1, gain2, w1, w2, n, devices, cid):
    t, dim = low.shape
    every = n * t
    width = dim // n
    heads = width // HEAD
    pairs = devices // 2
    rows = dim // devices
    half = dim // 2
    ff = 4 * dim
    scale = HEAD ** (-0.5)

    def kernel(
        low_ref, pool_a_ref, pool_b_ref, cot_ref, gain1_ref, gain2_ref, w1_hbm, w2_hbm,
        low_out, d_low, d_pool_a, d_pool_b, g_ln1, g_ln2, grads,
        wv, lhs, lhs2, rhs, gate, high, merged, resid, d_res, slope, mixed, heads_in, att_all, d_att, d_mixed,
        d_heads, probs, d_scores, stage, w_sem, q_send, q_got, a_send, a_got, b_send, b_got, c_send, c_got, own_sem,
        l_send, l_got, r_send, r_got, stage_sem,
    ):
        d = lax.axis_index("mp")
        dp = lax.axis_index("dp")
        core = lax.rem(dp, 2)
        mate = dp + 1 - 2 * core
        barrier = pltpu.get_barrier_semaphore()
        for k in range(1, n):
            pl.semaphore_signal(barrier, inc=1, device_id={"mp": lax.rem(d + k, n)}, device_id_type=MESH)
        pl.semaphore_signal(barrier, inc=1, device_id={"dp": mate}, device_id_type=MESH)

        def w_copy(p, c):
            src = (w1_hbm if p < 4 else w2_hbm).at[:, c, :, pl.ds((p % 4) * 2 * dim, 2 * dim)]
            return pltpu.make_async_copy(src, wv.at[c, :, :, pl.ds(p * 2 * dim, 2 * dim)], w_sem.at[p, c])

        for p in range(8):
            for c in range(2):
                w_copy(p, c).start()

        def w_wait(p):
            for c in range(2):
                w_copy(p, c).wait()

        def w_cols(at, size):
            return wv[:, :, :, pl.ds(at, size)].reshape(dim, size)

        def forward(x, first, count, put):
            def one(i, _):
                put(pl.multiple_of(i * TILE, TILE), nn(x, w_cols(pl.multiple_of(first * dim + i * TILE, TILE), TILE)))
                return 0
            lax.fori_loop(0, count * dim // TILE, one, 0)

        def backward(get, first, count, dst, fresh):
            def one(i, _):
                for c in range(2):
                    part = wv[c, :, :, pl.ds(pl.multiple_of((first + i) * dim, dim), dim)].reshape(half, dim)
                    y = nt(get(pl.multiple_of(i * dim, dim)), part)
                    cols = slice(c * half, (c + 1) * half)
                    if fresh and count == 1:
                        dst[:, cols] = y
                    else:
                        dst[:, cols] += y
                return 0
            if fresh and count > 1:
                dst[...] = jnp.zeros(dst.shape, F32)
            if count == 1:
                one(0, 0)
            else:
                lax.fori_loop(0, count, one, 0)

        def r_cols(block, count=1):
            return pl.ds(block * dim, count * dim)

        def r_at(block):
            return block * dim if block <= R_DUP else block * dim + 3 * dim

        def r_copy(block):
            cols = pl.ds(r_at(block), dim if block < R_DUP else ff)
            return pltpu.make_async_remote_copy(
                src_ref=rhs.at[0, :, cols], dst_ref=rhs.at[1, :, cols], send_sem=r_send.at[block],
                recv_sem=r_got.at[block], device_id={"dp": mate}, device_id_type=MESH)

        def l_copy(i):
            return pltpu.make_async_remote_copy(
                src_ref=lhs.at[i, :, pl.ds(pl.multiple_of((1 - core) * half, half), half)], dst_ref=lhs2.at[i],
                send_sem=l_send.at[i], recv_sem=l_got.at[i], device_id={"dp": mate}, device_id_type=MESH)

        stage_count = [0]

        def grad(i, block, at, count, shared=False):
            if not shared:
                r_copy(block).wait_recv()
            own_l = pl.ds(pl.multiple_of(core * half, half), half)

            def out_copy(slot, k):
                return pltpu.make_async_copy(
                    stage.at[slot], grads.at[:, :, pl.ds(at * dim + k * TILE, TILE)], stage_sem.at[slot])

            for k in range(count * dim // TILE):
                slot = stage_count[0] % 2
                if stage_count[0] >= 2:
                    out_copy(slot, k).wait()
                stage_count[0] += 1
                cols = pl.ds(r_at(block) + k * TILE, TILE)
                y = tn(lhs[i, :, own_l], rhs[0, :, cols]) + tn(lhs2[i], rhs[1, :, cols])
                stage[slot] = y.astype(BF).reshape(pairs, rows, TILE)
                out_copy(slot, k).start()

        def to_heads(k, src, dst, send, got):
            out = []
            for step in range(1, n):
                peer = lax.rem(d + step, n)
                out.append(pltpu.make_async_remote_copy(
                    src_ref=src.at[:, pl.ds(pl.multiple_of(peer * width, width), width)],
                    dst_ref=dst.at[pl.ds(pl.multiple_of(d * t, t), t)],
                    send_sem=send.at[k, step], recv_sem=got.at[k, step], device_id={"mp": peer}, device_id_type=MESH))
            out.append(pltpu.make_async_copy(
                src.at[:, pl.ds(pl.multiple_of(d * width, width), width)], dst.at[pl.ds(pl.multiple_of(d * t, t), t)], own_sem.at[k]))
            return out

        def to_tokens(k, src, dst, send, got):
            out = []
            for step in range(1, n):
                peer = lax.rem(d + step, n)
                out.append(pltpu.make_async_remote_copy(
                    src_ref=src.at[pl.ds(pl.multiple_of(peer * t, t), t)],
                    dst_ref=dst.at[:, pl.ds(pl.multiple_of(d * width, width), width)],
                    send_sem=send.at[k, step], recv_sem=got.at[k, step], device_id={"mp": peer}, device_id_type=MESH))
            out.append(pltpu.make_async_copy(
                src.at[pl.ds(pl.multiple_of(d * t, t), t)], dst.at[:, pl.ds(pl.multiple_of(d * width, width), width)], own_sem.at[k]))
            return out

        def start(copies):
            for c in copies:
                c.start()

        def wait(copies):
            for c in copies:
                c.wait()

        lhs[L_LOW] = low_ref[...]
        lhs[L_POOL_A] = pool_a_ref[...]
        lhs[L_POOL_B] = pool_b_ref[...]
        lhs[L_COT] = cot_ref[...]
        acc = d_low
        w_wait(0)

        def put_gate(at, y):
            gate[:, pl.ds(at, TILE)] = 1.0 / (1.0 + jnp.exp(-y))
        forward(lhs[L_LOW], GATE, 1, put_gate)
        w_wait(1)

        def put_high(at, y):
            high[:, pl.ds(at, TILE)] = y
        forward(lhs[L_POOL_A], HIGH_A, 1, put_high)

        def put_merging(at, y):
            cols = pl.ds(at, TILE)
            total = high[:, cols] + y
            high[:, cols] = total
            rhs[0, :, pl.ds(R_MERGE * dim + at, TILE)] = (total * gate[:, cols]).astype(BF)
        forward(lhs[L_POOL_B], HIGH_B, 1, put_merging)
        backward(lambda at: rhs[0, :, r_cols(R_MERGE)], OUT, 1, merged, True)
        merged[...] += lhs[L_LOW].astype(F32)
        lhs[L_FIRST] = normalise(merged[...], gain1_ref[...]).astype(BF)

        w_wait(2)
        w_wait(3)
        pl.semaphore_wait(barrier, n)
        for i in (L_LOW, L_POOL_A, L_POOL_B, L_COT, L_FIRST):
            l_copy(i).start()
        r_copy(R_MERGE).start()
        out_q = []
        for k in range(3):
            def put_mixed(at, y):
                mixed[k, :, pl.ds(at, TILE)] = y.astype(BF)
            forward(lhs[L_FIRST], QUERY + k, 1, put_mixed)
            copies = to_heads(k, mixed.at[k], heads_in.at[k], q_send, q_got)
            start(copies)
            out_q += copies
        wait(out_q)

        for h in range(heads):
            lanes = slice(h * HEAD, (h + 1) * HEAD)

            def rows_of(b, _):
                some = pl.ds(pl.multiple_of(b * t, t), t)
                s = nt(heads_in[0, some, lanes], heads_in[1, :, lanes]) * scale
                e = jnp.exp(s - jnp.max(s, -1, keepdims=True))
                p = (e * (1.0 / jnp.sum(e, -1, keepdims=True))).astype(BF)
                probs[h, some] = p
                att_all[some, lanes] = nn(p, heads_in[2, :, lanes]).astype(BF)
                return 0
            lax.fori_loop(0, n, rows_of, 0)
        out_a = to_tokens(0, att_all, rhs.at[0, :, r_cols(R_ATT)], a_send, a_got)
        start(out_a)
        wait(out_a)
        r_copy(R_ATT).start()
        backward(lambda at: rhs[0, :, r_cols(R_ATT)], PROJ, 1, resid, True)
        resid[...] += merged[...]
        lhs[L_SECOND] = normalise(resid[...], gain2_ref[...]).astype(BF)
        l_copy(L_SECOND).start()

        w_wait(4)
        w_wait(5)

        def put_up(at, y):
            value, rate = gelu_parts(y)
            rhs[0, :, pl.ds(r_at(R_ACT) + at, TILE)] = value.astype(BF)
            slope[:, pl.ds(at, TILE)] = rate.astype(BF)
        forward(lhs[L_SECOND], 8, 4, put_up)
        r_copy(R_ACT).start()
        w_wait(6)
        w_wait(7)
        backward(lambda at: rhs[0, :, pl.ds(r_at(R_ACT) + at, dim)], 12, 4, acc, True)
        low_out[...] = resid[...] + acc[...]

        def put_d_up(at, y):
            rhs[0, :, pl.ds(r_at(R_DUP) + at, TILE)] = (y * slope[:, pl.ds(at, TILE)].astype(F32)).astype(BF)
        forward(lhs[L_COT], 12, 4, put_d_up)
        r_copy(R_DUP).start()
        backward(lambda at: rhs[0, :, pl.ds(r_at(R_DUP) + at, dim)], 8, 4, acc, True)
        back, g = normalise_back(resid[...], gain2_ref[...], acc[...])
        g_ln2[...] = g
        d_res[...] = lhs[L_COT].astype(F32) + back
        lhs[L_DA] = d_res[...].astype(BF)
        l_copy(L_DA).start()

        def put_d_att(at, y):
            mixed[0, :, pl.ds(at, TILE)] = y.astype(BF)
        forward(lhs[L_DA], PROJ, 1, put_d_att)
        out_b = to_heads(0, mixed.at[0], d_att, b_send, b_got)
        start(out_b)
        l_copy(L_COT).wait_recv()
        grad(L_COT, R_ACT, 12, 4)
        wait(out_b)
        for h in range(heads):
            lanes = slice(h * HEAD, (h + 1) * HEAD)

            def rows_of(b, _):
                some = pl.ds(pl.multiple_of(b * t, t), t)
                p = probs[h, some].astype(F32)
                dp_ = nt(d_att[some, lanes], heads_in[2, :, lanes])
                ds = (p * (dp_ - jnp.sum(dp_ * p, -1, keepdims=True)) * scale).astype(BF)
                d_scores[some] = ds
                d_heads[0, some, lanes] = nn(ds, heads_in[1, :, lanes]).astype(BF)
                return 0
            lax.fori_loop(0, n, rows_of, 0)
            d_heads[1, :, lanes] = tn(d_scores[...], heads_in[0, :, lanes]).astype(BF)
            d_heads[2, :, lanes] = tn(probs[h], d_att[:, lanes]).astype(BF)
        out_c = []
        for k in range(3):
            copies = to_tokens(k, d_heads.at[k], rhs.at[0, :, r_cols(R_DQ + k)], c_send, c_got)
            start(copies)
            out_c += copies
        l_copy(L_SECOND).wait_recv()
        grad(L_SECOND, R_DUP, 8, 4)
        l_copy(L_DA).wait_recv()
        grad(L_DA, R_ATT, PROJ, 1)
        wait(out_c)
        for k in range(3):
            r_copy(R_DQ + k).start()
        backward(lambda at: rhs[0, :, pl.ds(R_DQ * dim + at, dim)], QUERY, 3, acc, True)
        back, g = normalise_back(merged[...], gain1_ref[...], acc[...])
        g_ln1[...] = g
        d_res[...] += back
        lhs[L_DF] = d_res[...].astype(BF)
        l_copy(L_DF).start()

        def put_d_gate(at, y):
            cols = pl.ds(at, TILE)
            gv = gate[:, cols]
            part = y * gv
            rhs[0, :, pl.ds(R_DHIGH * dim + at, TILE)] = part.astype(BF)
            rhs[0, :, pl.ds(R_DGATE * dim + at, TILE)] = (part * high[:, cols] * (1.0 - gv)).astype(BF)
        forward(lhs[L_DF], OUT, 1, put_d_gate)
        r_copy(R_DHIGH).start()
        r_copy(R_DGATE).start()
        backward(lambda at: rhs[0, :, r_cols(R_DHIGH)], HIGH_A, 1, d_pool_a, True)
        backward(lambda at: rhs[0, :, r_cols(R_DHIGH)], HIGH_B, 1, d_pool_b, True)
        backward(lambda at: rhs[0, :, r_cols(R_DGATE)], GATE, 1, acc, True)
        d_low[...] = d_res[...] + acc[...]
        l_copy(L_FIRST).wait_recv()
        for k in range(3):
            grad(L_FIRST, R_DQ + k, QUERY + k, 1)
        l_copy(L_DF).wait_recv()
        grad(L_DF, R_MERGE, OUT, 1)
        l_copy(L_POOL_A).wait_recv()
        grad(L_POOL_A, R_DHIGH, HIGH_A, 1)
        l_copy(L_POOL_B).wait_recv()
        grad(L_POOL_B, R_DHIGH, HIGH_B, 1, shared=True)
        l_copy(L_LOW).wait_recv()
        grad(L_LOW, R_DGATE, GATE, 1)
        for slot in range(2):
            pltpu.make_async_copy(stage.at[slot], grads.at[:, :, pl.ds(0, TILE)], stage_sem.at[slot]).wait()
        for i in range(8):
            l_copy(i).wait_send()
        for b in range(9):
            r_copy(b).wait_send()

    whole = pl.BlockSpec(memory_space=pl.ANY)
    local = pl.BlockSpec(memory_space=pltpu.VMEM)
    vm, dma = pltpu.VMEM, pltpu.SemaphoreType.DMA
    tok = jax.ShapeDtypeStruct((t, dim), F32)
    one = jax.ShapeDtypeStruct((1, dim), F32)
    return pl.pallas_call(
        kernel,
        out_shape=(tok, tok, tok, tok, one, one, jax.ShapeDtypeStruct((pairs, rows, 16 * dim), BF)),
        in_specs=[local] * 6 + [whole] * 2,
        out_specs=(local,) * 6 + (whole,),
        scratch_shapes=[
            vm((2, pairs, rows, 16 * dim), BF), vm((8, t, dim), BF), vm((8, t, half), BF), vm((2, t, 15 * dim), BF),
            vm((t, dim), F32), vm((t, dim), F32), vm((t, dim), F32), vm((t, dim), F32), vm((t, dim), F32),
            vm((t, ff), BF), vm((3, t, dim), BF), vm((3, every, width), BF), vm((every, width), BF), vm((every, width), BF),
            vm((1, 8, 128), BF), vm((3, every, width), BF), vm((heads, every, every), BF), vm((every, every), BF),
            vm((2, pairs, rows, TILE), BF),
            dma((8, 2)), dma((3, n)), dma((3, n)), dma((1, n)), dma((1, n)), dma((1, n)), dma((1, n)), dma((3, n)), dma((3, n)),
            dma((3,)), dma((8,)), dma((8,)), dma((9,)), dma((9,)), dma((2,)),
        ],
        compiler_params=pltpu.CompilerParams(collective_id=cid, has_side_effects=True, vmem_limit_bytes=61 * MIB),
        cost_estimate=pl.CostEstimate(flops=14 * 10**9, bytes_accessed=70 * 10**6, transcendentals=10**7),
    )(low, pool_a, pool_b, cot, gain1, gain2, w1.reshape(pairs, 2, rows, 8 * dim), w2.reshape(pairs, 2, rows, 8 * dim))
def own_part(w, axis):
    length = w.shape[axis] // lax.axis_size("dp")
    return lax.dynamic_slice_in_dim(w, lax.axis_index("dp") * length, length, axis)


def fold(w, rows):
    return w[:rows], jnp.pad(w[rows:], ((0, 2 * rows - w.shape[0]), (0, 0)))


def gather_packed(pieces, every):
    n = every.shape[0]
    parts, at = [], 0
    for w in pieces:
        parts.append(every[:, :, at : at + w].transpose(1, 0, 2).reshape(-1, n * w))
        at += w
    return lax.all_gather(jnp.concatenate(parts, axis=1), "dp", axis=0, tiled=True)


def core_first(x, devices):
    shape = x.shape
    return x.reshape(shape[:-1] + (devices // 2, 2, -1)).swapaxes(-3, -2).reshape(shape)


def core_last(x, devices):
    shape = x.shape
    return x.reshape(shape[:-1] + (2, devices // 2, -1)).swapaxes(-3, -2).reshape(shape)


def extended(value, sides, width):
    for axis, dim in sides:
        devices, length = (lax.axis_size(axis), value.shape[dim])
        up = [(i, (i + 1) % devices) for i in range(devices - 1)]
        down = [(j, i) for i, j in up]
        last = lax.slice_in_dim(value, length - width, length, axis=dim)
        first = lax.slice_in_dim(value, 0, width, axis=dim)
        before = lax.ppermute(last, axis, up)
        after = lax.ppermute(first, axis, down)
        value = jnp.concatenate([before, value, after], axis=dim)
    return value


def layer_norm(values, gain):
    centre = jnp.mean(values, -1, keepdims=True)
    centred = values - centre
    variance = jnp.mean(centred * centred, -1, keepdims=True)
    return centred * lax.rsqrt(variance + 1e-06) * gain


def per_device(
    hr_in,
    low_in,
    valid,
    conv_w,
    hr_gain,
    cn_up,
    cn_down,
    ad_gate,
    ad_high,
    ad_out,
    ln1_gain,
    w_qkv,
    w_proj,
    ln2_gain,
    w_up,
    w_down,
    cot_low,
    cot_hr,
):
    item_count, row_count, col_count, chan_count = hr_in.shape
    devices, shards = lax.axis_size("dp"), lax.axis_size("mp")
    dims = low_in.shape[2]
    share = dims // devices
    qkv = own_part(w_qkv, 1)
    first_pieces = [
        own_part(ad_gate, 0), own_part(ad_out, 1).T, *fold(own_part(ad_high, 0), share),
        qkv[0], qkv[1], qkv[2], own_part(w_proj, 1).T,
    ]
    second_pieces = [own_part(w_up, 0), own_part(w_down, 1).T]
    first_every = lax.all_gather(jnp.concatenate(first_pieces, axis=1), "mp", axis=0)
    second_every = lax.all_gather(jnp.concatenate(second_pieces, axis=1), "mp", axis=0)
    plane_mask = valid.astype(jnp.float32)
    cell_mask = plane_mask[..., None]
    masked = hr_in * valid.astype(jnp.bfloat16)[..., None]
    bordered = extended(masked, (("mp", 1),), 3)
    size = conv_w.shape[0]
    taps = conv_w.astype(F32).reshape(size * size, 1, chan_count)
    conv_out = conv_forward(bordered[0], taps, size)[None]
    conv_out, first_every, second_every = lax.optimization_barrier((conv_out, first_every, second_every))
    first_widths = [p.shape[1] for p in first_pieces]
    second_widths = [p.shape[1] for p in second_pieces]
    packed_first = gather_packed(first_widths, first_every)
    packed_second = gather_packed(second_widths, second_every)
    conv_out = conv_out * cell_mask
    hr_gainf = hr_gain.astype(jnp.float32)
    normed = layer_norm(conv_out, hr_gainf).astype(jnp.bfloat16)
    branch, normed_all, hidden_act, hidden_slope = big_forward(
        normed.reshape(row_count * col_count, chan_count), cn_up, cn_down, shards
    )
    branch = branch.reshape(hr_in.shape)
    hr_out = (masked.astype(jnp.float32) + branch) * cell_mask
    half_rows, half_cols = (row_count // 2, col_count // 2)
    block_sum = hr_out.reshape(item_count, half_rows, 2, half_cols, 2, chan_count).sum(axis=(2, 4))
    counts = plane_mask.reshape(item_count, half_rows, 2, half_cols, 2).sum(axis=(2, 4))
    divisor = jnp.maximum(counts, 1.0)[..., None]
    pooled = (
        (block_sum / divisor)
        .astype(jnp.bfloat16)
        .reshape(item_count, half_rows * half_cols, chan_count)
    )
    tokens = half_rows * half_cols
    by_share = pooled[0].reshape(tokens, devices, -1)
    pool_a = by_share[:, :, :share].reshape(tokens, dims)
    pool_b = jnp.pad(by_share[:, :, share:], ((0, 0), (0, 0), (0, 2 * share - by_share.shape[2]))).reshape(tokens, dims)
    low_out, d_low_in, d_pool_a, d_pool_b, g_ln1, g_ln2, low_grads = low_stage(
        *(core_first(v, devices) for v in (low_in[0], pool_a, pool_b, cot_low[0])),
        *(core_first(v.astype(F32), devices)[None] for v in (ln1_gain, ln2_gain)),
        packed_first, packed_second, shards, devices, 2,
    )
    low_out = core_last(low_out, devices)[None]
    d_low_in = core_last(d_low_in, devices)[None]
    g_ln1, g_ln2 = core_last(g_ln1[0], devices), core_last(g_ln2[0], devices)
    d_pooled = jnp.concatenate(
        [
            core_last(d_pool_a, devices).reshape(tokens, devices, share),
            core_last(d_pool_b, devices).reshape(tokens, devices, share)[:, :, : by_share.shape[2] - share],
        ],
        axis=2,
    )
    d_block = d_pooled.reshape(item_count, half_rows, half_cols, chan_count) / divisor
    d_block = d_block.reshape(item_count, half_rows, 1, half_cols, 1, chan_count)
    d_map = cot_hr.astype(jnp.float32) + jnp.broadcast_to(
        d_block, (item_count, half_rows, 2, half_cols, 2, chan_count)
    ).reshape(hr_in.shape)
    d_branch = d_map * cell_mask
    d_normed, d_branch_all, d_hidden, low_sums = big_backward(
        d_branch.astype(BF).reshape(row_count * col_count, chan_count),
        hidden_slope, cn_up, cn_down, low_grads, shards, devices,
    )
    d_normed = d_normed.reshape(hr_in.shape)
    by_slice, at = [], 0
    for whole, widths in zip(low_sums, (first_widths, second_widths)):
        at = 0
        for w in widths:
            by_slice.append(whole[:, at : at + shards * w].reshape(share, shards, w).transpose(1, 0, 2))
            at += shards * w
    own = lax.psum_scatter(jnp.concatenate(by_slice, axis=2), "mp", scatter_dimension=0).astype(F32)
    split, at = [], 0
    for w in first_widths + second_widths:
        split.append(own[:, at : at + w])
        at += w
    g_ad_gate, g_ad_out, g_high_a, g_high_b, g_query, g_key, g_value, g_proj, g_up, g_down = split
    g_ad_high = jnp.concatenate([g_high_a, g_high_b[: ad_high.shape[0] // devices - share]], axis=0)
    g_qkv = jnp.stack([g_query, g_key, g_value])
    g_ad_out, g_proj, g_down = g_ad_out.T, g_proj.T, g_down.T
    g_cn_down = jnp.einsum("tc,th->ch", d_branch_all, hidden_act, preferred_element_type=F32).astype(BF)
    g_cn_up = jnp.einsum("tc,th->ch", normed_all, d_hidden, preferred_element_type=F32).astype(BF)
    cn_grads = [g.reshape(devices, chan_count // devices, -1) for g in (g_cn_up, g_cn_down)]
    d_conv, g_hr_gain = jax.vjp(layer_norm, conv_out, hr_gainf)[1](d_normed)
    d_conv = d_conv * cell_mask
    d_bordered = extended(d_conv.astype(BF), (("mp", 1),), 3)
    d_conv_in, g_conv, (g_cn_up, g_cn_down) = conv_backward(
        d_bordered[0], bordered[0], taps, size, cn_grads, devices
    )
    g_cn_up, g_cn_down = g_cn_up.astype(F32), g_cn_down.astype(F32).T
    g_conv = g_conv.reshape(conv_w.shape)
    d_hr_in = (d_branch + d_conv_in) * cell_mask
    small = (g_conv, g_hr_gain, g_ln1, g_ln2)
    packed = jnp.concatenate([g.reshape(-1) for g in small])
    packed = lax.psum(lax.psum(packed, "mp"), "dp")
    parts, at = [], 0
    for g in small:
        parts.append(packed[at : at + g.size].reshape(g.shape))
        at += g.size
    g_conv, g_hr_gain, g_ln1, g_ln2 = parts
    return (
        low_out,
        hr_out,
        d_low_in,
        d_hr_in,
        g_conv,
        g_hr_gain,
        g_cn_up,
        g_cn_down,
        g_ad_gate,
        g_ad_high,
        g_ad_out,
        g_ln1,
        g_qkv,
        g_proj,
        g_ln2,
        g_up,
        g_down,
    )


def solution(mesh):
    return jax.shard_map(
        per_device,
        mesh=mesh,
        in_specs=(
            P("dp", "mp", None, None),
            P("dp", "mp", None),
            P("dp", "mp", None),
            P(),
            P(),
            P(None, "mp"),
            P("mp", None),
            P(None, "mp"),
            P(None, "mp"),
            P("mp", None),
            P(),
            P(None, None, "mp"),
            P("mp", None),
            P(),
            P(None, "mp"),
            P("mp", None),
            P("dp", "mp", None),
            P("dp", "mp", None, None),
        ),
        out_specs=(
            P("dp", "mp", None),
            P("dp", "mp", None, None),
            P("dp", "mp", None),
            P("dp", "mp", None, None),
            P(),
            P(),
            P("dp", "mp"),
            P("mp", "dp"),
            P("dp", "mp"),
            P("dp", "mp"),
            P("mp", "dp"),
            P(),
            P(None, "dp", "mp"),
            P("mp", "dp"),
            P(),
            P("dp", "mp"),
            P("mp", "dp"),
        ),
        check_vma=False,
    )
```

```python
import jax
import jax.numpy as jnp
from jax import lax
from jax.experimental import pallas as pl
from jax.experimental.pallas import tpu as pltpu
from jax.sharding import PartitionSpec as P

HEAD = 64
LANES = 128
EDGE = 8
CHUNKS = 6
TILE = 512
MIB = 1024 * 1024
MESH = pl.DeviceIdType.MESH
BF = jnp.bfloat16
F32 = jnp.float32

def gelu_parts(x):
    c = 0.7978845608028654
    x2 = x * x
    t = jnp.tanh(c * x * (1.0 + 0.044715 * x2))
    half = 0.5 * (1.0 + t)
    slope = half + 0.5 * x * (1.0 - t * t) * (c * (1.0 + 3 * 0.044715 * x2))
    return x * half, slope


def gelu(x):
    c = 0.7978845608028654
    t = jnp.tanh(c * x * (1.0 + 0.044715 * (x * x)))
    return 0.5 * x * (1.0 + t)


def dp_bit(position):
    return lax.rem(lax.axis_index("dp") // 2**position, 2)


def dp_mate(position):
    return lax.axis_index("dp") + 2**position * (1 - 2 * dp_bit(position))


class Halving:
    def __init__(self, bits, lasts, shape, block):
        self.lasts, self.shape, self.block = lasts, shape, block
        left = list(bits)
        self.bits = [left.pop(0 if last else -1) for last in lasts]

    def split(self, count, p):
        if count == 1:
            return (1, 1)
        return (count // 2, 2) if self.lasts[p] else (2, count // 2)

    def buffers(self):
        count, rows, cols = self.shape
        got, held = [], []
        for p in range(len(self.bits)):
            count //= 2
            got.append(jax.ShapeDtypeStruct((count, rows, cols), BF))
            held.append(jax.ShapeDtypeStruct(self.split(count, p + 1) + (rows, cols), BF))
        return got + held

    def semaphores(self):
        return [pltpu.SemaphoreType.DMA((len(self.bits),))] * 2

    def bind(self, first, buffers, send, recv):
        steps = len(self.bits)
        self.now = [first] + list(buffers[steps:])
        self.got, self.send, self.recv = buffers[:steps], send, recv

    def part(self, p, mine):
        bit = dp_bit(self.bits[p])
        index = bit if mine else 1 - bit
        return self.now[p].at[:, index] if self.lasts[p] else self.now[p].at[index]

    def copy(self, p):
        return pltpu.make_async_remote_copy(
            src_ref=self.part(p, False), dst_ref=self.got[p], send_sem=self.send.at[p], recv_sem=self.recv.at[p],
            device_id={"dp": dp_mate(self.bits[p])}, device_id_type=MESH,
        )

    def start(self, p):
        self.copy(p).start()

    def finish(self, p):
        self.copy(p).wait()
        count, rows, cols = self.got[p].shape
        ways = self.split(count, p + 1)

        def add(a, b, out):
            out[...] = (a[...].astype(F32) + b[...].astype(F32)).astype(BF).reshape(out.shape)

        flat = pl.BlockSpec((1, rows, self.block), lambda k, c: (k, 0, c))
        paired = pl.BlockSpec((1, 1, rows, self.block), lambda k, c: (k // ways[1], lax.rem(k, ways[1]), 0, c))
        pltpu.emit_pipeline(add, grid=(count, cols // self.block), in_specs=[flat, flat], out_specs=[paired])(
            self.part(p, True), self.got[p], self.now[p + 1]
        )


def chain_exchange(n, chunks, lag, own_hbm, gathered, partial, travel, compute, result_hbm,
                   sems, prepare, arrived, mates=(), begin=None, turn=None):
    ag_send, ag_recv, rs_send, rs_recv, local_sem = sems
    d = lax.axis_index("mp")
    has_left, has_right = d > 0, d < n - 1

    barrier = pltpu.get_barrier_semaphore()

    @pl.when(has_left)
    def _():
        pl.semaphore_signal(barrier, inc=1, device_id={"mp": d - 1}, device_id_type=MESH)

    @pl.when(has_right)
    def _():
        pl.semaphore_signal(barrier, inc=1, device_id={"mp": d + 1}, device_id_type=MESH)

    for mate in mates:
        pl.semaphore_signal(barrier, inc=1, device_id={"dp": mate}, device_id_type=MESH)

    load = pltpu.make_async_copy(own_hbm, gathered.at[d], local_sem)
    load.start()

    pl.semaphore_wait(barrier, has_left.astype(jnp.int32) + has_right.astype(jnp.int32) + len(mates))
    if begin is not None:
        begin()
    load.wait()

    def ag(way, s, j):
        return pltpu.make_async_remote_copy(
            src_ref=gathered.at[s, j], dst_ref=gathered.at[s, j],
            send_sem=ag_send.at[way, s, j], recv_sem=ag_recv.at[s, j],
            device_id={"mp": d + 1 - 2 * way}, device_id_type=MESH)

    def rs(way, s, j):
        there = d + 1 - 2 * way
        slot = jnp.where((s == there) & (way == 0), n, s)
        return pltpu.make_async_remote_copy(
            src_ref=travel.at[s, j], dst_ref=travel.at[slot, j],
            send_sem=rs_send.at[s, j], recv_sem=rs_recv.at[slot, j],
            device_id={"mp": there}, device_id_type=MESH)

    def rs_wait(slot, j):
        pltpu.make_async_copy(travel.at[slot, j], travel.at[slot, j], rs_recv.at[slot, j]).wait()

    def first(j, _):
        @pl.when(has_right)
        def _():
            ag(0, d, j).start()

        @pl.when(has_left)
        def _():
            ag(1, d, j).start()
        return 0
    lax.fori_loop(0, chunks, first, 0)

    def step(g, _):
        k, j = g // chunks, lax.rem(g, chunks)
        if turn is not None:
            turn(g)

        @pl.when(g < n * chunks)
        def _():
            def side(way, _):
                s = d - k + 2 * k * way
                ok = (s >= 0) & (s < n) & ((k > 0) | (way == 0))

                @pl.when(ok)
                def _():
                    prepare(s, j)

                    @pl.when(k > 0)
                    def _():
                        pltpu.make_async_copy(gathered.at[s, j], gathered.at[s, j], ag_recv.at[s, j]).wait()

                        @pl.when((way == 0) & has_right)
                        def _():
                            ag(0, s, j).start()

                        @pl.when((way == 1) & has_left)
                        def _():
                            ag(1, s, j).start()
                    arrived(s, j)
                    compute(s, j)
                return 0
            lax.fori_loop(0, 2, side, 0)

        q = g - (n - 1 - d) * lag
        ql = jnp.clip(q, 0, n * chunks - 1)
        s, jj = n - 1 - ql // chunks, lax.rem(ql, chunks)

        @pl.when((q >= 0) & (q < n * chunks) & (s <= d) & (has_right | (s < d)))
        def _():
            @pl.when(has_right)
            def _():
                rs_wait(s, jj)

                @pl.when(s < d)
                def _():
                    travel[s, jj] = (partial[s, jj].astype(F32) + travel[s, jj].astype(F32)).astype(BF)

                @pl.when(s == d)
                def _():
                    partial[s, jj] = (partial[s, jj].astype(F32) + travel[s, jj].astype(F32)).astype(partial.dtype)

            @pl.when(d == n - 1)
            def _():
                travel[s, jj] = partial[s, jj].astype(BF)

            @pl.when(s < d)
            def _():
                rs(1, s, jj).start()

        q2 = g - d * lag
        qr = jnp.clip(q2, 0, n * chunks - 1)
        s2, j2 = qr // chunks, lax.rem(qr, chunks)

        @pl.when((q2 >= 0) & (q2 < n * chunks) & (s2 >= d) & (has_left | (s2 > d)))
        def _():
            @pl.when(has_left)
            def _():
                slot = jnp.where(s2 == d, n, s2)
                rs_wait(slot, j2)

                @pl.when(s2 > d)
                def _():
                    travel[s2, j2] = (partial[s2, j2].astype(F32) + travel[s2, j2].astype(F32)).astype(BF)

                @pl.when(s2 == d)
                def _():
                    partial[s2, j2] = (partial[s2, j2].astype(F32) + travel[n, j2].astype(F32)).astype(partial.dtype)

            @pl.when(d == 0)
            def _():
                travel[s2, j2] = partial[s2, j2].astype(BF)

            @pl.when(s2 > d)
            def _():
                rs(0, s2, j2).start()
        return 0

    lax.fori_loop(0, n * chunks + (n - 1) * lag, step, 0)

    store = pltpu.make_async_copy(partial.at[d], result_hbm, local_sem)
    store.start()

    def drain(i, _):
        s, j = i // chunks, lax.rem(i, chunks)

        @pl.when(has_right & (s <= d))
        def _():
            ag(0, s, j).wait_send()

        @pl.when(has_left & (s >= d))
        def _():
            ag(1, s, j).wait_send()

        @pl.when(s < d)
        def _():
            rs(1, s, j).wait_send()

        @pl.when(s > d)
        def _():
            rs(0, s, j).wait_send()
        return 0
    lax.fori_loop(0, n * chunks, drain, 0)
    store.wait()


def chain_sems(n, chunks):
    dma = pltpu.SemaphoreType.DMA
    return [dma((2, n, chunks)), dma((n, chunks)), dma((n, chunks)), dma((n + 1, chunks)), dma]


def chunk_buffers(n, rows, c, kept):
    return [
        pltpu.VMEM((n, CHUNKS, rows, c), BF),
        pltpu.VMEM((n, CHUNKS, rows, c), kept),
        pltpu.VMEM((n + 1, CHUNKS, rows, c), BF),
    ]


def columns(i):
    return pl.ds(pl.multiple_of(i * TILE, TILE), TILE)


def drain_copies(n, copy):
    def one(i, _):
        copy(i // CHUNKS, lax.rem(i, CHUNKS)).wait()
        return 0

    lax.fori_loop(0, n * CHUNKS, one, 0)


def big_forward(x, w_up, w_down, n):
    t, c = x.shape
    h = w_up.shape[1]
    rows = t // CHUNKS

    def kernel(
        x_ref, wu, wd, out, x_all, act_all, slope_all,
        gathered, partial, travel, act, slope, copied, stored, *sems
    ):
        def x_copy(s, j):
            return pltpu.make_async_copy(gathered.at[s, j], x_all.at[s, j], copied.at[s, j])

        def prepare(s, j):
            pass

        def arrived(s, j):
            x_copy(s, j).start()

        def compute(s, j):
            block = gathered.at[s, j]

            def up(i, _):
                pre = jnp.dot(block[...], wu[:, columns(i)], preferred_element_type=F32)
                value, rate = gelu_parts(pre)
                act[:, columns(i)] = value.astype(BF)
                slope[:, columns(i)] = rate.astype(BF)
                return 0

            lax.fori_loop(0, h // TILE, up, 0)
            keep_act = pltpu.make_async_copy(act, act_all.at[s, j], stored.at[0])
            keep_slope = pltpu.make_async_copy(slope, slope_all.at[s, j], stored.at[1])
            keep_act.start()
            keep_slope.start()

            def down(i, _):
                partial[s, j, :, columns(i)] = jnp.dot(
                    act[...], wd[:, columns(i)], preferred_element_type=F32
                )
                return 0

            lax.fori_loop(0, c // TILE, down, 0)
            keep_act.wait()
            keep_slope.wait()

        chain_exchange(
            n, CHUNKS, 1, x_ref, gathered, partial, travel, compute, out, sems, prepare, arrived
        )
        drain_copies(n, x_copy)

    whole = pl.BlockSpec(memory_space=pl.ANY)
    local = pl.BlockSpec(memory_space=pltpu.VMEM)
    out, x_all, act_all, slope_all = pl.pallas_call(
        kernel,
        out_shape=(
            jax.ShapeDtypeStruct((CHUNKS, rows, c), F32),
            jax.ShapeDtypeStruct((n, CHUNKS, rows, c), BF),
            jax.ShapeDtypeStruct((n, CHUNKS, rows, h), BF),
            jax.ShapeDtypeStruct((n, CHUNKS, rows, h), BF),
        ),
        in_specs=[whole, local, local],
        out_specs=(whole,) * 4,
        scratch_shapes=chunk_buffers(n, rows, c, F32)
        + [pltpu.VMEM((rows, h), BF)] * 2
        + [pltpu.SemaphoreType.DMA((n, CHUNKS)), pltpu.SemaphoreType.DMA((2,))]
        + chain_sems(n, CHUNKS),
        compiler_params=pltpu.CompilerParams(
            collective_id=0, has_side_effects=True, vmem_limit_bytes=60 * MIB
        ),
        cost_estimate=pl.CostEstimate(
            flops=4 * n * t * c * h, bytes_accessed=8 * n * t * c, transcendentals=n * t * h
        ),
    )(x.reshape(CHUNKS, rows, c), w_up, w_down)
    return (
        out.reshape(t, c),
        x_all.reshape(n * t, c),
        act_all.reshape(n * t, h),
        slope_all.reshape(n * t, h),
    )


def big_backward(d, slope_all, w_up, w_down, grads, n, devices):
    t, c = d.shape
    h = w_up.shape[1]
    rows = t // CHUNKS
    pairs, g_rows, g_cols = grads.shape
    bits = range(1, devices.bit_length() - 1)
    split = g_rows // 2
    steps = len(bits)
    plans = [Halving(bits, [last] * steps, (pairs, split, g_cols), min(g_cols, 512)) for last in (True, False)]
    extras = [b for plan in plans for b in plan.buffers()[:-1]]
    each = 2 * steps - 1

    def kernel(d_ref, slopes, wu, wd, g_first, g_second, out, d_all, h_all, *rest):
        sums, extra, rest = rest[0], rest[1 : 1 + 2 * each], rest[1 + 2 * each :]
        gathered, partial, travel, slope, grad, copied, stored, send0, recv0, send1, recv1 = rest[:11]
        sems = rest[11:]
        plans[0].bind(g_first.at[:, :, pl.ds(0, split)], extra[:each] + (sums.at[0],), send0, recv0)
        plans[1].bind(g_second.at[:, :, pl.ds(split, split)], extra[each:] + (sums.at[1],), send1, recv1)

        def begin():
            for plan in plans:
                plan.start(0)

        def pass_on(p):
            for plan in plans:
                plan.finish(p)
            if p + 1 < steps:
                for plan in plans:
                    plan.start(p + 1)

        total = n * CHUNKS + n - 1
        due = [total * (2 ** steps - 2 ** (steps - 1 - p)) * 8 // (10 * (2 ** steps - 1)) for p in range(steps)]

        def turn(g):
            for p in range(steps - 1):
                pl.when(g == due[p])(lambda p=p: pass_on(p))

        def d_copy(s, j):
            return pltpu.make_async_copy(gathered.at[s, j], d_all.at[s, j], copied.at[s, j])

        def slope_copy(s, j):
            return pltpu.make_async_copy(slopes.at[s, j], slope, stored.at[0])

        def prepare(s, j):
            slope_copy(s, j).start()

        def arrived(s, j):
            d_copy(s, j).start()

        def compute(s, j):
            block = gathered.at[s, j]
            slope_copy(s, j).wait()

            def up(i, _):
                back = lax.dot_general(
                    block[...], wd[columns(i), :], (((1,), (1,)), ((), ())), preferred_element_type=F32
                )
                grad[:, columns(i)] = (back * slope[:, columns(i)].astype(F32)).astype(BF)
                return 0

            lax.fori_loop(0, h // TILE, up, 0)
            keep = pltpu.make_async_copy(grad, h_all.at[s, j], stored.at[1])
            keep.start()

            def down(i, _):
                partial[s, j, :, columns(i)] = lax.dot_general(
                    grad[...], wu[columns(i), :], (((1,), (1,)), ((), ())), preferred_element_type=F32
                )
                return 0

            lax.fori_loop(0, c // TILE, down, 0)
            keep.wait()

        chain_exchange(
            n, CHUNKS, 1, d_ref, gathered, partial, travel, compute, out, sems, prepare, arrived,
            [dp_mate(b) for b in bits], begin, turn
        )
        pass_on(steps - 1)
        drain_copies(n, d_copy)

    whole = pl.BlockSpec(memory_space=pl.ANY)
    local = pl.BlockSpec(memory_space=pltpu.VMEM)
    out, d_all, h_all, sums, *_ = pl.pallas_call(
        kernel,
        out_shape=(
            jax.ShapeDtypeStruct((CHUNKS, rows, c), F32),
            jax.ShapeDtypeStruct((n, CHUNKS, rows, c), BF),
            jax.ShapeDtypeStruct((n, CHUNKS, rows, h), BF),
            jax.ShapeDtypeStruct((2, 1, 1, split, g_cols), BF),
            *extras,
        ),
        in_specs=[whole, whole, local, local, whole, whole],
        out_specs=(whole,) * (4 + 2 * each),
        scratch_shapes=chunk_buffers(n, rows, c, F32)
        + [pltpu.VMEM((rows, h), BF)] * 2
        + [pltpu.SemaphoreType.DMA((n, CHUNKS)), pltpu.SemaphoreType.DMA((2,))]
        + plans[0].semaphores() + plans[1].semaphores()
        + chain_sems(n, CHUNKS),
        compiler_params=pltpu.CompilerParams(
            collective_id=1, has_side_effects=True, vmem_limit_bytes=60 * MIB
        ),
        cost_estimate=pl.CostEstimate(
            flops=4 * n * t * c * h, bytes_accessed=8 * n * t * c, transcendentals=0
        ),
    )(
        d.reshape(CHUNKS, rows, c), slope_all.reshape(n, CHUNKS, rows, h), w_up, w_down,
        grads.reshape(pairs // 2, 2, g_rows, g_cols), grads.reshape(2, pairs // 2, g_rows, g_cols),
    )
    return out.reshape(t, c), d_all.reshape(n * t, c), h_all.reshape(n * t, h), sums.reshape(g_rows, g_cols)


def frame(dst, src):
    rows, cols, _ = src.shape
    dst[:, :EDGE] = jnp.zeros((rows, EDGE, LANES), F32)
    dst[:, EDGE + cols:] = jnp.zeros((rows, EDGE, LANES), F32)
    dst[:, EDGE:EDGE + cols] = src[...].astype(F32)


def correlate(out, framed, taps, size, flip, group):
    rows, cols, _ = out.shape
    reach = size // 2
    def some(r, _):
        acc = jnp.zeros((group, cols, LANES), F32)
        for a in range(size):
            for b in range(size):
                tap = (size - 1 - a) * size + size - 1 - b if flip else a * size + b
                acc = acc + framed[pl.ds(r * group + a, group), pl.ds(EDGE - reach + b, cols), :] * taps[tap]
        out[pl.ds(r * group, group)] = acc
        return 0
    lax.fori_loop(0, rows // group, some, 0)


def conv_forward(x, w, size, n):
    rows, cols, c = x.shape
    reach = size // 2

    def kernel(x_ref, w_ref, out, bordered, framed, sent, got, own):
        d = lax.axis_index("mp")
        has_up, has_down = d > 0, d < n - 1
        barrier = pltpu.get_barrier_semaphore()

        @pl.when(has_up)
        def _():
            pl.semaphore_signal(barrier, inc=1, device_id={"mp": d - 1}, device_id_type=MESH)

        @pl.when(has_down)
        def _():
            pl.semaphore_signal(barrier, inc=1, device_id={"mp": d + 1}, device_id_type=MESH)

        keep = pltpu.make_async_copy(x_ref, bordered.at[pl.ds(reach, rows)], own)
        keep.start()
        pl.semaphore_wait(barrier, has_up.astype(jnp.int32) + has_down.astype(jnp.int32))
        up = pltpu.make_async_remote_copy(
            src_ref=x_ref.at[pl.ds(0, reach)], dst_ref=bordered.at[pl.ds(reach + rows, reach)],
            send_sem=sent.at[0], recv_sem=got.at[0], device_id={"mp": d - 1}, device_id_type=MESH,
        )
        down = pltpu.make_async_remote_copy(
            src_ref=x_ref.at[pl.ds(rows - reach, reach)], dst_ref=bordered.at[pl.ds(0, reach)],
            send_sem=sent.at[1], recv_sem=got.at[1], device_id={"mp": d + 1}, device_id_type=MESH,
        )
        nothing = jnp.zeros((reach, cols, c), BF)

        @pl.when(has_up)
        def _():
            up.start()

        @pl.when(has_down)
        def _():
            down.start()

        @pl.when(d == 0)
        def _():
            bordered[:reach] = nothing

        @pl.when(d == n - 1)
        def _():
            bordered[reach + rows :] = nothing

        keep.wait()

        @pl.when(has_up)
        def _():
            down.wait_recv()

        @pl.when(has_down)
        def _():
            up.wait_recv()

        def block(i, _):
            lanes = pl.ds(pl.multiple_of(i * LANES, LANES), LANES)
            frame(framed, bordered.at[:, :, lanes])
            correlate(out.at[:, :, lanes], framed, w_ref.at[:, :, lanes], size, False, 4)
            return 0

        lax.fori_loop(0, c // LANES, block, 0)

        @pl.when(has_up)
        def _():
            up.wait_send()

        @pl.when(has_down)
        def _():
            down.wait_send()

    local = pl.BlockSpec(memory_space=pltpu.VMEM)
    dma = pltpu.SemaphoreType.DMA
    return pl.pallas_call(
        kernel,
        out_shape=(
            jax.ShapeDtypeStruct((rows, cols, c), F32),
            jax.ShapeDtypeStruct((rows + 2 * reach, cols, c), BF),
        ),
        in_specs=[local, local],
        out_specs=(local, local),
        scratch_shapes=[pltpu.VMEM((rows + 2 * reach, cols + 2 * EDGE, LANES), F32), dma((2,)), dma((2,)), dma],
        compiler_params=pltpu.CompilerParams(
            collective_id=5, has_side_effects=True, vmem_limit_bytes=40 * MIB
        ),
    )(x, w)


def conv_backward(d, x, w, size, grads, devices, group=4, bgroup=4):
    high, cols, c = x.shape
    rows = high - size + 1
    reach = size // 2
    steps = devices.bit_length() - 1
    shape = grads[0].shape
    plans = [Halving(range(steps), [True] + [last] * (steps - 1), shape, shape[2]) for last in (True, False)]
    blocks = c // LANES
    due = [blocks * (p + 1) // (steps + 1) for p in range(steps)]

    def kernel(d_ref, x_ref, w_ref, g0, g1, out, g, *rest):
        extra, rest = rest[: 4 * steps], rest[4 * steps :]
        dframed, xframed, *sems = rest
        plans[0].bind(g0, extra[: 2 * steps], sems[0], sems[1])
        plans[1].bind(g1, extra[2 * steps :], sems[2], sems[3])
        i = pl.program_id(0)

        @pl.when(i == 0)
        def _():
            barrier = pltpu.get_barrier_semaphore()
            for b in range(steps):
                pl.semaphore_signal(barrier, inc=1, device_id={"dp": dp_mate(b)}, device_id_type=MESH)
            pl.semaphore_wait(barrier, steps)
            for plan in plans:
                plan.start(0)

        for p in range(steps - 1):
            @pl.when(i == due[p])
            def _():
                for plan in plans:
                    plan.finish(p)
                for plan in plans:
                    plan.start(p + 1)

        frame(dframed, d_ref)
        frame(xframed, x_ref)
        correlate(out, dframed, w_ref, size, True, group)
        for a in range(size):
            def some(r, accs):
                dv = dframed[pl.ds(reach + r * bgroup, bgroup), EDGE : EDGE + cols]
                new = []
                for b in range(size):
                    prod = dv * xframed[pl.ds(r * bgroup + a, bgroup), pl.ds(EDGE - reach + b, cols), :]
                    new.append(accs[b] + jnp.sum(prod.reshape(-1, 8, LANES), axis=0))
                return tuple(new)

            accs = lax.fori_loop(
                0, rows // bgroup, some, tuple(jnp.zeros((8, LANES), F32) for _ in range(size))
            )
            for b in range(size):
                g[a * size + b] = jnp.sum(accs[b], axis=0, keepdims=True)

        @pl.when(i == blocks - 1)
        def _():
            for plan in plans:
                plan.finish(steps - 1)

    whole = pl.BlockSpec(memory_space=pl.ANY)
    d_in, g, *extra = pl.pallas_call(
        kernel,
        grid=(blocks,),
        out_shape=(
            jax.ShapeDtypeStruct((rows, cols, c), F32),
            jax.ShapeDtypeStruct((size * size, 1, c), F32),
            *plans[0].buffers(),
            *plans[1].buffers(),
        ),
        in_specs=[pl.BlockSpec((high, cols, LANES), lambda i: (0, 0, i))] * 2
        + [pl.BlockSpec((size * size, 1, LANES), lambda i: (0, 0, i)), whole, whole],
        out_specs=(
            pl.BlockSpec((rows, cols, LANES), lambda i: (0, 0, i)),
            pl.BlockSpec((size * size, 1, LANES), lambda i: (0, 0, i)),
        )
        + (whole,) * (4 * steps),
        scratch_shapes=[pltpu.VMEM((high, cols + 2 * EDGE, LANES), F32)] * 2
        + plans[0].semaphores() + plans[1].semaphores(),
        compiler_params=pltpu.CompilerParams(
            collective_id=3, has_side_effects=True, vmem_limit_bytes=40 * MIB
        ),
    )(
        d, x, w, grads[0].reshape((shape[0] // 2, 2) + shape[1:]), grads[1].reshape((shape[0] // 2, 2) + shape[1:])
    )
    return d_in, g, [extra[2 * steps - 1].reshape(shape[1:]), extra[4 * steps - 1].reshape(shape[1:])]


GATE, OUT, HIGH_A, HIGH_B, QUERY, KEY, VALUE, PROJ = range(8)
L_LOW, L_DF, L_POOL_A, L_POOL_B, L_FIRST, L_DA, L_SECOND, L_COT = range(8)
R_DGATE, R_MERGE, R_DHIGH, R_DQ, R_DK, R_DV, R_ATT, R_DUP, R_ACT = range(9)


def nn(a, b):
    return jnp.dot(a, b, preferred_element_type=F32)


def nt(a, b):
    return lax.dot_general(a, b, (((1,), (1,)), ((), ())), preferred_element_type=F32)


def tn(a, b):
    return lax.dot_general(a, b, (((0,), (0,)), ((), ())), preferred_element_type=F32)


def normalise(x, gain):
    centred = x - jnp.mean(x, -1, keepdims=True)
    rate = lax.rsqrt(jnp.mean(centred * centred, -1, keepdims=True) + 1e-06)
    return centred * rate * gain


def normalise_back(x, gain, d):
    centred = x - jnp.mean(x, -1, keepdims=True)
    rate = lax.rsqrt(jnp.mean(centred * centred, -1, keepdims=True) + 1e-06)
    hat = centred * rate
    dg = d * gain
    back = rate * (dg - jnp.mean(dg, -1, keepdims=True) - hat * jnp.mean(dg * hat, -1, keepdims=True))
    return back, jnp.sum(d * hat, axis=0, keepdims=True)


def low_stage(low, pool_a, pool_b, cot, gain1, gain2, packed, n, devices, cid):
    t, dim = low.shape
    every = n * t
    width = dim // n
    heads = width // HEAD
    pairs = devices // 2
    rows = dim // devices
    half = dim // 2
    ff = 4 * dim
    scale = HEAD ** (-0.5)

    def kernel(
        low_ref, pool_a_ref, pool_b_ref, cot_ref, gain1_ref, gain2_ref, w_hbm,
        low_out, d_low, d_pool_a, d_pool_b, g_ln1, g_ln2, grads,
        wv, lhs, lhs2, rhs, gate, high, merged, resid, d_res, slope, mixed, heads_in, att_all, d_att, d_mixed,
        d_heads, probs, d_scores, stage, w_sem, q_send, q_got, a_send, a_got, b_send, b_got, c_send, c_got, own_sem,
        l_send, l_got, r_send, r_got, stage_sem,
    ):
        d = lax.axis_index("mp")
        dp = lax.axis_index("dp")
        core = lax.rem(dp, 2)
        mate = dp + 1 - 2 * core
        barrier = pltpu.get_barrier_semaphore()
        for k in range(1, n):
            pl.semaphore_signal(barrier, inc=1, device_id={"mp": lax.rem(d + k, n)}, device_id_type=MESH)
        pl.semaphore_signal(barrier, inc=1, device_id={"dp": mate}, device_id_type=MESH)

        def w_copy(w, k):
            c, z = k // n, lax.rem(k, n)
            wide, base, at = w_place(w)
            src = w_hbm.at[:, c, z, :, pl.ds(base, wide)]
            dst = wv.at[c, :, :, pl.ds(pl.multiple_of(at + z * wide, wide), wide)]
            return pltpu.make_async_copy(src, dst, w_sem.at[w, k])

        def w_place(w):
            if w < 8:
                return width, w * width, w * dim
            return ff // n, 8 * width + (w - 8) * ff // n, 8 * dim + (w - 8) * ff

        def w_each(w, act):
            def one(k, _):
                act(w_copy(w, k))
                return 0

            lax.fori_loop(0, 2 * n, one, 0)

        for w in range(10):
            w_each(w, lambda copy: copy.start())

        def w_wait(*which):
            for w in which:
                w_each(w, lambda copy: copy.wait())

        def w_cols(at, size):
            return wv[:, :, :, pl.ds(at, size)].reshape(dim, size)

        def forward(x, first, count, put):
            def one(i, _):
                put(pl.multiple_of(i * TILE, TILE), nn(x, w_cols(pl.multiple_of(first * dim + i * TILE, TILE), TILE)))
                return 0
            lax.fori_loop(0, count * dim // TILE, one, 0)

        def backward(get, first, count, dst, fresh):
            def one(i, _):
                for c in range(2):
                    part = wv[c, :, :, pl.ds(pl.multiple_of((first + i) * dim, dim), dim)].reshape(half, dim)
                    y = nt(get(pl.multiple_of(i * dim, dim)), part)
                    cols = slice(c * half, (c + 1) * half)
                    if fresh and count == 1:
                        dst[:, cols] = y
                    else:
                        dst[:, cols] += y
                return 0
            if fresh and count > 1:
                dst[...] = jnp.zeros(dst.shape, F32)
            if count == 1:
                one(0, 0)
            else:
                lax.fori_loop(0, count, one, 0)

        def r_cols(block, count=1):
            return pl.ds(block * dim, count * dim)

        def r_at(block):
            return block * dim if block <= R_DUP else block * dim + 3 * dim

        def r_copy(block):
            cols = pl.ds(r_at(block), dim if block < R_DUP else ff)
            return pltpu.make_async_remote_copy(
                src_ref=rhs.at[0, :, cols], dst_ref=rhs.at[1, :, cols], send_sem=r_send.at[block],
                recv_sem=r_got.at[block], device_id={"dp": mate}, device_id_type=MESH)

        def l_copy(i):
            return pltpu.make_async_remote_copy(
                src_ref=lhs.at[i, :, pl.ds(pl.multiple_of((1 - core) * half, half), half)], dst_ref=lhs2.at[i],
                send_sem=l_send.at[i], recv_sem=l_got.at[i], device_id={"dp": mate}, device_id_type=MESH)

        stored = []

        def grad(i, block, at, count, shared=False):
            if not shared:
                r_copy(block).wait_recv()
            own_l = pl.ds(pl.multiple_of(core * half, half), half)

            wide, base, first = w_place(at if at < 8 else 8 + (at - 8) * dim // ff)
            piece = min(TILE, wide)

            def out_copies(slot, k):
                out = []
                for q in range(TILE // piece):
                    z, col = divmod(at * dim - first + k * TILE + q * piece, wide)
                    out.append(
                        pltpu.make_async_copy(
                            stage.at[slot, :, :, pl.ds(q * piece, piece)],
                            grads.at[:, pl.ds(z * rows, rows), pl.ds(base + col, piece)],
                            stage_sem.at[slot, q],
                        )
                    )
                return out

            for k in range(count * dim // TILE):
                slot = len(stored) % 2
                if len(stored) >= 2:
                    wait(stored[-2])
                cols = pl.ds(r_at(block) + k * TILE, TILE)
                y = tn(lhs[i, :, own_l], rhs[0, :, cols]) + tn(lhs2[i], rhs[1, :, cols])
                stage[slot] = y.astype(BF).reshape(pairs, rows, TILE)
                stored.append(out_copies(slot, k))
                start(stored[-1])

        def to_heads(k, src, dst, send, got):
            out = []
            for step in range(1, n):
                peer = lax.rem(d + step, n)
                out.append(pltpu.make_async_remote_copy(
                    src_ref=src.at[:, pl.ds(pl.multiple_of(peer * width, width), width)],
                    dst_ref=dst.at[pl.ds(pl.multiple_of(d * t, t), t)],
                    send_sem=send.at[k, step], recv_sem=got.at[k, step], device_id={"mp": peer}, device_id_type=MESH))
            out.append(pltpu.make_async_copy(
                src.at[:, pl.ds(pl.multiple_of(d * width, width), width)], dst.at[pl.ds(pl.multiple_of(d * t, t), t)], own_sem.at[k]))
            return out

        def to_tokens(k, src, dst, send, got):
            out = []
            for step in range(1, n):
                peer = lax.rem(d + step, n)
                out.append(pltpu.make_async_remote_copy(
                    src_ref=src.at[pl.ds(pl.multiple_of(peer * t, t), t)],
                    dst_ref=dst.at[:, pl.ds(pl.multiple_of(d * width, width), width)],
                    send_sem=send.at[k, step], recv_sem=got.at[k, step], device_id={"mp": peer}, device_id_type=MESH))
            out.append(pltpu.make_async_copy(
                src.at[pl.ds(pl.multiple_of(d * t, t), t)], dst.at[:, pl.ds(pl.multiple_of(d * width, width), width)], own_sem.at[k]))
            return out

        def start(copies):
            for c in copies:
                c.start()

        def wait(copies):
            for c in copies:
                c.wait()

        lhs[L_LOW] = low_ref[...]
        lhs[L_POOL_A] = pool_a_ref[...]
        lhs[L_POOL_B] = pool_b_ref[...]
        lhs[L_COT] = cot_ref[...]
        acc = d_low
        w_wait(GATE)

        def put_gate(at, y):
            gate[:, pl.ds(at, TILE)] = 1.0 / (1.0 + jnp.exp(-y))
        forward(lhs[L_LOW], GATE, 1, put_gate)
        w_wait(HIGH_A, HIGH_B, OUT)

        def put_high(at, y):
            high[:, pl.ds(at, TILE)] = y
        forward(lhs[L_POOL_A], HIGH_A, 1, put_high)

        def put_merging(at, y):
            cols = pl.ds(at, TILE)
            total = high[:, cols] + y
            high[:, cols] = total
            rhs[0, :, pl.ds(R_MERGE * dim + at, TILE)] = (total * gate[:, cols]).astype(BF)
        forward(lhs[L_POOL_B], HIGH_B, 1, put_merging)
        backward(lambda at: rhs[0, :, r_cols(R_MERGE)], OUT, 1, merged, True)
        merged[...] += lhs[L_LOW].astype(F32)
        lhs[L_FIRST] = normalise(merged[...], gain1_ref[...]).astype(BF)

        w_wait(QUERY, KEY, VALUE, PROJ)
        pl.semaphore_wait(barrier, n)
        for i in (L_LOW, L_POOL_A, L_POOL_B, L_COT, L_FIRST):
            l_copy(i).start()
        r_copy(R_MERGE).start()
        out_q = []
        for k in range(3):
            def put_mixed(at, y):
                mixed[k, :, pl.ds(at, TILE)] = y.astype(BF)
            forward(lhs[L_FIRST], QUERY + k, 1, put_mixed)
            copies = to_heads(k, mixed.at[k], heads_in.at[k], q_send, q_got)
            start(copies)
            out_q += copies
        wait(out_q)

        for h in range(heads):
            lanes = slice(h * HEAD, (h + 1) * HEAD)

            def rows_of(b, _):
                some = pl.ds(pl.multiple_of(b * t, t), t)
                s = nt(heads_in[0, some, lanes], heads_in[1, :, lanes]) * scale
                e = jnp.exp(s - jnp.max(s, -1, keepdims=True))
                p = (e * (1.0 / jnp.sum(e, -1, keepdims=True))).astype(BF)
                probs[h, some] = p
                att_all[some, lanes] = nn(p, heads_in[2, :, lanes]).astype(BF)
                return 0
            lax.fori_loop(0, n, rows_of, 0)
        out_a = to_tokens(0, att_all, rhs.at[0, :, r_cols(R_ATT)], a_send, a_got)
        start(out_a)
        wait(out_a)
        r_copy(R_ATT).start()
        backward(lambda at: rhs[0, :, r_cols(R_ATT)], PROJ, 1, resid, True)
        resid[...] += merged[...]
        lhs[L_SECOND] = normalise(resid[...], gain2_ref[...]).astype(BF)
        l_copy(L_SECOND).start()

        w_wait(8)

        def put_up(at, y):
            value, rate = gelu_parts(y)
            rhs[0, :, pl.ds(r_at(R_ACT) + at, TILE)] = value.astype(BF)
            slope[:, pl.ds(at, TILE)] = rate.astype(BF)
        forward(lhs[L_SECOND], 8, 4, put_up)
        r_copy(R_ACT).start()
        w_wait(9)
        backward(lambda at: rhs[0, :, pl.ds(r_at(R_ACT) + at, dim)], 12, 4, acc, True)
        low_out[...] = resid[...] + acc[...]

        def put_d_up(at, y):
            rhs[0, :, pl.ds(r_at(R_DUP) + at, TILE)] = (y * slope[:, pl.ds(at, TILE)].astype(F32)).astype(BF)
        forward(lhs[L_COT], 12, 4, put_d_up)
        r_copy(R_DUP).start()
        backward(lambda at: rhs[0, :, pl.ds(r_at(R_DUP) + at, dim)], 8, 4, acc, True)
        back, g = normalise_back(resid[...], gain2_ref[...], acc[...])
        g_ln2[...] = g
        d_res[...] = lhs[L_COT].astype(F32) + back
        lhs[L_DA] = d_res[...].astype(BF)
        l_copy(L_DA).start()

        def put_d_att(at, y):
            mixed[0, :, pl.ds(at, TILE)] = y.astype(BF)
        forward(lhs[L_DA], PROJ, 1, put_d_att)
        out_b = to_heads(0, mixed.at[0], d_att, b_send, b_got)
        start(out_b)
        l_copy(L_COT).wait_recv()
        grad(L_COT, R_ACT, 12, 4)
        wait(out_b)
        for h in range(heads):
            lanes = slice(h * HEAD, (h + 1) * HEAD)

            def rows_of(b, _):
                some = pl.ds(pl.multiple_of(b * t, t), t)
                p = probs[h, some].astype(F32)
                dp_ = nt(d_att[some, lanes], heads_in[2, :, lanes])
                ds = (p * (dp_ - jnp.sum(dp_ * p, -1, keepdims=True)) * scale).astype(BF)
                d_scores[some] = ds
                d_heads[0, some, lanes] = nn(ds, heads_in[1, :, lanes]).astype(BF)
                return 0
            lax.fori_loop(0, n, rows_of, 0)
            d_heads[1, :, lanes] = tn(d_scores[...], heads_in[0, :, lanes]).astype(BF)
            d_heads[2, :, lanes] = tn(probs[h], d_att[:, lanes]).astype(BF)
        out_c = []
        for k in range(3):
            copies = to_tokens(k, d_heads.at[k], rhs.at[0, :, r_cols(R_DQ + k)], c_send, c_got)
            start(copies)
            out_c += copies
        l_copy(L_SECOND).wait_recv()
        grad(L_SECOND, R_DUP, 8, 4)
        l_copy(L_DA).wait_recv()
        grad(L_DA, R_ATT, PROJ, 1)
        wait(out_c)
        for k in range(3):
            r_copy(R_DQ + k).start()
        backward(lambda at: rhs[0, :, pl.ds(R_DQ * dim + at, dim)], QUERY, 3, acc, True)
        back, g = normalise_back(merged[...], gain1_ref[...], acc[...])
        g_ln1[...] = g
        d_res[...] += back
        lhs[L_DF] = d_res[...].astype(BF)
        l_copy(L_DF).start()

        def put_d_gate(at, y):
            cols = pl.ds(at, TILE)
            gv = gate[:, cols]
            part = y * gv
            rhs[0, :, pl.ds(R_DHIGH * dim + at, TILE)] = part.astype(BF)
            rhs[0, :, pl.ds(R_DGATE * dim + at, TILE)] = (part * high[:, cols] * (1.0 - gv)).astype(BF)
        forward(lhs[L_DF], OUT, 1, put_d_gate)
        r_copy(R_DHIGH).start()
        r_copy(R_DGATE).start()
        backward(lambda at: rhs[0, :, r_cols(R_DHIGH)], HIGH_A, 1, d_pool_a, True)
        backward(lambda at: rhs[0, :, r_cols(R_DHIGH)], HIGH_B, 1, d_pool_b, True)
        backward(lambda at: rhs[0, :, r_cols(R_DGATE)], GATE, 1, acc, True)
        d_low[...] = d_res[...] + acc[...]
        l_copy(L_FIRST).wait_recv()
        for k in range(3):
            grad(L_FIRST, R_DQ + k, QUERY + k, 1)
        l_copy(L_DF).wait_recv()
        grad(L_DF, R_MERGE, OUT, 1)
        l_copy(L_POOL_A).wait_recv()
        grad(L_POOL_A, R_DHIGH, HIGH_A, 1)
        l_copy(L_POOL_B).wait_recv()
        grad(L_POOL_B, R_DHIGH, HIGH_B, 1, shared=True)
        l_copy(L_LOW).wait_recv()
        grad(L_LOW, R_DGATE, GATE, 1)
        wait(stored[-2])
        wait(stored[-1])
        for i in range(8):
            l_copy(i).wait_send()
        for b in range(9):
            r_copy(b).wait_send()

    whole = pl.BlockSpec(memory_space=pl.ANY)
    local = pl.BlockSpec(memory_space=pltpu.VMEM)
    vm, dma = pltpu.VMEM, pltpu.SemaphoreType.DMA
    tok = jax.ShapeDtypeStruct((t, dim), F32)
    one = jax.ShapeDtypeStruct((1, dim), F32)
    return pl.pallas_call(
        kernel,
        out_shape=(tok, tok, tok, tok, one, one, jax.ShapeDtypeStruct((pairs, n * rows, 16 * width), BF)),
        in_specs=[local] * 6 + [whole],
        out_specs=(local,) * 6 + (whole,),
        scratch_shapes=[
            vm((2, pairs, rows, 16 * dim), BF), vm((8, t, dim), BF), vm((8, t, half), BF), vm((2, t, 15 * dim), BF),
            vm((t, dim), F32), vm((t, dim), F32), vm((t, dim), F32), vm((t, dim), F32), vm((t, dim), F32),
            vm((t, ff), BF), vm((3, t, dim), BF), vm((3, every, width), BF), vm((every, width), BF), vm((every, width), BF),
            vm((1, 8, 128), BF), vm((3, every, width), BF), vm((heads, every, every), BF), vm((every, every), BF),
            vm((2, pairs, rows, TILE), BF),
            dma((10, 2 * n)), dma((3, n)), dma((3, n)), dma((1, n)), dma((1, n)), dma((1, n)), dma((1, n)), dma((3, n)), dma((3, n)),
            dma((3,)), dma((8,)), dma((8,)), dma((9,)), dma((9,)), dma((2, 2)),
        ],
        compiler_params=pltpu.CompilerParams(collective_id=cid, has_side_effects=True, vmem_limit_bytes=61 * MIB),
        cost_estimate=pl.CostEstimate(flops=14 * 10**9, bytes_accessed=70 * 10**6, transcendentals=10**7),
    )(low, pool_a, pool_b, cot, gain1, gain2, packed.reshape(pairs, 2, n, rows, 16 * width))
def sum_everywhere(x, devices, n, cid):
    rows = x.shape[1]

    def kernel(x_ref, out, here, level, send1, recv1, send2, recv2, send3, recv3):
        me, d = lax.axis_index("dp"), lax.axis_index("mp")
        barrier = pltpu.get_barrier_semaphore()

        def greet(k, _):
            pl.semaphore_signal(
                barrier, inc=1, device_id={"dp": lax.rem(me + k, devices)}, device_id_type=MESH
            )
            return 0

        lax.fori_loop(1, devices, greet, 0)
        for k in range(1, n):
            pl.semaphore_signal(barrier, inc=1, device_id={"mp": lax.rem(d + k, n)}, device_id_type=MESH)
        here[me] = x_ref[me]
        pl.semaphore_wait(barrier, devices + n - 2)

        def spread(k):
            peer = lax.rem(me + k, devices)
            return pltpu.make_async_remote_copy(
                src_ref=x_ref.at[peer], dst_ref=here.at[me], send_sem=send1.at[k], recv_sem=recv1.at[k],
                device_id={"dp": peer}, device_id_type=MESH,
            )

        def across(k):
            return pltpu.make_async_remote_copy(
                src_ref=level.at[d], dst_ref=level.at[d], send_sem=send2.at[k], recv_sem=recv2.at[k],
                device_id={"mp": lax.rem(d + k, n)}, device_id_type=MESH,
            )

        def give(k):
            return pltpu.make_async_remote_copy(
                src_ref=out.at[me], dst_ref=out.at[me], send_sem=send3.at[k], recv_sem=recv3.at[k],
                device_id={"dp": lax.rem(me + k, devices)}, device_id_type=MESH,
            )

        def each(count, make, act):
            def one(k, _):
                act(make(k))
                return 0

            lax.fori_loop(1, count, one, 0)

        each(devices, spread, lambda c: c.start())
        each(devices, spread, lambda c: c.wait())
        level[d] = jnp.sum(here[...], axis=0)
        each(n, across, lambda c: c.start())
        each(n, across, lambda c: c.wait())
        out[me] = jnp.sum(level[...], axis=0)
        each(devices, give, lambda c: c.start())
        each(devices, give, lambda c: c.wait())

    vm, dma = pltpu.VMEM, pltpu.SemaphoreType.DMA
    return pl.pallas_call(
        kernel,
        out_shape=jax.ShapeDtypeStruct(x.shape, F32),
        in_specs=[pl.BlockSpec(memory_space=pltpu.VMEM)],
        out_specs=pl.BlockSpec(memory_space=pltpu.VMEM),
        scratch_shapes=[vm(x.shape, F32), vm((n, rows, LANES), F32)] + [dma((devices,)), dma((devices,)), dma((n,)), dma((n,)), dma((devices,)), dma((devices,))],
        compiler_params=pltpu.CompilerParams(
            collective_id=cid, has_side_effects=True, vmem_limit_bytes=16 * MIB
        ),
    )(x)


def own_part(w, axis):
    length = w.shape[axis] // lax.axis_size("dp")
    return lax.dynamic_slice_in_dim(w, lax.axis_index("dp") * length, length, axis)


def fold(w, rows):
    return w[:rows], jnp.pad(w[rows:], ((0, 2 * rows - w.shape[0]), (0, 0)))


def core_first(x, devices):
    shape = x.shape
    return x.reshape(shape[:-1] + (devices // 2, 2, -1)).swapaxes(-3, -2).reshape(shape)


def core_last(x, devices):
    shape = x.shape
    return x.reshape(shape[:-1] + (2, devices // 2, -1)).swapaxes(-3, -2).reshape(shape)


def extended(value, sides, width):
    for axis, dim in sides:
        devices, length = (lax.axis_size(axis), value.shape[dim])
        up = [(i, (i + 1) % devices) for i in range(devices - 1)]
        down = [(j, i) for i, j in up]
        last = lax.slice_in_dim(value, length - width, length, axis=dim)
        first = lax.slice_in_dim(value, 0, width, axis=dim)
        before = lax.ppermute(last, axis, up)
        after = lax.ppermute(first, axis, down)
        value = jnp.concatenate([before, value, after], axis=dim)
    return value


def layer_norm(values, gain):
    centre = jnp.mean(values, -1, keepdims=True)
    centred = values - centre
    variance = jnp.mean(centred * centred, -1, keepdims=True)
    return centred * lax.rsqrt(variance + 1e-06) * gain


def per_device(
    hr_in,
    low_in,
    valid,
    conv_w,
    hr_gain,
    cn_up,
    cn_down,
    ad_gate,
    ad_high,
    ad_out,
    ln1_gain,
    w_qkv,
    w_proj,
    ln2_gain,
    w_up,
    w_down,
    cot_low,
    cot_hr,
):
    item_count, row_count, col_count, chan_count = hr_in.shape
    devices, shards = lax.axis_size("dp"), lax.axis_size("mp")
    dims = low_in.shape[2]
    share = dims // devices
    qkv = own_part(w_qkv, 1)
    pieces = [
        own_part(ad_gate, 0), own_part(ad_out, 1).T, *fold(own_part(ad_high, 0), share),
        qkv[0], qkv[1], qkv[2], own_part(w_proj, 1).T, own_part(w_up, 0), own_part(w_down, 1).T,
    ]
    packed = lax.all_gather(jnp.concatenate(pieces, axis=1), ("dp", "mp"), axis=0)
    plane_mask = valid.astype(jnp.float32)
    cell_mask = plane_mask[..., None]
    masked = hr_in * valid.astype(jnp.bfloat16)[..., None]
    size = conv_w.shape[0]
    taps = conv_w.astype(F32).reshape(size * size, 1, chan_count)
    conv_out, bordered = conv_forward(masked[0], taps, size, shards)
    conv_out = conv_out[None]
    conv_out = conv_out * cell_mask
    hr_gainf = hr_gain.astype(jnp.float32)
    normed = layer_norm(conv_out, hr_gainf).astype(jnp.bfloat16)
    branch, normed_all, hidden_act, hidden_slope = big_forward(
        normed.reshape(row_count * col_count, chan_count), cn_up, cn_down, shards
    )
    branch = branch.reshape(hr_in.shape)
    hr_out = (masked.astype(jnp.float32) + branch) * cell_mask
    half_rows, half_cols = (row_count // 2, col_count // 2)
    block_sum = hr_out.reshape(item_count, half_rows, 2, half_cols, 2, chan_count).sum(axis=(2, 4))
    counts = plane_mask.reshape(item_count, half_rows, 2, half_cols, 2).sum(axis=(2, 4))
    divisor = jnp.maximum(counts, 1.0)[..., None]
    pooled = (
        (block_sum / divisor)
        .astype(jnp.bfloat16)
        .reshape(item_count, half_rows * half_cols, chan_count)
    )
    tokens = half_rows * half_cols
    by_share = pooled[0].reshape(tokens, devices, -1)
    pool_a = by_share[:, :, :share].reshape(tokens, dims)
    pool_b = jnp.pad(by_share[:, :, share:], ((0, 0), (0, 0), (0, 2 * share - by_share.shape[2]))).reshape(tokens, dims)
    low_out, d_low_in, d_pool_a, d_pool_b, g_ln1, g_ln2, low_grads = low_stage(
        *(core_first(v, devices) for v in (low_in[0], pool_a, pool_b, cot_low[0])),
        *(core_first(v.astype(F32), devices)[None] for v in (ln1_gain, ln2_gain)),
        packed, shards, devices, 2,
    )
    low_out = core_last(low_out, devices)[None]
    d_low_in = core_last(d_low_in, devices)[None]
    g_ln1, g_ln2 = core_last(g_ln1[0], devices), core_last(g_ln2[0], devices)
    d_pooled = jnp.concatenate(
        [
            core_last(d_pool_a, devices).reshape(tokens, devices, share),
            core_last(d_pool_b, devices).reshape(tokens, devices, share)[:, :, : by_share.shape[2] - share],
        ],
        axis=2,
    )
    d_block = d_pooled.reshape(item_count, half_rows, half_cols, chan_count) / divisor
    d_block = d_block.reshape(item_count, half_rows, 1, half_cols, 1, chan_count)
    d_map = cot_hr.astype(jnp.float32) + jnp.broadcast_to(
        d_block, (item_count, half_rows, 2, half_cols, 2, chan_count)
    ).reshape(hr_in.shape)
    d_branch = d_map * cell_mask
    d_normed, d_branch_all, d_hidden, low_sums = big_backward(
        d_branch.astype(BF).reshape(row_count * col_count, chan_count),
        hidden_slope, cn_up, cn_down, low_grads, shards, devices,
    )
    d_normed = d_normed.reshape(hr_in.shape)
    low_sums = lax.psum_scatter(low_sums.reshape(shards, share, -1), "mp", scatter_dimension=0)
    g_cn_down = jnp.einsum("tc,th->ch", d_branch_all, hidden_act, preferred_element_type=F32).astype(BF)
    g_cn_up = jnp.einsum("tc,th->ch", normed_all, d_hidden, preferred_element_type=F32).astype(BF)
    cn_grads = [g.reshape(devices, chan_count // devices, -1) for g in (g_cn_up, g_cn_down)]
    d_conv, g_hr_gain = jax.vjp(layer_norm, conv_out, hr_gainf)[1](d_normed)
    d_conv = d_conv * cell_mask
    d_bordered = extended(d_conv.astype(BF), (("mp", 1),), 3)
    d_bordered, low_sums = lax.optimization_barrier((d_bordered, low_sums))
    d_conv_in, g_conv, (g_cn_up, g_cn_down) = conv_backward(
        d_bordered[0], bordered, taps, size, cn_grads, devices
    )
    own = low_sums.astype(F32)
    split, at = [], 0
    for p in pieces:
        split.append(own[:, at : at + p.shape[1]])
        at += p.shape[1]
    g_ad_gate, g_ad_out, g_high_a, g_high_b, g_query, g_key, g_value, g_proj, g_up, g_down = split
    g_ad_high = jnp.concatenate([g_high_a, g_high_b[: ad_high.shape[0] // devices - share]], axis=0)
    g_qkv = jnp.stack([g_query, g_key, g_value])
    g_ad_out, g_proj, g_down = g_ad_out.T, g_proj.T, g_down.T
    g_cn_up, g_cn_down = g_cn_up.astype(F32), g_cn_down.astype(F32).T
    g_conv = g_conv.reshape(conv_w.shape)
    d_hr_in = (d_branch + d_conv_in) * cell_mask
    small = (g_conv, g_hr_gain, g_ln1, g_ln2)
    flat = jnp.concatenate([g.reshape(-1) for g in small])
    room = -(-flat.size // (devices * 8 * LANES)) * (devices * 8 * LANES)
    flat = jnp.pad(flat, (0, room - flat.size)).reshape(devices, -1, LANES)
    flat = sum_everywhere(flat, devices, shards, 4).reshape(-1)
    parts, at = [], 0
    for g in small:
        parts.append(flat[at : at + g.size].reshape(g.shape))
        at += g.size
    g_conv, g_hr_gain, g_ln1, g_ln2 = parts
    return (
        low_out,
        hr_out,
        d_low_in,
        d_hr_in,
        g_conv,
        g_hr_gain,
        g_cn_up,
        g_cn_down,
        g_ad_gate,
        g_ad_high,
        g_ad_out,
        g_ln1,
        g_qkv,
        g_proj,
        g_ln2,
        g_up,
        g_down,
    )


def solution(mesh):
    return jax.shard_map(
        per_device,
        mesh=mesh,
        in_specs=(
            P("dp", "mp", None, None),
            P("dp", "mp", None),
            P("dp", "mp", None),
            P(),
            P(),
            P(None, "mp"),
            P("mp", None),
            P(None, "mp"),
            P(None, "mp"),
            P("mp", None),
            P(),
            P(None, None, "mp"),
            P("mp", None),
            P(),
            P(None, "mp"),
            P("mp", None),
            P("dp", "mp", None),
            P("dp", "mp", None, None),
        ),
        out_specs=(
            P("dp", "mp", None),
            P("dp", "mp", None, None),
            P("dp", "mp", None),
            P("dp", "mp", None, None),
            P(),
            P(),
            P("dp", "mp"),
            P("mp", "dp"),
            P("dp", "mp"),
            P("dp", "mp"),
            P("mp", "dp"),
            P(),
            P(None, "dp", "mp"),
            P("mp", "dp"),
            P(),
            P("dp", "mp"),
            P("mp", "dp"),
        ),
        check_vma=False,
    )
```

```python
import jax
import jax.numpy as jnp
from jax import lax
from jax.experimental.layout import Layout, with_layout_constraint
from jax.experimental import pallas as pl
from jax.experimental.pallas import tpu as pltpu
from jax.sharding import PartitionSpec as P

HEAD = 64
LANES = 128
EDGE = 8
CHUNKS = 6
TILE = 512
MIB = 1024 * 1024
MESH = pl.DeviceIdType.MESH
BF = jnp.bfloat16
F32 = jnp.float32

def gelu_parts(x):
    c = 0.7978845608028654
    x2 = x * x
    t = jnp.tanh(c * x * (1.0 + 0.044715 * x2))
    half = 0.5 * (1.0 + t)
    slope = half + 0.5 * x * (1.0 - t * t) * (c * (1.0 + 3 * 0.044715 * x2))
    return x * half, slope


def gelu(x):
    c = 0.7978845608028654
    t = jnp.tanh(c * x * (1.0 + 0.044715 * (x * x)))
    return 0.5 * x * (1.0 + t)


def dp_bit(position):
    return lax.rem(lax.axis_index("dp") // 2**position, 2)


def dp_mate(position):
    return lax.axis_index("dp") + 2**position * (1 - 2 * dp_bit(position))


class Halving:
    def __init__(self, bits, lasts, shape, block):
        self.lasts, self.shape, self.block = lasts, shape, block
        left = list(bits)
        self.bits = [left.pop(0 if last else -1) for last in lasts]

    def split(self, count, p):
        if count == 1:
            return (1, 1)
        return (count // 2, 2) if self.lasts[p] else (2, count // 2)

    def buffers(self):
        count, rows, cols = self.shape
        got, held = [], []
        for p in range(len(self.bits)):
            count //= 2
            got.append(jax.ShapeDtypeStruct((count, rows, cols), BF))
            held.append(jax.ShapeDtypeStruct(self.split(count, p + 1) + (rows, cols), BF))
        return got + held

    def semaphores(self):
        return [pltpu.SemaphoreType.DMA((len(self.bits),))] * 2

    def bind(self, first, buffers, send, recv):
        steps = len(self.bits)
        self.now = [first] + list(buffers[steps:])
        self.got, self.send, self.recv = buffers[:steps], send, recv

    def part(self, p, mine):
        bit = dp_bit(self.bits[p])
        index = bit if mine else 1 - bit
        return self.now[p].at[:, index] if self.lasts[p] else self.now[p].at[index]

    def copy(self, p):
        return pltpu.make_async_remote_copy(
            src_ref=self.part(p, False), dst_ref=self.got[p], send_sem=self.send.at[p], recv_sem=self.recv.at[p],
            device_id={"dp": dp_mate(self.bits[p])}, device_id_type=MESH,
        )

    def start(self, p):
        self.copy(p).start()

    def finish(self, p):
        self.copy(p).wait()
        count, rows, cols = self.got[p].shape
        ways = self.split(count, p + 1)

        def add(a, b, out):
            out[...] = (a[...].astype(F32) + b[...].astype(F32)).astype(BF).reshape(out.shape)

        flat = pl.BlockSpec((1, rows, self.block), lambda k, c: (k, 0, c))
        paired = pl.BlockSpec((1, 1, rows, self.block), lambda k, c: (k // ways[1], lax.rem(k, ways[1]), 0, c))
        pltpu.emit_pipeline(add, grid=(count, cols // self.block), in_specs=[flat, flat], out_specs=[paired])(
            self.part(p, True), self.got[p], self.now[p + 1]
        )


def chain_exchange(n, chunks, lag, own_hbm, gathered, partial, travel, compute, result_hbm,
                   sems, prepare, arrived, mates=(), begin=None, turn=None):
    ag_send, ag_recv, rs_send, rs_recv, local_sem = sems
    d = lax.axis_index("mp")
    has_left, has_right = d > 0, d < n - 1

    barrier = pltpu.get_barrier_semaphore()

    @pl.when(has_left)
    def _():
        pl.semaphore_signal(barrier, inc=1, device_id={"mp": d - 1}, device_id_type=MESH)

    @pl.when(has_right)
    def _():
        pl.semaphore_signal(barrier, inc=1, device_id={"mp": d + 1}, device_id_type=MESH)

    for mate in mates:
        pl.semaphore_signal(barrier, inc=1, device_id={"dp": mate}, device_id_type=MESH)

    load = pltpu.make_async_copy(own_hbm, gathered.at[d], local_sem)
    load.start()

    pl.semaphore_wait(barrier, has_left.astype(jnp.int32) + has_right.astype(jnp.int32) + len(mates))
    if begin is not None:
        begin()
    load.wait()

    def ag(way, s, j):
        return pltpu.make_async_remote_copy(
            src_ref=gathered.at[s, j], dst_ref=gathered.at[s, j],
            send_sem=ag_send.at[way, s, j], recv_sem=ag_recv.at[s, j],
            device_id={"mp": d + 1 - 2 * way}, device_id_type=MESH)

    def rs(way, s, j):
        there = d + 1 - 2 * way
        slot = jnp.where((s == there) & (way == 0), n, s)
        return pltpu.make_async_remote_copy(
            src_ref=travel.at[s, j], dst_ref=travel.at[slot, j],
            send_sem=rs_send.at[s, j], recv_sem=rs_recv.at[slot, j],
            device_id={"mp": there}, device_id_type=MESH)

    def rs_wait(slot, j):
        pltpu.make_async_copy(travel.at[slot, j], travel.at[slot, j], rs_recv.at[slot, j]).wait()

    def first(j, _):
        @pl.when(has_right)
        def _():
            ag(0, d, j).start()

        @pl.when(has_left)
        def _():
            ag(1, d, j).start()
        return 0
    lax.fori_loop(0, chunks, first, 0)

    def step(g, _):
        k, j = g // chunks, lax.rem(g, chunks)
        if turn is not None:
            turn(g)

        @pl.when(g < n * chunks)
        def _():
            def side(way, _):
                s = d - k + 2 * k * way
                ok = (s >= 0) & (s < n) & ((k > 0) | (way == 0))

                @pl.when(ok)
                def _():
                    prepare(s, j)

                    @pl.when(k > 0)
                    def _():
                        pltpu.make_async_copy(gathered.at[s, j], gathered.at[s, j], ag_recv.at[s, j]).wait()

                        @pl.when((way == 0) & has_right)
                        def _():
                            ag(0, s, j).start()

                        @pl.when((way == 1) & has_left)
                        def _():
                            ag(1, s, j).start()
                    arrived(s, j)
                    compute(s, j)
                return 0
            lax.fori_loop(0, 2, side, 0)

        q = g - (n - 1 - d) * lag
        ql = jnp.clip(q, 0, n * chunks - 1)
        s, jj = n - 1 - ql // chunks, lax.rem(ql, chunks)

        @pl.when((q >= 0) & (q < n * chunks) & (s <= d) & (has_right | (s < d)))
        def _():
            @pl.when(has_right)
            def _():
                rs_wait(s, jj)

                @pl.when(s < d)
                def _():
                    travel[s, jj] = (partial[s, jj].astype(F32) + travel[s, jj].astype(F32)).astype(BF)

                @pl.when(s == d)
                def _():
                    partial[s, jj] = (partial[s, jj].astype(F32) + travel[s, jj].astype(F32)).astype(partial.dtype)

            @pl.when(d == n - 1)
            def _():
                travel[s, jj] = partial[s, jj].astype(BF)

            @pl.when(s < d)
            def _():
                rs(1, s, jj).start()

        q2 = g - d * lag
        qr = jnp.clip(q2, 0, n * chunks - 1)
        s2, j2 = qr // chunks, lax.rem(qr, chunks)

        @pl.when((q2 >= 0) & (q2 < n * chunks) & (s2 >= d) & (has_left | (s2 > d)))
        def _():
            @pl.when(has_left)
            def _():
                slot = jnp.where(s2 == d, n, s2)
                rs_wait(slot, j2)

                @pl.when(s2 > d)
                def _():
                    travel[s2, j2] = (partial[s2, j2].astype(F32) + travel[s2, j2].astype(F32)).astype(BF)

                @pl.when(s2 == d)
                def _():
                    partial[s2, j2] = (partial[s2, j2].astype(F32) + travel[n, j2].astype(F32)).astype(partial.dtype)

            @pl.when(d == 0)
            def _():
                travel[s2, j2] = partial[s2, j2].astype(BF)

            @pl.when(s2 > d)
            def _():
                rs(0, s2, j2).start()
        return 0

    lax.fori_loop(0, n * chunks + (n - 1) * lag, step, 0)

    store = pltpu.make_async_copy(partial.at[d], result_hbm, local_sem)
    store.start()

    def drain(i, _):
        s, j = i // chunks, lax.rem(i, chunks)

        @pl.when(has_right & (s <= d))
        def _():
            ag(0, s, j).wait_send()

        @pl.when(has_left & (s >= d))
        def _():
            ag(1, s, j).wait_send()

        @pl.when(s < d)
        def _():
            rs(1, s, j).wait_send()

        @pl.when(s > d)
        def _():
            rs(0, s, j).wait_send()
        return 0
    lax.fori_loop(0, n * chunks, drain, 0)
    store.wait()


def chain_sems(n, chunks):
    dma = pltpu.SemaphoreType.DMA
    return [dma((2, n, chunks)), dma((n, chunks)), dma((n, chunks)), dma((n + 1, chunks)), dma]


def chunk_buffers(n, rows, c, kept):
    return [
        pltpu.VMEM((n, CHUNKS, rows, c), BF),
        pltpu.VMEM((n, CHUNKS, rows, c), kept),
        pltpu.VMEM((n + 1, CHUNKS, rows, c), BF),
    ]


def columns(i):
    return pl.ds(pl.multiple_of(i * TILE, TILE), TILE)


def drain_copies(n, copy):
    def one(i, _):
        copy(i // CHUNKS, lax.rem(i, CHUNKS)).wait()
        return 0

    lax.fori_loop(0, n * CHUNKS, one, 0)


def big_forward(x, w_up, w_down, n):
    t, c = x.shape
    h = w_up.shape[1]
    rows = t // CHUNKS

    def kernel(
        x_ref, wu, wd, out, x_all, act_all, slope_all,
        gathered, partial, travel, act, slope, copied, stored, *sems
    ):
        def x_copy(s, j):
            return pltpu.make_async_copy(gathered.at[s, j], x_all.at[s, j], copied.at[s, j])

        def prepare(s, j):
            pass

        def arrived(s, j):
            x_copy(s, j).start()

        def compute(s, j):
            block = gathered.at[s, j]

            def up(i, _):
                pre = jnp.dot(block[...], wu[:, columns(i)], preferred_element_type=F32)
                value, rate = gelu_parts(pre)
                act[:, columns(i)] = value.astype(BF)
                slope[:, columns(i)] = rate.astype(BF)
                return 0

            lax.fori_loop(0, h // TILE, up, 0)
            keep_act = pltpu.make_async_copy(act, act_all.at[s, j], stored.at[0])
            keep_slope = pltpu.make_async_copy(slope, slope_all.at[s, j], stored.at[1])
            keep_act.start()
            keep_slope.start()

            def down(i, _):
                partial[s, j, :, columns(i)] = jnp.dot(
                    act[...], wd[:, columns(i)], preferred_element_type=F32
                )
                return 0

            lax.fori_loop(0, c // TILE, down, 0)
            keep_act.wait()
            keep_slope.wait()

        chain_exchange(
            n, CHUNKS, 1, x_ref, gathered, partial, travel, compute, out, sems, prepare, arrived
        )
        drain_copies(n, x_copy)

    whole = pl.BlockSpec(memory_space=pl.ANY)
    local = pl.BlockSpec(memory_space=pltpu.VMEM)
    out, x_all, act_all, slope_all = pl.pallas_call(
        kernel,
        out_shape=(
            jax.ShapeDtypeStruct((CHUNKS, rows, c), F32),
            jax.ShapeDtypeStruct((n, CHUNKS, rows, c), BF),
            jax.ShapeDtypeStruct((n, CHUNKS, rows, h), BF),
            jax.ShapeDtypeStruct((n, CHUNKS, rows, h), BF),
        ),
        in_specs=[whole, local, local],
        out_specs=(whole,) * 4,
        scratch_shapes=chunk_buffers(n, rows, c, F32)
        + [pltpu.VMEM((rows, h), BF)] * 2
        + [pltpu.SemaphoreType.DMA((n, CHUNKS)), pltpu.SemaphoreType.DMA((2,))]
        + chain_sems(n, CHUNKS),
        compiler_params=pltpu.CompilerParams(
            collective_id=0, has_side_effects=True, vmem_limit_bytes=60 * MIB
        ),
        cost_estimate=pl.CostEstimate(
            flops=4 * n * t * c * h, bytes_accessed=8 * n * t * c, transcendentals=n * t * h
        ),
    )(x.reshape(CHUNKS, rows, c), w_up, w_down)
    return (
        out.reshape(t, c),
        x_all.reshape(n * t, c),
        act_all.reshape(n * t, h),
        slope_all.reshape(n * t, h),
    )


def big_backward(d, slope_all, w_up, w_down, grads, n, devices):
    t, c = d.shape
    h = w_up.shape[1]
    rows = t // CHUNKS
    pairs, g_rows, g_cols = grads.shape
    bits = range(1, devices.bit_length() - 1)
    split = g_rows // 2
    steps = len(bits)
    plans = [Halving(bits, [last] * steps, (pairs, split, g_cols), min(g_cols, 2048)) for last in (True, False)]
    extras = [b for plan in plans for b in plan.buffers()[:-1]]
    each = 2 * steps - 1

    def kernel(d_ref, slopes, wu, wd, g_first, g_second, out, d_all, h_all, *rest):
        sums, extra, rest = rest[0], rest[1 : 1 + 2 * each], rest[1 + 2 * each :]
        gathered, partial, travel, slope, grad, copied, stored, send0, recv0, send1, recv1 = rest[:11]
        sems = rest[11:]
        plans[0].bind(g_first.at[:, :, pl.ds(0, split)], extra[:each] + (sums.at[0],), send0, recv0)
        plans[1].bind(g_second.at[:, :, pl.ds(split, split)], extra[each:] + (sums.at[1],), send1, recv1)

        def begin():
            for plan in plans:
                plan.start(0)

        def pass_on(p):
            for plan in plans:
                plan.finish(p)
            if p + 1 < steps:
                for plan in plans:
                    plan.start(p + 1)

        total = n * CHUNKS + n - 1
        due = [total * (2 ** steps - 2 ** (steps - 1 - p)) * 8 // (10 * (2 ** steps - 1)) for p in range(steps)]

        def turn(g):
            for p in range(steps - 1):
                pl.when(g == due[p])(lambda p=p: pass_on(p))

        def d_copy(s, j):
            return pltpu.make_async_copy(gathered.at[s, j], d_all.at[s, j], copied.at[s, j])

        def slope_copy(s, j):
            return pltpu.make_async_copy(slopes.at[s, j], slope, stored.at[0])

        def prepare(s, j):
            slope_copy(s, j).start()

        def arrived(s, j):
            d_copy(s, j).start()

        def compute(s, j):
            block = gathered.at[s, j]
            slope_copy(s, j).wait()

            def up(i, _):
                back = lax.dot_general(
                    block[...], wd[columns(i), :], (((1,), (1,)), ((), ())), preferred_element_type=F32
                )
                grad[:, columns(i)] = (back * slope[:, columns(i)].astype(F32)).astype(BF)
                return 0

            lax.fori_loop(0, h // TILE, up, 0)
            keep = pltpu.make_async_copy(grad, h_all.at[s, j], stored.at[1])
            keep.start()

            def down(i, _):
                partial[s, j, :, columns(i)] = lax.dot_general(
                    grad[...], wu[columns(i), :], (((1,), (1,)), ((), ())), preferred_element_type=F32
                )
                return 0

            lax.fori_loop(0, c // TILE, down, 0)
            keep.wait()

        chain_exchange(
            n, CHUNKS, 1, d_ref, gathered, partial, travel, compute, out, sems, prepare, arrived,
            [dp_mate(b) for b in bits], begin, turn
        )
        pass_on(steps - 1)
        drain_copies(n, d_copy)

    whole = pl.BlockSpec(memory_space=pl.ANY)
    local = pl.BlockSpec(memory_space=pltpu.VMEM)
    out, d_all, h_all, sums, *_ = pl.pallas_call(
        kernel,
        out_shape=(
            jax.ShapeDtypeStruct((CHUNKS, rows, c), F32),
            jax.ShapeDtypeStruct((n, CHUNKS, rows, c), BF),
            jax.ShapeDtypeStruct((n, CHUNKS, rows, h), BF),
            jax.ShapeDtypeStruct((2, 1, 1, split, g_cols), BF),
            *extras,
        ),
        in_specs=[whole, whole, local, local, whole, whole],
        out_specs=(whole,) * (4 + 2 * each),
        scratch_shapes=chunk_buffers(n, rows, c, F32)
        + [pltpu.VMEM((rows, h), BF)] * 2
        + [pltpu.SemaphoreType.DMA((n, CHUNKS)), pltpu.SemaphoreType.DMA((2,))]
        + plans[0].semaphores() + plans[1].semaphores()
        + chain_sems(n, CHUNKS),
        compiler_params=pltpu.CompilerParams(
            collective_id=1, has_side_effects=True, vmem_limit_bytes=60 * MIB
        ),
        cost_estimate=pl.CostEstimate(
            flops=4 * n * t * c * h, bytes_accessed=8 * n * t * c, transcendentals=0
        ),
    )(
        d.reshape(CHUNKS, rows, c), slope_all.reshape(n, CHUNKS, rows, h), w_up, w_down,
        grads.reshape(pairs // 2, 2, g_rows, g_cols), grads.reshape(2, pairs // 2, g_rows, g_cols),
    )
    return out.reshape(t, c), d_all.reshape(n * t, c), h_all.reshape(n * t, h), sums.reshape(g_rows, g_cols)


def frame(dst, src):
    rows, cols, _ = src.shape
    dst[:, :EDGE] = jnp.zeros((rows, EDGE, LANES), F32)
    dst[:, EDGE + cols:] = jnp.zeros((rows, EDGE, LANES), F32)
    dst[:, EDGE:EDGE + cols] = src[...].astype(F32)


def correlate(out, framed, taps, size, flip, group, first=0, last=None, every=1):
    rows, cols, _ = out.shape
    reach = size // 2
    def some(k, _):
        r = first + k * every
        acc = jnp.zeros((group, cols, LANES), F32)
        for a in range(size):
            for b in range(size):
                tap = (size - 1 - a) * size + size - 1 - b if flip else a * size + b
                acc = acc + framed[pl.ds(r * group + a, group), pl.ds(EDGE - reach + b, cols), :] * taps[tap]
        out[pl.ds(r * group, group)] = acc
        return 0
    lax.fori_loop(0, (rows // group if last is None else last) - first if every == 1 else 2, some, 0)


def conv_forward(x, w, size, n):
    rows, cols, c = x.shape
    reach = size // 2

    def kernel(x_ref, w_ref, out, bordered, framed, sent, got, own):
        d = lax.axis_index("mp")
        has_up, has_down = d > 0, d < n - 1
        barrier = pltpu.get_barrier_semaphore()

        @pl.when(has_up)
        def _():
            pl.semaphore_signal(barrier, inc=1, device_id={"mp": d - 1}, device_id_type=MESH)

        @pl.when(has_down)
        def _():
            pl.semaphore_signal(barrier, inc=1, device_id={"mp": d + 1}, device_id_type=MESH)

        keep = pltpu.make_async_copy(x_ref, bordered.at[pl.ds(reach, rows)], own)
        keep.start()
        pl.semaphore_wait(barrier, has_up.astype(jnp.int32) + has_down.astype(jnp.int32))
        up = pltpu.make_async_remote_copy(
            src_ref=x_ref.at[pl.ds(0, reach)], dst_ref=bordered.at[pl.ds(reach + rows, reach)],
            send_sem=sent.at[0], recv_sem=got.at[0], device_id={"mp": d - 1}, device_id_type=MESH,
        )
        down = pltpu.make_async_remote_copy(
            src_ref=x_ref.at[pl.ds(rows - reach, reach)], dst_ref=bordered.at[pl.ds(0, reach)],
            send_sem=sent.at[1], recv_sem=got.at[1], device_id={"mp": d + 1}, device_id_type=MESH,
        )
        nothing = jnp.zeros((reach, cols, c), BF)

        @pl.when(has_up)
        def _():
            up.start()

        @pl.when(has_down)
        def _():
            down.start()

        @pl.when(d == 0)
        def _():
            bordered[:reach] = nothing

        @pl.when(d == n - 1)
        def _():
            bordered[reach + rows :] = nothing

        groups = rows // reach

        def inner(i, _):
            lanes = pl.ds(pl.multiple_of(i * LANES, LANES), LANES)
            frame(framed.at[pl.ds(reach, rows)], x_ref.at[:, :, lanes])
            correlate(out.at[:, :, lanes], framed, w_ref.at[:, :, lanes], size, False, reach, 1, groups - 1)
            return 0

        lax.fori_loop(0, c // LANES, inner, 0)
        keep.wait()

        @pl.when(has_up)
        def _():
            down.wait_recv()

        @pl.when(has_down)
        def _():
            up.wait_recv()

        def block(i, _):
            lanes = pl.ds(pl.multiple_of(i * LANES, LANES), LANES)
            frame(framed, bordered.at[:, :, lanes])
            correlate(out.at[:, :, lanes], framed, w_ref.at[:, :, lanes], size, False, reach, 0, None, groups - 1)
            return 0

        lax.fori_loop(0, c // LANES, block, 0)

        @pl.when(has_up)
        def _():
            up.wait_send()

        @pl.when(has_down)
        def _():
            down.wait_send()

    local = pl.BlockSpec(memory_space=pltpu.VMEM)
    dma = pltpu.SemaphoreType.DMA
    return pl.pallas_call(
        kernel,
        out_shape=(
            jax.ShapeDtypeStruct((rows, cols, c), F32),
            jax.ShapeDtypeStruct((rows + 2 * reach, cols, c), BF),
        ),
        in_specs=[local, local],
        out_specs=(local, local),
        scratch_shapes=[pltpu.VMEM((rows + 2 * reach, cols + 2 * EDGE, LANES), F32), dma((2,)), dma((2,)), dma],
        compiler_params=pltpu.CompilerParams(
            collective_id=5, has_side_effects=True, vmem_limit_bytes=40 * MIB
        ),
    )(x, w)


def conv_backward(d, x, w, size, grads, devices, group=4, bgroup=4):
    high, cols, c = x.shape
    rows = high - size + 1
    reach = size // 2
    steps = devices.bit_length() - 1
    shape = grads[0].shape
    plans = [Halving(range(steps), [True] + [last] * (steps - 1), shape, shape[2]) for last in (True, False)]
    blocks = c // LANES
    due = [3 + (blocks - 4) * p // max(steps - 2, 1) for p in range(steps)]

    def kernel(d_ref, x_ref, w_ref, g0, g1, out, g, *rest):
        extra, rest = rest[: 4 * steps], rest[4 * steps :]
        dframed, xframed, *sems = rest
        plans[0].bind(g0, extra[: 2 * steps], sems[0], sems[1])
        plans[1].bind(g1, extra[2 * steps :], sems[2], sems[3])
        i = pl.program_id(0)

        @pl.when(i == 0)
        def _():
            barrier = pltpu.get_barrier_semaphore()
            for b in range(steps):
                pl.semaphore_signal(barrier, inc=1, device_id={"dp": dp_mate(b)}, device_id_type=MESH)
            pl.semaphore_wait(barrier, steps)
            for plan in plans:
                plan.start(0)

        for p in range(steps - 1):
            @pl.when(i == due[p])
            def _():
                for plan in plans:
                    plan.finish(p)
                for plan in plans:
                    plan.start(p + 1)

        frame(dframed, d_ref)
        frame(xframed, x_ref)
        correlate(out, dframed, w_ref, size, True, group)
        for a in range(size):
            def some(r, accs):
                dv = dframed[pl.ds(reach + r * bgroup, bgroup), EDGE : EDGE + cols]
                new = []
                for b in range(size):
                    prod = dv * xframed[pl.ds(r * bgroup + a, bgroup), pl.ds(EDGE - reach + b, cols), :]
                    new.append(accs[b] + jnp.sum(prod.reshape(-1, 8, LANES), axis=0))
                return tuple(new)

            accs = lax.fori_loop(
                0, rows // bgroup, some, tuple(jnp.zeros((8, LANES), F32) for _ in range(size))
            )
            for b in range(size):
                g[a * size + b] = jnp.sum(accs[b], axis=0, keepdims=True)

        @pl.when(i == blocks - 1)
        def _():
            for plan in plans:
                plan.finish(steps - 1)

    whole = pl.BlockSpec(memory_space=pl.ANY)
    d_in, g, *extra = pl.pallas_call(
        kernel,
        grid=(blocks,),
        out_shape=(
            jax.ShapeDtypeStruct((rows, cols, c), F32),
            jax.ShapeDtypeStruct((size * size, 1, c), F32),
            *plans[0].buffers(),
            *plans[1].buffers(),
        ),
        in_specs=[pl.BlockSpec((high, cols, LANES), lambda i: (0, 0, i))] * 2
        + [pl.BlockSpec((size * size, 1, LANES), lambda i: (0, 0, i)), whole, whole],
        out_specs=(
            pl.BlockSpec((rows, cols, LANES), lambda i: (0, 0, i)),
            pl.BlockSpec((size * size, 1, LANES), lambda i: (0, 0, i)),
        )
        + (whole,) * (4 * steps),
        scratch_shapes=[pltpu.VMEM((high, cols + 2 * EDGE, LANES), F32)] * 2
        + plans[0].semaphores() + plans[1].semaphores(),
        compiler_params=pltpu.CompilerParams(
            collective_id=3, has_side_effects=True, vmem_limit_bytes=40 * MIB
        ),
        cost_estimate=pl.CostEstimate(flops=6 * 10**10, bytes_accessed=10**8, transcendentals=0),
    )(
        d, x, w, grads[0].reshape((shape[0] // 2, 2) + shape[1:]), grads[1].reshape((shape[0] // 2, 2) + shape[1:])
    )
    return d_in, g, [extra[2 * steps - 1].reshape(shape[1:]), extra[4 * steps - 1].reshape(shape[1:])]


GATE, OUT, HIGH_A, HIGH_B, QUERY, KEY, VALUE, PROJ = range(8)
L_LOW, L_DF, L_POOL_A, L_POOL_B, L_FIRST, L_DA, L_SECOND, L_COT = range(8)
R_DGATE, R_MERGE, R_DHIGH, R_DQ, R_DK, R_DV, R_ATT, R_DUP, R_ACT = range(9)


def nn(a, b):
    return jnp.dot(a, b, preferred_element_type=F32)


def nt(a, b):
    return lax.dot_general(a, b, (((1,), (1,)), ((), ())), preferred_element_type=F32)


def tn(a, b):
    return lax.dot_general(a, b, (((0,), (0,)), ((), ())), preferred_element_type=F32)


def normalise(x, gain):
    centred = x - jnp.mean(x, -1, keepdims=True)
    rate = lax.rsqrt(jnp.mean(centred * centred, -1, keepdims=True) + 1e-06)
    return centred * rate * gain


def normalise_back(x, gain, d):
    centred = x - jnp.mean(x, -1, keepdims=True)
    rate = lax.rsqrt(jnp.mean(centred * centred, -1, keepdims=True) + 1e-06)
    hat = centred * rate
    dg = d * gain
    back = rate * (dg - jnp.mean(dg, -1, keepdims=True) - hat * jnp.mean(dg * hat, -1, keepdims=True))
    return back, jnp.sum(d * hat, axis=0, keepdims=True)


def low_stage(low, pool_a, pool_b, cot, gain1, gain2, packed, n, devices, cid):
    t, dim = low.shape
    every = n * t
    width = dim // n
    heads = width // HEAD
    pairs = devices // 2
    rows = dim // devices
    half = dim // 2
    ff = 4 * dim
    scale = HEAD ** (-0.5)

    def kernel(
        low_ref, pool_a_ref, pool_b_ref, cot_ref, gain1_ref, gain2_ref, w_hbm,
        low_out, d_low, d_pool_a, d_pool_b, g_ln1, g_ln2, grads,
        wv, lhs, lhs2, rhs, gate, high, merged, resid, d_res, slope, mixed, heads_in, att_all, d_att, d_mixed,
        d_heads, probs, d_scores, stage, w_sem, q_send, q_got, a_send, a_got, b_send, b_got, c_send, c_got, own_sem,
        l_send, l_got, r_send, r_got, stage_sem,
    ):
        d = lax.axis_index("mp")
        dp = lax.axis_index("dp")
        core = lax.rem(dp, 2)
        mate = dp + 1 - 2 * core
        barrier = pltpu.get_barrier_semaphore()
        for k in range(1, n):
            pl.semaphore_signal(barrier, inc=1, device_id={"mp": lax.rem(d + k, n)}, device_id_type=MESH)
        pl.semaphore_signal(barrier, inc=1, device_id={"dp": mate}, device_id_type=MESH)

        def w_copy(w, k):
            c, z = k // n, lax.rem(k, n)
            wide, base, at = w_place(w)
            src = w_hbm.at[:, c, z, :, pl.ds(base, wide)]
            dst = wv.at[c, :, :, pl.ds(pl.multiple_of(at + z * wide, wide), wide)]
            return pltpu.make_async_copy(src, dst, w_sem.at[w, k])

        def w_place(w):
            if w < 8:
                return width, w * width, w * dim
            return ff // n, 8 * width + (w - 8) * ff // n, 8 * dim + (w - 8) * ff

        def w_each(w, act):
            def one(k, _):
                act(w_copy(w, k))
                return 0

            lax.fori_loop(0, 2 * n, one, 0)

        for w in range(10):
            w_each(w, lambda copy: copy.start())

        def w_wait(*which):
            for w in which:
                w_each(w, lambda copy: copy.wait())

        def w_cols(at, size):
            return wv[:, :, :, pl.ds(at, size)].reshape(dim, size)

        def forward(x, first, count, put):
            def one(i, _):
                put(pl.multiple_of(i * TILE, TILE), nn(x, w_cols(pl.multiple_of(first * dim + i * TILE, TILE), TILE)))
                return 0
            lax.fori_loop(0, count * dim // TILE, one, 0)

        def backward(get, first, count, dst, fresh):
            def one(i, _):
                for c in range(2):
                    part = wv[c, :, :, pl.ds(pl.multiple_of((first + i) * dim, dim), dim)].reshape(half, dim)
                    y = nt(get(pl.multiple_of(i * dim, dim)), part)
                    cols = slice(c * half, (c + 1) * half)
                    if fresh and count == 1:
                        dst[:, cols] = y
                    else:
                        dst[:, cols] += y
                return 0
            if fresh and count > 1:
                dst[...] = jnp.zeros(dst.shape, F32)
            if count == 1:
                one(0, 0)
            else:
                lax.fori_loop(0, count, one, 0)

        def r_cols(block, count=1):
            return pl.ds(block * dim, count * dim)

        def r_at(block):
            return block * dim if block <= R_DUP else block * dim + 3 * dim

        def r_copy(block):
            cols = pl.ds(r_at(block), dim if block < R_DUP else ff)
            return pltpu.make_async_remote_copy(
                src_ref=rhs.at[0, :, cols], dst_ref=rhs.at[1, :, cols], send_sem=r_send.at[block],
                recv_sem=r_got.at[block], device_id={"dp": mate}, device_id_type=MESH)

        def l_copy(i):
            return pltpu.make_async_remote_copy(
                src_ref=lhs.at[i, :, pl.ds(pl.multiple_of((1 - core) * half, half), half)], dst_ref=lhs2.at[i],
                send_sem=l_send.at[i], recv_sem=l_got.at[i], device_id={"dp": mate}, device_id_type=MESH)

        stored = []

        def grad(i, block, at, count, shared=False):
            if not shared:
                r_copy(block).wait_recv()
            own_l = pl.ds(pl.multiple_of(core * half, half), half)

            wide, base, first = w_place(at if at < 8 else 8 + (at - 8) * dim // ff)
            piece = min(TILE, wide)

            def out_copies(slot, k):
                out = []
                for q in range(TILE // piece):
                    z, col = divmod(at * dim - first + k * TILE + q * piece, wide)
                    out.append(
                        pltpu.make_async_copy(
                            stage.at[slot, :, :, pl.ds(q * piece, piece)],
                            grads.at[:, pl.ds(z * rows, rows), pl.ds(base + col, piece)],
                            stage_sem.at[slot, q],
                        )
                    )
                return out

            for k in range(count * dim // TILE):
                slot = len(stored) % 2
                if len(stored) >= 2:
                    wait(stored[-2])
                cols = pl.ds(r_at(block) + k * TILE, TILE)
                y = tn(lhs[i, :, own_l], rhs[0, :, cols]) + tn(lhs2[i], rhs[1, :, cols])
                stage[slot] = y.astype(BF).reshape(pairs, rows, TILE)
                stored.append(out_copies(slot, k))
                start(stored[-1])

        def to_heads(k, src, dst, send, got):
            out = []
            for step in range(1, n):
                peer = lax.rem(d + step, n)
                out.append(pltpu.make_async_remote_copy(
                    src_ref=src.at[:, pl.ds(pl.multiple_of(peer * width, width), width)],
                    dst_ref=dst.at[pl.ds(pl.multiple_of(d * t, t), t)],
                    send_sem=send.at[k, step], recv_sem=got.at[k, step], device_id={"mp": peer}, device_id_type=MESH))
            out.append(pltpu.make_async_copy(
                src.at[:, pl.ds(pl.multiple_of(d * width, width), width)], dst.at[pl.ds(pl.multiple_of(d * t, t), t)], own_sem.at[k]))
            return out

        def to_tokens(k, src, dst, send, got):
            out = []
            for step in range(1, n):
                peer = lax.rem(d + step, n)
                out.append(pltpu.make_async_remote_copy(
                    src_ref=src.at[pl.ds(pl.multiple_of(peer * t, t), t)],
                    dst_ref=dst.at[:, pl.ds(pl.multiple_of(d * width, width), width)],
                    send_sem=send.at[k, step], recv_sem=got.at[k, step], device_id={"mp": peer}, device_id_type=MESH))
            out.append(pltpu.make_async_copy(
                src.at[pl.ds(pl.multiple_of(d * t, t), t)], dst.at[:, pl.ds(pl.multiple_of(d * width, width), width)], own_sem.at[k]))
            return out

        def start(copies):
            for c in copies:
                c.start()

        def wait(copies):
            for c in copies:
                c.wait()

        lhs[L_LOW] = low_ref[...]
        lhs[L_POOL_A] = pool_a_ref[...]
        lhs[L_POOL_B] = pool_b_ref[...]
        lhs[L_COT] = cot_ref[...]
        acc = d_low
        w_wait(GATE)

        def put_gate(at, y):
            gate[:, pl.ds(at, TILE)] = 1.0 / (1.0 + jnp.exp(-y))
        forward(lhs[L_LOW], GATE, 1, put_gate)
        w_wait(HIGH_A, HIGH_B, OUT)

        def put_high(at, y):
            high[:, pl.ds(at, TILE)] = y
        forward(lhs[L_POOL_A], HIGH_A, 1, put_high)

        def put_merging(at, y):
            cols = pl.ds(at, TILE)
            total = high[:, cols] + y
            high[:, cols] = total
            rhs[0, :, pl.ds(R_MERGE * dim + at, TILE)] = (total * gate[:, cols]).astype(BF)
        forward(lhs[L_POOL_B], HIGH_B, 1, put_merging)
        backward(lambda at: rhs[0, :, r_cols(R_MERGE)], OUT, 1, merged, True)
        merged[...] += lhs[L_LOW].astype(F32)
        lhs[L_FIRST] = normalise(merged[...], gain1_ref[...]).astype(BF)

        w_wait(QUERY, KEY, VALUE, PROJ)
        pl.semaphore_wait(barrier, n)
        for i in (L_LOW, L_POOL_A, L_POOL_B, L_COT, L_FIRST):
            l_copy(i).start()
        r_copy(R_MERGE).start()
        out_q = []
        for k in range(3):
            def put_mixed(at, y):
                mixed[k, :, pl.ds(at, TILE)] = y.astype(BF)
            forward(lhs[L_FIRST], QUERY + k, 1, put_mixed)
            copies = to_heads(k, mixed.at[k], heads_in.at[k], q_send, q_got)
            start(copies)
            out_q += copies
        wait(out_q)

        for h in range(heads):
            lanes = slice(h * HEAD, (h + 1) * HEAD)

            def rows_of(b, _):
                some = pl.ds(pl.multiple_of(b * t, t), t)
                s = nt(heads_in[0, some, lanes], heads_in[1, :, lanes]) * scale
                e = jnp.exp(s - jnp.max(s, -1, keepdims=True))
                p = (e * (1.0 / jnp.sum(e, -1, keepdims=True))).astype(BF)
                probs[h, some] = p
                att_all[some, lanes] = nn(p, heads_in[2, :, lanes]).astype(BF)
                return 0
            lax.fori_loop(0, n, rows_of, 0)
        out_a = to_tokens(0, att_all, rhs.at[0, :, r_cols(R_ATT)], a_send, a_got)
        start(out_a)
        wait(out_a)
        r_copy(R_ATT).start()
        backward(lambda at: rhs[0, :, r_cols(R_ATT)], PROJ, 1, resid, True)
        resid[...] += merged[...]
        lhs[L_SECOND] = normalise(resid[...], gain2_ref[...]).astype(BF)
        l_copy(L_SECOND).start()

        w_wait(8)

        def put_up(at, y):
            value, rate = gelu_parts(y)
            rhs[0, :, pl.ds(r_at(R_ACT) + at, TILE)] = value.astype(BF)
            slope[:, pl.ds(at, TILE)] = rate.astype(BF)
        forward(lhs[L_SECOND], 8, 4, put_up)
        r_copy(R_ACT).start()
        w_wait(9)
        backward(lambda at: rhs[0, :, pl.ds(r_at(R_ACT) + at, dim)], 12, 4, acc, True)
        low_out[...] = resid[...] + acc[...]

        def put_d_up(at, y):
            rhs[0, :, pl.ds(r_at(R_DUP) + at, TILE)] = (y * slope[:, pl.ds(at, TILE)].astype(F32)).astype(BF)
        forward(lhs[L_COT], 12, 4, put_d_up)
        r_copy(R_DUP).start()
        backward(lambda at: rhs[0, :, pl.ds(r_at(R_DUP) + at, dim)], 8, 4, acc, True)
        back, g = normalise_back(resid[...], gain2_ref[...], acc[...])
        g_ln2[...] = g
        d_res[...] = lhs[L_COT].astype(F32) + back
        lhs[L_DA] = d_res[...].astype(BF)
        l_copy(L_DA).start()

        def put_d_att(at, y):
            mixed[0, :, pl.ds(at, TILE)] = y.astype(BF)
        forward(lhs[L_DA], PROJ, 1, put_d_att)
        out_b = to_heads(0, mixed.at[0], d_att, b_send, b_got)
        start(out_b)
        l_copy(L_COT).wait_recv()
        grad(L_COT, R_ACT, 12, 4)
        wait(out_b)
        for h in range(heads):
            lanes = slice(h * HEAD, (h + 1) * HEAD)

            def rows_of(b, _):
                some = pl.ds(pl.multiple_of(b * t, t), t)
                p = probs[h, some].astype(F32)
                dp_ = nt(d_att[some, lanes], heads_in[2, :, lanes])
                ds = (p * (dp_ - jnp.sum(dp_ * p, -1, keepdims=True)) * scale).astype(BF)
                d_scores[some] = ds
                d_heads[0, some, lanes] = nn(ds, heads_in[1, :, lanes]).astype(BF)
                return 0
            lax.fori_loop(0, n, rows_of, 0)
            d_heads[1, :, lanes] = tn(d_scores[...], heads_in[0, :, lanes]).astype(BF)
            d_heads[2, :, lanes] = tn(probs[h], d_att[:, lanes]).astype(BF)
        out_c = []
        for k in range(3):
            copies = to_tokens(k, d_heads.at[k], rhs.at[0, :, r_cols(R_DQ + k)], c_send, c_got)
            start(copies)
            out_c += copies
        l_copy(L_SECOND).wait_recv()
        grad(L_SECOND, R_DUP, 8, 4)
        l_copy(L_DA).wait_recv()
        grad(L_DA, R_ATT, PROJ, 1)
        wait(out_c)
        for k in range(3):
            r_copy(R_DQ + k).start()
        backward(lambda at: rhs[0, :, pl.ds(R_DQ * dim + at, dim)], QUERY, 3, acc, True)
        back, g = normalise_back(merged[...], gain1_ref[...], acc[...])
        g_ln1[...] = g
        d_res[...] += back
        lhs[L_DF] = d_res[...].astype(BF)
        l_copy(L_DF).start()

        def put_d_gate(at, y):
            cols = pl.ds(at, TILE)
            gv = gate[:, cols]
            part = y * gv
            rhs[0, :, pl.ds(R_DHIGH * dim + at, TILE)] = part.astype(BF)
            rhs[0, :, pl.ds(R_DGATE * dim + at, TILE)] = (part * high[:, cols] * (1.0 - gv)).astype(BF)
        forward(lhs[L_DF], OUT, 1, put_d_gate)
        r_copy(R_DHIGH).start()
        r_copy(R_DGATE).start()
        backward(lambda at: rhs[0, :, r_cols(R_DHIGH)], HIGH_A, 1, d_pool_a, True)
        backward(lambda at: rhs[0, :, r_cols(R_DHIGH)], HIGH_B, 1, d_pool_b, True)
        backward(lambda at: rhs[0, :, r_cols(R_DGATE)], GATE, 1, acc, True)
        d_low[...] = d_res[...] + acc[...]
        l_copy(L_FIRST).wait_recv()
        for k in range(3):
            grad(L_FIRST, R_DQ + k, QUERY + k, 1)
        l_copy(L_DF).wait_recv()
        grad(L_DF, R_MERGE, OUT, 1)
        l_copy(L_POOL_A).wait_recv()
        grad(L_POOL_A, R_DHIGH, HIGH_A, 1)
        l_copy(L_POOL_B).wait_recv()
        grad(L_POOL_B, R_DHIGH, HIGH_B, 1, shared=True)
        l_copy(L_LOW).wait_recv()
        grad(L_LOW, R_DGATE, GATE, 1)
        wait(stored[-2])
        wait(stored[-1])
        for i in range(8):
            l_copy(i).wait_send()
        for b in range(9):
            r_copy(b).wait_send()

    whole = pl.BlockSpec(memory_space=pl.ANY)
    local = pl.BlockSpec(memory_space=pltpu.VMEM)
    vm, dma = pltpu.VMEM, pltpu.SemaphoreType.DMA
    tok = jax.ShapeDtypeStruct((t, dim), F32)
    one = jax.ShapeDtypeStruct((1, dim), F32)
    return pl.pallas_call(
        kernel,
        out_shape=(tok, tok, tok, tok, one, one, jax.ShapeDtypeStruct((pairs, n * rows, 16 * width), BF)),
        in_specs=[local] * 6 + [whole],
        out_specs=(local,) * 6 + (whole,),
        scratch_shapes=[
            vm((2, pairs, rows, 16 * dim), BF), vm((8, t, dim), BF), vm((8, t, half), BF), vm((2, t, 15 * dim), BF),
            vm((t, dim), F32), vm((t, dim), F32), vm((t, dim), F32), vm((t, dim), F32), vm((t, dim), F32),
            vm((t, ff), BF), vm((3, t, dim), BF), vm((3, every, width), BF), vm((every, width), BF), vm((every, width), BF),
            vm((1, 8, 128), BF), vm((3, every, width), BF), vm((heads, every, every), BF), vm((every, every), BF),
            vm((2, pairs, rows, TILE), BF),
            dma((10, 2 * n)), dma((3, n)), dma((3, n)), dma((1, n)), dma((1, n)), dma((1, n)), dma((1, n)), dma((3, n)), dma((3, n)),
            dma((3,)), dma((8,)), dma((8,)), dma((9,)), dma((9,)), dma((2, 2)),
        ],
        compiler_params=pltpu.CompilerParams(collective_id=cid, has_side_effects=True, vmem_limit_bytes=61 * MIB),
        cost_estimate=pl.CostEstimate(flops=14 * 10**9, bytes_accessed=70 * 10**6, transcendentals=10**7),
    )(low, pool_a, pool_b, cot, gain1, gain2, packed.reshape(pairs, 2, n, rows, 16 * width))
def sum_everywhere(x, devices, n, cid):
    rows = x.shape[1]

    def kernel(x_ref, out, here, level, send1, recv1, send2, recv2, send3, recv3):
        me, d = lax.axis_index("dp"), lax.axis_index("mp")
        barrier = pltpu.get_barrier_semaphore()

        def greet(k, _):
            pl.semaphore_signal(
                barrier, inc=1, device_id={"dp": lax.rem(me + k, devices)}, device_id_type=MESH
            )
            return 0

        lax.fori_loop(1, devices, greet, 0)
        for k in range(1, n):
            pl.semaphore_signal(barrier, inc=1, device_id={"mp": lax.rem(d + k, n)}, device_id_type=MESH)
        here[me] = x_ref[me]
        pl.semaphore_wait(barrier, devices + n - 2)

        def spread(k):
            peer = lax.rem(me + k, devices)
            return pltpu.make_async_remote_copy(
                src_ref=x_ref.at[peer], dst_ref=here.at[me], send_sem=send1.at[k], recv_sem=recv1.at[k],
                device_id={"dp": peer}, device_id_type=MESH,
            )

        def across(k):
            return pltpu.make_async_remote_copy(
                src_ref=level.at[d], dst_ref=level.at[d], send_sem=send2.at[k], recv_sem=recv2.at[k],
                device_id={"mp": lax.rem(d + k, n)}, device_id_type=MESH,
            )

        def give(k):
            return pltpu.make_async_remote_copy(
                src_ref=out.at[me], dst_ref=out.at[me], send_sem=send3.at[k], recv_sem=recv3.at[k],
                device_id={"dp": lax.rem(me + k, devices)}, device_id_type=MESH,
            )

        def each(count, make, act):
            def one(k, _):
                act(make(k))
                return 0

            lax.fori_loop(1, count, one, 0)

        each(devices, spread, lambda c: c.start())
        each(devices, spread, lambda c: c.wait())
        level[d] = jnp.sum(here[...], axis=0)
        each(n, across, lambda c: c.start())
        each(n, across, lambda c: c.wait())
        out[me] = jnp.sum(level[...], axis=0)
        each(devices, give, lambda c: c.start())
        each(devices, give, lambda c: c.wait())

    vm, dma = pltpu.VMEM, pltpu.SemaphoreType.DMA
    return pl.pallas_call(
        kernel,
        out_shape=jax.ShapeDtypeStruct(x.shape, F32),
        in_specs=[pl.BlockSpec(memory_space=pltpu.VMEM)],
        out_specs=pl.BlockSpec(memory_space=pltpu.VMEM),
        scratch_shapes=[vm(x.shape, F32), vm((n, rows, LANES), F32)] + [dma((devices,)), dma((devices,)), dma((n,)), dma((n,)), dma((devices,)), dma((devices,))],
        compiler_params=pltpu.CompilerParams(
            collective_id=cid, has_side_effects=True, vmem_limit_bytes=16 * MIB
        ),
    )(x)


def rows_first(x):
    return with_layout_constraint(x, Layout(major_to_minor=tuple(range(x.ndim))))


def own_part(w, axis):
    length = w.shape[axis] // lax.axis_size("dp")
    return lax.dynamic_slice_in_dim(w, lax.axis_index("dp") * length, length, axis)


def fold(w, rows):
    return w[:rows], jnp.pad(w[rows:], ((0, 2 * rows - w.shape[0]), (0, 0)))


def core_first(x, devices):
    shape = x.shape
    return x.reshape(shape[:-1] + (devices // 2, 2, -1)).swapaxes(-3, -2).reshape(shape)


def core_last(x, devices):
    shape = x.shape
    return x.reshape(shape[:-1] + (2, devices // 2, -1)).swapaxes(-3, -2).reshape(shape)


def extended(value, sides, width):
    for axis, dim in sides:
        devices, length = (lax.axis_size(axis), value.shape[dim])
        up = [(i, (i + 1) % devices) for i in range(devices - 1)]
        down = [(j, i) for i, j in up]
        last = lax.slice_in_dim(value, length - width, length, axis=dim)
        first = lax.slice_in_dim(value, 0, width, axis=dim)
        before = lax.ppermute(last, axis, up)
        after = lax.ppermute(first, axis, down)
        value = jnp.concatenate([before, value, after], axis=dim)
    return value


def layer_norm(values, gain):
    centre = jnp.mean(values, -1, keepdims=True)
    centred = values - centre
    variance = jnp.mean(centred * centred, -1, keepdims=True)
    return centred * lax.rsqrt(variance + 1e-06) * gain


def per_device(
    hr_in,
    low_in,
    valid,
    conv_w,
    hr_gain,
    cn_up,
    cn_down,
    ad_gate,
    ad_high,
    ad_out,
    ln1_gain,
    w_qkv,
    w_proj,
    ln2_gain,
    w_up,
    w_down,
    cot_low,
    cot_hr,
):
    item_count, row_count, col_count, chan_count = hr_in.shape
    devices, shards = lax.axis_size("dp"), lax.axis_size("mp")
    dims = low_in.shape[2]
    share = dims // devices
    qkv = own_part(w_qkv, 1)
    pieces = [
        own_part(ad_gate, 0), own_part(ad_out, 1).T, *fold(own_part(ad_high, 0), share),
        qkv[0], qkv[1], qkv[2], own_part(w_proj, 1).T, own_part(w_up, 0), own_part(w_down, 1).T,
    ]
    packed = rows_first(jnp.concatenate(pieces, axis=1))
    packed = rows_first(lax.all_gather(packed, "mp", axis=0, tiled=True))
    plane_mask = valid.astype(jnp.float32)
    cell_mask = plane_mask[..., None]
    masked = hr_in * valid.astype(jnp.bfloat16)[..., None]
    size = conv_w.shape[0]
    taps = conv_w.astype(F32).reshape(size * size, 1, chan_count)
    conv_out, bordered = conv_forward(masked[0], taps, size, shards)
    conv_out = conv_out[None]
    conv_out = conv_out * cell_mask
    hr_gainf = hr_gain.astype(jnp.float32)
    normed = layer_norm(conv_out, hr_gainf).astype(jnp.bfloat16)
    normed, packed = lax.optimization_barrier((normed, packed))
    packed = rows_first(lax.all_gather(packed, "dp", axis=0, tiled=True))
    branch, normed_all, hidden_act, hidden_slope = big_forward(
        normed.reshape(row_count * col_count, chan_count), cn_up, cn_down, shards
    )
    branch = branch.reshape(hr_in.shape)
    hr_out = (masked.astype(jnp.float32) + branch) * cell_mask
    half_rows, half_cols = (row_count // 2, col_count // 2)
    block_sum = hr_out.reshape(item_count, half_rows, 2, half_cols, 2, chan_count).sum(axis=(2, 4))
    counts = plane_mask.reshape(item_count, half_rows, 2, half_cols, 2).sum(axis=(2, 4))
    divisor = jnp.maximum(counts, 1.0)[..., None]
    pooled = (
        (block_sum / divisor)
        .astype(jnp.bfloat16)
        .reshape(item_count, half_rows * half_cols, chan_count)
    )
    tokens = half_rows * half_cols
    by_share = pooled[0].reshape(tokens, devices, -1)
    pool_a = by_share[:, :, :share].reshape(tokens, dims)
    pool_b = jnp.pad(by_share[:, :, share:], ((0, 0), (0, 0), (0, 2 * share - by_share.shape[2]))).reshape(tokens, dims)
    low_out, d_low_in, d_pool_a, d_pool_b, g_ln1, g_ln2, low_grads = low_stage(
        *(core_first(v, devices) for v in (low_in[0], pool_a, pool_b, cot_low[0])),
        *(core_first(v.astype(F32), devices)[None] for v in (ln1_gain, ln2_gain)),
        packed, shards, devices, 2,
    )
    low_out = core_last(low_out, devices)[None]
    d_low_in = core_last(d_low_in, devices)[None]
    g_ln1, g_ln2 = core_last(g_ln1[0], devices), core_last(g_ln2[0], devices)
    d_pooled = jnp.concatenate(
        [
            core_last(d_pool_a, devices).reshape(tokens, devices, share),
            core_last(d_pool_b, devices).reshape(tokens, devices, share)[:, :, : by_share.shape[2] - share],
        ],
        axis=2,
    )
    d_block = d_pooled.reshape(item_count, half_rows, half_cols, chan_count) / divisor
    d_block = d_block.reshape(item_count, half_rows, 1, half_cols, 1, chan_count)
    d_map = cot_hr.astype(jnp.float32) + jnp.broadcast_to(
        d_block, (item_count, half_rows, 2, half_cols, 2, chan_count)
    ).reshape(hr_in.shape)
    d_branch = d_map * cell_mask
    d_normed, d_branch_all, d_hidden, low_sums = big_backward(
        d_branch.astype(BF).reshape(row_count * col_count, chan_count),
        hidden_slope, cn_up, cn_down, low_grads, shards, devices,
    )
    d_normed = d_normed.reshape(hr_in.shape)
    low_sums = rows_first(low_sums.reshape(shards, share, -1))
    low_sums = rows_first(lax.psum_scatter(low_sums, "mp", scatter_dimension=0))
    g_cn_down = jnp.einsum("tc,th->ch", d_branch_all, hidden_act, preferred_element_type=F32).astype(BF)
    g_cn_up = jnp.einsum("tc,th->ch", normed_all, d_hidden, preferred_element_type=F32).astype(BF)
    cn_grads = [g.reshape(devices, chan_count // devices, -1) for g in (g_cn_up, g_cn_down)]
    d_conv, g_hr_gain = jax.vjp(layer_norm, conv_out, hr_gainf)[1](d_normed)
    d_conv = d_conv * cell_mask
    d_bordered = extended(d_conv.astype(BF), (("mp", 1),), 3)
    d_conv_in, g_conv, (g_cn_up, g_cn_down) = conv_backward(
        d_bordered[0], bordered, taps, size, cn_grads, devices
    )
    g_cn_up, g_cn_down = g_cn_up.astype(F32), g_cn_down.astype(F32).T
    g_conv = g_conv.reshape(conv_w.shape)
    d_hr_in = (d_branch + d_conv_in) * cell_mask
    small = (g_conv, g_hr_gain, g_ln1, g_ln2)
    flat = jnp.concatenate([g.reshape(-1) for g in small])
    room = -(-flat.size // (devices * 8 * LANES)) * (devices * 8 * LANES)
    flat = jnp.pad(flat, (0, room - flat.size)).reshape(devices, -1, LANES)
    flat, low_sums = lax.optimization_barrier((flat, low_sums))
    flat = sum_everywhere(flat, devices, shards, 4).reshape(-1)
    parts, at = [], 0
    for g in small:
        parts.append(flat[at : at + g.size].reshape(g.shape))
        at += g.size
    g_conv, g_hr_gain, g_ln1, g_ln2 = parts
    own = low_sums.astype(F32)
    split, at = [], 0
    for p in pieces:
        split.append(own[:, at : at + p.shape[1]])
        at += p.shape[1]
    g_ad_gate, g_ad_out, g_high_a, g_high_b, g_query, g_key, g_value, g_proj, g_up, g_down = split
    g_ad_high = jnp.concatenate([g_high_a, g_high_b[: ad_high.shape[0] // devices - share]], axis=0)
    g_qkv = jnp.stack([g_query, g_key, g_value])
    g_ad_out, g_proj, g_down = g_ad_out.T, g_proj.T, g_down.T
    return (
        low_out,
        hr_out,
        d_low_in,
        d_hr_in,
        g_conv,
        g_hr_gain,
        g_cn_up,
        g_cn_down,
        g_ad_gate,
        g_ad_high,
        g_ad_out,
        g_ln1,
        g_qkv,
        g_proj,
        g_ln2,
        g_up,
        g_down,
    )


def solution(mesh):
    return jax.shard_map(
        per_device,
        mesh=mesh,
        in_specs=(
            P("dp", "mp", None, None),
            P("dp", "mp", None),
            P("dp", "mp", None),
            P(),
            P(),
            P(None, "mp"),
            P("mp", None),
            P(None, "mp"),
            P(None, "mp"),
            P("mp", None),
            P(),
            P(None, None, "mp"),
            P("mp", None),
            P(),
            P(None, "mp"),
            P("mp", None),
            P("dp", "mp", None),
            P("dp", "mp", None, None),
        ),
        out_specs=(
            P("dp", "mp", None),
            P("dp", "mp", None, None),
            P("dp", "mp", None),
            P("dp", "mp", None, None),
            P(),
            P(),
            P("dp", "mp"),
            P("mp", "dp"),
            P("dp", "mp"),
            P("dp", "mp"),
            P("mp", "dp"),
            P(),
            P(None, "dp", "mp"),
            P("mp", "dp"),
            P(),
            P("dp", "mp"),
            P("mp", "dp"),
        ),
        check_vma=False,
    )
```

```python
import jax
import jax.numpy as jnp
from jax import lax
from jax.experimental.layout import Layout, with_layout_constraint
from jax.experimental import pallas as pl
from jax.experimental.pallas import tpu as pltpu
from jax.sharding import PartitionSpec as P

HEAD = 64
LANES = 128
EDGE = 8
CHUNKS = 6
TILE = 512
MIB = 1024 * 1024
MESH = pl.DeviceIdType.MESH
BF = jnp.bfloat16
F32 = jnp.float32

def gelu_parts(x):
    c = 0.7978845608028654
    x2 = x * x
    t = jnp.tanh(c * x * (1.0 + 0.044715 * x2))
    half = 0.5 * (1.0 + t)
    slope = half + 0.5 * x * (1.0 - t * t) * (c * (1.0 + 3 * 0.044715 * x2))
    return x * half, slope


def gelu(x):
    c = 0.7978845608028654
    t = jnp.tanh(c * x * (1.0 + 0.044715 * (x * x)))
    return 0.5 * x * (1.0 + t)


def dp_bit(position):
    return lax.rem(lax.axis_index("dp") // 2**position, 2)


def dp_mate(position):
    return lax.axis_index("dp") + 2**position * (1 - 2 * dp_bit(position))


class Halving:
    def __init__(self, bits, lasts, shape, block):
        self.lasts, self.shape, self.block = lasts, shape, block
        left = list(bits)
        self.bits = [left.pop(0 if last else -1) for last in lasts]

    def split(self, count, p):
        if count == 1:
            return (1, 1)
        return (count // 2, 2) if self.lasts[p] else (2, count // 2)

    def buffers(self):
        count, rows, cols = self.shape
        got, held = [], []
        for p in range(len(self.bits)):
            count //= 2
            got.append(jax.ShapeDtypeStruct((count, rows, cols), BF))
            held.append(jax.ShapeDtypeStruct(self.split(count, p + 1) + (rows, cols), BF))
        return got + held

    def semaphores(self):
        return [pltpu.SemaphoreType.DMA((len(self.bits),))] * 2

    def bind(self, first, buffers, send, recv):
        steps = len(self.bits)
        self.now = [first] + list(buffers[steps:])
        self.got, self.send, self.recv = buffers[:steps], send, recv

    def part(self, p, mine):
        bit = dp_bit(self.bits[p])
        index = bit if mine else 1 - bit
        return self.now[p].at[:, index] if self.lasts[p] else self.now[p].at[index]

    def copy(self, p):
        return pltpu.make_async_remote_copy(
            src_ref=self.part(p, False), dst_ref=self.got[p], send_sem=self.send.at[p], recv_sem=self.recv.at[p],
            device_id={"dp": dp_mate(self.bits[p])}, device_id_type=MESH,
        )

    def start(self, p):
        self.copy(p).start()

    def finish(self, p):
        self.copy(p).wait()
        count, rows, cols = self.got[p].shape
        ways = self.split(count, p + 1)

        def add(a, b, out):
            out[...] = (a[...].astype(F32) + b[...].astype(F32)).astype(BF).reshape(out.shape)

        flat = pl.BlockSpec((1, rows, self.block), lambda k, c: (k, 0, c))
        paired = pl.BlockSpec((1, 1, rows, self.block), lambda k, c: (k // ways[1], lax.rem(k, ways[1]), 0, c))
        pltpu.emit_pipeline(add, grid=(count, cols // self.block), in_specs=[flat, flat], out_specs=[paired])(
            self.part(p, True), self.got[p], self.now[p + 1]
        )


def chain_exchange(
    n, chunks, lag, gathered, partial, travel, sems, own_chunk, prepare, arrived, compute, mates=(), begin=None, turn=None
):
    ag_send, ag_recv, rs_send, rs_recv = sems
    d = lax.axis_index("mp")
    has_left, has_right = d > 0, d < n - 1

    barrier = pltpu.get_barrier_semaphore()

    @pl.when(has_left)
    def _():
        pl.semaphore_signal(barrier, inc=1, device_id={"mp": d - 1}, device_id_type=MESH)

    @pl.when(has_right)
    def _():
        pl.semaphore_signal(barrier, inc=1, device_id={"mp": d + 1}, device_id_type=MESH)

    for mate in mates:
        pl.semaphore_signal(barrier, inc=1, device_id={"dp": mate}, device_id_type=MESH)

    own_chunk(0)
    pl.semaphore_wait(barrier, has_left.astype(jnp.int32) + has_right.astype(jnp.int32) + len(mates))
    if begin is not None:
        begin()

    def ag(way, s, j):
        return pltpu.make_async_remote_copy(
            src_ref=gathered.at[s, j], dst_ref=gathered.at[s, j],
            send_sem=ag_send.at[way, s, j], recv_sem=ag_recv.at[s, j],
            device_id={"mp": d + 1 - 2 * way}, device_id_type=MESH,
        )

    def rs(way, s, j):
        there = d + 1 - 2 * way
        slot = jnp.where((s == there) & (way == 0), n, s)
        return pltpu.make_async_remote_copy(
            src_ref=travel.at[s, j], dst_ref=travel.at[slot, j],
            send_sem=rs_send.at[s, j], recv_sem=rs_recv.at[slot, j],
            device_id={"mp": there}, device_id_type=MESH,
        )

    def rs_wait(slot, j):
        pltpu.make_async_copy(travel.at[slot, j], travel.at[slot, j], rs_recv.at[slot, j]).wait()

    def first(j, _):
        @pl.when(j > 0)
        def _():
            own_chunk(j)

        @pl.when(has_right)
        def _():
            ag(0, d, j).start()

        @pl.when(has_left)
        def _():
            ag(1, d, j).start()

        return 0

    lax.fori_loop(0, chunks, first, 0)

    def flow(way, q):
        ql = jnp.clip(q, 0, n * chunks - 1)
        s, jj = ql // chunks, lax.rem(ql, chunks)
        if way == 1:
            s = n - 1 - s
        ahead = (s > d) if way == 0 else (s < d)
        source = has_left if way == 0 else has_right

        @pl.when((q >= 0) & (q < n * chunks) & (ahead | ((s == d) & source)))
        def _():
            @pl.when(source)
            def _():
                rs_wait(jnp.where(s == d, n, s) if way == 0 else s, jj)

            @pl.when(ahead & source)
            def _():
                travel[s, jj] = (partial[s, jj].astype(F32) + travel[s, jj].astype(F32)).astype(BF)

            @pl.when(ahead & jnp.logical_not(source))
            def _():
                travel[s, jj] = partial[s, jj].astype(BF)

            @pl.when(ahead)
            def _():
                rs(way, s, jj).start()

    def step(g, _):
        k, j = g // chunks, lax.rem(g, chunks)
        if turn is not None:
            turn(g)

        @pl.when(g < n * chunks)
        def _():
            def side(way, _):
                s = d - k + 2 * k * way
                ok = (s >= 0) & (s < n) & ((k > 0) | (way == 0))

                @pl.when(ok)
                def _():
                    prepare(way, s, j)

                    @pl.when(k > 0)
                    def _():
                        pltpu.make_async_copy(
                            gathered.at[s, j], gathered.at[s, j], ag_recv.at[s, j]
                        ).wait()

                        @pl.when((way == 0) & has_right)
                        def _():
                            ag(0, s, j).start()

                        @pl.when((way == 1) & has_left)
                        def _():
                            ag(1, s, j).start()

                    arrived(s, j)
                    compute(way, s, j)

                return 0

            lax.fori_loop(0, 2, side, 0)

        flow(1, g - (n - 1 - d) * lag)
        flow(0, g - d * lag)
        return 0

    lax.fori_loop(0, n * chunks + (n - 1) * lag, step, 0)

    def drain(i, _):
        s, j = i // chunks, lax.rem(i, chunks)

        @pl.when(has_right & (s <= d))
        def _():
            ag(0, s, j).wait_send()

        @pl.when(has_left & (s >= d))
        def _():
            ag(1, s, j).wait_send()

        @pl.when(s < d)
        def _():
            rs(1, s, j).wait_send()

        @pl.when(s > d)
        def _():
            rs(0, s, j).wait_send()

        return 0

    lax.fori_loop(0, n * chunks, drain, 0)


def own_sum(n, d, j, partial, travel, total):
    total[...] = partial[d, j].astype(F32)

    @pl.when(d > 0)
    def _():
        total[...] += travel[n, j].astype(F32)

    @pl.when(d < n - 1)
    def _():
        total[...] += travel[d, j].astype(F32)


def chain_sems(n, chunks):
    dma = pltpu.SemaphoreType.DMA
    return [dma((2, n, chunks)), dma((n, chunks)), dma((n, chunks)), dma((n + 1, chunks))]


def chunk_buffers(n, rows, c, kept):
    return [
        pltpu.VMEM((n, CHUNKS, rows, c), BF),
        pltpu.VMEM((n, CHUNKS, rows, c), kept),
        pltpu.VMEM((n + 1, CHUNKS, rows, c), BF),
    ]


def columns(i):
    return pl.ds(pl.multiple_of(i * TILE, TILE), TILE)


def drain_copies(n, copy):
    def one(i, _):
        copy(i // CHUNKS, lax.rem(i, CHUNKS)).wait()
        return 0

    lax.fori_loop(0, n * CHUNKS, one, 0)


def big_forward(x, w_up, w_down, residual, mask, share, n):
    t, c = x.shape
    h = w_up.shape[1]
    rows = t // CHUNKS
    cols = residual.shape[1]
    half = cols // 2
    pairs = rows // cols // 2

    def kernel(
        x_ref, wu, wd, res, mask_ref, share_ref, out, pooled, x_all, act_all, slope_all,
        gathered, partial, travel, act, slope, total, folded, copied, stored, load_sem, *sems
    ):
        d = lax.axis_index("mp")
        load = pltpu.make_async_copy(x_ref, gathered.at[d], load_sem)

        def own_chunk(j):
            if isinstance(j, int):
                load.start()
                load.wait()

        def x_copy(s, j):
            return pltpu.make_async_copy(gathered.at[s, j], x_all.at[s, j], copied.at[s, j])

        def prepare(way, s, j):
            pass

        def arrived(s, j):
            x_copy(s, j).start()

        def compute(way, s, j):
            block = gathered.at[s, j]

            def up(i, _):
                pre = jnp.dot(block[...], wu[:, columns(i)], preferred_element_type=F32)
                value, rate = gelu_parts(pre)
                act[:, columns(i)] = value.astype(BF)
                slope[:, columns(i)] = rate.astype(BF)
                return 0

            lax.fori_loop(0, h // TILE, up, 0)
            keep_act = pltpu.make_async_copy(act, act_all.at[s, j], stored.at[0])
            keep_slope = pltpu.make_async_copy(slope, slope_all.at[s, j], stored.at[1])
            keep_act.start()
            keep_slope.start()

            def down(i, _):
                partial[s, j, :, columns(i)] = jnp.dot(
                    act[...], wd[:, columns(i)], preferred_element_type=F32
                )
                return 0

            lax.fori_loop(0, c // TILE, down, 0)
            keep_act.wait()
            keep_slope.wait()

        chain_exchange(n, CHUNKS, 1, gathered, partial, travel, sems, own_chunk, prepare, arrived, compute)

        def finish(j, _):
            own_sum(n, d, j, partial, travel, total)
            values = (res[pl.ds(j * 2 * pairs, 2 * pairs)].reshape(rows, c).astype(F32) + total[...]) * mask_ref[j]
            partial[d, j] = values
            pltpu.make_async_copy(partial.at[d, j], out.at[j], stored.at[0]).start()
            both = values.reshape(pairs, 2, cols, c)
            summed = (both[:, 0] + both[:, 1]).reshape(pairs * cols, c)
            for b in range(c // LANES):
                lanes = slice(b * LANES, (b + 1) * LANES)
                folded[b] = summed[:, lanes]
                every = folded[b, pl.ds(0, pairs * half, 2), :] + folded[b, pl.ds(1, pairs * half, 2), :]
                pooled[j, :, lanes] = (every * share_ref[j]).astype(BF)
            pltpu.make_async_copy(partial.at[d, j], out.at[j], stored.at[0]).wait()
            return 0

        lax.fori_loop(0, CHUNKS, finish, 0)
        drain_copies(n, x_copy)

    whole = pl.BlockSpec(memory_space=pl.ANY)
    local = pl.BlockSpec(memory_space=pltpu.VMEM)
    out, pooled, x_all, act_all, slope_all = pl.pallas_call(
        kernel,
        out_shape=(
            jax.ShapeDtypeStruct((CHUNKS, rows, c), F32),
            jax.ShapeDtypeStruct((CHUNKS, pairs * half, c), BF),
            jax.ShapeDtypeStruct((n, CHUNKS, rows, c), BF),
            jax.ShapeDtypeStruct((n, CHUNKS, rows, h), BF),
            jax.ShapeDtypeStruct((n, CHUNKS, rows, h), BF),
        ),
        in_specs=[whole, local, local, local, local, local],
        out_specs=(whole, local, whole, whole, whole),
        scratch_shapes=chunk_buffers(n, rows, c, F32)
        + [pltpu.VMEM((rows, h), BF)] * 2
        + [pltpu.VMEM((rows, c), F32), pltpu.VMEM((c // LANES, pairs * cols, LANES), F32)]
        + [pltpu.SemaphoreType.DMA((n, CHUNKS)), pltpu.SemaphoreType.DMA((2,)), pltpu.SemaphoreType.DMA]
        + chain_sems(n, CHUNKS),
        compiler_params=pltpu.CompilerParams(
            collective_id=0, has_side_effects=True, vmem_limit_bytes=60 * MIB
        ),
        cost_estimate=pl.CostEstimate(
            flops=4 * n * t * c * h, bytes_accessed=8 * n * t * c, transcendentals=n * t * h
        ),
    )(
        x.reshape(CHUNKS, rows, c), w_up, w_down, residual,
        mask.reshape(CHUNKS, rows, 1), share.reshape(CHUNKS, pairs * half, 1),
    )
    return (
        out.reshape(t, c),
        pooled.reshape(t // 4, c),
        x_all,
        act_all,
        slope_all,
    )


def big_backward(cot, d_pooled, share, mask, x_all, act_all, slope_all, w_up, w_down, grads, n, devices):
    _, cols, c = cot.shape
    t = cot.shape[0] * cols
    h = w_up.shape[1]
    rows = t // CHUNKS
    half = cols // 2
    pairs_here = rows // cols // 2
    pieces = c // rows
    pairs, g_rows, g_cols = grads.shape
    bits = range(1, devices.bit_length() - 1)
    split = g_rows // 2
    steps = len(bits)
    plans = [Halving(bits, [last] * steps, (pairs, split, g_cols), min(g_cols, 1024)) for last in (True, False)]
    extras = [b for plan in plans for b in plan.buffers()[:-1]]
    each = 2 * steps - 1

    def kernel(
        cot_ref, pool_ref, share_ref, mask_ref, x_hbm, act_hbm, slopes, wu, wd, g_first, g_second,
        out, d_own, g_up_out, g_down_out, *rest
    ):
        sums, extra, rest = rest[0], rest[1 : 1 + 2 * each], rest[1 + 2 * each :]
        gathered, partial, travel, slope, grad, left, right, g_up, g_down, total, spread_rows = rest[:11]
        copied, stored, send0, recv0, send1, recv1 = rest[11:17]
        sems = rest[17:]
        d = lax.axis_index("mp")
        plans[0].bind(g_first.at[:, :, pl.ds(0, split)], extra[:each] + (sums.at[0],), send0, recv0)
        plans[1].bind(g_second.at[:, :, pl.ds(split, split)], extra[each:] + (sums.at[1],), send1, recv1)

        def begin():
            for plan in plans:
                plan.start(0)

        def pass_on(p):
            for plan in plans:
                plan.finish(p)
            if p + 1 < steps:
                for plan in plans:
                    plan.start(p + 1)

        all_steps = n * CHUNKS + n - 1
        due = [all_steps * (2**steps - 2 ** (steps - 1 - p)) // (2**steps - 1) for p in range(steps)]

        def turn(g):
            for p in range(steps - 1):
                pl.when(g == due[p])(lambda p=p: pass_on(p))

        def own_chunk(j):
            part = pool_ref[j] * share_ref[j]
            here = cot_ref.at[pl.ds(j * 2 * pairs_here, 2 * pairs_here)]
            for b in range(c // LANES):
                lanes = slice(b * LANES, (b + 1) * LANES)
                spread_rows[b, pl.ds(0, pairs_here * half, 2), :] = part[:, lanes]
                spread_rows[b, pl.ds(1, pairs_here * half, 2), :] = part[:, lanes]
                block = jnp.broadcast_to(
                    spread_rows[b].reshape(pairs_here, 1, cols, LANES), (pairs_here, 2, cols, LANES)
                ).reshape(rows, LANES)
                cell = here[:, :, lanes].reshape(rows, LANES).astype(F32)
                gathered[d, j, :, lanes] = ((cell + block) * mask_ref[j]).astype(BF)

        def slope_copy(s, j):
            return pltpu.make_async_copy(slopes.at[s, j], slope, stored.at[0])

        def pair_copies(s, j):
            two = pl.ds(j - 1, 2)
            return (
                pltpu.make_async_copy(x_hbm.at[s, two], left, stored.at[1]),
                pltpu.make_async_copy(act_hbm.at[s, two], right, stored.at[2]),
            )

        def prepare(way, s, j):
            slope_copy(s, j).start()

            @pl.when(lax.rem(j, 2) == 1)
            def _():
                for copy in pair_copies(s, j):
                    copy.start()

        def arrived(s, j):
            pass

        def compute(way, s, j):
            block = gathered.at[s, j]
            mine = grad.at[way, lax.rem(j, 2)]
            slope_copy(s, j).wait()

            def up(i, _):
                back = nt(block[...], wd[columns(i), :])
                mine[:, columns(i)] = (back * slope[:, columns(i)].astype(F32)).astype(BF)
                return 0

            lax.fori_loop(0, h // TILE, up, 0)

            def down(i, _):
                partial[s, j, :, columns(i)] = nt(mine[...], wu[columns(i), :]).astype(BF)
                return 0

            lax.fori_loop(0, c // TILE, down, 0)

            @pl.when(lax.rem(j, 2) == 1)
            def _():
                for copy in pair_copies(s, j):
                    copy.wait()

                def tile(i, _):
                    a, b = columns(i // (h // TILE)), columns(lax.rem(i, h // TILE))
                    two = pl.ds(j - 1, 2)
                    g_up[a, b] += tn(
                        left[:, :, a].reshape(2 * rows, TILE), grad[way, :, :, b].reshape(2 * rows, TILE)
                    )
                    g_down[a, b] += tn(
                        gathered[s, two, :, a].reshape(2 * rows, TILE), right[:, :, b].reshape(2 * rows, TILE)
                    )
                    return 0

                lax.fori_loop(0, (c // TILE) * (h // TILE), tile, 0)

        def clear(i, _):
            some = pl.ds(pl.multiple_of(i * rows, rows), rows)
            g_up[some] = jnp.zeros((rows, h), F32)
            g_down[some] = jnp.zeros((rows, h), F32)
            return 0

        def begin_all():
            begin()
            lax.fori_loop(0, pieces, clear, 0)

        chain_exchange(
            n, CHUNKS, 1, gathered, partial, travel, sems, own_chunk, prepare, arrived, compute,
            [dp_mate(b) for b in bits], begin_all, turn,
        )
        keep = pltpu.make_async_copy(gathered.at[d], d_own, stored.at[0])
        keep.start()

        def result(j):
            return pltpu.make_async_copy(total, out.at[j], stored.at[1])

        def finish(j, _):
            @pl.when(j > 0)
            def _():
                result(j - 1).wait()

            own_sum(n, d, j, partial, travel, total)
            result(j).start()
            return 0

        lax.fori_loop(0, CHUNKS, finish, 0)
        result(CHUNKS - 1).wait()
        keep.wait()

        def place(i):
            return i // CHUNKS, lax.rem(i, CHUNKS)

        def up_copy(i):
            s, j = place(i)
            return pltpu.make_async_copy(travel.at[s, j], g_up_out.at[i], copied.at[0, i])

        def down_copy(i):
            s, j = place(i)
            return pltpu.make_async_copy(gathered.at[s, j], g_down_out.at[i], copied.at[1, i])

        def give(i, _):
            s, j = place(i)
            some = pl.ds(pl.multiple_of(i * rows, rows), rows)
            travel[s, j] = g_up[some].astype(BF)
            up_copy(i).start()
            gathered[s, j] = g_down[some].astype(BF)
            down_copy(i).start()
            return 0

        lax.fori_loop(0, pieces, give, 0)
        pass_on(steps - 1)

        def given(i, _):
            up_copy(i).wait()
            down_copy(i).wait()
            return 0

        lax.fori_loop(0, pieces, given, 0)

    whole = pl.BlockSpec(memory_space=pl.ANY)
    local = pl.BlockSpec(memory_space=pltpu.VMEM)
    dma = pltpu.SemaphoreType.DMA
    out, d_own, g_up, g_down, sums, *_ = pl.pallas_call(
        kernel,
        out_shape=(
            jax.ShapeDtypeStruct((CHUNKS, rows, c), F32),
            jax.ShapeDtypeStruct((CHUNKS, rows, c), BF),
            jax.ShapeDtypeStruct((pieces, rows, h), BF),
            jax.ShapeDtypeStruct((pieces, rows, h), BF),
            jax.ShapeDtypeStruct((2, 1, 1, split, g_cols), BF),
            *extras,
        ),
        in_specs=[local] * 4 + [whole] * 3 + [local] * 2 + [whole] * 2,
        out_specs=(whole,) * (5 + 2 * each),
        scratch_shapes=chunk_buffers(n, rows, c, BF)
        + [
            pltpu.VMEM((rows, h), BF), pltpu.VMEM((2, 2, rows, h), BF),
            pltpu.VMEM((2, rows, c), BF), pltpu.VMEM((2, rows, h), BF),
            pltpu.VMEM((c, h), F32), pltpu.VMEM((c, h), F32),
            pltpu.VMEM((rows, c), F32), pltpu.VMEM((c // LANES, pairs_here * cols, LANES), F32),
            dma((2, pieces)), dma((3,)),
        ]
        + plans[0].semaphores() + plans[1].semaphores()
        + chain_sems(n, CHUNKS),
        compiler_params=pltpu.CompilerParams(
            collective_id=1, has_side_effects=True, vmem_limit_bytes=62 * MIB
        ),
        cost_estimate=pl.CostEstimate(
            flops=8 * n * t * c * h, bytes_accessed=8 * n * t * c, transcendentals=0
        ),
    )(
        cot, d_pooled.reshape(CHUNKS, pairs_here * half, c), share.reshape(CHUNKS, pairs_here * half, 1),
        mask.reshape(CHUNKS, rows, 1), x_all, act_all, slope_all, w_up, w_down,
        grads.reshape(pairs // 2, 2, g_rows, g_cols), grads.reshape(2, pairs // 2, g_rows, g_cols),
    )
    shaped = [g.reshape(devices, c // devices, h) for g in (g_up, g_down)]
    return out.reshape(cot.shape), d_own.reshape(cot.shape), shaped, sums.reshape(g_rows, g_cols)


def frame(dst, src):
    rows, cols, _ = src.shape
    dst[:, :EDGE] = jnp.zeros((rows, EDGE, LANES), F32)
    dst[:, EDGE + cols:] = jnp.zeros((rows, EDGE, LANES), F32)
    dst[:, EDGE:EDGE + cols] = src[...].astype(F32)


def correlate(out, framed, taps, size, flip, group, first=0, last=None, every=1):
    rows, cols, _ = out.shape
    reach = size // 2
    def some(k, _):
        r = first + k * every
        acc = jnp.zeros((group, cols, LANES), F32)
        for a in range(size):
            for b in range(size):
                tap = (size - 1 - a) * size + size - 1 - b if flip else a * size + b
                acc = acc + framed[pl.ds(r * group + a, group), pl.ds(EDGE - reach + b, cols), :] * taps[tap]
        out[pl.ds(r * group, group)] = acc
        return 0
    lax.fori_loop(0, (rows // group if last is None else last) - first if every == 1 else 2, some, 0)


def conv_forward(x, w, size, n):
    rows, cols, c = x.shape
    reach = size // 2

    def kernel(x_ref, w_ref, out, bordered, framed, sent, got, own):
        d = lax.axis_index("mp")
        has_up, has_down = d > 0, d < n - 1
        barrier = pltpu.get_barrier_semaphore()

        @pl.when(has_up)
        def _():
            pl.semaphore_signal(barrier, inc=1, device_id={"mp": d - 1}, device_id_type=MESH)

        @pl.when(has_down)
        def _():
            pl.semaphore_signal(barrier, inc=1, device_id={"mp": d + 1}, device_id_type=MESH)

        keep = pltpu.make_async_copy(x_ref, bordered.at[pl.ds(reach, rows)], own)
        keep.start()
        pl.semaphore_wait(barrier, has_up.astype(jnp.int32) + has_down.astype(jnp.int32))
        up = pltpu.make_async_remote_copy(
            src_ref=x_ref.at[pl.ds(0, reach)], dst_ref=bordered.at[pl.ds(reach + rows, reach)],
            send_sem=sent.at[0], recv_sem=got.at[0], device_id={"mp": d - 1}, device_id_type=MESH,
        )
        down = pltpu.make_async_remote_copy(
            src_ref=x_ref.at[pl.ds(rows - reach, reach)], dst_ref=bordered.at[pl.ds(0, reach)],
            send_sem=sent.at[1], recv_sem=got.at[1], device_id={"mp": d + 1}, device_id_type=MESH,
        )
        nothing = jnp.zeros((reach, cols, c), BF)

        @pl.when(has_up)
        def _():
            up.start()

        @pl.when(has_down)
        def _():
            down.start()

        @pl.when(d == 0)
        def _():
            bordered[:reach] = nothing

        @pl.when(d == n - 1)
        def _():
            bordered[reach + rows :] = nothing

        groups = rows // reach

        def inner(i, _):
            lanes = pl.ds(pl.multiple_of(i * LANES, LANES), LANES)
            frame(framed.at[pl.ds(reach, rows)], x_ref.at[:, :, lanes])
            correlate(out.at[:, :, lanes], framed, w_ref.at[:, :, lanes], size, False, reach, 1, groups - 1)
            return 0

        lax.fori_loop(0, c // LANES, inner, 0)
        keep.wait()

        @pl.when(has_up)
        def _():
            down.wait_recv()

        @pl.when(has_down)
        def _():
            up.wait_recv()

        def block(i, _):
            lanes = pl.ds(pl.multiple_of(i * LANES, LANES), LANES)
            frame(framed, bordered.at[:, :, lanes])
            correlate(out.at[:, :, lanes], framed, w_ref.at[:, :, lanes], size, False, reach, 0, None, groups - 1)
            return 0

        lax.fori_loop(0, c // LANES, block, 0)

        @pl.when(has_up)
        def _():
            up.wait_send()

        @pl.when(has_down)
        def _():
            down.wait_send()

    local = pl.BlockSpec(memory_space=pltpu.VMEM)
    dma = pltpu.SemaphoreType.DMA
    return pl.pallas_call(
        kernel,
        out_shape=(
            jax.ShapeDtypeStruct((rows, cols, c), F32),
            jax.ShapeDtypeStruct((rows + 2 * reach, cols, c), BF),
        ),
        in_specs=[local, local],
        out_specs=(local, local),
        scratch_shapes=[pltpu.VMEM((rows + 2 * reach, cols + 2 * EDGE, LANES), F32), dma((2,)), dma((2,)), dma],
        compiler_params=pltpu.CompilerParams(
            collective_id=5, has_side_effects=True, vmem_limit_bytes=40 * MIB
        ),
    )(x, w)


def conv_backward(d_normed, conv_out, gain, mask, bordered, d_map, w, size, grads, devices, n):
    rows, cols, c = conv_out.shape
    reach = size // 2
    high = rows + 2 * reach
    group = 4 if rows % 4 == 0 else 1
    steps = devices.bit_length() - 1
    shape = grads[0].shape
    plans = [Halving(range(steps), [True] + [last] * (steps - 1), shape, shape[2]) for last in (True, False)]
    blocks = c // LANES
    stops = [blocks * 3 * p // (4 * max(steps - 2, 1)) for p in range(1, steps - 1)] + [blocks]

    def kernel(dn, co, gain_ref, mask_ref, w_ref, b_hbm, dm_hbm, g0, g1, out, g, g_gain, *rest):
        extra, rest = rest[: 4 * steps], rest[4 * steps :]
        around, x_around, d_here, dframed, xframed, sent, got, own, *sems = rest
        plans[0].bind(g0, extra[: 2 * steps], sems[0], sems[1])
        plans[1].bind(g1, extra[2 * steps :], sems[2], sems[3])
        d = lax.axis_index("mp")
        has_up, has_down = d > 0, d < n - 1
        barrier = pltpu.get_barrier_semaphore()
        for b in range(steps):
            pl.semaphore_signal(barrier, inc=1, device_id={"dp": dp_mate(b)}, device_id_type=MESH)

        @pl.when(has_up)
        def _():
            pl.semaphore_signal(barrier, inc=1, device_id={"mp": d - 1}, device_id_type=MESH)

        @pl.when(has_down)
        def _():
            pl.semaphore_signal(barrier, inc=1, device_id={"mp": d + 1}, device_id_type=MESH)

        load_x = pltpu.make_async_copy(b_hbm, x_around, own.at[0])
        load_d = pltpu.make_async_copy(dm_hbm, d_here, own.at[1])
        load_x.start()
        load_d.start()
        pl.semaphore_wait(barrier, has_up.astype(jnp.int32) + has_down.astype(jnp.int32) + steps)
        for plan in plans:
            plan.start(0)

        g_gain[...] = jnp.zeros(g_gain.shape, F32)

        def norm(r, _):
            cells = mask_ref[r]
            back, part = normalise_back(co[r] * cells, gain_ref[...], dn[r])
            around[reach + r] = (back * cells).astype(BF)
            g_gain[...] += part
            return 0

        lax.fori_loop(0, rows, norm, 0)
        up = pltpu.make_async_remote_copy(
            src_ref=around.at[pl.ds(reach, reach)], dst_ref=around.at[pl.ds(reach + rows, reach)],
            send_sem=sent.at[0], recv_sem=got.at[0], device_id={"mp": d - 1}, device_id_type=MESH,
        )
        down = pltpu.make_async_remote_copy(
            src_ref=around.at[pl.ds(rows, reach)], dst_ref=around.at[pl.ds(0, reach)],
            send_sem=sent.at[1], recv_sem=got.at[1], device_id={"mp": d + 1}, device_id_type=MESH,
        )
        nothing = jnp.zeros((reach, cols, c), BF)

        @pl.when(has_up)
        def _():
            up.start()

        @pl.when(has_down)
        def _():
            down.start()

        @pl.when(d == 0)
        def _():
            around[:reach] = nothing

        @pl.when(d == n - 1)
        def _():
            around[reach + rows :] = nothing

        def pass_on(p):
            for plan in plans:
                plan.finish(p)
            if p + 1 < steps:
                for plan in plans:
                    plan.start(p + 1)

        pass_on(0)
        load_x.wait()
        load_d.wait()

        @pl.when(has_up)
        def _():
            down.wait_recv()

        @pl.when(has_down)
        def _():
            up.wait_recv()

        def block(i, _):
            lanes = pl.ds(pl.multiple_of(i * LANES, LANES), LANES)
            frame(dframed, around.at[:, :, lanes])
            frame(xframed, x_around.at[:, :, lanes])
            correlate(out.at[:, :, lanes], dframed, w_ref.at[:, :, lanes], size, True, group)
            for r in range(rows):
                out[r, :, lanes] = (out[r, :, lanes] + d_here[r, :, lanes].astype(F32)) * mask_ref[r]
            for a in range(size):
                def some(r, accs):
                    dv = dframed[pl.ds(reach + r * group, group), EDGE : EDGE + cols]
                    new = []
                    for b in range(size):
                        prod = dv * xframed[pl.ds(r * group + a, group), pl.ds(EDGE - reach + b, cols), :]
                        new.append(accs[b] + jnp.sum(prod.reshape(-1, 8, LANES), axis=0))
                    return tuple(new)

                accs = lax.fori_loop(
                    0, rows // group, some, tuple(jnp.zeros((8, LANES), F32) for _ in range(size))
                )
                for b in range(size):
                    g[a * size + b, :, lanes] = jnp.sum(accs[b], axis=0, keepdims=True)
            return 0

        at = 0
        for p, stop in enumerate(stops):
            lax.fori_loop(at, stop, block, 0)
            at = stop
            pass_on(p + 1)

        @pl.when(has_up)
        def _():
            up.wait_send()

        @pl.when(has_down)
        def _():
            down.wait_send()

    whole = pl.BlockSpec(memory_space=pl.ANY)
    local = pl.BlockSpec(memory_space=pltpu.VMEM)
    vm, dma = pltpu.VMEM, pltpu.SemaphoreType.DMA
    d_in, g, g_gain, *extra = pl.pallas_call(
        kernel,
        out_shape=(
            jax.ShapeDtypeStruct((rows, cols, c), F32),
            jax.ShapeDtypeStruct((size * size, 1, c), F32),
            jax.ShapeDtypeStruct((1, c), F32),
            *plans[0].buffers(),
            *plans[1].buffers(),
        ),
        in_specs=[local] * 5 + [whole] * 4,
        out_specs=(local,) * 3 + (whole,) * (4 * steps),
        scratch_shapes=[
            vm((high, cols, c), BF), vm((high, cols, c), BF), vm((rows, cols, c), BF),
            vm((high, cols + 2 * EDGE, LANES), F32), vm((high, cols + 2 * EDGE, LANES), F32),
            dma((2,)), dma((2,)), dma((2,)),
        ]
        + plans[0].semaphores() + plans[1].semaphores(),
        compiler_params=pltpu.CompilerParams(
            collective_id=3, has_side_effects=True, vmem_limit_bytes=50 * MIB
        ),
        cost_estimate=pl.CostEstimate(flops=6 * 10**10, bytes_accessed=10**8, transcendentals=0),
    )(
        d_normed, conv_out, gain, mask, w, bordered, d_map,
        *(v.reshape((shape[0] // 2, 2) + shape[1:]) for v in grads),
    )
    return d_in, g, g_gain[0], [extra[2 * steps - 1].reshape(shape[1:]), extra[4 * steps - 1].reshape(shape[1:])]


GATE, OUT, HIGH_A, HIGH_B, QUERY, KEY, VALUE, PROJ = range(8)
L_LOW, L_DF, L_POOL_A, L_POOL_B, L_FIRST, L_DA, L_SECOND, L_COT = range(8)
R_DGATE, R_MERGE, R_DHIGH, R_DQ, R_DK, R_DV, R_ATT, R_DUP, R_ACT = range(9)


def nn(a, b):
    return jnp.dot(a, b, preferred_element_type=F32)


def nt(a, b):
    return lax.dot_general(a, b, (((1,), (1,)), ((), ())), preferred_element_type=F32)


def tn(a, b):
    return lax.dot_general(a, b, (((0,), (0,)), ((), ())), preferred_element_type=F32)


def normalise(x, gain):
    centred = x - jnp.mean(x, -1, keepdims=True)
    rate = lax.rsqrt(jnp.mean(centred * centred, -1, keepdims=True) + 1e-06)
    return centred * rate * gain


def normalise_back(x, gain, d):
    centred = x - jnp.mean(x, -1, keepdims=True)
    rate = lax.rsqrt(jnp.mean(centred * centred, -1, keepdims=True) + 1e-06)
    hat = centred * rate
    dg = d * gain
    back = rate * (dg - jnp.mean(dg, -1, keepdims=True) - hat * jnp.mean(dg * hat, -1, keepdims=True))
    return back, jnp.sum(d * hat, axis=0, keepdims=True)


def low_stage(low, pool_a, pool_b, cot, gain1, gain2, packed, n, devices, cid):
    t, dim = low.shape
    every = n * t
    width = dim // n
    heads = width // HEAD
    pairs = devices // 2
    rows = dim // devices
    half = dim // 2
    ff = 4 * dim
    scale = HEAD ** (-0.5)

    def kernel(
        low_ref, pool_a_ref, pool_b_ref, cot_ref, gain1_ref, gain2_ref, w_hbm,
        low_out, d_low, d_pool_a, d_pool_b, g_ln1, g_ln2, grads,
        wv, lhs, lhs2, rhs, gate, high, merged, resid, d_res, slope, mixed, heads_in, att_all, d_att, d_mixed,
        d_heads, probs, d_scores, stage, w_sem, q_send, q_got, a_send, a_got, b_send, b_got, c_send, c_got, own_sem,
        l_send, l_got, r_send, r_got, stage_sem,
    ):
        d = lax.axis_index("mp")
        dp = lax.axis_index("dp")
        core = lax.rem(dp, 2)
        mate = dp + 1 - 2 * core
        barrier = pltpu.get_barrier_semaphore()
        for k in range(1, n):
            pl.semaphore_signal(barrier, inc=1, device_id={"mp": lax.rem(d + k, n)}, device_id_type=MESH)
        pl.semaphore_signal(barrier, inc=1, device_id={"dp": mate}, device_id_type=MESH)

        def w_copy(w, k):
            c, z = k // n, lax.rem(k, n)
            wide, base, at = w_place(w)
            src = w_hbm.at[:, c, z, :, pl.ds(base, wide)]
            dst = wv.at[c, :, :, pl.ds(pl.multiple_of(at + z * wide, wide), wide)]
            return pltpu.make_async_copy(src, dst, w_sem.at[w, k])

        def w_place(w):
            if w < 8:
                return width, w * width, w * dim
            return ff // n, 8 * width + (w - 8) * ff // n, 8 * dim + (w - 8) * ff

        def w_each(w, act):
            def one(k, _):
                act(w_copy(w, k))
                return 0

            lax.fori_loop(0, 2 * n, one, 0)

        for w in range(10):
            w_each(w, lambda copy: copy.start())

        def w_wait(*which):
            for w in which:
                w_each(w, lambda copy: copy.wait())

        def w_cols(at, size):
            return wv[:, :, :, pl.ds(at, size)].reshape(dim, size)

        def forward(x, first, count, put):
            def one(i, _):
                put(pl.multiple_of(i * TILE, TILE), nn(x, w_cols(pl.multiple_of(first * dim + i * TILE, TILE), TILE)))
                return 0
            lax.fori_loop(0, count * dim // TILE, one, 0)

        def backward(get, first, count, dst, fresh):
            def one(i, _):
                for c in range(2):
                    part = wv[c, :, :, pl.ds(pl.multiple_of((first + i) * dim, dim), dim)].reshape(half, dim)
                    y = nt(get(pl.multiple_of(i * dim, dim)), part)
                    cols = slice(c * half, (c + 1) * half)
                    if fresh and count == 1:
                        dst[:, cols] = y
                    else:
                        dst[:, cols] += y
                return 0
            if fresh and count > 1:
                dst[...] = jnp.zeros(dst.shape, F32)
            if count == 1:
                one(0, 0)
            else:
                lax.fori_loop(0, count, one, 0)

        def r_cols(block, count=1):
            return pl.ds(block * dim, count * dim)

        def r_at(block):
            return block * dim if block <= R_DUP else block * dim + 3 * dim

        def r_copy(block):
            cols = pl.ds(r_at(block), dim if block < R_DUP else ff)
            return pltpu.make_async_remote_copy(
                src_ref=rhs.at[0, :, cols], dst_ref=rhs.at[1, :, cols], send_sem=r_send.at[block],
                recv_sem=r_got.at[block], device_id={"dp": mate}, device_id_type=MESH)

        def l_copy(i):
            return pltpu.make_async_remote_copy(
                src_ref=lhs.at[i, :, pl.ds(pl.multiple_of((1 - core) * half, half), half)], dst_ref=lhs2.at[i],
                send_sem=l_send.at[i], recv_sem=l_got.at[i], device_id={"dp": mate}, device_id_type=MESH)

        stored = []

        def grad(i, block, at, count, shared=False):
            if not shared:
                r_copy(block).wait_recv()
            own_l = pl.ds(pl.multiple_of(core * half, half), half)

            wide, base, first = w_place(at if at < 8 else 8 + (at - 8) * dim // ff)
            piece = min(TILE, wide)

            def out_copies(slot, k):
                out = []
                for q in range(TILE // piece):
                    z, col = divmod(at * dim - first + k * TILE + q * piece, wide)
                    out.append(
                        pltpu.make_async_copy(
                            stage.at[slot, :, :, pl.ds(q * piece, piece)],
                            grads.at[:, pl.ds(z * rows, rows), pl.ds(base + col, piece)],
                            stage_sem.at[slot, q],
                        )
                    )
                return out

            for k in range(count * dim // TILE):
                slot = len(stored) % 2
                if len(stored) >= 2:
                    wait(stored[-2])
                cols = pl.ds(r_at(block) + k * TILE, TILE)
                y = tn(lhs[i, :, own_l], rhs[0, :, cols]) + tn(lhs2[i], rhs[1, :, cols])
                stage[slot] = y.astype(BF).reshape(pairs, rows, TILE)
                stored.append(out_copies(slot, k))
                start(stored[-1])

        def to_heads(k, src, dst, send, got):
            out = []
            for step in range(1, n):
                peer = lax.rem(d + step, n)
                out.append(pltpu.make_async_remote_copy(
                    src_ref=src.at[:, pl.ds(pl.multiple_of(peer * width, width), width)],
                    dst_ref=dst.at[pl.ds(pl.multiple_of(d * t, t), t)],
                    send_sem=send.at[k, step], recv_sem=got.at[k, step], device_id={"mp": peer}, device_id_type=MESH))
            out.append(pltpu.make_async_copy(
                src.at[:, pl.ds(pl.multiple_of(d * width, width), width)], dst.at[pl.ds(pl.multiple_of(d * t, t), t)], own_sem.at[k]))
            return out

        def to_tokens(k, src, dst, send, got):
            out = []
            for step in range(1, n):
                peer = lax.rem(d + step, n)
                out.append(pltpu.make_async_remote_copy(
                    src_ref=src.at[pl.ds(pl.multiple_of(peer * t, t), t)],
                    dst_ref=dst.at[:, pl.ds(pl.multiple_of(d * width, width), width)],
                    send_sem=send.at[k, step], recv_sem=got.at[k, step], device_id={"mp": peer}, device_id_type=MESH))
            out.append(pltpu.make_async_copy(
                src.at[pl.ds(pl.multiple_of(d * t, t), t)], dst.at[:, pl.ds(pl.multiple_of(d * width, width), width)], own_sem.at[k]))
            return out

        def start(copies):
            for c in copies:
                c.start()

        def wait(copies):
            for c in copies:
                c.wait()

        lhs[L_LOW] = low_ref[...]
        lhs[L_POOL_A] = pool_a_ref[...]
        lhs[L_POOL_B] = pool_b_ref[...]
        lhs[L_COT] = cot_ref[...]
        acc = d_low
        w_wait(GATE)

        def put_gate(at, y):
            gate[:, pl.ds(at, TILE)] = 1.0 / (1.0 + jnp.exp(-y))
        forward(lhs[L_LOW], GATE, 1, put_gate)
        w_wait(HIGH_A, HIGH_B, OUT)

        def put_high(at, y):
            high[:, pl.ds(at, TILE)] = y
        forward(lhs[L_POOL_A], HIGH_A, 1, put_high)

        def put_merging(at, y):
            cols = pl.ds(at, TILE)
            total = high[:, cols] + y
            high[:, cols] = total
            rhs[0, :, pl.ds(R_MERGE * dim + at, TILE)] = (total * gate[:, cols]).astype(BF)
        forward(lhs[L_POOL_B], HIGH_B, 1, put_merging)
        backward(lambda at: rhs[0, :, r_cols(R_MERGE)], OUT, 1, merged, True)
        merged[...] += lhs[L_LOW].astype(F32)
        lhs[L_FIRST] = normalise(merged[...], gain1_ref[...]).astype(BF)

        w_wait(QUERY, KEY, VALUE, PROJ)
        pl.semaphore_wait(barrier, n)
        for i in (L_LOW, L_POOL_A, L_POOL_B, L_COT, L_FIRST):
            l_copy(i).start()
        r_copy(R_MERGE).start()
        out_q = []
        for k in range(3):
            def put_mixed(at, y):
                mixed[k, :, pl.ds(at, TILE)] = y.astype(BF)
            forward(lhs[L_FIRST], QUERY + k, 1, put_mixed)
            copies = to_heads(k, mixed.at[k], heads_in.at[k], q_send, q_got)
            start(copies)
            out_q += copies
        wait(out_q)

        for h in range(heads):
            lanes = slice(h * HEAD, (h + 1) * HEAD)

            def rows_of(b, _):
                some = pl.ds(pl.multiple_of(b * t, t), t)
                s = nt(heads_in[0, some, lanes], heads_in[1, :, lanes]) * scale
                e = jnp.exp(s - jnp.max(s, -1, keepdims=True))
                p = (e * (1.0 / jnp.sum(e, -1, keepdims=True))).astype(BF)
                probs[h, some] = p
                att_all[some, lanes] = nn(p, heads_in[2, :, lanes]).astype(BF)
                return 0
            lax.fori_loop(0, n, rows_of, 0)
        out_a = to_tokens(0, att_all, rhs.at[0, :, r_cols(R_ATT)], a_send, a_got)
        start(out_a)
        wait(out_a)
        r_copy(R_ATT).start()
        backward(lambda at: rhs[0, :, r_cols(R_ATT)], PROJ, 1, resid, True)
        resid[...] += merged[...]
        lhs[L_SECOND] = normalise(resid[...], gain2_ref[...]).astype(BF)
        l_copy(L_SECOND).start()

        w_wait(8)

        def put_up(at, y):
            value, rate = gelu_parts(y)
            rhs[0, :, pl.ds(r_at(R_ACT) + at, TILE)] = value.astype(BF)
            slope[:, pl.ds(at, TILE)] = rate.astype(BF)
        forward(lhs[L_SECOND], 8, 4, put_up)
        r_copy(R_ACT).start()
        w_wait(9)
        backward(lambda at: rhs[0, :, pl.ds(r_at(R_ACT) + at, dim)], 12, 4, acc, True)
        low_out[...] = resid[...] + acc[...]

        def put_d_up(at, y):
            rhs[0, :, pl.ds(r_at(R_DUP) + at, TILE)] = (y * slope[:, pl.ds(at, TILE)].astype(F32)).astype(BF)
        forward(lhs[L_COT], 12, 4, put_d_up)
        r_copy(R_DUP).start()
        backward(lambda at: rhs[0, :, pl.ds(r_at(R_DUP) + at, dim)], 8, 4, acc, True)
        back, g = normalise_back(resid[...], gain2_ref[...], acc[...])
        g_ln2[...] = g
        d_res[...] = lhs[L_COT].astype(F32) + back
        lhs[L_DA] = d_res[...].astype(BF)
        l_copy(L_DA).start()

        def put_d_att(at, y):
            mixed[0, :, pl.ds(at, TILE)] = y.astype(BF)
        forward(lhs[L_DA], PROJ, 1, put_d_att)
        out_b = to_heads(0, mixed.at[0], d_att, b_send, b_got)
        start(out_b)
        l_copy(L_COT).wait_recv()
        grad(L_COT, R_ACT, 12, 4)
        wait(out_b)
        for h in range(heads):
            lanes = slice(h * HEAD, (h + 1) * HEAD)

            def rows_of(b, _):
                some = pl.ds(pl.multiple_of(b * t, t), t)
                p = probs[h, some].astype(F32)
                dp_ = nt(d_att[some, lanes], heads_in[2, :, lanes])
                ds = (p * (dp_ - jnp.sum(dp_ * p, -1, keepdims=True)) * scale).astype(BF)
                d_scores[some] = ds
                d_heads[0, some, lanes] = nn(ds, heads_in[1, :, lanes]).astype(BF)
                return 0
            lax.fori_loop(0, n, rows_of, 0)
            d_heads[1, :, lanes] = tn(d_scores[...], heads_in[0, :, lanes]).astype(BF)
            d_heads[2, :, lanes] = tn(probs[h], d_att[:, lanes]).astype(BF)
        out_c = []
        for k in range(3):
            copies = to_tokens(k, d_heads.at[k], rhs.at[0, :, r_cols(R_DQ + k)], c_send, c_got)
            start(copies)
            out_c += copies
        l_copy(L_SECOND).wait_recv()
        grad(L_SECOND, R_DUP, 8, 4)
        l_copy(L_DA).wait_recv()
        grad(L_DA, R_ATT, PROJ, 1)
        wait(out_c)
        for k in range(3):
            r_copy(R_DQ + k).start()
        backward(lambda at: rhs[0, :, pl.ds(R_DQ * dim + at, dim)], QUERY, 3, acc, True)
        back, g = normalise_back(merged[...], gain1_ref[...], acc[...])
        g_ln1[...] = g
        d_res[...] += back
        lhs[L_DF] = d_res[...].astype(BF)
        l_copy(L_DF).start()

        def put_d_gate(at, y):
            cols = pl.ds(at, TILE)
            gv = gate[:, cols]
            part = y * gv
            rhs[0, :, pl.ds(R_DHIGH * dim + at, TILE)] = part.astype(BF)
            rhs[0, :, pl.ds(R_DGATE * dim + at, TILE)] = (part * high[:, cols] * (1.0 - gv)).astype(BF)
        forward(lhs[L_DF], OUT, 1, put_d_gate)
        r_copy(R_DHIGH).start()
        r_copy(R_DGATE).start()
        backward(lambda at: rhs[0, :, r_cols(R_DHIGH)], HIGH_A, 1, d_pool_a, True)
        backward(lambda at: rhs[0, :, r_cols(R_DHIGH)], HIGH_B, 1, d_pool_b, True)
        backward(lambda at: rhs[0, :, r_cols(R_DGATE)], GATE, 1, acc, True)
        d_low[...] = d_res[...] + acc[...]
        l_copy(L_FIRST).wait_recv()
        for k in range(3):
            grad(L_FIRST, R_DQ + k, QUERY + k, 1)
        l_copy(L_DF).wait_recv()
        grad(L_DF, R_MERGE, OUT, 1)
        l_copy(L_POOL_A).wait_recv()
        grad(L_POOL_A, R_DHIGH, HIGH_A, 1)
        l_copy(L_POOL_B).wait_recv()
        grad(L_POOL_B, R_DHIGH, HIGH_B, 1, shared=True)
        l_copy(L_LOW).wait_recv()
        grad(L_LOW, R_DGATE, GATE, 1)
        wait(stored[-2])
        wait(stored[-1])
        for i in range(8):
            l_copy(i).wait_send()
        for b in range(9):
            r_copy(b).wait_send()

    whole = pl.BlockSpec(memory_space=pl.ANY)
    local = pl.BlockSpec(memory_space=pltpu.VMEM)
    vm, dma = pltpu.VMEM, pltpu.SemaphoreType.DMA
    tok = jax.ShapeDtypeStruct((t, dim), F32)
    one = jax.ShapeDtypeStruct((1, dim), F32)
    return pl.pallas_call(
        kernel,
        out_shape=(tok, tok, tok, tok, one, one, jax.ShapeDtypeStruct((pairs, n * rows, 16 * width), BF)),
        in_specs=[local] * 6 + [whole],
        out_specs=(local,) * 6 + (whole,),
        scratch_shapes=[
            vm((2, pairs, rows, 16 * dim), BF), vm((8, t, dim), BF), vm((8, t, half), BF), vm((2, t, 15 * dim), BF),
            vm((t, dim), F32), vm((t, dim), F32), vm((t, dim), F32), vm((t, dim), F32), vm((t, dim), F32),
            vm((t, ff), BF), vm((3, t, dim), BF), vm((3, every, width), BF), vm((every, width), BF), vm((every, width), BF),
            vm((1, 8, 128), BF), vm((3, every, width), BF), vm((heads, every, every), BF), vm((every, every), BF),
            vm((2, pairs, rows, TILE), BF),
            dma((10, 2 * n)), dma((3, n)), dma((3, n)), dma((1, n)), dma((1, n)), dma((1, n)), dma((1, n)), dma((3, n)), dma((3, n)),
            dma((3,)), dma((8,)), dma((8,)), dma((9,)), dma((9,)), dma((2, 2)),
        ],
        compiler_params=pltpu.CompilerParams(collective_id=cid, has_side_effects=True, vmem_limit_bytes=61 * MIB),
        cost_estimate=pl.CostEstimate(flops=14 * 10**9, bytes_accessed=70 * 10**6, transcendentals=10**7),
    )(low, pool_a, pool_b, cot, gain1, gain2, packed.reshape(pairs, 2, n, rows, 16 * width))
def sum_everywhere(x, devices, n, cid):
    rows = x.shape[1]

    def kernel(x_ref, out, here, level, send1, recv1, send2, recv2, send3, recv3):
        me, d = lax.axis_index("dp"), lax.axis_index("mp")
        barrier = pltpu.get_barrier_semaphore()

        def greet(k, _):
            pl.semaphore_signal(
                barrier, inc=1, device_id={"dp": lax.rem(me + k, devices)}, device_id_type=MESH
            )
            return 0

        lax.fori_loop(1, devices, greet, 0)
        for k in range(1, n):
            pl.semaphore_signal(barrier, inc=1, device_id={"mp": lax.rem(d + k, n)}, device_id_type=MESH)
        here[me] = x_ref[me]
        pl.semaphore_wait(barrier, devices + n - 2)

        def spread(k):
            peer = lax.rem(me + k, devices)
            return pltpu.make_async_remote_copy(
                src_ref=x_ref.at[peer], dst_ref=here.at[me], send_sem=send1.at[k], recv_sem=recv1.at[k],
                device_id={"dp": peer}, device_id_type=MESH,
            )

        def across(k):
            return pltpu.make_async_remote_copy(
                src_ref=level.at[d], dst_ref=level.at[d], send_sem=send2.at[k], recv_sem=recv2.at[k],
                device_id={"mp": lax.rem(d + k, n)}, device_id_type=MESH,
            )

        def give(k):
            return pltpu.make_async_remote_copy(
                src_ref=out.at[me], dst_ref=out.at[me], send_sem=send3.at[k], recv_sem=recv3.at[k],
                device_id={"dp": lax.rem(me + k, devices)}, device_id_type=MESH,
            )

        def each(count, make, act):
            def one(k, _):
                act(make(k))
                return 0

            lax.fori_loop(1, count, one, 0)

        each(devices, spread, lambda c: c.start())
        each(devices, spread, lambda c: c.wait())
        level[d] = jnp.sum(here[...], axis=0)
        each(n, across, lambda c: c.start())
        each(n, across, lambda c: c.wait())
        out[me] = jnp.sum(level[...], axis=0)
        each(devices, give, lambda c: c.start())
        each(devices, give, lambda c: c.wait())

    vm, dma = pltpu.VMEM, pltpu.SemaphoreType.DMA
    return pl.pallas_call(
        kernel,
        out_shape=jax.ShapeDtypeStruct(x.shape, F32),
        in_specs=[pl.BlockSpec(memory_space=pltpu.VMEM)],
        out_specs=pl.BlockSpec(memory_space=pltpu.VMEM),
        scratch_shapes=[vm(x.shape, F32), vm((n, rows, LANES), F32)] + [dma((devices,)), dma((devices,)), dma((n,)), dma((n,)), dma((devices,)), dma((devices,))],
        compiler_params=pltpu.CompilerParams(
            collective_id=cid, has_side_effects=True, vmem_limit_bytes=16 * MIB
        ),
    )(x)


def rows_first(x):
    return with_layout_constraint(x, Layout(major_to_minor=tuple(range(x.ndim))))


def own_part(w, axis):
    length = w.shape[axis] // lax.axis_size("dp")
    return lax.dynamic_slice_in_dim(w, lax.axis_index("dp") * length, length, axis)


def fold(w, rows):
    return w[:rows], jnp.pad(w[rows:], ((0, 2 * rows - w.shape[0]), (0, 0)))


def core_first(x, devices):
    shape = x.shape
    return x.reshape(shape[:-1] + (devices // 2, 2, -1)).swapaxes(-3, -2).reshape(shape)


def core_last(x, devices):
    shape = x.shape
    return x.reshape(shape[:-1] + (2, devices // 2, -1)).swapaxes(-3, -2).reshape(shape)


def layer_norm(values, gain):
    centre = jnp.mean(values, -1, keepdims=True)
    centred = values - centre
    variance = jnp.mean(centred * centred, -1, keepdims=True)
    return centred * lax.rsqrt(variance + 1e-06) * gain


def per_device(
    hr_in,
    low_in,
    valid,
    conv_w,
    hr_gain,
    cn_up,
    cn_down,
    ad_gate,
    ad_high,
    ad_out,
    ln1_gain,
    w_qkv,
    w_proj,
    ln2_gain,
    w_up,
    w_down,
    cot_low,
    cot_hr,
):
    _, row_count, col_count, chan_count = hr_in.shape
    devices, shards = lax.axis_size("dp"), lax.axis_size("mp")
    dims = low_in.shape[2]
    share = dims // devices
    qkv = own_part(w_qkv, 1)
    pieces = [
        own_part(ad_gate, 0), own_part(ad_out, 1).T, *fold(own_part(ad_high, 0), share),
        qkv[0], qkv[1], qkv[2], own_part(w_proj, 1).T, own_part(w_up, 0), own_part(w_down, 1).T,
    ]
    packed = rows_first(jnp.concatenate(pieces, axis=1))
    packed = rows_first(lax.all_gather(packed, "mp", axis=0, tiled=True))
    plane_mask = valid[0].astype(F32)
    cell_mask = plane_mask[..., None]
    masked = hr_in[0] * valid[0].astype(BF)[..., None]
    half_rows, half_cols = (row_count // 2, col_count // 2)
    counts = plane_mask.reshape(half_rows, 2, half_cols, 2).sum(axis=(1, 3))
    shares = 1.0 / jnp.maximum(counts, 1.0)
    size = conv_w.shape[0]
    taps = conv_w.astype(F32).reshape(size * size, 1, chan_count)
    conv_out, bordered = conv_forward(masked, taps, size, shards)
    hr_gainf = hr_gain.astype(F32)
    normed = layer_norm(conv_out * cell_mask, hr_gainf).astype(BF)
    normed, packed = lax.optimization_barrier((normed, packed))
    packed = rows_first(lax.all_gather(packed, "dp", axis=0, tiled=True))
    hr_out, pooled, normed_all, hidden_act, hidden_slope = big_forward(
        normed.reshape(row_count * col_count, chan_count), cn_up, cn_down, masked, plane_mask, shares, shards
    )
    hr_out = hr_out.reshape(hr_in.shape)
    tokens = half_rows * half_cols
    by_share = pooled.reshape(tokens, devices, -1)
    pool_a = by_share[:, :, :share].reshape(tokens, dims)
    pool_b = jnp.pad(by_share[:, :, share:], ((0, 0), (0, 0), (0, 2 * share - by_share.shape[2]))).reshape(tokens, dims)
    low_out, d_low_in, d_pool_a, d_pool_b, g_ln1, g_ln2, low_grads = low_stage(
        *(core_first(v, devices) for v in (low_in[0], pool_a, pool_b, cot_low[0])),
        *(core_first(v.astype(F32), devices)[None] for v in (ln1_gain, ln2_gain)),
        packed, shards, devices, 2,
    )
    low_out = core_last(low_out, devices)[None]
    d_low_in = core_last(d_low_in, devices)[None]
    g_ln1, g_ln2 = core_last(g_ln1[0], devices), core_last(g_ln2[0], devices)
    d_pooled = jnp.concatenate(
        [
            core_last(d_pool_a, devices).reshape(tokens, devices, share),
            core_last(d_pool_b, devices).reshape(tokens, devices, share)[:, :, : by_share.shape[2] - share],
        ],
        axis=2,
    )
    d_normed, d_map, cn_grads, low_sums = big_backward(
        cot_hr[0], d_pooled.reshape(tokens, chan_count), shares, plane_mask, normed_all, hidden_act, hidden_slope,
        cn_up, cn_down, low_grads, shards, devices,
    )
    low_sums = rows_first(low_sums.reshape(shards, share, -1))
    low_sums = rows_first(lax.psum_scatter(low_sums, "mp", scatter_dimension=0))
    d_hr_in, g_conv, g_hr_gain, (g_cn_up, g_cn_down) = conv_backward(
        d_normed, conv_out, hr_gainf[None], cell_mask, bordered, d_map, taps, size, cn_grads, devices, shards
    )
    d_hr_in = d_hr_in[None]
    g_cn_up, g_cn_down = g_cn_up.astype(F32), g_cn_down.astype(F32).T
    g_conv = g_conv.reshape(conv_w.shape)
    small = (g_conv, g_hr_gain, g_ln1, g_ln2)
    flat = jnp.concatenate([g.reshape(-1) for g in small])
    room = -(-flat.size // (devices * 8 * LANES)) * (devices * 8 * LANES)
    flat = jnp.pad(flat, (0, room - flat.size)).reshape(devices, -1, LANES)
    flat, low_sums = lax.optimization_barrier((flat, low_sums))
    flat = sum_everywhere(flat, devices, shards, 4).reshape(-1)
    parts, at = [], 0
    for g in small:
        parts.append(flat[at : at + g.size].reshape(g.shape))
        at += g.size
    g_conv, g_hr_gain, g_ln1, g_ln2 = parts
    own = low_sums.astype(F32)
    split, at = [], 0
    for p in pieces:
        split.append(own[:, at : at + p.shape[1]])
        at += p.shape[1]
    g_ad_gate, g_ad_out, g_high_a, g_high_b, g_query, g_key, g_value, g_proj, g_up, g_down = split
    g_ad_high = jnp.concatenate([g_high_a, g_high_b[: ad_high.shape[0] // devices - share]], axis=0)
    g_qkv = jnp.stack([g_query, g_key, g_value])
    g_ad_out, g_proj, g_down = g_ad_out.T, g_proj.T, g_down.T
    return (
        low_out,
        hr_out,
        d_low_in,
        d_hr_in,
        g_conv,
        g_hr_gain,
        g_cn_up,
        g_cn_down,
        g_ad_gate,
        g_ad_high,
        g_ad_out,
        g_ln1,
        g_qkv,
        g_proj,
        g_ln2,
        g_up,
        g_down,
    )


def solution(mesh):
    return jax.shard_map(
        per_device,
        mesh=mesh,
        in_specs=(
            P("dp", "mp", None, None),
            P("dp", "mp", None),
            P("dp", "mp", None),
            P(),
            P(),
            P(None, "mp"),
            P("mp", None),
            P(None, "mp"),
            P(None, "mp"),
            P("mp", None),
            P(),
            P(None, None, "mp"),
            P("mp", None),
            P(),
            P(None, "mp"),
            P("mp", None),
            P("dp", "mp", None),
            P("dp", "mp", None, None),
        ),
        out_specs=(
            P("dp", "mp", None),
            P("dp", "mp", None, None),
            P("dp", "mp", None),
            P("dp", "mp", None, None),
            P(),
            P(),
            P("dp", "mp"),
            P("mp", "dp"),
            P("dp", "mp"),
            P("dp", "mp"),
            P("mp", "dp"),
            P(),
            P(None, "dp", "mp"),
            P("mp", "dp"),
            P(),
            P("dp", "mp"),
            P("mp", "dp"),
        ),
        check_vma=False,
    )
```

```python
import jax
import jax.numpy as jnp
from jax import lax
from jax.experimental.layout import Layout, with_layout_constraint
from jax.experimental import pallas as pl
from jax.experimental.pallas import tpu as pltpu
from jax.sharding import PartitionSpec as P

HEAD = 64
LANES = 128
EDGE = 8
CHUNKS = 6
TILE = 512
MIB = 1024 * 1024
MESH = pl.DeviceIdType.MESH
BF = jnp.bfloat16
F32 = jnp.float32

def gelu_parts(x):
    c = 0.7978845608028654
    x2 = x * x
    t = jnp.tanh(c * x * (1.0 + 0.044715 * x2))
    half = 0.5 * (1.0 + t)
    slope = half + 0.5 * x * (1.0 - t * t) * (c * (1.0 + 3 * 0.044715 * x2))
    return x * half, slope


def gelu(x):
    c = 0.7978845608028654
    t = jnp.tanh(c * x * (1.0 + 0.044715 * (x * x)))
    return 0.5 * x * (1.0 + t)


def dp_bit(position):
    return lax.rem(lax.axis_index("dp") // 2**position, 2)


def dp_mate(position):
    return lax.axis_index("dp") + 2**position * (1 - 2 * dp_bit(position))


class Halving:
    def __init__(self, bits, lasts, shape, block):
        self.lasts, self.shape, self.block = lasts, shape, block
        left = list(bits)
        self.bits = [left.pop(0 if last else -1) for last in lasts]

    def split(self, count, p):
        if count == 1:
            return (1, 1)
        return (count // 2, 2) if self.lasts[p] else (2, count // 2)

    def buffers(self):
        count, rows, cols = self.shape
        got, held = [], []
        for p in range(len(self.bits)):
            count //= 2
            got.append(jax.ShapeDtypeStruct((count, rows, cols), BF))
            held.append(jax.ShapeDtypeStruct(self.split(count, p + 1) + (rows, cols), BF))
        return got + held

    def semaphores(self):
        return [pltpu.SemaphoreType.DMA((len(self.bits),))] * 2

    def bind(self, first, buffers, send, recv):
        steps = len(self.bits)
        self.now = [first] + list(buffers[steps:])
        self.got, self.send, self.recv = buffers[:steps], send, recv

    def part(self, p, mine):
        bit = dp_bit(self.bits[p])
        index = bit if mine else 1 - bit
        return self.now[p].at[:, index] if self.lasts[p] else self.now[p].at[index]

    def copy(self, p):
        return pltpu.make_async_remote_copy(
            src_ref=self.part(p, False), dst_ref=self.got[p], send_sem=self.send.at[p], recv_sem=self.recv.at[p],
            device_id={"dp": dp_mate(self.bits[p])}, device_id_type=MESH,
        )

    def start(self, p):
        self.copy(p).start()

    def finish(self, p, wait=True):
        if wait:
            self.copy(p).wait()
        count, rows, cols = self.got[p].shape
        ways = self.split(count, p + 1)

        def add(a, b, out):
            out[...] = (a[...].astype(F32) + b[...].astype(F32)).astype(BF).reshape(out.shape)

        flat = pl.BlockSpec((1, rows, self.block), lambda k, c: (k, 0, c))
        paired = pl.BlockSpec((1, 1, rows, self.block), lambda k, c: (k // ways[1], lax.rem(k, ways[1]), 0, c))
        pltpu.emit_pipeline(add, grid=(count, cols // self.block), in_specs=[flat, flat], out_specs=[paired])(
            self.part(p, True), self.got[p], self.now[p + 1]
        )


def chain_exchange(
    n, chunks, lag, gathered, partial, travel, sems, own_chunk, prepare, arrived, compute, mates=(), begin=None, turn=None, after=None
):
    ag_send, ag_recv, rs_send, rs_recv = sems
    d = lax.axis_index("mp")
    has_left, has_right = d > 0, d < n - 1

    barrier = pltpu.get_barrier_semaphore()

    @pl.when(has_left)
    def _():
        pl.semaphore_signal(barrier, inc=1, device_id={"mp": d - 1}, device_id_type=MESH)

    @pl.when(has_right)
    def _():
        pl.semaphore_signal(barrier, inc=1, device_id={"mp": d + 1}, device_id_type=MESH)

    for mate in mates:
        pl.semaphore_signal(barrier, inc=1, device_id={"dp": mate}, device_id_type=MESH)

    own_chunk(0)
    pl.semaphore_wait(barrier, has_left.astype(jnp.int32) + has_right.astype(jnp.int32) + len(mates))
    if begin is not None:
        begin()

    def ag(way, s, j):
        return pltpu.make_async_remote_copy(
            src_ref=gathered.at[s, j], dst_ref=gathered.at[s, j],
            send_sem=ag_send.at[way, s, j], recv_sem=ag_recv.at[s, j],
            device_id={"mp": d + 1 - 2 * way}, device_id_type=MESH,
        )

    def rs(way, s, j):
        there = d + 1 - 2 * way
        slot = jnp.where((s == there) & (way == 0), n, s)
        return pltpu.make_async_remote_copy(
            src_ref=travel.at[s, j], dst_ref=travel.at[slot, j],
            send_sem=rs_send.at[s, j], recv_sem=rs_recv.at[slot, j],
            device_id={"mp": there}, device_id_type=MESH,
        )

    def rs_wait(slot, j):
        pltpu.make_async_copy(travel.at[slot, j], travel.at[slot, j], rs_recv.at[slot, j]).wait()

    def first(j, _):
        @pl.when(j > 0)
        def _():
            own_chunk(j)

        @pl.when(has_right)
        def _():
            ag(0, d, j).start()

        @pl.when(has_left)
        def _():
            ag(1, d, j).start()

        return 0

    lax.fori_loop(0, chunks, first, 0)

    def flow(way, q):
        ql = jnp.clip(q, 0, n * chunks - 1)
        s, jj = ql // chunks, lax.rem(ql, chunks)
        if way == 1:
            s = n - 1 - s
        ahead = (s > d) if way == 0 else (s < d)
        source = has_left if way == 0 else has_right

        @pl.when((q >= 0) & (q < n * chunks) & (ahead | ((s == d) & source)))
        def _():
            @pl.when(source)
            def _():
                rs_wait(jnp.where(s == d, n, s) if way == 0 else s, jj)

            @pl.when(ahead & source)
            def _():
                travel[s, jj] = (partial[s, jj].astype(F32) + travel[s, jj].astype(F32)).astype(BF)

            @pl.when(ahead & jnp.logical_not(source))
            def _():
                travel[s, jj] = partial[s, jj].astype(BF)

            @pl.when(ahead)
            def _():
                rs(way, s, jj).start()

    def step(g, _):
        k, j = g // chunks, lax.rem(g, chunks)
        if turn is not None:
            turn(g)

        @pl.when(g < n * chunks)
        def _():
            def side(way, _):
                s = d - k + 2 * k * way
                ok = (s >= 0) & (s < n) & ((k > 0) | (way == 0))

                @pl.when(ok)
                def _():
                    prepare(way, s, j)

                    @pl.when(k > 0)
                    def _():
                        pltpu.make_async_copy(
                            gathered.at[s, j], gathered.at[s, j], ag_recv.at[s, j]
                        ).wait()

                        @pl.when((way == 0) & has_right)
                        def _():
                            ag(0, s, j).start()

                        @pl.when((way == 1) & has_left)
                        def _():
                            ag(1, s, j).start()

                    arrived(s, j)
                    compute(way, s, j)

                return 0

            lax.fori_loop(0, 2, side, 0)

        flow(1, g - (n - 1 - d) * lag)
        flow(0, g - d * lag)
        if after is not None:
            after(g)
        return 0

    lax.fori_loop(0, n * chunks + (n - 1) * lag, step, 0)

    def drain(i, _):
        s, j = i // chunks, lax.rem(i, chunks)

        @pl.when(has_right & (s <= d))
        def _():
            ag(0, s, j).wait_send()

        @pl.when(has_left & (s >= d))
        def _():
            ag(1, s, j).wait_send()

        @pl.when(s < d)
        def _():
            rs(1, s, j).wait_send()

        @pl.when(s > d)
        def _():
            rs(0, s, j).wait_send()

        return 0

    lax.fori_loop(0, n * chunks, drain, 0)


def own_sum(n, d, j, partial, travel, total):
    total[...] = partial[d, j].astype(F32)

    @pl.when(d > 0)
    def _():
        total[...] += travel[n, j].astype(F32)

    @pl.when(d < n - 1)
    def _():
        total[...] += travel[d, j].astype(F32)


def chain_sems(n, chunks):
    dma = pltpu.SemaphoreType.DMA
    return [dma((2, n, chunks)), dma((n, chunks)), dma((n, chunks)), dma((n + 1, chunks))]


def chunk_buffers(n, rows, c, kept):
    return [
        pltpu.VMEM((n, CHUNKS, rows, c), BF),
        pltpu.VMEM((n, CHUNKS, rows, c), kept),
        pltpu.VMEM((n + 1, CHUNKS, rows, c), BF),
    ]


def columns(i):
    return pl.ds(pl.multiple_of(i * TILE, TILE), TILE)


def drain_copies(n, copy):
    def one(i, _):
        copy(i // CHUNKS, lax.rem(i, CHUNKS)).wait()
        return 0

    lax.fori_loop(0, n * CHUNKS, one, 0)


def big_forward(x, w_up, w_down, residual, mask, share, n):
    t, c = x.shape
    h = w_up.shape[1]
    rows = t // CHUNKS
    cols = residual.shape[1]
    half = cols // 2
    pairs = rows // cols // 2

    def kernel(
        x_ref, wu, wd, res, mask_ref, share_ref, out, pooled, x_all, act_all, slope_all,
        gathered, partial, travel, act, slope, total, folded, copied, stored, load_sem, *sems
    ):
        d = lax.axis_index("mp")
        load = pltpu.make_async_copy(x_ref, gathered.at[d], load_sem)

        def own_chunk(j):
            if isinstance(j, int):
                load.start()
                load.wait()

        def x_copy(s, j):
            return pltpu.make_async_copy(gathered.at[s, j], x_all.at[s, j], copied.at[s, j])

        def prepare(way, s, j):
            pass

        def arrived(s, j):
            x_copy(s, j).start()

        def compute(way, s, j):
            block = gathered.at[s, j]

            def up(i, _):
                pre = jnp.dot(block[...], wu[:, columns(i)], preferred_element_type=F32)
                value, rate = gelu_parts(pre)
                act[:, columns(i)] = value.astype(BF)
                slope[:, columns(i)] = rate.astype(BF)
                return 0

            lax.fori_loop(0, h // TILE, up, 0)
            keep_act = pltpu.make_async_copy(act, act_all.at[s, j], stored.at[0])
            keep_slope = pltpu.make_async_copy(slope, slope_all.at[s, j], stored.at[1])
            keep_act.start()
            keep_slope.start()

            def down(i, _):
                partial[s, j, :, columns(i)] = jnp.dot(
                    act[...], wd[:, columns(i)], preferred_element_type=F32
                )
                return 0

            lax.fori_loop(0, c // TILE, down, 0)
            keep_act.wait()
            keep_slope.wait()

        chain_exchange(n, CHUNKS, 1, gathered, partial, travel, sems, own_chunk, prepare, arrived, compute)

        def finish(j, _):
            own_sum(n, d, j, partial, travel, total)
            values = (res[pl.ds(j * 2 * pairs, 2 * pairs)].reshape(rows, c).astype(F32) + total[...]) * mask_ref[j]
            partial[d, j] = values
            pltpu.make_async_copy(partial.at[d, j], out.at[j], stored.at[0]).start()
            both = values.reshape(pairs, 2, cols, c)
            summed = (both[:, 0] + both[:, 1]).reshape(pairs * cols, c)
            for b in range(c // LANES):
                lanes = slice(b * LANES, (b + 1) * LANES)
                folded[b] = summed[:, lanes]
                every = folded[b, pl.ds(0, pairs * half, 2), :] + folded[b, pl.ds(1, pairs * half, 2), :]
                pooled[j, :, lanes] = (every * share_ref[j]).astype(BF)
            pltpu.make_async_copy(partial.at[d, j], out.at[j], stored.at[0]).wait()
            return 0

        lax.fori_loop(0, CHUNKS, finish, 0)
        drain_copies(n, x_copy)

    whole = pl.BlockSpec(memory_space=pl.ANY)
    local = pl.BlockSpec(memory_space=pltpu.VMEM)
    out, pooled, x_all, act_all, slope_all = pl.pallas_call(
        kernel,
        out_shape=(
            jax.ShapeDtypeStruct((CHUNKS, rows, c), F32),
            jax.ShapeDtypeStruct((CHUNKS, pairs * half, c), BF),
            jax.ShapeDtypeStruct((n, CHUNKS, rows, c), BF),
            jax.ShapeDtypeStruct((n, CHUNKS, rows, h), BF),
            jax.ShapeDtypeStruct((n, CHUNKS, rows, h), BF),
        ),
        in_specs=[whole, local, local, local, local, local],
        out_specs=(whole, local, whole, whole, whole),
        scratch_shapes=chunk_buffers(n, rows, c, F32)
        + [pltpu.VMEM((rows, h), BF)] * 2
        + [pltpu.VMEM((rows, c), F32), pltpu.VMEM((c // LANES, pairs * cols, LANES), F32)]
        + [pltpu.SemaphoreType.DMA((n, CHUNKS)), pltpu.SemaphoreType.DMA((2,)), pltpu.SemaphoreType.DMA]
        + chain_sems(n, CHUNKS),
        compiler_params=pltpu.CompilerParams(
            collective_id=0, has_side_effects=True, vmem_limit_bytes=60 * MIB
        ),
        cost_estimate=pl.CostEstimate(
            flops=4 * n * t * c * h, bytes_accessed=8 * n * t * c, transcendentals=n * t * h
        ),
    )(
        x.reshape(CHUNKS, rows, c), w_up, w_down, residual,
        mask.reshape(CHUNKS, rows, 1), share.reshape(CHUNKS, pairs * half, 1),
    )
    return (
        out.reshape(t, c),
        pooled.reshape(t // 4, c),
        x_all,
        act_all,
        slope_all,
    )


def big_backward(cot, d_pooled, share, mask, x_all, act_all, slope_all, w_up, w_down, grads, n, devices):
    _, cols, c = cot.shape
    t = cot.shape[0] * cols
    h = w_up.shape[1]
    rows = t // CHUNKS
    half = cols // 2
    pairs_here = rows // cols // 2
    piece = c // devices
    items = n * CHUNKS // 2
    pairs, g_rows, g_cols = grads.shape
    bits = range(1, devices.bit_length() - 1)
    split = g_rows // 2
    steps = len(bits)
    plans = [Halving(bits, [last] * steps, (pairs, split, g_cols), min(g_cols, 1024)) for last in (True, False)]
    extras = [b for plan in plans for b in plan.buffers()[:-1]]
    each = 2 * steps - 1

    def kernel(
        cot_ref, pool_ref, share_ref, mask_ref, x_hbm, act_hbm, slopes, wu, wd, g_first, g_second,
        out, d_own, g_up_out, g_down_out, got_up, got_down, h_all, *rest
    ):
        sums, extra, rest = rest[0], rest[1 : 1 + 2 * each], rest[1 + 2 * each :]
        gathered, partial, travel, slope, grad, left, right, middle, g_up, g_down, total, spread_rows = rest[:12]
        core_send, core_recv, stored, send0, recv0, send1, recv1 = rest[12:19]
        sems = rest[19:]
        d = lax.axis_index("mp")
        plans[0].bind(g_first.at[:, :, pl.ds(0, split)], extra[:each] + (sums.at[0],), send0, recv0)
        plans[1].bind(g_second.at[:, :, pl.ds(split, split)], extra[each:] + (sums.at[1],), send1, recv1)

        def begin():
            for plan in plans:
                plan.start(0)

        def pass_on(p):
            for plan in plans:
                plan.finish(p)
            if p + 1 < steps:
                for plan in plans:
                    plan.start(p + 1)

        all_steps = n * CHUNKS + n - 1
        due = [all_steps * (2**steps - 2 ** (steps - 1 - p)) // (2**steps - 1) for p in range(steps)]

        def turn(g):
            for p in range(steps - 1):
                pl.when(g == due[p])(lambda p=p: pass_on(p))

            @pl.when(item_due(g))
            def _():
                for copy in item_copies((g - 3) // 2):
                    copy.start()

        def own_chunk(j):
            part = pool_ref[j] * share_ref[j]
            here = cot_ref.at[pl.ds(j * 2 * pairs_here, 2 * pairs_here)]
            for b in range(c // LANES):
                lanes = slice(b * LANES, (b + 1) * LANES)
                spread_rows[b, pl.ds(0, pairs_here * half, 2), :] = part[:, lanes]
                spread_rows[b, pl.ds(1, pairs_here * half, 2), :] = part[:, lanes]
                block = jnp.broadcast_to(
                    spread_rows[b].reshape(pairs_here, 1, cols, LANES), (pairs_here, 2, cols, LANES)
                ).reshape(rows, LANES)
                cell = here[:, :, lanes].reshape(rows, LANES).astype(F32)
                gathered[d, j, :, lanes] = ((cell + block) * mask_ref[j]).astype(BF)

        def slope_copy(s, j):
            return pltpu.make_async_copy(slopes.at[s, j], slope, stored.at[0])

        def prepare(way, s, j):
            slope_copy(s, j).start()

        def arrived(s, j):
            pass

        def compute(way, s, j):
            block = gathered.at[s, j]
            slope_copy(s, j).wait()

            def up(i, _):
                back = nt(block[...], wd[columns(i), :])
                grad[:, columns(i)] = (back * slope[:, columns(i)].astype(F32)).astype(BF)
                return 0

            lax.fori_loop(0, h // TILE, up, 0)
            half_pair = pl.ds(pl.multiple_of(lax.rem(j, 2) * rows, rows), rows)
            keep = pltpu.make_async_copy(grad, h_all.at[s, j // 2, half_pair], stored.at[1])
            keep.start()

            def down(i, _):
                partial[s, j, :, columns(i)] = nt(grad[...], wu[columns(i), :]).astype(BF)
                return 0

            lax.fori_loop(0, c // TILE, down, 0)
            keep.wait()

        def item_place(q):
            s, jj, base = d, q, CHUNKS // 2
            for k in range(1, n):
                to_left, to_right = d - k >= 0, d + k < n
                two = to_left & to_right
                r = q - base
                here = (r >= 0) & (to_left | to_right)
                s = jnp.where(here, jnp.where(to_left & (jnp.logical_not(two) | (lax.rem(r, 2) == 0)), d - k, d + k), s)
                jj = jnp.where(here, jnp.where(two, r // 2, r), jj)
                base = base + (CHUNKS // 2) * (to_left.astype(jnp.int32) + to_right.astype(jnp.int32))
            return s, jj

        def item_copies(q):
            s, jj = item_place(q)
            return (
                pltpu.make_async_copy(x_hbm.at[s, jj], left, stored.at[2]),
                pltpu.make_async_copy(act_hbm.at[s, jj], right, stored.at[3]),
                pltpu.make_async_copy(h_all.at[s, jj], middle, stored.at[4]),
            )

        def item_due(g):
            return (lax.rem(g, 2) == 1) & (g >= 3) & (g < 2 * items + 3)

        def after(g):
            @pl.when(item_due(g))
            def _():
                q = (g - 3) // 2
                s, jj = item_place(q)
                for copy in item_copies(q):
                    copy.wait()

                def tile(i, _):
                    a = columns(i)
                    g_up[a] += tn(left[:, a], middle[...])
                    db = gathered[s, pl.ds(2 * jj, 2), :, a].reshape(2 * rows, TILE)
                    g_down[a] += tn(db, right[...])
                    return 0

                lax.fori_loop(0, c // TILE, tile, 0)

        def clear(i, _):
            some = pl.ds(pl.multiple_of(i * TILE, TILE), TILE)
            g_up[some] = jnp.zeros((TILE, h), F32)
            g_down[some] = jnp.zeros((TILE, h), F32)
            return 0

        def begin_all():
            begin()
            lax.fori_loop(0, c // TILE, clear, 0)

        chain_exchange(
            n, CHUNKS, 1, gathered, partial, travel, sems, own_chunk, prepare, arrived, compute,
            [dp_mate(b) for b in range(steps + 1)], begin_all, turn, after,
        )
        keep = pltpu.make_async_copy(gathered.at[d], d_own, stored.at[0])
        keep.start()
        core = dp_bit(0)

        def give(i, _):
            some = pl.ds(pl.multiple_of(i * piece, piece), piece)
            left[pl.ds(0, piece)] = g_up[some].astype(BF)
            up = pltpu.make_async_copy(left.at[pl.ds(0, piece)], g_up_out.at[i // 2, lax.rem(i, 2)], stored.at[2])
            up.start()
            right[pl.ds(0, piece)] = g_down[some].astype(BF)
            down = pltpu.make_async_copy(right.at[pl.ds(0, piece)], g_down_out.at[i // 2, lax.rem(i, 2)], stored.at[3])
            down.start()
            up.wait()
            down.wait()
            return 0

        lax.fori_loop(0, devices, give, 0)
        swaps = [
            pltpu.make_async_remote_copy(
                src_ref=src.at[:, 1 - core], dst_ref=dst, send_sem=core_send.at[i], recv_sem=core_recv.at[i],
                device_id={"dp": dp_mate(0)}, device_id_type=MESH,
            )
            for i, (src, dst) in enumerate(((g_up_out, got_up), (g_down_out, got_down)))
        ]
        for swap in swaps:
            swap.start()

        def result(j):
            return pltpu.make_async_copy(total, out.at[j], stored.at[1])

        def finish(j, _):
            @pl.when(j > 0)
            def _():
                result(j - 1).wait()

            own_sum(n, d, j, partial, travel, total)
            result(j).start()
            return 0

        lax.fori_loop(0, CHUNKS, finish, 0)
        result(CHUNKS - 1).wait()
        keep.wait()
        pass_on(steps - 1)
        for swap in swaps:
            swap.wait()

    whole = pl.BlockSpec(memory_space=pl.ANY)
    local = pl.BlockSpec(memory_space=pltpu.VMEM)
    dma = pltpu.SemaphoreType.DMA
    out, d_own, g_up, g_down, got_up, got_down, _, sums, *_ = pl.pallas_call(
        kernel,
        out_shape=(
            jax.ShapeDtypeStruct((CHUNKS, rows, c), F32),
            jax.ShapeDtypeStruct((CHUNKS, rows, c), BF),
            jax.ShapeDtypeStruct((devices // 2, 2, piece, h), BF),
            jax.ShapeDtypeStruct((devices // 2, 2, piece, h), BF),
            jax.ShapeDtypeStruct((devices // 2, piece, h), BF),
            jax.ShapeDtypeStruct((devices // 2, piece, h), BF),
            jax.ShapeDtypeStruct((n, CHUNKS // 2, 2 * rows, h), BF),
            jax.ShapeDtypeStruct((2, 1, 1, split, g_cols), BF),
            *extras,
        ),
        in_specs=[local] * 4 + [whole] * 3 + [local] * 2 + [whole] * 2,
        out_specs=(whole,) * (8 + 2 * each),
        scratch_shapes=chunk_buffers(n, rows, c, BF)
        + [
            pltpu.VMEM((rows, h), BF), pltpu.VMEM((rows, h), BF),
            pltpu.VMEM((2 * rows, c), BF), pltpu.VMEM((2 * rows, h), BF), pltpu.VMEM((2 * rows, h), BF),
            pltpu.VMEM((c, h), F32), pltpu.VMEM((c, h), F32),
            pltpu.VMEM((rows, c), F32), pltpu.VMEM((c // LANES, pairs_here * cols, LANES), F32),
            dma((2,)), dma((2,)), dma((5,)),
        ]
        + plans[0].semaphores() + plans[1].semaphores()
        + chain_sems(n, CHUNKS),
        compiler_params=pltpu.CompilerParams(
            collective_id=1, has_side_effects=True, vmem_limit_bytes=62 * MIB
        ),
        cost_estimate=pl.CostEstimate(
            flops=8 * n * t * c * h, bytes_accessed=8 * n * t * c, transcendentals=0
        ),
    )(
        cot, d_pooled.reshape(CHUNKS, pairs_here * half, c), share.reshape(CHUNKS, pairs_here * half, 1),
        mask.reshape(CHUNKS, rows, 1), *(v.reshape(n, CHUNKS // 2, 2 * rows, -1) for v in (x_all, act_all)),
        slope_all, w_up, w_down,
        grads.reshape(pairs // 2, 2, g_rows, g_cols), grads.reshape(2, pairs // 2, g_rows, g_cols),
    )
    return (
        out.reshape(cot.shape), d_own.reshape(cot.shape), [(g_up, got_up), (g_down, got_down)],
        sums.reshape(g_rows, g_cols),
    )


def frame(dst, src):
    rows, cols, _ = src.shape
    dst[:, :EDGE] = jnp.zeros((rows, EDGE, LANES), F32)
    dst[:, EDGE + cols:] = jnp.zeros((rows, EDGE, LANES), F32)
    dst[:, EDGE:EDGE + cols] = src[...].astype(F32)


def correlate(out, framed, taps, size, flip, group, first=0, last=None, every=1):
    rows, cols, _ = out.shape
    reach = size // 2
    def some(k, _):
        r = first + k * every
        acc = jnp.zeros((group, cols, LANES), F32)
        for a in range(size):
            for b in range(size):
                tap = (size - 1 - a) * size + size - 1 - b if flip else a * size + b
                acc = acc + framed[pl.ds(r * group + a, group), pl.ds(EDGE - reach + b, cols), :] * taps[tap]
        out[pl.ds(r * group, group)] = acc
        return 0
    lax.fori_loop(0, (rows // group if last is None else last) - first if every == 1 else 2, some, 0)


def conv_forward(x, w, size, n):
    rows, cols, c = x.shape
    reach = size // 2

    def kernel(x_ref, w_ref, out, bordered, framed, sent, got, own):
        d = lax.axis_index("mp")
        has_up, has_down = d > 0, d < n - 1
        barrier = pltpu.get_barrier_semaphore()

        @pl.when(has_up)
        def _():
            pl.semaphore_signal(barrier, inc=1, device_id={"mp": d - 1}, device_id_type=MESH)

        @pl.when(has_down)
        def _():
            pl.semaphore_signal(barrier, inc=1, device_id={"mp": d + 1}, device_id_type=MESH)

        keep = pltpu.make_async_copy(x_ref, bordered.at[pl.ds(reach, rows)], own)
        keep.start()
        pl.semaphore_wait(barrier, has_up.astype(jnp.int32) + has_down.astype(jnp.int32))
        up = pltpu.make_async_remote_copy(
            src_ref=x_ref.at[pl.ds(0, reach)], dst_ref=bordered.at[pl.ds(reach + rows, reach)],
            send_sem=sent.at[0], recv_sem=got.at[0], device_id={"mp": d - 1}, device_id_type=MESH,
        )
        down = pltpu.make_async_remote_copy(
            src_ref=x_ref.at[pl.ds(rows - reach, reach)], dst_ref=bordered.at[pl.ds(0, reach)],
            send_sem=sent.at[1], recv_sem=got.at[1], device_id={"mp": d + 1}, device_id_type=MESH,
        )
        nothing = jnp.zeros((reach, cols, c), BF)

        @pl.when(has_up)
        def _():
            up.start()

        @pl.when(has_down)
        def _():
            down.start()

        @pl.when(d == 0)
        def _():
            bordered[:reach] = nothing

        @pl.when(d == n - 1)
        def _():
            bordered[reach + rows :] = nothing

        groups = rows // reach

        def inner(i, _):
            lanes = pl.ds(pl.multiple_of(i * LANES, LANES), LANES)
            frame(framed.at[pl.ds(reach, rows)], x_ref.at[:, :, lanes])
            correlate(out.at[:, :, lanes], framed, w_ref.at[:, :, lanes], size, False, reach, 1, groups - 1)
            return 0

        lax.fori_loop(0, c // LANES, inner, 0)
        keep.wait()

        @pl.when(has_up)
        def _():
            down.wait_recv()

        @pl.when(has_down)
        def _():
            up.wait_recv()

        def block(i, _):
            lanes = pl.ds(pl.multiple_of(i * LANES, LANES), LANES)
            frame(framed, bordered.at[:, :, lanes])
            correlate(out.at[:, :, lanes], framed, w_ref.at[:, :, lanes], size, False, reach, 0, None, groups - 1)
            return 0

        lax.fori_loop(0, c // LANES, block, 0)

        @pl.when(has_up)
        def _():
            up.wait_send()

        @pl.when(has_down)
        def _():
            down.wait_send()

    local = pl.BlockSpec(memory_space=pltpu.VMEM)
    dma = pltpu.SemaphoreType.DMA
    return pl.pallas_call(
        kernel,
        out_shape=(
            jax.ShapeDtypeStruct((rows, cols, c), F32),
            jax.ShapeDtypeStruct((rows + 2 * reach, cols, c), BF),
        ),
        in_specs=[local, local],
        out_specs=(local, local),
        scratch_shapes=[pltpu.VMEM((rows + 2 * reach, cols + 2 * EDGE, LANES), F32), dma((2,)), dma((2,)), dma],
        compiler_params=pltpu.CompilerParams(
            collective_id=5, has_side_effects=True, vmem_limit_bytes=40 * MIB
        ),
    )(x, w)


def conv_backward(d_normed, conv_out, gain, mask, bordered, d_map, w, low_gains, size, grads, devices, n):
    rows, cols, c = conv_out.shape
    reach = size // 2
    high = rows + 2 * reach
    group = 4 if rows % 4 == 0 else 1
    steps = devices.bit_length() - 1
    shape = (devices,) + grads[0][0].shape[2:]
    plans = [Halving(range(steps), [True] + [last] * (steps - 1), shape, shape[2]) for last in (True, False)]
    each = 2 * steps - 1
    blocks = c // LANES
    taps = size * size
    count = taps + 1 + low_gains.shape[0]
    small = -(-count // devices)
    halving = {2 * blocks * 2 * p // (3 * max(steps - 2, 1)): p for p in range(1, steps - 1)}
    rounds = {blocks + blocks // 3: 1, blocks + 2 * blocks // 3: 2}

    def kernel(
        dn, co, gain_ref, mask_ref, w_ref, low_ref, b_hbm, dm_hbm, g0, got0, g1, got1, out, g_all, *rest
    ):
        extra, rest = rest[: 2 * each], rest[2 * each :]
        around, x_around, d_here, dframed, xframed, g_own, here, level, sent, got, own = rest[:11]
        ar, halving_sems = rest[11:17], rest[17:]
        plans[0].bind(g0, (got0,) + extra[:each], halving_sems[0], halving_sems[1])
        plans[1].bind(g1, (got1,) + extra[each:], halving_sems[2], halving_sems[3])
        me, d = lax.axis_index("dp"), lax.axis_index("mp")
        has_up, has_down = d > 0, d < n - 1
        barrier = pltpu.get_barrier_semaphore()

        def greet(k, _):
            pl.semaphore_signal(
                barrier, inc=1, device_id={"dp": lax.rem(me + k, devices)}, device_id_type=MESH
            )
            return 0

        lax.fori_loop(1, devices, greet, 0)
        for k in range(1, n):
            pl.semaphore_signal(barrier, inc=1, device_id={"mp": lax.rem(d + k, n)}, device_id_type=MESH)
        load_x = pltpu.make_async_copy(b_hbm, x_around, own.at[0])
        load_d = pltpu.make_async_copy(dm_hbm, d_here, own.at[1])
        load_x.start()
        load_d.start()

        def pass_on(p):
            for plan in plans:
                plan.finish(p, p > 0)
                if p + 1 < steps:
                    plan.start(p + 1)

        def keep(row, lanes, value):
            g_own[row // small, row % small : row % small + 1, lanes] = value

        pl.semaphore_wait(barrier, devices + n - 2)
        pass_on(0)

        g_own[...] = jnp.zeros(g_own.shape, F32)

        def norm(r, total):
            cells = mask_ref[r]
            back, part = normalise_back(co[r] * cells, gain_ref[...], dn[r])
            around[reach + r] = (back * cells).astype(BF)
            return total + part

        keep(taps, slice(None), lax.fori_loop(0, rows, norm, jnp.zeros((1, c), F32)))
        for i in range(low_gains.shape[0]):
            keep(taps + 1 + i, slice(None), low_ref[i : i + 1])
        up = pltpu.make_async_remote_copy(
            src_ref=around.at[pl.ds(reach, reach)], dst_ref=around.at[pl.ds(reach + rows, reach)],
            send_sem=sent.at[0], recv_sem=got.at[0], device_id={"mp": d - 1}, device_id_type=MESH,
        )
        down = pltpu.make_async_remote_copy(
            src_ref=around.at[pl.ds(rows, reach)], dst_ref=around.at[pl.ds(0, reach)],
            send_sem=sent.at[1], recv_sem=got.at[1], device_id={"mp": d + 1}, device_id_type=MESH,
        )
        nothing = jnp.zeros((reach, cols, c), BF)

        @pl.when(has_up)
        def _():
            up.start()

        @pl.when(has_down)
        def _():
            down.start()

        @pl.when(d == 0)
        def _():
            around[:reach] = nothing

        @pl.when(d == n - 1)
        def _():
            around[reach + rows :] = nothing

        load_x.wait()

        def lanes_of(i):
            return pl.ds(pl.multiple_of(i * LANES, LANES), LANES)

        def kernel_block(i, _):
            lanes = lanes_of(i)
            frame(dframed.at[pl.ds(reach, rows)], around.at[pl.ds(reach, rows), :, lanes])
            frame(xframed, x_around.at[:, :, lanes])
            for a in range(size):
                def some(r, accs):
                    dv = dframed[pl.ds(reach + r * group, group), EDGE : EDGE + cols]
                    new = []
                    for b in range(size):
                        prod = dv * xframed[pl.ds(r * group + a, group), pl.ds(EDGE - reach + b, cols), :]
                        new.append(accs[b] + jnp.sum(prod.reshape(-1, 8, LANES), axis=0))
                    return tuple(new)

                accs = lax.fori_loop(
                    0, rows // group, some, tuple(jnp.zeros((8, LANES), F32) for _ in range(size))
                )
                for b in range(size):
                    keep(a * size + b, lanes, jnp.sum(accs[b], axis=0, keepdims=True))
            return 0

        def input_block(i, _):
            lanes = lanes_of(i)
            frame(dframed, around.at[:, :, lanes])
            correlate(out.at[:, :, lanes], dframed, w_ref.at[:, :, lanes], size, True, group)
            for r in range(rows):
                out[r, :, lanes] = (out[r, :, lanes] + d_here[r, :, lanes].astype(F32)) * mask_ref[r]
            return 0

        def spread(k):
            peer = lax.rem(me + k, devices)
            return pltpu.make_async_remote_copy(
                src_ref=g_own.at[peer], dst_ref=here.at[me], send_sem=ar[0].at[k], recv_sem=ar[1].at[k],
                device_id={"dp": peer}, device_id_type=MESH,
            )

        def across(k):
            return pltpu.make_async_remote_copy(
                src_ref=level.at[d], dst_ref=level.at[d], send_sem=ar[2].at[k], recv_sem=ar[3].at[k],
                device_id={"mp": lax.rem(d + k, n)}, device_id_type=MESH,
            )

        def tell(k):
            return pltpu.make_async_remote_copy(
                src_ref=g_all.at[me], dst_ref=g_all.at[me], send_sem=ar[4].at[k], recv_sem=ar[5].at[k],
                device_id={"dp": lax.rem(me + k, devices)}, device_id_type=MESH,
            )

        def all_of(length, make, act):
            def one(k, _):
                act(make(k))
                return 0

            lax.fori_loop(1, length, one, 0)

        def sum_round(p):
            if p == 0:
                here[me] = g_own[me]
                all_of(devices, spread, lambda x: x.start())
            elif p == 1:
                all_of(devices, spread, lambda x: x.wait())
                level[d] = jnp.sum(here[...], axis=0)
                all_of(n, across, lambda x: x.start())
            elif p == 2:
                all_of(n, across, lambda x: x.wait())
                g_all[me] = jnp.sum(level[...], axis=0)
                all_of(devices, tell, lambda x: x.start())
            else:
                all_of(devices, tell, lambda x: x.wait())

        marks = sorted(set(halving) | set(rounds) | {blocks, 2 * blocks})
        at = 0
        for mark in marks:
            if at < blocks:
                lax.fori_loop(at, min(mark, blocks), kernel_block, 0)
            else:
                lax.fori_loop(at - blocks, mark - blocks, input_block, 0)
            at = mark
            if mark in halving:
                pass_on(halving[mark])
            if mark == blocks:
                sum_round(0)
                load_d.wait()

                @pl.when(has_up)
                def _():
                    down.wait_recv()

                @pl.when(has_down)
                def _():
                    up.wait_recv()
            if mark in rounds:
                sum_round(rounds[mark])
        pass_on(steps - 1)
        sum_round(3)

        @pl.when(has_up)
        def _():
            up.wait_send()

        @pl.when(has_down)
        def _():
            down.wait_send()

    whole = pl.BlockSpec(memory_space=pl.ANY)
    local = pl.BlockSpec(memory_space=pltpu.VMEM)
    vm, dma = pltpu.VMEM, pltpu.SemaphoreType.DMA
    d_in, g_all, *extra = pl.pallas_call(
        kernel,
        out_shape=(
            jax.ShapeDtypeStruct((rows, cols, c), F32),
            jax.ShapeDtypeStruct((devices, small, c), F32),
            *plans[0].buffers()[1:],
            *plans[1].buffers()[1:],
        ),
        in_specs=[local] * 6 + [whole] * 6,
        out_specs=(local,) * 2 + (whole,) * (2 * each),
        scratch_shapes=[
            vm((high, cols, c), BF), vm((high, cols, c), BF), vm((rows, cols, c), BF),
            vm((high, cols + 2 * EDGE, LANES), F32), vm((high, cols + 2 * EDGE, LANES), F32),
            vm((devices, small, c), F32), vm((devices, small, c), F32), vm((n, small, c), F32),
            dma((2,)), dma((2,)), dma((2,)),
            dma((devices,)), dma((devices,)), dma((n,)), dma((n,)), dma((devices,)), dma((devices,)),
        ]
        + plans[0].semaphores() + plans[1].semaphores(),
        compiler_params=pltpu.CompilerParams(
            collective_id=3, has_side_effects=True, vmem_limit_bytes=50 * MIB
        ),
        cost_estimate=pl.CostEstimate(flops=6 * 10**10, bytes_accessed=10**8, transcendentals=0),
    )(d_normed, conv_out, gain, mask, w, low_gains, bordered, d_map, *grads[0], *grads[1])
    sums = g_all.reshape(devices * small, c)[:count]
    return d_in, sums, [extra[each - 1].reshape(shape[1:]), extra[2 * each - 1].reshape(shape[1:])]


GATE, OUT, HIGH_A, HIGH_B, QUERY, KEY, VALUE, PROJ = range(8)
L_LOW, L_DF, L_POOL_A, L_POOL_B, L_FIRST, L_DA, L_SECOND, L_COT = range(8)
R_DGATE, R_MERGE, R_DHIGH, R_DQ, R_DK, R_DV, R_ATT, R_DUP, R_ACT = range(9)


def nn(a, b):
    return jnp.dot(a, b, preferred_element_type=F32)


def nt(a, b):
    return lax.dot_general(a, b, (((1,), (1,)), ((), ())), preferred_element_type=F32)


def tn(a, b):
    return lax.dot_general(a, b, (((0,), (0,)), ((), ())), preferred_element_type=F32)


def normalise(x, gain):
    centred = x - jnp.mean(x, -1, keepdims=True)
    rate = lax.rsqrt(jnp.mean(centred * centred, -1, keepdims=True) + 1e-06)
    return centred * rate * gain


def normalise_back(x, gain, d):
    centred = x - jnp.mean(x, -1, keepdims=True)
    rate = lax.rsqrt(jnp.mean(centred * centred, -1, keepdims=True) + 1e-06)
    hat = centred * rate
    dg = d * gain
    back = rate * (dg - jnp.mean(dg, -1, keepdims=True) - hat * jnp.mean(dg * hat, -1, keepdims=True))
    return back, jnp.sum(d * hat, axis=0, keepdims=True)


def low_stage(low, pool_a, pool_b, cot, gain1, gain2, packed, n, devices, cid):
    t, dim = low.shape
    every = n * t
    width = dim // n
    heads = width // HEAD
    pairs = devices // 2
    rows = dim // devices
    half = dim // 2
    ff = 4 * dim
    scale = HEAD ** (-0.5)

    def kernel(
        low_ref, pool_a_ref, pool_b_ref, cot_ref, gain1_ref, gain2_ref, w_hbm,
        low_out, d_low, d_pool_a, d_pool_b, g_ln1, g_ln2, grads,
        wv, lhs, lhs2, rhs, gate, high, merged, resid, d_res, slope, mixed, heads_in, att_all, d_att, d_mixed,
        d_heads, probs, d_scores, stage, w_sem, q_send, q_got, a_send, a_got, b_send, b_got, c_send, c_got, own_sem,
        l_send, l_got, r_send, r_got, stage_sem,
    ):
        d = lax.axis_index("mp")
        dp = lax.axis_index("dp")
        core = lax.rem(dp, 2)
        mate = dp + 1 - 2 * core
        barrier = pltpu.get_barrier_semaphore()
        for k in range(1, n):
            pl.semaphore_signal(barrier, inc=1, device_id={"mp": lax.rem(d + k, n)}, device_id_type=MESH)
        pl.semaphore_signal(barrier, inc=1, device_id={"dp": mate}, device_id_type=MESH)

        def w_copy(w, k):
            c, z = k // n, lax.rem(k, n)
            wide, base, at = w_place(w)
            src = w_hbm.at[:, c, z, :, pl.ds(base, wide)]
            dst = wv.at[c, :, :, pl.ds(pl.multiple_of(at + z * wide, wide), wide)]
            return pltpu.make_async_copy(src, dst, w_sem.at[w, k])

        def w_place(w):
            if w < 8:
                return width, w * width, w * dim
            return ff // n, 8 * width + (w - 8) * ff // n, 8 * dim + (w - 8) * ff

        def w_each(w, act):
            def one(k, _):
                act(w_copy(w, k))
                return 0

            lax.fori_loop(0, 2 * n, one, 0)

        for w in range(10):
            w_each(w, lambda copy: copy.start())

        def w_wait(*which):
            for w in which:
                w_each(w, lambda copy: copy.wait())

        def w_cols(at, size):
            return wv[:, :, :, pl.ds(at, size)].reshape(dim, size)

        def forward(x, first, count, put):
            def one(i, _):
                put(pl.multiple_of(i * TILE, TILE), nn(x, w_cols(pl.multiple_of(first * dim + i * TILE, TILE), TILE)))
                return 0
            lax.fori_loop(0, count * dim // TILE, one, 0)

        def backward(get, first, count, dst, fresh):
            def one(i, _):
                for c in range(2):
                    part = wv[c, :, :, pl.ds(pl.multiple_of((first + i) * dim, dim), dim)].reshape(half, dim)
                    y = nt(get(pl.multiple_of(i * dim, dim)), part)
                    cols = slice(c * half, (c + 1) * half)
                    if fresh and count == 1:
                        dst[:, cols] = y
                    else:
                        dst[:, cols] += y
                return 0
            if fresh and count > 1:
                dst[...] = jnp.zeros(dst.shape, F32)
            if count == 1:
                one(0, 0)
            else:
                lax.fori_loop(0, count, one, 0)

        def r_cols(block, count=1):
            return pl.ds(block * dim, count * dim)

        def r_at(block):
            return block * dim if block <= R_DUP else block * dim + 3 * dim

        def r_copy(block):
            cols = pl.ds(r_at(block), dim if block < R_DUP else ff)
            return pltpu.make_async_remote_copy(
                src_ref=rhs.at[0, :, cols], dst_ref=rhs.at[1, :, cols], send_sem=r_send.at[block],
                recv_sem=r_got.at[block], device_id={"dp": mate}, device_id_type=MESH)

        def l_copy(i):
            return pltpu.make_async_remote_copy(
                src_ref=lhs.at[i, :, pl.ds(pl.multiple_of((1 - core) * half, half), half)], dst_ref=lhs2.at[i],
                send_sem=l_send.at[i], recv_sem=l_got.at[i], device_id={"dp": mate}, device_id_type=MESH)

        stored = []

        def grad(i, block, at, count, shared=False):
            if not shared:
                r_copy(block).wait_recv()
            own_l = pl.ds(pl.multiple_of(core * half, half), half)

            wide, base, first = w_place(at if at < 8 else 8 + (at - 8) * dim // ff)
            piece = min(TILE, wide)

            def out_copies(slot, k):
                out = []
                for q in range(TILE // piece):
                    z, col = divmod(at * dim - first + k * TILE + q * piece, wide)
                    out.append(
                        pltpu.make_async_copy(
                            stage.at[slot, :, :, pl.ds(q * piece, piece)],
                            grads.at[:, pl.ds(z * rows, rows), pl.ds(base + col, piece)],
                            stage_sem.at[slot, q],
                        )
                    )
                return out

            for k in range(count * dim // TILE):
                slot = len(stored) % 2
                if len(stored) >= 2:
                    wait(stored[-2])
                cols = pl.ds(r_at(block) + k * TILE, TILE)
                y = tn(lhs[i, :, own_l], rhs[0, :, cols]) + tn(lhs2[i], rhs[1, :, cols])
                stage[slot] = y.astype(BF).reshape(pairs, rows, TILE)
                stored.append(out_copies(slot, k))
                start(stored[-1])

        def to_heads(k, src, dst, send, got):
            out = []
            for step in range(1, n):
                peer = lax.rem(d + step, n)
                out.append(pltpu.make_async_remote_copy(
                    src_ref=src.at[:, pl.ds(pl.multiple_of(peer * width, width), width)],
                    dst_ref=dst.at[pl.ds(pl.multiple_of(d * t, t), t)],
                    send_sem=send.at[k, step], recv_sem=got.at[k, step], device_id={"mp": peer}, device_id_type=MESH))
            out.append(pltpu.make_async_copy(
                src.at[:, pl.ds(pl.multiple_of(d * width, width), width)], dst.at[pl.ds(pl.multiple_of(d * t, t), t)], own_sem.at[k]))
            return out

        def to_tokens(k, src, dst, send, got):
            out = []
            for step in range(1, n):
                peer = lax.rem(d + step, n)
                out.append(pltpu.make_async_remote_copy(
                    src_ref=src.at[pl.ds(pl.multiple_of(peer * t, t), t)],
                    dst_ref=dst.at[:, pl.ds(pl.multiple_of(d * width, width), width)],
                    send_sem=send.at[k, step], recv_sem=got.at[k, step], device_id={"mp": peer}, device_id_type=MESH))
            out.append(pltpu.make_async_copy(
                src.at[pl.ds(pl.multiple_of(d * t, t), t)], dst.at[:, pl.ds(pl.multiple_of(d * width, width), width)], own_sem.at[k]))
            return out

        def start(copies):
            for c in copies:
                c.start()

        def wait(copies):
            for c in copies:
                c.wait()

        lhs[L_LOW] = low_ref[...]
        lhs[L_POOL_A] = pool_a_ref[...]
        lhs[L_POOL_B] = pool_b_ref[...]
        lhs[L_COT] = cot_ref[...]
        acc = d_low
        w_wait(GATE)

        def put_gate(at, y):
            gate[:, pl.ds(at, TILE)] = 1.0 / (1.0 + jnp.exp(-y))
        forward(lhs[L_LOW], GATE, 1, put_gate)
        w_wait(HIGH_A, HIGH_B, OUT)

        def put_high(at, y):
            high[:, pl.ds(at, TILE)] = y
        forward(lhs[L_POOL_A], HIGH_A, 1, put_high)

        def put_merging(at, y):
            cols = pl.ds(at, TILE)
            total = high[:, cols] + y
            high[:, cols] = total
            rhs[0, :, pl.ds(R_MERGE * dim + at, TILE)] = (total * gate[:, cols]).astype(BF)
        forward(lhs[L_POOL_B], HIGH_B, 1, put_merging)
        backward(lambda at: rhs[0, :, r_cols(R_MERGE)], OUT, 1, merged, True)
        merged[...] += lhs[L_LOW].astype(F32)
        lhs[L_FIRST] = normalise(merged[...], gain1_ref[...]).astype(BF)

        w_wait(QUERY, KEY, VALUE, PROJ)
        pl.semaphore_wait(barrier, n)
        for i in (L_LOW, L_POOL_A, L_POOL_B, L_COT, L_FIRST):
            l_copy(i).start()
        r_copy(R_MERGE).start()
        out_q = []
        for k in range(3):
            def put_mixed(at, y):
                mixed[k, :, pl.ds(at, TILE)] = y.astype(BF)
            forward(lhs[L_FIRST], QUERY + k, 1, put_mixed)
            copies = to_heads(k, mixed.at[k], heads_in.at[k], q_send, q_got)
            start(copies)
            out_q += copies
        wait(out_q)

        for h in range(heads):
            lanes = slice(h * HEAD, (h + 1) * HEAD)

            def rows_of(b, _):
                some = pl.ds(pl.multiple_of(b * t, t), t)
                s = nt(heads_in[0, some, lanes], heads_in[1, :, lanes]) * scale
                e = jnp.exp(s - jnp.max(s, -1, keepdims=True))
                p = (e * (1.0 / jnp.sum(e, -1, keepdims=True))).astype(BF)
                probs[h, some] = p
                att_all[some, lanes] = nn(p, heads_in[2, :, lanes]).astype(BF)
                return 0
            lax.fori_loop(0, n, rows_of, 0)
        out_a = to_tokens(0, att_all, rhs.at[0, :, r_cols(R_ATT)], a_send, a_got)
        start(out_a)
        wait(out_a)
        r_copy(R_ATT).start()
        backward(lambda at: rhs[0, :, r_cols(R_ATT)], PROJ, 1, resid, True)
        resid[...] += merged[...]
        lhs[L_SECOND] = normalise(resid[...], gain2_ref[...]).astype(BF)
        l_copy(L_SECOND).start()

        w_wait(8)

        def put_up(at, y):
            value, rate = gelu_parts(y)
            rhs[0, :, pl.ds(r_at(R_ACT) + at, TILE)] = value.astype(BF)
            slope[:, pl.ds(at, TILE)] = rate.astype(BF)
        forward(lhs[L_SECOND], 8, 4, put_up)
        r_copy(R_ACT).start()
        w_wait(9)
        backward(lambda at: rhs[0, :, pl.ds(r_at(R_ACT) + at, dim)], 12, 4, acc, True)
        low_out[...] = resid[...] + acc[...]

        def put_d_up(at, y):
            rhs[0, :, pl.ds(r_at(R_DUP) + at, TILE)] = (y * slope[:, pl.ds(at, TILE)].astype(F32)).astype(BF)
        forward(lhs[L_COT], 12, 4, put_d_up)
        r_copy(R_DUP).start()
        backward(lambda at: rhs[0, :, pl.ds(r_at(R_DUP) + at, dim)], 8, 4, acc, True)
        back, g = normalise_back(resid[...], gain2_ref[...], acc[...])
        g_ln2[...] = g
        d_res[...] = lhs[L_COT].astype(F32) + back
        lhs[L_DA] = d_res[...].astype(BF)
        l_copy(L_DA).start()

        def put_d_att(at, y):
            mixed[0, :, pl.ds(at, TILE)] = y.astype(BF)
        forward(lhs[L_DA], PROJ, 1, put_d_att)
        out_b = to_heads(0, mixed.at[0], d_att, b_send, b_got)
        start(out_b)
        l_copy(L_COT).wait_recv()
        grad(L_COT, R_ACT, 12, 4)
        wait(out_b)
        for h in range(heads):
            lanes = slice(h * HEAD, (h + 1) * HEAD)

            def rows_of(b, _):
                some = pl.ds(pl.multiple_of(b * t, t), t)
                p = probs[h, some].astype(F32)
                dp_ = nt(d_att[some, lanes], heads_in[2, :, lanes])
                ds = (p * (dp_ - jnp.sum(dp_ * p, -1, keepdims=True)) * scale).astype(BF)
                d_scores[some] = ds
                d_heads[0, some, lanes] = nn(ds, heads_in[1, :, lanes]).astype(BF)
                return 0
            lax.fori_loop(0, n, rows_of, 0)
            d_heads[1, :, lanes] = tn(d_scores[...], heads_in[0, :, lanes]).astype(BF)
            d_heads[2, :, lanes] = tn(probs[h], d_att[:, lanes]).astype(BF)
        out_c = []
        for k in range(3):
            copies = to_tokens(k, d_heads.at[k], rhs.at[0, :, r_cols(R_DQ + k)], c_send, c_got)
            start(copies)
            out_c += copies
        l_copy(L_SECOND).wait_recv()
        grad(L_SECOND, R_DUP, 8, 4)
        l_copy(L_DA).wait_recv()
        grad(L_DA, R_ATT, PROJ, 1)
        wait(out_c)
        for k in range(3):
            r_copy(R_DQ + k).start()
        backward(lambda at: rhs[0, :, pl.ds(R_DQ * dim + at, dim)], QUERY, 3, acc, True)
        back, g = normalise_back(merged[...], gain1_ref[...], acc[...])
        g_ln1[...] = g
        d_res[...] += back
        lhs[L_DF] = d_res[...].astype(BF)
        l_copy(L_DF).start()

        def put_d_gate(at, y):
            cols = pl.ds(at, TILE)
            gv = gate[:, cols]
            part = y * gv
            rhs[0, :, pl.ds(R_DHIGH * dim + at, TILE)] = part.astype(BF)
            rhs[0, :, pl.ds(R_DGATE * dim + at, TILE)] = (part * high[:, cols] * (1.0 - gv)).astype(BF)
        forward(lhs[L_DF], OUT, 1, put_d_gate)
        r_copy(R_DHIGH).start()
        r_copy(R_DGATE).start()
        backward(lambda at: rhs[0, :, r_cols(R_DHIGH)], HIGH_A, 1, d_pool_a, True)
        backward(lambda at: rhs[0, :, r_cols(R_DHIGH)], HIGH_B, 1, d_pool_b, True)
        backward(lambda at: rhs[0, :, r_cols(R_DGATE)], GATE, 1, acc, True)
        d_low[...] = d_res[...] + acc[...]
        l_copy(L_FIRST).wait_recv()
        for k in range(3):
            grad(L_FIRST, R_DQ + k, QUERY + k, 1)
        l_copy(L_DF).wait_recv()
        grad(L_DF, R_MERGE, OUT, 1)
        l_copy(L_POOL_A).wait_recv()
        grad(L_POOL_A, R_DHIGH, HIGH_A, 1)
        l_copy(L_POOL_B).wait_recv()
        grad(L_POOL_B, R_DHIGH, HIGH_B, 1, shared=True)
        l_copy(L_LOW).wait_recv()
        grad(L_LOW, R_DGATE, GATE, 1)
        wait(stored[-2])
        wait(stored[-1])
        for i in range(8):
            l_copy(i).wait_send()
        for b in range(9):
            r_copy(b).wait_send()

    whole = pl.BlockSpec(memory_space=pl.ANY)
    local = pl.BlockSpec(memory_space=pltpu.VMEM)
    vm, dma = pltpu.VMEM, pltpu.SemaphoreType.DMA
    tok = jax.ShapeDtypeStruct((t, dim), F32)
    one = jax.ShapeDtypeStruct((1, dim), F32)
    return pl.pallas_call(
        kernel,
        out_shape=(tok, tok, tok, tok, one, one, jax.ShapeDtypeStruct((pairs, n * rows, 16 * width), BF)),
        in_specs=[local] * 6 + [whole],
        out_specs=(local,) * 6 + (whole,),
        scratch_shapes=[
            vm((2, pairs, rows, 16 * dim), BF), vm((8, t, dim), BF), vm((8, t, half), BF), vm((2, t, 15 * dim), BF),
            vm((t, dim), F32), vm((t, dim), F32), vm((t, dim), F32), vm((t, dim), F32), vm((t, dim), F32),
            vm((t, ff), BF), vm((3, t, dim), BF), vm((3, every, width), BF), vm((every, width), BF), vm((every, width), BF),
            vm((1, 8, 128), BF), vm((3, every, width), BF), vm((heads, every, every), BF), vm((every, every), BF),
            vm((2, pairs, rows, TILE), BF),
            dma((10, 2 * n)), dma((3, n)), dma((3, n)), dma((1, n)), dma((1, n)), dma((1, n)), dma((1, n)), dma((3, n)), dma((3, n)),
            dma((3,)), dma((8,)), dma((8,)), dma((9,)), dma((9,)), dma((2, 2)),
        ],
        compiler_params=pltpu.CompilerParams(collective_id=cid, has_side_effects=True, vmem_limit_bytes=61 * MIB),
        cost_estimate=pl.CostEstimate(flops=14 * 10**9, bytes_accessed=70 * 10**6, transcendentals=10**7),
    )(low, pool_a, pool_b, cot, gain1, gain2, packed.reshape(pairs, 2, n, rows, 16 * width))
def rows_first(x):
    return with_layout_constraint(x, Layout(major_to_minor=tuple(range(x.ndim))))


def own_part(w, axis):
    length = w.shape[axis] // lax.axis_size("dp")
    return lax.dynamic_slice_in_dim(w, lax.axis_index("dp") * length, length, axis)


def fold(w, rows):
    return w[:rows], jnp.pad(w[rows:], ((0, 2 * rows - w.shape[0]), (0, 0)))


def core_first(x, devices):
    shape = x.shape
    return x.reshape(shape[:-1] + (devices // 2, 2, -1)).swapaxes(-3, -2).reshape(shape)


def core_last(x, devices):
    shape = x.shape
    return x.reshape(shape[:-1] + (2, devices // 2, -1)).swapaxes(-3, -2).reshape(shape)


def layer_norm(values, gain):
    centre = jnp.mean(values, -1, keepdims=True)
    centred = values - centre
    variance = jnp.mean(centred * centred, -1, keepdims=True)
    return centred * lax.rsqrt(variance + 1e-06) * gain


def per_device(
    hr_in,
    low_in,
    valid,
    conv_w,
    hr_gain,
    cn_up,
    cn_down,
    ad_gate,
    ad_high,
    ad_out,
    ln1_gain,
    w_qkv,
    w_proj,
    ln2_gain,
    w_up,
    w_down,
    cot_low,
    cot_hr,
):
    _, row_count, col_count, chan_count = hr_in.shape
    devices, shards = lax.axis_size("dp"), lax.axis_size("mp")
    dims = low_in.shape[2]
    share = dims // devices
    qkv = own_part(w_qkv, 1)
    pieces = [
        own_part(ad_gate, 0), own_part(ad_out, 1).T, *fold(own_part(ad_high, 0), share),
        qkv[0], qkv[1], qkv[2], own_part(w_proj, 1).T, own_part(w_up, 0), own_part(w_down, 1).T,
    ]
    packed = rows_first(jnp.concatenate(pieces, axis=1))
    packed = rows_first(lax.all_gather(packed, "mp", axis=0, tiled=True))
    plane_mask = valid[0].astype(F32)
    cell_mask = plane_mask[..., None]
    masked = hr_in[0] * valid[0].astype(BF)[..., None]
    half_rows, half_cols = (row_count // 2, col_count // 2)
    counts = plane_mask.reshape(half_rows, 2, half_cols, 2).sum(axis=(1, 3))
    shares = 1.0 / jnp.maximum(counts, 1.0)
    size = conv_w.shape[0]
    taps = conv_w.astype(F32).reshape(size * size, 1, chan_count)
    conv_out, bordered = conv_forward(masked, taps, size, shards)
    hr_gainf = hr_gain.astype(F32)
    normed = layer_norm(conv_out * cell_mask, hr_gainf).astype(BF)
    normed, packed = lax.optimization_barrier((normed, packed))
    packed = rows_first(lax.all_gather(packed, "dp", axis=0, tiled=True))
    hr_out, pooled, normed_all, hidden_act, hidden_slope = big_forward(
        normed.reshape(row_count * col_count, chan_count), cn_up, cn_down, masked, plane_mask, shares, shards
    )
    hr_out = hr_out.reshape(hr_in.shape)
    tokens = half_rows * half_cols
    by_share = pooled.reshape(tokens, devices, -1)
    pool_a = by_share[:, :, :share].reshape(tokens, dims)
    pool_b = jnp.pad(by_share[:, :, share:], ((0, 0), (0, 0), (0, 2 * share - by_share.shape[2]))).reshape(tokens, dims)
    low_out, d_low_in, d_pool_a, d_pool_b, g_ln1, g_ln2, low_grads = low_stage(
        *(core_first(v, devices) for v in (low_in[0], pool_a, pool_b, cot_low[0])),
        *(core_first(v.astype(F32), devices)[None] for v in (ln1_gain, ln2_gain)),
        packed, shards, devices, 2,
    )
    low_out = core_last(low_out, devices)[None]
    d_low_in = core_last(d_low_in, devices)[None]
    g_ln1, g_ln2 = core_last(g_ln1[0], devices), core_last(g_ln2[0], devices)
    d_pooled = jnp.concatenate(
        [
            core_last(d_pool_a, devices).reshape(tokens, devices, share),
            core_last(d_pool_b, devices).reshape(tokens, devices, share)[:, :, : by_share.shape[2] - share],
        ],
        axis=2,
    )
    d_normed, d_map, cn_grads, low_sums = big_backward(
        cot_hr[0], d_pooled.reshape(tokens, chan_count), shares, plane_mask, normed_all, hidden_act, hidden_slope,
        cn_up, cn_down, low_grads, shards, devices,
    )
    low_sums = rows_first(low_sums.reshape(shards, share, -1))
    low_sums = rows_first(lax.psum_scatter(low_sums, "mp", scatter_dimension=0))
    low_gains = jnp.pad(jnp.stack([g_ln1, g_ln2]), ((0, 0), (0, chan_count - dims)))
    d_hr_in, small_sums, (g_cn_up, g_cn_down) = conv_backward(
        d_normed, conv_out, hr_gainf[None], cell_mask, bordered, d_map, taps, low_gains, size, cn_grads, devices, shards
    )
    d_hr_in = d_hr_in[None]
    g_cn_up, g_cn_down = g_cn_up.astype(F32), g_cn_down.astype(F32).T
    g_conv = small_sums[: size * size].reshape(conv_w.shape)
    g_hr_gain, g_ln1, g_ln2 = small_sums[size * size], small_sums[-2, :dims], small_sums[-1, :dims]
    own = low_sums.astype(F32)
    split, at = [], 0
    for p in pieces:
        split.append(own[:, at : at + p.shape[1]])
        at += p.shape[1]
    g_ad_gate, g_ad_out, g_high_a, g_high_b, g_query, g_key, g_value, g_proj, g_up, g_down = split
    g_ad_high = jnp.concatenate([g_high_a, g_high_b[: ad_high.shape[0] // devices - share]], axis=0)
    g_qkv = jnp.stack([g_query, g_key, g_value])
    g_ad_out, g_proj, g_down = g_ad_out.T, g_proj.T, g_down.T
    return (
        low_out,
        hr_out,
        d_low_in,
        d_hr_in,
        g_conv,
        g_hr_gain,
        g_cn_up,
        g_cn_down,
        g_ad_gate,
        g_ad_high,
        g_ad_out,
        g_ln1,
        g_qkv,
        g_proj,
        g_ln2,
        g_up,
        g_down,
    )


def solution(mesh):
    return jax.shard_map(
        per_device,
        mesh=mesh,
        in_specs=(
            P("dp", "mp", None, None),
            P("dp", "mp", None),
            P("dp", "mp", None),
            P(),
            P(),
            P(None, "mp"),
            P("mp", None),
            P(None, "mp"),
            P(None, "mp"),
            P("mp", None),
            P(),
            P(None, None, "mp"),
            P("mp", None),
            P(),
            P(None, "mp"),
            P("mp", None),
            P("dp", "mp", None),
            P("dp", "mp", None, None),
        ),
        out_specs=(
            P("dp", "mp", None),
            P("dp", "mp", None, None),
            P("dp", "mp", None),
            P("dp", "mp", None, None),
            P(),
            P(),
            P("dp", "mp"),
            P("mp", "dp"),
            P("dp", "mp"),
            P("dp", "mp"),
            P("mp", "dp"),
            P(),
            P(None, "dp", "mp"),
            P("mp", "dp"),
            P(),
            P("dp", "mp"),
            P("mp", "dp"),
        ),
        check_vma=False,
    )
```

```python
import jax
import jax.numpy as jnp
from jax import lax
from jax.experimental.layout import Layout, with_layout_constraint
from jax.experimental import pallas as pl
from jax.experimental.pallas import tpu as pltpu
from jax.sharding import PartitionSpec as P

HEAD = 64
LANES = 128
EDGE = 8
CHUNKS = 6
TILE = 512
MIB = 1024 * 1024
MESH = pl.DeviceIdType.MESH
BF = jnp.bfloat16
F32 = jnp.float32

def gelu_parts(x):
    c = 0.7978845608028654
    x2 = x * x
    t = jnp.tanh(c * x * (1.0 + 0.044715 * x2))
    half = 0.5 * (1.0 + t)
    slope = half + 0.5 * x * (1.0 - t * t) * (c * (1.0 + 3 * 0.044715 * x2))
    return x * half, slope


def gelu(x):
    c = 0.7978845608028654
    t = jnp.tanh(c * x * (1.0 + 0.044715 * (x * x)))
    return 0.5 * x * (1.0 + t)


def dp_bit(position):
    return lax.rem(lax.axis_index("dp") // 2**position, 2)


def dp_mate(position):
    return lax.axis_index("dp") + 2**position * (1 - 2 * dp_bit(position))


class Halving:
    def __init__(self, bits, lasts, shape, block):
        self.lasts, self.shape, self.block = lasts, shape, block
        left = list(bits)
        self.bits = [left.pop(0 if last else -1) for last in lasts]

    def split(self, count, p):
        if count == 1:
            return (1, 1)
        return (count // 2, 2) if self.lasts[p] else (2, count // 2)

    def buffers(self):
        count, rows, cols = self.shape
        got, held = [], []
        for p in range(len(self.bits)):
            count //= 2
            got.append(jax.ShapeDtypeStruct((count, rows, cols), BF))
            held.append(jax.ShapeDtypeStruct(self.split(count, p + 1) + (rows, cols), BF))
        return got + held

    def semaphores(self):
        return [pltpu.SemaphoreType.DMA((len(self.bits),))] * 2

    def bind(self, first, buffers, send, recv):
        steps = len(self.bits)
        self.now = [first] + list(buffers[steps:])
        self.got, self.send, self.recv = buffers[:steps], send, recv

    def part(self, p, mine):
        bit = dp_bit(self.bits[p])
        index = bit if mine else 1 - bit
        return self.now[p].at[:, index] if self.lasts[p] else self.now[p].at[index]

    def copy(self, p):
        return pltpu.make_async_remote_copy(
            src_ref=self.part(p, False), dst_ref=self.got[p], send_sem=self.send.at[p], recv_sem=self.recv.at[p],
            device_id={"dp": dp_mate(self.bits[p])}, device_id_type=MESH,
        )

    def start(self, p):
        self.copy(p).start()

    def finish(self, p, wait=True):
        if wait:
            self.copy(p).wait()
        count, rows, cols = self.got[p].shape
        ways = self.split(count, p + 1)

        def add(a, b, out):
            out[...] = (a[...].astype(F32) + b[...].astype(F32)).astype(BF).reshape(out.shape)

        flat = pl.BlockSpec((1, rows, self.block), lambda k, c: (k, 0, c))
        paired = pl.BlockSpec((1, 1, rows, self.block), lambda k, c: (k // ways[1], lax.rem(k, ways[1]), 0, c))
        pltpu.emit_pipeline(add, grid=(count, cols // self.block), in_specs=[flat, flat], out_specs=[paired])(
            self.part(p, True), self.got[p], self.now[p + 1]
        )


def chain_exchange(
    n, chunks, lag, gathered, partial, travel, sems, own_chunk, prepare, arrived, compute, mates=(), begin=None, turn=None, after=None, early=False
):
    ag_send, ag_recv, rs_send, rs_recv = sems
    d = lax.axis_index("mp")
    has_left, has_right = d > 0, d < n - 1

    barrier = pltpu.get_barrier_semaphore()

    @pl.when(has_left)
    def _():
        pl.semaphore_signal(barrier, inc=1, device_id={"mp": d - 1}, device_id_type=MESH)

    @pl.when(has_right)
    def _():
        pl.semaphore_signal(barrier, inc=1, device_id={"mp": d + 1}, device_id_type=MESH)

    for mate in mates:
        pl.semaphore_signal(barrier, inc=1, device_id={"dp": mate}, device_id_type=MESH)

    own_chunk(0)
    pl.semaphore_wait(barrier, has_left.astype(jnp.int32) + has_right.astype(jnp.int32) + len(mates))
    if begin is not None:
        begin()

    def ag(way, s, j):
        return pltpu.make_async_remote_copy(
            src_ref=gathered.at[s, j], dst_ref=gathered.at[s, j],
            send_sem=ag_send.at[way, s, j], recv_sem=ag_recv.at[s, j],
            device_id={"mp": d + 1 - 2 * way}, device_id_type=MESH,
        )

    def rs(way, s, j):
        there = d + 1 - 2 * way
        slot = jnp.where((s == there) & (way == 0), n, s)
        return pltpu.make_async_remote_copy(
            src_ref=travel.at[s, j], dst_ref=travel.at[slot, j],
            send_sem=rs_send.at[s, j], recv_sem=rs_recv.at[slot, j],
            device_id={"mp": there}, device_id_type=MESH,
        )

    def rs_wait(slot, j):
        pltpu.make_async_copy(travel.at[slot, j], travel.at[slot, j], rs_recv.at[slot, j]).wait()

    def first(j, _):
        @pl.when(j > 0)
        def _():
            own_chunk(j)

        @pl.when(has_right)
        def _():
            ag(0, d, j).start()

        @pl.when(has_left)
        def _():
            ag(1, d, j).start()

        return 0

    lax.fori_loop(0, chunks, first, 0)

    def flow(way, q):
        ql = jnp.clip(q, 0, n * chunks - 1)
        s, jj = ql // chunks, lax.rem(ql, chunks)
        if way == 1:
            s = n - 1 - s
        ahead = (s > d) if way == 0 else (s < d)
        source = has_left if way == 0 else has_right

        @pl.when((q >= 0) & (q < n * chunks) & (ahead | ((s == d) & source)))
        def _():
            @pl.when(source)
            def _():
                rs_wait(jnp.where(s == d, n, s) if way == 0 else s, jj)

            @pl.when(ahead & source)
            def _():
                travel[s, jj] = (partial[s, jj].astype(F32) + travel[s, jj].astype(F32)).astype(BF)

            @pl.when(ahead & jnp.logical_not(source))
            def _():
                travel[s, jj] = partial[s, jj].astype(BF)

            @pl.when(ahead)
            def _():
                rs(way, s, jj).start()

    def block_of(k, way):
        s = d - k + 2 * k * way
        return s, (s >= 0) & (s < n) & ((k > 0) | (way == 0))

    def receive(k, way, s, j):
        @pl.when(k > 0)
        def _():
            pltpu.make_async_copy(gathered.at[s, j], gathered.at[s, j], ag_recv.at[s, j]).wait()

            @pl.when((way == 0) & has_right)
            def _():
                ag(0, s, j).start()

            @pl.when((way == 1) & has_left)
            def _():
                ag(1, s, j).start()

        arrived(s, j)

    wait_one = 1 if early else 0

    def step(g, _):
        k, j = g // chunks, lax.rem(g, chunks)

        def sides(act):
            @pl.when(g < n * chunks)
            def _():
                def side(way, _):
                    s, ok = block_of(k, way)
                    pl.when(ok)(lambda: act(way, s))
                    return 0

                lax.fori_loop(0, 2, side, 0)

        def flows():
            flow(1, g - wait_one - (n - 1 - d) * lag)
            flow(0, g - wait_one - d * lag)

        if turn is not None:
            turn(g)
        if early:
            sides(lambda way, s: receive(k, way, s, j))
            flows()

            def later(way, s):
                prepare(way, s, j)
                compute(way, s, j)

            sides(later)
        else:
            def work(way, s):
                prepare(way, s, j)
                receive(k, way, s, j)
                compute(way, s, j)

            sides(work)
            flows()
        if after is not None:
            after(g)
        return 0

    lax.fori_loop(0, n * chunks + (n - 1) * lag + wait_one, step, 0)

    def drain(i, _):
        s, j = i // chunks, lax.rem(i, chunks)

        @pl.when(has_right & (s <= d))
        def _():
            ag(0, s, j).wait_send()

        @pl.when(has_left & (s >= d))
        def _():
            ag(1, s, j).wait_send()

        @pl.when(s < d)
        def _():
            rs(1, s, j).wait_send()

        @pl.when(s > d)
        def _():
            rs(0, s, j).wait_send()

        return 0

    lax.fori_loop(0, n * chunks, drain, 0)


def own_sum(n, d, j, partial, travel, total):
    total[...] = partial[d, j].astype(F32)

    @pl.when(d > 0)
    def _():
        total[...] += travel[n, j].astype(F32)

    @pl.when(d < n - 1)
    def _():
        total[...] += travel[d, j].astype(F32)


def chain_sems(n, chunks):
    dma = pltpu.SemaphoreType.DMA
    return [dma((2, n, chunks)), dma((n, chunks)), dma((n, chunks)), dma((n + 1, chunks))]


def chunk_buffers(n, rows, c, kept):
    return [
        pltpu.VMEM((n, CHUNKS, rows, c), BF),
        pltpu.VMEM((n, CHUNKS, rows, c), kept),
        pltpu.VMEM((n + 1, CHUNKS, rows, c), BF),
    ]


def columns(i):
    return pl.ds(pl.multiple_of(i * TILE, TILE), TILE)


def drain_copies(n, copy):
    def one(i, _):
        copy(i // CHUNKS, lax.rem(i, CHUNKS)).wait()
        return 0

    lax.fori_loop(0, n * CHUNKS, one, 0)


def big_forward(x, w_up, w_down, residual, mask, share, n):
    t, c = x.shape
    h = w_up.shape[1]
    rows = t // CHUNKS
    cols = residual.shape[1]
    half = cols // 2
    pairs = rows // cols // 2

    def kernel(
        x_ref, wu, wd, res, mask_ref, share_ref, out, pooled, x_all, act_all, slope_all, wu_t, wd_t,
        gathered, partial, travel, act, slope, total, folded, turned, copied, stored, load_sem, *sems
    ):
        d = lax.axis_index("mp")
        load = pltpu.make_async_copy(x_ref, gathered.at[d], load_sem)

        def own_chunk(j):
            if isinstance(j, int):
                load.start()
                load.wait()

        def x_copy(s, j):
            return pltpu.make_async_copy(gathered.at[s, j], x_all.at[s, j], copied.at[s, j])

        def prepare(way, s, j):
            pass

        def arrived(s, j):
            x_copy(s, j).start()

        def compute(way, s, j):
            block = gathered.at[s, j]

            def up(i, _):
                pre = jnp.dot(block[...], wu[:, columns(i)], preferred_element_type=F32)
                value, rate = gelu_parts(pre)
                act[:, columns(i)] = value.astype(BF)
                slope[:, columns(i)] = rate.astype(BF)
                return 0

            lax.fori_loop(0, h // TILE, up, 0)
            keep_act = pltpu.make_async_copy(act, act_all.at[s, j], stored.at[0])
            keep_slope = pltpu.make_async_copy(slope, slope_all.at[s, j], stored.at[1])
            keep_act.start()
            keep_slope.start()

            def down(i, _):
                partial[s, j, :, columns(i)] = jnp.dot(
                    act[...], wd[:, columns(i)], preferred_element_type=F32
                )
                return 0

            lax.fori_loop(0, c // TILE, down, 0)
            keep_act.wait()
            keep_slope.wait()

        def after(g):
            for i, (w, target, size) in enumerate(((wu, wu_t, h), (wd, wd_t, c))):
                @pl.when(g < size // LANES)
                def _():
                    some = pl.ds(pl.multiple_of(g * LANES, LANES), LANES)
                    turned[i, :, pl.ds(0, w.shape[0])] = w[:, some].T
                    copy = pltpu.make_async_copy(turned.at[i, :, pl.ds(0, w.shape[0])], target.at[some], stored.at[i])
                    copy.start()
                    copy.wait()

        chain_exchange(
            n, CHUNKS, 1, gathered, partial, travel, sems, own_chunk, prepare, arrived, compute, after=after
        )

        def finish(j, _):
            own_sum(n, d, j, partial, travel, total)
            values = (res[pl.ds(j * 2 * pairs, 2 * pairs)].reshape(rows, c).astype(F32) + total[...]) * mask_ref[j]
            partial[d, j] = values
            pltpu.make_async_copy(partial.at[d, j], out.at[j], stored.at[0]).start()
            both = values.reshape(pairs, 2, cols, c)
            summed = (both[:, 0] + both[:, 1]).reshape(pairs * cols, c)
            for b in range(c // LANES):
                lanes = slice(b * LANES, (b + 1) * LANES)
                folded[b] = summed[:, lanes]
                every = folded[b, pl.ds(0, pairs * half, 2), :] + folded[b, pl.ds(1, pairs * half, 2), :]
                pooled[j, :, lanes] = (every * share_ref[j]).astype(BF)
            pltpu.make_async_copy(partial.at[d, j], out.at[j], stored.at[0]).wait()
            return 0

        lax.fori_loop(0, CHUNKS, finish, 0)
        drain_copies(n, x_copy)

    whole = pl.BlockSpec(memory_space=pl.ANY)
    local = pl.BlockSpec(memory_space=pltpu.VMEM)
    out, pooled, x_all, act_all, slope_all, wu_t, wd_t = pl.pallas_call(
        kernel,
        out_shape=(
            jax.ShapeDtypeStruct((CHUNKS, rows, c), F32),
            jax.ShapeDtypeStruct((CHUNKS, pairs * half, c), BF),
            jax.ShapeDtypeStruct((n, CHUNKS, rows, c), BF),
            jax.ShapeDtypeStruct((n, CHUNKS, rows, h), BF),
            jax.ShapeDtypeStruct((n, CHUNKS, rows, h), BF),
            jax.ShapeDtypeStruct((h, c), BF),
            jax.ShapeDtypeStruct((c, h), BF),
        ),
        in_specs=[whole, local, local, local, local, local],
        out_specs=(whole, local, whole, whole, whole, whole, whole),
        scratch_shapes=chunk_buffers(n, rows, c, F32)
        + [pltpu.VMEM((rows, h), BF)] * 2
        + [pltpu.VMEM((rows, c), F32), pltpu.VMEM((c // LANES, pairs * cols, LANES), F32), pltpu.VMEM((2, LANES, max(c, h)), BF)]
        + [pltpu.SemaphoreType.DMA((n, CHUNKS)), pltpu.SemaphoreType.DMA((2,)), pltpu.SemaphoreType.DMA]
        + chain_sems(n, CHUNKS),
        compiler_params=pltpu.CompilerParams(
            collective_id=0, has_side_effects=True, vmem_limit_bytes=60 * MIB
        ),
        cost_estimate=pl.CostEstimate(
            flops=4 * n * t * c * h, bytes_accessed=8 * n * t * c, transcendentals=n * t * h
        ),
    )(
        x.reshape(CHUNKS, rows, c), w_up, w_down, residual,
        mask.reshape(CHUNKS, rows, 1), share.reshape(CHUNKS, pairs * half, 1),
    )
    return (
        out.reshape(t, c),
        pooled.reshape(t // 4, c),
        x_all,
        act_all,
        slope_all,
        wu_t,
        wd_t,
    )


def big_backward(cot, d_pooled, share, mask, x_all, act_all, slope_all, up_t, down_t, grads, n, devices):
    _, cols, c = cot.shape
    t = cot.shape[0] * cols
    h = up_t.shape[0]
    rows = t // CHUNKS
    half = cols // 2
    pairs_here = rows // cols // 2
    piece = c // devices
    items = n * CHUNKS // 2
    pairs, g_rows, g_cols = grads.shape
    bits = range(1, devices.bit_length() - 1)
    split = g_rows // 2
    steps = len(bits)
    plans = [Halving(bits, [last] * steps, (pairs, split, g_cols), min(g_cols, 1024)) for last in (True, False)]
    extras = [b for plan in plans for b in plan.buffers()[:-1]]
    each = 2 * steps - 1

    def kernel(
        cot_ref, pool_ref, share_ref, mask_ref, x_hbm, act_hbm, slopes, wu, wd, g_first, g_second,
        out, d_own, g_up_out, g_down_out, got_up, got_down, h_all, *rest
    ):
        sums, extra, rest = rest[0], rest[1 : 1 + 2 * each], rest[1 + 2 * each :]
        gathered, partial, travel, slope, grad, left, right, middle, g_up, g_down, total, spread_rows = rest[:12]
        core_send, core_recv, stored, send0, recv0, send1, recv1 = rest[12:19]
        sems = rest[19:]
        d = lax.axis_index("mp")
        plans[0].bind(g_first.at[:, :, pl.ds(0, split)], extra[:each] + (sums.at[0],), send0, recv0)
        plans[1].bind(g_second.at[:, :, pl.ds(split, split)], extra[each:] + (sums.at[1],), send1, recv1)

        def begin():
            for plan in plans:
                plan.start(0)

        def pass_on(p, plan):
            plan.finish(p)
            if p + 1 < steps:
                plan.start(p + 1)

        all_steps = n * CHUNKS + n
        due = [all_steps * 9 * (2**steps - 2 ** (steps - 1 - p)) // (10 * (2**steps - 1)) // 2 * 2 for p in range(steps)]

        def turn(g):
            for p in range(steps - 1):
                for i, plan in enumerate(plans):
                    pl.when(g == due[p] + 2 * i)(lambda p=p, plan=plan: pass_on(p, plan))

            q, due_now = item_of(g)

            @pl.when(due_now)
            def _():
                for copy in item_copies(q):
                    copy.start()

        def own_chunk(j):
            part = pool_ref[j] * share_ref[j]
            here = cot_ref.at[pl.ds(j * 2 * pairs_here, 2 * pairs_here)]
            for b in range(c // LANES):
                lanes = slice(b * LANES, (b + 1) * LANES)
                spread_rows[b, pl.ds(0, pairs_here * half, 2), :] = part[:, lanes]
                spread_rows[b, pl.ds(1, pairs_here * half, 2), :] = part[:, lanes]
                block = jnp.broadcast_to(
                    spread_rows[b].reshape(pairs_here, 1, cols, LANES), (pairs_here, 2, cols, LANES)
                ).reshape(rows, LANES)
                cell = here[:, :, lanes].reshape(rows, LANES).astype(F32)
                gathered[d, j, :, lanes] = ((cell + block) * mask_ref[j]).astype(BF)

        def slope_copy(s, j):
            return pltpu.make_async_copy(slopes.at[s, j], slope, stored.at[0])

        def prepare(way, s, j):
            slope_copy(s, j).start()

        def arrived(s, j):
            pass

        def compute(way, s, j):
            block = gathered.at[s, j]
            slope_copy(s, j).wait()

            def up(i, _):
                back = nn(block[...], wd[:, columns(i)])
                grad[:, columns(i)] = (back * slope[:, columns(i)].astype(F32)).astype(BF)
                return 0

            lax.fori_loop(0, h // TILE, up, 0)
            half_pair = pl.ds(pl.multiple_of(lax.rem(j, 2) * rows, rows), rows)
            keep = pltpu.make_async_copy(grad, h_all.at[s, j // 2, half_pair], stored.at[1])
            keep.start()

            def down(i, _):
                partial[s, j, :, columns(i)] = nn(grad[...], wu[:, columns(i)]).astype(BF)
                return 0

            lax.fori_loop(0, c // TILE, down, 0)
            keep.wait()

        def item_place(q):
            s, jj, base = d, q, CHUNKS // 2
            for k in range(1, n):
                to_left, to_right = d - k >= 0, d + k < n
                two = to_left & to_right
                r = q - base
                here = (r >= 0) & (to_left | to_right)
                s = jnp.where(here, jnp.where(to_left & (jnp.logical_not(two) | (lax.rem(r, 2) == 0)), d - k, d + k), s)
                jj = jnp.where(here, jnp.where(two, r // 2, r), jj)
                base = base + (CHUNKS // 2) * (to_left.astype(jnp.int32) + to_right.astype(jnp.int32))
            return s, jj

        def item_copies(q):
            s, jj = item_place(q)
            return (
                pltpu.make_async_copy(x_hbm.at[s, jj], left, stored.at[2]),
                pltpu.make_async_copy(act_hbm.at[s, jj], right, stored.at[3]),
                pltpu.make_async_copy(h_all.at[s, jj], middle, stored.at[4]),
            )

        between = (d > 0) & (d < n - 1)

        def item_of(g):
            q = jnp.where(between, g - items, (g - 3) // 2)
            return q, (q >= 0) & (q < items) & (g >= 3) & (between | (lax.rem(g, 2) == 1))

        def after(g):
            q, due_now = item_of(g)

            @pl.when(due_now)
            def _():
                s, jj = item_place(q)
                for copy in item_copies(q):
                    copy.wait()

                def tile(i, _):
                    a = columns(i)
                    g_up[a] += tn(left[:, a], middle[...])
                    db = gathered[s, pl.ds(2 * jj, 2), :, a].reshape(2 * rows, TILE)
                    g_down[a] += tn(db, right[...])
                    return 0

                lax.fori_loop(0, c // TILE, tile, 0)

            @pl.when(g == 2 * items + 2)
            def _():
                give(g_up, left, g_up_out, stored.at[2])
                swaps[0].start()

            @pl.when(g == 2 * items + 3)
            def _():
                give(g_down, right, g_down_out, stored.at[3])
                swaps[1].start()

        core = dp_bit(0)

        def give(source, stage, target, sem):
            def one(i, _):
                stage[pl.ds(0, piece)] = source[pl.ds(pl.multiple_of(i * piece, piece), piece)].astype(BF)
                copy = pltpu.make_async_copy(stage.at[pl.ds(0, piece)], target.at[i // 2, lax.rem(i, 2)], sem)
                copy.start()
                copy.wait()
                return 0

            lax.fori_loop(0, devices, one, 0)

        swaps = [
            pltpu.make_async_remote_copy(
                src_ref=src.at[:, 1 - core], dst_ref=dst, send_sem=core_send.at[i], recv_sem=core_recv.at[i],
                device_id={"dp": dp_mate(0)}, device_id_type=MESH,
            )
            for i, (src, dst) in enumerate(((g_up_out, got_up), (g_down_out, got_down)))
        ]
        def clear(i, _):
            some = pl.ds(pl.multiple_of(i * TILE, TILE), TILE)
            g_up[some] = jnp.zeros((TILE, h), F32)
            g_down[some] = jnp.zeros((TILE, h), F32)
            return 0

        def begin_all():
            begin()
            lax.fori_loop(0, c // TILE, clear, 0)

        chain_exchange(
            n, CHUNKS, 1, gathered, partial, travel, sems, own_chunk, prepare, arrived, compute,
            [dp_mate(b) for b in range(steps + 1)], begin_all, turn, after, True,
        )
        keep = pltpu.make_async_copy(gathered.at[d], d_own, stored.at[0])
        keep.start()
        def result(j):
            return pltpu.make_async_copy(total, out.at[j], stored.at[1])

        def finish(j, _):
            @pl.when(j > 0)
            def _():
                result(j - 1).wait()

            own_sum(n, d, j, partial, travel, total)
            result(j).start()
            return 0

        lax.fori_loop(0, CHUNKS, finish, 0)
        result(CHUNKS - 1).wait()
        keep.wait()
        for plan in plans:
            pass_on(steps - 1, plan)
        for swap in swaps:
            swap.wait()

    whole = pl.BlockSpec(memory_space=pl.ANY)
    local = pl.BlockSpec(memory_space=pltpu.VMEM)
    dma = pltpu.SemaphoreType.DMA
    out, d_own, g_up, g_down, got_up, got_down, _, sums, *_ = pl.pallas_call(
        kernel,
        out_shape=(
            jax.ShapeDtypeStruct((CHUNKS, rows, c), F32),
            jax.ShapeDtypeStruct((CHUNKS, rows, c), BF),
            jax.ShapeDtypeStruct((devices // 2, 2, piece, h), BF),
            jax.ShapeDtypeStruct((devices // 2, 2, piece, h), BF),
            jax.ShapeDtypeStruct((devices // 2, piece, h), BF),
            jax.ShapeDtypeStruct((devices // 2, piece, h), BF),
            jax.ShapeDtypeStruct((n, CHUNKS // 2, 2 * rows, h), BF),
            jax.ShapeDtypeStruct((2, 1, 1, split, g_cols), BF),
            *extras,
        ),
        in_specs=[local] * 4 + [whole] * 3 + [local] * 2 + [whole] * 2,
        out_specs=(whole,) * (8 + 2 * each),
        scratch_shapes=chunk_buffers(n, rows, c, BF)
        + [
            pltpu.VMEM((rows, h), BF), pltpu.VMEM((rows, h), BF),
            pltpu.VMEM((2 * rows, c), BF), pltpu.VMEM((2 * rows, h), BF), pltpu.VMEM((2 * rows, h), BF),
            pltpu.VMEM((c, h), F32), pltpu.VMEM((c, h), F32),
            pltpu.VMEM((rows, c), F32), pltpu.VMEM((c // LANES, pairs_here * cols, LANES), F32),
            dma((2,)), dma((2,)), dma((5,)),
        ]
        + plans[0].semaphores() + plans[1].semaphores()
        + chain_sems(n, CHUNKS),
        compiler_params=pltpu.CompilerParams(
            collective_id=1, has_side_effects=True, vmem_limit_bytes=62 * MIB
        ),
        cost_estimate=pl.CostEstimate(
            flops=8 * n * t * c * h, bytes_accessed=8 * n * t * c, transcendentals=0
        ),
    )(
        cot, d_pooled.reshape(CHUNKS, pairs_here * half, c), share.reshape(CHUNKS, pairs_here * half, 1),
        mask.reshape(CHUNKS, rows, 1), *(v.reshape(n, CHUNKS // 2, 2 * rows, -1) for v in (x_all, act_all)),
        slope_all, up_t, down_t,
        grads.reshape(pairs // 2, 2, g_rows, g_cols), grads.reshape(2, pairs // 2, g_rows, g_cols),
    )
    return (
        out.reshape(cot.shape), d_own.reshape(cot.shape), [(g_up, got_up), (g_down, got_down)],
        sums.reshape(g_rows, g_cols),
    )


def frame(dst, src):
    rows, cols, _ = src.shape
    dst[:, :EDGE] = jnp.zeros((rows, EDGE, LANES), F32)
    dst[:, EDGE + cols:] = jnp.zeros((rows, EDGE, LANES), F32)
    dst[:, EDGE:EDGE + cols] = src[...].astype(F32)


def correlate(out, framed, taps, size, flip, group, first=0, last=None, every=1):
    rows, cols, _ = out.shape
    reach = size // 2
    def some(k, _):
        r = first + k * every
        acc = jnp.zeros((group, cols, LANES), F32)
        for a in range(size):
            for b in range(size):
                tap = (size - 1 - a) * size + size - 1 - b if flip else a * size + b
                acc = acc + framed[pl.ds(r * group + a, group), pl.ds(EDGE - reach + b, cols), :] * taps[tap]
        out[pl.ds(r * group, group)] = acc
        return 0
    lax.fori_loop(0, (rows // group if last is None else last) - first if every == 1 else 2, some, 0)


def conv_forward(x, w, size, n):
    rows, cols, c = x.shape
    reach = size // 2

    def kernel(x_ref, w_ref, out, bordered, framed, sent, got, own):
        d = lax.axis_index("mp")
        has_up, has_down = d > 0, d < n - 1
        barrier = pltpu.get_barrier_semaphore()

        @pl.when(has_up)
        def _():
            pl.semaphore_signal(barrier, inc=1, device_id={"mp": d - 1}, device_id_type=MESH)

        @pl.when(has_down)
        def _():
            pl.semaphore_signal(barrier, inc=1, device_id={"mp": d + 1}, device_id_type=MESH)

        keep = pltpu.make_async_copy(x_ref, bordered.at[pl.ds(reach, rows)], own)
        keep.start()
        pl.semaphore_wait(barrier, has_up.astype(jnp.int32) + has_down.astype(jnp.int32))
        up = pltpu.make_async_remote_copy(
            src_ref=x_ref.at[pl.ds(0, reach)], dst_ref=bordered.at[pl.ds(reach + rows, reach)],
            send_sem=sent.at[0], recv_sem=got.at[0], device_id={"mp": d - 1}, device_id_type=MESH,
        )
        down = pltpu.make_async_remote_copy(
            src_ref=x_ref.at[pl.ds(rows - reach, reach)], dst_ref=bordered.at[pl.ds(0, reach)],
            send_sem=sent.at[1], recv_sem=got.at[1], device_id={"mp": d + 1}, device_id_type=MESH,
        )
        nothing = jnp.zeros((reach, cols, c), BF)

        @pl.when(has_up)
        def _():
            up.start()

        @pl.when(has_down)
        def _():
            down.start()

        @pl.when(d == 0)
        def _():
            bordered[:reach] = nothing

        @pl.when(d == n - 1)
        def _():
            bordered[reach + rows :] = nothing

        groups = rows // reach

        def inner(i, _):
            lanes = pl.ds(pl.multiple_of(i * LANES, LANES), LANES)
            frame(framed.at[pl.ds(reach, rows)], x_ref.at[:, :, lanes])
            correlate(out.at[:, :, lanes], framed, w_ref.at[:, :, lanes], size, False, reach, 1, groups - 1)
            return 0

        lax.fori_loop(0, c // LANES, inner, 0)
        keep.wait()

        @pl.when(has_up)
        def _():
            down.wait_recv()

        @pl.when(has_down)
        def _():
            up.wait_recv()

        def block(i, _):
            lanes = pl.ds(pl.multiple_of(i * LANES, LANES), LANES)
            frame(framed, bordered.at[:, :, lanes])
            correlate(out.at[:, :, lanes], framed, w_ref.at[:, :, lanes], size, False, reach, 0, None, groups - 1)
            return 0

        lax.fori_loop(0, c // LANES, block, 0)

        @pl.when(has_up)
        def _():
            up.wait_send()

        @pl.when(has_down)
        def _():
            down.wait_send()

    local = pl.BlockSpec(memory_space=pltpu.VMEM)
    dma = pltpu.SemaphoreType.DMA
    return pl.pallas_call(
        kernel,
        out_shape=(
            jax.ShapeDtypeStruct((rows, cols, c), F32),
            jax.ShapeDtypeStruct((rows + 2 * reach, cols, c), BF),
        ),
        in_specs=[local, local],
        out_specs=(local, local),
        scratch_shapes=[pltpu.VMEM((rows + 2 * reach, cols + 2 * EDGE, LANES), F32), dma((2,)), dma((2,)), dma],
        compiler_params=pltpu.CompilerParams(
            collective_id=5, has_side_effects=True, vmem_limit_bytes=40 * MIB
        ),
    )(x, w)


def conv_backward(d_normed, conv_out, gain, mask, bordered, d_map, w, low_gains, size, grads, devices, n):
    rows, cols, c = conv_out.shape
    reach = size // 2
    high = rows + 2 * reach
    group = 4 if rows % 4 == 0 else 1
    steps = devices.bit_length() - 1
    shape = (devices,) + grads[0][0].shape[2:]
    plans = [Halving(range(steps), [True] + [last] * (steps - 1), shape, shape[2]) for last in (True, False)]
    each = 2 * steps - 1
    blocks = c // LANES
    taps = size * size
    count = taps + 1 + low_gains.shape[0]
    small = -(-count // devices)
    halving = {2 * blocks * 2 * p // (3 * max(steps - 2, 1)): p for p in range(1, steps - 1)}
    rounds = {blocks + blocks // 3: 1, blocks + 2 * blocks // 3: 2}

    def kernel(
        dn, co, gain_ref, mask_ref, w_ref, low_ref, b_hbm, dm_hbm, g0, got0, g1, got1, out, g_all, *rest
    ):
        extra, rest = rest[: 2 * each], rest[2 * each :]
        around, x_around, d_here, dframed, xframed, g_own, here, level, sent, got, own = rest[:11]
        ar, halving_sems = rest[11:17], rest[17:]
        plans[0].bind(g0, (got0,) + extra[:each], halving_sems[0], halving_sems[1])
        plans[1].bind(g1, (got1,) + extra[each:], halving_sems[2], halving_sems[3])
        me, d = lax.axis_index("dp"), lax.axis_index("mp")
        has_up, has_down = d > 0, d < n - 1
        barrier = pltpu.get_barrier_semaphore()

        def greet(k, _):
            pl.semaphore_signal(
                barrier, inc=1, device_id={"dp": lax.rem(me + k, devices)}, device_id_type=MESH
            )
            return 0

        lax.fori_loop(1, devices, greet, 0)
        for k in range(1, n):
            pl.semaphore_signal(barrier, inc=1, device_id={"mp": lax.rem(d + k, n)}, device_id_type=MESH)
        load_x = pltpu.make_async_copy(b_hbm, x_around, own.at[0])
        load_d = pltpu.make_async_copy(dm_hbm, d_here, own.at[1])
        load_x.start()
        load_d.start()

        def pass_on(p):
            for plan in plans:
                plan.finish(p, p > 0)
                if p + 1 < steps:
                    plan.start(p + 1)

        def keep(row, lanes, value):
            g_own[row // small, row % small : row % small + 1, lanes] = value

        pl.semaphore_wait(barrier, devices + n - 2)
        pass_on(0)

        g_own[...] = jnp.zeros(g_own.shape, F32)

        def norm(r, total):
            cells = mask_ref[r]
            back, part = normalise_back(co[r] * cells, gain_ref[...], dn[r])
            around[reach + r] = (back * cells).astype(BF)
            return total + part

        keep(taps, slice(None), lax.fori_loop(0, rows, norm, jnp.zeros((1, c), F32)))
        for i in range(low_gains.shape[0]):
            keep(taps + 1 + i, slice(None), low_ref[i : i + 1])
        up = pltpu.make_async_remote_copy(
            src_ref=around.at[pl.ds(reach, reach)], dst_ref=around.at[pl.ds(reach + rows, reach)],
            send_sem=sent.at[0], recv_sem=got.at[0], device_id={"mp": d - 1}, device_id_type=MESH,
        )
        down = pltpu.make_async_remote_copy(
            src_ref=around.at[pl.ds(rows, reach)], dst_ref=around.at[pl.ds(0, reach)],
            send_sem=sent.at[1], recv_sem=got.at[1], device_id={"mp": d + 1}, device_id_type=MESH,
        )
        nothing = jnp.zeros((reach, cols, c), BF)

        @pl.when(has_up)
        def _():
            up.start()

        @pl.when(has_down)
        def _():
            down.start()

        @pl.when(d == 0)
        def _():
            around[:reach] = nothing

        @pl.when(d == n - 1)
        def _():
            around[reach + rows :] = nothing

        load_x.wait()

        def lanes_of(i):
            return pl.ds(pl.multiple_of(i * LANES, LANES), LANES)

        def kernel_block(i, _):
            lanes = lanes_of(i)
            frame(dframed.at[pl.ds(reach, rows)], around.at[pl.ds(reach, rows), :, lanes])
            frame(xframed, x_around.at[:, :, lanes])
            for a in range(size):
                def some(r, accs):
                    dv = dframed[pl.ds(reach + r * group, group), EDGE : EDGE + cols]
                    new = []
                    for b in range(size):
                        prod = dv * xframed[pl.ds(r * group + a, group), pl.ds(EDGE - reach + b, cols), :]
                        new.append(accs[b] + jnp.sum(prod.reshape(-1, 8, LANES), axis=0))
                    return tuple(new)

                accs = lax.fori_loop(
                    0, rows // group, some, tuple(jnp.zeros((8, LANES), F32) for _ in range(size))
                )
                for b in range(size):
                    keep(a * size + b, lanes, jnp.sum(accs[b], axis=0, keepdims=True))
            return 0

        def input_block(i, _):
            lanes = lanes_of(i)
            frame(dframed, around.at[:, :, lanes])
            correlate(out.at[:, :, lanes], dframed, w_ref.at[:, :, lanes], size, True, group)
            for r in range(rows):
                out[r, :, lanes] = (out[r, :, lanes] + d_here[r, :, lanes].astype(F32)) * mask_ref[r]
            return 0

        def spread(k):
            peer = lax.rem(me + k, devices)
            return pltpu.make_async_remote_copy(
                src_ref=g_own.at[peer], dst_ref=here.at[me], send_sem=ar[0].at[k], recv_sem=ar[1].at[k],
                device_id={"dp": peer}, device_id_type=MESH,
            )

        def across(k):
            return pltpu.make_async_remote_copy(
                src_ref=level.at[d], dst_ref=level.at[d], send_sem=ar[2].at[k], recv_sem=ar[3].at[k],
                device_id={"mp": lax.rem(d + k, n)}, device_id_type=MESH,
            )

        def tell(k):
            return pltpu.make_async_remote_copy(
                src_ref=g_all.at[me], dst_ref=g_all.at[me], send_sem=ar[4].at[k], recv_sem=ar[5].at[k],
                device_id={"dp": lax.rem(me + k, devices)}, device_id_type=MESH,
            )

        def all_of(length, make, act):
            def one(k, _):
                act(make(k))
                return 0

            lax.fori_loop(1, length, one, 0)

        def sum_round(p):
            if p == 0:
                here[me] = g_own[me]
                all_of(devices, spread, lambda x: x.start())
            elif p == 1:
                all_of(devices, spread, lambda x: x.wait())
                level[d] = jnp.sum(here[...], axis=0)
                all_of(n, across, lambda x: x.start())
            elif p == 2:
                all_of(n, across, lambda x: x.wait())
                g_all[me] = jnp.sum(level[...], axis=0)
                all_of(devices, tell, lambda x: x.start())
            else:
                all_of(devices, tell, lambda x: x.wait())

        marks = sorted(set(halving) | set(rounds) | {blocks, 2 * blocks})
        at = 0
        for mark in marks:
            if at < blocks:
                lax.fori_loop(at, min(mark, blocks), kernel_block, 0)
            else:
                lax.fori_loop(at - blocks, mark - blocks, input_block, 0)
            at = mark
            if mark in halving:
                pass_on(halving[mark])
            if mark == blocks:
                sum_round(0)
                load_d.wait()

                @pl.when(has_up)
                def _():
                    down.wait_recv()

                @pl.when(has_down)
                def _():
                    up.wait_recv()
            if mark in rounds:
                sum_round(rounds[mark])
        pass_on(steps - 1)
        sum_round(3)

        @pl.when(has_up)
        def _():
            up.wait_send()

        @pl.when(has_down)
        def _():
            down.wait_send()

    whole = pl.BlockSpec(memory_space=pl.ANY)
    local = pl.BlockSpec(memory_space=pltpu.VMEM)
    vm, dma = pltpu.VMEM, pltpu.SemaphoreType.DMA
    d_in, g_all, *extra = pl.pallas_call(
        kernel,
        out_shape=(
            jax.ShapeDtypeStruct((rows, cols, c), F32),
            jax.ShapeDtypeStruct((devices, small, c), F32),
            *plans[0].buffers()[1:],
            *plans[1].buffers()[1:],
        ),
        in_specs=[local] * 6 + [whole] * 6,
        out_specs=(local,) * 2 + (whole,) * (2 * each),
        scratch_shapes=[
            vm((high, cols, c), BF), vm((high, cols, c), BF), vm((rows, cols, c), BF),
            vm((high, cols + 2 * EDGE, LANES), F32), vm((high, cols + 2 * EDGE, LANES), F32),
            vm((devices, small, c), F32), vm((devices, small, c), F32), vm((n, small, c), F32),
            dma((2,)), dma((2,)), dma((2,)),
            dma((devices,)), dma((devices,)), dma((n,)), dma((n,)), dma((devices,)), dma((devices,)),
        ]
        + plans[0].semaphores() + plans[1].semaphores(),
        compiler_params=pltpu.CompilerParams(
            collective_id=3, has_side_effects=True, vmem_limit_bytes=50 * MIB
        ),
        cost_estimate=pl.CostEstimate(flops=6 * 10**10, bytes_accessed=10**8, transcendentals=0),
    )(d_normed, conv_out, gain, mask, w, low_gains, bordered, d_map, *grads[0], *grads[1])
    sums = g_all.reshape(devices * small, c)[:count]
    return d_in, sums, [extra[each - 1].reshape(shape[1:]), extra[2 * each - 1].reshape(shape[1:])]


GATE, OUT, HIGH_A, HIGH_B, QUERY, KEY, VALUE, PROJ = range(8)
L_LOW, L_DF, L_POOL_A, L_POOL_B, L_FIRST, L_DA, L_SECOND, L_COT = range(8)
R_DGATE, R_MERGE, R_DHIGH, R_DQ, R_DK, R_DV, R_ATT, R_DUP, R_ACT = range(9)


def nn(a, b):
    return jnp.dot(a, b, preferred_element_type=F32)


def nt(a, b):
    return lax.dot_general(a, b, (((1,), (1,)), ((), ())), preferred_element_type=F32)


def tn(a, b):
    return lax.dot_general(a, b, (((0,), (0,)), ((), ())), preferred_element_type=F32)


def normalise(x, gain):
    centred = x - jnp.mean(x, -1, keepdims=True)
    rate = lax.rsqrt(jnp.mean(centred * centred, -1, keepdims=True) + 1e-06)
    return centred * rate * gain


def normalise_back(x, gain, d):
    centred = x - jnp.mean(x, -1, keepdims=True)
    rate = lax.rsqrt(jnp.mean(centred * centred, -1, keepdims=True) + 1e-06)
    hat = centred * rate
    dg = d * gain
    back = rate * (dg - jnp.mean(dg, -1, keepdims=True) - hat * jnp.mean(dg * hat, -1, keepdims=True))
    return back, jnp.sum(d * hat, axis=0, keepdims=True)


def low_stage(low, pool_a, pool_b, cot, gain1, gain2, packed, n, devices, cid):
    t, dim = low.shape
    every = n * t
    width = dim // n
    heads = width // HEAD
    pairs = devices // 2
    rows = dim // devices
    half = dim // 2
    ff = 4 * dim
    scale = HEAD ** (-0.5)

    def kernel(
        low_ref, pool_a_ref, pool_b_ref, cot_ref, gain1_ref, gain2_ref, w_hbm,
        low_out, d_low, d_pool_a, d_pool_b, g_ln1, g_ln2, grads,
        wv, lhs, lhs2, rhs, gate, high, merged, resid, d_res, slope, mixed, heads_in, att_all, d_att, d_mixed,
        d_heads, probs, d_scores, stage, w_sem, q_send, q_got, a_send, a_got, b_send, b_got, c_send, c_got, own_sem,
        l_send, l_got, r_send, r_got, stage_sem,
    ):
        d = lax.axis_index("mp")
        dp = lax.axis_index("dp")
        core = lax.rem(dp, 2)
        mate = dp + 1 - 2 * core
        barrier = pltpu.get_barrier_semaphore()
        for k in range(1, n):
            pl.semaphore_signal(barrier, inc=1, device_id={"mp": lax.rem(d + k, n)}, device_id_type=MESH)
        pl.semaphore_signal(barrier, inc=1, device_id={"dp": mate}, device_id_type=MESH)

        def w_copy(w, k):
            c, z = k // n, lax.rem(k, n)
            wide, base, at = w_place(w)
            src = w_hbm.at[:, c, z, :, pl.ds(base, wide)]
            dst = wv.at[c, :, :, pl.ds(pl.multiple_of(at + z * wide, wide), wide)]
            return pltpu.make_async_copy(src, dst, w_sem.at[w, k])

        def w_place(w):
            if w < 8:
                return width, w * width, w * dim
            return ff // n, 8 * width + (w - 8) * ff // n, 8 * dim + (w - 8) * ff

        def w_each(w, act):
            def one(k, _):
                act(w_copy(w, k))
                return 0

            lax.fori_loop(0, 2 * n, one, 0)

        for w in range(10):
            w_each(w, lambda copy: copy.start())

        def w_wait(*which):
            for w in which:
                w_each(w, lambda copy: copy.wait())

        def w_cols(at, size):
            return wv[:, :, :, pl.ds(at, size)].reshape(dim, size)

        def forward(x, first, count, put):
            def one(i, _):
                put(pl.multiple_of(i * TILE, TILE), nn(x, w_cols(pl.multiple_of(first * dim + i * TILE, TILE), TILE)))
                return 0
            lax.fori_loop(0, count * dim // TILE, one, 0)

        def backward(get, first, count, dst, fresh):
            def one(i, _):
                for c in range(2):
                    part = wv[c, :, :, pl.ds(pl.multiple_of((first + i) * dim, dim), dim)].reshape(half, dim)
                    y = nt(get(pl.multiple_of(i * dim, dim)), part)
                    cols = slice(c * half, (c + 1) * half)
                    if fresh and count == 1:
                        dst[:, cols] = y
                    else:
                        dst[:, cols] += y
                return 0
            if fresh and count > 1:
                dst[...] = jnp.zeros(dst.shape, F32)
            if count == 1:
                one(0, 0)
            else:
                lax.fori_loop(0, count, one, 0)

        def r_cols(block, count=1):
            return pl.ds(block * dim, count * dim)

        def r_at(block):
            return block * dim if block <= R_DUP else block * dim + 3 * dim

        def r_copy(block):
            cols = pl.ds(r_at(block), dim if block < R_DUP else ff)
            return pltpu.make_async_remote_copy(
                src_ref=rhs.at[0, :, cols], dst_ref=rhs.at[1, :, cols], send_sem=r_send.at[block],
                recv_sem=r_got.at[block], device_id={"dp": mate}, device_id_type=MESH)

        def l_copy(i):
            return pltpu.make_async_remote_copy(
                src_ref=lhs.at[i, :, pl.ds(pl.multiple_of((1 - core) * half, half), half)], dst_ref=lhs2.at[i],
                send_sem=l_send.at[i], recv_sem=l_got.at[i], device_id={"dp": mate}, device_id_type=MESH)

        stored = []

        def grad(i, block, at, count, shared=False):
            if not shared:
                r_copy(block).wait_recv()
            own_l = pl.ds(pl.multiple_of(core * half, half), half)

            wide, base, first = w_place(at if at < 8 else 8 + (at - 8) * dim // ff)
            piece = min(TILE, wide)

            def out_copies(slot, k):
                out = []
                for q in range(TILE // piece):
                    z, col = divmod(at * dim - first + k * TILE + q * piece, wide)
                    out.append(
                        pltpu.make_async_copy(
                            stage.at[slot, :, :, pl.ds(q * piece, piece)],
                            grads.at[:, pl.ds(z * rows, rows), pl.ds(base + col, piece)],
                            stage_sem.at[slot, q],
                        )
                    )
                return out

            for k in range(count * dim // TILE):
                slot = len(stored) % 2
                if len(stored) >= 2:
                    wait(stored[-2])
                cols = pl.ds(r_at(block) + k * TILE, TILE)
                y = tn(lhs[i, :, own_l], rhs[0, :, cols]) + tn(lhs2[i], rhs[1, :, cols])
                stage[slot] = y.astype(BF).reshape(pairs, rows, TILE)
                stored.append(out_copies(slot, k))
                start(stored[-1])

        def to_heads(k, src, dst, send, got):
            out = []
            for step in range(1, n):
                peer = lax.rem(d + step, n)
                out.append(pltpu.make_async_remote_copy(
                    src_ref=src.at[:, pl.ds(pl.multiple_of(peer * width, width), width)],
                    dst_ref=dst.at[pl.ds(pl.multiple_of(d * t, t), t)],
                    send_sem=send.at[k, step], recv_sem=got.at[k, step], device_id={"mp": peer}, device_id_type=MESH))
            out.append(pltpu.make_async_copy(
                src.at[:, pl.ds(pl.multiple_of(d * width, width), width)], dst.at[pl.ds(pl.multiple_of(d * t, t), t)], own_sem.at[k]))
            return out

        def to_tokens(k, src, dst, send, got):
            out = []
            for step in range(1, n):
                peer = lax.rem(d + step, n)
                out.append(pltpu.make_async_remote_copy(
                    src_ref=src.at[pl.ds(pl.multiple_of(peer * t, t), t)],
                    dst_ref=dst.at[:, pl.ds(pl.multiple_of(d * width, width), width)],
                    send_sem=send.at[k, step], recv_sem=got.at[k, step], device_id={"mp": peer}, device_id_type=MESH))
            out.append(pltpu.make_async_copy(
                src.at[pl.ds(pl.multiple_of(d * t, t), t)], dst.at[:, pl.ds(pl.multiple_of(d * width, width), width)], own_sem.at[k]))
            return out

        def start(copies):
            for c in copies:
                c.start()

        def wait(copies):
            for c in copies:
                c.wait()

        lhs[L_LOW] = low_ref[...]
        lhs[L_POOL_A] = pool_a_ref[...]
        lhs[L_POOL_B] = pool_b_ref[...]
        lhs[L_COT] = cot_ref[...]
        acc = d_low
        w_wait(GATE)

        def put_gate(at, y):
            gate[:, pl.ds(at, TILE)] = 1.0 / (1.0 + jnp.exp(-y))
        forward(lhs[L_LOW], GATE, 1, put_gate)
        w_wait(HIGH_A, HIGH_B, OUT)

        def put_high(at, y):
            high[:, pl.ds(at, TILE)] = y
        forward(lhs[L_POOL_A], HIGH_A, 1, put_high)

        def put_merging(at, y):
            cols = pl.ds(at, TILE)
            total = high[:, cols] + y
            high[:, cols] = total
            rhs[0, :, pl.ds(R_MERGE * dim + at, TILE)] = (total * gate[:, cols]).astype(BF)
        forward(lhs[L_POOL_B], HIGH_B, 1, put_merging)
        backward(lambda at: rhs[0, :, r_cols(R_MERGE)], OUT, 1, merged, True)
        merged[...] += lhs[L_LOW].astype(F32)
        lhs[L_FIRST] = normalise(merged[...], gain1_ref[...]).astype(BF)

        w_wait(QUERY, KEY, VALUE, PROJ)
        pl.semaphore_wait(barrier, n)
        for i in (L_LOW, L_POOL_A, L_POOL_B, L_COT, L_FIRST):
            l_copy(i).start()
        r_copy(R_MERGE).start()
        out_q = []
        for k in range(3):
            def put_mixed(at, y):
                mixed[k, :, pl.ds(at, TILE)] = y.astype(BF)
            forward(lhs[L_FIRST], QUERY + k, 1, put_mixed)
            copies = to_heads(k, mixed.at[k], heads_in.at[k], q_send, q_got)
            start(copies)
            out_q += copies
        wait(out_q)

        for h in range(heads):
            lanes = slice(h * HEAD, (h + 1) * HEAD)

            def rows_of(b, _):
                some = pl.ds(pl.multiple_of(b * t, t), t)
                s = nt(heads_in[0, some, lanes], heads_in[1, :, lanes]) * scale
                e = jnp.exp(s - jnp.max(s, -1, keepdims=True))
                p = (e * (1.0 / jnp.sum(e, -1, keepdims=True))).astype(BF)
                probs[h, some] = p
                att_all[some, lanes] = nn(p, heads_in[2, :, lanes]).astype(BF)
                return 0
            lax.fori_loop(0, n, rows_of, 0)
        out_a = to_tokens(0, att_all, rhs.at[0, :, r_cols(R_ATT)], a_send, a_got)
        start(out_a)
        wait(out_a)
        r_copy(R_ATT).start()
        backward(lambda at: rhs[0, :, r_cols(R_ATT)], PROJ, 1, resid, True)
        resid[...] += merged[...]
        lhs[L_SECOND] = normalise(resid[...], gain2_ref[...]).astype(BF)
        l_copy(L_SECOND).start()

        w_wait(8)

        def put_up(at, y):
            value, rate = gelu_parts(y)
            rhs[0, :, pl.ds(r_at(R_ACT) + at, TILE)] = value.astype(BF)
            slope[:, pl.ds(at, TILE)] = rate.astype(BF)
        forward(lhs[L_SECOND], 8, 4, put_up)
        r_copy(R_ACT).start()
        w_wait(9)
        backward(lambda at: rhs[0, :, pl.ds(r_at(R_ACT) + at, dim)], 12, 4, acc, True)
        low_out[...] = resid[...] + acc[...]

        def put_d_up(at, y):
            rhs[0, :, pl.ds(r_at(R_DUP) + at, TILE)] = (y * slope[:, pl.ds(at, TILE)].astype(F32)).astype(BF)
        forward(lhs[L_COT], 12, 4, put_d_up)
        r_copy(R_DUP).start()
        backward(lambda at: rhs[0, :, pl.ds(r_at(R_DUP) + at, dim)], 8, 4, acc, True)
        back, g = normalise_back(resid[...], gain2_ref[...], acc[...])
        g_ln2[...] = g
        d_res[...] = lhs[L_COT].astype(F32) + back
        lhs[L_DA] = d_res[...].astype(BF)
        l_copy(L_DA).start()

        def put_d_att(at, y):
            mixed[0, :, pl.ds(at, TILE)] = y.astype(BF)
        forward(lhs[L_DA], PROJ, 1, put_d_att)
        out_b = to_heads(0, mixed.at[0], d_att, b_send, b_got)
        start(out_b)
        l_copy(L_COT).wait_recv()
        grad(L_COT, R_ACT, 12, 4)
        wait(out_b)
        for h in range(heads):
            lanes = slice(h * HEAD, (h + 1) * HEAD)

            def rows_of(b, _):
                some = pl.ds(pl.multiple_of(b * t, t), t)
                p = probs[h, some].astype(F32)
                dp_ = nt(d_att[some, lanes], heads_in[2, :, lanes])
                ds = (p * (dp_ - jnp.sum(dp_ * p, -1, keepdims=True)) * scale).astype(BF)
                d_scores[some] = ds
                d_heads[0, some, lanes] = nn(ds, heads_in[1, :, lanes]).astype(BF)
                return 0
            lax.fori_loop(0, n, rows_of, 0)
            d_heads[1, :, lanes] = tn(d_scores[...], heads_in[0, :, lanes]).astype(BF)
            d_heads[2, :, lanes] = tn(probs[h], d_att[:, lanes]).astype(BF)
        out_c = []
        for k in range(3):
            copies = to_tokens(k, d_heads.at[k], rhs.at[0, :, r_cols(R_DQ + k)], c_send, c_got)
            start(copies)
            out_c += copies
        l_copy(L_SECOND).wait_recv()
        grad(L_SECOND, R_DUP, 8, 4)
        l_copy(L_DA).wait_recv()
        grad(L_DA, R_ATT, PROJ, 1)
        wait(out_c)
        for k in range(3):
            r_copy(R_DQ + k).start()
        backward(lambda at: rhs[0, :, pl.ds(R_DQ * dim + at, dim)], QUERY, 3, acc, True)
        back, g = normalise_back(merged[...], gain1_ref[...], acc[...])
        g_ln1[...] = g
        d_res[...] += back
        lhs[L_DF] = d_res[...].astype(BF)
        l_copy(L_DF).start()

        def put_d_gate(at, y):
            cols = pl.ds(at, TILE)
            gv = gate[:, cols]
            part = y * gv
            rhs[0, :, pl.ds(R_DHIGH * dim + at, TILE)] = part.astype(BF)
            rhs[0, :, pl.ds(R_DGATE * dim + at, TILE)] = (part * high[:, cols] * (1.0 - gv)).astype(BF)
        forward(lhs[L_DF], OUT, 1, put_d_gate)
        r_copy(R_DHIGH).start()
        r_copy(R_DGATE).start()
        backward(lambda at: rhs[0, :, r_cols(R_DHIGH)], HIGH_A, 1, d_pool_a, True)
        backward(lambda at: rhs[0, :, r_cols(R_DHIGH)], HIGH_B, 1, d_pool_b, True)
        backward(lambda at: rhs[0, :, r_cols(R_DGATE)], GATE, 1, acc, True)
        d_low[...] = d_res[...] + acc[...]
        l_copy(L_FIRST).wait_recv()
        for k in range(3):
            grad(L_FIRST, R_DQ + k, QUERY + k, 1)
        l_copy(L_DF).wait_recv()
        grad(L_DF, R_MERGE, OUT, 1)
        l_copy(L_POOL_A).wait_recv()
        grad(L_POOL_A, R_DHIGH, HIGH_A, 1)
        l_copy(L_POOL_B).wait_recv()
        grad(L_POOL_B, R_DHIGH, HIGH_B, 1, shared=True)
        l_copy(L_LOW).wait_recv()
        grad(L_LOW, R_DGATE, GATE, 1)
        wait(stored[-2])
        wait(stored[-1])
        for i in range(8):
            l_copy(i).wait_send()
        for b in range(9):
            r_copy(b).wait_send()

    whole = pl.BlockSpec(memory_space=pl.ANY)
    local = pl.BlockSpec(memory_space=pltpu.VMEM)
    vm, dma = pltpu.VMEM, pltpu.SemaphoreType.DMA
    tok = jax.ShapeDtypeStruct((t, dim), F32)
    one = jax.ShapeDtypeStruct((1, dim), F32)
    return pl.pallas_call(
        kernel,
        out_shape=(tok, tok, tok, tok, one, one, jax.ShapeDtypeStruct((pairs, n * rows, 16 * width), BF)),
        in_specs=[local] * 6 + [whole],
        out_specs=(local,) * 6 + (whole,),
        scratch_shapes=[
            vm((2, pairs, rows, 16 * dim), BF), vm((8, t, dim), BF), vm((8, t, half), BF), vm((2, t, 15 * dim), BF),
            vm((t, dim), F32), vm((t, dim), F32), vm((t, dim), F32), vm((t, dim), F32), vm((t, dim), F32),
            vm((t, ff), BF), vm((3, t, dim), BF), vm((3, every, width), BF), vm((every, width), BF), vm((every, width), BF),
            vm((1, 8, 128), BF), vm((3, every, width), BF), vm((heads, every, every), BF), vm((every, every), BF),
            vm((2, pairs, rows, TILE), BF),
            dma((10, 2 * n)), dma((3, n)), dma((3, n)), dma((1, n)), dma((1, n)), dma((1, n)), dma((1, n)), dma((3, n)), dma((3, n)),
            dma((3,)), dma((8,)), dma((8,)), dma((9,)), dma((9,)), dma((2, 2)),
        ],
        compiler_params=pltpu.CompilerParams(collective_id=cid, has_side_effects=True, vmem_limit_bytes=61 * MIB),
        cost_estimate=pl.CostEstimate(flops=14 * 10**9, bytes_accessed=70 * 10**6, transcendentals=10**7),
    )(low, pool_a, pool_b, cot, gain1, gain2, packed.reshape(pairs, 2, n, rows, 16 * width))
def rows_first(x):
    return with_layout_constraint(x, Layout(major_to_minor=tuple(range(x.ndim))))


def own_part(w, axis):
    length = w.shape[axis] // lax.axis_size("dp")
    return lax.dynamic_slice_in_dim(w, lax.axis_index("dp") * length, length, axis)


def fold(w, rows):
    return w[:rows], jnp.pad(w[rows:], ((0, 2 * rows - w.shape[0]), (0, 0)))


def core_first(x, devices):
    shape = x.shape
    return x.reshape(shape[:-1] + (devices // 2, 2, -1)).swapaxes(-3, -2).reshape(shape)


def core_last(x, devices):
    shape = x.shape
    return x.reshape(shape[:-1] + (2, devices // 2, -1)).swapaxes(-3, -2).reshape(shape)


def layer_norm(values, gain):
    centre = jnp.mean(values, -1, keepdims=True)
    centred = values - centre
    variance = jnp.mean(centred * centred, -1, keepdims=True)
    return centred * lax.rsqrt(variance + 1e-06) * gain


def per_device(
    hr_in,
    low_in,
    valid,
    conv_w,
    hr_gain,
    cn_up,
    cn_down,
    ad_gate,
    ad_high,
    ad_out,
    ln1_gain,
    w_qkv,
    w_proj,
    ln2_gain,
    w_up,
    w_down,
    cot_low,
    cot_hr,
):
    _, row_count, col_count, chan_count = hr_in.shape
    devices, shards = lax.axis_size("dp"), lax.axis_size("mp")
    dims = low_in.shape[2]
    share = dims // devices
    qkv = own_part(w_qkv, 1)
    pieces = [
        own_part(ad_gate, 0), own_part(ad_out, 1).T, *fold(own_part(ad_high, 0), share),
        qkv[0], qkv[1], qkv[2], own_part(w_proj, 1).T, own_part(w_up, 0), own_part(w_down, 1).T,
    ]
    packed = rows_first(jnp.concatenate(pieces, axis=1))
    packed = rows_first(lax.all_gather(packed, "mp", axis=0, tiled=True))
    plane_mask = valid[0].astype(F32)
    cell_mask = plane_mask[..., None]
    masked = hr_in[0] * valid[0].astype(BF)[..., None]
    half_rows, half_cols = (row_count // 2, col_count // 2)
    counts = plane_mask.reshape(half_rows, 2, half_cols, 2).sum(axis=(1, 3))
    shares = 1.0 / jnp.maximum(counts, 1.0)
    size = conv_w.shape[0]
    taps = conv_w.astype(F32).reshape(size * size, 1, chan_count)
    conv_out, bordered = conv_forward(masked, taps, size, shards)
    hr_gainf = hr_gain.astype(F32)
    normed = layer_norm(conv_out * cell_mask, hr_gainf).astype(BF)
    normed, packed = lax.optimization_barrier((normed, packed))
    packed = rows_first(lax.all_gather(packed, "dp", axis=0, tiled=True))
    hr_out, pooled, normed_all, hidden_act, hidden_slope, up_t, down_t = big_forward(
        normed.reshape(row_count * col_count, chan_count), cn_up, cn_down, masked, plane_mask, shares, shards
    )
    hr_out = hr_out.reshape(hr_in.shape)
    tokens = half_rows * half_cols
    by_share = pooled.reshape(tokens, devices, -1)
    pool_a = by_share[:, :, :share].reshape(tokens, dims)
    pool_b = jnp.pad(by_share[:, :, share:], ((0, 0), (0, 0), (0, 2 * share - by_share.shape[2]))).reshape(tokens, dims)
    low_out, d_low_in, d_pool_a, d_pool_b, g_ln1, g_ln2, low_grads = low_stage(
        *(core_first(v, devices) for v in (low_in[0], pool_a, pool_b, cot_low[0])),
        *(core_first(v.astype(F32), devices)[None] for v in (ln1_gain, ln2_gain)),
        packed, shards, devices, 2,
    )
    low_out = core_last(low_out, devices)[None]
    d_low_in = core_last(d_low_in, devices)[None]
    g_ln1, g_ln2 = core_last(g_ln1[0], devices), core_last(g_ln2[0], devices)
    d_pooled = jnp.concatenate(
        [
            core_last(d_pool_a, devices).reshape(tokens, devices, share),
            core_last(d_pool_b, devices).reshape(tokens, devices, share)[:, :, : by_share.shape[2] - share],
        ],
        axis=2,
    )
    d_normed, d_map, cn_grads, low_sums = big_backward(
        cot_hr[0], d_pooled.reshape(tokens, chan_count), shares, plane_mask, normed_all, hidden_act, hidden_slope,
        up_t, down_t, low_grads, shards, devices,
    )
    low_sums = rows_first(low_sums.reshape(shards, share, -1))
    low_sums = rows_first(lax.psum_scatter(low_sums, "mp", scatter_dimension=0))
    low_gains = jnp.pad(jnp.stack([g_ln1, g_ln2]), ((0, 0), (0, chan_count - dims)))
    d_hr_in, small_sums, (g_cn_up, g_cn_down) = conv_backward(
        d_normed, conv_out, hr_gainf[None], cell_mask, bordered, d_map, taps, low_gains, size, cn_grads, devices, shards
    )
    d_hr_in = d_hr_in[None]
    g_cn_up, g_cn_down = g_cn_up.astype(F32), g_cn_down.astype(F32).T
    g_conv = small_sums[: size * size].reshape(conv_w.shape)
    g_hr_gain, g_ln1, g_ln2 = small_sums[size * size], small_sums[-2, :dims], small_sums[-1, :dims]
    own = low_sums.astype(F32)
    split, at = [], 0
    for p in pieces:
        split.append(own[:, at : at + p.shape[1]])
        at += p.shape[1]
    g_ad_gate, g_ad_out, g_high_a, g_high_b, g_query, g_key, g_value, g_proj, g_up, g_down = split
    g_ad_high = jnp.concatenate([g_high_a, g_high_b[: ad_high.shape[0] // devices - share]], axis=0)
    g_qkv = jnp.stack([g_query, g_key, g_value])
    g_ad_out, g_proj, g_down = g_ad_out.T, g_proj.T, g_down.T
    return (
        low_out,
        hr_out,
        d_low_in,
        d_hr_in,
        g_conv,
        g_hr_gain,
        g_cn_up,
        g_cn_down,
        g_ad_gate,
        g_ad_high,
        g_ad_out,
        g_ln1,
        g_qkv,
        g_proj,
        g_ln2,
        g_up,
        g_down,
    )


def solution(mesh):
    return jax.shard_map(
        per_device,
        mesh=mesh,
        in_specs=(
            P("dp", "mp", None, None),
            P("dp", "mp", None),
            P("dp", "mp", None),
            P(),
            P(),
            P(None, "mp"),
            P("mp", None),
            P(None, "mp"),
            P(None, "mp"),
            P("mp", None),
            P(),
            P(None, None, "mp"),
            P("mp", None),
            P(),
            P(None, "mp"),
            P("mp", None),
            P("dp", "mp", None),
            P("dp", "mp", None, None),
        ),
        out_specs=(
            P("dp", "mp", None),
            P("dp", "mp", None, None),
            P("dp", "mp", None),
            P("dp", "mp", None, None),
            P(),
            P(),
            P("dp", "mp"),
            P("mp", "dp"),
            P("dp", "mp"),
            P("dp", "mp"),
            P("mp", "dp"),
            P(),
            P(None, "dp", "mp"),
            P("mp", "dp"),
            P(),
            P("dp", "mp"),
            P("mp", "dp"),
        ),
        check_vma=False,
    )
```

```python
import jax
import jax.numpy as jnp
from jax import lax
from jax.experimental.layout import Layout, with_layout_constraint
from jax.experimental import pallas as pl
from jax.experimental.pallas import tpu as pltpu
from jax.sharding import PartitionSpec as P

HEAD = 64
LANES = 128
EDGE = 8
CHUNKS = 6
TILE = 512
MIB = 1024 * 1024
MESH = pl.DeviceIdType.MESH
BF = jnp.bfloat16
F32 = jnp.float32

def gelu_parts(x):
    c = 0.7978845608028654
    x2 = x * x
    t = jnp.tanh(c * x * (1.0 + 0.044715 * x2))
    half = 0.5 * (1.0 + t)
    slope = half + 0.5 * x * (1.0 - t * t) * (c * (1.0 + 3 * 0.044715 * x2))
    return x * half, slope


def gelu(x):
    c = 0.7978845608028654
    t = jnp.tanh(c * x * (1.0 + 0.044715 * (x * x)))
    return 0.5 * x * (1.0 + t)


def dp_bit(position):
    return lax.rem(lax.axis_index("dp") // 2**position, 2)


def dp_mate(position):
    return lax.axis_index("dp") + 2**position * (1 - 2 * dp_bit(position))


class Halving:
    def __init__(self, bits, lasts, shape, block):
        self.lasts, self.shape, self.block = lasts, shape, block
        left = list(bits)
        self.bits = [left.pop(0 if last else -1) for last in lasts]

    def split(self, count, p):
        if count == 1:
            return (1, 1)
        return (count // 2, 2) if self.lasts[p] else (2, count // 2)

    def buffers(self):
        count, rows, cols = self.shape
        got, held = [], []
        for p in range(len(self.bits)):
            count //= 2
            got.append(jax.ShapeDtypeStruct((count, rows, cols), BF))
            held.append(jax.ShapeDtypeStruct(self.split(count, p + 1) + (rows, cols), BF))
        return got + held

    def semaphores(self):
        return [pltpu.SemaphoreType.DMA((len(self.bits),))] * 2

    def bind(self, first, buffers, send, recv):
        steps = len(self.bits)
        self.now = [first] + list(buffers[steps:])
        self.got, self.send, self.recv = buffers[:steps], send, recv

    def part(self, p, mine):
        bit = dp_bit(self.bits[p])
        index = bit if mine else 1 - bit
        return self.now[p].at[:, index] if self.lasts[p] else self.now[p].at[index]

    def copy(self, p):
        return pltpu.make_async_remote_copy(
            src_ref=self.part(p, False), dst_ref=self.got[p], send_sem=self.send.at[p], recv_sem=self.recv.at[p],
            device_id={"dp": dp_mate(self.bits[p])}, device_id_type=MESH,
        )

    def start(self, p):
        self.copy(p).start()

    def finish(self, p, wait=True):
        if wait:
            self.copy(p).wait()
        count, rows, cols = self.got[p].shape
        ways = self.split(count, p + 1)

        def add(a, b, out):
            out[...] = (a[...].astype(F32) + b[...].astype(F32)).astype(BF).reshape(out.shape)

        flat = pl.BlockSpec((1, rows, self.block), lambda k, c: (k, 0, c))
        paired = pl.BlockSpec((1, 1, rows, self.block), lambda k, c: (k // ways[1], lax.rem(k, ways[1]), 0, c))
        pltpu.emit_pipeline(add, grid=(count, cols // self.block), in_specs=[flat, flat], out_specs=[paired])(
            self.part(p, True), self.got[p], self.now[p + 1]
        )


def chain_exchange(
    n, chunks, lag, gathered, partial, travel, sems, own_chunk, prepare, arrived, compute, mates=(), begin=None, turn=None, after=None, early=False
):
    ag_send, ag_recv, rs_send, rs_recv = sems
    d = lax.axis_index("mp")
    has_left, has_right = d > 0, d < n - 1

    barrier = pltpu.get_barrier_semaphore()

    @pl.when(has_left)
    def _():
        pl.semaphore_signal(barrier, inc=1, device_id={"mp": d - 1}, device_id_type=MESH)

    @pl.when(has_right)
    def _():
        pl.semaphore_signal(barrier, inc=1, device_id={"mp": d + 1}, device_id_type=MESH)

    for mate in mates:
        pl.semaphore_signal(barrier, inc=1, device_id={"dp": mate}, device_id_type=MESH)

    own_chunk(0)
    pl.semaphore_wait(barrier, has_left.astype(jnp.int32) + has_right.astype(jnp.int32) + len(mates))
    if begin is not None:
        begin()

    def ag(way, s, j):
        return pltpu.make_async_remote_copy(
            src_ref=gathered.at[s, j], dst_ref=gathered.at[s, j],
            send_sem=ag_send.at[way, s, j], recv_sem=ag_recv.at[s, j],
            device_id={"mp": d + 1 - 2 * way}, device_id_type=MESH,
        )

    def rs(way, s, j):
        there = d + 1 - 2 * way
        slot = jnp.where((s == there) & (way == 0), n, s)
        return pltpu.make_async_remote_copy(
            src_ref=travel.at[s, j], dst_ref=travel.at[slot, j],
            send_sem=rs_send.at[s, j], recv_sem=rs_recv.at[slot, j],
            device_id={"mp": there}, device_id_type=MESH,
        )

    def rs_wait(slot, j):
        pltpu.make_async_copy(travel.at[slot, j], travel.at[slot, j], rs_recv.at[slot, j]).wait()

    def first(j, _):
        @pl.when(j > 0)
        def _():
            own_chunk(j)

        @pl.when(has_right)
        def _():
            ag(0, d, j).start()

        @pl.when(has_left)
        def _():
            ag(1, d, j).start()

        return 0

    lax.fori_loop(0, chunks, first, 0)

    def flow(way, q):
        ql = jnp.clip(q, 0, n * chunks - 1)
        s, jj = ql // chunks, lax.rem(ql, chunks)
        if way == 1:
            s = n - 1 - s
        ahead = (s > d) if way == 0 else (s < d)
        source = has_left if way == 0 else has_right

        @pl.when((q >= 0) & (q < n * chunks) & (ahead | ((s == d) & source)))
        def _():
            @pl.when(source)
            def _():
                rs_wait(jnp.where(s == d, n, s) if way == 0 else s, jj)

            @pl.when(ahead & source)
            def _():
                travel[s, jj] = (partial[s, jj].astype(F32) + travel[s, jj].astype(F32)).astype(BF)

            @pl.when(ahead & jnp.logical_not(source))
            def _():
                travel[s, jj] = partial[s, jj].astype(BF)

            @pl.when(ahead)
            def _():
                rs(way, s, jj).start()

    def block_of(k, way):
        s = d - k + 2 * k * way
        return s, (s >= 0) & (s < n) & ((k > 0) | (way == 0))

    def receive(k, way, s, j):
        @pl.when(k > 0)
        def _():
            pltpu.make_async_copy(gathered.at[s, j], gathered.at[s, j], ag_recv.at[s, j]).wait()

            @pl.when((way == 0) & has_right)
            def _():
                ag(0, s, j).start()

            @pl.when((way == 1) & has_left)
            def _():
                ag(1, s, j).start()

        arrived(s, j)

    wait_one = 1 if early else 0

    def step(g, _):
        k, j = g // chunks, lax.rem(g, chunks)

        def sides(act):
            @pl.when(g < n * chunks)
            def _():
                def side(way, _):
                    s, ok = block_of(k, way)
                    pl.when(ok)(lambda: act(way, s))
                    return 0

                lax.fori_loop(0, 2, side, 0)

        def flows():
            flow(1, g - wait_one - (n - 1 - d) * lag)
            flow(0, g - wait_one - d * lag)

        if turn is not None:
            turn(g)
        if early:
            sides(lambda way, s: receive(k, way, s, j))
            flows()

            def later(way, s):
                prepare(way, s, j)
                compute(way, s, j)

            sides(later)
        else:
            def work(way, s):
                prepare(way, s, j)
                receive(k, way, s, j)
                compute(way, s, j)

            sides(work)
            flows()
        if after is not None:
            after(g)
        return 0

    lax.fori_loop(0, n * chunks + (n - 1) * lag + wait_one, step, 0)

    def drain(i, _):
        s, j = i // chunks, lax.rem(i, chunks)

        @pl.when(has_right & (s <= d))
        def _():
            ag(0, s, j).wait_send()

        @pl.when(has_left & (s >= d))
        def _():
            ag(1, s, j).wait_send()

        @pl.when(s < d)
        def _():
            rs(1, s, j).wait_send()

        @pl.when(s > d)
        def _():
            rs(0, s, j).wait_send()

        return 0

    lax.fori_loop(0, n * chunks, drain, 0)


def own_sum(n, d, j, partial, travel, total):
    total[...] = partial[d, j].astype(F32)

    @pl.when(d > 0)
    def _():
        total[...] += travel[n, j].astype(F32)

    @pl.when(d < n - 1)
    def _():
        total[...] += travel[d, j].astype(F32)


def chain_sems(n, chunks):
    dma = pltpu.SemaphoreType.DMA
    return [dma((2, n, chunks)), dma((n, chunks)), dma((n, chunks)), dma((n + 1, chunks))]


def chunk_buffers(n, rows, c, kept):
    return [
        pltpu.VMEM((n, CHUNKS, rows, c), BF),
        pltpu.VMEM((n, CHUNKS, rows, c), kept),
        pltpu.VMEM((n + 1, CHUNKS, rows, c), BF),
    ]


def columns(i):
    return pl.ds(pl.multiple_of(i * TILE, TILE), TILE)


def drain_copies(n, copy):
    def one(i, _):
        copy(i // CHUNKS, lax.rem(i, CHUNKS)).wait()
        return 0

    lax.fori_loop(0, n * CHUNKS, one, 0)


def big_forward(x, w_up, w_down, residual, mask, share, n):
    t, c = x.shape
    h = w_up.shape[1]
    rows = t // CHUNKS
    cols = residual.shape[1]
    half = cols // 2
    pairs = rows // cols // 2

    def kernel(
        x_ref, wu, wd, res, mask_ref, share_ref, out, pooled, x_all, act_all, slope_all, wu_t, wd_t,
        gathered, partial, travel, act, slope, total, folded, turned, copied, stored, load_sem, *sems
    ):
        d = lax.axis_index("mp")
        load = pltpu.make_async_copy(x_ref, gathered.at[d], load_sem)

        def own_chunk(j):
            if isinstance(j, int):
                load.start()
                load.wait()

        def x_copy(s, j):
            return pltpu.make_async_copy(gathered.at[s, j], x_all.at[s, j], copied.at[s, j])

        def prepare(way, s, j):
            pass

        def arrived(s, j):
            x_copy(s, j).start()

        def compute(way, s, j):
            block = gathered.at[s, j]

            def up(i, _):
                pre = jnp.dot(block[...], wu[:, columns(i)], preferred_element_type=F32)
                value, rate = gelu_parts(pre)
                act[:, columns(i)] = value.astype(BF)
                slope[:, columns(i)] = rate.astype(BF)
                return 0

            lax.fori_loop(0, h // TILE, up, 0)
            keep_act = pltpu.make_async_copy(act, act_all.at[s, j], stored.at[0])
            keep_slope = pltpu.make_async_copy(slope, slope_all.at[s, j], stored.at[1])
            keep_act.start()
            keep_slope.start()

            def down(i, _):
                partial[s, j, :, columns(i)] = jnp.dot(
                    act[...], wd[:, columns(i)], preferred_element_type=F32
                )
                return 0

            lax.fori_loop(0, c // TILE, down, 0)
            keep_act.wait()
            keep_slope.wait()

        def after(g):
            for i, (w, target, size) in enumerate(((wu, wu_t, h), (wd, wd_t, c))):
                @pl.when(g < size // LANES)
                def _():
                    some = pl.ds(pl.multiple_of(g * LANES, LANES), LANES)
                    turned[i, :, pl.ds(0, w.shape[0])] = w[:, some].T
                    copy = pltpu.make_async_copy(turned.at[i, :, pl.ds(0, w.shape[0])], target.at[some], stored.at[i])
                    copy.start()
                    copy.wait()

        chain_exchange(
            n, CHUNKS, 1, gathered, partial, travel, sems, own_chunk, prepare, arrived, compute, after=after
        )

        def finish(j, _):
            own_sum(n, d, j, partial, travel, total)
            values = (res[pl.ds(j * 2 * pairs, 2 * pairs)].reshape(rows, c).astype(F32) + total[...]) * mask_ref[j]
            partial[d, j] = values
            pltpu.make_async_copy(partial.at[d, j], out.at[j], stored.at[0]).start()
            both = values.reshape(pairs, 2, cols, c)
            summed = (both[:, 0] + both[:, 1]).reshape(pairs * cols, c)
            for b in range(c // LANES):
                lanes = slice(b * LANES, (b + 1) * LANES)
                folded[b] = summed[:, lanes]
                every = folded[b, pl.ds(0, pairs * half, 2), :] + folded[b, pl.ds(1, pairs * half, 2), :]
                pooled[j, :, lanes] = (every * share_ref[j]).astype(BF)
            pltpu.make_async_copy(partial.at[d, j], out.at[j], stored.at[0]).wait()
            return 0

        lax.fori_loop(0, CHUNKS, finish, 0)
        drain_copies(n, x_copy)

    whole = pl.BlockSpec(memory_space=pl.ANY)
    local = pl.BlockSpec(memory_space=pltpu.VMEM)
    out, pooled, x_all, act_all, slope_all, wu_t, wd_t = pl.pallas_call(
        kernel,
        out_shape=(
            jax.ShapeDtypeStruct((CHUNKS, rows, c), F32),
            jax.ShapeDtypeStruct((CHUNKS, pairs * half, c), BF),
            jax.ShapeDtypeStruct((n, CHUNKS, rows, c), BF),
            jax.ShapeDtypeStruct((n, CHUNKS, rows, h), BF),
            jax.ShapeDtypeStruct((n, CHUNKS, rows, h), BF),
            jax.ShapeDtypeStruct((h, c), BF),
            jax.ShapeDtypeStruct((c, h), BF),
        ),
        in_specs=[whole, local, local, local, local, local],
        out_specs=(whole, local, whole, whole, whole, whole, whole),
        scratch_shapes=chunk_buffers(n, rows, c, F32)
        + [pltpu.VMEM((rows, h), BF)] * 2
        + [pltpu.VMEM((rows, c), F32), pltpu.VMEM((c // LANES, pairs * cols, LANES), F32), pltpu.VMEM((2, LANES, max(c, h)), BF)]
        + [pltpu.SemaphoreType.DMA((n, CHUNKS)), pltpu.SemaphoreType.DMA((2,)), pltpu.SemaphoreType.DMA]
        + chain_sems(n, CHUNKS),
        compiler_params=pltpu.CompilerParams(
            collective_id=0, has_side_effects=True, vmem_limit_bytes=60 * MIB
        ),
        cost_estimate=pl.CostEstimate(
            flops=4 * n * t * c * h, bytes_accessed=8 * n * t * c, transcendentals=n * t * h
        ),
    )(
        x.reshape(CHUNKS, rows, c), w_up, w_down, residual,
        mask.reshape(CHUNKS, rows, 1), share.reshape(CHUNKS, pairs * half, 1),
    )
    return (
        out.reshape(t, c),
        pooled.reshape(t // 4, c),
        x_all,
        act_all,
        slope_all,
        wu_t,
        wd_t,
    )


def big_backward(cot, d_pooled, share, mask, x_all, act_all, slope_all, up_t, down_t, grads, n, devices):
    _, cols, c = cot.shape
    t = cot.shape[0] * cols
    h = up_t.shape[0]
    rows = t // CHUNKS
    half = cols // 2
    pairs_here = rows // cols // 2
    piece = c // devices
    items = n * CHUNKS // 2
    pairs, g_rows, g_cols = grads.shape
    bits = range(1, devices.bit_length() - 1)
    split = g_rows // 2
    steps = len(bits)
    plans = [Halving(bits, [last] * steps, (pairs, split, g_cols), min(g_cols, 1024)) for last in (True, False)]
    extras = [b for plan in plans for b in plan.buffers()[:-1]]
    each = 2 * steps - 1

    def kernel(
        cot_ref, pool_ref, share_ref, mask_ref, x_hbm, act_hbm, slopes, wu, wd, g_first, g_second,
        out, d_own, g_up_out, g_down_out, out_up, out_down, got_up, got_down, h_all, *rest
    ):
        sums, extra, rest = rest[0], rest[1 : 1 + 2 * each], rest[1 + 2 * each :]
        gathered, partial, travel, slope, grad, left, right, middle, g_up, g_down, total, spread_rows = rest[:12]
        core_send, core_recv, stored, send0, recv0, send1, recv1 = rest[12:19]
        sems = rest[19:]
        d = lax.axis_index("mp")
        plans[0].bind(g_first.at[:, :, pl.ds(0, split)], extra[:each] + (sums.at[0],), send0, recv0)
        plans[1].bind(g_second.at[:, :, pl.ds(split, split)], extra[each:] + (sums.at[1],), send1, recv1)

        def begin():
            for plan in plans:
                plan.start(0)

        def pass_on(p, plan):
            plan.finish(p)
            if p + 1 < steps:
                plan.start(p + 1)

        all_steps = n * CHUNKS + n
        due = [all_steps * 9 * (2**steps - 2 ** (steps - 1 - p)) // (10 * (2**steps - 1)) // 2 * 2 for p in range(steps)]

        def turn(g):
            for p in range(steps - 1):
                for i, plan in enumerate(plans):
                    pl.when(g == due[p] + 2 * i)(lambda p=p, plan=plan: pass_on(p, plan))

            q, due_now = item_of(g)

            @pl.when(due_now)
            def _():
                for copy in item_copies(q):
                    copy.start()

        def own_chunk(j):
            part = pool_ref[j] * share_ref[j]
            here = cot_ref.at[pl.ds(j * 2 * pairs_here, 2 * pairs_here)]
            for b in range(c // LANES):
                lanes = slice(b * LANES, (b + 1) * LANES)
                spread_rows[b, pl.ds(0, pairs_here * half, 2), :] = part[:, lanes]
                spread_rows[b, pl.ds(1, pairs_here * half, 2), :] = part[:, lanes]
                block = jnp.broadcast_to(
                    spread_rows[b].reshape(pairs_here, 1, cols, LANES), (pairs_here, 2, cols, LANES)
                ).reshape(rows, LANES)
                cell = here[:, :, lanes].reshape(rows, LANES).astype(F32)
                gathered[d, j, :, lanes] = ((cell + block) * mask_ref[j]).astype(BF)

        def slope_copy(s, j):
            return pltpu.make_async_copy(slopes.at[s, j], slope, stored.at[0])

        def prepare(way, s, j):
            slope_copy(s, j).start()

        def arrived(s, j):
            pass

        def compute(way, s, j):
            block = gathered.at[s, j]
            slope_copy(s, j).wait()

            def up(i, _):
                back = nn(block[...], wd[:, columns(i)])
                grad[:, columns(i)] = (back * slope[:, columns(i)].astype(F32)).astype(BF)
                return 0

            lax.fori_loop(0, h // TILE, up, 0)
            half_pair = pl.ds(pl.multiple_of(lax.rem(j, 2) * rows, rows), rows)
            keep = pltpu.make_async_copy(grad, h_all.at[s, j // 2, half_pair], stored.at[1])
            keep.start()

            def down(i, _):
                partial[s, j, :, columns(i)] = nn(grad[...], wu[:, columns(i)]).astype(BF)
                return 0

            lax.fori_loop(0, c // TILE, down, 0)
            keep.wait()

        def item_place(q):
            s, jj, base = d, q, CHUNKS // 2
            for k in range(1, n):
                to_left, to_right = d - k >= 0, d + k < n
                two = to_left & to_right
                r = q - base
                here = (r >= 0) & (to_left | to_right)
                s = jnp.where(here, jnp.where(to_left & (jnp.logical_not(two) | (lax.rem(r, 2) == 0)), d - k, d + k), s)
                jj = jnp.where(here, jnp.where(two, r // 2, r), jj)
                base = base + (CHUNKS // 2) * (to_left.astype(jnp.int32) + to_right.astype(jnp.int32))
            return s, jj

        def item_copies(q):
            s, jj = item_place(q)
            return (
                pltpu.make_async_copy(x_hbm.at[s, jj], left, stored.at[2]),
                pltpu.make_async_copy(act_hbm.at[s, jj], right, stored.at[3]),
                pltpu.make_async_copy(h_all.at[s, jj], middle, stored.at[4]),
            )

        between = (d > 0) & (d < n - 1)

        def item_of(g):
            q = jnp.where(between, g - items, (g - 3) // 2)
            return q, (q >= 0) & (q < items) & (g >= 3) & (between | (lax.rem(g, 2) == 1))

        def after(g):
            q, due_now = item_of(g)

            @pl.when(due_now)
            def _():
                s, jj = item_place(q)
                for copy in item_copies(q):
                    copy.wait()

                def tile(i, _):
                    a = columns(i)
                    g_up[a] += tn(left[:, a], middle[...])
                    db = gathered[s, pl.ds(2 * jj, 2), :, a].reshape(2 * rows, TILE)
                    g_down[a] += tn(db, right[...])
                    return 0

                lax.fori_loop(0, c // TILE, tile, 0)

            @pl.when(g == 2 * items + 2)
            def _():
                give(g_up, left, out_up, stored.at[2])
                swaps[0].start()

            @pl.when(g == 2 * items + 3)
            def _():
                give(g_down, right, out_down, stored.at[3])
                swaps[1].start()

        core = dp_bit(0)

        def rows_at(i):
            return pl.ds(pl.multiple_of(i * piece, piece), piece)

        def give(source, stage, target, sem):
            def one(i, _):
                stage[pl.ds(0, piece)] = source[rows_at(2 * i + 1 - core)].astype(BF)
                copy = pltpu.make_async_copy(stage.at[pl.ds(0, piece)], target.at[i], sem)
                copy.start()
                copy.wait()
                return 0

            lax.fori_loop(0, devices // 2, one, 0)

        def keep_sums():
            sets = ((g_up, left, got_up, g_up_out, 2), (g_down, right, got_down, g_down_out, 3))

            def loads(i):
                return [
                    pltpu.make_async_copy(got.at[i], stage.at[pl.ds(0, piece)], stored.at[sem])
                    for _, stage, got, _, sem in sets
                ]

            def one(i, _):
                for load in loads(i):
                    load.start()
                saves = []
                for load, (source, stage, _, target, sem) in zip(loads(i), sets):
                    load.wait()
                    here = stage.at[pl.ds(0, piece)]
                    here[...] = (source[rows_at(2 * i + core)] + here[...].astype(F32)).astype(BF)
                    saves.append(pltpu.make_async_copy(here, target.at[i], stored.at[sem]))
                    saves[-1].start()
                for save in saves:
                    save.wait()
                return 0

            lax.fori_loop(0, devices // 2, one, 0)

        swaps = [
            pltpu.make_async_remote_copy(
                src_ref=src, dst_ref=dst, send_sem=core_send.at[i], recv_sem=core_recv.at[i],
                device_id={"dp": dp_mate(0)}, device_id_type=MESH,
            )
            for i, (src, dst) in enumerate(((out_up, got_up), (out_down, got_down)))
        ]
        def clear(i, _):
            some = pl.ds(pl.multiple_of(i * TILE, TILE), TILE)
            g_up[some] = jnp.zeros((TILE, h), F32)
            g_down[some] = jnp.zeros((TILE, h), F32)
            return 0

        def begin_all():
            begin()
            lax.fori_loop(0, c // TILE, clear, 0)

        chain_exchange(
            n, CHUNKS, 1, gathered, partial, travel, sems, own_chunk, prepare, arrived, compute,
            [dp_mate(b) for b in range(steps + 1)], begin_all, turn, after, True,
        )
        keep = pltpu.make_async_copy(gathered.at[d], d_own, stored.at[0])
        keep.start()
        def result(j):
            return pltpu.make_async_copy(total, out.at[j], stored.at[1])

        def finish(j, _):
            @pl.when(j > 0)
            def _():
                result(j - 1).wait()

            own_sum(n, d, j, partial, travel, total)
            result(j).start()
            return 0

        lax.fori_loop(0, CHUNKS, finish, 0)
        result(CHUNKS - 1).wait()
        keep.wait()
        for plan in plans:
            pass_on(steps - 1, plan)
        for swap in swaps:
            swap.wait()
        keep_sums()

    whole = pl.BlockSpec(memory_space=pl.ANY)
    local = pl.BlockSpec(memory_space=pltpu.VMEM)
    dma = pltpu.SemaphoreType.DMA
    out, d_own, g_up, g_down, _, _, _, _, _, sums, *_ = pl.pallas_call(
        kernel,
        out_shape=(
            jax.ShapeDtypeStruct((CHUNKS, rows, c), F32),
            jax.ShapeDtypeStruct((CHUNKS, rows, c), BF),
            *[jax.ShapeDtypeStruct((devices // 2, piece, h), BF)] * 6,
            jax.ShapeDtypeStruct((n, CHUNKS // 2, 2 * rows, h), BF),
            jax.ShapeDtypeStruct((2, 1, 1, split, g_cols), BF),
            *extras,
        ),
        in_specs=[local] * 4 + [whole] * 3 + [local] * 2 + [whole] * 2,
        out_specs=(whole,) * (10 + 2 * each),
        scratch_shapes=chunk_buffers(n, rows, c, BF)
        + [
            pltpu.VMEM((rows, h), BF), pltpu.VMEM((rows, h), BF),
            pltpu.VMEM((2 * rows, c), BF), pltpu.VMEM((2 * rows, h), BF), pltpu.VMEM((2 * rows, h), BF),
            pltpu.VMEM((c, h), F32), pltpu.VMEM((c, h), F32),
            pltpu.VMEM((rows, c), F32), pltpu.VMEM((c // LANES, pairs_here * cols, LANES), F32),
            dma((2,)), dma((2,)), dma((5,)),
        ]
        + plans[0].semaphores() + plans[1].semaphores()
        + chain_sems(n, CHUNKS),
        compiler_params=pltpu.CompilerParams(
            collective_id=1, has_side_effects=True, vmem_limit_bytes=62 * MIB
        ),
        cost_estimate=pl.CostEstimate(
            flops=8 * n * t * c * h, bytes_accessed=8 * n * t * c, transcendentals=0
        ),
    )(
        cot, d_pooled.reshape(CHUNKS, pairs_here * half, c), share.reshape(CHUNKS, pairs_here * half, 1),
        mask.reshape(CHUNKS, rows, 1), *(v.reshape(n, CHUNKS // 2, 2 * rows, -1) for v in (x_all, act_all)),
        slope_all, up_t, down_t,
        grads.reshape(pairs // 2, 2, g_rows, g_cols), grads.reshape(2, pairs // 2, g_rows, g_cols),
    )
    return (
        out.reshape(cot.shape), d_own.reshape(cot.shape), [g_up, g_down],
        sums.reshape(g_rows, g_cols),
    )


def frame(dst, src):
    rows, cols, _ = src.shape
    dst[:, :EDGE] = jnp.zeros((rows, EDGE, LANES), F32)
    dst[:, EDGE + cols:] = jnp.zeros((rows, EDGE, LANES), F32)
    dst[:, EDGE:EDGE + cols] = src[...].astype(F32)


def correlate(out, framed, taps, size, flip, group, first=0, last=None, every=1):
    rows, cols, _ = out.shape
    reach = size // 2
    def some(k, _):
        r = first + k * every
        acc = jnp.zeros((group, cols, LANES), F32)
        for a in range(size):
            for b in range(size):
                tap = (size - 1 - a) * size + size - 1 - b if flip else a * size + b
                acc = acc + framed[pl.ds(r * group + a, group), pl.ds(EDGE - reach + b, cols), :] * taps[tap]
        out[pl.ds(r * group, group)] = acc
        return 0
    lax.fori_loop(0, (rows // group if last is None else last) - first if every == 1 else 2, some, 0)


def conv_forward(x, w, size, n):
    rows, cols, c = x.shape
    reach = size // 2

    def kernel(x_ref, w_ref, out, bordered, framed, sent, got, own):
        d = lax.axis_index("mp")
        has_up, has_down = d > 0, d < n - 1
        barrier = pltpu.get_barrier_semaphore()

        @pl.when(has_up)
        def _():
            pl.semaphore_signal(barrier, inc=1, device_id={"mp": d - 1}, device_id_type=MESH)

        @pl.when(has_down)
        def _():
            pl.semaphore_signal(barrier, inc=1, device_id={"mp": d + 1}, device_id_type=MESH)

        keep = pltpu.make_async_copy(x_ref, bordered.at[pl.ds(reach, rows)], own)
        keep.start()
        pl.semaphore_wait(barrier, has_up.astype(jnp.int32) + has_down.astype(jnp.int32))
        up = pltpu.make_async_remote_copy(
            src_ref=x_ref.at[pl.ds(0, reach)], dst_ref=bordered.at[pl.ds(reach + rows, reach)],
            send_sem=sent.at[0], recv_sem=got.at[0], device_id={"mp": d - 1}, device_id_type=MESH,
        )
        down = pltpu.make_async_remote_copy(
            src_ref=x_ref.at[pl.ds(rows - reach, reach)], dst_ref=bordered.at[pl.ds(0, reach)],
            send_sem=sent.at[1], recv_sem=got.at[1], device_id={"mp": d + 1}, device_id_type=MESH,
        )
        nothing = jnp.zeros((reach, cols, c), BF)

        @pl.when(has_up)
        def _():
            up.start()

        @pl.when(has_down)
        def _():
            down.start()

        @pl.when(d == 0)
        def _():
            bordered[:reach] = nothing

        @pl.when(d == n - 1)
        def _():
            bordered[reach + rows :] = nothing

        groups = rows // reach

        def inner(i, _):
            lanes = pl.ds(pl.multiple_of(i * LANES, LANES), LANES)
            frame(framed.at[pl.ds(reach, rows)], x_ref.at[:, :, lanes])
            correlate(out.at[:, :, lanes], framed, w_ref.at[:, :, lanes], size, False, reach, 1, groups - 1)
            return 0

        lax.fori_loop(0, c // LANES, inner, 0)
        keep.wait()

        @pl.when(has_up)
        def _():
            down.wait_recv()

        @pl.when(has_down)
        def _():
            up.wait_recv()

        def block(i, _):
            lanes = pl.ds(pl.multiple_of(i * LANES, LANES), LANES)
            frame(framed, bordered.at[:, :, lanes])
            correlate(out.at[:, :, lanes], framed, w_ref.at[:, :, lanes], size, False, reach, 0, None, groups - 1)
            return 0

        lax.fori_loop(0, c // LANES, block, 0)

        @pl.when(has_up)
        def _():
            up.wait_send()

        @pl.when(has_down)
        def _():
            down.wait_send()

    local = pl.BlockSpec(memory_space=pltpu.VMEM)
    dma = pltpu.SemaphoreType.DMA
    return pl.pallas_call(
        kernel,
        out_shape=(
            jax.ShapeDtypeStruct((rows, cols, c), F32),
            jax.ShapeDtypeStruct((rows + 2 * reach, cols, c), BF),
        ),
        in_specs=[local, local],
        out_specs=(local, local),
        scratch_shapes=[pltpu.VMEM((rows + 2 * reach, cols + 2 * EDGE, LANES), F32), dma((2,)), dma((2,)), dma],
        compiler_params=pltpu.CompilerParams(
            collective_id=5, has_side_effects=True, vmem_limit_bytes=40 * MIB
        ),
    )(x, w)


def conv_backward(d_normed, conv_out, gain, mask, bordered, d_map, w, low_gains, size, grads, devices, n):
    rows, cols, c = conv_out.shape
    reach = size // 2
    high = rows + 2 * reach
    group = 4 if rows % 4 == 0 else 1
    bits = range(1, devices.bit_length() - 1)
    steps = len(bits)
    shape = grads[0].shape
    plans = [Halving(bits, [last] * steps, shape, shape[2]) for last in (True, False)]
    each = 2 * steps
    blocks = c // LANES
    taps = size * size
    count = taps + 1 + low_gains.shape[0]
    small = -(-count // devices)
    first_due = blocks + blocks // 3
    halving = {first_due + 2 * blocks // 3 * p // (steps - 1): p for p in range(steps - 1)}
    rounds = {blocks + 7 * blocks // 12: 1, blocks + 10 * blocks // 12: 2}

    def kernel(
        dn, co, gain_ref, mask_ref, w_ref, low_ref, b_hbm, dm_hbm, g0, g1, out, g_all, *rest
    ):
        extra, rest = rest[: 2 * each], rest[2 * each :]
        around, x_around, d_here, dframed, xframed, g_own, here, level, sent, got, own = rest[:11]
        ar, halving_sems = rest[11:17], rest[17:]
        plans[0].bind(g0, extra[:each], halving_sems[0], halving_sems[1])
        plans[1].bind(g1, extra[each:], halving_sems[2], halving_sems[3])
        me, d = lax.axis_index("dp"), lax.axis_index("mp")
        has_up, has_down = d > 0, d < n - 1
        barrier = pltpu.get_barrier_semaphore()

        def greet(k, _):
            pl.semaphore_signal(
                barrier, inc=1, device_id={"dp": lax.rem(me + k, devices)}, device_id_type=MESH
            )
            return 0

        lax.fori_loop(1, devices, greet, 0)
        for k in range(1, n):
            pl.semaphore_signal(barrier, inc=1, device_id={"mp": lax.rem(d + k, n)}, device_id_type=MESH)
        load_x = pltpu.make_async_copy(b_hbm, x_around, own.at[0])
        load_d = pltpu.make_async_copy(dm_hbm, d_here, own.at[1])
        load_x.start()
        load_d.start()

        def pass_on(p):
            for plan in plans:
                plan.finish(p)
            if p == 0:
                sum_round(0)
            if p + 1 < steps:
                for plan in plans:
                    plan.start(p + 1)

        def keep(row, lanes, value):
            g_own[row // small, row % small : row % small + 1, lanes] = value

        pl.semaphore_wait(barrier, devices + n - 2)
        for plan in plans:
            plan.start(0)
        g_own[...] = jnp.zeros(g_own.shape, F32)

        def norm(r, total):
            cells = mask_ref[r]
            back, part = normalise_back(co[r] * cells, gain_ref[...], dn[r])
            around[reach + r] = (back * cells).astype(BF)
            return total + part

        keep(taps, slice(None), lax.fori_loop(0, rows, norm, jnp.zeros((1, c), F32)))
        for i in range(low_gains.shape[0]):
            keep(taps + 1 + i, slice(None), low_ref[i : i + 1])
        up = pltpu.make_async_remote_copy(
            src_ref=around.at[pl.ds(reach, reach)], dst_ref=around.at[pl.ds(reach + rows, reach)],
            send_sem=sent.at[0], recv_sem=got.at[0], device_id={"mp": d - 1}, device_id_type=MESH,
        )
        down = pltpu.make_async_remote_copy(
            src_ref=around.at[pl.ds(rows, reach)], dst_ref=around.at[pl.ds(0, reach)],
            send_sem=sent.at[1], recv_sem=got.at[1], device_id={"mp": d + 1}, device_id_type=MESH,
        )
        nothing = jnp.zeros((reach, cols, c), BF)

        @pl.when(has_up)
        def _():
            up.start()

        @pl.when(has_down)
        def _():
            down.start()

        @pl.when(d == 0)
        def _():
            around[:reach] = nothing

        @pl.when(d == n - 1)
        def _():
            around[reach + rows :] = nothing

        load_x.wait()

        def lanes_of(i):
            return pl.ds(pl.multiple_of(i * LANES, LANES), LANES)

        def kernel_block(i, _):
            lanes = lanes_of(i)
            frame(dframed.at[pl.ds(reach, rows)], around.at[pl.ds(reach, rows), :, lanes])
            frame(xframed, x_around.at[:, :, lanes])
            for a in range(size):
                def some(r, accs):
                    dv = dframed[pl.ds(reach + r * group, group), EDGE : EDGE + cols]
                    new = []
                    for b in range(size):
                        prod = dv * xframed[pl.ds(r * group + a, group), pl.ds(EDGE - reach + b, cols), :]
                        new.append(accs[b] + jnp.sum(prod.reshape(-1, 8, LANES), axis=0))
                    return tuple(new)

                accs = lax.fori_loop(
                    0, rows // group, some, tuple(jnp.zeros((8, LANES), F32) for _ in range(size))
                )
                for b in range(size):
                    keep(a * size + b, lanes, jnp.sum(accs[b], axis=0, keepdims=True))
            return 0

        def input_block(i, _):
            lanes = lanes_of(i)
            frame(dframed, around.at[:, :, lanes])
            correlate(out.at[:, :, lanes], dframed, w_ref.at[:, :, lanes], size, True, group)
            for r in range(rows):
                out[r, :, lanes] = (out[r, :, lanes] + d_here[r, :, lanes].astype(F32)) * mask_ref[r]
            return 0

        def spread(k):
            peer = lax.rem(me + k, devices)
            return pltpu.make_async_remote_copy(
                src_ref=g_own.at[peer], dst_ref=here.at[me], send_sem=ar[0].at[k], recv_sem=ar[1].at[k],
                device_id={"dp": peer}, device_id_type=MESH,
            )

        def across(k):
            return pltpu.make_async_remote_copy(
                src_ref=level.at[d], dst_ref=level.at[d], send_sem=ar[2].at[k], recv_sem=ar[3].at[k],
                device_id={"mp": lax.rem(d + k, n)}, device_id_type=MESH,
            )

        def tell(k):
            return pltpu.make_async_remote_copy(
                src_ref=g_all.at[me], dst_ref=g_all.at[me], send_sem=ar[4].at[k], recv_sem=ar[5].at[k],
                device_id={"dp": lax.rem(me + k, devices)}, device_id_type=MESH,
            )

        def all_of(length, make, act):
            def one(k, _):
                act(make(k))
                return 0

            lax.fori_loop(1, length, one, 0)

        def sum_round(p):
            if p == 0:
                here[me] = g_own[me]
                all_of(devices, spread, lambda x: x.start())
            elif p == 1:
                all_of(devices, spread, lambda x: x.wait())
                level[d] = jnp.sum(here[...], axis=0)
                all_of(n, across, lambda x: x.start())
            elif p == 2:
                all_of(n, across, lambda x: x.wait())
                g_all[me] = jnp.sum(level[...], axis=0)
                all_of(devices, tell, lambda x: x.start())
            else:
                all_of(devices, tell, lambda x: x.wait())

        marks = sorted(set(halving) | set(rounds) | {blocks, 2 * blocks})
        at = 0
        for mark in marks:
            if at < blocks:
                lax.fori_loop(at, min(mark, blocks), kernel_block, 0)
            else:
                lax.fori_loop(at - blocks, mark - blocks, input_block, 0)
            at = mark
            if mark in halving:
                pass_on(halving[mark])
            if mark == blocks:
                load_d.wait()

                @pl.when(has_up)
                def _():
                    down.wait_recv()

                @pl.when(has_down)
                def _():
                    up.wait_recv()
            if mark in rounds:
                sum_round(rounds[mark])
        pass_on(steps - 1)
        sum_round(3)

        @pl.when(has_up)
        def _():
            up.wait_send()

        @pl.when(has_down)
        def _():
            down.wait_send()

    whole = pl.BlockSpec(memory_space=pl.ANY)
    local = pl.BlockSpec(memory_space=pltpu.VMEM)
    vm, dma = pltpu.VMEM, pltpu.SemaphoreType.DMA
    d_in, g_all, *extra = pl.pallas_call(
        kernel,
        out_shape=(
            jax.ShapeDtypeStruct((rows, cols, c), F32),
            jax.ShapeDtypeStruct((devices, small, c), F32),
            *plans[0].buffers(),
            *plans[1].buffers(),
        ),
        in_specs=[local] * 6 + [whole] * 4,
        out_specs=(local,) * 2 + (whole,) * (2 * each),
        scratch_shapes=[
            vm((high, cols, c), BF), vm((high, cols, c), BF), vm((rows, cols, c), BF),
            vm((high, cols + 2 * EDGE, LANES), F32), vm((high, cols + 2 * EDGE, LANES), F32),
            vm((devices, small, c), F32), vm((devices, small, c), F32), vm((n, small, c), F32),
            dma((2,)), dma((2,)), dma((2,)),
            dma((devices,)), dma((devices,)), dma((n,)), dma((n,)), dma((devices,)), dma((devices,)),
        ]
        + plans[0].semaphores() + plans[1].semaphores(),
        compiler_params=pltpu.CompilerParams(
            collective_id=3, has_side_effects=True, vmem_limit_bytes=50 * MIB
        ),
        cost_estimate=pl.CostEstimate(flops=6 * 10**10, bytes_accessed=10**8, transcendentals=0),
    )(
        d_normed, conv_out, gain, mask, w, low_gains, bordered, d_map,
        grads[0].reshape((shape[0] // 2, 2) + shape[1:]), grads[1].reshape((2, shape[0] // 2) + shape[1:]),
    )
    sums = g_all.reshape(devices * small, c)[:count]
    return d_in, sums, [extra[each - 1].reshape(shape[1:]), extra[2 * each - 1].reshape(shape[1:])]


GATE, OUT, HIGH_A, HIGH_B, QUERY, KEY, VALUE, PROJ = range(8)
L_LOW, L_DF, L_POOL_A, L_POOL_B, L_FIRST, L_DA, L_SECOND, L_COT = range(8)
R_DGATE, R_MERGE, R_DHIGH, R_DQ, R_DK, R_DV, R_ATT, R_DUP, R_ACT = range(9)


def nn(a, b):
    return jnp.dot(a, b, preferred_element_type=F32)


def nt(a, b):
    return lax.dot_general(a, b, (((1,), (1,)), ((), ())), preferred_element_type=F32)


def tn(a, b):
    return lax.dot_general(a, b, (((0,), (0,)), ((), ())), preferred_element_type=F32)


def normalise(x, gain):
    centred = x - jnp.mean(x, -1, keepdims=True)
    rate = lax.rsqrt(jnp.mean(centred * centred, -1, keepdims=True) + 1e-06)
    return centred * rate * gain


def normalise_back(x, gain, d):
    centred = x - jnp.mean(x, -1, keepdims=True)
    rate = lax.rsqrt(jnp.mean(centred * centred, -1, keepdims=True) + 1e-06)
    hat = centred * rate
    dg = d * gain
    back = rate * (dg - jnp.mean(dg, -1, keepdims=True) - hat * jnp.mean(dg * hat, -1, keepdims=True))
    return back, jnp.sum(d * hat, axis=0, keepdims=True)


def low_stage(low, pool_a, pool_b, cot, gain1, gain2, packed, n, devices, cid):
    t, dim = low.shape
    every = n * t
    width = dim // n
    heads = width // HEAD
    pairs = devices // 2
    rows = dim // devices
    half = dim // 2
    ff = 4 * dim
    scale = HEAD ** (-0.5)

    def kernel(
        low_ref, pool_a_ref, pool_b_ref, cot_ref, gain1_ref, gain2_ref, w_hbm,
        low_out, d_low, d_pool_a, d_pool_b, g_ln1, g_ln2, grads,
        wv, lhs, lhs2, rhs, gate, high, merged, resid, d_res, slope, mixed, heads_in, att_all, d_att, d_mixed,
        d_heads, probs, d_scores, stage, left, w_sem, q_send, q_got, a_send, a_got, b_send, b_got, c_send, c_got, own_sem,
        l_send, l_got, r_send, r_got, stage_sem,
    ):
        d = lax.axis_index("mp")
        dp = lax.axis_index("dp")
        core = lax.rem(dp, 2)
        mate = dp + 1 - 2 * core
        barrier = pltpu.get_barrier_semaphore()
        for k in range(1, n):
            pl.semaphore_signal(barrier, inc=1, device_id={"mp": lax.rem(d + k, n)}, device_id_type=MESH)
        pl.semaphore_signal(barrier, inc=1, device_id={"dp": mate}, device_id_type=MESH)

        def w_copy(w, k):
            c, z = k // n, lax.rem(k, n)
            wide, base, at = w_place(w)
            src = w_hbm.at[:, c, z, :, pl.ds(base, wide)]
            dst = wv.at[c, :, :, pl.ds(pl.multiple_of(at + z * wide, wide), wide)]
            return pltpu.make_async_copy(src, dst, w_sem.at[w, k])

        def w_place(w):
            if w < 8:
                return width, w * width, w * dim
            return ff // n, 8 * width + (w - 8) * ff // n, 8 * dim + (w - 8) * ff

        def w_each(w, act):
            def one(k, _):
                act(w_copy(w, k))
                return 0

            lax.fori_loop(0, 2 * n, one, 0)

        for w in range(10):
            w_each(w, lambda copy: copy.start())

        def w_wait(*which):
            for w in which:
                w_each(w, lambda copy: copy.wait())

        def w_cols(at, size):
            return wv[:, :, :, pl.ds(at, size)].reshape(dim, size)

        def forward(x, first, count, put):
            def one(i, _):
                put(pl.multiple_of(i * TILE, TILE), nn(x, w_cols(pl.multiple_of(first * dim + i * TILE, TILE), TILE)))
                return 0
            lax.fori_loop(0, count * dim // TILE, one, 0)

        def backward(get, first, count, dst, fresh):
            def one(i, _):
                for c in range(2):
                    part = wv[c, :, :, pl.ds(pl.multiple_of((first + i) * dim, dim), dim)].reshape(half, dim)
                    y = nt(get(pl.multiple_of(i * dim, dim)), part)
                    cols = slice(c * half, (c + 1) * half)
                    if fresh and count == 1:
                        dst[:, cols] = y
                    else:
                        dst[:, cols] += y
                return 0
            if fresh and count > 1:
                dst[...] = jnp.zeros(dst.shape, F32)
            if count == 1:
                one(0, 0)
            else:
                lax.fori_loop(0, count, one, 0)

        def r_cols(block, count=1):
            return pl.ds(block * dim, count * dim)

        def r_at(block):
            return block * dim if block <= R_DUP else block * dim + 3 * dim

        def r_copy(block):
            cols = pl.ds(r_at(block), dim if block < R_DUP else ff)
            return pltpu.make_async_remote_copy(
                src_ref=rhs.at[0, :, cols], dst_ref=rhs.at[1, :, cols], send_sem=r_send.at[block],
                recv_sem=r_got.at[block], device_id={"dp": mate}, device_id_type=MESH)

        def l_copy(i):
            return pltpu.make_async_remote_copy(
                src_ref=lhs.at[i, :, pl.ds(pl.multiple_of((1 - core) * half, half), half)], dst_ref=lhs2.at[i],
                send_sem=l_send.at[i], recv_sem=l_got.at[i], device_id={"dp": mate}, device_id_type=MESH)

        stored = []
        turned = [None]

        def put_natural(dst, value):
            if rows % LANES:
                dst[...] = value
            else:
                for k in range(devices):
                    at = (k % 2) * half + k // 2 * rows
                    dst[:, k * rows : (k + 1) * rows] = value[:, at : at + rows]

        def grad(i, block, at, count, shared=False):
            if not shared:
                r_copy(block).wait_recv()
            if turned[0] != i:
                left[0] = lhs[i, :, pl.ds(pl.multiple_of(core * half, half), half)].T
                left[1] = lhs2[i].T
                turned[0] = i

            wide, base, first = w_place(at if at < 8 else 8 + (at - 8) * dim // ff)
            piece = min(TILE, wide)

            def out_copies(slot, k):
                out = []
                for q in range(TILE // piece):
                    z, col = divmod(at * dim - first + k * TILE + q * piece, wide)
                    out.append(
                        pltpu.make_async_copy(
                            stage.at[slot, :, :, pl.ds(q * piece, piece)],
                            grads.at[:, pl.ds(z * rows, rows), pl.ds(base + col, piece)],
                            stage_sem.at[slot, q],
                        )
                    )
                return out

            for k in range(count * dim // TILE):
                slot = len(stored) % 2
                if len(stored) >= 2:
                    wait(stored[-2])
                cols = pl.ds(r_at(block) + k * TILE, TILE)
                y = nn(left[0], rhs[0, :, cols]) + nn(left[1], rhs[1, :, cols])
                stage[slot] = y.astype(BF).reshape(pairs, rows, TILE)
                stored.append(out_copies(slot, k))
                start(stored[-1])

        def to_heads(k, src, dst, send, got):
            out = []
            for step in range(1, n):
                peer = lax.rem(d + step, n)
                out.append(pltpu.make_async_remote_copy(
                    src_ref=src.at[:, pl.ds(pl.multiple_of(peer * width, width), width)],
                    dst_ref=dst.at[pl.ds(pl.multiple_of(d * t, t), t)],
                    send_sem=send.at[k, step], recv_sem=got.at[k, step], device_id={"mp": peer}, device_id_type=MESH))
            out.append(pltpu.make_async_copy(
                src.at[:, pl.ds(pl.multiple_of(d * width, width), width)], dst.at[pl.ds(pl.multiple_of(d * t, t), t)], own_sem.at[k]))
            return out

        def to_tokens(k, src, dst, send, got):
            out = []
            for step in range(1, n):
                peer = lax.rem(d + step, n)
                out.append(pltpu.make_async_remote_copy(
                    src_ref=src.at[pl.ds(pl.multiple_of(peer * t, t), t)],
                    dst_ref=dst.at[:, pl.ds(pl.multiple_of(d * width, width), width)],
                    send_sem=send.at[k, step], recv_sem=got.at[k, step], device_id={"mp": peer}, device_id_type=MESH))
            out.append(pltpu.make_async_copy(
                src.at[pl.ds(pl.multiple_of(d * t, t), t)], dst.at[:, pl.ds(pl.multiple_of(d * width, width), width)], own_sem.at[k]))
            return out

        def start(copies):
            for c in copies:
                c.start()

        def wait(copies):
            for c in copies:
                c.wait()

        lhs[L_LOW] = low_ref[...]
        lhs[L_POOL_A] = pool_a_ref[...]
        lhs[L_POOL_B] = pool_b_ref[...]
        lhs[L_COT] = cot_ref[...]
        acc = d_low
        w_wait(GATE)

        def put_gate(at, y):
            gate[:, pl.ds(at, TILE)] = 1.0 / (1.0 + jnp.exp(-y))
        forward(lhs[L_LOW], GATE, 1, put_gate)
        w_wait(HIGH_A, HIGH_B, OUT)

        def put_high(at, y):
            high[:, pl.ds(at, TILE)] = y
        forward(lhs[L_POOL_A], HIGH_A, 1, put_high)

        def put_merging(at, y):
            cols = pl.ds(at, TILE)
            total = high[:, cols] + y
            high[:, cols] = total
            rhs[0, :, pl.ds(R_MERGE * dim + at, TILE)] = (total * gate[:, cols]).astype(BF)
        forward(lhs[L_POOL_B], HIGH_B, 1, put_merging)
        backward(lambda at: rhs[0, :, r_cols(R_MERGE)], OUT, 1, merged, True)
        merged[...] += lhs[L_LOW].astype(F32)
        lhs[L_FIRST] = normalise(merged[...], gain1_ref[...]).astype(BF)

        w_wait(QUERY, KEY, VALUE, PROJ)
        pl.semaphore_wait(barrier, n)
        for i in (L_LOW, L_POOL_A, L_POOL_B, L_COT, L_FIRST):
            l_copy(i).start()
        r_copy(R_MERGE).start()
        out_q = []
        for k in range(3):
            def put_mixed(at, y):
                mixed[k, :, pl.ds(at, TILE)] = y.astype(BF)
            forward(lhs[L_FIRST], QUERY + k, 1, put_mixed)
            copies = to_heads(k, mixed.at[k], heads_in.at[k], q_send, q_got)
            start(copies)
            out_q += copies
        wait(out_q)

        for h in range(heads):
            lanes = slice(h * HEAD, (h + 1) * HEAD)

            def rows_of(b, _):
                some = pl.ds(pl.multiple_of(b * t, t), t)
                s = nt(heads_in[0, some, lanes], heads_in[1, :, lanes]) * scale
                e = jnp.exp(s - jnp.max(s, -1, keepdims=True))
                p = (e * (1.0 / jnp.sum(e, -1, keepdims=True))).astype(BF)
                probs[h, some] = p
                att_all[some, lanes] = nn(p, heads_in[2, :, lanes]).astype(BF)
                return 0
            lax.fori_loop(0, n, rows_of, 0)
        out_a = to_tokens(0, att_all, rhs.at[0, :, r_cols(R_ATT)], a_send, a_got)
        start(out_a)
        wait(out_a)
        r_copy(R_ATT).start()
        backward(lambda at: rhs[0, :, r_cols(R_ATT)], PROJ, 1, resid, True)
        resid[...] += merged[...]
        lhs[L_SECOND] = normalise(resid[...], gain2_ref[...]).astype(BF)
        l_copy(L_SECOND).start()

        w_wait(8)

        def put_up(at, y):
            value, rate = gelu_parts(y)
            rhs[0, :, pl.ds(r_at(R_ACT) + at, TILE)] = value.astype(BF)
            slope[:, pl.ds(at, TILE)] = rate.astype(BF)
        forward(lhs[L_SECOND], 8, 4, put_up)
        r_copy(R_ACT).start()
        w_wait(9)
        backward(lambda at: rhs[0, :, pl.ds(r_at(R_ACT) + at, dim)], 12, 4, acc, True)
        put_natural(low_out, resid[...] + acc[...])

        def put_d_up(at, y):
            rhs[0, :, pl.ds(r_at(R_DUP) + at, TILE)] = (y * slope[:, pl.ds(at, TILE)].astype(F32)).astype(BF)
        forward(lhs[L_COT], 12, 4, put_d_up)
        r_copy(R_DUP).start()
        backward(lambda at: rhs[0, :, pl.ds(r_at(R_DUP) + at, dim)], 8, 4, acc, True)
        back, g = normalise_back(resid[...], gain2_ref[...], acc[...])
        g_ln2[...] = g
        d_res[...] = lhs[L_COT].astype(F32) + back
        lhs[L_DA] = d_res[...].astype(BF)
        l_copy(L_DA).start()

        def put_d_att(at, y):
            mixed[0, :, pl.ds(at, TILE)] = y.astype(BF)
        forward(lhs[L_DA], PROJ, 1, put_d_att)
        out_b = to_heads(0, mixed.at[0], d_att, b_send, b_got)
        start(out_b)
        l_copy(L_COT).wait_recv()
        grad(L_COT, R_ACT, 12, 4)
        wait(out_b)
        for h in range(heads):
            lanes = slice(h * HEAD, (h + 1) * HEAD)

            def rows_of(b, _):
                some = pl.ds(pl.multiple_of(b * t, t), t)
                p = probs[h, some].astype(F32)
                dp_ = nt(d_att[some, lanes], heads_in[2, :, lanes])
                ds = (p * (dp_ - jnp.sum(dp_ * p, -1, keepdims=True)) * scale).astype(BF)
                d_scores[some] = ds
                d_heads[0, some, lanes] = nn(ds, heads_in[1, :, lanes]).astype(BF)
                return 0
            lax.fori_loop(0, n, rows_of, 0)
            d_heads[1, :, lanes] = tn(d_scores[...], heads_in[0, :, lanes]).astype(BF)
            d_heads[2, :, lanes] = tn(probs[h], d_att[:, lanes]).astype(BF)
        out_c = []
        for k in range(3):
            copies = to_tokens(k, d_heads.at[k], rhs.at[0, :, r_cols(R_DQ + k)], c_send, c_got)
            start(copies)
            out_c += copies
        l_copy(L_SECOND).wait_recv()
        grad(L_SECOND, R_DUP, 8, 4)
        l_copy(L_DA).wait_recv()
        grad(L_DA, R_ATT, PROJ, 1)
        wait(out_c)
        for k in range(3):
            r_copy(R_DQ + k).start()
        backward(lambda at: rhs[0, :, pl.ds(R_DQ * dim + at, dim)], QUERY, 3, acc, True)
        back, g = normalise_back(merged[...], gain1_ref[...], acc[...])
        g_ln1[...] = g
        d_res[...] += back
        lhs[L_DF] = d_res[...].astype(BF)
        l_copy(L_DF).start()

        def put_d_gate(at, y):
            cols = pl.ds(at, TILE)
            gv = gate[:, cols]
            part = y * gv
            rhs[0, :, pl.ds(R_DHIGH * dim + at, TILE)] = part.astype(BF)
            rhs[0, :, pl.ds(R_DGATE * dim + at, TILE)] = (part * high[:, cols] * (1.0 - gv)).astype(BF)
        forward(lhs[L_DF], OUT, 1, put_d_gate)
        r_copy(R_DHIGH).start()
        r_copy(R_DGATE).start()
        backward(lambda at: rhs[0, :, r_cols(R_DHIGH)], HIGH_A, 1, d_pool_a, True)
        backward(lambda at: rhs[0, :, r_cols(R_DHIGH)], HIGH_B, 1, d_pool_b, True)
        backward(lambda at: rhs[0, :, r_cols(R_DGATE)], GATE, 1, acc, True)
        put_natural(d_low, d_res[...] + acc[...])
        l_copy(L_FIRST).wait_recv()
        for k in range(3):
            grad(L_FIRST, R_DQ + k, QUERY + k, 1)
        l_copy(L_DF).wait_recv()
        grad(L_DF, R_MERGE, OUT, 1)
        l_copy(L_POOL_A).wait_recv()
        grad(L_POOL_A, R_DHIGH, HIGH_A, 1)
        l_copy(L_POOL_B).wait_recv()
        grad(L_POOL_B, R_DHIGH, HIGH_B, 1, shared=True)
        l_copy(L_LOW).wait_recv()
        grad(L_LOW, R_DGATE, GATE, 1)
        wait(stored[-2])
        wait(stored[-1])
        for i in range(8):
            l_copy(i).wait_send()
        for b in range(9):
            r_copy(b).wait_send()

    whole = pl.BlockSpec(memory_space=pl.ANY)
    local = pl.BlockSpec(memory_space=pltpu.VMEM)
    vm, dma = pltpu.VMEM, pltpu.SemaphoreType.DMA
    tok = jax.ShapeDtypeStruct((t, dim), F32)
    one = jax.ShapeDtypeStruct((1, dim), F32)
    return pl.pallas_call(
        kernel,
        out_shape=(tok, tok, tok, tok, one, one, jax.ShapeDtypeStruct((pairs, n * rows, 16 * width), BF)),
        in_specs=[local] * 6 + [whole],
        out_specs=(local,) * 6 + (whole,),
        scratch_shapes=[
            vm((2, pairs, rows, 16 * dim), BF), vm((8, t, dim), BF), vm((8, t, half), BF), vm((2, t, 15 * dim), BF),
            vm((t, dim), F32), vm((t, dim), F32), vm((t, dim), F32), vm((t, dim), F32), vm((t, dim), F32),
            vm((t, ff), BF), vm((3, t, dim), BF), vm((3, every, width), BF), vm((every, width), BF), vm((every, width), BF),
            vm((1, 8, 128), BF), vm((3, every, width), BF), vm((heads, every, every), BF), vm((every, every), BF),
            vm((2, pairs, rows, TILE), BF), vm((2, half, t), BF),
            dma((10, 2 * n)), dma((3, n)), dma((3, n)), dma((1, n)), dma((1, n)), dma((1, n)), dma((1, n)), dma((3, n)), dma((3, n)),
            dma((3,)), dma((8,)), dma((8,)), dma((9,)), dma((9,)), dma((2, 2)),
        ],
        compiler_params=pltpu.CompilerParams(collective_id=cid, has_side_effects=True, vmem_limit_bytes=62 * MIB),
        cost_estimate=pl.CostEstimate(flops=14 * 10**9, bytes_accessed=70 * 10**6, transcendentals=10**7),
    )(low, pool_a, pool_b, cot, gain1, gain2, packed.reshape(pairs, 2, n, rows, 16 * width))
def weight_outputs(own, g_cn_up, g_cn_down, widths, high_rows):
    share = own.shape[0]
    width, wide = widths[0], widths[-1]
    piece, h = g_cn_up.shape

    def kernel(x, cn_up, cn_down, gate, high, out, qkv, proj, up, down, o_cn_up, o_cn_down):
        def part(i, size=width):
            at = sum(widths[:i])
            return x[:, at : at + size].astype(F32)

        gate[...] = part(0)
        out[...] = part(1).T
        high[:share] = part(2)
        high[share:] = part(3)[: high_rows - share]
        for k in range(3):
            qkv[k] = part(4 + k)
        proj[...] = part(7).T
        up[...] = part(8, wide)
        down[...] = part(9, wide).T
        o_cn_up[...] = cn_up[...].astype(F32)
        o_cn_down[...] = cn_down[...].astype(F32).T

    local = pl.BlockSpec(memory_space=pltpu.VMEM)
    shapes = [
        (share, width), (high_rows, width), (width, share), (3, share, width), (width, share), (share, wide),
        (wide, share), (piece, h), (h, piece),
    ]
    return pl.pallas_call(
        kernel,
        out_shape=[jax.ShapeDtypeStruct(s, F32) for s in shapes],
        in_specs=[local] * 3,
        out_specs=[local] * 9,
        compiler_params=pltpu.CompilerParams(vmem_limit_bytes=32 * MIB),
    )(own, g_cn_up, g_cn_down)


def pack_weights(ad_gate, ad_out, ad_high, w_qkv, w_proj, w_up, w_down, devices):
    dim, width = ad_gate.shape
    share, high_rows, wide = dim // devices, ad_high.shape[0] // devices, w_up.shape[1]
    rest = high_rows - share

    def kernel(gate, out, high, qkv, proj, up, down, packed, side, side_wide, sems):
        me = lax.axis_index("dp")
        mine = pl.ds(pl.multiple_of(me * share, share), share)
        lanes = mine

        def at(i, size=width):
            return packed.at[:, pl.ds(i * width, size)]

        straight = [(gate.at[mine], at(0)), (up.at[mine], at(8, wide))]
        straight += [(qkv.at[k, mine], at(4 + k)) for k in range(3)]
        straight.append((high.at[pl.ds(pl.multiple_of(me * high_rows, rest), share)], at(2)))
        straight.append((high.at[pl.ds(pl.multiple_of(me * high_rows + share, rest), rest)], at(3).at[pl.ds(0, rest)]))
        straight += [(out.at[:, lanes], side.at[0]), (proj.at[:, lanes], side.at[1]), (down.at[:, lanes], side_wide)]
        copies = [pltpu.make_async_copy(a, b, sems.at[i]) for i, (a, b) in enumerate(straight)]
        for copy in copies:
            copy.start()
        packed[rest:, 3 * width : 4 * width] = jnp.zeros((share - rest, width), BF)
        for copy in copies:
            copy.wait()
        packed[:, width : 2 * width] = side[0].T
        packed[:, 7 * width : 8 * width] = side[1].T
        packed[:, 8 * width + wide :] = side_wide[...].T

    whole = pl.BlockSpec(memory_space=pl.ANY)
    return pl.pallas_call(
        kernel,
        out_shape=jax.ShapeDtypeStruct((share, 8 * width + 2 * wide), BF),
        in_specs=[whole] * 7,
        out_specs=pl.BlockSpec(memory_space=pltpu.VMEM),
        scratch_shapes=[
            pltpu.VMEM((2, width, share), BF), pltpu.VMEM((wide, share), BF), pltpu.SemaphoreType.DMA((10,)),
        ],
        compiler_params=pltpu.CompilerParams(vmem_limit_bytes=16 * MIB),
    )(ad_gate, ad_out, ad_high, w_qkv, w_proj, w_up, w_down)


def rows_first(x):
    return with_layout_constraint(x, Layout(major_to_minor=tuple(range(x.ndim))))


def own_part(w, axis):
    length = w.shape[axis] // lax.axis_size("dp")
    return lax.dynamic_slice_in_dim(w, lax.axis_index("dp") * length, length, axis)


def fold(w, rows):
    return w[:rows], jnp.pad(w[rows:], ((0, 2 * rows - w.shape[0]), (0, 0)))


def core_first(x, devices):
    shape = x.shape
    return x.reshape(shape[:-1] + (devices // 2, 2, -1)).swapaxes(-3, -2).reshape(shape)


def core_last(x, devices):
    shape = x.shape
    return x.reshape(shape[:-1] + (2, devices // 2, -1)).swapaxes(-3, -2).reshape(shape)


def layer_norm(values, gain):
    centre = jnp.mean(values, -1, keepdims=True)
    centred = values - centre
    variance = jnp.mean(centred * centred, -1, keepdims=True)
    return centred * lax.rsqrt(variance + 1e-06) * gain


def per_device(
    hr_in,
    low_in,
    valid,
    conv_w,
    hr_gain,
    cn_up,
    cn_down,
    ad_gate,
    ad_high,
    ad_out,
    ln1_gain,
    w_qkv,
    w_proj,
    ln2_gain,
    w_up,
    w_down,
    cot_low,
    cot_hr,
):
    _, row_count, col_count, chan_count = hr_in.shape
    devices, shards = lax.axis_size("dp"), lax.axis_size("mp")
    dims = low_in.shape[2]
    share = dims // devices
    qkv = own_part(w_qkv, 1)
    low_weights = (ad_gate, ad_out, ad_high, w_qkv, w_proj, w_up, w_down)
    pieces = [
        own_part(ad_gate, 0), own_part(ad_out, 1).T, *fold(own_part(ad_high, 0), share),
        qkv[0], qkv[1], qkv[2], own_part(w_proj, 1).T, own_part(w_up, 0), own_part(w_down, 1).T,
    ]
    if share % LANES:
        packed = rows_first(jnp.concatenate(pieces, axis=1))
    else:
        packed = pack_weights(*low_weights, devices)
    packed = rows_first(lax.all_gather(packed, "mp", axis=0, tiled=True))
    plane_mask = valid[0].astype(F32)
    cell_mask = plane_mask[..., None]
    masked = hr_in[0] * valid[0].astype(BF)[..., None]
    half_rows, half_cols = (row_count // 2, col_count // 2)
    counts = plane_mask.reshape(half_rows, 2, half_cols, 2).sum(axis=(1, 3))
    shares = 1.0 / jnp.maximum(counts, 1.0)
    size = conv_w.shape[0]
    taps = conv_w.astype(F32).reshape(size * size, 1, chan_count)
    conv_out, bordered = conv_forward(masked, taps, size, shards)
    hr_gainf = hr_gain.astype(F32)
    normed = layer_norm(conv_out * cell_mask, hr_gainf).astype(BF)
    normed, packed = lax.optimization_barrier((normed, packed))
    packed = rows_first(lax.all_gather(packed, "dp", axis=0, tiled=True))
    hr_out, pooled, normed_all, hidden_act, hidden_slope, up_t, down_t = big_forward(
        normed.reshape(row_count * col_count, chan_count), cn_up, cn_down, masked, plane_mask, shares, shards
    )
    hr_out = hr_out.reshape(hr_in.shape)
    tokens = half_rows * half_cols
    by_share = pooled.reshape(tokens, devices, -1)
    pool_a = by_share[:, :, :share].reshape(tokens, dims)
    pool_b = jnp.pad(by_share[:, :, share:], ((0, 0), (0, 0), (0, 2 * share - by_share.shape[2]))).reshape(tokens, dims)
    low_out, d_low_in, d_pool_a, d_pool_b, g_ln1, g_ln2, low_grads = low_stage(
        *(core_first(v, devices) for v in (low_in[0], pool_a, pool_b, cot_low[0])),
        *(core_first(v.astype(F32), devices)[None] for v in (ln1_gain, ln2_gain)),
        packed, shards, devices, 2,
    )
    if share % LANES:
        low_out, d_low_in = core_last(low_out, devices), core_last(d_low_in, devices)
    low_out, d_low_in = low_out[None], d_low_in[None]
    g_ln1, g_ln2 = core_last(g_ln1[0], devices), core_last(g_ln2[0], devices)
    d_pooled = jnp.concatenate(
        [
            core_last(d_pool_a, devices).reshape(tokens, devices, share),
            core_last(d_pool_b, devices).reshape(tokens, devices, share)[:, :, : by_share.shape[2] - share],
        ],
        axis=2,
    )
    d_normed, d_map, cn_grads, low_sums = big_backward(
        cot_hr[0], d_pooled.reshape(tokens, chan_count), shares, plane_mask, normed_all, hidden_act, hidden_slope,
        up_t, down_t, low_grads, shards, devices,
    )
    low_sums = rows_first(low_sums.reshape(shards, share, -1))
    low_sums = rows_first(lax.psum_scatter(low_sums, "mp", scatter_dimension=0))
    low_gains = jnp.pad(jnp.stack([g_ln1, g_ln2]), ((0, 0), (0, chan_count - dims)))
    d_hr_in, small_sums, (g_cn_up, g_cn_down) = conv_backward(
        d_normed, conv_out, hr_gainf[None], cell_mask, bordered, d_map, taps, low_gains, size, cn_grads, devices, shards
    )
    d_hr_in = d_hr_in[None]
    g_conv = small_sums[: size * size].reshape(conv_w.shape)
    g_hr_gain, g_ln1, g_ln2 = small_sums[size * size], small_sums[-2, :dims], small_sums[-1, :dims]
    g_ad_gate, g_ad_high, g_ad_out, g_qkv, g_proj, g_up, g_down, g_cn_up, g_cn_down = weight_outputs(
        low_sums.reshape(share, -1), g_cn_up, g_cn_down, [p.shape[1] for p in pieces], ad_high.shape[0] // devices
    )
    return (
        low_out,
        hr_out,
        d_low_in,
        d_hr_in,
        g_conv,
        g_hr_gain,
        g_cn_up,
        g_cn_down,
        g_ad_gate,
        g_ad_high,
        g_ad_out,
        g_ln1,
        g_qkv,
        g_proj,
        g_ln2,
        g_up,
        g_down,
    )


def solution(mesh):
    return jax.shard_map(
        per_device,
        mesh=mesh,
        in_specs=(
            P("dp", "mp", None, None),
            P("dp", "mp", None),
            P("dp", "mp", None),
            P(),
            P(),
            P(None, "mp"),
            P("mp", None),
            P(None, "mp"),
            P(None, "mp"),
            P("mp", None),
            P(),
            P(None, None, "mp"),
            P("mp", None),
            P(),
            P(None, "mp"),
            P("mp", None),
            P("dp", "mp", None),
            P("dp", "mp", None, None),
        ),
        out_specs=(
            P("dp", "mp", None),
            P("dp", "mp", None, None),
            P("dp", "mp", None),
            P("dp", "mp", None, None),
            P(),
            P(),
            P("dp", "mp"),
            P("mp", "dp"),
            P("dp", "mp"),
            P("dp", "mp"),
            P("mp", "dp"),
            P(),
            P(None, "dp", "mp"),
            P("mp", "dp"),
            P(),
            P("dp", "mp"),
            P("mp", "dp"),
        ),
        check_vma=False,
    )
```

```python
import jax
import jax.numpy as jnp
from jax import lax
from jax.experimental.layout import Layout, with_layout_constraint
from jax.experimental import pallas as pl
from jax.experimental.pallas import tpu as pltpu
from jax.sharding import PartitionSpec as P

HEAD = 64
LANES = 128
EDGE = 8
CHUNKS = 6
TILE = 512
MIB = 1024 * 1024
MESH = pl.DeviceIdType.MESH
BF = jnp.bfloat16
F32 = jnp.float32

def gelu_parts(x):
    c = 0.7978845608028654
    x2 = x * x
    t = jnp.tanh(c * x * (1.0 + 0.044715 * x2))
    half = 0.5 * (1.0 + t)
    slope = half + 0.5 * x * (1.0 - t * t) * (c * (1.0 + 3 * 0.044715 * x2))
    return x * half, slope


def gelu(x):
    c = 0.7978845608028654
    t = jnp.tanh(c * x * (1.0 + 0.044715 * (x * x)))
    return 0.5 * x * (1.0 + t)


def dp_bit(position):
    return lax.rem(lax.axis_index("dp") // 2**position, 2)


def dp_mate(position):
    return lax.axis_index("dp") + 2**position * (1 - 2 * dp_bit(position))


class Halving:
    def __init__(self, bits, lasts, shape, block):
        self.lasts, self.shape, self.block = lasts, shape, block
        left = list(bits)
        self.bits = [left.pop(0 if last else -1) for last in lasts]

    def split(self, count, p):
        if count == 1:
            return (1, 1)
        return (count // 2, 2) if self.lasts[p] else (2, count // 2)

    def buffers(self):
        count, rows, cols = self.shape
        got, held = [], []
        for p in range(len(self.bits)):
            count //= 2
            got.append(jax.ShapeDtypeStruct((count, rows, cols), BF))
            held.append(jax.ShapeDtypeStruct(self.split(count, p + 1) + (rows, cols), BF))
        return got + held

    def semaphores(self):
        return [pltpu.SemaphoreType.DMA((len(self.bits),))] * 2

    def bind(self, first, buffers, send, recv):
        steps = len(self.bits)
        self.now = [first] + list(buffers[steps:])
        self.got, self.send, self.recv = buffers[:steps], send, recv

    def part(self, p, mine):
        bit = dp_bit(self.bits[p])
        index = bit if mine else 1 - bit
        return self.now[p].at[:, index] if self.lasts[p] else self.now[p].at[index]

    def copy(self, p):
        return pltpu.make_async_remote_copy(
            src_ref=self.part(p, False), dst_ref=self.got[p], send_sem=self.send.at[p], recv_sem=self.recv.at[p],
            device_id={"dp": dp_mate(self.bits[p])}, device_id_type=MESH,
        )

    def start(self, p):
        self.copy(p).start()

    def finish(self, p, wait=True):
        if wait:
            self.copy(p).wait()
        count, rows, cols = self.got[p].shape
        ways = self.split(count, p + 1)

        def add(a, b, out):
            out[...] = (a[...].astype(F32) + b[...].astype(F32)).astype(BF).reshape(out.shape)

        flat = pl.BlockSpec((1, rows, self.block), lambda k, c: (k, 0, c))
        paired = pl.BlockSpec((1, 1, rows, self.block), lambda k, c: (k // ways[1], lax.rem(k, ways[1]), 0, c))
        pltpu.emit_pipeline(add, grid=(count, cols // self.block), in_specs=[flat, flat], out_specs=[paired])(
            self.part(p, True), self.got[p], self.now[p + 1]
        )


def chain_exchange(
    n, chunks, lag, gathered, partial, travel, sems, own_chunk, prepare, arrived, compute, mates=(), begin=None, turn=None, after=None, early=False
):
    ag_send, ag_recv, rs_send, rs_recv = sems
    d = lax.axis_index("mp")
    has_left, has_right = d > 0, d < n - 1

    barrier = pltpu.get_barrier_semaphore()

    @pl.when(has_left)
    def _():
        pl.semaphore_signal(barrier, inc=1, device_id={"mp": d - 1}, device_id_type=MESH)

    @pl.when(has_right)
    def _():
        pl.semaphore_signal(barrier, inc=1, device_id={"mp": d + 1}, device_id_type=MESH)

    for mate in mates:
        pl.semaphore_signal(barrier, inc=1, device_id={"dp": mate}, device_id_type=MESH)

    own_chunk(0)
    pl.semaphore_wait(barrier, has_left.astype(jnp.int32) + has_right.astype(jnp.int32) + len(mates))
    if begin is not None:
        begin()

    def ag(way, s, j):
        return pltpu.make_async_remote_copy(
            src_ref=gathered.at[s, j], dst_ref=gathered.at[s, j],
            send_sem=ag_send.at[way, s, j], recv_sem=ag_recv.at[s, j],
            device_id={"mp": d + 1 - 2 * way}, device_id_type=MESH,
        )

    def rs(way, s, j):
        there = d + 1 - 2 * way
        slot = jnp.where((s == there) & (way == 0), n, s)
        return pltpu.make_async_remote_copy(
            src_ref=travel.at[s, j], dst_ref=travel.at[slot, j],
            send_sem=rs_send.at[s, j], recv_sem=rs_recv.at[slot, j],
            device_id={"mp": there}, device_id_type=MESH,
        )

    def rs_wait(slot, j):
        pltpu.make_async_copy(travel.at[slot, j], travel.at[slot, j], rs_recv.at[slot, j]).wait()

    def first(j, _):
        @pl.when(j > 0)
        def _():
            own_chunk(j)

        @pl.when(has_right)
        def _():
            ag(0, d, j).start()

        @pl.when(has_left)
        def _():
            ag(1, d, j).start()

        return 0

    lax.fori_loop(0, chunks, first, 0)

    def flow(way, q):
        ql = jnp.clip(q, 0, n * chunks - 1)
        s, jj = ql // chunks, lax.rem(ql, chunks)
        if way == 1:
            s = n - 1 - s
        ahead = (s > d) if way == 0 else (s < d)
        source = has_left if way == 0 else has_right

        @pl.when((q >= 0) & (q < n * chunks) & (ahead | ((s == d) & source)))
        def _():
            @pl.when(source)
            def _():
                rs_wait(jnp.where(s == d, n, s) if way == 0 else s, jj)

            @pl.when(ahead & source)
            def _():
                travel[s, jj] = (partial[s, jj].astype(F32) + travel[s, jj].astype(F32)).astype(BF)

            @pl.when(ahead & jnp.logical_not(source))
            def _():
                travel[s, jj] = partial[s, jj].astype(BF)

            @pl.when(ahead)
            def _():
                rs(way, s, jj).start()

    def block_of(k, way):
        s = d - k + 2 * k * way
        return s, (s >= 0) & (s < n) & ((k > 0) | (way == 0))

    def receive(k, way, s, j):
        @pl.when(k > 0)
        def _():
            pltpu.make_async_copy(gathered.at[s, j], gathered.at[s, j], ag_recv.at[s, j]).wait()

            @pl.when((way == 0) & has_right)
            def _():
                ag(0, s, j).start()

            @pl.when((way == 1) & has_left)
            def _():
                ag(1, s, j).start()

        arrived(s, j)

    wait_one = 1 if early else 0

    def step(g, _):
        k, j = g // chunks, lax.rem(g, chunks)

        def sides(act):
            @pl.when(g < n * chunks)
            def _():
                def side(way, _):
                    s, ok = block_of(k, way)
                    pl.when(ok)(lambda: act(way, s))
                    return 0

                lax.fori_loop(0, 2, side, 0)

        def flows():
            flow(1, g - wait_one - (n - 1 - d) * lag)
            flow(0, g - wait_one - d * lag)

        if turn is not None:
            turn(g)
        if early:
            sides(lambda way, s: receive(k, way, s, j))
            flows()

            def later(way, s):
                prepare(way, s, j)
                compute(way, s, j)

            sides(later)
        else:
            def work(way, s):
                prepare(way, s, j)
                receive(k, way, s, j)
                compute(way, s, j)

            sides(work)
            flows()
        if after is not None:
            after(g)
        return 0

    lax.fori_loop(0, n * chunks + (n - 1) * lag + wait_one, step, 0)

    def drain(i, _):
        s, j = i // chunks, lax.rem(i, chunks)

        @pl.when(has_right & (s <= d))
        def _():
            ag(0, s, j).wait_send()

        @pl.when(has_left & (s >= d))
        def _():
            ag(1, s, j).wait_send()

        @pl.when(s < d)
        def _():
            rs(1, s, j).wait_send()

        @pl.when(s > d)
        def _():
            rs(0, s, j).wait_send()

        return 0

    lax.fori_loop(0, n * chunks, drain, 0)


def own_sum(n, d, j, partial, travel, total):
    total[...] = partial[d, j].astype(F32)

    @pl.when(d > 0)
    def _():
        total[...] += travel[n, j].astype(F32)

    @pl.when(d < n - 1)
    def _():
        total[...] += travel[d, j].astype(F32)


def chain_sems(n, chunks):
    dma = pltpu.SemaphoreType.DMA
    return [dma((2, n, chunks)), dma((n, chunks)), dma((n, chunks)), dma((n + 1, chunks))]


def chunk_buffers(n, rows, c, kept):
    return [
        pltpu.VMEM((n, CHUNKS, rows, c), BF),
        pltpu.VMEM((n, CHUNKS, rows, c), kept),
        pltpu.VMEM((n + 1, CHUNKS, rows, c), BF),
    ]


def columns(i):
    return pl.ds(pl.multiple_of(i * TILE, TILE), TILE)


def drain_copies(n, copy):
    def one(i, _):
        copy(i // CHUNKS, lax.rem(i, CHUNKS)).wait()
        return 0

    lax.fori_loop(0, n * CHUNKS, one, 0)


def big_forward(x, w_up, w_down, residual, mask, share, n):
    t, c = x.shape
    h = w_up.shape[1]
    rows = t // CHUNKS
    cols = residual.shape[1]
    half = cols // 2
    pairs = rows // cols // 2

    def kernel(
        x_ref, wu, wd, res, mask_ref, share_ref, out, pooled, x_all, act_all, slope_all, wu_t, wd_t,
        gathered, partial, travel, act, slope, total, folded, turned, copied, stored, load_sem, *sems
    ):
        d = lax.axis_index("mp")
        load = pltpu.make_async_copy(x_ref, gathered.at[d], load_sem)

        def own_chunk(j):
            if isinstance(j, int):
                load.start()
                load.wait()

        def x_copy(s, j):
            return pltpu.make_async_copy(gathered.at[s, j], x_all.at[s, j], copied.at[s, j])

        def prepare(way, s, j):
            pass

        def arrived(s, j):
            x_copy(s, j).start()

        def compute(way, s, j):
            block = gathered.at[s, j]

            def up(i, _):
                pre = jnp.dot(block[...], wu[:, columns(i)], preferred_element_type=F32)
                value, rate = gelu_parts(pre)
                act[:, columns(i)] = value.astype(BF)
                slope[:, columns(i)] = rate.astype(BF)
                return 0

            lax.fori_loop(0, h // TILE, up, 0)
            keep_act = pltpu.make_async_copy(act, act_all.at[s, j], stored.at[0])
            keep_slope = pltpu.make_async_copy(slope, slope_all.at[s, j], stored.at[1])
            keep_act.start()
            keep_slope.start()

            def down(i, _):
                partial[s, j, :, columns(i)] = jnp.dot(
                    act[...], wd[:, columns(i)], preferred_element_type=F32
                )
                return 0

            lax.fori_loop(0, c // TILE, down, 0)
            keep_act.wait()
            keep_slope.wait()

        def finish(j):
            pl.when(j > 0)(lambda: put(j - 1).wait())
            own_sum(n, d, j, partial, travel, total)
            values = (res[pl.ds(j * 2 * pairs, 2 * pairs)].reshape(rows, c).astype(F32) + total[...]) * mask_ref[j]
            partial[d, j] = values
            put(j).start()
            both = values.reshape(pairs, 2, cols, c)
            summed = (both[:, 0] + both[:, 1]).reshape(pairs * cols, c)
            for b in range(c // LANES):
                lanes = slice(b * LANES, (b + 1) * LANES)
                folded[b] = summed[:, lanes]
                every = folded[b, pl.ds(0, pairs * half, 2), :] + folded[b, pl.ds(1, pairs * half, 2), :]
                pooled[j, :, lanes] = (every * share_ref[j]).astype(BF)

        def put(j):
            return pltpu.make_async_copy(partial.at[d, j], out.at[j], load_sem)

        def after(g):
            last = g - (n - 1) * (CHUNKS + 1)
            pl.when(last >= 0)(lambda: finish(last))
            for i, (w, target, size) in enumerate(((wu, wu_t, h), (wd, wd_t, c))):
                @pl.when(g < size // LANES)
                def _():
                    some = pl.ds(pl.multiple_of(g * LANES, LANES), LANES)
                    turned[i, :, pl.ds(0, w.shape[0])] = w[:, some].T
                    copy = pltpu.make_async_copy(turned.at[i, :, pl.ds(0, w.shape[0])], target.at[some], stored.at[i])
                    copy.start()
                    copy.wait()

        chain_exchange(
            n, CHUNKS, 1, gathered, partial, travel, sems, own_chunk, prepare, arrived, compute, after=after
        )

        put(CHUNKS - 1).wait()
        drain_copies(n, x_copy)

    whole = pl.BlockSpec(memory_space=pl.ANY)
    local = pl.BlockSpec(memory_space=pltpu.VMEM)
    out, pooled, x_all, act_all, slope_all, wu_t, wd_t = pl.pallas_call(
        kernel,
        out_shape=(
            jax.ShapeDtypeStruct((CHUNKS, rows, c), F32),
            jax.ShapeDtypeStruct((CHUNKS, pairs * half, c), BF),
            jax.ShapeDtypeStruct((n, CHUNKS, rows, c), BF),
            jax.ShapeDtypeStruct((n, CHUNKS, rows, h), BF),
            jax.ShapeDtypeStruct((n, CHUNKS, rows, h), BF),
            jax.ShapeDtypeStruct((h, c), BF),
            jax.ShapeDtypeStruct((c, h), BF),
        ),
        in_specs=[whole, local, local, local, local, local],
        out_specs=(whole, local, whole, whole, whole, whole, whole),
        scratch_shapes=chunk_buffers(n, rows, c, F32)
        + [pltpu.VMEM((rows, h), BF)] * 2
        + [pltpu.VMEM((rows, c), F32), pltpu.VMEM((c // LANES, pairs * cols, LANES), F32), pltpu.VMEM((2, LANES, max(c, h)), BF)]
        + [pltpu.SemaphoreType.DMA((n, CHUNKS)), pltpu.SemaphoreType.DMA((2,)), pltpu.SemaphoreType.DMA]
        + chain_sems(n, CHUNKS),
        compiler_params=pltpu.CompilerParams(
            collective_id=0, has_side_effects=True, vmem_limit_bytes=60 * MIB
        ),
        cost_estimate=pl.CostEstimate(
            flops=4 * n * t * c * h, bytes_accessed=8 * n * t * c, transcendentals=n * t * h
        ),
    )(
        x.reshape(CHUNKS, rows, c), w_up, w_down, residual,
        mask.reshape(CHUNKS, rows, 1), share.reshape(CHUNKS, pairs * half, 1),
    )
    return (
        out.reshape(t, c),
        pooled.reshape(t // 4, c),
        x_all,
        act_all,
        slope_all,
        wu_t,
        wd_t,
    )


def big_backward(cot, d_pooled, share, mask, x_all, act_all, slope_all, up_t, down_t, grads, n, devices):
    _, cols, c = cot.shape
    t = cot.shape[0] * cols
    h = up_t.shape[0]
    rows = t // CHUNKS
    half = cols // 2
    pairs_here = rows // cols // 2
    piece = c // devices
    items = n * CHUNKS // 2
    pairs, g_rows, g_cols = grads.shape
    bits = range(1, devices.bit_length() - 1)
    split = g_rows // 2
    steps = len(bits)
    plans = [Halving(bits, [last] * steps, (pairs, split, g_cols), min(g_cols, 1024)) for last in (True, False)]
    extras = [b for plan in plans for b in plan.buffers()[:-1]]
    each = 2 * steps - 1

    def kernel(
        cot_ref, pool_ref, share_ref, mask_ref, x_hbm, act_hbm, slopes, wu, wd, g_first, g_second,
        out, d_own, g_up_out, g_down_out, out_up, out_down, got_up, got_down, h_all, *rest
    ):
        sums, extra, rest = rest[0], rest[1 : 1 + 2 * each], rest[1 + 2 * each :]
        gathered, partial, travel, slope, grad, left, right, middle, g_up, g_down, total, spread_rows, addend = rest[:13]
        core_send, core_recv, stored, add_sem, send0, recv0, send1, recv1 = rest[13:21]
        sems = rest[21:]
        d = lax.axis_index("mp")
        plans[0].bind(g_first.at[:, :, pl.ds(0, split)], extra[:each] + (sums.at[0],), send0, recv0)
        plans[1].bind(g_second.at[:, :, pl.ds(split, split)], extra[each:] + (sums.at[1],), send1, recv1)

        def begin():
            for plan in plans:
                plan.start(0)

        def pass_on(p, plan):
            plan.finish(p)
            if p + 1 < steps:
                plan.start(p + 1)

        first_due = 2 * CHUNKS + 3
        ticks = {}
        if steps == 2:
            for p, start in ((0, first_due), (1, n * CHUNKS + n - 2)):
                tiles = [
                    (plan, k, q)
                    for plan in plans
                    for k in range(plan.got[p].shape[0])
                    for q in range(g_cols // plan.block)
                ]
                for m in range(0, len(tiles), 4):
                    ticks[start + m // 4] = (p, m == 0, m + 4 >= len(tiles), tiles[m : m + 4])

        def tile_copy(which, p, i, plan, k, q):
            lanes = pl.ds(q * plan.block, plan.block)
            if which == 0:
                source, target = plan.part(p, True).at[k, :, lanes], addend.at[0, i]
            elif which == 1:
                source, target = plan.got[p].at[k, :, lanes], addend.at[1, i]
            else:
                ways = plan.split(plan.got[p].shape[0], p + 1)
                source, target = addend.at[0, i], plan.now[p + 1].at[k // ways[1], k % ways[1], :, lanes]
            return pltpu.make_async_copy(source, target, add_sem.at[which, i])

        def tick_begin(p, fresh, final, tiles):
            if fresh:
                for plan in plans:
                    plan.copy(p).wait()
            for i, tile in enumerate(tiles):
                for which in range(2):
                    tile_copy(which, p, i, *tile).start()

        def tick_add(p, fresh, final, tiles):
            for i, tile in enumerate(tiles):
                for which in range(2):
                    tile_copy(which, p, i, *tile).wait()
                addend[0, i] = (addend[0, i].astype(F32) + addend[1, i].astype(F32)).astype(BF)
                tile_copy(2, p, i, *tile).start()
            for i, tile in enumerate(tiles):
                tile_copy(2, p, i, *tile).wait()
            if final and p + 1 < steps:
                for plan in plans:
                    plan.start(p + 1)

        all_steps = n * CHUNKS + n
        due = [all_steps * 9 * (2**steps - 2 ** (steps - 1 - p)) // (10 * (2**steps - 1)) // 2 * 2 for p in range(steps)]

        def turn(g):
            if ticks:
                for at, tick in ticks.items():
                    pl.when(g == at)(lambda tick=tick: tick_begin(*tick))
            else:
                for p in range(steps - 1):
                    for i, plan in enumerate(plans):
                        pl.when(g == due[p] + 2 * i)(lambda p=p, plan=plan: pass_on(p, plan))

            q, due_now = item_of(g)

            @pl.when(due_now)
            def _():
                for copy in item_copies(q):
                    copy.start()

        def own_chunk(j):
            part = pool_ref[j] * share_ref[j]
            here = cot_ref.at[pl.ds(j * 2 * pairs_here, 2 * pairs_here)]
            for b in range(c // LANES):
                lanes = slice(b * LANES, (b + 1) * LANES)
                spread_rows[b, pl.ds(0, pairs_here * half, 2), :] = part[:, lanes]
                spread_rows[b, pl.ds(1, pairs_here * half, 2), :] = part[:, lanes]
                block = jnp.broadcast_to(
                    spread_rows[b].reshape(pairs_here, 1, cols, LANES), (pairs_here, 2, cols, LANES)
                ).reshape(rows, LANES)
                cell = here[:, :, lanes].reshape(rows, LANES).astype(F32)
                gathered[d, j, :, lanes] = ((cell + block) * mask_ref[j]).astype(BF)

        def slope_copy(s, j):
            return pltpu.make_async_copy(slopes.at[s, j], slope, stored.at[0])

        def prepare(way, s, j):
            slope_copy(s, j).start()

        def arrived(s, j):
            pass

        def compute(way, s, j):
            block = gathered.at[s, j]
            slope_copy(s, j).wait()

            def up(i, _):
                back = nn(block[...], wd[:, columns(i)])
                grad[:, columns(i)] = (back * slope[:, columns(i)].astype(F32)).astype(BF)
                return 0

            lax.fori_loop(0, h // TILE, up, 0)
            half_pair = pl.ds(pl.multiple_of(lax.rem(j, 2) * rows, rows), rows)
            keep = pltpu.make_async_copy(grad, h_all.at[s, j // 2, half_pair], stored.at[1])
            keep.start()

            def down(i, _):
                partial[s, j, :, columns(i)] = nn(grad[...], wu[:, columns(i)]).astype(BF)
                return 0

            lax.fori_loop(0, c // TILE, down, 0)
            keep.wait()

        def item_place(q):
            s, jj, base = d, q, CHUNKS // 2
            for k in range(1, n):
                to_left, to_right = d - k >= 0, d + k < n
                two = to_left & to_right
                r = q - base
                here = (r >= 0) & (to_left | to_right)
                s = jnp.where(here, jnp.where(to_left & (jnp.logical_not(two) | (lax.rem(r, 2) == 0)), d - k, d + k), s)
                jj = jnp.where(here, jnp.where(two, r // 2, r), jj)
                base = base + (CHUNKS // 2) * (to_left.astype(jnp.int32) + to_right.astype(jnp.int32))
            return s, jj

        def item_copies(q):
            s, jj = item_place(q)
            return (
                pltpu.make_async_copy(x_hbm.at[s, jj], left, stored.at[2]),
                pltpu.make_async_copy(act_hbm.at[s, jj], right, stored.at[3]),
                pltpu.make_async_copy(h_all.at[s, jj], middle, stored.at[4]),
            )

        between = (d > 0) & (d < n - 1)

        def item_of(g):
            q = jnp.where(between, g - items, (g - 3) // 2)
            return q, (q >= 0) & (q < items) & (g >= 3) & (between | (lax.rem(g, 2) == 1))

        def after(g):
            for at, tick in ticks.items():
                pl.when(g == at)(lambda tick=tick: tick_add(*tick))
            last = g - 1 - (n - 1) * (CHUNKS + 1)
            pl.when(last >= 0)(lambda: finish(last))
            q, due_now = item_of(g)

            @pl.when(due_now)
            def _():
                s, jj = item_place(q)
                for copy in item_copies(q):
                    copy.wait()

                def tile(i, _):
                    a = columns(i)
                    g_up[a] += tn(left[:, a], middle[...])
                    db = gathered[s, pl.ds(2 * jj, 2), :, a].reshape(2 * rows, TILE)
                    g_down[a] += tn(db, right[...])
                    return 0

                lax.fori_loop(0, c // TILE, tile, 0)

            @pl.when(g == 2 * items + 2)
            def _():
                give(g_up, left, out_up, stored.at[2])
                swaps[0].start()

            @pl.when(g == 2 * items + 3)
            def _():
                give(g_down, right, out_down, stored.at[3])
                swaps[1].start()

        core = dp_bit(0)

        def result(j):
            return pltpu.make_async_copy(total, out.at[j], stored.at[5])

        def finish(j):
            pl.when(j > 0)(lambda: result(j - 1).wait())
            own_sum(n, d, j, partial, travel, total)
            result(j).start()

        def rows_at(i):
            return pl.ds(pl.multiple_of(i * piece, piece), piece)

        def give(source, stage, target, sem):
            def one(i, _):
                stage[pl.ds(0, piece)] = source[rows_at(2 * i + 1 - core)].astype(BF)
                copy = pltpu.make_async_copy(stage.at[pl.ds(0, piece)], target.at[i], sem)
                copy.start()
                copy.wait()
                return 0

            lax.fori_loop(0, devices // 2, one, 0)

        def keep_sums():
            sets = ((g_up, left, got_up, g_up_out, 2), (g_down, right, got_down, g_down_out, 3))

            def loads(i):
                return [
                    pltpu.make_async_copy(got.at[i], stage.at[pl.ds(0, piece)], stored.at[sem])
                    for _, stage, got, _, sem in sets
                ]

            def one(i, _):
                for load in loads(i):
                    load.start()
                saves = []
                for load, (source, stage, _, target, sem) in zip(loads(i), sets):
                    load.wait()
                    here = stage.at[pl.ds(0, piece)]
                    here[...] = (source[rows_at(2 * i + core)] + here[...].astype(F32)).astype(BF)
                    saves.append(pltpu.make_async_copy(here, target.at[i], stored.at[sem]))
                    saves[-1].start()
                for save in saves:
                    save.wait()
                return 0

            lax.fori_loop(0, devices // 2, one, 0)

        swaps = [
            pltpu.make_async_remote_copy(
                src_ref=src, dst_ref=dst, send_sem=core_send.at[i], recv_sem=core_recv.at[i],
                device_id={"dp": dp_mate(0)}, device_id_type=MESH,
            )
            for i, (src, dst) in enumerate(((out_up, got_up), (out_down, got_down)))
        ]
        def clear(i, _):
            some = pl.ds(pl.multiple_of(i * TILE, TILE), TILE)
            g_up[some] = jnp.zeros((TILE, h), F32)
            g_down[some] = jnp.zeros((TILE, h), F32)
            return 0

        def begin_all():
            begin()
            lax.fori_loop(0, c // TILE, clear, 0)

        chain_exchange(
            n, CHUNKS, 1, gathered, partial, travel, sems, own_chunk, prepare, arrived, compute,
            [dp_mate(b) for b in range(steps + 1)], begin_all, turn, after, True,
        )
        keep = pltpu.make_async_copy(gathered.at[d], d_own, stored.at[0])
        keep.start()
        result(CHUNKS - 1).wait()
        keep.wait()
        if not ticks:
            for plan in plans:
                pass_on(steps - 1, plan)
        for swap in swaps:
            swap.wait()
        keep_sums()

    whole = pl.BlockSpec(memory_space=pl.ANY)
    local = pl.BlockSpec(memory_space=pltpu.VMEM)
    dma = pltpu.SemaphoreType.DMA
    out, d_own, g_up, g_down, _, _, _, _, _, sums, *_ = pl.pallas_call(
        kernel,
        out_shape=(
            jax.ShapeDtypeStruct((CHUNKS, rows, c), F32),
            jax.ShapeDtypeStruct((CHUNKS, rows, c), BF),
            *[jax.ShapeDtypeStruct((devices // 2, piece, h), BF)] * 6,
            jax.ShapeDtypeStruct((n, CHUNKS // 2, 2 * rows, h), BF),
            jax.ShapeDtypeStruct((2, 1, 1, split, g_cols), BF),
            *extras,
        ),
        in_specs=[local] * 4 + [whole] * 3 + [local] * 2 + [whole] * 2,
        out_specs=(whole,) * (10 + 2 * each),
        scratch_shapes=chunk_buffers(n, rows, c, BF)
        + [
            pltpu.VMEM((rows, h), BF), pltpu.VMEM((rows, h), BF),
            pltpu.VMEM((2 * rows, c), BF), pltpu.VMEM((2 * rows, h), BF), pltpu.VMEM((2 * rows, h), BF),
            pltpu.VMEM((c, h), F32), pltpu.VMEM((c, h), F32),
            pltpu.VMEM((rows, c), F32), pltpu.VMEM((c // LANES, pairs_here * cols, LANES), F32),
            pltpu.VMEM((2, 4, split, plans[0].block), BF),
            dma((2,)), dma((2,)), dma((6,)), dma((3, 4)),
        ]
        + plans[0].semaphores() + plans[1].semaphores()
        + chain_sems(n, CHUNKS),
        compiler_params=pltpu.CompilerParams(
            collective_id=1, has_side_effects=True, vmem_limit_bytes=62 * MIB
        ),
        cost_estimate=pl.CostEstimate(
            flops=8 * n * t * c * h, bytes_accessed=8 * n * t * c, transcendentals=0
        ),
    )(
        cot, d_pooled.reshape(CHUNKS, pairs_here * half, c), share.reshape(CHUNKS, pairs_here * half, 1),
        mask.reshape(CHUNKS, rows, 1), *(v.reshape(n, CHUNKS // 2, 2 * rows, -1) for v in (x_all, act_all)),
        slope_all, up_t, down_t,
        grads.reshape(pairs // 2, 2, g_rows, g_cols), grads.reshape(2, pairs // 2, g_rows, g_cols),
    )
    return (
        out.reshape(cot.shape), d_own.reshape(cot.shape), [g_up, g_down],
        sums.reshape(g_rows, g_cols),
    )


def frame(dst, src):
    rows, cols, _ = src.shape
    dst[:, :EDGE] = jnp.zeros((rows, EDGE, LANES), F32)
    dst[:, EDGE + cols:] = jnp.zeros((rows, EDGE, LANES), F32)
    dst[:, EDGE:EDGE + cols] = src[...].astype(F32)


def correlate(out, framed, taps, size, flip, group, first=0, last=None, every=1):
    rows, cols, _ = out.shape
    reach = size // 2
    def some(k, _):
        r = first + k * every
        acc = jnp.zeros((group, cols, LANES), F32)
        for a in range(size):
            for b in range(size):
                tap = (size - 1 - a) * size + size - 1 - b if flip else a * size + b
                acc = acc + framed[pl.ds(r * group + a, group), pl.ds(EDGE - reach + b, cols), :] * taps[tap]
        out[pl.ds(r * group, group)] = acc
        return 0
    lax.fori_loop(0, (rows // group if last is None else last) - first if every == 1 else 2, some, 0)


def conv_forward(x, w, size, n):
    rows, cols, c = x.shape
    reach = size // 2

    def kernel(x_ref, w_ref, out, bordered, framed, sent, got, own):
        d = lax.axis_index("mp")
        has_up, has_down = d > 0, d < n - 1
        barrier = pltpu.get_barrier_semaphore()

        @pl.when(has_up)
        def _():
            pl.semaphore_signal(barrier, inc=1, device_id={"mp": d - 1}, device_id_type=MESH)

        @pl.when(has_down)
        def _():
            pl.semaphore_signal(barrier, inc=1, device_id={"mp": d + 1}, device_id_type=MESH)

        keep = pltpu.make_async_copy(x_ref, bordered.at[pl.ds(reach, rows)], own)
        keep.start()
        pl.semaphore_wait(barrier, has_up.astype(jnp.int32) + has_down.astype(jnp.int32))
        up = pltpu.make_async_remote_copy(
            src_ref=x_ref.at[pl.ds(0, reach)], dst_ref=bordered.at[pl.ds(reach + rows, reach)],
            send_sem=sent.at[0], recv_sem=got.at[0], device_id={"mp": d - 1}, device_id_type=MESH,
        )
        down = pltpu.make_async_remote_copy(
            src_ref=x_ref.at[pl.ds(rows - reach, reach)], dst_ref=bordered.at[pl.ds(0, reach)],
            send_sem=sent.at[1], recv_sem=got.at[1], device_id={"mp": d + 1}, device_id_type=MESH,
        )
        nothing = jnp.zeros((reach, cols, c), BF)

        @pl.when(has_up)
        def _():
            up.start()

        @pl.when(has_down)
        def _():
            down.start()

        @pl.when(d == 0)
        def _():
            bordered[:reach] = nothing

        @pl.when(d == n - 1)
        def _():
            bordered[reach + rows :] = nothing

        groups = rows // reach

        def inner(i, _):
            lanes = pl.ds(pl.multiple_of(i * LANES, LANES), LANES)
            frame(framed.at[pl.ds(reach, rows)], x_ref.at[:, :, lanes])
            correlate(out.at[:, :, lanes], framed, w_ref.at[:, :, lanes], size, False, reach, 1, groups - 1)
            return 0

        lax.fori_loop(0, c // LANES, inner, 0)
        keep.wait()

        @pl.when(has_up)
        def _():
            down.wait_recv()

        @pl.when(has_down)
        def _():
            up.wait_recv()

        def block(i, _):
            lanes = pl.ds(pl.multiple_of(i * LANES, LANES), LANES)
            frame(framed, bordered.at[:, :, lanes])
            correlate(out.at[:, :, lanes], framed, w_ref.at[:, :, lanes], size, False, reach, 0, None, groups - 1)
            return 0

        lax.fori_loop(0, c // LANES, block, 0)

        @pl.when(has_up)
        def _():
            up.wait_send()

        @pl.when(has_down)
        def _():
            down.wait_send()

    local = pl.BlockSpec(memory_space=pltpu.VMEM)
    dma = pltpu.SemaphoreType.DMA
    return pl.pallas_call(
        kernel,
        out_shape=(
            jax.ShapeDtypeStruct((rows, cols, c), F32),
            jax.ShapeDtypeStruct((rows + 2 * reach, cols, c), BF),
        ),
        in_specs=[local, local],
        out_specs=(local, local),
        scratch_shapes=[pltpu.VMEM((rows + 2 * reach, cols + 2 * EDGE, LANES), F32), dma((2,)), dma((2,)), dma],
        compiler_params=pltpu.CompilerParams(
            collective_id=5, has_side_effects=True, vmem_limit_bytes=40 * MIB
        ),
    )(x, w)


def conv_backward(d_normed, conv_out, gain, mask, bordered, d_map, w, low_gains, size, grads, devices, n):
    rows, cols, c = conv_out.shape
    reach = size // 2
    high = rows + 2 * reach
    group = 4 if rows % 4 == 0 else 1
    bits = range(1, devices.bit_length() - 1)
    steps = len(bits)
    shape = grads[0].shape
    plans = [Halving(bits, [last] * steps, shape, shape[2]) for last in (True, False)]
    each = 2 * steps
    blocks = c // LANES
    taps = size * size
    count = taps + 1 + low_gains.shape[0]
    small = -(-count // devices)
    first_due = blocks + blocks // 3
    halving = {first_due + 2 * blocks // 3 * p // (steps - 1): p for p in range(steps - 1)}
    rounds = {blocks + 7 * blocks // 12: 1, blocks + 10 * blocks // 12: 2}

    def kernel(
        dn, co, gain_ref, mask_ref, w_ref, low_ref, b_hbm, dm_hbm, g0, g1, out, g_all, *rest
    ):
        extra, rest = rest[: 2 * each], rest[2 * each :]
        around, x_around, d_here, dframed, xframed, g_own, here, level, sent, got, own = rest[:11]
        ar, halving_sems = rest[11:17], rest[17:]
        plans[0].bind(g0, extra[:each], halving_sems[0], halving_sems[1])
        plans[1].bind(g1, extra[each:], halving_sems[2], halving_sems[3])
        me, d = lax.axis_index("dp"), lax.axis_index("mp")
        has_up, has_down = d > 0, d < n - 1
        barrier = pltpu.get_barrier_semaphore()

        def greet(k, _):
            pl.semaphore_signal(
                barrier, inc=1, device_id={"dp": lax.rem(me + k, devices)}, device_id_type=MESH
            )
            return 0

        lax.fori_loop(1, devices, greet, 0)
        for k in range(1, n):
            pl.semaphore_signal(barrier, inc=1, device_id={"mp": lax.rem(d + k, n)}, device_id_type=MESH)
        load_x = pltpu.make_async_copy(b_hbm, x_around, own.at[0])
        load_d = pltpu.make_async_copy(dm_hbm, d_here, own.at[1])
        load_x.start()
        load_d.start()

        def pass_on(p):
            for plan in plans:
                plan.finish(p)
            if p == 0:
                sum_round(0)
            if p + 1 < steps:
                for plan in plans:
                    plan.start(p + 1)

        def keep(row, lanes, value):
            g_own[row // small, row % small : row % small + 1, lanes] = value

        pl.semaphore_wait(barrier, devices + n - 2)
        for plan in plans:
            plan.start(0)
        g_own[...] = jnp.zeros(g_own.shape, F32)

        def norm(r, total):
            cells = mask_ref[r]
            back, part = normalise_back(co[r] * cells, gain_ref[...], dn[r])
            around[reach + r] = (back * cells).astype(BF)
            return total + part

        keep(taps, slice(None), lax.fori_loop(0, rows, norm, jnp.zeros((1, c), F32)))
        for i in range(low_gains.shape[0]):
            keep(taps + 1 + i, slice(None), low_ref[i : i + 1])
        up = pltpu.make_async_remote_copy(
            src_ref=around.at[pl.ds(reach, reach)], dst_ref=around.at[pl.ds(reach + rows, reach)],
            send_sem=sent.at[0], recv_sem=got.at[0], device_id={"mp": d - 1}, device_id_type=MESH,
        )
        down = pltpu.make_async_remote_copy(
            src_ref=around.at[pl.ds(rows, reach)], dst_ref=around.at[pl.ds(0, reach)],
            send_sem=sent.at[1], recv_sem=got.at[1], device_id={"mp": d + 1}, device_id_type=MESH,
        )
        nothing = jnp.zeros((reach, cols, c), BF)

        @pl.when(has_up)
        def _():
            up.start()

        @pl.when(has_down)
        def _():
            down.start()

        @pl.when(d == 0)
        def _():
            around[:reach] = nothing

        @pl.when(d == n - 1)
        def _():
            around[reach + rows :] = nothing

        load_x.wait()

        def lanes_of(i):
            return pl.ds(pl.multiple_of(i * LANES, LANES), LANES)

        def kernel_block(i, _):
            lanes = lanes_of(i)
            frame(dframed.at[pl.ds(reach, rows)], around.at[pl.ds(reach, rows), :, lanes])
            frame(xframed, x_around.at[:, :, lanes])
            for a in range(size):
                def some(r, accs):
                    dv = dframed[pl.ds(reach + r * group, group), EDGE : EDGE + cols]
                    new = []
                    for b in range(size):
                        prod = dv * xframed[pl.ds(r * group + a, group), pl.ds(EDGE - reach + b, cols), :]
                        new.append(accs[b] + jnp.sum(prod.reshape(-1, 8, LANES), axis=0))
                    return tuple(new)

                accs = lax.fori_loop(
                    0, rows // group, some, tuple(jnp.zeros((8, LANES), F32) for _ in range(size))
                )
                for b in range(size):
                    keep(a * size + b, lanes, jnp.sum(accs[b], axis=0, keepdims=True))
            return 0

        def input_block(i, _):
            lanes = lanes_of(i)
            frame(dframed, around.at[:, :, lanes])
            correlate(out.at[:, :, lanes], dframed, w_ref.at[:, :, lanes], size, True, group)
            for r in range(rows):
                out[r, :, lanes] = (out[r, :, lanes] + d_here[r, :, lanes].astype(F32)) * mask_ref[r]
            return 0

        def spread(k):
            peer = lax.rem(me + k, devices)
            return pltpu.make_async_remote_copy(
                src_ref=g_own.at[peer], dst_ref=here.at[me], send_sem=ar[0].at[k], recv_sem=ar[1].at[k],
                device_id={"dp": peer}, device_id_type=MESH,
            )

        def across(k):
            return pltpu.make_async_remote_copy(
                src_ref=level.at[d], dst_ref=level.at[d], send_sem=ar[2].at[k], recv_sem=ar[3].at[k],
                device_id={"mp": lax.rem(d + k, n)}, device_id_type=MESH,
            )

        def tell(k):
            return pltpu.make_async_remote_copy(
                src_ref=g_all.at[me], dst_ref=g_all.at[me], send_sem=ar[4].at[k], recv_sem=ar[5].at[k],
                device_id={"dp": lax.rem(me + k, devices)}, device_id_type=MESH,
            )

        def all_of(length, make, act):
            def one(k, _):
                act(make(k))
                return 0

            lax.fori_loop(1, length, one, 0)

        def sum_round(p):
            if p == 0:
                here[me] = g_own[me]
                all_of(devices, spread, lambda x: x.start())
            elif p == 1:
                all_of(devices, spread, lambda x: x.wait())
                level[d] = jnp.sum(here[...], axis=0)
                all_of(n, across, lambda x: x.start())
            elif p == 2:
                all_of(n, across, lambda x: x.wait())
                g_all[me] = jnp.sum(level[...], axis=0)
                all_of(devices, tell, lambda x: x.start())
            else:
                all_of(devices, tell, lambda x: x.wait())

        marks = sorted(set(halving) | set(rounds) | {blocks, 2 * blocks})
        at = 0
        for mark in marks:
            if at < blocks:
                lax.fori_loop(at, min(mark, blocks), kernel_block, 0)
            else:
                lax.fori_loop(at - blocks, mark - blocks, input_block, 0)
            at = mark
            if mark in halving:
                pass_on(halving[mark])
            if mark == blocks:
                load_d.wait()

                @pl.when(has_up)
                def _():
                    down.wait_recv()

                @pl.when(has_down)
                def _():
                    up.wait_recv()
            if mark in rounds:
                sum_round(rounds[mark])
        pass_on(steps - 1)
        sum_round(3)

        @pl.when(has_up)
        def _():
            up.wait_send()

        @pl.when(has_down)
        def _():
            down.wait_send()

    whole = pl.BlockSpec(memory_space=pl.ANY)
    local = pl.BlockSpec(memory_space=pltpu.VMEM)
    vm, dma = pltpu.VMEM, pltpu.SemaphoreType.DMA
    d_in, g_all, *extra = pl.pallas_call(
        kernel,
        out_shape=(
            jax.ShapeDtypeStruct((rows, cols, c), F32),
            jax.ShapeDtypeStruct((devices, small, c), F32),
            *plans[0].buffers(),
            *plans[1].buffers(),
        ),
        in_specs=[local] * 6 + [whole] * 4,
        out_specs=(local,) * 2 + (whole,) * (2 * each),
        scratch_shapes=[
            vm((high, cols, c), BF), vm((high, cols, c), BF), vm((rows, cols, c), BF),
            vm((high, cols + 2 * EDGE, LANES), F32), vm((high, cols + 2 * EDGE, LANES), F32),
            vm((devices, small, c), F32), vm((devices, small, c), F32), vm((n, small, c), F32),
            dma((2,)), dma((2,)), dma((2,)),
            dma((devices,)), dma((devices,)), dma((n,)), dma((n,)), dma((devices,)), dma((devices,)),
        ]
        + plans[0].semaphores() + plans[1].semaphores(),
        compiler_params=pltpu.CompilerParams(
            collective_id=3, has_side_effects=True, vmem_limit_bytes=50 * MIB
        ),
        cost_estimate=pl.CostEstimate(flops=6 * 10**10, bytes_accessed=10**8, transcendentals=0),
    )(
        d_normed, conv_out, gain, mask, w, low_gains, bordered, d_map,
        grads[0].reshape((shape[0] // 2, 2) + shape[1:]), grads[1].reshape((2, shape[0] // 2) + shape[1:]),
    )
    sums = g_all.reshape(devices * small, c)[:count]
    return d_in, sums, [extra[each - 1].reshape(shape[1:]), extra[2 * each - 1].reshape(shape[1:])]


GATE, OUT, HIGH_A, HIGH_B, QUERY, KEY, VALUE, PROJ = range(8)
L_LOW, L_DF, L_POOL_A, L_POOL_B, L_FIRST, L_DA, L_SECOND, L_COT = range(8)
R_DGATE, R_MERGE, R_DHIGH, R_DQ, R_DK, R_DV, R_ATT, R_DUP, R_ACT = range(9)


def nn(a, b):
    return jnp.dot(a, b, preferred_element_type=F32)


def nt(a, b):
    return lax.dot_general(a, b, (((1,), (1,)), ((), ())), preferred_element_type=F32)


def tn(a, b):
    return lax.dot_general(a, b, (((0,), (0,)), ((), ())), preferred_element_type=F32)


def normalise(x, gain):
    centred = x - jnp.mean(x, -1, keepdims=True)
    rate = lax.rsqrt(jnp.mean(centred * centred, -1, keepdims=True) + 1e-06)
    return centred * rate * gain


def normalise_back(x, gain, d):
    centred = x - jnp.mean(x, -1, keepdims=True)
    rate = lax.rsqrt(jnp.mean(centred * centred, -1, keepdims=True) + 1e-06)
    hat = centred * rate
    dg = d * gain
    back = rate * (dg - jnp.mean(dg, -1, keepdims=True) - hat * jnp.mean(dg * hat, -1, keepdims=True))
    return back, jnp.sum(d * hat, axis=0, keepdims=True)


def low_stage(low, pool_a, pool_b, cot, gain1, gain2, packed, n, devices, cid):
    t, dim = low.shape
    every = n * t
    width = dim // n
    heads = width // HEAD
    pairs = devices // 2
    rows = dim // devices
    half = dim // 2
    ff = 4 * dim
    scale = HEAD ** (-0.5)

    def kernel(
        low_ref, pool_a_ref, pool_b_ref, cot_ref, gain1_ref, gain2_ref, w_hbm,
        low_out, d_low, d_pool_a, d_pool_b, g_ln1, g_ln2, grads,
        wv, lhs, lhs2, rhs, gate, high, merged, resid, d_res, slope, mixed, heads_in, att_all, d_att, d_mixed,
        d_heads, probs, d_scores, stage, left, w_sem, q_send, q_got, a_send, a_got, b_send, b_got, c_send, c_got, own_sem,
        l_send, l_got, r_send, r_got, stage_sem,
    ):
        d = lax.axis_index("mp")
        dp = lax.axis_index("dp")
        core = lax.rem(dp, 2)
        mate = dp + 1 - 2 * core
        barrier = pltpu.get_barrier_semaphore()
        for k in range(1, n):
            pl.semaphore_signal(barrier, inc=1, device_id={"mp": lax.rem(d + k, n)}, device_id_type=MESH)
        pl.semaphore_signal(barrier, inc=1, device_id={"dp": mate}, device_id_type=MESH)

        def w_copy(w, k):
            c, z = k // n, lax.rem(k, n)
            wide, base, at = w_place(w)
            src = w_hbm.at[:, c, z, :, pl.ds(base, wide)]
            dst = wv.at[c, :, :, pl.ds(pl.multiple_of(at + z * wide, wide), wide)]
            return pltpu.make_async_copy(src, dst, w_sem.at[w, k])

        def w_place(w):
            if w < 8:
                return width, w * width, w * dim
            return ff // n, 8 * width + (w - 8) * ff // n, 8 * dim + (w - 8) * ff

        def w_each(w, act):
            def one(k, _):
                act(w_copy(w, k))
                return 0

            lax.fori_loop(0, 2 * n, one, 0)

        for w in range(10):
            w_each(w, lambda copy: copy.start())

        def w_wait(*which):
            for w in which:
                w_each(w, lambda copy: copy.wait())

        def w_cols(at, size):
            return wv[:, :, :, pl.ds(at, size)].reshape(dim, size)

        def forward(x, first, count, put):
            def one(i, _):
                put(pl.multiple_of(i * TILE, TILE), nn(x, w_cols(pl.multiple_of(first * dim + i * TILE, TILE), TILE)))
                return 0
            lax.fori_loop(0, count * dim // TILE, one, 0)

        def backward(get, first, count, dst, fresh):
            def one(i, _):
                for c in range(2):
                    part = wv[c, :, :, pl.ds(pl.multiple_of((first + i) * dim, dim), dim)].reshape(half, dim)
                    y = nt(get(pl.multiple_of(i * dim, dim)), part)
                    cols = slice(c * half, (c + 1) * half)
                    if fresh and count == 1:
                        dst[:, cols] = y
                    else:
                        dst[:, cols] += y
                return 0
            if fresh and count > 1:
                dst[...] = jnp.zeros(dst.shape, F32)
            if count == 1:
                one(0, 0)
            else:
                lax.fori_loop(0, count, one, 0)

        def r_cols(block, count=1):
            return pl.ds(block * dim, count * dim)

        def r_at(block):
            return block * dim if block <= R_DUP else block * dim + 3 * dim

        def r_copy(block):
            cols = pl.ds(r_at(block), dim if block < R_DUP else ff)
            return pltpu.make_async_remote_copy(
                src_ref=rhs.at[0, :, cols], dst_ref=rhs.at[1, :, cols], send_sem=r_send.at[block],
                recv_sem=r_got.at[block], device_id={"dp": mate}, device_id_type=MESH)

        def l_copy(i):
            return pltpu.make_async_remote_copy(
                src_ref=lhs.at[i, :, pl.ds(pl.multiple_of((1 - core) * half, half), half)], dst_ref=lhs2.at[i],
                send_sem=l_send.at[i], recv_sem=l_got.at[i], device_id={"dp": mate}, device_id_type=MESH)

        stored = []
        turned = [None]

        def put_natural(dst, value):
            if rows % LANES:
                dst[...] = value
            else:
                for k in range(devices):
                    at = (k % 2) * half + k // 2 * rows
                    dst[:, k * rows : (k + 1) * rows] = value[:, at : at + rows]

        def grad(i, block, at, count, shared=False):
            if not shared:
                r_copy(block).wait_recv()
            if turned[0] != i:
                left[0] = lhs[i, :, pl.ds(pl.multiple_of(core * half, half), half)].T
                left[1] = lhs2[i].T
                turned[0] = i

            wide, base, first = w_place(at if at < 8 else 8 + (at - 8) * dim // ff)
            piece = min(TILE, wide)

            def out_copies(slot, k):
                out = []
                for q in range(TILE // piece):
                    z, col = divmod(at * dim - first + k * TILE + q * piece, wide)
                    out.append(
                        pltpu.make_async_copy(
                            stage.at[slot, :, :, pl.ds(q * piece, piece)],
                            grads.at[:, pl.ds(z * rows, rows), pl.ds(base + col, piece)],
                            stage_sem.at[slot, q],
                        )
                    )
                return out

            for k in range(count * dim // TILE):
                slot = len(stored) % 2
                if len(stored) >= 2:
                    wait(stored[-2])
                cols = pl.ds(r_at(block) + k * TILE, TILE)
                y = nn(left[0], rhs[0, :, cols]) + nn(left[1], rhs[1, :, cols])
                stage[slot] = y.astype(BF).reshape(pairs, rows, TILE)
                stored.append(out_copies(slot, k))
                start(stored[-1])

        def to_heads(k, src, dst, send, got):
            out = []
            for step in range(1, n):
                peer = lax.rem(d + step, n)
                out.append(pltpu.make_async_remote_copy(
                    src_ref=src.at[:, pl.ds(pl.multiple_of(peer * width, width), width)],
                    dst_ref=dst.at[pl.ds(pl.multiple_of(d * t, t), t)],
                    send_sem=send.at[k, step], recv_sem=got.at[k, step], device_id={"mp": peer}, device_id_type=MESH))
            out.append(pltpu.make_async_copy(
                src.at[:, pl.ds(pl.multiple_of(d * width, width), width)], dst.at[pl.ds(pl.multiple_of(d * t, t), t)], own_sem.at[k]))
            return out

        def to_tokens(k, src, dst, send, got):
            out = []
            for step in range(1, n):
                peer = lax.rem(d + step, n)
                out.append(pltpu.make_async_remote_copy(
                    src_ref=src.at[pl.ds(pl.multiple_of(peer * t, t), t)],
                    dst_ref=dst.at[:, pl.ds(pl.multiple_of(d * width, width), width)],
                    send_sem=send.at[k, step], recv_sem=got.at[k, step], device_id={"mp": peer}, device_id_type=MESH))
            out.append(pltpu.make_async_copy(
                src.at[pl.ds(pl.multiple_of(d * t, t), t)], dst.at[:, pl.ds(pl.multiple_of(d * width, width), width)], own_sem.at[k]))
            return out

        def start(copies):
            for c in copies:
                c.start()

        def wait(copies):
            for c in copies:
                c.wait()

        lhs[L_LOW] = low_ref[...]
        lhs[L_POOL_A] = pool_a_ref[...]
        lhs[L_POOL_B] = pool_b_ref[...]
        lhs[L_COT] = cot_ref[...]
        acc = d_low
        w_wait(GATE)

        def put_gate(at, y):
            gate[:, pl.ds(at, TILE)] = 1.0 / (1.0 + jnp.exp(-y))
        forward(lhs[L_LOW], GATE, 1, put_gate)
        w_wait(HIGH_A, HIGH_B, OUT)

        def put_high(at, y):
            high[:, pl.ds(at, TILE)] = y
        forward(lhs[L_POOL_A], HIGH_A, 1, put_high)

        def put_merging(at, y):
            cols = pl.ds(at, TILE)
            total = high[:, cols] + y
            high[:, cols] = total
            rhs[0, :, pl.ds(R_MERGE * dim + at, TILE)] = (total * gate[:, cols]).astype(BF)
        forward(lhs[L_POOL_B], HIGH_B, 1, put_merging)
        backward(lambda at: rhs[0, :, r_cols(R_MERGE)], OUT, 1, merged, True)
        merged[...] += lhs[L_LOW].astype(F32)
        lhs[L_FIRST] = normalise(merged[...], gain1_ref[...]).astype(BF)

        w_wait(QUERY, KEY, VALUE, PROJ)
        pl.semaphore_wait(barrier, n)
        for i in (L_LOW, L_POOL_A, L_POOL_B, L_COT, L_FIRST):
            l_copy(i).start()
        r_copy(R_MERGE).start()
        out_q = []
        for k in range(3):
            def put_mixed(at, y):
                mixed[k, :, pl.ds(at, TILE)] = y.astype(BF)
            forward(lhs[L_FIRST], QUERY + k, 1, put_mixed)
            copies = to_heads(k, mixed.at[k], heads_in.at[k], q_send, q_got)
            start(copies)
            out_q += copies
        wait(out_q)

        for h in range(heads):
            lanes = slice(h * HEAD, (h + 1) * HEAD)

            def rows_of(b, _):
                some = pl.ds(pl.multiple_of(b * t, t), t)
                s = nt(heads_in[0, some, lanes], heads_in[1, :, lanes]) * scale
                e = jnp.exp(s - jnp.max(s, -1, keepdims=True))
                p = (e * (1.0 / jnp.sum(e, -1, keepdims=True))).astype(BF)
                probs[h, some] = p
                att_all[some, lanes] = nn(p, heads_in[2, :, lanes]).astype(BF)
                return 0
            lax.fori_loop(0, n, rows_of, 0)
        out_a = to_tokens(0, att_all, rhs.at[0, :, r_cols(R_ATT)], a_send, a_got)
        start(out_a)
        wait(out_a)
        r_copy(R_ATT).start()
        backward(lambda at: rhs[0, :, r_cols(R_ATT)], PROJ, 1, resid, True)
        resid[...] += merged[...]
        lhs[L_SECOND] = normalise(resid[...], gain2_ref[...]).astype(BF)
        l_copy(L_SECOND).start()

        w_wait(8)

        def put_up(at, y):
            value, rate = gelu_parts(y)
            rhs[0, :, pl.ds(r_at(R_ACT) + at, TILE)] = value.astype(BF)
            slope[:, pl.ds(at, TILE)] = rate.astype(BF)
        forward(lhs[L_SECOND], 8, 4, put_up)
        r_copy(R_ACT).start()
        w_wait(9)
        backward(lambda at: rhs[0, :, pl.ds(r_at(R_ACT) + at, dim)], 12, 4, acc, True)
        put_natural(low_out, resid[...] + acc[...])

        def put_d_up(at, y):
            rhs[0, :, pl.ds(r_at(R_DUP) + at, TILE)] = (y * slope[:, pl.ds(at, TILE)].astype(F32)).astype(BF)
        forward(lhs[L_COT], 12, 4, put_d_up)
        r_copy(R_DUP).start()
        backward(lambda at: rhs[0, :, pl.ds(r_at(R_DUP) + at, dim)], 8, 4, acc, True)
        back, g = normalise_back(resid[...], gain2_ref[...], acc[...])
        g_ln2[...] = g
        d_res[...] = lhs[L_COT].astype(F32) + back
        lhs[L_DA] = d_res[...].astype(BF)
        l_copy(L_DA).start()

        def put_d_att(at, y):
            mixed[0, :, pl.ds(at, TILE)] = y.astype(BF)
        forward(lhs[L_DA], PROJ, 1, put_d_att)
        out_b = to_heads(0, mixed.at[0], d_att, b_send, b_got)
        start(out_b)
        l_copy(L_COT).wait_recv()
        grad(L_COT, R_ACT, 12, 4)
        wait(out_b)
        for h in range(heads):
            lanes = slice(h * HEAD, (h + 1) * HEAD)

            def rows_of(b, _):
                some = pl.ds(pl.multiple_of(b * t, t), t)
                p = probs[h, some].astype(F32)
                dp_ = nt(d_att[some, lanes], heads_in[2, :, lanes])
                ds = (p * (dp_ - jnp.sum(dp_ * p, -1, keepdims=True)) * scale).astype(BF)
                d_scores[some] = ds
                d_heads[0, some, lanes] = nn(ds, heads_in[1, :, lanes]).astype(BF)
                return 0
            lax.fori_loop(0, n, rows_of, 0)
            d_heads[1, :, lanes] = tn(d_scores[...], heads_in[0, :, lanes]).astype(BF)
            d_heads[2, :, lanes] = tn(probs[h], d_att[:, lanes]).astype(BF)
        out_c = []
        for k in range(3):
            copies = to_tokens(k, d_heads.at[k], rhs.at[0, :, r_cols(R_DQ + k)], c_send, c_got)
            start(copies)
            out_c += copies
        l_copy(L_SECOND).wait_recv()
        grad(L_SECOND, R_DUP, 8, 4)
        l_copy(L_DA).wait_recv()
        grad(L_DA, R_ATT, PROJ, 1)
        wait(out_c)
        for k in range(3):
            r_copy(R_DQ + k).start()
        backward(lambda at: rhs[0, :, pl.ds(R_DQ * dim + at, dim)], QUERY, 3, acc, True)
        back, g = normalise_back(merged[...], gain1_ref[...], acc[...])
        g_ln1[...] = g
        d_res[...] += back
        lhs[L_DF] = d_res[...].astype(BF)
        l_copy(L_DF).start()

        def put_d_gate(at, y):
            cols = pl.ds(at, TILE)
            gv = gate[:, cols]
            part = y * gv
            rhs[0, :, pl.ds(R_DHIGH * dim + at, TILE)] = part.astype(BF)
            rhs[0, :, pl.ds(R_DGATE * dim + at, TILE)] = (part * high[:, cols] * (1.0 - gv)).astype(BF)
        forward(lhs[L_DF], OUT, 1, put_d_gate)
        r_copy(R_DHIGH).start()
        r_copy(R_DGATE).start()
        backward(lambda at: rhs[0, :, r_cols(R_DHIGH)], HIGH_A, 1, d_pool_a, True)
        backward(lambda at: rhs[0, :, r_cols(R_DHIGH)], HIGH_B, 1, d_pool_b, True)
        backward(lambda at: rhs[0, :, r_cols(R_DGATE)], GATE, 1, acc, True)
        put_natural(d_low, d_res[...] + acc[...])
        l_copy(L_FIRST).wait_recv()
        for k in range(3):
            grad(L_FIRST, R_DQ + k, QUERY + k, 1)
        l_copy(L_DF).wait_recv()
        grad(L_DF, R_MERGE, OUT, 1)
        l_copy(L_POOL_A).wait_recv()
        grad(L_POOL_A, R_DHIGH, HIGH_A, 1)
        l_copy(L_POOL_B).wait_recv()
        grad(L_POOL_B, R_DHIGH, HIGH_B, 1, shared=True)
        l_copy(L_LOW).wait_recv()
        grad(L_LOW, R_DGATE, GATE, 1)
        wait(stored[-2])
        wait(stored[-1])
        for i in range(8):
            l_copy(i).wait_send()
        for b in range(9):
            r_copy(b).wait_send()

    whole = pl.BlockSpec(memory_space=pl.ANY)
    local = pl.BlockSpec(memory_space=pltpu.VMEM)
    vm, dma = pltpu.VMEM, pltpu.SemaphoreType.DMA
    tok = jax.ShapeDtypeStruct((t, dim), F32)
    one = jax.ShapeDtypeStruct((1, dim), F32)
    return pl.pallas_call(
        kernel,
        out_shape=(tok, tok, tok, tok, one, one, jax.ShapeDtypeStruct((pairs, n * rows, 16 * width), BF)),
        in_specs=[local] * 6 + [whole],
        out_specs=(local,) * 6 + (whole,),
        scratch_shapes=[
            vm((2, pairs, rows, 16 * dim), BF), vm((8, t, dim), BF), vm((8, t, half), BF), vm((2, t, 15 * dim), BF),
            vm((t, dim), F32), vm((t, dim), F32), vm((t, dim), F32), vm((t, dim), F32), vm((t, dim), F32),
            vm((t, ff), BF), vm((3, t, dim), BF), vm((3, every, width), BF), vm((every, width), BF), vm((every, width), BF),
            vm((1, 8, 128), BF), vm((3, every, width), BF), vm((heads, every, every), BF), vm((every, every), BF),
            vm((2, pairs, rows, TILE), BF), vm((2, half, t), BF),
            dma((10, 2 * n)), dma((3, n)), dma((3, n)), dma((1, n)), dma((1, n)), dma((1, n)), dma((1, n)), dma((3, n)), dma((3, n)),
            dma((3,)), dma((8,)), dma((8,)), dma((9,)), dma((9,)), dma((2, 2)),
        ],
        compiler_params=pltpu.CompilerParams(collective_id=cid, has_side_effects=True, vmem_limit_bytes=62 * MIB),
        cost_estimate=pl.CostEstimate(flops=14 * 10**9, bytes_accessed=70 * 10**6, transcendentals=10**7),
    )(low, pool_a, pool_b, cot, gain1, gain2, packed.reshape(pairs, 2, n, rows, 16 * width))
def weight_outputs(own, g_cn_up, g_cn_down, widths, high_rows, others):
    share = own.shape[0]
    width, wide = widths[0], widths[-1]
    piece, h = g_cn_up.shape

    def kernel(x, cn_up, cn_down, *rest):
        sources, rest = rest[: len(others)], rest[len(others) :]
        gate, high, out, qkv, proj, up, down, o_cn_up, o_cn_down = rest[:9]
        copies = [
            pltpu.make_async_copy(a, b, rest[-1].at[i]) for i, (a, b) in enumerate(zip(sources, rest[9:-1]))
        ]
        for copy in copies:
            copy.start()

        def part(i, size=width):
            at = sum(widths[:i])
            return x[:, at : at + size].astype(F32)

        gate[...] = part(0)
        out[...] = part(1).T
        high[:share] = part(2)
        high[share:] = part(3)[: high_rows - share]
        for k in range(3):
            qkv[k] = part(4 + k)
        proj[...] = part(7).T
        up[...] = part(8, wide)
        down[...] = part(9, wide).T
        o_cn_up[...] = cn_up[...].astype(F32)
        o_cn_down[...] = cn_down[...].astype(F32)
        for copy in copies:
            copy.wait()

    whole = pl.BlockSpec(memory_space=pl.ANY)
    local = pl.BlockSpec(memory_space=pltpu.VMEM)
    shapes = [
        (share, width), (high_rows, width), (width, share), (3, share, width), (width, share), (share, wide),
        (wide, share), (piece, h), (piece, h),
    ]
    return pl.pallas_call(
        kernel,
        out_shape=[jax.ShapeDtypeStruct(s, F32) for s in shapes + [o.shape for o in others]],
        in_specs=[local] * 3 + [whole] * len(others),
        out_specs=[local] * 9 + [whole] * len(others),
        scratch_shapes=[pltpu.SemaphoreType.DMA((len(others),))],
        compiler_params=pltpu.CompilerParams(vmem_limit_bytes=60 * MIB),
    )(own, g_cn_up, g_cn_down, *others)


def pack_weights(ad_gate, ad_out, ad_high, w_qkv, w_proj, w_up, w_down, devices):
    dim, width = ad_gate.shape
    share, high_rows, wide = dim // devices, ad_high.shape[0] // devices, w_up.shape[1]
    rest = high_rows - share

    def kernel(gate, out, high, qkv, proj, up, down, packed, side, side_wide, sems):
        me = lax.axis_index("dp")
        mine = pl.ds(pl.multiple_of(me * share, share), share)
        lanes = mine

        def at(i, size=width):
            return packed.at[:, pl.ds(i * width, size)]

        straight = [(gate.at[mine], at(0)), (up.at[mine], at(8, wide))]
        straight += [(qkv.at[k, mine], at(4 + k)) for k in range(3)]
        straight.append((high.at[pl.ds(pl.multiple_of(me * high_rows, rest), share)], at(2)))
        straight.append((high.at[pl.ds(pl.multiple_of(me * high_rows + share, rest), rest)], at(3).at[pl.ds(0, rest)]))
        straight += [(out.at[:, lanes], side.at[0]), (proj.at[:, lanes], side.at[1]), (down.at[:, lanes], side_wide)]
        copies = [pltpu.make_async_copy(a, b, sems.at[i]) for i, (a, b) in enumerate(straight)]
        for copy in copies:
            copy.start()
        packed[rest:, 3 * width : 4 * width] = jnp.zeros((share - rest, width), BF)
        for copy in copies:
            copy.wait()
        packed[:, width : 2 * width] = side[0].T
        packed[:, 7 * width : 8 * width] = side[1].T
        packed[:, 8 * width + wide :] = side_wide[...].T

    whole = pl.BlockSpec(memory_space=pl.ANY)
    return pl.pallas_call(
        kernel,
        out_shape=jax.ShapeDtypeStruct((share, 8 * width + 2 * wide), BF),
        in_specs=[whole] * 7,
        out_specs=pl.BlockSpec(memory_space=pltpu.VMEM),
        scratch_shapes=[
            pltpu.VMEM((2, width, share), BF), pltpu.VMEM((wide, share), BF), pltpu.SemaphoreType.DMA((10,)),
        ],
        compiler_params=pltpu.CompilerParams(vmem_limit_bytes=60 * MIB),
    )(ad_gate, ad_out, ad_high, w_qkv, w_proj, w_up, w_down)


def rows_first(x):
    return with_layout_constraint(x, Layout(major_to_minor=tuple(range(x.ndim))))


def own_part(w, axis):
    length = w.shape[axis] // lax.axis_size("dp")
    return lax.dynamic_slice_in_dim(w, lax.axis_index("dp") * length, length, axis)


def fold(w, rows):
    return w[:rows], jnp.pad(w[rows:], ((0, 2 * rows - w.shape[0]), (0, 0)))


def core_first(x, devices):
    shape = x.shape
    return x.reshape(shape[:-1] + (devices // 2, 2, -1)).swapaxes(-3, -2).reshape(shape)


def core_last(x, devices):
    shape = x.shape
    return x.reshape(shape[:-1] + (2, devices // 2, -1)).swapaxes(-3, -2).reshape(shape)


def layer_norm(values, gain):
    centre = jnp.mean(values, -1, keepdims=True)
    centred = values - centre
    variance = jnp.mean(centred * centred, -1, keepdims=True)
    return centred * lax.rsqrt(variance + 1e-06) * gain


def per_device(
    hr_in,
    low_in,
    valid,
    conv_w,
    hr_gain,
    cn_up,
    cn_down,
    ad_gate,
    ad_high,
    ad_out,
    ln1_gain,
    w_qkv,
    w_proj,
    ln2_gain,
    w_up,
    w_down,
    cot_low,
    cot_hr,
):
    _, row_count, col_count, chan_count = hr_in.shape
    devices, shards = lax.axis_size("dp"), lax.axis_size("mp")
    dims = low_in.shape[2]
    share = dims // devices
    qkv = own_part(w_qkv, 1)
    low_weights = (ad_gate, ad_out, ad_high, w_qkv, w_proj, w_up, w_down)
    pieces = [
        own_part(ad_gate, 0), own_part(ad_out, 1).T, *fold(own_part(ad_high, 0), share),
        qkv[0], qkv[1], qkv[2], own_part(w_proj, 1).T, own_part(w_up, 0), own_part(w_down, 1).T,
    ]
    if share % LANES:
        packed = rows_first(jnp.concatenate(pieces, axis=1))
    else:
        packed = pack_weights(*low_weights, devices)
    packed = rows_first(lax.all_gather(packed, "mp", axis=0, tiled=True))
    plane_mask = valid[0].astype(F32)
    cell_mask = plane_mask[..., None]
    masked = hr_in[0] * valid[0].astype(BF)[..., None]
    half_rows, half_cols = (row_count // 2, col_count // 2)
    counts = plane_mask.reshape(half_rows, 2, half_cols, 2).sum(axis=(1, 3))
    shares = 1.0 / jnp.maximum(counts, 1.0)
    size = conv_w.shape[0]
    taps = conv_w.astype(F32).reshape(size * size, 1, chan_count)
    conv_out, bordered = conv_forward(masked, taps, size, shards)
    hr_gainf = hr_gain.astype(F32)
    normed = layer_norm(conv_out * cell_mask, hr_gainf).astype(BF)
    normed, packed = lax.optimization_barrier((normed, packed))
    packed = rows_first(lax.all_gather(packed, "dp", axis=0, tiled=True))
    hr_out, pooled, normed_all, hidden_act, hidden_slope, up_t, down_t = big_forward(
        normed.reshape(row_count * col_count, chan_count), cn_up, cn_down, masked, plane_mask, shares, shards
    )
    hr_out = hr_out.reshape(hr_in.shape)
    tokens = half_rows * half_cols
    by_share = pooled.reshape(tokens, devices, -1)
    pool_a = by_share[:, :, :share].reshape(tokens, dims)
    pool_b = jnp.pad(by_share[:, :, share:], ((0, 0), (0, 0), (0, 2 * share - by_share.shape[2]))).reshape(tokens, dims)
    low_out, d_low_in, d_pool_a, d_pool_b, g_ln1, g_ln2, low_grads = low_stage(
        *(core_first(v, devices) for v in (low_in[0], pool_a, pool_b, cot_low[0])),
        *(core_first(v.astype(F32), devices)[None] for v in (ln1_gain, ln2_gain)),
        packed, shards, devices, 2,
    )
    if share % LANES:
        low_out, d_low_in = core_last(low_out, devices), core_last(d_low_in, devices)
    low_out, d_low_in = low_out[None], d_low_in[None]
    g_ln1, g_ln2 = core_last(g_ln1[0], devices), core_last(g_ln2[0], devices)
    d_pooled = jnp.concatenate(
        [
            core_last(d_pool_a, devices).reshape(tokens, devices, share),
            core_last(d_pool_b, devices).reshape(tokens, devices, share)[:, :, : by_share.shape[2] - share],
        ],
        axis=2,
    )
    d_normed, d_map, cn_grads, low_sums = big_backward(
        cot_hr[0], d_pooled.reshape(tokens, chan_count), shares, plane_mask, normed_all, hidden_act, hidden_slope,
        up_t, down_t, low_grads, shards, devices,
    )
    low_sums = rows_first(low_sums.reshape(shards, share, -1))
    low_sums = rows_first(lax.psum_scatter(low_sums, "mp", scatter_dimension=0))
    low_gains = jnp.pad(jnp.stack([g_ln1, g_ln2]), ((0, 0), (0, chan_count - dims)))
    d_hr_in, small_sums, (g_cn_up, g_cn_down) = conv_backward(
        d_normed, conv_out, hr_gainf[None], cell_mask, bordered, d_map, taps, low_gains, size, cn_grads, devices, shards
    )
    d_hr_in = d_hr_in[None]
    g_conv = small_sums[: size * size].reshape(conv_w.shape)
    g_hr_gain, g_ln1, g_ln2 = small_sums[size * size], small_sums[-2, :dims], small_sums[-1, :dims]
    (
        g_ad_gate, g_ad_high, g_ad_out, g_qkv, g_proj, g_up, g_down, g_cn_up, g_cn_down,
        low_out, hr_out, d_low_in, d_hr_in,
    ) = weight_outputs(
        low_sums.reshape(share, -1), g_cn_up, g_cn_down, [p.shape[1] for p in pieces], ad_high.shape[0] // devices,
        (low_out, hr_out, d_low_in, d_hr_in),
    )
    g_cn_down = g_cn_down.T
    return (
        low_out,
        hr_out,
        d_low_in,
        d_hr_in,
        g_conv,
        g_hr_gain,
        g_cn_up,
        g_cn_down,
        g_ad_gate,
        g_ad_high,
        g_ad_out,
        g_ln1,
        g_qkv,
        g_proj,
        g_ln2,
        g_up,
        g_down,
    )


def solution(mesh):
    return jax.shard_map(
        per_device,
        mesh=mesh,
        in_specs=(
            P("dp", "mp", None, None),
            P("dp", "mp", None),
            P("dp", "mp", None),
            P(),
            P(),
            P(None, "mp"),
            P("mp", None),
            P(None, "mp"),
            P(None, "mp"),
            P("mp", None),
            P(),
            P(None, None, "mp"),
            P("mp", None),
            P(),
            P(None, "mp"),
            P("mp", None),
            P("dp", "mp", None),
            P("dp", "mp", None, None),
        ),
        out_specs=(
            P("dp", "mp", None),
            P("dp", "mp", None, None),
            P("dp", "mp", None),
            P("dp", "mp", None, None),
            P(),
            P(),
            P("dp", "mp"),
            P("mp", "dp"),
            P("dp", "mp"),
            P("dp", "mp"),
            P("mp", "dp"),
            P(),
            P(None, "dp", "mp"),
            P("mp", "dp"),
            P(),
            P("dp", "mp"),
            P("mp", "dp"),
        ),
        check_vma=False,
    )
```

```python
import jax
import jax.numpy as jnp
from jax import lax
from jax.experimental.layout import Layout, with_layout_constraint
from jax.experimental import pallas as pl
from jax.experimental.pallas import tpu as pltpu
from jax.sharding import PartitionSpec as P

HEAD = 64
LANES = 128
EDGE = 8
CHUNKS = 6
TILE = 512
MIB = 1024 * 1024
MESH = pl.DeviceIdType.MESH
BF = jnp.bfloat16
F32 = jnp.float32

def gelu_parts(x):
    c = 0.7978845608028654
    x2 = x * x
    t = jnp.tanh(c * x * (1.0 + 0.044715 * x2))
    half = 0.5 * (1.0 + t)
    slope = half + 0.5 * x * (1.0 - t * t) * (c * (1.0 + 3 * 0.044715 * x2))
    return x * half, slope


def gelu(x):
    c = 0.7978845608028654
    t = jnp.tanh(c * x * (1.0 + 0.044715 * (x * x)))
    return 0.5 * x * (1.0 + t)


def dp_bit(position):
    return lax.rem(lax.axis_index("dp") // 2**position, 2)


def dp_mate(position):
    return lax.axis_index("dp") + 2**position * (1 - 2 * dp_bit(position))


class Halving:
    def __init__(self, bits, lasts, shape, block):
        self.lasts, self.shape, self.block = lasts, shape, block
        left = list(bits)
        self.bits = [left.pop(0 if last else -1) for last in lasts]

    def split(self, count, p):
        if count == 1:
            return (1, 1)
        return (count // 2, 2) if self.lasts[p] else (2, count // 2)

    def buffers(self):
        count, rows, cols = self.shape
        got, held = [], []
        for p in range(len(self.bits)):
            count //= 2
            got.append(jax.ShapeDtypeStruct((count, rows, cols), BF))
            held.append(jax.ShapeDtypeStruct(self.split(count, p + 1) + (rows, cols), BF))
        return got + held

    def semaphores(self):
        return [pltpu.SemaphoreType.DMA((len(self.bits),))] * 2

    def bind(self, first, buffers, send, recv):
        steps = len(self.bits)
        self.now = [first] + list(buffers[steps:])
        self.got, self.send, self.recv = buffers[:steps], send, recv

    def part(self, p, mine):
        bit = dp_bit(self.bits[p])
        index = bit if mine else 1 - bit
        return self.now[p].at[:, index] if self.lasts[p] else self.now[p].at[index]

    def copy(self, p):
        return pltpu.make_async_remote_copy(
            src_ref=self.part(p, False), dst_ref=self.got[p], send_sem=self.send.at[p], recv_sem=self.recv.at[p],
            device_id={"dp": dp_mate(self.bits[p])}, device_id_type=MESH,
        )

    def start(self, p):
        self.copy(p).start()

    def finish(self, p, wait=True):
        if wait:
            self.copy(p).wait()
        count, rows, cols = self.got[p].shape
        ways = self.split(count, p + 1)

        def add(a, b, out):
            out[...] = (a[...].astype(F32) + b[...].astype(F32)).astype(BF).reshape(out.shape)

        flat = pl.BlockSpec((1, rows, self.block), lambda k, c: (k, 0, c))
        paired = pl.BlockSpec((1, 1, rows, self.block), lambda k, c: (k // ways[1], lax.rem(k, ways[1]), 0, c))
        pltpu.emit_pipeline(add, grid=(count, cols // self.block), in_specs=[flat, flat], out_specs=[paired])(
            self.part(p, True), self.got[p], self.now[p + 1]
        )


def chain_exchange(
    n, chunks, lag, gathered, partial, travel, sems, own_chunk, prepare, arrived, compute, mates=(), begin=None, turn=None, after=None, early=False
):
    ag_send, ag_recv, rs_send, rs_recv = sems
    d = lax.axis_index("mp")
    has_left, has_right = d > 0, d < n - 1

    barrier = pltpu.get_barrier_semaphore()

    @pl.when(has_left)
    def _():
        pl.semaphore_signal(barrier, inc=1, device_id={"mp": d - 1}, device_id_type=MESH)

    @pl.when(has_right)
    def _():
        pl.semaphore_signal(barrier, inc=1, device_id={"mp": d + 1}, device_id_type=MESH)

    for mate in mates:
        pl.semaphore_signal(barrier, inc=1, device_id={"dp": mate}, device_id_type=MESH)

    own_chunk(0)
    pl.semaphore_wait(barrier, has_left.astype(jnp.int32) + has_right.astype(jnp.int32) + len(mates))
    if begin is not None:
        begin()

    def ag(way, s, j):
        return pltpu.make_async_remote_copy(
            src_ref=gathered.at[s, j], dst_ref=gathered.at[s, j],
            send_sem=ag_send.at[way, s, j], recv_sem=ag_recv.at[s, j],
            device_id={"mp": d + 1 - 2 * way}, device_id_type=MESH,
        )

    def rs(way, s, j):
        there = d + 1 - 2 * way
        slot = jnp.where((s == there) & (way == 0), n, s)
        return pltpu.make_async_remote_copy(
            src_ref=travel.at[s, j], dst_ref=travel.at[slot, j],
            send_sem=rs_send.at[s, j], recv_sem=rs_recv.at[slot, j],
            device_id={"mp": there}, device_id_type=MESH,
        )

    def rs_wait(slot, j):
        pltpu.make_async_copy(travel.at[slot, j], travel.at[slot, j], rs_recv.at[slot, j]).wait()

    def first(j, _):
        @pl.when(j > 0)
        def _():
            own_chunk(j)

        @pl.when(has_right)
        def _():
            ag(0, d, j).start()

        @pl.when(has_left)
        def _():
            ag(1, d, j).start()

        return 0

    lax.fori_loop(0, chunks, first, 0)

    def flow(way, q):
        ql = jnp.clip(q, 0, n * chunks - 1)
        s, jj = ql // chunks, lax.rem(ql, chunks)
        if way == 1:
            s = n - 1 - s
        ahead = (s > d) if way == 0 else (s < d)
        source = has_left if way == 0 else has_right

        @pl.when((q >= 0) & (q < n * chunks) & (ahead | ((s == d) & source)))
        def _():
            @pl.when(source)
            def _():
                rs_wait(jnp.where(s == d, n, s) if way == 0 else s, jj)

            @pl.when(ahead & source)
            def _():
                travel[s, jj] = (partial[s, jj].astype(F32) + travel[s, jj].astype(F32)).astype(BF)

            @pl.when(ahead & jnp.logical_not(source))
            def _():
                travel[s, jj] = partial[s, jj].astype(BF)

            @pl.when(ahead)
            def _():
                rs(way, s, jj).start()

    def block_of(k, way):
        s = d - k + 2 * k * way
        return s, (s >= 0) & (s < n) & ((k > 0) | (way == 0))

    def receive(k, way, s, j):
        @pl.when(k > 0)
        def _():
            pltpu.make_async_copy(gathered.at[s, j], gathered.at[s, j], ag_recv.at[s, j]).wait()

            @pl.when((way == 0) & has_right)
            def _():
                ag(0, s, j).start()

            @pl.when((way == 1) & has_left)
            def _():
                ag(1, s, j).start()

        arrived(s, j)

    wait_one = 1 if early else 0

    def step(g, _):
        k, j = g // chunks, lax.rem(g, chunks)

        def sides(act):
            @pl.when(g < n * chunks)
            def _():
                def side(way, _):
                    s, ok = block_of(k, way)
                    pl.when(ok)(lambda: act(way, s))
                    return 0

                lax.fori_loop(0, 2, side, 0)

        def flows():
            flow(1, g - wait_one - (n - 1 - d) * lag)
            flow(0, g - wait_one - d * lag)

        if turn is not None:
            turn(g)
        if early:
            sides(lambda way, s: receive(k, way, s, j))
            flows()

            def later(way, s):
                prepare(way, s, j)
                compute(way, s, j)

            sides(later)
        else:
            def work(way, s):
                prepare(way, s, j)
                receive(k, way, s, j)
                compute(way, s, j)

            sides(work)
            flows()
        if after is not None:
            after(g)
        return 0

    lax.fori_loop(0, n * chunks + (n - 1) * lag + wait_one, step, 0)

    def drain(i, _):
        s, j = i // chunks, lax.rem(i, chunks)

        @pl.when(has_right & (s <= d))
        def _():
            ag(0, s, j).wait_send()

        @pl.when(has_left & (s >= d))
        def _():
            ag(1, s, j).wait_send()

        @pl.when(s < d)
        def _():
            rs(1, s, j).wait_send()

        @pl.when(s > d)
        def _():
            rs(0, s, j).wait_send()

        return 0

    lax.fori_loop(0, n * chunks, drain, 0)


def own_sum(n, d, j, partial, travel, total):
    total[...] = partial[d, j].astype(F32)

    @pl.when(d > 0)
    def _():
        total[...] += travel[n, j].astype(F32)

    @pl.when(d < n - 1)
    def _():
        total[...] += travel[d, j].astype(F32)


def chain_sems(n, chunks):
    dma = pltpu.SemaphoreType.DMA
    return [dma((2, n, chunks)), dma((n, chunks)), dma((n, chunks)), dma((n + 1, chunks))]


def chunk_buffers(n, rows, c, kept):
    return [
        pltpu.VMEM((n, CHUNKS, rows, c), BF),
        pltpu.VMEM((n, CHUNKS, rows, c), kept),
        pltpu.VMEM((n + 1, CHUNKS, rows, c), BF),
    ]


def columns(i):
    return pl.ds(pl.multiple_of(i * TILE, TILE), TILE)


def drain_copies(n, copy):
    def one(i, _):
        copy(i // CHUNKS, lax.rem(i, CHUNKS)).wait()
        return 0

    lax.fori_loop(0, n * CHUNKS, one, 0)


def big_forward(x, w_up, w_down, residual, mask, share, n):
    t, c = x.shape
    h = w_up.shape[1]
    rows = t // CHUNKS
    cols = residual.shape[1]
    half = cols // 2
    pairs = rows // cols // 2

    def kernel(
        x_ref, wu, wd, res, mask_ref, share_ref, out, pooled, x_all, act_all, slope_all, wu_t, wd_t,
        gathered, partial, travel, act, slope, total, folded, turned, copied, stored, load_sem, *sems
    ):
        d = lax.axis_index("mp")
        load = pltpu.make_async_copy(x_ref, gathered.at[d], load_sem)

        def own_chunk(j):
            if isinstance(j, int):
                load.start()
                load.wait()

        def x_copy(s, j):
            return pltpu.make_async_copy(gathered.at[s, j], x_all.at[s, j], copied.at[s, j])

        def prepare(way, s, j):
            pass

        def arrived(s, j):
            x_copy(s, j).start()

        def compute(way, s, j):
            block = gathered.at[s, j]

            def up(i, _):
                pre = jnp.dot(block[...], wu[:, columns(i)], preferred_element_type=F32)
                value, rate = gelu_parts(pre)
                act[:, columns(i)] = value.astype(BF)
                slope[:, columns(i)] = rate.astype(BF)
                return 0

            lax.fori_loop(0, h // TILE, up, 0)
            keep_act = pltpu.make_async_copy(act, act_all.at[s, j], stored.at[0])
            keep_slope = pltpu.make_async_copy(slope, slope_all.at[s, j], stored.at[1])
            keep_act.start()
            keep_slope.start()

            def down(i, _):
                partial[s, j, :, columns(i)] = jnp.dot(
                    act[...], wd[:, columns(i)], preferred_element_type=F32
                )
                return 0

            lax.fori_loop(0, c // TILE, down, 0)
            keep_act.wait()
            keep_slope.wait()

        def finish(j):
            pl.when(j > 0)(lambda: put(j - 1).wait())
            own_sum(n, d, j, partial, travel, total)
            values = (res[pl.ds(j * 2 * pairs, 2 * pairs)].reshape(rows, c).astype(F32) + total[...]) * mask_ref[j]
            partial[d, j] = values
            put(j).start()
            both = values.reshape(pairs, 2, cols, c)
            summed = (both[:, 0] + both[:, 1]).reshape(pairs * cols, c)
            for b in range(c // LANES):
                lanes = slice(b * LANES, (b + 1) * LANES)
                folded[b] = summed[:, lanes]
                every = folded[b, pl.ds(0, pairs * half, 2), :] + folded[b, pl.ds(1, pairs * half, 2), :]
                pooled[j, :, lanes] = (every * share_ref[j]).astype(BF)

        def put(j):
            return pltpu.make_async_copy(partial.at[d, j], out.at[j], load_sem)

        def after(g):
            last = g - (n - 1) * (CHUNKS + 1)
            pl.when(last >= 0)(lambda: finish(last))
            for i, (w, target, size) in enumerate(((wu, wu_t, h), (wd, wd_t, c))):
                @pl.when(g < size // LANES)
                def _():
                    some = pl.ds(pl.multiple_of(g * LANES, LANES), LANES)
                    turned[i, :, pl.ds(0, w.shape[0])] = w[:, some].T
                    copy = pltpu.make_async_copy(turned.at[i, :, pl.ds(0, w.shape[0])], target.at[some], stored.at[i])
                    copy.start()
                    copy.wait()

        chain_exchange(
            n, CHUNKS, 1, gathered, partial, travel, sems, own_chunk, prepare, arrived, compute, after=after
        )

        put(CHUNKS - 1).wait()
        drain_copies(n, x_copy)

    whole = pl.BlockSpec(memory_space=pl.ANY)
    local = pl.BlockSpec(memory_space=pltpu.VMEM)
    out, pooled, x_all, act_all, slope_all, wu_t, wd_t = pl.pallas_call(
        kernel,
        out_shape=(
            jax.ShapeDtypeStruct((CHUNKS, rows, c), F32),
            jax.ShapeDtypeStruct((CHUNKS, pairs * half, c), BF),
            jax.ShapeDtypeStruct((n, CHUNKS, rows, c), BF),
            jax.ShapeDtypeStruct((n, CHUNKS, rows, h), BF),
            jax.ShapeDtypeStruct((n, CHUNKS, rows, h), BF),
            jax.ShapeDtypeStruct((h, c), BF),
            jax.ShapeDtypeStruct((c, h), BF),
        ),
        in_specs=[whole, local, local, local, local, local],
        out_specs=(whole, local, whole, whole, whole, whole, whole),
        scratch_shapes=chunk_buffers(n, rows, c, F32)
        + [pltpu.VMEM((rows, h), BF)] * 2
        + [pltpu.VMEM((rows, c), F32), pltpu.VMEM((c // LANES, pairs * cols, LANES), F32), pltpu.VMEM((2, LANES, max(c, h)), BF)]
        + [pltpu.SemaphoreType.DMA((n, CHUNKS)), pltpu.SemaphoreType.DMA((2,)), pltpu.SemaphoreType.DMA]
        + chain_sems(n, CHUNKS),
        compiler_params=pltpu.CompilerParams(
            collective_id=0, has_side_effects=True, vmem_limit_bytes=60 * MIB
        ),
        cost_estimate=pl.CostEstimate(
            flops=4 * n * t * c * h, bytes_accessed=8 * n * t * c, transcendentals=n * t * h
        ),
    )(
        x.reshape(CHUNKS, rows, c), w_up, w_down, residual,
        mask.reshape(CHUNKS, rows, 1), share.reshape(CHUNKS, pairs * half, 1),
    )
    return (
        out.reshape(t, c),
        pooled.reshape(t // 4, c),
        x_all,
        act_all,
        slope_all,
        wu_t,
        wd_t,
    )


def big_backward(cot, d_pooled, share, mask, x_all, act_all, slope_all, up_t, down_t, grads, n, devices):
    _, cols, c = cot.shape
    t = cot.shape[0] * cols
    h = up_t.shape[0]
    rows = t // CHUNKS
    half = cols // 2
    pairs_here = rows // cols // 2
    piece = c // devices
    items = n * CHUNKS // 2
    pairs, g_rows, g_cols = grads.shape
    bits = range(1, devices.bit_length() - 1)
    split = g_rows // 2
    steps = len(bits)
    plans = [Halving(bits, [last] * steps, (pairs, split, g_cols), min(g_cols, 1024)) for last in (True, False)]
    extras = [b for plan in plans for b in plan.buffers()[:-1]]
    each = 2 * steps - 1

    def kernel(
        cot_ref, pool_ref, share_ref, mask_ref, x_hbm, act_hbm, slopes, wu, wd, g_first, g_second,
        out, d_own, g_up_out, g_down_out, out_up, out_down, got_up, got_down, h_all, *rest
    ):
        sums, extra, rest = rest[0], rest[1 : 1 + 2 * each], rest[1 + 2 * each :]
        gathered, partial, travel, slope, grad, left, right, middle, g_up, g_down, total, spread_rows, addend = rest[:13]
        core_send, core_recv, stored, add_sem, send0, recv0, send1, recv1 = rest[13:21]
        sems = rest[21:]
        d = lax.axis_index("mp")
        plans[0].bind(g_first.at[:, :, pl.ds(0, split)], extra[:each] + (sums.at[0],), send0, recv0)
        plans[1].bind(g_second.at[:, :, pl.ds(split, split)], extra[each:] + (sums.at[1],), send1, recv1)

        def begin():
            for plan in plans:
                plan.start(0)

        def pass_on(p, plan):
            plan.finish(p)
            if p + 1 < steps:
                plan.start(p + 1)

        first_due = 2 * CHUNKS + 3
        ticks = {}
        if steps == 2:
            for p, start in ((0, first_due), (1, n * CHUNKS + n - 2)):
                tiles = [
                    (plan, k, q)
                    for plan in plans
                    for k in range(plan.got[p].shape[0])
                    for q in range(g_cols // plan.block)
                ]
                for m in range(0, len(tiles), 4):
                    ticks[start + m // 4] = (p, m == 0, m + 4 >= len(tiles), tiles[m : m + 4])

        def tile_copy(which, p, i, plan, k, q):
            lanes = pl.ds(q * plan.block, plan.block)
            if which == 0:
                source, target = plan.part(p, True).at[k, :, lanes], addend.at[0, i]
            elif which == 1:
                source, target = plan.got[p].at[k, :, lanes], addend.at[1, i]
            else:
                ways = plan.split(plan.got[p].shape[0], p + 1)
                source, target = addend.at[0, i], plan.now[p + 1].at[k // ways[1], k % ways[1], :, lanes]
            return pltpu.make_async_copy(source, target, add_sem.at[which, i])

        def tick_begin(p, fresh, final, tiles):
            if fresh:
                for plan in plans:
                    plan.copy(p).wait()
            for i, tile in enumerate(tiles):
                for which in range(2):
                    tile_copy(which, p, i, *tile).start()

        def tick_add(p, fresh, final, tiles):
            for i, tile in enumerate(tiles):
                for which in range(2):
                    tile_copy(which, p, i, *tile).wait()
                addend[0, i] = (addend[0, i].astype(F32) + addend[1, i].astype(F32)).astype(BF)
                tile_copy(2, p, i, *tile).start()
            for i, tile in enumerate(tiles):
                tile_copy(2, p, i, *tile).wait()
            if final and p + 1 < steps:
                for plan in plans:
                    plan.start(p + 1)

        all_steps = n * CHUNKS + n
        due = [all_steps * 9 * (2**steps - 2 ** (steps - 1 - p)) // (10 * (2**steps - 1)) // 2 * 2 for p in range(steps)]

        def turn(g):
            if ticks:
                for at, tick in ticks.items():
                    pl.when(g == at)(lambda tick=tick: tick_begin(*tick))
            else:
                for p in range(steps - 1):
                    for i, plan in enumerate(plans):
                        pl.when(g == due[p] + 2 * i)(lambda p=p, plan=plan: pass_on(p, plan))

            q, due_now = item_of(g)

            @pl.when(due_now)
            def _():
                for copy in item_copies(q):
                    copy.start()

        def own_chunk(j):
            part = pool_ref[j] * share_ref[j]
            here = cot_ref.at[pl.ds(j * 2 * pairs_here, 2 * pairs_here)]
            for b in range(c // LANES):
                lanes = slice(b * LANES, (b + 1) * LANES)
                spread_rows[b, pl.ds(0, pairs_here * half, 2), :] = part[:, lanes]
                spread_rows[b, pl.ds(1, pairs_here * half, 2), :] = part[:, lanes]
                block = jnp.broadcast_to(
                    spread_rows[b].reshape(pairs_here, 1, cols, LANES), (pairs_here, 2, cols, LANES)
                ).reshape(rows, LANES)
                cell = here[:, :, lanes].reshape(rows, LANES).astype(F32)
                gathered[d, j, :, lanes] = ((cell + block) * mask_ref[j]).astype(BF)

        def slope_copy(s, j):
            return pltpu.make_async_copy(slopes.at[s, j], slope, stored.at[0])

        def prepare(way, s, j):
            slope_copy(s, j).start()

        def arrived(s, j):
            pass

        def compute(way, s, j):
            block = gathered.at[s, j]
            slope_copy(s, j).wait()

            def up(i, _):
                back = nn(block[...], wd[:, columns(i)])
                grad[:, columns(i)] = (back * slope[:, columns(i)].astype(F32)).astype(BF)
                return 0

            lax.fori_loop(0, h // TILE, up, 0)
            half_pair = pl.ds(pl.multiple_of(lax.rem(j, 2) * rows, rows), rows)
            keep = pltpu.make_async_copy(grad, h_all.at[s, j // 2, half_pair], stored.at[1])
            keep.start()

            def down(i, _):
                partial[s, j, :, columns(i)] = nn(grad[...], wu[:, columns(i)]).astype(BF)
                return 0

            lax.fori_loop(0, c // TILE, down, 0)
            keep.wait()

        def item_place(q):
            s, jj, base = d, q, CHUNKS // 2
            for k in range(1, n):
                to_left, to_right = d - k >= 0, d + k < n
                two = to_left & to_right
                r = q - base
                here = (r >= 0) & (to_left | to_right)
                s = jnp.where(here, jnp.where(to_left & (jnp.logical_not(two) | (lax.rem(r, 2) == 0)), d - k, d + k), s)
                jj = jnp.where(here, jnp.where(two, r // 2, r), jj)
                base = base + (CHUNKS // 2) * (to_left.astype(jnp.int32) + to_right.astype(jnp.int32))
            return s, jj

        def item_copies(q):
            s, jj = item_place(q)
            return (
                pltpu.make_async_copy(x_hbm.at[s, jj], left, stored.at[2]),
                pltpu.make_async_copy(act_hbm.at[s, jj], right, stored.at[3]),
                pltpu.make_async_copy(h_all.at[s, jj], middle, stored.at[4]),
            )

        between = (d > 0) & (d < n - 1)

        def item_of(g):
            q = jnp.where(between, g - items, (g - 3) // 2)
            return q, (q >= 0) & (q < items) & (g >= 3) & (between | (lax.rem(g, 2) == 1))

        def after(g):
            for at, tick in ticks.items():
                pl.when(g == at)(lambda tick=tick: tick_add(*tick))
            last = g - 1 - (n - 1) * (CHUNKS + 1)
            pl.when(last >= 0)(lambda: finish(last))
            q, due_now = item_of(g)

            @pl.when(due_now)
            def _():
                s, jj = item_place(q)
                for copy in item_copies(q):
                    copy.wait()

                def tile(i, _):
                    a = columns(i)
                    g_up[a] += tn(left[:, a], middle[...])
                    db = gathered[s, pl.ds(2 * jj, 2), :, a].reshape(2 * rows, TILE)
                    g_down[a] += tn(db, right[...])
                    return 0

                lax.fori_loop(0, c // TILE, tile, 0)

            @pl.when(g == 2 * items + 2)
            def _():
                give(g_up, left, out_up, stored.at[2])
                swaps[0].start()

            @pl.when(g == 2 * items + 3)
            def _():
                give(g_down, right, out_down, stored.at[3])
                swaps[1].start()

        core = dp_bit(0)

        def result(j):
            return pltpu.make_async_copy(total, out.at[j], stored.at[5])

        def finish(j):
            pl.when(j > 0)(lambda: result(j - 1).wait())
            own_sum(n, d, j, partial, travel, total)
            result(j).start()

        def rows_at(i):
            return pl.ds(pl.multiple_of(i * piece, piece), piece)

        def give(source, stage, target, sem):
            def one(i, _):
                stage[pl.ds(0, piece)] = source[rows_at(2 * i + 1 - core)].astype(BF)
                copy = pltpu.make_async_copy(stage.at[pl.ds(0, piece)], target.at[i], sem)
                copy.start()
                copy.wait()
                return 0

            lax.fori_loop(0, devices // 2, one, 0)

        def keep_sums():
            sets = ((g_up, left, got_up, g_up_out, 2), (g_down, right, got_down, g_down_out, 3))

            def loads(i):
                return [
                    pltpu.make_async_copy(got.at[i], stage.at[pl.ds(0, piece)], stored.at[sem])
                    for _, stage, got, _, sem in sets
                ]

            def one(i, _):
                for load in loads(i):
                    load.start()
                saves = []
                for load, (source, stage, _, target, sem) in zip(loads(i), sets):
                    load.wait()
                    here = stage.at[pl.ds(0, piece)]
                    here[...] = (source[rows_at(2 * i + core)] + here[...].astype(F32)).astype(BF)
                    saves.append(pltpu.make_async_copy(here, target.at[i], stored.at[sem]))
                    saves[-1].start()
                for save in saves:
                    save.wait()
                return 0

            lax.fori_loop(0, devices // 2, one, 0)

        swaps = [
            pltpu.make_async_remote_copy(
                src_ref=src, dst_ref=dst, send_sem=core_send.at[i], recv_sem=core_recv.at[i],
                device_id={"dp": dp_mate(0)}, device_id_type=MESH,
            )
            for i, (src, dst) in enumerate(((out_up, got_up), (out_down, got_down)))
        ]
        def clear(i, _):
            some = pl.ds(pl.multiple_of(i * TILE, TILE), TILE)
            g_up[some] = jnp.zeros((TILE, h), F32)
            g_down[some] = jnp.zeros((TILE, h), F32)
            return 0

        def begin_all():
            begin()
            lax.fori_loop(0, c // TILE, clear, 0)

        chain_exchange(
            n, CHUNKS, 1, gathered, partial, travel, sems, own_chunk, prepare, arrived, compute,
            [dp_mate(b) for b in range(steps + 1)], begin_all, turn, after, True,
        )
        keep = pltpu.make_async_copy(gathered.at[d], d_own, stored.at[0])
        keep.start()
        result(CHUNKS - 1).wait()
        keep.wait()
        if not ticks:
            for plan in plans:
                pass_on(steps - 1, plan)
        for swap in swaps:
            swap.wait()
        keep_sums()

    whole = pl.BlockSpec(memory_space=pl.ANY)
    local = pl.BlockSpec(memory_space=pltpu.VMEM)
    dma = pltpu.SemaphoreType.DMA
    out, d_own, g_up, g_down, _, _, _, _, _, sums, *_ = pl.pallas_call(
        kernel,
        out_shape=(
            jax.ShapeDtypeStruct((CHUNKS, rows, c), F32),
            jax.ShapeDtypeStruct((CHUNKS, rows, c), BF),
            *[jax.ShapeDtypeStruct((devices // 2, piece, h), BF)] * 6,
            jax.ShapeDtypeStruct((n, CHUNKS // 2, 2 * rows, h), BF),
            jax.ShapeDtypeStruct((2, 1, 1, split, g_cols), BF),
            *extras,
        ),
        in_specs=[local] * 4 + [whole] * 3 + [local] * 2 + [whole] * 2,
        out_specs=(whole,) * (10 + 2 * each),
        scratch_shapes=chunk_buffers(n, rows, c, BF)
        + [
            pltpu.VMEM((rows, h), BF), pltpu.VMEM((rows, h), BF),
            pltpu.VMEM((2 * rows, c), BF), pltpu.VMEM((2 * rows, h), BF), pltpu.VMEM((2 * rows, h), BF),
            pltpu.VMEM((c, h), F32), pltpu.VMEM((c, h), F32),
            pltpu.VMEM((rows, c), F32), pltpu.VMEM((c // LANES, pairs_here * cols, LANES), F32),
            pltpu.VMEM((2, 4, split, plans[0].block), BF),
            dma((2,)), dma((2,)), dma((6,)), dma((3, 4)),
        ]
        + plans[0].semaphores() + plans[1].semaphores()
        + chain_sems(n, CHUNKS),
        compiler_params=pltpu.CompilerParams(
            collective_id=1, has_side_effects=True, vmem_limit_bytes=62 * MIB
        ),
        cost_estimate=pl.CostEstimate(
            flops=8 * n * t * c * h, bytes_accessed=8 * n * t * c, transcendentals=0
        ),
    )(
        cot, d_pooled.reshape(CHUNKS, pairs_here * half, c), share.reshape(CHUNKS, pairs_here * half, 1),
        mask.reshape(CHUNKS, rows, 1), *(v.reshape(n, CHUNKS // 2, 2 * rows, -1) for v in (x_all, act_all)),
        slope_all, up_t, down_t,
        grads.reshape(pairs // 2, 2, g_rows, g_cols), grads.reshape(2, pairs // 2, g_rows, g_cols),
    )
    return (
        out.reshape(cot.shape), d_own.reshape(cot.shape), [g_up, g_down],
        sums.reshape(g_rows, g_cols),
    )


def frame(dst, src):
    rows, cols, _ = src.shape
    dst[:, :EDGE] = jnp.zeros((rows, EDGE, LANES), F32)
    dst[:, EDGE + cols:] = jnp.zeros((rows, EDGE, LANES), F32)
    dst[:, EDGE:EDGE + cols] = src[...].astype(F32)


def correlate(out, framed, taps, size, flip, group, first=0, last=None, every=1):
    rows, cols, _ = out.shape
    reach = size // 2
    def some(k, _):
        r = first + k * every
        acc = jnp.zeros((group, cols, LANES), F32)
        for a in range(size):
            for b in range(size):
                tap = (size - 1 - a) * size + size - 1 - b if flip else a * size + b
                acc = acc + framed[pl.ds(r * group + a, group), pl.ds(EDGE - reach + b, cols), :] * taps[tap]
        out[pl.ds(r * group, group)] = acc
        return 0
    lax.fori_loop(0, (rows // group if last is None else last) - first if every == 1 else 2, some, 0)


def conv_forward(x, w, size, n):
    rows, cols, c = x.shape
    reach = size // 2

    def kernel(x_ref, w_ref, out, bordered, framed, sent, got, own):
        d = lax.axis_index("mp")
        has_up, has_down = d > 0, d < n - 1
        barrier = pltpu.get_barrier_semaphore()

        @pl.when(has_up)
        def _():
            pl.semaphore_signal(barrier, inc=1, device_id={"mp": d - 1}, device_id_type=MESH)

        @pl.when(has_down)
        def _():
            pl.semaphore_signal(barrier, inc=1, device_id={"mp": d + 1}, device_id_type=MESH)

        keep = pltpu.make_async_copy(x_ref, bordered.at[pl.ds(reach, rows)], own)
        keep.start()
        pl.semaphore_wait(barrier, has_up.astype(jnp.int32) + has_down.astype(jnp.int32))
        up = pltpu.make_async_remote_copy(
            src_ref=x_ref.at[pl.ds(0, reach)], dst_ref=bordered.at[pl.ds(reach + rows, reach)],
            send_sem=sent.at[0], recv_sem=got.at[0], device_id={"mp": d - 1}, device_id_type=MESH,
        )
        down = pltpu.make_async_remote_copy(
            src_ref=x_ref.at[pl.ds(rows - reach, reach)], dst_ref=bordered.at[pl.ds(0, reach)],
            send_sem=sent.at[1], recv_sem=got.at[1], device_id={"mp": d + 1}, device_id_type=MESH,
        )
        nothing = jnp.zeros((reach, cols, c), BF)

        @pl.when(has_up)
        def _():
            up.start()

        @pl.when(has_down)
        def _():
            down.start()

        @pl.when(d == 0)
        def _():
            bordered[:reach] = nothing

        @pl.when(d == n - 1)
        def _():
            bordered[reach + rows :] = nothing

        groups = rows // reach

        def inner(i, _):
            lanes = pl.ds(pl.multiple_of(i * LANES, LANES), LANES)
            frame(framed.at[pl.ds(reach, rows)], x_ref.at[:, :, lanes])
            correlate(out.at[:, :, lanes], framed, w_ref.at[:, :, lanes], size, False, reach, 1, groups - 1)
            return 0

        lax.fori_loop(0, c // LANES, inner, 0)
        keep.wait()

        @pl.when(has_up)
        def _():
            down.wait_recv()

        @pl.when(has_down)
        def _():
            up.wait_recv()

        def block(i, _):
            lanes = pl.ds(pl.multiple_of(i * LANES, LANES), LANES)
            frame(framed, bordered.at[:, :, lanes])
            correlate(out.at[:, :, lanes], framed, w_ref.at[:, :, lanes], size, False, reach, 0, None, groups - 1)
            return 0

        lax.fori_loop(0, c // LANES, block, 0)

        @pl.when(has_up)
        def _():
            up.wait_send()

        @pl.when(has_down)
        def _():
            down.wait_send()

    local = pl.BlockSpec(memory_space=pltpu.VMEM)
    dma = pltpu.SemaphoreType.DMA
    return pl.pallas_call(
        kernel,
        out_shape=(
            jax.ShapeDtypeStruct((rows, cols, c), F32),
            jax.ShapeDtypeStruct((rows + 2 * reach, cols, c), BF),
        ),
        in_specs=[local, local],
        out_specs=(local, local),
        scratch_shapes=[pltpu.VMEM((rows + 2 * reach, cols + 2 * EDGE, LANES), F32), dma((2,)), dma((2,)), dma],
        compiler_params=pltpu.CompilerParams(
            collective_id=5, has_side_effects=True, vmem_limit_bytes=40 * MIB
        ),
    )(x, w)


def conv_backward(d_normed, conv_out, gain, mask, bordered, d_map, w, low_gains, size, grads, devices, n):
    rows, cols, c = conv_out.shape
    reach = size // 2
    high = rows + 2 * reach
    group = 4 if rows % 4 == 0 else 1
    bits = range(1, devices.bit_length() - 1)
    steps = len(bits)
    shape = grads[0].shape
    plans = [Halving(bits, [last] * steps, shape, shape[2]) for last in (True, False)]
    each = 2 * steps
    blocks = c // LANES
    taps = size * size
    count = taps + 1 + low_gains.shape[0]
    small = -(-count // devices)
    first_due = blocks + blocks // 3
    halving = {first_due + 2 * blocks // 3 * p // (steps - 1): p for p in range(steps - 1)}
    rounds = {blocks + 7 * blocks // 12: 1, blocks + 10 * blocks // 12: 2}

    def kernel(
        dn, co, gain_ref, mask_ref, w_ref, low_ref, b_hbm, dm_hbm, g0, g1, out, g_all, *rest
    ):
        extra, rest = rest[: 2 * each], rest[2 * each :]
        around, x_around, d_here, dframed, xframed, g_own, here, level, sent, got, own = rest[:11]
        ar, halving_sems = rest[11:17], rest[17:]
        plans[0].bind(g0, extra[:each], halving_sems[0], halving_sems[1])
        plans[1].bind(g1, extra[each:], halving_sems[2], halving_sems[3])
        me, d = lax.axis_index("dp"), lax.axis_index("mp")
        has_up, has_down = d > 0, d < n - 1
        barrier = pltpu.get_barrier_semaphore()

        def greet(k, _):
            pl.semaphore_signal(
                barrier, inc=1, device_id={"dp": lax.rem(me + k, devices)}, device_id_type=MESH
            )
            return 0

        lax.fori_loop(1, devices, greet, 0)
        for k in range(1, n):
            pl.semaphore_signal(barrier, inc=1, device_id={"mp": lax.rem(d + k, n)}, device_id_type=MESH)
        load_x = pltpu.make_async_copy(b_hbm, x_around, own.at[0])
        load_d = pltpu.make_async_copy(dm_hbm, d_here, own.at[1])
        load_x.start()
        load_d.start()

        def pass_on(p):
            for plan in plans:
                plan.finish(p)
            if p == 0:
                sum_round(0)
            if p + 1 < steps:
                for plan in plans:
                    plan.start(p + 1)

        def keep(row, lanes, value):
            g_own[row // small, row % small : row % small + 1, lanes] = value

        pl.semaphore_wait(barrier, devices + n - 2)
        for plan in plans:
            plan.start(0)
        g_own[...] = jnp.zeros(g_own.shape, F32)

        def norm(r, total):
            cells = mask_ref[r]
            back, part = normalise_back(co[r] * cells, gain_ref[...], dn[r])
            around[reach + r] = (back * cells).astype(BF)
            return total + part

        keep(taps, slice(None), lax.fori_loop(0, rows, norm, jnp.zeros((1, c), F32)))
        for i in range(low_gains.shape[0]):
            keep(taps + 1 + i, slice(None), low_ref[i : i + 1])
        up = pltpu.make_async_remote_copy(
            src_ref=around.at[pl.ds(reach, reach)], dst_ref=around.at[pl.ds(reach + rows, reach)],
            send_sem=sent.at[0], recv_sem=got.at[0], device_id={"mp": d - 1}, device_id_type=MESH,
        )
        down = pltpu.make_async_remote_copy(
            src_ref=around.at[pl.ds(rows, reach)], dst_ref=around.at[pl.ds(0, reach)],
            send_sem=sent.at[1], recv_sem=got.at[1], device_id={"mp": d + 1}, device_id_type=MESH,
        )
        nothing = jnp.zeros((reach, cols, c), BF)

        @pl.when(has_up)
        def _():
            up.start()

        @pl.when(has_down)
        def _():
            down.start()

        @pl.when(d == 0)
        def _():
            around[:reach] = nothing

        @pl.when(d == n - 1)
        def _():
            around[reach + rows :] = nothing

        load_x.wait()

        def lanes_of(i):
            return pl.ds(pl.multiple_of(i * LANES, LANES), LANES)

        def kernel_block(i, _):
            lanes = lanes_of(i)
            frame(dframed.at[pl.ds(reach, rows)], around.at[pl.ds(reach, rows), :, lanes])
            frame(xframed, x_around.at[:, :, lanes])
            for a in range(size):
                def some(r, accs):
                    dv = dframed[pl.ds(reach + r * group, group), EDGE : EDGE + cols]
                    new = []
                    for b in range(size):
                        prod = dv * xframed[pl.ds(r * group + a, group), pl.ds(EDGE - reach + b, cols), :]
                        new.append(accs[b] + jnp.sum(prod.reshape(-1, 8, LANES), axis=0))
                    return tuple(new)

                accs = lax.fori_loop(
                    0, rows // group, some, tuple(jnp.zeros((8, LANES), F32) for _ in range(size))
                )
                for b in range(size):
                    keep(a * size + b, lanes, jnp.sum(accs[b], axis=0, keepdims=True))
            return 0

        def input_block(i, _):
            lanes = lanes_of(i)
            frame(dframed, around.at[:, :, lanes])
            correlate(out.at[:, :, lanes], dframed, w_ref.at[:, :, lanes], size, True, group)
            for r in range(rows):
                out[r, :, lanes] = (out[r, :, lanes] + d_here[r, :, lanes].astype(F32)) * mask_ref[r]
            return 0

        def spread(k):
            peer = lax.rem(me + k, devices)
            return pltpu.make_async_remote_copy(
                src_ref=g_own.at[peer], dst_ref=here.at[me], send_sem=ar[0].at[k], recv_sem=ar[1].at[k],
                device_id={"dp": peer}, device_id_type=MESH,
            )

        def across(k):
            return pltpu.make_async_remote_copy(
                src_ref=level.at[d], dst_ref=level.at[d], send_sem=ar[2].at[k], recv_sem=ar[3].at[k],
                device_id={"mp": lax.rem(d + k, n)}, device_id_type=MESH,
            )

        def tell(k):
            return pltpu.make_async_remote_copy(
                src_ref=g_all.at[me], dst_ref=g_all.at[me], send_sem=ar[4].at[k], recv_sem=ar[5].at[k],
                device_id={"dp": lax.rem(me + k, devices)}, device_id_type=MESH,
            )

        def all_of(length, make, act):
            def one(k, _):
                act(make(k))
                return 0

            lax.fori_loop(1, length, one, 0)

        def sum_round(p):
            if p == 0:
                here[me] = g_own[me]
                all_of(devices, spread, lambda x: x.start())
            elif p == 1:
                all_of(devices, spread, lambda x: x.wait())
                level[d] = jnp.sum(here[...], axis=0)
                all_of(n, across, lambda x: x.start())
            elif p == 2:
                all_of(n, across, lambda x: x.wait())
                g_all[me] = jnp.sum(level[...], axis=0)
                all_of(devices, tell, lambda x: x.start())
            else:
                all_of(devices, tell, lambda x: x.wait())

        marks = sorted(set(halving) | set(rounds) | {blocks, 2 * blocks})
        at = 0
        for mark in marks:
            if at < blocks:
                lax.fori_loop(at, min(mark, blocks), kernel_block, 0)
            else:
                lax.fori_loop(at - blocks, mark - blocks, input_block, 0)
            at = mark
            if mark in halving:
                pass_on(halving[mark])
            if mark == blocks:
                load_d.wait()

                @pl.when(has_up)
                def _():
                    down.wait_recv()

                @pl.when(has_down)
                def _():
                    up.wait_recv()
            if mark in rounds:
                sum_round(rounds[mark])
        pass_on(steps - 1)
        sum_round(3)

        @pl.when(has_up)
        def _():
            up.wait_send()

        @pl.when(has_down)
        def _():
            down.wait_send()

    whole = pl.BlockSpec(memory_space=pl.ANY)
    local = pl.BlockSpec(memory_space=pltpu.VMEM)
    vm, dma = pltpu.VMEM, pltpu.SemaphoreType.DMA
    d_in, g_all, *extra = pl.pallas_call(
        kernel,
        out_shape=(
            jax.ShapeDtypeStruct((rows, cols, c), F32),
            jax.ShapeDtypeStruct((devices, small, c), F32),
            *plans[0].buffers(),
            *plans[1].buffers(),
        ),
        in_specs=[local] * 6 + [whole] * 4,
        out_specs=(local,) * 2 + (whole,) * (2 * each),
        scratch_shapes=[
            vm((high, cols, c), BF), vm((high, cols, c), BF), vm((rows, cols, c), BF),
            vm((high, cols + 2 * EDGE, LANES), F32), vm((high, cols + 2 * EDGE, LANES), F32),
            vm((devices, small, c), F32), vm((devices, small, c), F32), vm((n, small, c), F32),
            dma((2,)), dma((2,)), dma((2,)),
            dma((devices,)), dma((devices,)), dma((n,)), dma((n,)), dma((devices,)), dma((devices,)),
        ]
        + plans[0].semaphores() + plans[1].semaphores(),
        compiler_params=pltpu.CompilerParams(
            collective_id=3, has_side_effects=True, vmem_limit_bytes=50 * MIB
        ),
        cost_estimate=pl.CostEstimate(flops=6 * 10**10, bytes_accessed=10**8, transcendentals=0),
    )(
        d_normed, conv_out, gain, mask, w, low_gains, bordered, d_map,
        grads[0].reshape((shape[0] // 2, 2) + shape[1:]), grads[1].reshape((2, shape[0] // 2) + shape[1:]),
    )
    sums = g_all.reshape(devices * small, c)[:count]
    return d_in, sums, [extra[each - 1].reshape(shape[1:]), extra[2 * each - 1].reshape(shape[1:])]


GATE, OUT, HIGH_A, HIGH_B, QUERY, KEY, VALUE, PROJ = range(8)
L_LOW, L_DF, L_POOL_A, L_POOL_B, L_FIRST, L_DA, L_SECOND, L_COT = range(8)
R_DGATE, R_MERGE, R_DHIGH, R_DQ, R_DK, R_DV, R_ATT, R_DUP, R_ACT = range(9)


def nn(a, b):
    return jnp.dot(a, b, preferred_element_type=F32)


def nt(a, b):
    return lax.dot_general(a, b, (((1,), (1,)), ((), ())), preferred_element_type=F32)


def tn(a, b):
    return lax.dot_general(a, b, (((0,), (0,)), ((), ())), preferred_element_type=F32)


def normalise(x, gain):
    centred = x - jnp.mean(x, -1, keepdims=True)
    rate = lax.rsqrt(jnp.mean(centred * centred, -1, keepdims=True) + 1e-06)
    return centred * rate * gain


def normalise_back(x, gain, d):
    centred = x - jnp.mean(x, -1, keepdims=True)
    rate = lax.rsqrt(jnp.mean(centred * centred, -1, keepdims=True) + 1e-06)
    hat = centred * rate
    dg = d * gain
    back = rate * (dg - jnp.mean(dg, -1, keepdims=True) - hat * jnp.mean(dg * hat, -1, keepdims=True))
    return back, jnp.sum(d * hat, axis=0, keepdims=True)


def low_stage(low, pool_a, pool_b, cot, gain1, gain2, packed, n, devices, cid):
    t, dim = low.shape
    every = n * t
    width = dim // n
    heads = width // HEAD
    pairs = devices // 2
    rows = dim // devices
    half = dim // 2
    ff = 4 * dim
    scale = HEAD ** (-0.5)

    def kernel(
        low_ref, pool_a_ref, pool_b_ref, cot_ref, gain1_ref, gain2_ref, w_hbm,
        low_out, d_low, d_pool_a, d_pool_b, g_ln1, g_ln2, grads,
        wv, lhs, lhs2, rhs, gate, high, merged, resid, d_res, slope, mixed, heads_in, att_all, d_att, d_mixed,
        d_heads, probs, d_scores, stage, left, w_sem, q_send, q_got, a_send, a_got, b_send, b_got, c_send, c_got, own_sem,
        l_send, l_got, r_send, r_got, stage_sem,
    ):
        d = lax.axis_index("mp")
        dp = lax.axis_index("dp")
        core = lax.rem(dp, 2)
        mate = dp + 1 - 2 * core
        barrier = pltpu.get_barrier_semaphore()
        for k in range(1, n):
            pl.semaphore_signal(barrier, inc=1, device_id={"mp": lax.rem(d + k, n)}, device_id_type=MESH)
        pl.semaphore_signal(barrier, inc=1, device_id={"dp": mate}, device_id_type=MESH)

        def w_copy(w, k):
            c, z = k // n, lax.rem(k, n)
            wide, base, at = w_place(w)
            src = w_hbm.at[:, c, z, :, pl.ds(base, wide)]
            dst = wv.at[c, :, :, pl.ds(pl.multiple_of(at + z * wide, wide), wide)]
            return pltpu.make_async_copy(src, dst, w_sem.at[w, k])

        def w_place(w):
            if w < 8:
                return width, w * width, w * dim
            return ff // n, 8 * width + (w - 8) * ff // n, 8 * dim + (w - 8) * ff

        def w_each(w, act):
            def one(k, _):
                act(w_copy(w, k))
                return 0

            lax.fori_loop(0, 2 * n, one, 0)

        for w in range(10):
            w_each(w, lambda copy: copy.start())

        def w_wait(*which):
            for w in which:
                w_each(w, lambda copy: copy.wait())

        def w_cols(at, size):
            return wv[:, :, :, pl.ds(at, size)].reshape(dim, size)

        def forward(x, first, count, put):
            def one(i, _):
                put(pl.multiple_of(i * TILE, TILE), nn(x, w_cols(pl.multiple_of(first * dim + i * TILE, TILE), TILE)))
                return 0
            lax.fori_loop(0, count * dim // TILE, one, 0)

        def backward(get, first, count, dst, fresh):
            def one(i, _):
                for c in range(2):
                    part = wv[c, :, :, pl.ds(pl.multiple_of((first + i) * dim, dim), dim)].reshape(half, dim)
                    y = nt(get(pl.multiple_of(i * dim, dim)), part)
                    cols = slice(c * half, (c + 1) * half)
                    if fresh and count == 1:
                        dst[:, cols] = y
                    else:
                        dst[:, cols] += y
                return 0
            if fresh and count > 1:
                dst[...] = jnp.zeros(dst.shape, F32)
            if count == 1:
                one(0, 0)
            else:
                lax.fori_loop(0, count, one, 0)

        def r_cols(block, count=1):
            return pl.ds(block * dim, count * dim)

        def r_at(block):
            return block * dim if block <= R_DUP else block * dim + 3 * dim

        def r_copy(block):
            cols = pl.ds(r_at(block), dim if block < R_DUP else ff)
            return pltpu.make_async_remote_copy(
                src_ref=rhs.at[0, :, cols], dst_ref=rhs.at[1, :, cols], send_sem=r_send.at[block],
                recv_sem=r_got.at[block], device_id={"dp": mate}, device_id_type=MESH)

        def l_copy(i):
            return pltpu.make_async_remote_copy(
                src_ref=lhs.at[i, :, pl.ds(pl.multiple_of((1 - core) * half, half), half)], dst_ref=lhs2.at[i],
                send_sem=l_send.at[i], recv_sem=l_got.at[i], device_id={"dp": mate}, device_id_type=MESH)

        stored = []
        turned = [None]

        def put_natural(dst, value):
            if rows % LANES:
                dst[...] = value
            else:
                for k in range(devices):
                    at = (k % 2) * half + k // 2 * rows
                    dst[:, k * rows : (k + 1) * rows] = value[:, at : at + rows]

        def grad(i, block, at, count, shared=False):
            if not shared:
                r_copy(block).wait_recv()
            if turned[0] != i:
                left[0] = lhs[i, :, pl.ds(pl.multiple_of(core * half, half), half)].T
                left[1] = lhs2[i].T
                turned[0] = i

            wide, base, first = w_place(at if at < 8 else 8 + (at - 8) * dim // ff)
            piece = min(TILE, wide)

            def out_copies(slot, k):
                out = []
                for q in range(TILE // piece):
                    z, col = divmod(at * dim - first + k * TILE + q * piece, wide)
                    out.append(
                        pltpu.make_async_copy(
                            stage.at[slot, :, :, pl.ds(q * piece, piece)],
                            grads.at[:, pl.ds(z * rows, rows), pl.ds(base + col, piece)],
                            stage_sem.at[slot, q],
                        )
                    )
                return out

            for k in range(count * dim // TILE):
                slot = len(stored) % 2
                if len(stored) >= 2:
                    wait(stored[-2])
                cols = pl.ds(r_at(block) + k * TILE, TILE)
                y = nn(left[0], rhs[0, :, cols]) + nn(left[1], rhs[1, :, cols])
                stage[slot] = y.astype(BF).reshape(pairs, rows, TILE)
                stored.append(out_copies(slot, k))
                start(stored[-1])

        def to_heads(k, src, dst, send, got):
            out = []
            for step in range(1, n):
                peer = lax.rem(d + step, n)
                out.append(pltpu.make_async_remote_copy(
                    src_ref=src.at[:, pl.ds(pl.multiple_of(peer * width, width), width)],
                    dst_ref=dst.at[pl.ds(pl.multiple_of(d * t, t), t)],
                    send_sem=send.at[k, step], recv_sem=got.at[k, step], device_id={"mp": peer}, device_id_type=MESH))
            out.append(pltpu.make_async_copy(
                src.at[:, pl.ds(pl.multiple_of(d * width, width), width)], dst.at[pl.ds(pl.multiple_of(d * t, t), t)], own_sem.at[k]))
            return out

        def to_tokens(k, src, dst, send, got):
            out = []
            for step in range(1, n):
                peer = lax.rem(d + step, n)
                out.append(pltpu.make_async_remote_copy(
                    src_ref=src.at[pl.ds(pl.multiple_of(peer * t, t), t)],
                    dst_ref=dst.at[:, pl.ds(pl.multiple_of(d * width, width), width)],
                    send_sem=send.at[k, step], recv_sem=got.at[k, step], device_id={"mp": peer}, device_id_type=MESH))
            out.append(pltpu.make_async_copy(
                src.at[pl.ds(pl.multiple_of(d * t, t), t)], dst.at[:, pl.ds(pl.multiple_of(d * width, width), width)], own_sem.at[k]))
            return out

        def start(copies):
            for c in copies:
                c.start()

        def wait(copies):
            for c in copies:
                c.wait()

        lhs[L_LOW] = low_ref[...]
        lhs[L_POOL_A] = pool_a_ref[...]
        lhs[L_POOL_B] = pool_b_ref[...]
        lhs[L_COT] = cot_ref[...]
        acc = d_low
        w_wait(GATE)

        def put_gate(at, y):
            gate[:, pl.ds(at, TILE)] = 1.0 / (1.0 + jnp.exp(-y))
        forward(lhs[L_LOW], GATE, 1, put_gate)
        w_wait(HIGH_A, HIGH_B, OUT)

        def put_high(at, y):
            high[:, pl.ds(at, TILE)] = y
        forward(lhs[L_POOL_A], HIGH_A, 1, put_high)

        def put_merging(at, y):
            cols = pl.ds(at, TILE)
            total = high[:, cols] + y
            high[:, cols] = total
            rhs[0, :, pl.ds(R_MERGE * dim + at, TILE)] = (total * gate[:, cols]).astype(BF)
        forward(lhs[L_POOL_B], HIGH_B, 1, put_merging)
        backward(lambda at: rhs[0, :, r_cols(R_MERGE)], OUT, 1, merged, True)
        merged[...] += lhs[L_LOW].astype(F32)
        lhs[L_FIRST] = normalise(merged[...], gain1_ref[...]).astype(BF)

        w_wait(QUERY, KEY, VALUE, PROJ)
        pl.semaphore_wait(barrier, n)
        for i in (L_LOW, L_POOL_A, L_POOL_B, L_COT, L_FIRST):
            l_copy(i).start()
        r_copy(R_MERGE).start()
        out_q = []
        for k in range(3):
            def put_mixed(at, y):
                mixed[k, :, pl.ds(at, TILE)] = y.astype(BF)
            forward(lhs[L_FIRST], QUERY + k, 1, put_mixed)
            copies = to_heads(k, mixed.at[k], heads_in.at[k], q_send, q_got)
            start(copies)
            out_q += copies
        wait(out_q)

        for h in range(heads):
            lanes = slice(h * HEAD, (h + 1) * HEAD)

            def rows_of(b, _):
                some = pl.ds(pl.multiple_of(b * t, t), t)
                s = nt(heads_in[0, some, lanes], heads_in[1, :, lanes]) * scale
                e = jnp.exp(s - jnp.max(s, -1, keepdims=True))
                p = (e * (1.0 / jnp.sum(e, -1, keepdims=True))).astype(BF)
                probs[h, some] = p
                att_all[some, lanes] = nn(p, heads_in[2, :, lanes]).astype(BF)
                return 0
            lax.fori_loop(0, n, rows_of, 0)
        out_a = to_tokens(0, att_all, rhs.at[0, :, r_cols(R_ATT)], a_send, a_got)
        start(out_a)
        wait(out_a)
        r_copy(R_ATT).start()
        backward(lambda at: rhs[0, :, r_cols(R_ATT)], PROJ, 1, resid, True)
        resid[...] += merged[...]
        lhs[L_SECOND] = normalise(resid[...], gain2_ref[...]).astype(BF)
        l_copy(L_SECOND).start()

        w_wait(8)

        def put_up(at, y):
            value, rate = gelu_parts(y)
            rhs[0, :, pl.ds(r_at(R_ACT) + at, TILE)] = value.astype(BF)
            slope[:, pl.ds(at, TILE)] = rate.astype(BF)
        forward(lhs[L_SECOND], 8, 4, put_up)
        r_copy(R_ACT).start()
        w_wait(9)
        backward(lambda at: rhs[0, :, pl.ds(r_at(R_ACT) + at, dim)], 12, 4, acc, True)
        put_natural(low_out, resid[...] + acc[...])

        def put_d_up(at, y):
            rhs[0, :, pl.ds(r_at(R_DUP) + at, TILE)] = (y * slope[:, pl.ds(at, TILE)].astype(F32)).astype(BF)
        forward(lhs[L_COT], 12, 4, put_d_up)
        r_copy(R_DUP).start()
        backward(lambda at: rhs[0, :, pl.ds(r_at(R_DUP) + at, dim)], 8, 4, acc, True)
        back, g = normalise_back(resid[...], gain2_ref[...], acc[...])
        g_ln2[...] = g
        d_res[...] = lhs[L_COT].astype(F32) + back
        lhs[L_DA] = d_res[...].astype(BF)
        l_copy(L_DA).start()

        def put_d_att(at, y):
            mixed[0, :, pl.ds(at, TILE)] = y.astype(BF)
        forward(lhs[L_DA], PROJ, 1, put_d_att)
        out_b = to_heads(0, mixed.at[0], d_att, b_send, b_got)
        start(out_b)
        l_copy(L_COT).wait_recv()
        grad(L_COT, R_ACT, 12, 4)
        wait(out_b)
        for h in range(heads):
            lanes = slice(h * HEAD, (h + 1) * HEAD)

            def rows_of(b, _):
                some = pl.ds(pl.multiple_of(b * t, t), t)
                p = probs[h, some].astype(F32)
                dp_ = nt(d_att[some, lanes], heads_in[2, :, lanes])
                ds = (p * (dp_ - jnp.sum(dp_ * p, -1, keepdims=True)) * scale).astype(BF)
                d_scores[some] = ds
                d_heads[0, some, lanes] = nn(ds, heads_in[1, :, lanes]).astype(BF)
                return 0
            lax.fori_loop(0, n, rows_of, 0)
            d_heads[1, :, lanes] = tn(d_scores[...], heads_in[0, :, lanes]).astype(BF)
            d_heads[2, :, lanes] = tn(probs[h], d_att[:, lanes]).astype(BF)
        out_c = []
        for k in range(3):
            copies = to_tokens(k, d_heads.at[k], rhs.at[0, :, r_cols(R_DQ + k)], c_send, c_got)
            start(copies)
            out_c += copies
        l_copy(L_SECOND).wait_recv()
        grad(L_SECOND, R_DUP, 8, 4)
        l_copy(L_DA).wait_recv()
        grad(L_DA, R_ATT, PROJ, 1)
        wait(out_c)
        for k in range(3):
            r_copy(R_DQ + k).start()
        backward(lambda at: rhs[0, :, pl.ds(R_DQ * dim + at, dim)], QUERY, 3, acc, True)
        back, g = normalise_back(merged[...], gain1_ref[...], acc[...])
        g_ln1[...] = g
        d_res[...] += back
        lhs[L_DF] = d_res[...].astype(BF)
        l_copy(L_DF).start()

        def put_d_gate(at, y):
            cols = pl.ds(at, TILE)
            gv = gate[:, cols]
            part = y * gv
            rhs[0, :, pl.ds(R_DHIGH * dim + at, TILE)] = part.astype(BF)
            rhs[0, :, pl.ds(R_DGATE * dim + at, TILE)] = (part * high[:, cols] * (1.0 - gv)).astype(BF)
        forward(lhs[L_DF], OUT, 1, put_d_gate)
        r_copy(R_DHIGH).start()
        r_copy(R_DGATE).start()
        backward(lambda at: rhs[0, :, r_cols(R_DHIGH)], HIGH_A, 1, d_pool_a, True)
        backward(lambda at: rhs[0, :, r_cols(R_DHIGH)], HIGH_B, 1, d_pool_b, True)
        backward(lambda at: rhs[0, :, r_cols(R_DGATE)], GATE, 1, acc, True)
        put_natural(d_low, d_res[...] + acc[...])
        l_copy(L_FIRST).wait_recv()
        for k in range(3):
            grad(L_FIRST, R_DQ + k, QUERY + k, 1)
        l_copy(L_DF).wait_recv()
        grad(L_DF, R_MERGE, OUT, 1)
        l_copy(L_POOL_A).wait_recv()
        grad(L_POOL_A, R_DHIGH, HIGH_A, 1)
        l_copy(L_POOL_B).wait_recv()
        grad(L_POOL_B, R_DHIGH, HIGH_B, 1, shared=True)
        l_copy(L_LOW).wait_recv()
        grad(L_LOW, R_DGATE, GATE, 1)
        wait(stored[-2])
        wait(stored[-1])
        for i in range(8):
            l_copy(i).wait_send()
        for b in range(9):
            r_copy(b).wait_send()

    whole = pl.BlockSpec(memory_space=pl.ANY)
    local = pl.BlockSpec(memory_space=pltpu.VMEM)
    vm, dma = pltpu.VMEM, pltpu.SemaphoreType.DMA
    tok = jax.ShapeDtypeStruct((t, dim), F32)
    one = jax.ShapeDtypeStruct((1, dim), F32)
    return pl.pallas_call(
        kernel,
        out_shape=(tok, tok, tok, tok, one, one, jax.ShapeDtypeStruct((pairs, n * rows, 16 * width), BF)),
        in_specs=[local] * 6 + [whole],
        out_specs=(local,) * 6 + (whole,),
        scratch_shapes=[
            vm((2, pairs, rows, 16 * dim), BF), vm((8, t, dim), BF), vm((8, t, half), BF), vm((2, t, 15 * dim), BF),
            vm((t, dim), F32), vm((t, dim), F32), vm((t, dim), F32), vm((t, dim), F32), vm((t, dim), F32),
            vm((t, ff), BF), vm((3, t, dim), BF), vm((3, every, width), BF), vm((every, width), BF), vm((every, width), BF),
            vm((1, 8, 128), BF), vm((3, every, width), BF), vm((heads, every, every), BF), vm((every, every), BF),
            vm((2, pairs, rows, TILE), BF), vm((2, half, t), BF),
            dma((10, 2 * n)), dma((3, n)), dma((3, n)), dma((1, n)), dma((1, n)), dma((1, n)), dma((1, n)), dma((3, n)), dma((3, n)),
            dma((3,)), dma((8,)), dma((8,)), dma((9,)), dma((9,)), dma((2, 2)),
        ],
        compiler_params=pltpu.CompilerParams(collective_id=cid, has_side_effects=True, vmem_limit_bytes=62 * MIB),
        cost_estimate=pl.CostEstimate(flops=14 * 10**9, bytes_accessed=70 * 10**6, transcendentals=10**7),
    )(low, pool_a, pool_b, cot, gain1, gain2, packed.reshape(pairs, 2, n, rows, 16 * width))
def weight_outputs(own, g_cn_up, g_cn_down, widths, high_rows, others):
    share = own.shape[0]
    width, wide = widths[0], widths[-1]
    piece, h = g_cn_up.shape

    def kernel(x, cn_up, cn_down, *rest):
        sources, rest = rest[: len(others)], rest[len(others) :]
        gate, high, out, qkv, proj, up, down, o_cn_up, o_cn_down = rest[:9]
        count = len(others)
        targets, held, sems = rest[9 : 9 + count], rest[9 + count : -1], rest[-1]
        loads = [pltpu.make_async_copy(a, b, sems.at[0, i]) for i, (a, b) in enumerate(zip(sources, held))]
        saves = [pltpu.make_async_copy(a, b, sems.at[1, i]) for i, (a, b) in enumerate(zip(held, targets))]
        for load in loads:
            load.start()

        def part(i, size=width):
            at = sum(widths[:i])
            return x[:, at : at + size].astype(F32)

        gate[...] = part(0)
        out[...] = part(1).T
        high[:share] = part(2)
        high[share:] = part(3)[: high_rows - share]
        for k in range(3):
            qkv[k] = part(4 + k)
        proj[...] = part(7).T
        up[...] = part(8, wide)
        down[...] = part(9, wide).T
        o_cn_up[...] = cn_up[...].astype(F32)
        for load, save in zip(loads, saves):
            load.wait()
            save.start()
        o_cn_down[...] = cn_down[...].astype(F32)
        for save in saves:
            save.wait()

    whole = pl.BlockSpec(memory_space=pl.ANY)
    local = pl.BlockSpec(memory_space=pltpu.VMEM)
    shapes = [
        (share, width), (high_rows, width), (width, share), (3, share, width), (width, share), (share, wide),
        (wide, share), (piece, h), (piece, h),
    ]
    return pl.pallas_call(
        kernel,
        out_shape=[jax.ShapeDtypeStruct(s, F32) for s in shapes + [o.shape for o in others]],
        in_specs=[local] * 3 + [whole] * len(others),
        out_specs=[local] * 9 + [whole] * len(others),
        scratch_shapes=[pltpu.VMEM(o.shape, o.dtype) for o in others] + [pltpu.SemaphoreType.DMA((2, len(others)))],
        compiler_params=pltpu.CompilerParams(vmem_limit_bytes=60 * MIB),
    )(own, g_cn_up, g_cn_down, *others)


def pack_weights(ad_gate, ad_out, ad_high, w_qkv, w_proj, w_up, w_down, devices):
    dim, width = ad_gate.shape
    share, high_rows, wide = dim // devices, ad_high.shape[0] // devices, w_up.shape[1]
    rest = high_rows - share

    def kernel(gate, out, high, qkv, proj, up, down, packed, side, side_wide, sems):
        me = lax.axis_index("dp")
        mine = pl.ds(pl.multiple_of(me * share, share), share)
        lanes = mine

        def at(i, size=width):
            return packed.at[:, pl.ds(i * width, size)]

        straight = [(gate.at[mine], at(0)), (up.at[mine], at(8, wide))]
        straight += [(qkv.at[k, mine], at(4 + k)) for k in range(3)]
        straight.append((high.at[pl.ds(pl.multiple_of(me * high_rows, rest), share)], at(2)))
        straight.append((high.at[pl.ds(pl.multiple_of(me * high_rows + share, rest), rest)], at(3).at[pl.ds(0, rest)]))
        straight += [(out.at[:, lanes], side.at[0]), (proj.at[:, lanes], side.at[1]), (down.at[:, lanes], side_wide)]
        copies = [pltpu.make_async_copy(a, b, sems.at[i]) for i, (a, b) in enumerate(straight)]
        for copy in copies:
            copy.start()
        packed[rest:, 3 * width : 4 * width] = jnp.zeros((share - rest, width), BF)
        for copy in copies:
            copy.wait()
        packed[:, width : 2 * width] = side[0].T
        packed[:, 7 * width : 8 * width] = side[1].T
        packed[:, 8 * width + wide :] = side_wide[...].T

    whole = pl.BlockSpec(memory_space=pl.ANY)
    return pl.pallas_call(
        kernel,
        out_shape=jax.ShapeDtypeStruct((share, 8 * width + 2 * wide), BF),
        in_specs=[whole] * 7,
        out_specs=pl.BlockSpec(memory_space=pltpu.VMEM),
        scratch_shapes=[
            pltpu.VMEM((2, width, share), BF), pltpu.VMEM((wide, share), BF), pltpu.SemaphoreType.DMA((10,)),
        ],
        compiler_params=pltpu.CompilerParams(vmem_limit_bytes=60 * MIB),
    )(ad_gate, ad_out, ad_high, w_qkv, w_proj, w_up, w_down)


def rows_first(x):
    return with_layout_constraint(x, Layout(major_to_minor=tuple(range(x.ndim))))


def own_part(w, axis):
    length = w.shape[axis] // lax.axis_size("dp")
    return lax.dynamic_slice_in_dim(w, lax.axis_index("dp") * length, length, axis)


def fold(w, rows):
    return w[:rows], jnp.pad(w[rows:], ((0, 2 * rows - w.shape[0]), (0, 0)))


def core_first(x, devices):
    shape = x.shape
    return x.reshape(shape[:-1] + (devices // 2, 2, -1)).swapaxes(-3, -2).reshape(shape)


def core_last(x, devices):
    shape = x.shape
    return x.reshape(shape[:-1] + (2, devices // 2, -1)).swapaxes(-3, -2).reshape(shape)


def layer_norm(values, gain):
    centre = jnp.mean(values, -1, keepdims=True)
    centred = values - centre
    variance = jnp.mean(centred * centred, -1, keepdims=True)
    return centred * lax.rsqrt(variance + 1e-06) * gain


def per_device(
    hr_in,
    low_in,
    valid,
    conv_w,
    hr_gain,
    cn_up,
    cn_down,
    ad_gate,
    ad_high,
    ad_out,
    ln1_gain,
    w_qkv,
    w_proj,
    ln2_gain,
    w_up,
    w_down,
    cot_low,
    cot_hr,
):
    _, row_count, col_count, chan_count = hr_in.shape
    devices, shards = lax.axis_size("dp"), lax.axis_size("mp")
    dims = low_in.shape[2]
    share = dims // devices
    qkv = own_part(w_qkv, 1)
    low_weights = (ad_gate, ad_out, ad_high, w_qkv, w_proj, w_up, w_down)
    pieces = [
        own_part(ad_gate, 0), own_part(ad_out, 1).T, *fold(own_part(ad_high, 0), share),
        qkv[0], qkv[1], qkv[2], own_part(w_proj, 1).T, own_part(w_up, 0), own_part(w_down, 1).T,
    ]
    if share % LANES:
        packed = rows_first(jnp.concatenate(pieces, axis=1))
    else:
        packed = pack_weights(*low_weights, devices)
    packed = rows_first(lax.all_gather(packed, "mp", axis=0, tiled=True))
    plane_mask = valid[0].astype(F32)
    cell_mask = plane_mask[..., None]
    masked = hr_in[0] * valid[0].astype(BF)[..., None]
    half_rows, half_cols = (row_count // 2, col_count // 2)
    counts = plane_mask.reshape(half_rows, 2, half_cols, 2).sum(axis=(1, 3))
    shares = 1.0 / jnp.maximum(counts, 1.0)
    size = conv_w.shape[0]
    taps = conv_w.astype(F32).reshape(size * size, 1, chan_count)
    conv_out, bordered = conv_forward(masked, taps, size, shards)
    hr_gainf = hr_gain.astype(F32)
    normed = layer_norm(conv_out * cell_mask, hr_gainf).astype(BF)
    normed, packed = lax.optimization_barrier((normed, packed))
    packed = rows_first(lax.all_gather(packed, "dp", axis=0, tiled=True))
    hr_out, pooled, normed_all, hidden_act, hidden_slope, up_t, down_t = big_forward(
        normed.reshape(row_count * col_count, chan_count), cn_up, cn_down, masked, plane_mask, shares, shards
    )
    hr_out = hr_out.reshape(hr_in.shape)
    tokens = half_rows * half_cols
    by_share = pooled.reshape(tokens, devices, -1)
    pool_a = by_share[:, :, :share].reshape(tokens, dims)
    pool_b = jnp.pad(by_share[:, :, share:], ((0, 0), (0, 0), (0, 2 * share - by_share.shape[2]))).reshape(tokens, dims)
    low_out, d_low_in, d_pool_a, d_pool_b, g_ln1, g_ln2, low_grads = low_stage(
        *(core_first(v, devices) for v in (low_in[0], pool_a, pool_b, cot_low[0])),
        *(core_first(v.astype(F32), devices)[None] for v in (ln1_gain, ln2_gain)),
        packed, shards, devices, 2,
    )
    if share % LANES:
        low_out, d_low_in = core_last(low_out, devices), core_last(d_low_in, devices)
    low_out, d_low_in = low_out[None], d_low_in[None]
    g_ln1, g_ln2 = core_last(g_ln1[0], devices), core_last(g_ln2[0], devices)
    d_pooled = jnp.concatenate(
        [
            core_last(d_pool_a, devices).reshape(tokens, devices, share),
            core_last(d_pool_b, devices).reshape(tokens, devices, share)[:, :, : by_share.shape[2] - share],
        ],
        axis=2,
    )
    d_normed, d_map, cn_grads, low_sums = big_backward(
        cot_hr[0], d_pooled.reshape(tokens, chan_count), shares, plane_mask, normed_all, hidden_act, hidden_slope,
        up_t, down_t, low_grads, shards, devices,
    )
    low_sums = rows_first(low_sums.reshape(shards, share, -1))
    low_sums = rows_first(lax.psum_scatter(low_sums, "mp", scatter_dimension=0))
    low_gains = jnp.pad(jnp.stack([g_ln1, g_ln2]), ((0, 0), (0, chan_count - dims)))
    d_hr_in, small_sums, (g_cn_up, g_cn_down) = conv_backward(
        d_normed, conv_out, hr_gainf[None], cell_mask, bordered, d_map, taps, low_gains, size, cn_grads, devices, shards
    )
    d_hr_in = d_hr_in[None]
    g_conv = small_sums[: size * size].reshape(conv_w.shape)
    g_hr_gain, g_ln1, g_ln2 = small_sums[size * size], small_sums[-2, :dims], small_sums[-1, :dims]
    (
        g_ad_gate, g_ad_high, g_ad_out, g_qkv, g_proj, g_up, g_down, g_cn_up, g_cn_down,
        low_out, hr_out, d_low_in, d_hr_in,
    ) = weight_outputs(
        low_sums.reshape(share, -1), g_cn_up, g_cn_down, [p.shape[1] for p in pieces], ad_high.shape[0] // devices,
        (low_out, hr_out, d_low_in, d_hr_in),
    )
    g_cn_down = g_cn_down.T
    return (
        low_out,
        hr_out,
        d_low_in,
        d_hr_in,
        g_conv,
        g_hr_gain,
        g_cn_up,
        g_cn_down,
        g_ad_gate,
        g_ad_high,
        g_ad_out,
        g_ln1,
        g_qkv,
        g_proj,
        g_ln2,
        g_up,
        g_down,
    )


def solution(mesh):
    return jax.shard_map(
        per_device,
        mesh=mesh,
        in_specs=(
            P("dp", "mp", None, None),
            P("dp", "mp", None),
            P("dp", "mp", None),
            P(),
            P(),
            P(None, "mp"),
            P("mp", None),
            P(None, "mp"),
            P(None, "mp"),
            P("mp", None),
            P(),
            P(None, None, "mp"),
            P("mp", None),
            P(),
            P(None, "mp"),
            P("mp", None),
            P("dp", "mp", None),
            P("dp", "mp", None, None),
        ),
        out_specs=(
            P("dp", "mp", None),
            P("dp", "mp", None, None),
            P("dp", "mp", None),
            P("dp", "mp", None, None),
            P(),
            P(),
            P("dp", "mp"),
            P("mp", "dp"),
            P("dp", "mp"),
            P("dp", "mp"),
            P("mp", "dp"),
            P(),
            P(None, "dp", "mp"),
            P("mp", "dp"),
            P(),
            P("dp", "mp"),
            P("mp", "dp"),
        ),
        check_vma=False,
    )
```

```python
import jax
import jax.numpy as jnp
from jax import lax
from jax.experimental.layout import Layout, with_layout_constraint
from jax.experimental import pallas as pl
from jax.experimental.pallas import tpu as pltpu
from jax.sharding import PartitionSpec as P

HEAD = 64
LANES = 128
EDGE = 8
CHUNKS = 6
TILE = 512
MIB = 1024 * 1024
MESH = pl.DeviceIdType.MESH
BF = jnp.bfloat16
F32 = jnp.float32

def gelu_parts(x):
    c = 0.7978845608028654
    x2 = x * x
    t = jnp.tanh(c * x * (1.0 + 0.044715 * x2))
    half = 0.5 * (1.0 + t)
    slope = half + 0.5 * x * (1.0 - t * t) * (c * (1.0 + 3 * 0.044715 * x2))
    return x * half, slope


def gelu(x):
    c = 0.7978845608028654
    t = jnp.tanh(c * x * (1.0 + 0.044715 * (x * x)))
    return 0.5 * x * (1.0 + t)


def dp_bit(position):
    return lax.rem(lax.axis_index("dp") // 2**position, 2)


def dp_mate(position):
    return lax.axis_index("dp") + 2**position * (1 - 2 * dp_bit(position))


class Halving:
    def __init__(self, bits, lasts, shape, block):
        self.lasts, self.shape, self.block = lasts, shape, block
        left = list(bits)
        self.bits = [left.pop(0 if last else -1) for last in lasts]

    def split(self, count, p):
        if count == 1:
            return (1, 1)
        return (count // 2, 2) if self.lasts[p] else (2, count // 2)

    def buffers(self):
        count, rows, cols = self.shape
        got, held = [], []
        for p in range(len(self.bits)):
            count //= 2
            got.append(jax.ShapeDtypeStruct((count, rows, cols), BF))
            held.append(jax.ShapeDtypeStruct(self.split(count, p + 1) + (rows, cols), BF))
        return got + held

    def semaphores(self):
        return [pltpu.SemaphoreType.DMA((len(self.bits),))] * 2

    def bind(self, first, buffers, send, recv):
        steps = len(self.bits)
        self.now = [first] + list(buffers[steps:])
        self.got, self.send, self.recv = buffers[:steps], send, recv

    def part(self, p, mine):
        bit = dp_bit(self.bits[p])
        index = bit if mine else 1 - bit
        return self.now[p].at[:, index] if self.lasts[p] else self.now[p].at[index]

    def copy(self, p):
        return pltpu.make_async_remote_copy(
            src_ref=self.part(p, False), dst_ref=self.got[p], send_sem=self.send.at[p], recv_sem=self.recv.at[p],
            device_id={"dp": dp_mate(self.bits[p])}, device_id_type=MESH,
        )

    def start(self, p):
        self.copy(p).start()

    def finish(self, p, wait=True):
        if wait:
            self.copy(p).wait()
        count, rows, cols = self.got[p].shape
        ways = self.split(count, p + 1)

        def add(a, b, out):
            out[...] = (a[...].astype(F32) + b[...].astype(F32)).astype(BF).reshape(out.shape)

        flat = pl.BlockSpec((1, rows, self.block), lambda k, c: (k, 0, c))
        paired = pl.BlockSpec((1, 1, rows, self.block), lambda k, c: (k // ways[1], lax.rem(k, ways[1]), 0, c))
        pltpu.emit_pipeline(add, grid=(count, cols // self.block), in_specs=[flat, flat], out_specs=[paired])(
            self.part(p, True), self.got[p], self.now[p + 1]
        )


def chain_exchange(
    n, chunks, lag, gathered, partial, travel, sems, own_chunk, prepare, arrived, compute, mates=(), begin=None, turn=None, after=None, early=False
):
    ag_send, ag_recv, rs_send, rs_recv = sems
    d = lax.axis_index("mp")
    has_left, has_right = d > 0, d < n - 1

    barrier = pltpu.get_barrier_semaphore()

    @pl.when(has_left)
    def _():
        pl.semaphore_signal(barrier, inc=1, device_id={"mp": d - 1}, device_id_type=MESH)

    @pl.when(has_right)
    def _():
        pl.semaphore_signal(barrier, inc=1, device_id={"mp": d + 1}, device_id_type=MESH)

    for mate in mates:
        pl.semaphore_signal(barrier, inc=1, device_id={"dp": mate}, device_id_type=MESH)

    own_chunk(0)
    pl.semaphore_wait(barrier, has_left.astype(jnp.int32) + has_right.astype(jnp.int32) + len(mates))
    if begin is not None:
        begin()

    def ag(way, s, j):
        return pltpu.make_async_remote_copy(
            src_ref=gathered.at[s, j], dst_ref=gathered.at[s, j],
            send_sem=ag_send.at[way, s, j], recv_sem=ag_recv.at[s, j],
            device_id={"mp": d + 1 - 2 * way}, device_id_type=MESH,
        )

    def rs(way, s, j):
        there = d + 1 - 2 * way
        slot = jnp.where((s == there) & (way == 0), n, s)
        return pltpu.make_async_remote_copy(
            src_ref=travel.at[s, j], dst_ref=travel.at[slot, j],
            send_sem=rs_send.at[s, j], recv_sem=rs_recv.at[slot, j],
            device_id={"mp": there}, device_id_type=MESH,
        )

    def rs_wait(slot, j):
        pltpu.make_async_copy(travel.at[slot, j], travel.at[slot, j], rs_recv.at[slot, j]).wait()

    def first(j, _):
        @pl.when(j > 0)
        def _():
            own_chunk(j)

        @pl.when(has_right)
        def _():
            ag(0, d, j).start()

        @pl.when(has_left)
        def _():
            ag(1, d, j).start()

        return 0

    lax.fori_loop(0, chunks, first, 0)

    def flow(way, q):
        ql = jnp.clip(q, 0, n * chunks - 1)
        s, jj = ql // chunks, lax.rem(ql, chunks)
        if way == 1:
            s = n - 1 - s
        ahead = (s > d) if way == 0 else (s < d)
        source = has_left if way == 0 else has_right

        @pl.when((q >= 0) & (q < n * chunks) & (ahead | ((s == d) & source)))
        def _():
            @pl.when(source)
            def _():
                rs_wait(jnp.where(s == d, n, s) if way == 0 else s, jj)

            @pl.when(ahead & source)
            def _():
                travel[s, jj] = (partial[s, jj].astype(F32) + travel[s, jj].astype(F32)).astype(BF)

            @pl.when(ahead & jnp.logical_not(source))
            def _():
                travel[s, jj] = partial[s, jj].astype(BF)

            @pl.when(ahead)
            def _():
                rs(way, s, jj).start()

    def block_of(k, way):
        s = d - k + 2 * k * way
        return s, (s >= 0) & (s < n) & ((k > 0) | (way == 0))

    def receive(k, way, s, j):
        @pl.when(k > 0)
        def _():
            pltpu.make_async_copy(gathered.at[s, j], gathered.at[s, j], ag_recv.at[s, j]).wait()

            @pl.when((way == 0) & has_right)
            def _():
                ag(0, s, j).start()

            @pl.when((way == 1) & has_left)
            def _():
                ag(1, s, j).start()

        arrived(s, j)

    wait_one = 1 if early else 0

    def step(g, _):
        k, j = g // chunks, lax.rem(g, chunks)

        def sides(act):
            @pl.when(g < n * chunks)
            def _():
                def side(way, _):
                    s, ok = block_of(k, way)
                    pl.when(ok)(lambda: act(way, s))
                    return 0

                lax.fori_loop(0, 2, side, 0)

        def flows():
            flow(1, g - wait_one - (n - 1 - d) * lag)
            flow(0, g - wait_one - d * lag)

        if turn is not None:
            turn(g)
        if early:
            sides(lambda way, s: receive(k, way, s, j))
            flows()

            def later(way, s):
                prepare(way, s, j)
                compute(way, s, j)

            sides(later)
        else:
            def work(way, s):
                prepare(way, s, j)
                receive(k, way, s, j)
                compute(way, s, j)

            sides(work)
            flows()
        if after is not None:
            after(g)
        return 0

    lax.fori_loop(0, n * chunks + (n - 1) * lag + wait_one, step, 0)

    def drain(i, _):
        s, j = i // chunks, lax.rem(i, chunks)

        @pl.when(has_right & (s <= d))
        def _():
            ag(0, s, j).wait_send()

        @pl.when(has_left & (s >= d))
        def _():
            ag(1, s, j).wait_send()

        @pl.when(s < d)
        def _():
            rs(1, s, j).wait_send()

        @pl.when(s > d)
        def _():
            rs(0, s, j).wait_send()

        return 0

    lax.fori_loop(0, n * chunks, drain, 0)


def own_sum(n, d, j, partial, travel, total):
    total[...] = partial[d, j].astype(F32)

    @pl.when(d > 0)
    def _():
        total[...] += travel[n, j].astype(F32)

    @pl.when(d < n - 1)
    def _():
        total[...] += travel[d, j].astype(F32)


def chain_sems(n, chunks):
    dma = pltpu.SemaphoreType.DMA
    return [dma((2, n, chunks)), dma((n, chunks)), dma((n, chunks)), dma((n + 1, chunks))]


def chunk_buffers(n, rows, c, kept):
    return [
        pltpu.VMEM((n, CHUNKS, rows, c), BF),
        pltpu.VMEM((n, CHUNKS, rows, c), kept),
        pltpu.VMEM((n + 1, CHUNKS, rows, c), BF),
    ]


def columns(i):
    return pl.ds(pl.multiple_of(i * TILE, TILE), TILE)


def drain_copies(n, copy):
    def one(i, _):
        copy(i // CHUNKS, lax.rem(i, CHUNKS)).wait()
        return 0

    lax.fori_loop(0, n * CHUNKS, one, 0)


def big_forward(x, w_up, w_down, residual, mask, share, n):
    t, c = x.shape
    h = w_up.shape[1]
    rows = t // CHUNKS
    cols = residual.shape[1]
    half = cols // 2
    pairs = rows // cols // 2

    def kernel(
        x_ref, wu, wd, res, mask_ref, share_ref, out, pooled, x_all, act_all, slope_all, wu_t, wd_t,
        gathered, partial, travel, act, slope, total, folded, turned, copied, stored, load_sem, *sems
    ):
        d = lax.axis_index("mp")
        load = pltpu.make_async_copy(x_ref, gathered.at[d], load_sem)

        def own_chunk(j):
            if isinstance(j, int):
                load.start()
                load.wait()

        def x_copy(s, j):
            return pltpu.make_async_copy(gathered.at[s, j], x_all.at[s, j], copied.at[s, j])

        def prepare(way, s, j):
            pass

        def arrived(s, j):
            x_copy(s, j).start()

        def compute(way, s, j):
            block = gathered.at[s, j]

            def up(i, _):
                pre = jnp.dot(block[...], wu[:, columns(i)], preferred_element_type=F32)
                value, rate = gelu_parts(pre)
                act[:, columns(i)] = value.astype(BF)
                slope[:, columns(i)] = rate.astype(BF)
                return 0

            lax.fori_loop(0, h // TILE, up, 0)
            keep_act = pltpu.make_async_copy(act, act_all.at[s, j], stored.at[0])
            keep_slope = pltpu.make_async_copy(slope, slope_all.at[s, j], stored.at[1])
            keep_act.start()
            keep_slope.start()

            def down(i, _):
                partial[s, j, :, columns(i)] = jnp.dot(
                    act[...], wd[:, columns(i)], preferred_element_type=F32
                )
                return 0

            lax.fori_loop(0, c // TILE, down, 0)
            keep_act.wait()
            keep_slope.wait()

        def finish(j):
            pl.when(j > 0)(lambda: put(j - 1).wait())
            own_sum(n, d, j, partial, travel, total)
            values = (res[pl.ds(j * 2 * pairs, 2 * pairs)].reshape(rows, c).astype(F32) + total[...]) * mask_ref[j]
            partial[d, j] = values
            put(j).start()
            both = values.reshape(pairs, 2, cols, c)
            summed = (both[:, 0] + both[:, 1]).reshape(pairs * cols, c)
            for b in range(c // LANES):
                lanes = slice(b * LANES, (b + 1) * LANES)
                folded[b] = summed[:, lanes]
                every = folded[b, pl.ds(0, pairs * half, 2), :] + folded[b, pl.ds(1, pairs * half, 2), :]
                pooled[j, :, lanes] = (every * share_ref[j]).astype(BF)

        def put(j):
            return pltpu.make_async_copy(partial.at[d, j], out.at[j], load_sem)

        def after(g):
            last = g - (n - 1) * (CHUNKS + 1)
            pl.when(last >= 0)(lambda: finish(last))
            for i, (w, target, size) in enumerate(((wu, wu_t, h), (wd, wd_t, c))):
                @pl.when(g < size // LANES)
                def _():
                    some = pl.ds(pl.multiple_of(g * LANES, LANES), LANES)
                    turned[i, :, pl.ds(0, w.shape[0])] = w[:, some].T
                    copy = pltpu.make_async_copy(turned.at[i, :, pl.ds(0, w.shape[0])], target.at[some], stored.at[i])
                    copy.start()
                    copy.wait()

        chain_exchange(
            n, CHUNKS, 1, gathered, partial, travel, sems, own_chunk, prepare, arrived, compute, after=after
        )

        put(CHUNKS - 1).wait()
        drain_copies(n, x_copy)

    whole = pl.BlockSpec(memory_space=pl.ANY)
    local = pl.BlockSpec(memory_space=pltpu.VMEM)
    out, pooled, x_all, act_all, slope_all, wu_t, wd_t = pl.pallas_call(
        kernel,
        out_shape=(
            jax.ShapeDtypeStruct((CHUNKS, rows, c), F32),
            jax.ShapeDtypeStruct((CHUNKS, pairs * half, c), BF),
            jax.ShapeDtypeStruct((n, CHUNKS, rows, c), BF),
            jax.ShapeDtypeStruct((n, CHUNKS, rows, h), BF),
            jax.ShapeDtypeStruct((n, CHUNKS, rows, h), BF),
            jax.ShapeDtypeStruct((h, c), BF),
            jax.ShapeDtypeStruct((c, h), BF),
        ),
        in_specs=[whole, local, local, local, local, local],
        out_specs=(whole, local, whole, whole, whole, whole, whole),
        scratch_shapes=chunk_buffers(n, rows, c, F32)
        + [pltpu.VMEM((rows, h), BF)] * 2
        + [pltpu.VMEM((rows, c), F32), pltpu.VMEM((c // LANES, pairs * cols, LANES), F32), pltpu.VMEM((2, LANES, max(c, h)), BF)]
        + [pltpu.SemaphoreType.DMA((n, CHUNKS)), pltpu.SemaphoreType.DMA((2,)), pltpu.SemaphoreType.DMA]
        + chain_sems(n, CHUNKS),
        compiler_params=pltpu.CompilerParams(
            collective_id=0, has_side_effects=True, vmem_limit_bytes=60 * MIB
        ),
        cost_estimate=pl.CostEstimate(
            flops=4 * n * t * c * h, bytes_accessed=8 * n * t * c, transcendentals=n * t * h
        ),
    )(
        x.reshape(CHUNKS, rows, c), w_up, w_down, residual,
        mask.reshape(CHUNKS, rows, 1), share.reshape(CHUNKS, pairs * half, 1),
    )
    return (
        out.reshape(t, c),
        pooled.reshape(t // 4, c),
        x_all,
        act_all,
        slope_all,
        wu_t,
        wd_t,
    )


def big_backward(cot, d_pooled, share, mask, x_all, act_all, slope_all, up_t, down_t, grads, n, devices):
    _, cols, c = cot.shape
    t = cot.shape[0] * cols
    h = up_t.shape[0]
    rows = t // CHUNKS
    half = cols // 2
    pairs_here = rows // cols // 2
    piece = c // devices
    items = n * CHUNKS // 2
    pairs, g_rows, g_cols = grads.shape
    bits = range(1, devices.bit_length() - 1)
    split = g_rows // 2
    steps = len(bits)
    plans = [Halving(bits, [last] * steps, (pairs, split, g_cols), min(g_cols, 1024)) for last in (True, False)]
    extras = [b for plan in plans for b in plan.buffers()[:-1]]
    each = 2 * steps - 1

    def kernel(
        cot_ref, pool_ref, share_ref, mask_ref, x_hbm, act_hbm, slopes, wu, wd, g_first, g_second,
        out, d_own, g_up_out, g_down_out, out_up, out_down, got_up, got_down, h_all, *rest
    ):
        sums, extra, rest = rest[0], rest[1 : 1 + 2 * each], rest[1 + 2 * each :]
        gathered, partial, travel, slope, grad, left, right, middle, g_up, g_down, total, spread_rows, addend = rest[:13]
        core_send, core_recv, stored, add_sem, send0, recv0, send1, recv1 = rest[13:21]
        sems = rest[21:]
        d = lax.axis_index("mp")
        plans[0].bind(g_first.at[:, :, pl.ds(0, split)], extra[:each] + (sums.at[0],), send0, recv0)
        plans[1].bind(g_second.at[:, :, pl.ds(split, split)], extra[each:] + (sums.at[1],), send1, recv1)

        def begin():
            for plan in plans:
                plan.start(0)

        def pass_on(p, plan):
            plan.finish(p)
            if p + 1 < steps:
                plan.start(p + 1)

        first_due = 2 * CHUNKS + 3
        ticks = {}
        if steps == 2:
            for p, start in ((0, first_due), (1, n * CHUNKS + n - 2)):
                tiles = [
                    (plan, k, q)
                    for plan in plans
                    for k in range(plan.got[p].shape[0])
                    for q in range(g_cols // plan.block)
                ]
                for m in range(0, len(tiles), 4):
                    ticks[start + m // 4] = (p, m == 0, m + 4 >= len(tiles), tiles[m : m + 4])

        def tile_copy(which, p, i, plan, k, q):
            lanes = pl.ds(q * plan.block, plan.block)
            if which == 0:
                source, target = plan.part(p, True).at[k, :, lanes], addend.at[0, i]
            elif which == 1:
                source, target = plan.got[p].at[k, :, lanes], addend.at[1, i]
            else:
                ways = plan.split(plan.got[p].shape[0], p + 1)
                source, target = addend.at[0, i], plan.now[p + 1].at[k // ways[1], k % ways[1], :, lanes]
            return pltpu.make_async_copy(source, target, add_sem.at[which, i])

        def tick_begin(p, fresh, final, tiles):
            if fresh:
                for plan in plans:
                    plan.copy(p).wait()
            for i, tile in enumerate(tiles):
                for which in range(2):
                    tile_copy(which, p, i, *tile).start()

        def tick_add(p, fresh, final, tiles):
            for i, tile in enumerate(tiles):
                for which in range(2):
                    tile_copy(which, p, i, *tile).wait()
                addend[0, i] = (addend[0, i].astype(F32) + addend[1, i].astype(F32)).astype(BF)
                tile_copy(2, p, i, *tile).start()
            for i, tile in enumerate(tiles):
                tile_copy(2, p, i, *tile).wait()
            if final and p + 1 < steps:
                for plan in plans:
                    plan.start(p + 1)

        all_steps = n * CHUNKS + n
        due = [all_steps * 9 * (2**steps - 2 ** (steps - 1 - p)) // (10 * (2**steps - 1)) // 2 * 2 for p in range(steps)]

        def turn(g):
            if ticks:
                for at, tick in ticks.items():
                    pl.when(g == at)(lambda tick=tick: tick_begin(*tick))
            else:
                for p in range(steps - 1):
                    for i, plan in enumerate(plans):
                        pl.when(g == due[p] + 2 * i)(lambda p=p, plan=plan: pass_on(p, plan))

            q, due_now = item_of(g)

            @pl.when(due_now)
            def _():
                for copy in item_copies(q):
                    copy.start()

        def own_chunk(j):
            part = pool_ref[j] * share_ref[j]
            here = cot_ref.at[pl.ds(j * 2 * pairs_here, 2 * pairs_here)]
            for b in range(c // LANES):
                lanes = slice(b * LANES, (b + 1) * LANES)
                spread_rows[b, pl.ds(0, pairs_here * half, 2), :] = part[:, lanes]
                spread_rows[b, pl.ds(1, pairs_here * half, 2), :] = part[:, lanes]
                block = jnp.broadcast_to(
                    spread_rows[b].reshape(pairs_here, 1, cols, LANES), (pairs_here, 2, cols, LANES)
                ).reshape(rows, LANES)
                cell = here[:, :, lanes].reshape(rows, LANES).astype(F32)
                gathered[d, j, :, lanes] = ((cell + block) * mask_ref[j]).astype(BF)

        def slope_copy(s, j):
            return pltpu.make_async_copy(slopes.at[s, j], slope, stored.at[0])

        def prepare(way, s, j):
            slope_copy(s, j).start()

        def arrived(s, j):
            pass

        def compute(way, s, j):
            block = gathered.at[s, j]
            slope_copy(s, j).wait()

            def up(i, _):
                back = nn(block[...], wd[:, columns(i)])
                grad[:, columns(i)] = (back * slope[:, columns(i)].astype(F32)).astype(BF)
                return 0

            lax.fori_loop(0, h // TILE, up, 0)
            half_pair = pl.ds(pl.multiple_of(lax.rem(j, 2) * rows, rows), rows)
            keep = pltpu.make_async_copy(grad, h_all.at[s, j // 2, half_pair], stored.at[1])
            keep.start()

            def down(i, _):
                partial[s, j, :, columns(i)] = nn(grad[...], wu[:, columns(i)]).astype(BF)
                return 0

            lax.fori_loop(0, c // TILE, down, 0)
            keep.wait()

        def item_place(q):
            s, jj, base = d, q, CHUNKS // 2
            for k in range(1, n):
                to_left, to_right = d - k >= 0, d + k < n
                two = to_left & to_right
                r = q - base
                here = (r >= 0) & (to_left | to_right)
                s = jnp.where(here, jnp.where(to_left & (jnp.logical_not(two) | (lax.rem(r, 2) == 0)), d - k, d + k), s)
                jj = jnp.where(here, jnp.where(two, r // 2, r), jj)
                base = base + (CHUNKS // 2) * (to_left.astype(jnp.int32) + to_right.astype(jnp.int32))
            return s, jj

        def item_copies(q):
            s, jj = item_place(q)
            return (
                pltpu.make_async_copy(x_hbm.at[s, jj], left, stored.at[2]),
                pltpu.make_async_copy(act_hbm.at[s, jj], right, stored.at[3]),
                pltpu.make_async_copy(h_all.at[s, jj], middle, stored.at[4]),
            )

        between = (d > 0) & (d < n - 1)

        def item_of(g):
            q = jnp.where(between, g - items, (g - 3) // 2)
            return q, (q >= 0) & (q < items) & (g >= 3) & (between | (lax.rem(g, 2) == 1))

        def after(g):
            for at, tick in ticks.items():
                pl.when(g == at)(lambda tick=tick: tick_add(*tick))
            last = g - 1 - (n - 1) * (CHUNKS + 1)
            pl.when(last >= 0)(lambda: finish(last))
            q, due_now = item_of(g)

            @pl.when(due_now)
            def _():
                s, jj = item_place(q)
                for copy in item_copies(q):
                    copy.wait()

                def tile(i, _):
                    a = columns(i)
                    g_up[a] += tn(left[:, a], middle[...])
                    db = gathered[s, pl.ds(2 * jj, 2), :, a].reshape(2 * rows, TILE)
                    g_down[a] += tn(db, right[...])
                    return 0

                lax.fori_loop(0, c // TILE, tile, 0)

            @pl.when(g == 2 * items + 2)
            def _():
                give(g_up, left, out_up, stored.at[2])
                swaps[0].start()

            @pl.when(g == 2 * items + 3)
            def _():
                give(g_down, right, out_down, stored.at[3])
                swaps[1].start()

        core = dp_bit(0)

        def result(j):
            return pltpu.make_async_copy(total, out.at[j], stored.at[5])

        def finish(j):
            pl.when(j > 0)(lambda: result(j - 1).wait())
            own_sum(n, d, j, partial, travel, total)
            result(j).start()

        def rows_at(i):
            return pl.ds(pl.multiple_of(i * piece, piece), piece)

        def give(source, stage, target, sem):
            def one(i, _):
                stage[pl.ds(0, piece)] = source[rows_at(2 * i + 1 - core)].astype(BF)
                copy = pltpu.make_async_copy(stage.at[pl.ds(0, piece)], target.at[i], sem)
                copy.start()
                copy.wait()
                return 0

            lax.fori_loop(0, devices // 2, one, 0)

        def keep_sums():
            sets = ((g_up, left, got_up, g_up_out, 2), (g_down, right, got_down, g_down_out, 3))

            def loads(i):
                return [
                    pltpu.make_async_copy(got.at[i], stage.at[pl.ds(0, piece)], stored.at[sem])
                    for _, stage, got, _, sem in sets
                ]

            def one(i, _):
                for load in loads(i):
                    load.start()
                saves = []
                for load, (source, stage, _, target, sem) in zip(loads(i), sets):
                    load.wait()
                    here = stage.at[pl.ds(0, piece)]
                    here[...] = (source[rows_at(2 * i + core)] + here[...].astype(F32)).astype(BF)
                    saves.append(pltpu.make_async_copy(here, target.at[i], stored.at[sem]))
                    saves[-1].start()
                for save in saves:
                    save.wait()
                return 0

            lax.fori_loop(0, devices // 2, one, 0)

        swaps = [
            pltpu.make_async_remote_copy(
                src_ref=src, dst_ref=dst, send_sem=core_send.at[i], recv_sem=core_recv.at[i],
                device_id={"dp": dp_mate(0)}, device_id_type=MESH,
            )
            for i, (src, dst) in enumerate(((out_up, got_up), (out_down, got_down)))
        ]
        def clear(i, _):
            some = pl.ds(pl.multiple_of(i * TILE, TILE), TILE)
            g_up[some] = jnp.zeros((TILE, h), F32)
            g_down[some] = jnp.zeros((TILE, h), F32)
            return 0

        def begin_all():
            begin()
            lax.fori_loop(0, c // TILE, clear, 0)

        chain_exchange(
            n, CHUNKS, 1, gathered, partial, travel, sems, own_chunk, prepare, arrived, compute,
            [dp_mate(b) for b in range(steps + 1)], begin_all, turn, after, True,
        )
        keep = pltpu.make_async_copy(gathered.at[d], d_own, stored.at[0])
        keep.start()
        result(CHUNKS - 1).wait()
        keep.wait()
        if not ticks:
            for plan in plans:
                pass_on(steps - 1, plan)
        for swap in swaps:
            swap.wait()
        keep_sums()

    whole = pl.BlockSpec(memory_space=pl.ANY)
    local = pl.BlockSpec(memory_space=pltpu.VMEM)
    dma = pltpu.SemaphoreType.DMA
    out, d_own, g_up, g_down, _, _, _, _, _, sums, *_ = pl.pallas_call(
        kernel,
        out_shape=(
            jax.ShapeDtypeStruct((CHUNKS, rows, c), F32),
            jax.ShapeDtypeStruct((CHUNKS, rows, c), BF),
            *[jax.ShapeDtypeStruct((devices // 2, piece, h), BF)] * 6,
            jax.ShapeDtypeStruct((n, CHUNKS // 2, 2 * rows, h), BF),
            jax.ShapeDtypeStruct((2, 1, 1, split, g_cols), BF),
            *extras,
        ),
        in_specs=[local] * 4 + [whole] * 3 + [local] * 2 + [whole] * 2,
        out_specs=(whole,) * (10 + 2 * each),
        scratch_shapes=chunk_buffers(n, rows, c, BF)
        + [
            pltpu.VMEM((rows, h), BF), pltpu.VMEM((rows, h), BF),
            pltpu.VMEM((2 * rows, c), BF), pltpu.VMEM((2 * rows, h), BF), pltpu.VMEM((2 * rows, h), BF),
            pltpu.VMEM((c, h), F32), pltpu.VMEM((c, h), F32),
            pltpu.VMEM((rows, c), F32), pltpu.VMEM((c // LANES, pairs_here * cols, LANES), F32),
            pltpu.VMEM((2, 4, split, plans[0].block), BF),
            dma((2,)), dma((2,)), dma((6,)), dma((3, 4)),
        ]
        + plans[0].semaphores() + plans[1].semaphores()
        + chain_sems(n, CHUNKS),
        compiler_params=pltpu.CompilerParams(
            collective_id=1, has_side_effects=True, vmem_limit_bytes=62 * MIB
        ),
        cost_estimate=pl.CostEstimate(
            flops=8 * n * t * c * h, bytes_accessed=8 * n * t * c, transcendentals=0
        ),
    )(
        cot, d_pooled.reshape(CHUNKS, pairs_here * half, c), share.reshape(CHUNKS, pairs_here * half, 1),
        mask.reshape(CHUNKS, rows, 1), *(v.reshape(n, CHUNKS // 2, 2 * rows, -1) for v in (x_all, act_all)),
        slope_all, up_t, down_t,
        grads.reshape(pairs // 2, 2, g_rows, g_cols), grads.reshape(2, pairs // 2, g_rows, g_cols),
    )
    return (
        out.reshape(cot.shape), d_own.reshape(cot.shape), [g_up, g_down],
        sums.reshape(g_rows, g_cols),
    )


def frame(dst, src):
    rows, cols, _ = src.shape
    dst[:, :EDGE] = jnp.zeros((rows, EDGE, LANES), F32)
    dst[:, EDGE + cols:] = jnp.zeros((rows, EDGE, LANES), F32)
    dst[:, EDGE:EDGE + cols] = src[...].astype(F32)


def correlate(out, framed, taps, size, flip, group, first=0, last=None, every=1):
    rows, cols, _ = out.shape
    reach = size // 2
    def some(k, _):
        r = first + k * every
        acc = jnp.zeros((group, cols, LANES), F32)
        for a in range(size):
            for b in range(size):
                tap = (size - 1 - a) * size + size - 1 - b if flip else a * size + b
                acc = acc + framed[pl.ds(r * group + a, group), pl.ds(EDGE - reach + b, cols), :] * taps[tap]
        out[pl.ds(r * group, group)] = acc
        return 0
    lax.fori_loop(0, (rows // group if last is None else last) - first if every == 1 else 2, some, 0)


def conv_forward(x, w, size, n):
    rows, cols, c = x.shape
    reach = size // 2

    def kernel(x_ref, w_ref, out, bordered, framed, sent, got, own):
        d = lax.axis_index("mp")
        has_up, has_down = d > 0, d < n - 1
        barrier = pltpu.get_barrier_semaphore()

        @pl.when(has_up)
        def _():
            pl.semaphore_signal(barrier, inc=1, device_id={"mp": d - 1}, device_id_type=MESH)

        @pl.when(has_down)
        def _():
            pl.semaphore_signal(barrier, inc=1, device_id={"mp": d + 1}, device_id_type=MESH)

        keep = pltpu.make_async_copy(x_ref, bordered.at[pl.ds(reach, rows)], own)
        keep.start()
        pl.semaphore_wait(barrier, has_up.astype(jnp.int32) + has_down.astype(jnp.int32))
        up = pltpu.make_async_remote_copy(
            src_ref=x_ref.at[pl.ds(0, reach)], dst_ref=bordered.at[pl.ds(reach + rows, reach)],
            send_sem=sent.at[0], recv_sem=got.at[0], device_id={"mp": d - 1}, device_id_type=MESH,
        )
        down = pltpu.make_async_remote_copy(
            src_ref=x_ref.at[pl.ds(rows - reach, reach)], dst_ref=bordered.at[pl.ds(0, reach)],
            send_sem=sent.at[1], recv_sem=got.at[1], device_id={"mp": d + 1}, device_id_type=MESH,
        )
        nothing = jnp.zeros((reach, cols, c), BF)

        @pl.when(has_up)
        def _():
            up.start()

        @pl.when(has_down)
        def _():
            down.start()

        @pl.when(d == 0)
        def _():
            bordered[:reach] = nothing

        @pl.when(d == n - 1)
        def _():
            bordered[reach + rows :] = nothing

        groups = rows // reach

        def inner(i, _):
            lanes = pl.ds(pl.multiple_of(i * LANES, LANES), LANES)
            frame(framed.at[pl.ds(reach, rows)], x_ref.at[:, :, lanes])
            correlate(out.at[:, :, lanes], framed, w_ref.at[:, :, lanes], size, False, reach, 1, groups - 1)
            return 0

        lax.fori_loop(0, c // LANES, inner, 0)
        keep.wait()

        @pl.when(has_up)
        def _():
            down.wait_recv()

        @pl.when(has_down)
        def _():
            up.wait_recv()

        def block(i, _):
            lanes = pl.ds(pl.multiple_of(i * LANES, LANES), LANES)
            frame(framed, bordered.at[:, :, lanes])
            correlate(out.at[:, :, lanes], framed, w_ref.at[:, :, lanes], size, False, reach, 0, None, groups - 1)
            return 0

        lax.fori_loop(0, c // LANES, block, 0)

        @pl.when(has_up)
        def _():
            up.wait_send()

        @pl.when(has_down)
        def _():
            down.wait_send()

    local = pl.BlockSpec(memory_space=pltpu.VMEM)
    dma = pltpu.SemaphoreType.DMA
    return pl.pallas_call(
        kernel,
        out_shape=(
            jax.ShapeDtypeStruct((rows, cols, c), F32),
            jax.ShapeDtypeStruct((rows + 2 * reach, cols, c), BF),
        ),
        in_specs=[local, local],
        out_specs=(local, local),
        scratch_shapes=[pltpu.VMEM((rows + 2 * reach, cols + 2 * EDGE, LANES), F32), dma((2,)), dma((2,)), dma],
        compiler_params=pltpu.CompilerParams(
            collective_id=5, has_side_effects=True, vmem_limit_bytes=40 * MIB
        ),
    )(x, w)


def conv_backward(d_normed, conv_out, gain, mask, bordered, d_map, w, low_gains, size, grads, devices, n):
    rows, cols, c = conv_out.shape
    reach = size // 2
    high = rows + 2 * reach
    group = 4 if rows % 4 == 0 else 1
    bits = range(1, devices.bit_length() - 1)
    steps = len(bits)
    shape = grads[0].shape
    plans = [Halving(bits, [last] * steps, shape, shape[2]) for last in (True, False)]
    each = 2 * steps
    blocks = c // LANES
    taps = size * size
    count = taps + 1 + low_gains.shape[0]
    small = -(-count // devices)
    first_due = blocks + blocks // 3
    begins = {first_due + blocks // 2 * p // (steps - 1): p for p in range(steps - 1)}
    ends = {mark + 1: p for mark, p in begins.items()}
    rounds = {blocks + 10 * blocks // 12: 1}

    def kernel(
        dn, co, gain_ref, mask_ref, w_ref, low_ref, b_hbm, dm_hbm, g0, g1, out, g_all, *rest
    ):
        extra, rest = rest[: 2 * each], rest[2 * each :]
        around, x_around, d_here, dframed, xframed, g_own, here, level, addend, sent, got, own, add_sem = rest[:13]
        ar, halving_sems = rest[13:19], rest[19:]
        plans[0].bind(g0, extra[:each], halving_sems[0], halving_sems[1])
        plans[1].bind(g1, extra[each:], halving_sems[2], halving_sems[3])
        me, d = lax.axis_index("dp"), lax.axis_index("mp")
        has_up, has_down = d > 0, d < n - 1
        barrier = pltpu.get_barrier_semaphore()

        def greet(k, _):
            pl.semaphore_signal(
                barrier, inc=1, device_id={"dp": lax.rem(me + k, devices)}, device_id_type=MESH
            )
            return 0

        lax.fori_loop(1, devices, greet, 0)
        for k in range(1, n):
            pl.semaphore_signal(barrier, inc=1, device_id={"mp": lax.rem(d + k, n)}, device_id_type=MESH)
        load_x = pltpu.make_async_copy(b_hbm, x_around, own.at[0])
        load_d = pltpu.make_async_copy(dm_hbm, d_here, own.at[1])
        load_x.start()
        load_d.start()

        def halving_loads(p, i):
            plan, count = plans[i], plans[i].got[p].shape[0]
            some = pl.ds(0, count)
            return [
                pltpu.make_async_copy(plan.part(p, True), addend.at[0, i, some], add_sem.at[0, i]),
                pltpu.make_async_copy(plan.got[p], addend.at[1, i, some], add_sem.at[1, i]),
            ]

        def halving_save(p, i, k):
            plan = plans[i]
            ways = plan.split(plan.got[p].shape[0], p + 1)
            target = plan.now[p + 1].at[k // ways[1], k % ways[1]]
            return pltpu.make_async_copy(addend.at[0, i, k], target, add_sem.at[2 + i, k])

        def halving_begin(p):
            for i, plan in enumerate(plans):
                plan.copy(p).wait()
                for load in halving_loads(p, i):
                    load.start()

        def halving_end(p):
            for i, plan in enumerate(plans):
                for load in halving_loads(p, i):
                    load.wait()
                for k in range(plan.got[p].shape[0]):
                    addend[0, i, k] = (addend[0, i, k].astype(F32) + addend[1, i, k].astype(F32)).astype(BF)
                    halving_save(p, i, k).start()
            for i, plan in enumerate(plans):
                for k in range(plan.got[p].shape[0]):
                    halving_save(p, i, k).wait()
            if p + 1 < steps:
                for plan in plans:
                    plan.start(p + 1)

        def keep(row, lanes, value):
            g_own[row // small, row % small : row % small + 1, lanes] = value

        pl.semaphore_wait(barrier, devices + n - 2)
        for plan in plans:
            plan.start(0)
        g_own[...] = jnp.zeros(g_own.shape, F32)

        def norm(r, total):
            cells = mask_ref[r]
            back, part = normalise_back(co[r] * cells, gain_ref[...], dn[r])
            around[reach + r] = (back * cells).astype(BF)
            return total + part

        keep(taps, slice(None), lax.fori_loop(0, rows, norm, jnp.zeros((1, c), F32)))
        for i in range(low_gains.shape[0]):
            keep(taps + 1 + i, slice(None), low_ref[i : i + 1])
        up = pltpu.make_async_remote_copy(
            src_ref=around.at[pl.ds(reach, reach)], dst_ref=around.at[pl.ds(reach + rows, reach)],
            send_sem=sent.at[0], recv_sem=got.at[0], device_id={"mp": d - 1}, device_id_type=MESH,
        )
        down = pltpu.make_async_remote_copy(
            src_ref=around.at[pl.ds(rows, reach)], dst_ref=around.at[pl.ds(0, reach)],
            send_sem=sent.at[1], recv_sem=got.at[1], device_id={"mp": d + 1}, device_id_type=MESH,
        )
        nothing = jnp.zeros((reach, cols, c), BF)

        @pl.when(has_up)
        def _():
            up.start()

        @pl.when(has_down)
        def _():
            down.start()

        @pl.when(d == 0)
        def _():
            around[:reach] = nothing

        @pl.when(d == n - 1)
        def _():
            around[reach + rows :] = nothing

        load_x.wait()

        def lanes_of(i):
            return pl.ds(pl.multiple_of(i * LANES, LANES), LANES)

        def kernel_block(i, _):
            lanes = lanes_of(i)
            frame(dframed.at[pl.ds(reach, rows)], around.at[pl.ds(reach, rows), :, lanes])
            frame(xframed, x_around.at[:, :, lanes])
            for a in range(size):
                def some(r, accs):
                    dv = dframed[pl.ds(reach + r * group, group), EDGE : EDGE + cols]
                    new = []
                    for b in range(size):
                        prod = dv * xframed[pl.ds(r * group + a, group), pl.ds(EDGE - reach + b, cols), :]
                        new.append(accs[b] + jnp.sum(prod.reshape(-1, 8, LANES), axis=0))
                    return tuple(new)

                accs = lax.fori_loop(
                    0, rows // group, some, tuple(jnp.zeros((8, LANES), F32) for _ in range(size))
                )
                for b in range(size):
                    keep(a * size + b, lanes, jnp.sum(accs[b], axis=0, keepdims=True))
            return 0

        def input_block(i, _):
            lanes = lanes_of(i)
            frame(dframed, around.at[:, :, lanes])
            correlate(out.at[:, :, lanes], dframed, w_ref.at[:, :, lanes], size, True, group)
            for r in range(rows):
                out[r, :, lanes] = (out[r, :, lanes] + d_here[r, :, lanes].astype(F32)) * mask_ref[r]
            return 0

        def spread(k):
            peer = lax.rem(me + k, devices)
            return pltpu.make_async_remote_copy(
                src_ref=g_own.at[peer], dst_ref=here.at[me], send_sem=ar[0].at[k], recv_sem=ar[1].at[k],
                device_id={"dp": peer}, device_id_type=MESH,
            )

        def across(k):
            return pltpu.make_async_remote_copy(
                src_ref=level.at[d], dst_ref=level.at[d], send_sem=ar[2].at[k], recv_sem=ar[3].at[k],
                device_id={"mp": lax.rem(d + k, n)}, device_id_type=MESH,
            )

        def tell(k):
            return pltpu.make_async_remote_copy(
                src_ref=g_all.at[me], dst_ref=g_all.at[me], send_sem=ar[4].at[k], recv_sem=ar[5].at[k],
                device_id={"dp": lax.rem(me + k, devices)}, device_id_type=MESH,
            )

        def all_of(length, make, act):
            def one(k, _):
                act(make(k))
                return 0

            lax.fori_loop(1, length, one, 0)

        def sum_round(p):
            if p == 0:
                here[me] = g_own[me]
                all_of(devices, spread, lambda x: x.start())
            elif p == 1:
                all_of(devices, spread, lambda x: x.wait())
                level[d] = jnp.sum(here[...], axis=0)
                all_of(n, across, lambda x: x.start())
            elif p == 2:
                all_of(n, across, lambda x: x.wait())
                g_all[me] = jnp.sum(level[...], axis=0)
                all_of(devices, tell, lambda x: x.start())
            else:
                all_of(devices, tell, lambda x: x.wait())

        marks = sorted(set(begins) | set(ends) | set(rounds) | {blocks, 2 * blocks})
        at = 0
        for mark in marks:
            if at < blocks:
                lax.fori_loop(at, min(mark, blocks), kernel_block, 0)
            else:
                lax.fori_loop(at - blocks, mark - blocks, input_block, 0)
            at = mark
            if mark in ends:
                halving_end(ends[mark])
            if mark in begins:
                halving_begin(begins[mark])
            if mark == first_due:
                sum_round(0)
            if mark == blocks:
                load_d.wait()

                @pl.when(has_up)
                def _():
                    down.wait_recv()

                @pl.when(has_down)
                def _():
                    up.wait_recv()
            if mark in rounds:
                sum_round(rounds[mark])
        sum_round(2)
        halving_begin(steps - 1)
        halving_end(steps - 1)
        sum_round(3)

        @pl.when(has_up)
        def _():
            up.wait_send()

        @pl.when(has_down)
        def _():
            down.wait_send()

    whole = pl.BlockSpec(memory_space=pl.ANY)
    local = pl.BlockSpec(memory_space=pltpu.VMEM)
    vm, dma = pltpu.VMEM, pltpu.SemaphoreType.DMA
    d_in, g_all, *extra = pl.pallas_call(
        kernel,
        out_shape=(
            jax.ShapeDtypeStruct((rows, cols, c), F32),
            jax.ShapeDtypeStruct((devices, small, c), F32),
            *plans[0].buffers(),
            *plans[1].buffers(),
        ),
        in_specs=[local] * 6 + [whole] * 4,
        out_specs=(local,) * 2 + (whole,) * (2 * each),
        scratch_shapes=[
            vm((high, cols, c), BF), vm((high, cols, c), BF), vm((rows, cols, c), BF),
            vm((high, cols + 2 * EDGE, LANES), F32), vm((high, cols + 2 * EDGE, LANES), F32),
            vm((devices, small, c), F32), vm((devices, small, c), F32), vm((n, small, c), F32),
            vm((2, 2, shape[0] // 2) + shape[1:], BF),
            dma((2,)), dma((2,)), dma((2,)), dma((4, max(2, shape[0] // 2))),
            dma((devices,)), dma((devices,)), dma((n,)), dma((n,)), dma((devices,)), dma((devices,)),
        ]
        + plans[0].semaphores() + plans[1].semaphores(),
        compiler_params=pltpu.CompilerParams(
            collective_id=3, has_side_effects=True, vmem_limit_bytes=50 * MIB
        ),
        cost_estimate=pl.CostEstimate(flops=6 * 10**10, bytes_accessed=10**8, transcendentals=0),
    )(
        d_normed, conv_out, gain, mask, w, low_gains, bordered, d_map,
        grads[0].reshape((shape[0] // 2, 2) + shape[1:]), grads[1].reshape((2, shape[0] // 2) + shape[1:]),
    )
    sums = g_all.reshape(devices * small, c)[:count]
    return d_in, sums, [extra[each - 1].reshape(shape[1:]), extra[2 * each - 1].reshape(shape[1:])]


GATE, OUT, HIGH_A, HIGH_B, QUERY, KEY, VALUE, PROJ = range(8)
L_LOW, L_DF, L_POOL_A, L_POOL_B, L_FIRST, L_DA, L_SECOND, L_COT = range(8)
R_DGATE, R_MERGE, R_DHIGH, R_DQ, R_DK, R_DV, R_ATT, R_DUP, R_ACT = range(9)


def nn(a, b):
    return jnp.dot(a, b, preferred_element_type=F32)


def nt(a, b):
    return lax.dot_general(a, b, (((1,), (1,)), ((), ())), preferred_element_type=F32)


def tn(a, b):
    return lax.dot_general(a, b, (((0,), (0,)), ((), ())), preferred_element_type=F32)


def normalise(x, gain):
    centred = x - jnp.mean(x, -1, keepdims=True)
    rate = lax.rsqrt(jnp.mean(centred * centred, -1, keepdims=True) + 1e-06)
    return centred * rate * gain


def normalise_back(x, gain, d):
    centred = x - jnp.mean(x, -1, keepdims=True)
    rate = lax.rsqrt(jnp.mean(centred * centred, -1, keepdims=True) + 1e-06)
    hat = centred * rate
    dg = d * gain
    back = rate * (dg - jnp.mean(dg, -1, keepdims=True) - hat * jnp.mean(dg * hat, -1, keepdims=True))
    return back, jnp.sum(d * hat, axis=0, keepdims=True)


def low_stage(low, pool_a, pool_b, cot, gain1, gain2, packed, n, devices, cid):
    t, dim = low.shape
    every = n * t
    width = dim // n
    heads = width // HEAD
    groups = width // LANES
    pairs = devices // 2
    rows = dim // devices
    half = dim // 2
    ff = 4 * dim
    scale = HEAD ** (-0.5)

    def kernel(
        low_ref, pool_a_ref, pool_b_ref, cot_ref, gain1_ref, gain2_ref, w_hbm,
        low_out, d_low, d_pool_a, d_pool_b, g_ln1, g_ln2, grads,
        wv, lhs, lhs2, rhs, gate, high, merged, resid, d_res, slope, mixed, heads_in, att_all, d_att, d_mixed,
        d_heads, probs, d_scores, stage, left, w_sem, q_send, q_got, a_send, a_got, b_send, b_got, c_send, c_got, own_sem,
        l_send, l_got, r_send, r_got, stage_sem,
    ):
        d = lax.axis_index("mp")
        dp = lax.axis_index("dp")
        core = lax.rem(dp, 2)
        mate = dp + 1 - 2 * core
        barrier = pltpu.get_barrier_semaphore()
        for k in range(1, n):
            pl.semaphore_signal(barrier, inc=1, device_id={"mp": lax.rem(d + k, n)}, device_id_type=MESH)
        pl.semaphore_signal(barrier, inc=1, device_id={"dp": mate}, device_id_type=MESH)

        def w_copy(w, k):
            c, z = k // n, lax.rem(k, n)
            wide, base, at = w_place(w)
            src = w_hbm.at[:, c, z, :, pl.ds(base, wide)]
            dst = wv.at[c, :, :, pl.ds(pl.multiple_of(at + z * wide, wide), wide)]
            return pltpu.make_async_copy(src, dst, w_sem.at[w, k])

        def w_place(w):
            if w < 8:
                return width, w * width, w * dim
            return ff // n, 8 * width + (w - 8) * ff // n, 8 * dim + (w - 8) * ff

        def w_each(w, act):
            def one(k, _):
                act(w_copy(w, k))
                return 0

            lax.fori_loop(0, 2 * n, one, 0)

        for w in range(10):
            w_each(w, lambda copy: copy.start())

        def w_wait(*which):
            for w in which:
                w_each(w, lambda copy: copy.wait())

        def w_cols(at, size):
            return wv[:, :, :, pl.ds(at, size)].reshape(dim, size)

        def forward(x, first, count, put):
            def one(i, _):
                put(pl.multiple_of(i * TILE, TILE), nn(x, w_cols(pl.multiple_of(first * dim + i * TILE, TILE), TILE)))
                return 0
            lax.fori_loop(0, count * dim // TILE, one, 0)

        def backward(get, first, count, dst, fresh):
            def one(i, _):
                for c in range(2):
                    part = wv[c, :, :, pl.ds(pl.multiple_of((first + i) * dim, dim), dim)].reshape(half, dim)
                    y = nt(get(pl.multiple_of(i * dim, dim)), part)
                    cols = slice(c * half, (c + 1) * half)
                    if fresh and count == 1:
                        dst[:, cols] = y
                    else:
                        dst[:, cols] += y
                return 0
            if fresh and count > 1:
                dst[...] = jnp.zeros(dst.shape, F32)
            if count == 1:
                one(0, 0)
            else:
                lax.fori_loop(0, count, one, 0)

        def r_cols(block, count=1):
            return pl.ds(block * dim, count * dim)

        def r_at(block):
            return block * dim if block <= R_DUP else block * dim + 3 * dim

        def r_copy(block):
            cols = pl.ds(r_at(block), dim if block < R_DUP else ff)
            return pltpu.make_async_remote_copy(
                src_ref=rhs.at[0, :, cols], dst_ref=rhs.at[1, :, cols], send_sem=r_send.at[block],
                recv_sem=r_got.at[block], device_id={"dp": mate}, device_id_type=MESH)

        def l_copy(i):
            return pltpu.make_async_remote_copy(
                src_ref=lhs.at[i, :, pl.ds(pl.multiple_of((1 - core) * half, half), half)], dst_ref=lhs2.at[i],
                send_sem=l_send.at[i], recv_sem=l_got.at[i], device_id={"dp": mate}, device_id_type=MESH)

        stored = []
        turned = [None]

        def put_natural(dst, value):
            if rows % LANES:
                dst[...] = value
            else:
                for k in range(devices):
                    at = (k % 2) * half + k // 2 * rows
                    dst[:, k * rows : (k + 1) * rows] = value[:, at : at + rows]

        def grad(i, block, at, count, shared=False):
            if not shared:
                r_copy(block).wait_recv()
            if turned[0] != i:
                left[0] = lhs[i, :, pl.ds(pl.multiple_of(core * half, half), half)].T
                left[1] = lhs2[i].T
                turned[0] = i

            wide, base, first = w_place(at if at < 8 else 8 + (at - 8) * dim // ff)
            piece = min(TILE, wide)

            def out_copies(slot, k):
                out = []
                for q in range(TILE // piece):
                    z, col = divmod(at * dim - first + k * TILE + q * piece, wide)
                    out.append(
                        pltpu.make_async_copy(
                            stage.at[slot, :, :, pl.ds(q * piece, piece)],
                            grads.at[:, pl.ds(z * rows, rows), pl.ds(base + col, piece)],
                            stage_sem.at[slot, q],
                        )
                    )
                return out

            for k in range(count * dim // TILE):
                slot = len(stored) % 2
                if len(stored) >= 2:
                    wait(stored[-2])
                cols = pl.ds(r_at(block) + k * TILE, TILE)
                y = nn(left[0], rhs[0, :, cols]) + nn(left[1], rhs[1, :, cols])
                stage[slot] = y.astype(BF).reshape(pairs, rows, TILE)
                stored.append(out_copies(slot, k))
                start(stored[-1])

        def to_heads(k, src, dst, send, got):
            out = []
            for step in range(1, n):
                peer = lax.rem(d + step, n)
                out.append(pltpu.make_async_remote_copy(
                    src_ref=src.at[:, pl.ds(pl.multiple_of(peer * width, width), width)],
                    dst_ref=dst.at[pl.ds(pl.multiple_of(d * t, t), t)],
                    send_sem=send.at[k, step], recv_sem=got.at[k, step], device_id={"mp": peer}, device_id_type=MESH))
            out.append(pltpu.make_async_copy(
                src.at[:, pl.ds(pl.multiple_of(d * width, width), width)], dst.at[pl.ds(pl.multiple_of(d * t, t), t)], own_sem.at[k]))
            return out

        def to_tokens(k, src, dst, send, got, group):
            out = []
            slot = k * groups + group
            lanes = pl.ds(group * LANES, LANES)
            there = pl.ds(pl.multiple_of(d * width + group * LANES, LANES), LANES)
            for step in range(1, n):
                peer = lax.rem(d + step, n)
                out.append(pltpu.make_async_remote_copy(
                    src_ref=src.at[pl.ds(pl.multiple_of(peer * t, t), t), lanes], dst_ref=dst.at[:, there],
                    send_sem=send.at[slot, step], recv_sem=got.at[slot, step], device_id={"mp": peer}, device_id_type=MESH))
            out.append(pltpu.make_async_copy(
                src.at[pl.ds(pl.multiple_of(d * t, t), t), lanes], dst.at[:, there], own_sem.at[slot]))
            return out

        def start(copies):
            for c in copies:
                c.start()

        def wait(copies):
            for c in copies:
                c.wait()

        lhs[L_LOW] = low_ref[...]
        lhs[L_POOL_A] = pool_a_ref[...]
        lhs[L_POOL_B] = pool_b_ref[...]
        lhs[L_COT] = cot_ref[...]
        acc = d_low
        w_wait(GATE)

        def put_gate(at, y):
            gate[:, pl.ds(at, TILE)] = 1.0 / (1.0 + jnp.exp(-y))
        forward(lhs[L_LOW], GATE, 1, put_gate)
        w_wait(HIGH_A, HIGH_B, OUT)

        def put_high(at, y):
            high[:, pl.ds(at, TILE)] = y
        forward(lhs[L_POOL_A], HIGH_A, 1, put_high)

        def put_merging(at, y):
            cols = pl.ds(at, TILE)
            total = high[:, cols] + y
            high[:, cols] = total
            rhs[0, :, pl.ds(R_MERGE * dim + at, TILE)] = (total * gate[:, cols]).astype(BF)
        forward(lhs[L_POOL_B], HIGH_B, 1, put_merging)
        backward(lambda at: rhs[0, :, r_cols(R_MERGE)], OUT, 1, merged, True)
        merged[...] += lhs[L_LOW].astype(F32)
        lhs[L_FIRST] = normalise(merged[...], gain1_ref[...]).astype(BF)

        w_wait(QUERY, KEY, VALUE, PROJ)
        pl.semaphore_wait(barrier, n)
        for i in (L_LOW, L_POOL_A, L_POOL_B, L_COT, L_FIRST):
            l_copy(i).start()
        r_copy(R_MERGE).start()
        out_q = []
        for k in range(3):
            def put_mixed(at, y):
                mixed[k, :, pl.ds(at, TILE)] = y.astype(BF)
            forward(lhs[L_FIRST], QUERY + k, 1, put_mixed)
            copies = to_heads(k, mixed.at[k], heads_in.at[k], q_send, q_got)
            start(copies)
            out_q.append(copies)
        wait(out_q[0] + out_q[1])

        for h in range(heads):
            lanes = slice(h * HEAD, (h + 1) * HEAD)

            def rows_of(b, _):
                some = pl.ds(pl.multiple_of(b * t, t), t)
                s = nt(heads_in[0, some, lanes], heads_in[1, :, lanes]) * scale
                e = jnp.exp(s - jnp.max(s, -1, keepdims=True))
                p = (e * (1.0 / jnp.sum(e, -1, keepdims=True))).astype(BF)
                probs[h, some] = p
                return 0
            lax.fori_loop(0, n, rows_of, 0)
        wait(out_q[2])
        out_a = []
        for h in range(heads):
            lanes = slice(h * HEAD, (h + 1) * HEAD)

            def attend(b, _):
                some = pl.ds(pl.multiple_of(b * t, t), t)
                att_all[some, lanes] = nn(probs[h, some], heads_in[2, :, lanes]).astype(BF)
                return 0
            lax.fori_loop(0, n, attend, 0)
            if (h + 1) * HEAD % LANES == 0:
                copies = to_tokens(0, att_all, rhs.at[0, :, r_cols(R_ATT)], a_send, a_got, h * HEAD // LANES)
                start(copies)
                out_a += copies
        wait(out_a)
        r_copy(R_ATT).start()
        backward(lambda at: rhs[0, :, r_cols(R_ATT)], PROJ, 1, resid, True)
        resid[...] += merged[...]
        lhs[L_SECOND] = normalise(resid[...], gain2_ref[...]).astype(BF)
        l_copy(L_SECOND).start()

        w_wait(8)

        def put_up(at, y):
            value, rate = gelu_parts(y)
            rhs[0, :, pl.ds(r_at(R_ACT) + at, TILE)] = value.astype(BF)
            slope[:, pl.ds(at, TILE)] = rate.astype(BF)
        forward(lhs[L_SECOND], 8, 4, put_up)
        r_copy(R_ACT).start()
        w_wait(9)
        backward(lambda at: rhs[0, :, pl.ds(r_at(R_ACT) + at, dim)], 12, 4, acc, True)
        put_natural(low_out, resid[...] + acc[...])

        def put_d_up(at, y):
            rhs[0, :, pl.ds(r_at(R_DUP) + at, TILE)] = (y * slope[:, pl.ds(at, TILE)].astype(F32)).astype(BF)
        forward(lhs[L_COT], 12, 4, put_d_up)
        r_copy(R_DUP).start()
        backward(lambda at: rhs[0, :, pl.ds(r_at(R_DUP) + at, dim)], 8, 4, acc, True)
        back, g = normalise_back(resid[...], gain2_ref[...], acc[...])
        g_ln2[...] = g
        d_res[...] = lhs[L_COT].astype(F32) + back
        lhs[L_DA] = d_res[...].astype(BF)
        l_copy(L_DA).start()

        def put_d_att(at, y):
            mixed[0, :, pl.ds(at, TILE)] = y.astype(BF)
        forward(lhs[L_DA], PROJ, 1, put_d_att)
        out_b = to_heads(0, mixed.at[0], d_att, b_send, b_got)
        start(out_b)
        l_copy(L_COT).wait_recv()
        grad(L_COT, R_ACT, 12, 4)
        wait(out_b)
        out_c = []

        def send_back(k, h):
            if (h + 1) * HEAD % LANES == 0:
                copies = to_tokens(k, d_heads.at[k], rhs.at[0, :, r_cols(R_DQ + k)], c_send, c_got, h * HEAD // LANES)
                start(copies)
                out_c.extend(copies)

        for h in range(heads):
            lanes = slice(h * HEAD, (h + 1) * HEAD)
            d_heads[2, :, lanes] = tn(probs[h], d_att[:, lanes]).astype(BF)
            send_back(2, h)
        for h in range(heads):
            lanes = slice(h * HEAD, (h + 1) * HEAD)

            def rows_of(b, _):
                some = pl.ds(pl.multiple_of(b * t, t), t)
                p = probs[h, some].astype(F32)
                dp_ = nt(d_att[some, lanes], heads_in[2, :, lanes])
                ds = (p * (dp_ - jnp.sum(dp_ * p, -1, keepdims=True)) * scale).astype(BF)
                d_scores[some] = ds
                d_heads[0, some, lanes] = nn(ds, heads_in[1, :, lanes]).astype(BF)
                return 0
            lax.fori_loop(0, n, rows_of, 0)
            d_heads[1, :, lanes] = tn(d_scores[...], heads_in[0, :, lanes]).astype(BF)
            send_back(0, h)
            send_back(1, h)
        l_copy(L_SECOND).wait_recv()
        grad(L_SECOND, R_DUP, 8, 4)
        l_copy(L_DA).wait_recv()
        grad(L_DA, R_ATT, PROJ, 1)
        wait(out_c)
        for k in range(3):
            r_copy(R_DQ + k).start()
        backward(lambda at: rhs[0, :, pl.ds(R_DQ * dim + at, dim)], QUERY, 3, acc, True)
        back, g = normalise_back(merged[...], gain1_ref[...], acc[...])
        g_ln1[...] = g
        d_res[...] += back
        lhs[L_DF] = d_res[...].astype(BF)
        l_copy(L_DF).start()

        def put_d_gate(at, y):
            cols = pl.ds(at, TILE)
            gv = gate[:, cols]
            part = y * gv
            rhs[0, :, pl.ds(R_DHIGH * dim + at, TILE)] = part.astype(BF)
            rhs[0, :, pl.ds(R_DGATE * dim + at, TILE)] = (part * high[:, cols] * (1.0 - gv)).astype(BF)
        forward(lhs[L_DF], OUT, 1, put_d_gate)
        r_copy(R_DHIGH).start()
        r_copy(R_DGATE).start()
        backward(lambda at: rhs[0, :, r_cols(R_DHIGH)], HIGH_A, 1, d_pool_a, True)
        backward(lambda at: rhs[0, :, r_cols(R_DHIGH)], HIGH_B, 1, d_pool_b, True)
        backward(lambda at: rhs[0, :, r_cols(R_DGATE)], GATE, 1, acc, True)
        put_natural(d_low, d_res[...] + acc[...])
        l_copy(L_FIRST).wait_recv()
        for k in range(3):
            grad(L_FIRST, R_DQ + k, QUERY + k, 1)
        l_copy(L_DF).wait_recv()
        grad(L_DF, R_MERGE, OUT, 1)
        l_copy(L_POOL_A).wait_recv()
        grad(L_POOL_A, R_DHIGH, HIGH_A, 1)
        l_copy(L_POOL_B).wait_recv()
        grad(L_POOL_B, R_DHIGH, HIGH_B, 1, shared=True)
        l_copy(L_LOW).wait_recv()
        grad(L_LOW, R_DGATE, GATE, 1)
        wait(stored[-2])
        wait(stored[-1])
        for i in range(8):
            l_copy(i).wait_send()
        for b in range(9):
            r_copy(b).wait_send()

    whole = pl.BlockSpec(memory_space=pl.ANY)
    local = pl.BlockSpec(memory_space=pltpu.VMEM)
    vm, dma = pltpu.VMEM, pltpu.SemaphoreType.DMA
    tok = jax.ShapeDtypeStruct((t, dim), F32)
    one = jax.ShapeDtypeStruct((1, dim), F32)
    return pl.pallas_call(
        kernel,
        out_shape=(tok, tok, tok, tok, one, one, jax.ShapeDtypeStruct((pairs, n * rows, 16 * width), BF)),
        in_specs=[local] * 6 + [whole],
        out_specs=(local,) * 6 + (whole,),
        scratch_shapes=[
            vm((2, pairs, rows, 16 * dim), BF), vm((8, t, dim), BF), vm((8, t, half), BF), vm((2, t, 15 * dim), BF),
            vm((t, dim), F32), vm((t, dim), F32), vm((t, dim), F32), vm((t, dim), F32), vm((t, dim), F32),
            vm((t, ff), BF), vm((3, t, dim), BF), vm((3, every, width), BF), vm((every, width), BF), vm((every, width), BF),
            vm((1, 8, 128), BF), vm((3, every, width), BF), vm((heads, every, every), BF), vm((every, every), BF),
            vm((2, pairs, rows, TILE), BF), vm((2, half, t), BF),
            dma((10, 2 * n)), dma((3, n)), dma((3, n)), dma((groups, n)), dma((groups, n)), dma((1, n)), dma((1, n)),
            dma((3 * groups, n)), dma((3 * groups, n)), dma((3 * groups,)), dma((8,)), dma((8,)), dma((9,)), dma((9,)), dma((2, 2)),
        ],
        compiler_params=pltpu.CompilerParams(collective_id=cid, has_side_effects=True, vmem_limit_bytes=62 * MIB),
        cost_estimate=pl.CostEstimate(flops=14 * 10**9, bytes_accessed=70 * 10**6, transcendentals=10**7),
    )(low, pool_a, pool_b, cot, gain1, gain2, packed.reshape(pairs, 2, n, rows, 16 * width))
def low_outputs(own, widths, high_rows):
    share = own.shape[0]
    width, wide = widths[0], widths[-1]

    def kernel(x, gate, high, out, qkv, proj, up, down):
        def part(i, size=width):
            at = sum(widths[:i])
            return x[:, at : at + size].astype(F32)

        gate[...] = part(0)
        out[...] = part(1).T
        high[:share] = part(2)
        high[share:] = part(3)[: high_rows - share]
        for k in range(3):
            qkv[k] = part(4 + k)
        proj[...] = part(7).T
        up[...] = part(8, wide)
        down[...] = part(9, wide).T

    local = pl.BlockSpec(memory_space=pltpu.VMEM)
    shapes = [
        (share, width), (high_rows, width), (width, share), (3, share, width), (width, share), (share, wide), (wide, share),
    ]
    return pl.pallas_call(
        kernel,
        out_shape=[jax.ShapeDtypeStruct(s, F32) for s in shapes],
        in_specs=[local],
        out_specs=[local] * 7,
        compiler_params=pltpu.CompilerParams(vmem_limit_bytes=32 * MIB),
    )(own)


def map_outputs(g_up, g_down, others):
    count = len(others)

    def kernel(up, down, *rest):
        sources, o_up, o_down = rest[:count], rest[count], rest[count + 1]
        targets, held, sems = rest[count + 2 : 2 * count + 2], rest[2 * count + 2 : -1], rest[-1]
        loads = [pltpu.make_async_copy(a, b, sems.at[0, i]) for i, (a, b) in enumerate(zip(sources, held))]
        saves = [pltpu.make_async_copy(a, b, sems.at[1, i]) for i, (a, b) in enumerate(zip(held, targets))]
        for load in loads:
            load.start()
        o_up[...] = up[...].astype(F32)
        o_down[...] = down[...].astype(F32)
        for load, save in zip(loads, saves):
            load.wait()
            save.start()
        for save in saves:
            save.wait()

    whole = pl.BlockSpec(memory_space=pl.ANY)
    local = pl.BlockSpec(memory_space=pltpu.VMEM)
    return pl.pallas_call(
        kernel,
        out_shape=[jax.ShapeDtypeStruct(x.shape, F32) for x in (g_up, g_down, *others)],
        in_specs=[local] * 2 + [whole] * count,
        out_specs=[local] * 2 + [whole] * count,
        scratch_shapes=[pltpu.VMEM(o.shape, o.dtype) for o in others] + [pltpu.SemaphoreType.DMA((2, count))],
        compiler_params=pltpu.CompilerParams(vmem_limit_bytes=60 * MIB),
        cost_estimate=pl.CostEstimate(flops=10**9, bytes_accessed=24 * 10**6, transcendentals=0),
    )(g_up, g_down, *others)


def pack_weights(ad_gate, ad_out, ad_high, w_qkv, w_proj, w_up, w_down, devices):
    dim, width = ad_gate.shape
    share, high_rows, wide = dim // devices, ad_high.shape[0] // devices, w_up.shape[1]
    rest = high_rows - share

    def kernel(gate, out, high, qkv, proj, up, down, packed, side, side_wide, sems):
        me = lax.axis_index("dp")
        mine = pl.ds(pl.multiple_of(me * share, share), share)
        lanes = mine

        def at(i, size=width):
            return packed.at[:, pl.ds(i * width, size)]

        straight = [(gate.at[mine], at(0)), (up.at[mine], at(8, wide))]
        straight += [(qkv.at[k, mine], at(4 + k)) for k in range(3)]
        straight.append((high.at[pl.ds(pl.multiple_of(me * high_rows, rest), share)], at(2)))
        straight.append((high.at[pl.ds(pl.multiple_of(me * high_rows + share, rest), rest)], at(3).at[pl.ds(0, rest)]))
        straight += [(out.at[:, lanes], side.at[0]), (proj.at[:, lanes], side.at[1]), (down.at[:, lanes], side_wide)]
        copies = [pltpu.make_async_copy(a, b, sems.at[i]) for i, (a, b) in enumerate(straight)]
        for copy in copies:
            copy.start()
        packed[rest:, 3 * width : 4 * width] = jnp.zeros((share - rest, width), BF)
        for copy in copies:
            copy.wait()
        packed[:, width : 2 * width] = side[0].T
        packed[:, 7 * width : 8 * width] = side[1].T
        packed[:, 8 * width + wide :] = side_wide[...].T

    whole = pl.BlockSpec(memory_space=pl.ANY)
    return pl.pallas_call(
        kernel,
        out_shape=jax.ShapeDtypeStruct((share, 8 * width + 2 * wide), BF),
        in_specs=[whole] * 7,
        out_specs=pl.BlockSpec(memory_space=pltpu.VMEM),
        scratch_shapes=[
            pltpu.VMEM((2, width, share), BF), pltpu.VMEM((wide, share), BF), pltpu.SemaphoreType.DMA((10,)),
        ],
        compiler_params=pltpu.CompilerParams(vmem_limit_bytes=60 * MIB),
    )(ad_gate, ad_out, ad_high, w_qkv, w_proj, w_up, w_down)


def rows_first(x):
    return with_layout_constraint(x, Layout(major_to_minor=tuple(range(x.ndim))))


def own_part(w, axis):
    length = w.shape[axis] // lax.axis_size("dp")
    return lax.dynamic_slice_in_dim(w, lax.axis_index("dp") * length, length, axis)


def fold(w, rows):
    return w[:rows], jnp.pad(w[rows:], ((0, 2 * rows - w.shape[0]), (0, 0)))


def core_first(x, devices):
    shape = x.shape
    return x.reshape(shape[:-1] + (devices // 2, 2, -1)).swapaxes(-3, -2).reshape(shape)


def core_last(x, devices):
    shape = x.shape
    return x.reshape(shape[:-1] + (2, devices // 2, -1)).swapaxes(-3, -2).reshape(shape)


def layer_norm(values, gain):
    centre = jnp.mean(values, -1, keepdims=True)
    centred = values - centre
    variance = jnp.mean(centred * centred, -1, keepdims=True)
    return centred * lax.rsqrt(variance + 1e-06) * gain


def per_device(
    hr_in,
    low_in,
    valid,
    conv_w,
    hr_gain,
    cn_up,
    cn_down,
    ad_gate,
    ad_high,
    ad_out,
    ln1_gain,
    w_qkv,
    w_proj,
    ln2_gain,
    w_up,
    w_down,
    cot_low,
    cot_hr,
):
    _, row_count, col_count, chan_count = hr_in.shape
    devices, shards = lax.axis_size("dp"), lax.axis_size("mp")
    dims = low_in.shape[2]
    share = dims // devices
    qkv = own_part(w_qkv, 1)
    low_weights = (ad_gate, ad_out, ad_high, w_qkv, w_proj, w_up, w_down)
    pieces = [
        own_part(ad_gate, 0), own_part(ad_out, 1).T, *fold(own_part(ad_high, 0), share),
        qkv[0], qkv[1], qkv[2], own_part(w_proj, 1).T, own_part(w_up, 0), own_part(w_down, 1).T,
    ]
    if share % LANES:
        packed = rows_first(jnp.concatenate(pieces, axis=1))
    else:
        packed = pack_weights(*low_weights, devices)
    packed = rows_first(lax.all_gather(packed, "mp", axis=0, tiled=True))
    plane_mask = valid[0].astype(F32)
    cell_mask = plane_mask[..., None]
    masked = hr_in[0] * valid[0].astype(BF)[..., None]
    half_rows, half_cols = (row_count // 2, col_count // 2)
    counts = plane_mask.reshape(half_rows, 2, half_cols, 2).sum(axis=(1, 3))
    shares = 1.0 / jnp.maximum(counts, 1.0)
    size = conv_w.shape[0]
    taps = conv_w.astype(F32).reshape(size * size, 1, chan_count)
    conv_out, bordered = conv_forward(masked, taps, size, shards)
    hr_gainf = hr_gain.astype(F32)
    normed = layer_norm(conv_out * cell_mask, hr_gainf).astype(BF)
    normed, packed = lax.optimization_barrier((normed, packed))
    packed = rows_first(lax.all_gather(packed, "dp", axis=0, tiled=True))
    hr_out, pooled, normed_all, hidden_act, hidden_slope, up_t, down_t = big_forward(
        normed.reshape(row_count * col_count, chan_count), cn_up, cn_down, masked, plane_mask, shares, shards
    )
    hr_out = hr_out.reshape(hr_in.shape)
    tokens = half_rows * half_cols
    by_share = pooled.reshape(tokens, devices, -1)
    pool_a = by_share[:, :, :share].reshape(tokens, dims)
    pool_b = jnp.pad(by_share[:, :, share:], ((0, 0), (0, 0), (0, 2 * share - by_share.shape[2]))).reshape(tokens, dims)
    low_out, d_low_in, d_pool_a, d_pool_b, g_ln1, g_ln2, low_grads = low_stage(
        *(core_first(v, devices) for v in (low_in[0], pool_a, pool_b, cot_low[0])),
        *(core_first(v.astype(F32), devices)[None] for v in (ln1_gain, ln2_gain)),
        packed, shards, devices, 2,
    )
    if share % LANES:
        low_out, d_low_in = core_last(low_out, devices), core_last(d_low_in, devices)
    low_out, d_low_in = low_out[None], d_low_in[None]
    g_ln1, g_ln2 = core_last(g_ln1[0], devices), core_last(g_ln2[0], devices)
    d_pooled = jnp.concatenate(
        [
            core_last(d_pool_a, devices).reshape(tokens, devices, share),
            core_last(d_pool_b, devices).reshape(tokens, devices, share)[:, :, : by_share.shape[2] - share],
        ],
        axis=2,
    )
    d_normed, d_map, cn_grads, low_sums = big_backward(
        cot_hr[0], d_pooled.reshape(tokens, chan_count), shares, plane_mask, normed_all, hidden_act, hidden_slope,
        up_t, down_t, low_grads, shards, devices,
    )
    low_sums = rows_first(low_sums.reshape(shards, share, -1))
    low_sums = rows_first(lax.psum_scatter(low_sums, "mp", scatter_dimension=0))
    low_gains = jnp.pad(jnp.stack([g_ln1, g_ln2]), ((0, 0), (0, chan_count - dims)))
    d_hr_in, small_sums, (g_cn_up, g_cn_down) = conv_backward(
        d_normed, conv_out, hr_gainf[None], cell_mask, bordered, d_map, taps, low_gains, size, cn_grads, devices, shards
    )
    d_hr_in = d_hr_in[None]
    g_conv = small_sums[: size * size].reshape(conv_w.shape)
    g_hr_gain, g_ln1, g_ln2 = small_sums[size * size], small_sums[-2, :dims], small_sums[-1, :dims]
    g_cn_up, g_cn_down, low_out, hr_out, d_low_in, d_hr_in = map_outputs(
        g_cn_up, g_cn_down, (low_out, hr_out, d_low_in, d_hr_in)
    )
    g_ad_gate, g_ad_high, g_ad_out, g_qkv, g_proj, g_up, g_down = low_outputs(
        low_sums.reshape(share, -1), [p.shape[1] for p in pieces], ad_high.shape[0] // devices
    )
    g_cn_down = g_cn_down.T
    return (
        low_out,
        hr_out,
        d_low_in,
        d_hr_in,
        g_conv,
        g_hr_gain,
        g_cn_up,
        g_cn_down,
        g_ad_gate,
        g_ad_high,
        g_ad_out,
        g_ln1,
        g_qkv,
        g_proj,
        g_ln2,
        g_up,
        g_down,
    )


def solution(mesh):
    return jax.shard_map(
        per_device,
        mesh=mesh,
        in_specs=(
            P("dp", "mp", None, None),
            P("dp", "mp", None),
            P("dp", "mp", None),
            P(),
            P(),
            P(None, "mp"),
            P("mp", None),
            P(None, "mp"),
            P(None, "mp"),
            P("mp", None),
            P(),
            P(None, None, "mp"),
            P("mp", None),
            P(),
            P(None, "mp"),
            P("mp", None),
            P("dp", "mp", None),
            P("dp", "mp", None, None),
        ),
        out_specs=(
            P("dp", "mp", None),
            P("dp", "mp", None, None),
            P("dp", "mp", None),
            P("dp", "mp", None, None),
            P(),
            P(),
            P("dp", "mp"),
            P("mp", "dp"),
            P("dp", "mp"),
            P("dp", "mp"),
            P("mp", "dp"),
            P(),
            P(None, "dp", "mp"),
            P("mp", "dp"),
            P(),
            P("dp", "mp"),
            P("mp", "dp"),
        ),
        check_vma=False,
    )
```

```python
import jax
import jax.numpy as jnp
from jax import lax
from jax.experimental.layout import Layout, with_layout_constraint
from jax.experimental import pallas as pl
from jax.experimental.pallas import tpu as pltpu
from jax.sharding import PartitionSpec as P

HEAD = 64
LANES = 128
EDGE = 8
CHUNKS = 6
TILE = 512
MIB = 1024 * 1024
MESH = pl.DeviceIdType.MESH
BF = jnp.bfloat16
F32 = jnp.float32

def gelu_parts(x):
    c = 0.7978845608028654
    x2 = x * x
    t = jnp.tanh(c * x * (1.0 + 0.044715 * x2))
    half = 0.5 * (1.0 + t)
    slope = half + 0.5 * x * (1.0 - t * t) * (c * (1.0 + 3 * 0.044715 * x2))
    return x * half, slope


def gelu(x):
    c = 0.7978845608028654
    t = jnp.tanh(c * x * (1.0 + 0.044715 * (x * x)))
    return 0.5 * x * (1.0 + t)


def dp_bit(position):
    return lax.rem(lax.axis_index("dp") // 2**position, 2)


def dp_mate(position):
    return lax.axis_index("dp") + 2**position * (1 - 2 * dp_bit(position))


class Halving:
    def __init__(self, bits, lasts, shape, block):
        self.lasts, self.shape, self.block = lasts, shape, block
        left = list(bits)
        self.bits = [left.pop(0 if last else -1) for last in lasts]

    def split(self, count, p):
        if count == 1:
            return (1, 1)
        return (count // 2, 2) if self.lasts[p] else (2, count // 2)

    def buffers(self):
        count, rows, cols = self.shape
        got, held = [], []
        for p in range(len(self.bits)):
            count //= 2
            got.append(jax.ShapeDtypeStruct((count, rows, cols), BF))
            held.append(jax.ShapeDtypeStruct(self.split(count, p + 1) + (rows, cols), BF))
        return got + held

    def semaphores(self):
        return [pltpu.SemaphoreType.DMA((len(self.bits),))] * 2

    def bind(self, first, buffers, send, recv):
        steps = len(self.bits)
        self.now = [first] + list(buffers[steps:])
        self.got, self.send, self.recv = buffers[:steps], send, recv

    def part(self, p, mine):
        bit = dp_bit(self.bits[p])
        index = bit if mine else 1 - bit
        return self.now[p].at[:, index] if self.lasts[p] else self.now[p].at[index]

    def copy(self, p):
        return pltpu.make_async_remote_copy(
            src_ref=self.part(p, False), dst_ref=self.got[p], send_sem=self.send.at[p], recv_sem=self.recv.at[p],
            device_id={"dp": dp_mate(self.bits[p])}, device_id_type=MESH,
        )

    def start(self, p):
        self.copy(p).start()

    def finish(self, p, wait=True):
        if wait:
            self.copy(p).wait()
        count, rows, cols = self.got[p].shape
        ways = self.split(count, p + 1)

        def add(a, b, out):
            out[...] = (a[...].astype(F32) + b[...].astype(F32)).astype(BF).reshape(out.shape)

        flat = pl.BlockSpec((1, rows, self.block), lambda k, c: (k, 0, c))
        paired = pl.BlockSpec((1, 1, rows, self.block), lambda k, c: (k // ways[1], lax.rem(k, ways[1]), 0, c))
        pltpu.emit_pipeline(add, grid=(count, cols // self.block), in_specs=[flat, flat], out_specs=[paired])(
            self.part(p, True), self.got[p], self.now[p + 1]
        )


def chain_exchange(
    n, chunks, lag, gathered, partial, travel, sems, own_chunk, prepare, arrived, compute, mates=(), begin=None, turn=None, after=None, early=False
):
    ag_send, ag_recv, rs_send, rs_recv = sems
    d = lax.axis_index("mp")
    has_left, has_right = d > 0, d < n - 1

    barrier = pltpu.get_barrier_semaphore()

    @pl.when(has_left)
    def _():
        pl.semaphore_signal(barrier, inc=1, device_id={"mp": d - 1}, device_id_type=MESH)

    @pl.when(has_right)
    def _():
        pl.semaphore_signal(barrier, inc=1, device_id={"mp": d + 1}, device_id_type=MESH)

    for mate in mates:
        pl.semaphore_signal(barrier, inc=1, device_id={"dp": mate}, device_id_type=MESH)

    own_chunk(0)
    pl.semaphore_wait(barrier, has_left.astype(jnp.int32) + has_right.astype(jnp.int32) + len(mates))
    if begin is not None:
        begin()

    def ag(way, s, j):
        return pltpu.make_async_remote_copy(
            src_ref=gathered.at[s, j], dst_ref=gathered.at[s, j],
            send_sem=ag_send.at[way, s, j], recv_sem=ag_recv.at[s, j],
            device_id={"mp": d + 1 - 2 * way}, device_id_type=MESH,
        )

    def rs(way, s, j):
        there = d + 1 - 2 * way
        slot = jnp.where((s == there) & (way == 0), n, s)
        return pltpu.make_async_remote_copy(
            src_ref=travel.at[s, j], dst_ref=travel.at[slot, j],
            send_sem=rs_send.at[s, j], recv_sem=rs_recv.at[slot, j],
            device_id={"mp": there}, device_id_type=MESH,
        )

    def rs_wait(slot, j):
        pltpu.make_async_copy(travel.at[slot, j], travel.at[slot, j], rs_recv.at[slot, j]).wait()

    def first(j, _):
        @pl.when(j > 0)
        def _():
            own_chunk(j)

        @pl.when(has_right)
        def _():
            ag(0, d, j).start()

        @pl.when(has_left)
        def _():
            ag(1, d, j).start()

        return 0

    lax.fori_loop(0, chunks, first, 0)

    def flow(way, q):
        ql = jnp.clip(q, 0, n * chunks - 1)
        s, jj = ql // chunks, lax.rem(ql, chunks)
        if way == 1:
            s = n - 1 - s
        ahead = (s > d) if way == 0 else (s < d)
        source = has_left if way == 0 else has_right

        @pl.when((q >= 0) & (q < n * chunks) & (ahead | ((s == d) & source)))
        def _():
            @pl.when(source)
            def _():
                rs_wait(jnp.where(s == d, n, s) if way == 0 else s, jj)

            @pl.when(ahead & source)
            def _():
                travel[s, jj] = (partial[s, jj].astype(F32) + travel[s, jj].astype(F32)).astype(BF)

            @pl.when(ahead & jnp.logical_not(source))
            def _():
                travel[s, jj] = partial[s, jj].astype(BF)

            @pl.when(ahead)
            def _():
                rs(way, s, jj).start()

    def block_of(k, way):
        s = d - k + 2 * k * way
        return s, (s >= 0) & (s < n) & ((k > 0) | (way == 0))

    def receive(k, way, s, j):
        @pl.when(k > 0)
        def _():
            pltpu.make_async_copy(gathered.at[s, j], gathered.at[s, j], ag_recv.at[s, j]).wait()

            @pl.when((way == 0) & has_right)
            def _():
                ag(0, s, j).start()

            @pl.when((way == 1) & has_left)
            def _():
                ag(1, s, j).start()

        arrived(s, j)

    wait_one = 1 if early else 0

    def step(g, _):
        k, j = g // chunks, lax.rem(g, chunks)

        def sides(act):
            @pl.when(g < n * chunks)
            def _():
                def side(way, _):
                    s, ok = block_of(k, way)
                    pl.when(ok)(lambda: act(way, s))
                    return 0

                lax.fori_loop(0, 2, side, 0)

        def flows():
            flow(1, g - wait_one - (n - 1 - d) * lag)
            flow(0, g - wait_one - d * lag)

        if turn is not None:
            turn(g)
        if early:
            sides(lambda way, s: receive(k, way, s, j))
            flows()

            def later(way, s):
                prepare(way, s, j)
                compute(way, s, j)

            sides(later)
        else:
            def work(way, s):
                prepare(way, s, j)
                receive(k, way, s, j)
                compute(way, s, j)

            sides(work)
            flows()
        if after is not None:
            after(g)
        return 0

    lax.fori_loop(0, n * chunks + (n - 1) * lag + wait_one, step, 0)

    def drain(i, _):
        s, j = i // chunks, lax.rem(i, chunks)

        @pl.when(has_right & (s <= d))
        def _():
            ag(0, s, j).wait_send()

        @pl.when(has_left & (s >= d))
        def _():
            ag(1, s, j).wait_send()

        @pl.when(s < d)
        def _():
            rs(1, s, j).wait_send()

        @pl.when(s > d)
        def _():
            rs(0, s, j).wait_send()

        return 0

    lax.fori_loop(0, n * chunks, drain, 0)


def own_sum(n, d, j, partial, travel, total):
    total[...] = partial[d, j].astype(F32)

    @pl.when(d > 0)
    def _():
        total[...] += travel[n, j].astype(F32)

    @pl.when(d < n - 1)
    def _():
        total[...] += travel[d, j].astype(F32)


def chain_sems(n, chunks):
    dma = pltpu.SemaphoreType.DMA
    return [dma((2, n, chunks)), dma((n, chunks)), dma((n, chunks)), dma((n + 1, chunks))]


def chunk_buffers(n, rows, c, kept):
    return [
        pltpu.VMEM((n, CHUNKS, rows, c), BF),
        pltpu.VMEM((n, CHUNKS, rows, c), kept),
        pltpu.VMEM((n + 1, CHUNKS, rows, c), BF),
    ]


def columns(i):
    return pl.ds(pl.multiple_of(i * TILE, TILE), TILE)


def drain_copies(n, copy):
    def one(i, _):
        copy(i // CHUNKS, lax.rem(i, CHUNKS)).wait()
        return 0

    lax.fori_loop(0, n * CHUNKS, one, 0)


def big_forward(x, w_up, w_down, residual, mask, share, n):
    t, c = x.shape
    h = w_up.shape[1]
    rows = t // CHUNKS
    cols = residual.shape[1]
    half = cols // 2
    pairs = rows // cols // 2

    def kernel(
        x_ref, wu, wd, res, mask_ref, share_ref, out, pooled, x_all, act_all, slope_all, wu_t, wd_t,
        gathered, partial, travel, act, slope, total, folded, turned, copied, stored, load_sem, *sems
    ):
        d = lax.axis_index("mp")
        load = pltpu.make_async_copy(x_ref, gathered.at[d], load_sem)

        def own_chunk(j):
            if isinstance(j, int):
                load.start()
                load.wait()

        def x_copy(s, j):
            return pltpu.make_async_copy(gathered.at[s, j], x_all.at[s, j], copied.at[s, j])

        def prepare(way, s, j):
            pass

        def arrived(s, j):
            x_copy(s, j).start()

        def compute(way, s, j):
            block = gathered.at[s, j]

            def up(i, _):
                pre = jnp.dot(block[...], wu[:, columns(i)], preferred_element_type=F32)
                value, rate = gelu_parts(pre)
                act[:, columns(i)] = value.astype(BF)
                slope[:, columns(i)] = rate.astype(BF)
                return 0

            lax.fori_loop(0, h // TILE, up, 0)
            keep_act = pltpu.make_async_copy(act, act_all.at[s, j], stored.at[0])
            keep_slope = pltpu.make_async_copy(slope, slope_all.at[s, j], stored.at[1])
            keep_act.start()
            keep_slope.start()

            def down(i, _):
                partial[s, j, :, columns(i)] = jnp.dot(
                    act[...], wd[:, columns(i)], preferred_element_type=F32
                )
                return 0

            lax.fori_loop(0, c // TILE, down, 0)
            keep_act.wait()
            keep_slope.wait()

        def finish(j):
            pl.when(j > 0)(lambda: put(j - 1).wait())
            own_sum(n, d, j, partial, travel, total)
            values = (res[pl.ds(j * 2 * pairs, 2 * pairs)].reshape(rows, c).astype(F32) + total[...]) * mask_ref[j]
            partial[d, j] = values
            put(j).start()
            both = values.reshape(pairs, 2, cols, c)
            summed = (both[:, 0] + both[:, 1]).reshape(pairs * cols, c)
            for b in range(c // LANES):
                lanes = slice(b * LANES, (b + 1) * LANES)
                folded[b] = summed[:, lanes]
                every = folded[b, pl.ds(0, pairs * half, 2), :] + folded[b, pl.ds(1, pairs * half, 2), :]
                pooled[j, :, lanes] = every * share_ref[j]

        def put(j):
            return pltpu.make_async_copy(partial.at[d, j], out.at[j], load_sem)

        def after(g):
            last = g - (n - 1) * (CHUNKS + 1)
            pl.when(last >= 0)(lambda: finish(last))
            for i, (w, target, size) in enumerate(((wu, wu_t, h), (wd, wd_t, c))):
                @pl.when(g < size // LANES)
                def _():
                    some = pl.ds(pl.multiple_of(g * LANES, LANES), LANES)
                    turned[i, :, pl.ds(0, w.shape[0])] = w[:, some].T
                    copy = pltpu.make_async_copy(turned.at[i, :, pl.ds(0, w.shape[0])], target.at[some], stored.at[i])
                    copy.start()
                    copy.wait()

        chain_exchange(
            n, CHUNKS, 1, gathered, partial, travel, sems, own_chunk, prepare, arrived, compute, after=after
        )

        put(CHUNKS - 1).wait()
        drain_copies(n, x_copy)

    whole = pl.BlockSpec(memory_space=pl.ANY)
    local = pl.BlockSpec(memory_space=pltpu.VMEM)
    out, pooled, x_all, act_all, slope_all, wu_t, wd_t = pl.pallas_call(
        kernel,
        out_shape=(
            jax.ShapeDtypeStruct((CHUNKS, rows, c), F32),
            jax.ShapeDtypeStruct((CHUNKS, pairs * half, c), F32),
            jax.ShapeDtypeStruct((n, CHUNKS, rows, c), BF),
            jax.ShapeDtypeStruct((n, CHUNKS, rows, h), BF),
            jax.ShapeDtypeStruct((n, CHUNKS, rows, h), BF),
            jax.ShapeDtypeStruct((h, c), BF),
            jax.ShapeDtypeStruct((c, h), BF),
        ),
        in_specs=[whole, local, local, local, local, local],
        out_specs=(whole, local, whole, whole, whole, whole, whole),
        scratch_shapes=chunk_buffers(n, rows, c, F32)
        + [pltpu.VMEM((rows, h), BF)] * 2
        + [pltpu.VMEM((rows, c), F32), pltpu.VMEM((c // LANES, pairs * cols, LANES), F32), pltpu.VMEM((2, LANES, max(c, h)), BF)]
        + [pltpu.SemaphoreType.DMA((n, CHUNKS)), pltpu.SemaphoreType.DMA((2,)), pltpu.SemaphoreType.DMA]
        + chain_sems(n, CHUNKS),
        compiler_params=pltpu.CompilerParams(
            collective_id=0, has_side_effects=True, vmem_limit_bytes=60 * MIB
        ),
        cost_estimate=pl.CostEstimate(
            flops=4 * n * t * c * h, bytes_accessed=8 * n * t * c, transcendentals=n * t * h
        ),
    )(
        x.reshape(CHUNKS, rows, c), w_up, w_down, residual,
        mask.reshape(CHUNKS, rows, 1), share.reshape(CHUNKS, pairs * half, 1),
    )
    return (
        out.reshape(t, c),
        pooled.reshape(t // 4, c),
        x_all,
        act_all,
        slope_all,
        wu_t,
        wd_t,
    )


def big_backward(cot, d_pooled, share, mask, x_all, act_all, slope_all, up_t, down_t, grads, n, devices):
    _, cols, c = cot.shape
    t = cot.shape[0] * cols
    h = up_t.shape[0]
    rows = t // CHUNKS
    half = cols // 2
    pairs_here = rows // cols // 2
    piece = c // devices
    items = n * CHUNKS // 2
    pairs, g_rows, g_cols = grads.shape
    bits = range(1, devices.bit_length() - 1)
    split = g_rows // 2
    steps = len(bits)
    plans = [Halving(bits, [last] * steps, (pairs, split, g_cols), min(g_cols, 1024)) for last in (True, False)]
    extras = [b for plan in plans for b in plan.buffers()[:-1]]
    each = 2 * steps - 1

    def kernel(
        cot_ref, pool_ref, share_ref, mask_ref, x_hbm, act_hbm, slopes, wu, wd, g_first, g_second,
        out, d_own, g_up_out, g_down_out, out_up, out_down, got_up, got_down, h_all, *rest
    ):
        sums, extra, rest = rest[0], rest[1 : 1 + 2 * each], rest[1 + 2 * each :]
        gathered, partial, travel, slope, grad, left, right, middle, g_up, g_down, total, spread_rows, addend = rest[:13]
        core_send, core_recv, stored, add_sem, send0, recv0, send1, recv1 = rest[13:21]
        sems = rest[21:]
        d = lax.axis_index("mp")
        plans[0].bind(g_first.at[:, :, pl.ds(0, split)], extra[:each] + (sums.at[0],), send0, recv0)
        plans[1].bind(g_second.at[:, :, pl.ds(split, split)], extra[each:] + (sums.at[1],), send1, recv1)

        def begin():
            for plan in plans:
                plan.start(0)

        def pass_on(p, plan):
            plan.finish(p)
            if p + 1 < steps:
                plan.start(p + 1)

        first_due = 2 * CHUNKS + 4
        ticks = {}
        if steps == 2:
            for p, start in ((0, first_due), (1, n * CHUNKS + n - 2)):
                tiles = [
                    (plan, k, q)
                    for plan in plans
                    for k in range(plan.got[p].shape[0])
                    for q in range(g_cols // plan.block)
                ]
                for m in range(0, len(tiles), 4):
                    ticks[start + m // 4] = (p, m == 0, m + 4 >= len(tiles), tiles[m : m + 4])

        def tile_copy(which, p, i, plan, k, q):
            lanes = pl.ds(q * plan.block, plan.block)
            if which == 0:
                source, target = plan.part(p, True).at[k, :, lanes], addend.at[0, i]
            elif which == 1:
                source, target = plan.got[p].at[k, :, lanes], addend.at[1, i]
            else:
                ways = plan.split(plan.got[p].shape[0], p + 1)
                source, target = addend.at[0, i], plan.now[p + 1].at[k // ways[1], k % ways[1], :, lanes]
            return pltpu.make_async_copy(source, target, add_sem.at[which, i])

        def tick_begin(p, fresh, final, tiles):
            if fresh:
                for plan in plans:
                    plan.copy(p).wait()
            for i, tile in enumerate(tiles):
                for which in range(2):
                    tile_copy(which, p, i, *tile).start()

        def tick_add(p, fresh, final, tiles):
            for i, tile in enumerate(tiles):
                for which in range(2):
                    tile_copy(which, p, i, *tile).wait()
                addend[0, i] = (addend[0, i].astype(F32) + addend[1, i].astype(F32)).astype(BF)
                tile_copy(2, p, i, *tile).start()
            for i, tile in enumerate(tiles):
                tile_copy(2, p, i, *tile).wait()
            if final and p + 1 < steps:
                for plan in plans:
                    plan.start(p + 1)

        all_steps = n * CHUNKS + n
        due = [all_steps * 9 * (2**steps - 2 ** (steps - 1 - p)) // (10 * (2**steps - 1)) // 2 * 2 for p in range(steps)]

        def turn(g):
            if ticks:
                for at, tick in ticks.items():
                    pl.when(g == at)(lambda tick=tick: tick_begin(*tick))
            else:
                for p in range(steps - 1):
                    for i, plan in enumerate(plans):
                        pl.when(g == due[p] + 2 * i)(lambda p=p, plan=plan: pass_on(p, plan))

            q, due_now = item_of(g)

            @pl.when(due_now)
            def _():
                for copy in item_copies(q):
                    copy.start()

        def own_chunk(j):
            part = pool_ref[j] * share_ref[j]
            here = cot_ref.at[pl.ds(j * 2 * pairs_here, 2 * pairs_here)]
            for b in range(c // LANES):
                lanes = slice(b * LANES, (b + 1) * LANES)
                spread_rows[b, pl.ds(0, pairs_here * half, 2), :] = part[:, lanes]
                spread_rows[b, pl.ds(1, pairs_here * half, 2), :] = part[:, lanes]
                block = jnp.broadcast_to(
                    spread_rows[b].reshape(pairs_here, 1, cols, LANES), (pairs_here, 2, cols, LANES)
                ).reshape(rows, LANES)
                cell = here[:, :, lanes].reshape(rows, LANES).astype(F32)
                gathered[d, j, :, lanes] = ((cell + block) * mask_ref[j]).astype(BF)

        def slope_copy(s, j):
            return pltpu.make_async_copy(slopes.at[s, j], slope, stored.at[0])

        def prepare(way, s, j):
            slope_copy(s, j).start()

        def arrived(s, j):
            pass

        def compute(way, s, j):
            block = gathered.at[s, j]
            slope_copy(s, j).wait()

            def up(i, _):
                back = nn(block[...], wd[:, columns(i)])
                grad[:, columns(i)] = (back * slope[:, columns(i)].astype(F32)).astype(BF)
                return 0

            lax.fori_loop(0, h // TILE, up, 0)
            half_pair = pl.ds(pl.multiple_of(lax.rem(j, 2) * rows, rows), rows)
            keep = pltpu.make_async_copy(grad, h_all.at[s, j // 2, half_pair], stored.at[1])
            keep.start()

            def down(i, _):
                partial[s, j, :, columns(i)] = nn(grad[...], wu[:, columns(i)]).astype(BF)
                return 0

            lax.fori_loop(0, c // TILE, down, 0)
            keep.wait()

        def item_place(q):
            s, jj, base = d, q, CHUNKS // 2
            for k in range(1, n):
                to_left, to_right = d - k >= 0, d + k < n
                two = to_left & to_right
                r = q - base
                here = (r >= 0) & (to_left | to_right)
                s = jnp.where(here, jnp.where(to_left & (jnp.logical_not(two) | (lax.rem(r, 2) == 0)), d - k, d + k), s)
                jj = jnp.where(here, jnp.where(two, r // 2, r), jj)
                base = base + (CHUNKS // 2) * (to_left.astype(jnp.int32) + to_right.astype(jnp.int32))
            return s, jj

        def item_copies(q):
            s, jj = item_place(q)
            return (
                pltpu.make_async_copy(x_hbm.at[s, jj], left, stored.at[2]),
                pltpu.make_async_copy(act_hbm.at[s, jj], right, stored.at[3]),
                pltpu.make_async_copy(h_all.at[s, jj], middle, stored.at[4]),
            )

        between = (d > 0) & (d < n - 1)

        def item_of(g):
            q = jnp.where(between, g - items, (g - 3) // 2)
            return q, (q >= 0) & (q < items) & (g >= 3) & (between | (lax.rem(g, 2) == 1))

        def after(g):
            for at, tick in ticks.items():
                pl.when(g == at)(lambda tick=tick: tick_add(*tick))
            last = g - 1 - (n - 1) * (CHUNKS + 1)
            pl.when(last >= 0)(lambda: finish(last))
            q, due_now = item_of(g)

            @pl.when(due_now)
            def _():
                of_x, _, of_h = item_copies(q)
                of_x.wait()
                of_h.wait()

                def tile(i, _):
                    a = columns(i)
                    g_up[a] += tn(left[:, a], middle[...])
                    return 0

                lax.fori_loop(0, c // TILE, tile, 0)

            r = jnp.where(between, q, (g - 4) // 2)

            @pl.when((between & due_now) | (jnp.logical_not(between) & (lax.rem(g, 2) == 0) & (g >= 4) & (r < items)))
            def _():
                s, jj = item_place(r)
                item_copies(r)[1].wait()

                def tile(i, _):
                    a = columns(i)
                    db = gathered[s, pl.ds(2 * jj, 2), :, a].reshape(2 * rows, TILE)
                    g_down[a] += tn(db, right[...])
                    return 0

                lax.fori_loop(0, c // TILE, tile, 0)

            @pl.when(g == 2 * items + 2)
            def _():
                give(g_up, left, out_up, stored.at[2])
                swaps[0].start()

            @pl.when(g == 2 * items + 3)
            def _():
                give(g_down, right, out_down, stored.at[3])
                swaps[1].start()

        core = dp_bit(0)

        def result(j):
            return pltpu.make_async_copy(total, out.at[j], stored.at[5])

        def finish(j):
            pl.when(j > 0)(lambda: result(j - 1).wait())
            own_sum(n, d, j, partial, travel, total)
            result(j).start()

        def rows_at(i):
            return pl.ds(pl.multiple_of(i * piece, piece), piece)

        def give(source, stage, target, sem):
            def one(i, _):
                stage[pl.ds(0, piece)] = source[rows_at(2 * i + 1 - core)].astype(BF)
                copy = pltpu.make_async_copy(stage.at[pl.ds(0, piece)], target.at[i], sem)
                copy.start()
                copy.wait()
                return 0

            lax.fori_loop(0, devices // 2, one, 0)

        def keep_sums():
            sets = ((g_up, left, got_up, g_up_out, 2), (g_down, right, got_down, g_down_out, 3))

            def loads(i):
                return [
                    pltpu.make_async_copy(got.at[i], stage.at[pl.ds(0, piece)], stored.at[sem])
                    for _, stage, got, _, sem in sets
                ]

            def one(i, _):
                for load in loads(i):
                    load.start()
                saves = []
                for load, (source, stage, _, target, sem) in zip(loads(i), sets):
                    load.wait()
                    here = stage.at[pl.ds(0, piece)]
                    here[...] = (source[rows_at(2 * i + core)] + here[...].astype(F32)).astype(BF)
                    saves.append(pltpu.make_async_copy(here, target.at[i], stored.at[sem]))
                    saves[-1].start()
                for save in saves:
                    save.wait()
                return 0

            lax.fori_loop(0, devices // 2, one, 0)

        swaps = [
            pltpu.make_async_remote_copy(
                src_ref=src, dst_ref=dst, send_sem=core_send.at[i], recv_sem=core_recv.at[i],
                device_id={"dp": dp_mate(0)}, device_id_type=MESH,
            )
            for i, (src, dst) in enumerate(((out_up, got_up), (out_down, got_down)))
        ]
        def clear(i, _):
            some = pl.ds(pl.multiple_of(i * TILE, TILE), TILE)
            g_up[some] = jnp.zeros((TILE, h), F32)
            g_down[some] = jnp.zeros((TILE, h), F32)
            return 0

        def begin_all():
            begin()
            lax.fori_loop(0, c // TILE, clear, 0)

        chain_exchange(
            n, CHUNKS, 1, gathered, partial, travel, sems, own_chunk, prepare, arrived, compute,
            [dp_mate(b) for b in range(steps + 1)], begin_all, turn, after, True,
        )
        keep = pltpu.make_async_copy(gathered.at[d], d_own, stored.at[0])
        keep.start()
        result(CHUNKS - 1).wait()
        keep.wait()
        if not ticks:
            for plan in plans:
                pass_on(steps - 1, plan)
        for swap in swaps:
            swap.wait()
        keep_sums()

    whole = pl.BlockSpec(memory_space=pl.ANY)
    local = pl.BlockSpec(memory_space=pltpu.VMEM)
    dma = pltpu.SemaphoreType.DMA
    out, d_own, g_up, g_down, _, _, _, _, _, sums, *_ = pl.pallas_call(
        kernel,
        out_shape=(
            jax.ShapeDtypeStruct((CHUNKS, rows, c), F32),
            jax.ShapeDtypeStruct((CHUNKS, rows, c), BF),
            *[jax.ShapeDtypeStruct((devices // 2, piece, h), BF)] * 6,
            jax.ShapeDtypeStruct((n, CHUNKS // 2, 2 * rows, h), BF),
            jax.ShapeDtypeStruct((2, 1, 1, split, g_cols), BF),
            *extras,
        ),
        in_specs=[local] * 4 + [whole] * 3 + [local] * 2 + [whole] * 2,
        out_specs=(whole,) * (10 + 2 * each),
        scratch_shapes=chunk_buffers(n, rows, c, BF)
        + [
            pltpu.VMEM((rows, h), BF), pltpu.VMEM((rows, h), BF),
            pltpu.VMEM((2 * rows, c), BF), pltpu.VMEM((2 * rows, h), BF), pltpu.VMEM((2 * rows, h), BF),
            pltpu.VMEM((c, h), F32), pltpu.VMEM((c, h), F32),
            pltpu.VMEM((rows, c), F32), pltpu.VMEM((c // LANES, pairs_here * cols, LANES), F32),
            pltpu.VMEM((2, 4, split, plans[0].block), BF),
            dma((2,)), dma((2,)), dma((6,)), dma((3, 4)),
        ]
        + plans[0].semaphores() + plans[1].semaphores()
        + chain_sems(n, CHUNKS),
        compiler_params=pltpu.CompilerParams(
            collective_id=1, has_side_effects=True, vmem_limit_bytes=62 * MIB
        ),
        cost_estimate=pl.CostEstimate(
            flops=8 * n * t * c * h, bytes_accessed=8 * n * t * c, transcendentals=0
        ),
    )(
        cot, d_pooled.reshape(CHUNKS, pairs_here * half, c), share.reshape(CHUNKS, pairs_here * half, 1),
        mask.reshape(CHUNKS, rows, 1), *(v.reshape(n, CHUNKS // 2, 2 * rows, -1) for v in (x_all, act_all)),
        slope_all, up_t, down_t,
        grads.reshape(pairs // 2, 2, g_rows, g_cols), grads.reshape(2, pairs // 2, g_rows, g_cols),
    )
    return (
        out.reshape(cot.shape), d_own.reshape(cot.shape), [g_up, g_down],
        sums.reshape(g_rows, g_cols),
    )


def frame(dst, src):
    rows, cols, _ = src.shape
    dst[:, :EDGE] = jnp.zeros((rows, EDGE, LANES), F32)
    dst[:, EDGE + cols:] = jnp.zeros((rows, EDGE, LANES), F32)
    dst[:, EDGE:EDGE + cols] = src[...].astype(F32)


def correlate(out, framed, taps, size, flip, group, first=0, last=None, every=1):
    rows, cols, _ = out.shape
    reach = size // 2
    def some(k, _):
        r = first + k * every
        acc = jnp.zeros((group, cols, LANES), F32)
        for a in range(size):
            for b in range(size):
                tap = (size - 1 - a) * size + size - 1 - b if flip else a * size + b
                acc = acc + framed[pl.ds(r * group + a, group), pl.ds(EDGE - reach + b, cols), :] * taps[tap]
        out[pl.ds(r * group, group)] = acc
        return 0
    lax.fori_loop(0, (rows // group if last is None else last) - first if every == 1 else 2, some, 0)


def conv_forward(x, w, size, n):
    rows, cols, c = x.shape
    reach = size // 2

    def kernel(x_ref, w_ref, out, bordered, framed, sent, got, own):
        d = lax.axis_index("mp")
        has_up, has_down = d > 0, d < n - 1
        barrier = pltpu.get_barrier_semaphore()

        @pl.when(has_up)
        def _():
            pl.semaphore_signal(barrier, inc=1, device_id={"mp": d - 1}, device_id_type=MESH)

        @pl.when(has_down)
        def _():
            pl.semaphore_signal(barrier, inc=1, device_id={"mp": d + 1}, device_id_type=MESH)

        keep = pltpu.make_async_copy(x_ref, bordered.at[pl.ds(reach, rows)], own)
        keep.start()
        pl.semaphore_wait(barrier, has_up.astype(jnp.int32) + has_down.astype(jnp.int32))
        up = pltpu.make_async_remote_copy(
            src_ref=x_ref.at[pl.ds(0, reach)], dst_ref=bordered.at[pl.ds(reach + rows, reach)],
            send_sem=sent.at[0], recv_sem=got.at[0], device_id={"mp": d - 1}, device_id_type=MESH,
        )
        down = pltpu.make_async_remote_copy(
            src_ref=x_ref.at[pl.ds(rows - reach, reach)], dst_ref=bordered.at[pl.ds(0, reach)],
            send_sem=sent.at[1], recv_sem=got.at[1], device_id={"mp": d + 1}, device_id_type=MESH,
        )
        nothing = jnp.zeros((reach, cols, c), BF)

        @pl.when(has_up)
        def _():
            up.start()

        @pl.when(has_down)
        def _():
            down.start()

        @pl.when(d == 0)
        def _():
            bordered[:reach] = nothing

        @pl.when(d == n - 1)
        def _():
            bordered[reach + rows :] = nothing

        groups = rows // reach

        def inner(i, _):
            lanes = pl.ds(pl.multiple_of(i * LANES, LANES), LANES)
            frame(framed.at[pl.ds(reach, rows)], x_ref.at[:, :, lanes])
            correlate(out.at[:, :, lanes], framed, w_ref.at[:, :, lanes], size, False, reach, 1, groups - 1)
            return 0

        lax.fori_loop(0, c // LANES, inner, 0)
        keep.wait()

        @pl.when(has_up)
        def _():
            down.wait_recv()

        @pl.when(has_down)
        def _():
            up.wait_recv()

        def block(i, _):
            lanes = pl.ds(pl.multiple_of(i * LANES, LANES), LANES)
            frame(framed, bordered.at[:, :, lanes])
            correlate(out.at[:, :, lanes], framed, w_ref.at[:, :, lanes], size, False, reach, 0, None, groups - 1)
            return 0

        lax.fori_loop(0, c // LANES, block, 0)

        @pl.when(has_up)
        def _():
            up.wait_send()

        @pl.when(has_down)
        def _():
            down.wait_send()

    local = pl.BlockSpec(memory_space=pltpu.VMEM)
    dma = pltpu.SemaphoreType.DMA
    return pl.pallas_call(
        kernel,
        out_shape=(
            jax.ShapeDtypeStruct((rows, cols, c), F32),
            jax.ShapeDtypeStruct((rows + 2 * reach, cols, c), BF),
        ),
        in_specs=[local, local],
        out_specs=(local, local),
        scratch_shapes=[pltpu.VMEM((rows + 2 * reach, cols + 2 * EDGE, LANES), F32), dma((2,)), dma((2,)), dma],
        compiler_params=pltpu.CompilerParams(
            collective_id=5, has_side_effects=True, vmem_limit_bytes=40 * MIB
        ),
    )(x, w)


def conv_backward(d_normed, conv_out, gain, mask, bordered, d_map, w, low_gains, size, grads, devices, n):
    rows, cols, c = conv_out.shape
    reach = size // 2
    high = rows + 2 * reach
    group = 4 if rows % 4 == 0 else 1
    bits = range(1, devices.bit_length() - 1)
    steps = len(bits)
    shape = grads[0].shape
    plans = [Halving(bits, [last] * steps, shape, shape[2]) for last in (True, False)]
    each = 2 * steps
    blocks = c // LANES
    taps = size * size
    count = taps + 1 + low_gains.shape[0]
    small = -(-count // devices)
    first_due = blocks + blocks // 3
    begins = {first_due + blocks // 2 * p // (steps - 1): p for p in range(steps - 1)}
    ends = {mark + 1: p for mark, p in begins.items()}
    rounds = {blocks + 10 * blocks // 12: 1}

    def kernel(
        dn, co, gain_ref, mask_ref, w_ref, low_ref, b_hbm, dm_hbm, g0, g1, out, g_all, *rest
    ):
        extra, rest = rest[: 2 * each], rest[2 * each :]
        around, x_around, d_here, dframed, xframed, g_own, here, level, addend, sent, got, own, add_sem = rest[:13]
        ar, halving_sems = rest[13:19], rest[19:]
        plans[0].bind(g0, extra[:each], halving_sems[0], halving_sems[1])
        plans[1].bind(g1, extra[each:], halving_sems[2], halving_sems[3])
        me, d = lax.axis_index("dp"), lax.axis_index("mp")
        has_up, has_down = d > 0, d < n - 1
        barrier = pltpu.get_barrier_semaphore()

        def greet(k, _):
            pl.semaphore_signal(
                barrier, inc=1, device_id={"dp": lax.rem(me + k, devices)}, device_id_type=MESH
            )
            return 0

        lax.fori_loop(1, devices, greet, 0)
        for k in range(1, n):
            pl.semaphore_signal(barrier, inc=1, device_id={"mp": lax.rem(d + k, n)}, device_id_type=MESH)
        load_x = pltpu.make_async_copy(b_hbm, x_around, own.at[0])
        load_d = pltpu.make_async_copy(dm_hbm, d_here, own.at[1])
        load_x.start()
        load_d.start()

        def halving_loads(p, i):
            plan, count = plans[i], plans[i].got[p].shape[0]
            some = pl.ds(0, count)
            return [
                pltpu.make_async_copy(plan.part(p, True), addend.at[0, i, some], add_sem.at[0, i]),
                pltpu.make_async_copy(plan.got[p], addend.at[1, i, some], add_sem.at[1, i]),
            ]

        def halving_save(p, i, k):
            plan = plans[i]
            ways = plan.split(plan.got[p].shape[0], p + 1)
            target = plan.now[p + 1].at[k // ways[1], k % ways[1]]
            return pltpu.make_async_copy(addend.at[0, i, k], target, add_sem.at[2 + i, k])

        def halving_begin(p):
            for i, plan in enumerate(plans):
                plan.copy(p).wait()
                for load in halving_loads(p, i):
                    load.start()

        def halving_end(p):
            for i, plan in enumerate(plans):
                for load in halving_loads(p, i):
                    load.wait()
                for k in range(plan.got[p].shape[0]):
                    addend[0, i, k] = (addend[0, i, k].astype(F32) + addend[1, i, k].astype(F32)).astype(BF)
                    halving_save(p, i, k).start()
            for i, plan in enumerate(plans):
                for k in range(plan.got[p].shape[0]):
                    halving_save(p, i, k).wait()
            if p + 1 < steps:
                for plan in plans:
                    plan.start(p + 1)

        def keep(row, lanes, value):
            g_own[row // small, row % small : row % small + 1, lanes] = value

        pl.semaphore_wait(barrier, devices + n - 2)
        for plan in plans:
            plan.start(0)
        g_own[...] = jnp.zeros(g_own.shape, F32)

        def norm(r, total):
            cells = mask_ref[r]
            back, part = normalise_back(co[r] * cells, gain_ref[...], dn[r])
            around[reach + r] = (back * cells).astype(BF)
            return total + part

        keep(taps, slice(None), lax.fori_loop(0, rows, norm, jnp.zeros((1, c), F32)))
        for i in range(low_gains.shape[0]):
            keep(taps + 1 + i, slice(None), low_ref[i : i + 1])
        up = pltpu.make_async_remote_copy(
            src_ref=around.at[pl.ds(reach, reach)], dst_ref=around.at[pl.ds(reach + rows, reach)],
            send_sem=sent.at[0], recv_sem=got.at[0], device_id={"mp": d - 1}, device_id_type=MESH,
        )
        down = pltpu.make_async_remote_copy(
            src_ref=around.at[pl.ds(rows, reach)], dst_ref=around.at[pl.ds(0, reach)],
            send_sem=sent.at[1], recv_sem=got.at[1], device_id={"mp": d + 1}, device_id_type=MESH,
        )
        nothing = jnp.zeros((reach, cols, c), BF)

        @pl.when(has_up)
        def _():
            up.start()

        @pl.when(has_down)
        def _():
            down.start()

        @pl.when(d == 0)
        def _():
            around[:reach] = nothing

        @pl.when(d == n - 1)
        def _():
            around[reach + rows :] = nothing

        load_x.wait()

        def lanes_of(i):
            return pl.ds(pl.multiple_of(i * LANES, LANES), LANES)

        def kernel_block(i, _):
            lanes = lanes_of(i)
            frame(dframed.at[pl.ds(reach, rows)], around.at[pl.ds(reach, rows), :, lanes])
            frame(xframed, x_around.at[:, :, lanes])
            for a in range(size):
                def some(r, accs):
                    dv = dframed[pl.ds(reach + r * group, group), EDGE : EDGE + cols]
                    new = []
                    for b in range(size):
                        prod = dv * xframed[pl.ds(r * group + a, group), pl.ds(EDGE - reach + b, cols), :]
                        new.append(accs[b] + jnp.sum(prod.reshape(-1, 8, LANES), axis=0))
                    return tuple(new)

                accs = lax.fori_loop(
                    0, rows // group, some, tuple(jnp.zeros((8, LANES), F32) for _ in range(size))
                )
                for b in range(size):
                    keep(a * size + b, lanes, jnp.sum(accs[b], axis=0, keepdims=True))
            return 0

        def input_block(i, _):
            lanes = lanes_of(i)
            frame(dframed, around.at[:, :, lanes])
            correlate(out.at[:, :, lanes], dframed, w_ref.at[:, :, lanes], size, True, group)
            for r in range(rows):
                out[r, :, lanes] = (out[r, :, lanes] + d_here[r, :, lanes].astype(F32)) * mask_ref[r]
            return 0

        def spread(k):
            peer = lax.rem(me + k, devices)
            return pltpu.make_async_remote_copy(
                src_ref=g_own.at[peer], dst_ref=here.at[me], send_sem=ar[0].at[k], recv_sem=ar[1].at[k],
                device_id={"dp": peer}, device_id_type=MESH,
            )

        def across(k):
            return pltpu.make_async_remote_copy(
                src_ref=level.at[d], dst_ref=level.at[d], send_sem=ar[2].at[k], recv_sem=ar[3].at[k],
                device_id={"mp": lax.rem(d + k, n)}, device_id_type=MESH,
            )

        def tell(k):
            return pltpu.make_async_remote_copy(
                src_ref=g_all.at[me], dst_ref=g_all.at[me], send_sem=ar[4].at[k], recv_sem=ar[5].at[k],
                device_id={"dp": lax.rem(me + k, devices)}, device_id_type=MESH,
            )

        def all_of(length, make, act):
            def one(k, _):
                act(make(k))
                return 0

            lax.fori_loop(1, length, one, 0)

        def sum_round(p):
            if p == 0:
                here[me] = g_own[me]
                all_of(devices, spread, lambda x: x.start())
            elif p == 1:
                all_of(devices, spread, lambda x: x.wait())
                level[d] = jnp.sum(here[...], axis=0)
                all_of(n, across, lambda x: x.start())
            elif p == 2:
                all_of(n, across, lambda x: x.wait())
                g_all[me] = jnp.sum(level[...], axis=0)
                all_of(devices, tell, lambda x: x.start())
            else:
                all_of(devices, tell, lambda x: x.wait())

        marks = sorted(set(begins) | set(ends) | set(rounds) | {blocks, 2 * blocks})
        at = 0
        for mark in marks:
            if at < blocks:
                lax.fori_loop(at, min(mark, blocks), kernel_block, 0)
            else:
                lax.fori_loop(at - blocks, mark - blocks, input_block, 0)
            at = mark
            if mark in ends:
                halving_end(ends[mark])
            if mark in begins:
                halving_begin(begins[mark])
            if mark == first_due:
                sum_round(0)
            if mark == blocks:
                load_d.wait()

                @pl.when(has_up)
                def _():
                    down.wait_recv()

                @pl.when(has_down)
                def _():
                    up.wait_recv()
            if mark in rounds:
                sum_round(rounds[mark])
        sum_round(2)
        halving_begin(steps - 1)
        halving_end(steps - 1)
        sum_round(3)

        @pl.when(has_up)
        def _():
            up.wait_send()

        @pl.when(has_down)
        def _():
            down.wait_send()

    whole = pl.BlockSpec(memory_space=pl.ANY)
    local = pl.BlockSpec(memory_space=pltpu.VMEM)
    vm, dma = pltpu.VMEM, pltpu.SemaphoreType.DMA
    d_in, g_all, *extra = pl.pallas_call(
        kernel,
        out_shape=(
            jax.ShapeDtypeStruct((rows, cols, c), F32),
            jax.ShapeDtypeStruct((devices, small, c), F32),
            *plans[0].buffers(),
            *plans[1].buffers(),
        ),
        in_specs=[local] * 6 + [whole] * 4,
        out_specs=(local,) * 2 + (whole,) * (2 * each),
        scratch_shapes=[
            vm((high, cols, c), BF), vm((high, cols, c), BF), vm((rows, cols, c), BF),
            vm((high, cols + 2 * EDGE, LANES), F32), vm((high, cols + 2 * EDGE, LANES), F32),
            vm((devices, small, c), F32), vm((devices, small, c), F32), vm((n, small, c), F32),
            vm((2, 2, shape[0] // 2) + shape[1:], BF),
            dma((2,)), dma((2,)), dma((2,)), dma((4, max(2, shape[0] // 2))),
            dma((devices,)), dma((devices,)), dma((n,)), dma((n,)), dma((devices,)), dma((devices,)),
        ]
        + plans[0].semaphores() + plans[1].semaphores(),
        compiler_params=pltpu.CompilerParams(
            collective_id=3, has_side_effects=True, vmem_limit_bytes=50 * MIB
        ),
        cost_estimate=pl.CostEstimate(flops=6 * 10**10, bytes_accessed=10**8, transcendentals=0),
    )(
        d_normed, conv_out, gain, mask, w, low_gains, bordered, d_map,
        grads[0].reshape((shape[0] // 2, 2) + shape[1:]), grads[1].reshape((2, shape[0] // 2) + shape[1:]),
    )
    sums = g_all.reshape(devices * small, c)[:count]
    return d_in, sums, [extra[each - 1].reshape(shape[1:]), extra[2 * each - 1].reshape(shape[1:])]


GATE, OUT, HIGH_A, HIGH_B, QUERY, KEY, VALUE, PROJ = range(8)
L_LOW, L_DF, L_POOL_A, L_POOL_B, L_FIRST, L_DA, L_SECOND, L_COT = range(8)
R_DGATE, R_MERGE, R_DHIGH, R_DQ, R_DK, R_DV, R_ATT, R_DUP, R_ACT = range(9)


def nn(a, b):
    return jnp.dot(a, b, preferred_element_type=F32)


def nt(a, b):
    return lax.dot_general(a, b, (((1,), (1,)), ((), ())), preferred_element_type=F32)


def tn(a, b):
    return lax.dot_general(a, b, (((0,), (0,)), ((), ())), preferred_element_type=F32)


def normalise(x, gain):
    centred = x - jnp.mean(x, -1, keepdims=True)
    rate = lax.rsqrt(jnp.mean(centred * centred, -1, keepdims=True) + 1e-06)
    return centred * rate * gain


def normalise_back(x, gain, d):
    centred = x - jnp.mean(x, -1, keepdims=True)
    rate = lax.rsqrt(jnp.mean(centred * centred, -1, keepdims=True) + 1e-06)
    hat = centred * rate
    dg = d * gain
    back = rate * (dg - jnp.mean(dg, -1, keepdims=True) - hat * jnp.mean(dg * hat, -1, keepdims=True))
    return back, jnp.sum(d * hat, axis=0, keepdims=True)


def low_stage(low, pooled, cot, gain1, gain2, packed, n, devices, cid):
    t, dim = low.shape
    every = n * t
    width = dim // n
    heads = width // HEAD
    groups = width // LANES
    pairs = devices // 2
    rows = dim // devices
    half = dim // 2
    ff = 4 * dim
    natural = rows % LANES == 0
    high_rows = pooled.shape[1] // devices

    def place_of(k):
        return (k % 2) * half + k // 2 * rows

    def in_order(ref):
        if not natural:
            return ref[...]
        order = sorted(range(devices), key=place_of)
        return jnp.concatenate([ref[:, k * rows : (k + 1) * rows] for k in order], axis=1)

    scale = HEAD ** (-0.5)

    def kernel(
        low_ref, pooled_ref, cot_ref, gain1_ref, gain2_ref, w_hbm,
        low_out, d_low, d_pooled, g_ln1, g_ln2, grads,
        wv, lhs, lhs2, rhs, gate, high, merged, resid, d_res, slope, mixed, heads_in, att_all, d_att, d_mixed,
        d_heads, probs, d_scores, stage, left, w_sem, q_send, q_got, a_send, a_got, b_send, b_got, c_send, c_got, own_sem,
        l_send, l_got, r_send, r_got, stage_sem,
    ):
        d = lax.axis_index("mp")
        dp = lax.axis_index("dp")
        core = lax.rem(dp, 2)
        mate = dp + 1 - 2 * core
        barrier = pltpu.get_barrier_semaphore()
        for k in range(1, n):
            pl.semaphore_signal(barrier, inc=1, device_id={"mp": lax.rem(d + k, n)}, device_id_type=MESH)
        pl.semaphore_signal(barrier, inc=1, device_id={"dp": mate}, device_id_type=MESH)

        def w_copy(w, k):
            c, z = k // n, lax.rem(k, n)
            wide, base, at = w_place(w)
            src = w_hbm.at[:, c, z, :, pl.ds(base, wide)]
            dst = wv.at[c, :, :, pl.ds(pl.multiple_of(at + z * wide, wide), wide)]
            return pltpu.make_async_copy(src, dst, w_sem.at[w, k])

        def w_place(w):
            if w < 8:
                return width, w * width, w * dim
            return ff // n, 8 * width + (w - 8) * ff // n, 8 * dim + (w - 8) * ff

        def w_each(w, act):
            def one(k, _):
                act(w_copy(w, k))
                return 0

            lax.fori_loop(0, 2 * n, one, 0)

        for w in range(10):
            w_each(w, lambda copy: copy.start())

        def w_wait(*which):
            for w in which:
                w_each(w, lambda copy: copy.wait())

        def w_cols(at, size):
            return wv[:, :, :, pl.ds(at, size)].reshape(dim, size)

        def forward(x, first, count, put):
            def one(i, _):
                put(pl.multiple_of(i * TILE, TILE), nn(x, w_cols(pl.multiple_of(first * dim + i * TILE, TILE), TILE)))
                return 0
            lax.fori_loop(0, count * dim // TILE, one, 0)

        def backward(get, first, count, dst, fresh):
            def one(i, _):
                for c in range(2):
                    part = wv[c, :, :, pl.ds(pl.multiple_of((first + i) * dim, dim), dim)].reshape(half, dim)
                    y = nt(get(pl.multiple_of(i * dim, dim)), part)
                    cols = slice(c * half, (c + 1) * half)
                    if fresh and count == 1:
                        dst[:, cols] = y
                    else:
                        dst[:, cols] += y
                return 0
            if fresh and count > 1:
                dst[...] = jnp.zeros(dst.shape, F32)
            if count == 1:
                one(0, 0)
            else:
                lax.fori_loop(0, count, one, 0)

        def r_cols(block, count=1):
            return pl.ds(block * dim, count * dim)

        def r_at(block):
            return block * dim if block <= R_DUP else block * dim + 3 * dim

        def r_copy(block):
            cols = pl.ds(r_at(block), dim if block < R_DUP else ff)
            return pltpu.make_async_remote_copy(
                src_ref=rhs.at[0, :, cols], dst_ref=rhs.at[1, :, cols], send_sem=r_send.at[block],
                recv_sem=r_got.at[block], device_id={"dp": mate}, device_id_type=MESH)

        def l_copy(i):
            return pltpu.make_async_remote_copy(
                src_ref=lhs.at[i, :, pl.ds(pl.multiple_of((1 - core) * half, half), half)], dst_ref=lhs2.at[i],
                send_sem=l_send.at[i], recv_sem=l_got.at[i], device_id={"dp": mate}, device_id_type=MESH)

        stored = []
        turned = [None]

        def put_natural(dst, value):
            if natural:
                for k in range(devices):
                    dst[:, k * rows : (k + 1) * rows] = value[:, place_of(k) : place_of(k) + rows]
            else:
                dst[...] = value

        def grad(i, block, at, count, shared=False):
            if not shared:
                r_copy(block).wait_recv()
            if turned[0] != i:
                left[0] = lhs[i, :, pl.ds(pl.multiple_of(core * half, half), half)].T
                left[1] = lhs2[i].T
                turned[0] = i

            wide, base, first = w_place(at if at < 8 else 8 + (at - 8) * dim // ff)
            piece = min(TILE, wide)

            def out_copies(slot, k):
                out = []
                for q in range(TILE // piece):
                    z, col = divmod(at * dim - first + k * TILE + q * piece, wide)
                    out.append(
                        pltpu.make_async_copy(
                            stage.at[slot, :, :, pl.ds(q * piece, piece)],
                            grads.at[:, pl.ds(z * rows, rows), pl.ds(base + col, piece)],
                            stage_sem.at[slot, q],
                        )
                    )
                return out

            for k in range(count * dim // TILE):
                slot = len(stored) % 2
                if len(stored) >= 2:
                    wait(stored[-2])
                cols = pl.ds(r_at(block) + k * TILE, TILE)
                y = nn(left[0], rhs[0, :, cols]) + nn(left[1], rhs[1, :, cols])
                stage[slot] = y.astype(BF).reshape(pairs, rows, TILE)
                stored.append(out_copies(slot, k))
                start(stored[-1])

        def to_heads(k, src, dst, send, got):
            out = []
            for step in range(1, n):
                peer = lax.rem(d + step, n)
                out.append(pltpu.make_async_remote_copy(
                    src_ref=src.at[:, pl.ds(pl.multiple_of(peer * width, width), width)],
                    dst_ref=dst.at[pl.ds(pl.multiple_of(d * t, t), t)],
                    send_sem=send.at[k, step], recv_sem=got.at[k, step], device_id={"mp": peer}, device_id_type=MESH))
            out.append(pltpu.make_async_copy(
                src.at[:, pl.ds(pl.multiple_of(d * width, width), width)], dst.at[pl.ds(pl.multiple_of(d * t, t), t)], own_sem.at[k]))
            return out

        def to_tokens(k, src, dst, send, got, group):
            out = []
            slot = k * groups + group
            lanes = pl.ds(group * LANES, LANES)
            there = pl.ds(pl.multiple_of(d * width + group * LANES, LANES), LANES)
            for step in range(1, n):
                peer = lax.rem(d + step, n)
                out.append(pltpu.make_async_remote_copy(
                    src_ref=src.at[pl.ds(pl.multiple_of(peer * t, t), t), lanes], dst_ref=dst.at[:, there],
                    send_sem=send.at[slot, step], recv_sem=got.at[slot, step], device_id={"mp": peer}, device_id_type=MESH))
            out.append(pltpu.make_async_copy(
                src.at[pl.ds(pl.multiple_of(d * t, t), t), lanes], dst.at[:, there], own_sem.at[slot]))
            return out

        def start(copies):
            for c in copies:
                c.start()

        def wait(copies):
            for c in copies:
                c.wait()

        gain1_here, gain2_here = in_order(gain1_ref), in_order(gain2_ref)
        if natural:
            for i, ref in ((L_LOW, low_ref), (L_COT, cot_ref)):
                for k in range(devices):
                    lhs[i, :, place_of(k) : place_of(k) + rows] = ref[:, k * rows : (k + 1) * rows]
            for k in range(devices):
                own = slice(place_of(k), place_of(k) + rows)
                lhs[L_POOL_A, :, own] = pooled_ref[:, k * high_rows : k * high_rows + rows].astype(BF)
                more = pooled_ref[:, k * high_rows + rows : (k + 1) * high_rows].astype(BF)
                lhs[L_POOL_B, :, own] = jnp.concatenate([more, jnp.zeros((t, 2 * rows - high_rows), BF)], axis=1)
        else:
            lhs[L_LOW] = low_ref[...]
            lhs[L_COT] = cot_ref[...]
            lhs[L_POOL_A] = pooled_ref[:, :dim].astype(BF)
            lhs[L_POOL_B] = pooled_ref[:, dim:].astype(BF)
        acc = d_low
        w_wait(GATE)

        def put_gate(at, y):
            gate[:, pl.ds(at, TILE)] = 1.0 / (1.0 + jnp.exp(-y))
        forward(lhs[L_LOW], GATE, 1, put_gate)
        w_wait(HIGH_A, HIGH_B, OUT)

        def put_high(at, y):
            high[:, pl.ds(at, TILE)] = y
        forward(lhs[L_POOL_A], HIGH_A, 1, put_high)

        def put_merging(at, y):
            cols = pl.ds(at, TILE)
            total = high[:, cols] + y
            high[:, cols] = total
            rhs[0, :, pl.ds(R_MERGE * dim + at, TILE)] = (total * gate[:, cols]).astype(BF)
        forward(lhs[L_POOL_B], HIGH_B, 1, put_merging)
        backward(lambda at: rhs[0, :, r_cols(R_MERGE)], OUT, 1, merged, True)
        merged[...] += lhs[L_LOW].astype(F32)
        lhs[L_FIRST] = normalise(merged[...], gain1_here).astype(BF)

        w_wait(QUERY, KEY, VALUE, PROJ)
        pl.semaphore_wait(barrier, n)
        for i in (L_LOW, L_POOL_A, L_POOL_B, L_COT, L_FIRST):
            l_copy(i).start()
        r_copy(R_MERGE).start()
        out_q = []
        for k in range(3):
            def put_mixed(at, y):
                mixed[k, :, pl.ds(at, TILE)] = y.astype(BF)
            forward(lhs[L_FIRST], QUERY + k, 1, put_mixed)
            copies = to_heads(k, mixed.at[k], heads_in.at[k], q_send, q_got)
            start(copies)
            out_q.append(copies)
        wait(out_q[0] + out_q[1])

        for h in range(heads):
            lanes = slice(h * HEAD, (h + 1) * HEAD)

            def rows_of(b, _):
                some = pl.ds(pl.multiple_of(b * t, t), t)
                s = nt(heads_in[0, some, lanes], heads_in[1, :, lanes]) * scale
                e = jnp.exp(s - jnp.max(s, -1, keepdims=True))
                p = (e * (1.0 / jnp.sum(e, -1, keepdims=True))).astype(BF)
                probs[h, some] = p
                return 0
            lax.fori_loop(0, n, rows_of, 0)
        wait(out_q[2])
        out_a = []
        for h in range(heads):
            lanes = slice(h * HEAD, (h + 1) * HEAD)

            def attend(b, _):
                some = pl.ds(pl.multiple_of(b * t, t), t)
                att_all[some, lanes] = nn(probs[h, some], heads_in[2, :, lanes]).astype(BF)
                return 0
            lax.fori_loop(0, n, attend, 0)
            if (h + 1) * HEAD % LANES == 0:
                copies = to_tokens(0, att_all, rhs.at[0, :, r_cols(R_ATT)], a_send, a_got, h * HEAD // LANES)
                start(copies)
                out_a += copies
        wait(out_a)
        r_copy(R_ATT).start()
        backward(lambda at: rhs[0, :, r_cols(R_ATT)], PROJ, 1, resid, True)
        resid[...] += merged[...]
        lhs[L_SECOND] = normalise(resid[...], gain2_here).astype(BF)
        l_copy(L_SECOND).start()

        w_wait(8)

        def put_up(at, y):
            value, rate = gelu_parts(y)
            rhs[0, :, pl.ds(r_at(R_ACT) + at, TILE)] = value.astype(BF)
            slope[:, pl.ds(at, TILE)] = rate.astype(BF)
        forward(lhs[L_SECOND], 8, 4, put_up)
        r_copy(R_ACT).start()
        w_wait(9)
        backward(lambda at: rhs[0, :, pl.ds(r_at(R_ACT) + at, dim)], 12, 4, acc, True)
        put_natural(low_out, resid[...] + acc[...])

        def put_d_up(at, y):
            rhs[0, :, pl.ds(r_at(R_DUP) + at, TILE)] = (y * slope[:, pl.ds(at, TILE)].astype(F32)).astype(BF)
        forward(lhs[L_COT], 12, 4, put_d_up)
        r_copy(R_DUP).start()
        backward(lambda at: rhs[0, :, pl.ds(r_at(R_DUP) + at, dim)], 8, 4, acc, True)
        back, g = normalise_back(resid[...], gain2_here, acc[...])
        put_natural(g_ln2, g)
        d_res[...] = lhs[L_COT].astype(F32) + back
        lhs[L_DA] = d_res[...].astype(BF)
        l_copy(L_DA).start()

        def put_d_att(at, y):
            mixed[0, :, pl.ds(at, TILE)] = y.astype(BF)
        forward(lhs[L_DA], PROJ, 1, put_d_att)
        out_b = to_heads(0, mixed.at[0], d_att, b_send, b_got)
        start(out_b)
        l_copy(L_COT).wait_recv()
        grad(L_COT, R_ACT, 12, 4)
        wait(out_b)
        out_c = []

        def send_back(k, h):
            if (h + 1) * HEAD % LANES == 0:
                copies = to_tokens(k, d_heads.at[k], rhs.at[0, :, r_cols(R_DQ + k)], c_send, c_got, h * HEAD // LANES)
                start(copies)
                out_c.extend(copies)

        for h in range(heads):
            lanes = slice(h * HEAD, (h + 1) * HEAD)
            d_heads[2, :, lanes] = tn(probs[h], d_att[:, lanes]).astype(BF)
            send_back(2, h)
        for h in range(heads):
            lanes = slice(h * HEAD, (h + 1) * HEAD)

            def rows_of(b, _):
                some = pl.ds(pl.multiple_of(b * t, t), t)
                p = probs[h, some].astype(F32)
                dp_ = nt(d_att[some, lanes], heads_in[2, :, lanes])
                ds = (p * (dp_ - jnp.sum(dp_ * p, -1, keepdims=True)) * scale).astype(BF)
                d_scores[some] = ds
                d_heads[0, some, lanes] = nn(ds, heads_in[1, :, lanes]).astype(BF)
                return 0
            lax.fori_loop(0, n, rows_of, 0)
            d_heads[1, :, lanes] = tn(d_scores[...], heads_in[0, :, lanes]).astype(BF)
            send_back(0, h)
            send_back(1, h)
        l_copy(L_SECOND).wait_recv()
        grad(L_SECOND, R_DUP, 8, 4)
        l_copy(L_DA).wait_recv()
        grad(L_DA, R_ATT, PROJ, 1)
        wait(out_c)
        for k in range(3):
            r_copy(R_DQ + k).start()
        backward(lambda at: rhs[0, :, pl.ds(R_DQ * dim + at, dim)], QUERY, 3, acc, True)
        back, g = normalise_back(merged[...], gain1_here, acc[...])
        put_natural(g_ln1, g)
        d_res[...] += back
        lhs[L_DF] = d_res[...].astype(BF)
        l_copy(L_DF).start()

        def put_d_gate(at, y):
            cols = pl.ds(at, TILE)
            gv = gate[:, cols]
            part = y * gv
            rhs[0, :, pl.ds(R_DHIGH * dim + at, TILE)] = part.astype(BF)
            rhs[0, :, pl.ds(R_DGATE * dim + at, TILE)] = (part * high[:, cols] * (1.0 - gv)).astype(BF)
        forward(lhs[L_DF], OUT, 1, put_d_gate)
        r_copy(R_DHIGH).start()
        r_copy(R_DGATE).start()
        backward(lambda at: rhs[0, :, r_cols(R_DHIGH)], HIGH_A, 1, gate, True)
        backward(lambda at: rhs[0, :, r_cols(R_DHIGH)], HIGH_B, 1, high, True)
        if natural:
            for k in range(devices):
                at = place_of(k)
                d_pooled[:, k * high_rows : k * high_rows + rows] = gate[:, at : at + rows]
                d_pooled[:, k * high_rows + rows : (k + 1) * high_rows] = high[:, at : at + high_rows - rows]
        else:
            d_pooled[:, :dim] = gate[...]
            d_pooled[:, dim:] = high[...]
        backward(lambda at: rhs[0, :, r_cols(R_DGATE)], GATE, 1, acc, True)
        put_natural(d_low, d_res[...] + acc[...])
        l_copy(L_FIRST).wait_recv()
        for k in range(3):
            grad(L_FIRST, R_DQ + k, QUERY + k, 1)
        l_copy(L_DF).wait_recv()
        grad(L_DF, R_MERGE, OUT, 1)
        l_copy(L_POOL_A).wait_recv()
        grad(L_POOL_A, R_DHIGH, HIGH_A, 1)
        l_copy(L_POOL_B).wait_recv()
        grad(L_POOL_B, R_DHIGH, HIGH_B, 1, shared=True)
        l_copy(L_LOW).wait_recv()
        grad(L_LOW, R_DGATE, GATE, 1)
        wait(stored[-2])
        wait(stored[-1])
        for i in range(8):
            l_copy(i).wait_send()
        for b in range(9):
            r_copy(b).wait_send()

    whole = pl.BlockSpec(memory_space=pl.ANY)
    local = pl.BlockSpec(memory_space=pltpu.VMEM)
    vm, dma = pltpu.VMEM, pltpu.SemaphoreType.DMA
    tok = jax.ShapeDtypeStruct((t, dim), F32)
    one = jax.ShapeDtypeStruct((1, dim), F32)
    return pl.pallas_call(
        kernel,
        out_shape=(tok, tok, jax.ShapeDtypeStruct(pooled.shape, F32), one, one, jax.ShapeDtypeStruct((pairs, n * rows, 16 * width), BF)),
        in_specs=[local] * 5 + [whole],
        out_specs=(local,) * 5 + (whole,),
        scratch_shapes=[
            vm((2, pairs, rows, 16 * dim), BF), vm((8, t, dim), BF), vm((8, t, half), BF), vm((2, t, 15 * dim), BF),
            vm((t, dim), F32), vm((t, dim), F32), vm((t, dim), F32), vm((t, dim), F32), vm((t, dim), F32),
            vm((t, ff), BF), vm((3, t, dim), BF), vm((3, every, width), BF), vm((every, width), BF), vm((every, width), BF),
            vm((1, 8, 128), BF), vm((3, every, width), BF), vm((heads, every, every), BF), vm((every, every), BF),
            vm((2, pairs, rows, TILE), BF), vm((2, half, t), BF),
            dma((10, 2 * n)), dma((3, n)), dma((3, n)), dma((groups, n)), dma((groups, n)), dma((1, n)), dma((1, n)),
            dma((3 * groups, n)), dma((3 * groups, n)), dma((3 * groups,)), dma((8,)), dma((8,)), dma((9,)), dma((9,)), dma((2, 2)),
        ],
        compiler_params=pltpu.CompilerParams(collective_id=cid, has_side_effects=True, vmem_limit_bytes=62 * MIB),
        cost_estimate=pl.CostEstimate(flops=14 * 10**9, bytes_accessed=70 * 10**6, transcendentals=10**7),
    )(low, pooled, cot, gain1, gain2, packed.reshape(pairs, 2, n, rows, 16 * width))
def low_outputs(own, widths, high_rows):
    share = own.shape[0]
    width, wide = widths[0], widths[-1]

    def kernel(x, gate, high, out, qkv, proj, up, down):
        def part(i, size=width):
            at = sum(widths[:i])
            return x[:, at : at + size].astype(F32)

        gate[...] = part(0)
        out[...] = part(1).T
        high[:share] = part(2)
        high[share:] = part(3)[: high_rows - share]
        for k in range(3):
            qkv[k] = part(4 + k)
        proj[...] = part(7).T
        up[...] = part(8, wide)
        down[...] = part(9, wide).T

    local = pl.BlockSpec(memory_space=pltpu.VMEM)
    shapes = [
        (share, width), (high_rows, width), (width, share), (3, share, width), (width, share), (share, wide), (wide, share),
    ]
    return pl.pallas_call(
        kernel,
        out_shape=[jax.ShapeDtypeStruct(s, F32) for s in shapes],
        in_specs=[local],
        out_specs=[local] * 7,
        compiler_params=pltpu.CompilerParams(vmem_limit_bytes=32 * MIB),
    )(own)


def map_outputs(g_up, g_down, others):
    count = len(others)

    def kernel(up, down, *rest):
        sources, o_up, o_down = rest[:count], rest[count], rest[count + 1]
        targets, held, sems = rest[count + 2 : 2 * count + 2], rest[2 * count + 2 : -1], rest[-1]
        loads = [pltpu.make_async_copy(a, b, sems.at[0, i]) for i, (a, b) in enumerate(zip(sources, held))]
        saves = [pltpu.make_async_copy(a, b, sems.at[1, i]) for i, (a, b) in enumerate(zip(held, targets))]
        for load in loads:
            load.start()
        o_up[...] = up[...].astype(F32)
        o_down[...] = down[...].astype(F32)
        for load, save in zip(loads, saves):
            load.wait()
            save.start()
        for save in saves:
            save.wait()

    whole = pl.BlockSpec(memory_space=pl.ANY)
    local = pl.BlockSpec(memory_space=pltpu.VMEM)
    return pl.pallas_call(
        kernel,
        out_shape=[jax.ShapeDtypeStruct(x.shape, F32) for x in (g_up, g_down, *others)],
        in_specs=[local] * 2 + [whole] * count,
        out_specs=[local] * 2 + [whole] * count,
        scratch_shapes=[pltpu.VMEM(o.shape, o.dtype) for o in others] + [pltpu.SemaphoreType.DMA((2, count))],
        compiler_params=pltpu.CompilerParams(vmem_limit_bytes=60 * MIB),
        cost_estimate=pl.CostEstimate(flops=10**9, bytes_accessed=24 * 10**6, transcendentals=0),
    )(g_up, g_down, *others)


def pack_weights(ad_gate, ad_out, ad_high, w_qkv, w_proj, w_up, w_down, devices):
    dim, width = ad_gate.shape
    share, high_rows, wide = dim // devices, ad_high.shape[0] // devices, w_up.shape[1]
    rest = high_rows - share

    def kernel(gate, out, high, qkv, proj, up, down, packed, side, side_wide, sems):
        me = lax.axis_index("dp")
        mine = pl.ds(pl.multiple_of(me * share, share), share)
        lanes = mine

        def at(i, size=width):
            return packed.at[:, pl.ds(i * width, size)]

        straight = [(gate.at[mine], at(0)), (up.at[mine], at(8, wide))]
        straight += [(qkv.at[k, mine], at(4 + k)) for k in range(3)]
        straight.append((high.at[pl.ds(pl.multiple_of(me * high_rows, rest), share)], at(2)))
        straight.append((high.at[pl.ds(pl.multiple_of(me * high_rows + share, rest), rest)], at(3).at[pl.ds(0, rest)]))
        straight += [(out.at[:, lanes], side.at[0]), (proj.at[:, lanes], side.at[1]), (down.at[:, lanes], side_wide)]
        copies = [pltpu.make_async_copy(a, b, sems.at[i]) for i, (a, b) in enumerate(straight)]
        for copy in copies:
            copy.start()
        packed[rest:, 3 * width : 4 * width] = jnp.zeros((share - rest, width), BF)
        for copy in copies:
            copy.wait()
        packed[:, width : 2 * width] = side[0].T
        packed[:, 7 * width : 8 * width] = side[1].T
        packed[:, 8 * width + wide :] = side_wide[...].T

    whole = pl.BlockSpec(memory_space=pl.ANY)
    return pl.pallas_call(
        kernel,
        out_shape=jax.ShapeDtypeStruct((share, 8 * width + 2 * wide), BF),
        in_specs=[whole] * 7,
        out_specs=pl.BlockSpec(memory_space=pltpu.VMEM),
        scratch_shapes=[
            pltpu.VMEM((2, width, share), BF), pltpu.VMEM((wide, share), BF), pltpu.SemaphoreType.DMA((10,)),
        ],
        compiler_params=pltpu.CompilerParams(vmem_limit_bytes=60 * MIB),
    )(ad_gate, ad_out, ad_high, w_qkv, w_proj, w_up, w_down)


def rows_first(x):
    return with_layout_constraint(x, Layout(major_to_minor=tuple(range(x.ndim))))


def own_part(w, axis):
    length = w.shape[axis] // lax.axis_size("dp")
    return lax.dynamic_slice_in_dim(w, lax.axis_index("dp") * length, length, axis)


def fold(w, rows):
    return w[:rows], jnp.pad(w[rows:], ((0, 2 * rows - w.shape[0]), (0, 0)))


def core_first(x, devices):
    shape = x.shape
    return x.reshape(shape[:-1] + (devices // 2, 2, -1)).swapaxes(-3, -2).reshape(shape)


def core_last(x, devices):
    shape = x.shape
    return x.reshape(shape[:-1] + (2, devices // 2, -1)).swapaxes(-3, -2).reshape(shape)


def layer_norm(values, gain):
    centre = jnp.mean(values, -1, keepdims=True)
    centred = values - centre
    variance = jnp.mean(centred * centred, -1, keepdims=True)
    return centred * lax.rsqrt(variance + 1e-06) * gain


def per_device(
    hr_in,
    low_in,
    valid,
    conv_w,
    hr_gain,
    cn_up,
    cn_down,
    ad_gate,
    ad_high,
    ad_out,
    ln1_gain,
    w_qkv,
    w_proj,
    ln2_gain,
    w_up,
    w_down,
    cot_low,
    cot_hr,
):
    _, row_count, col_count, chan_count = hr_in.shape
    devices, shards = lax.axis_size("dp"), lax.axis_size("mp")
    dims = low_in.shape[2]
    share = dims // devices
    qkv = own_part(w_qkv, 1)
    low_weights = (ad_gate, ad_out, ad_high, w_qkv, w_proj, w_up, w_down)
    pieces = [
        own_part(ad_gate, 0), own_part(ad_out, 1).T, *fold(own_part(ad_high, 0), share),
        qkv[0], qkv[1], qkv[2], own_part(w_proj, 1).T, own_part(w_up, 0), own_part(w_down, 1).T,
    ]
    if share % LANES:
        packed = rows_first(jnp.concatenate(pieces, axis=1))
    else:
        packed = pack_weights(*low_weights, devices)
    packed = rows_first(lax.all_gather(packed, "mp", axis=0, tiled=True))
    plane_mask = valid[0].astype(F32)
    cell_mask = plane_mask[..., None]
    masked = hr_in[0] * valid[0].astype(BF)[..., None]
    half_rows, half_cols = (row_count // 2, col_count // 2)
    counts = plane_mask.reshape(half_rows, 2, half_cols, 2).sum(axis=(1, 3))
    shares = 1.0 / jnp.maximum(counts, 1.0)
    size = conv_w.shape[0]
    taps = conv_w.astype(F32).reshape(size * size, 1, chan_count)
    conv_out, bordered = conv_forward(masked, taps, size, shards)
    hr_gainf = hr_gain.astype(F32)
    normed = layer_norm(conv_out * cell_mask, hr_gainf).astype(BF)
    normed, packed = lax.optimization_barrier((normed, packed))
    packed = rows_first(lax.all_gather(packed, "dp", axis=0, tiled=True))
    hr_out, pooled, normed_all, hidden_act, hidden_slope, up_t, down_t = big_forward(
        normed.reshape(row_count * col_count, chan_count), cn_up, cn_down, masked, plane_mask, shares, shards
    )
    hr_out = hr_out.reshape(hr_in.shape)
    tokens = half_rows * half_cols
    low_ins, gains = [low_in[0], pooled, cot_low[0]], [ln1_gain.astype(F32)[None], ln2_gain.astype(F32)[None]]
    if share % LANES:
        by_share = pooled.reshape(tokens, devices, -1)
        pool_a = by_share[:, :, :share].reshape(tokens, dims)
        pool_b = by_share[:, :, share:]
        pool_b = jnp.pad(pool_b, ((0, 0), (0, 0), (0, share - pool_b.shape[2]))).reshape(tokens, dims)
        low_ins = [core_first(low_in[0], devices), None, core_first(cot_low[0], devices)]
        low_ins[1] = jnp.concatenate([core_first(pool_a, devices), core_first(pool_b, devices)], axis=1)
        gains = [core_first(g, devices) for g in gains]
    low_out, d_low_in, d_pooled, g_ln1, g_ln2, low_grads = low_stage(*low_ins, *gains, packed, shards, devices, 2)
    if share % LANES:
        low_out, d_low_in = core_last(low_out, devices), core_last(d_low_in, devices)
        g_ln1, g_ln2 = core_last(g_ln1, devices), core_last(g_ln2, devices)
        d_pooled = jnp.concatenate(
            [
                core_last(d_pooled[:, :dims], devices).reshape(tokens, devices, share),
                core_last(d_pooled[:, dims:], devices).reshape(tokens, devices, share)[:, :, : by_share.shape[2] - share],
            ],
            axis=2,
        ).reshape(tokens, chan_count)
    low_out, d_low_in, g_ln1, g_ln2 = low_out[None], d_low_in[None], g_ln1[0], g_ln2[0]
    d_normed, d_map, cn_grads, low_sums = big_backward(
        cot_hr[0], d_pooled, shares, plane_mask, normed_all, hidden_act, hidden_slope,
        up_t, down_t, low_grads, shards, devices,
    )
    low_sums = rows_first(low_sums.reshape(shards, share, -1))
    low_sums = rows_first(lax.psum_scatter(low_sums, "mp", scatter_dimension=0))
    low_gains = jnp.pad(jnp.stack([g_ln1, g_ln2]), ((0, 0), (0, chan_count - dims)))
    d_hr_in, small_sums, (g_cn_up, g_cn_down) = conv_backward(
        d_normed, conv_out, hr_gainf[None], cell_mask, bordered, d_map, taps, low_gains, size, cn_grads, devices, shards
    )
    d_hr_in = d_hr_in[None]
    g_conv = small_sums[: size * size].reshape(conv_w.shape)
    g_hr_gain, g_ln1, g_ln2 = small_sums[size * size], small_sums[-2, :dims], small_sums[-1, :dims]
    g_cn_up, g_cn_down, low_out, hr_out, d_low_in, d_hr_in = map_outputs(
        g_cn_up, g_cn_down, (low_out, hr_out, d_low_in, d_hr_in)
    )
    g_ad_gate, g_ad_high, g_ad_out, g_qkv, g_proj, g_up, g_down = low_outputs(
        low_sums.reshape(share, -1), [p.shape[1] for p in pieces], ad_high.shape[0] // devices
    )
    g_cn_down = g_cn_down.T
    return (
        low_out,
        hr_out,
        d_low_in,
        d_hr_in,
        g_conv,
        g_hr_gain,
        g_cn_up,
        g_cn_down,
        g_ad_gate,
        g_ad_high,
        g_ad_out,
        g_ln1,
        g_qkv,
        g_proj,
        g_ln2,
        g_up,
        g_down,
    )


def solution(mesh):
    return jax.shard_map(
        per_device,
        mesh=mesh,
        in_specs=(
            P("dp", "mp", None, None),
            P("dp", "mp", None),
            P("dp", "mp", None),
            P(),
            P(),
            P(None, "mp"),
            P("mp", None),
            P(None, "mp"),
            P(None, "mp"),
            P("mp", None),
            P(),
            P(None, None, "mp"),
            P("mp", None),
            P(),
            P(None, "mp"),
            P("mp", None),
            P("dp", "mp", None),
            P("dp", "mp", None, None),
        ),
        out_specs=(
            P("dp", "mp", None),
            P("dp", "mp", None, None),
            P("dp", "mp", None),
            P("dp", "mp", None, None),
            P(),
            P(),
            P("dp", "mp"),
            P("mp", "dp"),
            P("dp", "mp"),
            P("dp", "mp"),
            P("mp", "dp"),
            P(),
            P(None, "dp", "mp"),
            P("mp", "dp"),
            P(),
            P("dp", "mp"),
            P("mp", "dp"),
        ),
        check_vma=False,
    )
```

```python
import jax
import jax.numpy as jnp
from jax import lax
from jax.experimental.layout import Layout, with_layout_constraint
from jax.experimental import pallas as pl
from jax.experimental.pallas import tpu as pltpu
from jax.sharding import PartitionSpec as P

HEAD = 64
LANES = 128
EDGE = 8
CHUNKS = 6
TILE = 512
MIB = 1024 * 1024
MESH = pl.DeviceIdType.MESH
BF = jnp.bfloat16
F32 = jnp.float32

def gelu_parts(x):
    c = 0.7978845608028654
    x2 = x * x
    t = jnp.tanh(c * x * (1.0 + 0.044715 * x2))
    half = 0.5 * (1.0 + t)
    slope = half + 0.5 * x * (1.0 - t * t) * (c * (1.0 + 3 * 0.044715 * x2))
    return x * half, slope


def gelu(x):
    c = 0.7978845608028654
    t = jnp.tanh(c * x * (1.0 + 0.044715 * (x * x)))
    return 0.5 * x * (1.0 + t)


def dp_bit(position):
    return lax.rem(lax.axis_index("dp") // 2**position, 2)


def dp_mate(position):
    return lax.axis_index("dp") + 2**position * (1 - 2 * dp_bit(position))


class Halving:
    def __init__(self, bits, lasts, shape, block):
        self.lasts, self.shape, self.block = lasts, shape, block
        left = list(bits)
        self.bits = [left.pop(0 if last else -1) for last in lasts]

    def split(self, count, p):
        if count == 1:
            return (1, 1)
        return (count // 2, 2) if self.lasts[p] else (2, count // 2)

    def buffers(self):
        count, rows, cols = self.shape
        got, held = [], []
        for p in range(len(self.bits)):
            count //= 2
            got.append(jax.ShapeDtypeStruct((count, rows, cols), BF))
            held.append(jax.ShapeDtypeStruct(self.split(count, p + 1) + (rows, cols), BF))
        return got + held

    def semaphores(self):
        return [pltpu.SemaphoreType.DMA((len(self.bits),))] * 2

    def bind(self, first, buffers, send, recv):
        steps = len(self.bits)
        self.now = [first] + list(buffers[steps:])
        self.got, self.send, self.recv = buffers[:steps], send, recv

    def part(self, p, mine):
        bit = dp_bit(self.bits[p])
        index = bit if mine else 1 - bit
        return self.now[p].at[:, index] if self.lasts[p] else self.now[p].at[index]

    def copy(self, p):
        return pltpu.make_async_remote_copy(
            src_ref=self.part(p, False), dst_ref=self.got[p], send_sem=self.send.at[p], recv_sem=self.recv.at[p],
            device_id={"dp": dp_mate(self.bits[p])}, device_id_type=MESH,
        )

    def start(self, p):
        self.copy(p).start()

    def finish(self, p, wait=True):
        if wait:
            self.copy(p).wait()
        count, rows, cols = self.got[p].shape
        ways = self.split(count, p + 1)

        def add(a, b, out):
            out[...] = (a[...].astype(F32) + b[...].astype(F32)).astype(BF).reshape(out.shape)

        flat = pl.BlockSpec((1, rows, self.block), lambda k, c: (k, 0, c))
        paired = pl.BlockSpec((1, 1, rows, self.block), lambda k, c: (k // ways[1], lax.rem(k, ways[1]), 0, c))
        pltpu.emit_pipeline(add, grid=(count, cols // self.block), in_specs=[flat, flat], out_specs=[paired])(
            self.part(p, True), self.got[p], self.now[p + 1]
        )


def chain_exchange(
    n, chunks, lag, gathered, partial, travel, sems, own_chunk, prepare, arrived, compute, mates=(), begin=None, turn=None, after=None, early=False
):
    ag_send, ag_recv, rs_send, rs_recv = sems
    d = lax.axis_index("mp")
    has_left, has_right = d > 0, d < n - 1

    barrier = pltpu.get_barrier_semaphore()

    @pl.when(has_left)
    def _():
        pl.semaphore_signal(barrier, inc=1, device_id={"mp": d - 1}, device_id_type=MESH)

    @pl.when(has_right)
    def _():
        pl.semaphore_signal(barrier, inc=1, device_id={"mp": d + 1}, device_id_type=MESH)

    for mate in mates:
        pl.semaphore_signal(barrier, inc=1, device_id={"dp": mate}, device_id_type=MESH)

    own_chunk(0)
    pl.semaphore_wait(barrier, has_left.astype(jnp.int32) + has_right.astype(jnp.int32) + len(mates))
    if begin is not None:
        begin()

    def ag(way, s, j):
        return pltpu.make_async_remote_copy(
            src_ref=gathered.at[s, j], dst_ref=gathered.at[s, j],
            send_sem=ag_send.at[way, s, j], recv_sem=ag_recv.at[s, j],
            device_id={"mp": d + 1 - 2 * way}, device_id_type=MESH,
        )

    def rs(way, s, j):
        there = d + 1 - 2 * way
        slot = jnp.where((s == there) & (way == 0), n, s)
        return pltpu.make_async_remote_copy(
            src_ref=travel.at[s, j], dst_ref=travel.at[slot, j],
            send_sem=rs_send.at[s, j], recv_sem=rs_recv.at[slot, j],
            device_id={"mp": there}, device_id_type=MESH,
        )

    def rs_wait(slot, j):
        pltpu.make_async_copy(travel.at[slot, j], travel.at[slot, j], rs_recv.at[slot, j]).wait()

    def first(j, _):
        @pl.when(j > 0)
        def _():
            own_chunk(j)

        @pl.when(has_right)
        def _():
            ag(0, d, j).start()

        @pl.when(has_left)
        def _():
            ag(1, d, j).start()

        return 0

    lax.fori_loop(0, chunks, first, 0)

    def flow(way, q):
        ql = jnp.clip(q, 0, n * chunks - 1)
        s, jj = ql // chunks, lax.rem(ql, chunks)
        if way == 1:
            s = n - 1 - s
        ahead = (s > d) if way == 0 else (s < d)
        source = has_left if way == 0 else has_right

        @pl.when((q >= 0) & (q < n * chunks) & (ahead | ((s == d) & source)))
        def _():
            @pl.when(source)
            def _():
                rs_wait(jnp.where(s == d, n, s) if way == 0 else s, jj)

            @pl.when(ahead & source)
            def _():
                travel[s, jj] = (partial[s, jj].astype(F32) + travel[s, jj].astype(F32)).astype(BF)

            @pl.when(ahead & jnp.logical_not(source))
            def _():
                travel[s, jj] = partial[s, jj].astype(BF)

            @pl.when(ahead)
            def _():
                rs(way, s, jj).start()

    def block_of(k, way):
        s = d - k + 2 * k * way
        return s, (s >= 0) & (s < n) & ((k > 0) | (way == 0))

    def receive(k, way, s, j):
        @pl.when(k > 0)
        def _():
            pltpu.make_async_copy(gathered.at[s, j], gathered.at[s, j], ag_recv.at[s, j]).wait()

            @pl.when((way == 0) & has_right)
            def _():
                ag(0, s, j).start()

            @pl.when((way == 1) & has_left)
            def _():
                ag(1, s, j).start()

        arrived(s, j)

    wait_one = 1 if early else 0

    def step(g, _):
        k, j = g // chunks, lax.rem(g, chunks)

        def sides(act):
            @pl.when(g < n * chunks)
            def _():
                def side(way, _):
                    s, ok = block_of(k, way)
                    pl.when(ok)(lambda: act(way, s))
                    return 0

                lax.fori_loop(0, 2, side, 0)

        def flows():
            flow(1, g - wait_one - (n - 1 - d) * lag)
            flow(0, g - wait_one - d * lag)

        if turn is not None:
            turn(g)
        if early:
            sides(lambda way, s: receive(k, way, s, j))
            flows()

            def later(way, s):
                prepare(way, s, j)
                compute(way, s, j)

            sides(later)
        else:
            def work(way, s):
                prepare(way, s, j)
                receive(k, way, s, j)
                compute(way, s, j)

            sides(work)
            flows()
        if after is not None:
            after(g)
        return 0

    lax.fori_loop(0, n * chunks + (n - 1) * lag + wait_one, step, 0)

    def drain(i, _):
        s, j = i // chunks, lax.rem(i, chunks)

        @pl.when(has_right & (s <= d))
        def _():
            ag(0, s, j).wait_send()

        @pl.when(has_left & (s >= d))
        def _():
            ag(1, s, j).wait_send()

        @pl.when(s < d)
        def _():
            rs(1, s, j).wait_send()

        @pl.when(s > d)
        def _():
            rs(0, s, j).wait_send()

        return 0

    lax.fori_loop(0, n * chunks, drain, 0)


def own_sum(n, d, j, partial, travel, total):
    total[...] = partial[d, j].astype(F32)

    @pl.when(d > 0)
    def _():
        total[...] += travel[n, j].astype(F32)

    @pl.when(d < n - 1)
    def _():
        total[...] += travel[d, j].astype(F32)


def chain_sems(n, chunks):
    dma = pltpu.SemaphoreType.DMA
    return [dma((2, n, chunks)), dma((n, chunks)), dma((n, chunks)), dma((n + 1, chunks))]


def chunk_buffers(n, rows, c, kept):
    return [
        pltpu.VMEM((n, CHUNKS, rows, c), BF),
        pltpu.VMEM((n, CHUNKS, rows, c), kept),
        pltpu.VMEM((n + 1, CHUNKS, rows, c), BF),
    ]


def columns(i):
    return pl.ds(pl.multiple_of(i * TILE, TILE), TILE)


def drain_copies(n, copy):
    def one(i, _):
        copy(i // CHUNKS, lax.rem(i, CHUNKS)).wait()
        return 0

    lax.fori_loop(0, n * CHUNKS, one, 0)


def big_forward(x, w_up, w_down, residual, mask, share, n):
    t, c = x.shape
    h = w_up.shape[1]
    rows = t // CHUNKS
    cols = residual.shape[1]
    half = cols // 2
    pairs = rows // cols // 2

    def kernel(
        x_ref, wu, wd, res, mask_ref, share_ref, out, pooled, x_all, act_all, slope_all, wu_t, wd_t,
        gathered, partial, travel, act, slope, total, folded, turned, copied, stored, load_sem, *sems
    ):
        d = lax.axis_index("mp")
        load = pltpu.make_async_copy(x_ref, gathered.at[d], load_sem)

        def own_chunk(j):
            if isinstance(j, int):
                load.start()
                load.wait()

        def x_copy(s, j):
            return pltpu.make_async_copy(gathered.at[s, j], x_all.at[s, j], copied.at[s, j])

        def prepare(way, s, j):
            pass

        def arrived(s, j):
            x_copy(s, j).start()

        def compute(way, s, j):
            block = gathered.at[s, j]

            def up(i, _):
                pre = jnp.dot(block[...], wu[:, columns(i)], preferred_element_type=F32)
                value, rate = gelu_parts(pre)
                act[:, columns(i)] = value.astype(BF)
                slope[:, columns(i)] = rate.astype(BF)
                return 0

            lax.fori_loop(0, h // TILE, up, 0)
            keep_act = pltpu.make_async_copy(act, act_all.at[s, j], stored.at[0])
            keep_slope = pltpu.make_async_copy(slope, slope_all.at[s, j], stored.at[1])
            keep_act.start()
            keep_slope.start()

            def down(i, _):
                partial[s, j, :, columns(i)] = jnp.dot(
                    act[...], wd[:, columns(i)], preferred_element_type=F32
                )
                return 0

            lax.fori_loop(0, c // TILE, down, 0)
            keep_act.wait()
            keep_slope.wait()

        def finish(j):
            pl.when(j > 0)(lambda: put(j - 1).wait())
            own_sum(n, d, j, partial, travel, total)
            values = (res[pl.ds(j * 2 * pairs, 2 * pairs)].reshape(rows, c).astype(F32) + total[...]) * mask_ref[j]
            partial[d, j] = values
            put(j).start()
            both = values.reshape(pairs, 2, cols, c)
            summed = (both[:, 0] + both[:, 1]).reshape(pairs * cols, c)
            for b in range(c // LANES):
                lanes = slice(b * LANES, (b + 1) * LANES)
                folded[b] = summed[:, lanes]
                every = folded[b, pl.ds(0, pairs * half, 2), :] + folded[b, pl.ds(1, pairs * half, 2), :]
                pooled[j, :, lanes] = every * share_ref[j]

        def put(j):
            return pltpu.make_async_copy(partial.at[d, j], out.at[j], load_sem)

        def after(g):
            last = g - (n - 1) * (CHUNKS + 1)
            pl.when(last >= 0)(lambda: finish(last))
            for i, (w, target, size) in enumerate(((wu, wu_t, h), (wd, wd_t, c))):
                @pl.when(g < size // LANES)
                def _():
                    some = pl.ds(pl.multiple_of(g * LANES, LANES), LANES)
                    turned[i, :, pl.ds(0, w.shape[0])] = w[:, some].T
                    copy = pltpu.make_async_copy(turned.at[i, :, pl.ds(0, w.shape[0])], target.at[some], stored.at[i])
                    copy.start()
                    copy.wait()

        chain_exchange(
            n, CHUNKS, 1, gathered, partial, travel, sems, own_chunk, prepare, arrived, compute, after=after
        )

        put(CHUNKS - 1).wait()
        drain_copies(n, x_copy)

    whole = pl.BlockSpec(memory_space=pl.ANY)
    local = pl.BlockSpec(memory_space=pltpu.VMEM)
    out, pooled, x_all, act_all, slope_all, wu_t, wd_t = pl.pallas_call(
        kernel,
        out_shape=(
            jax.ShapeDtypeStruct((CHUNKS, rows, c), F32),
            jax.ShapeDtypeStruct((CHUNKS, pairs * half, c), F32),
            jax.ShapeDtypeStruct((n, CHUNKS, rows, c), BF),
            jax.ShapeDtypeStruct((n, CHUNKS, rows, h), BF),
            jax.ShapeDtypeStruct((n, CHUNKS, rows, h), BF),
            jax.ShapeDtypeStruct((h, c), BF),
            jax.ShapeDtypeStruct((c, h), BF),
        ),
        in_specs=[whole, local, local, local, local, local],
        out_specs=(whole, local, whole, whole, whole, whole, whole),
        scratch_shapes=chunk_buffers(n, rows, c, F32)
        + [pltpu.VMEM((rows, h), BF)] * 2
        + [pltpu.VMEM((rows, c), F32), pltpu.VMEM((c // LANES, pairs * cols, LANES), F32), pltpu.VMEM((2, LANES, max(c, h)), BF)]
        + [pltpu.SemaphoreType.DMA((n, CHUNKS)), pltpu.SemaphoreType.DMA((2,)), pltpu.SemaphoreType.DMA]
        + chain_sems(n, CHUNKS),
        compiler_params=pltpu.CompilerParams(
            collective_id=0, has_side_effects=True, vmem_limit_bytes=60 * MIB
        ),
        cost_estimate=pl.CostEstimate(
            flops=4 * n * t * c * h, bytes_accessed=8 * n * t * c, transcendentals=n * t * h
        ),
    )(
        x.reshape(CHUNKS, rows, c), w_up, w_down, residual,
        mask.reshape(CHUNKS, rows, 1), share.reshape(CHUNKS, pairs * half, 1),
    )
    return (
        out.reshape(t, c),
        pooled.reshape(t // 4, c),
        x_all,
        act_all,
        slope_all,
        wu_t,
        wd_t,
    )


def big_backward(cot, d_pooled, share, mask, x_all, act_all, slope_all, up_t, down_t, grads, n, devices):
    _, cols, c = cot.shape
    t = cot.shape[0] * cols
    h = up_t.shape[0]
    rows = t // CHUNKS
    half = cols // 2
    pairs_here = rows // cols // 2
    piece = c // devices
    items = n * CHUNKS // 2
    pairs, g_rows, g_cols = grads.shape
    bits = range(1, devices.bit_length() - 1)
    split = g_rows // 2
    steps = len(bits)
    plans = [Halving(bits, [last] * steps, (pairs, split, g_cols), min(g_cols, 1024)) for last in (True, False)]
    extras = [b for plan in plans for b in plan.buffers()[:-1]]
    each = 2 * steps - 1

    def kernel(
        cot_ref, pool_ref, share_ref, mask_ref, x_hbm, act_hbm, slopes, wu, wd, g_first, g_second,
        out, d_own, g_up_out, g_down_out, out_up, out_down, got_up, got_down, h_all, *rest
    ):
        sums, extra, rest = rest[0], rest[1 : 1 + 2 * each], rest[1 + 2 * each :]
        gathered, partial, travel, slope, grad, left, right, middle, g_up, g_down, total, spread_rows, addend = rest[:13]
        core_send, core_recv, stored, add_sem, send0, recv0, send1, recv1 = rest[13:21]
        sems = rest[21:]
        d = lax.axis_index("mp")
        plans[0].bind(g_first.at[:, :, pl.ds(0, split)], extra[:each] + (sums.at[0],), send0, recv0)
        plans[1].bind(g_second.at[:, :, pl.ds(split, split)], extra[each:] + (sums.at[1],), send1, recv1)

        def begin():
            for plan in plans:
                plan.start(0)

        def pass_on(p, plan):
            plan.finish(p)
            if p + 1 < steps:
                plan.start(p + 1)

        first_due = 2 * CHUNKS + 4
        ticks = {}
        if steps == 2:
            for p, start in ((0, first_due), (1, n * CHUNKS + n - 2)):
                tiles = [
                    (plan, k, q)
                    for plan in plans
                    for k in range(plan.got[p].shape[0])
                    for q in range(g_cols // plan.block)
                ]
                for m in range(0, len(tiles), 4):
                    ticks[start + m // 4] = (p, m == 0, m + 4 >= len(tiles), tiles[m : m + 4])

        def tile_copy(which, p, i, plan, k, q):
            lanes = pl.ds(q * plan.block, plan.block)
            if which == 0:
                source, target = plan.part(p, True).at[k, :, lanes], addend.at[0, i]
            elif which == 1:
                source, target = plan.got[p].at[k, :, lanes], addend.at[1, i]
            else:
                ways = plan.split(plan.got[p].shape[0], p + 1)
                source, target = addend.at[0, i], plan.now[p + 1].at[k // ways[1], k % ways[1], :, lanes]
            return pltpu.make_async_copy(source, target, add_sem.at[which, i])

        def tick_begin(p, fresh, final, tiles):
            if fresh:
                for plan in plans:
                    plan.copy(p).wait()
            for i, tile in enumerate(tiles):
                for which in range(2):
                    tile_copy(which, p, i, *tile).start()

        def tick_add(p, fresh, final, tiles):
            for i, tile in enumerate(tiles):
                for which in range(2):
                    tile_copy(which, p, i, *tile).wait()
                addend[0, i] = (addend[0, i].astype(F32) + addend[1, i].astype(F32)).astype(BF)
                tile_copy(2, p, i, *tile).start()
            for i, tile in enumerate(tiles):
                tile_copy(2, p, i, *tile).wait()
            if final and p + 1 < steps:
                for plan in plans:
                    plan.start(p + 1)

        all_steps = n * CHUNKS + n
        due = [all_steps * 9 * (2**steps - 2 ** (steps - 1 - p)) // (10 * (2**steps - 1)) // 2 * 2 for p in range(steps)]

        def turn(g):
            if ticks:
                for at, tick in ticks.items():
                    pl.when(g == at)(lambda tick=tick: tick_begin(*tick))
            else:
                for p in range(steps - 1):
                    for i, plan in enumerate(plans):
                        pl.when(g == due[p] + 2 * i)(lambda p=p, plan=plan: pass_on(p, plan))

            q, due_now = item_of(g)

            @pl.when(due_now)
            def _():
                for copy in item_copies(q):
                    copy.start()

        def own_chunk(j):
            part = pool_ref[j] * share_ref[j]
            here = cot_ref.at[pl.ds(j * 2 * pairs_here, 2 * pairs_here)]
            for b in range(c // LANES):
                lanes = slice(b * LANES, (b + 1) * LANES)
                spread_rows[b, pl.ds(0, pairs_here * half, 2), :] = part[:, lanes]
                spread_rows[b, pl.ds(1, pairs_here * half, 2), :] = part[:, lanes]
                block = jnp.broadcast_to(
                    spread_rows[b].reshape(pairs_here, 1, cols, LANES), (pairs_here, 2, cols, LANES)
                ).reshape(rows, LANES)
                cell = here[:, :, lanes].reshape(rows, LANES).astype(F32)
                gathered[d, j, :, lanes] = ((cell + block) * mask_ref[j]).astype(BF)

        def slope_copy(s, j):
            return pltpu.make_async_copy(slopes.at[s, j], slope, stored.at[0])

        def prepare(way, s, j):
            slope_copy(s, j).start()

        def arrived(s, j):
            pass

        def compute(way, s, j):
            block = gathered.at[s, j]
            slope_copy(s, j).wait()

            def up(i, _):
                back = nn(block[...], wd[:, columns(i)])
                grad[:, columns(i)] = (back * slope[:, columns(i)].astype(F32)).astype(BF)
                return 0

            lax.fori_loop(0, h // TILE, up, 0)
            half_pair = pl.ds(pl.multiple_of(lax.rem(j, 2) * rows, rows), rows)
            keep = pltpu.make_async_copy(grad, h_all.at[s, j // 2, half_pair], stored.at[1])
            keep.start()

            def down(i, _):
                partial[s, j, :, columns(i)] = nn(grad[...], wu[:, columns(i)]).astype(BF)
                return 0

            lax.fori_loop(0, c // TILE, down, 0)
            keep.wait()

        def item_place(q):
            s, jj, base = d, q, CHUNKS // 2
            for k in range(1, n):
                to_left, to_right = d - k >= 0, d + k < n
                two = to_left & to_right
                r = q - base
                here = (r >= 0) & (to_left | to_right)
                s = jnp.where(here, jnp.where(to_left & (jnp.logical_not(two) | (lax.rem(r, 2) == 0)), d - k, d + k), s)
                jj = jnp.where(here, jnp.where(two, r // 2, r), jj)
                base = base + (CHUNKS // 2) * (to_left.astype(jnp.int32) + to_right.astype(jnp.int32))
            return s, jj

        def item_copies(q):
            s, jj = item_place(q)
            return (
                pltpu.make_async_copy(x_hbm.at[s, jj], left, stored.at[2]),
                pltpu.make_async_copy(act_hbm.at[s, jj], right, stored.at[3]),
                pltpu.make_async_copy(h_all.at[s, jj], middle, stored.at[4]),
            )

        between = (d > 0) & (d < n - 1)
        middle_steps = [n * CHUNKS - items + i for i in range(items)]
        if n == 4 and CHUNKS == 6:
            middle_steps = [2, 4, 12, 13, 14, 15, 17, 19, 20, 21, 22, 23]

        def item_of(g):
            q = jnp.where(between, -1, (g - 3) // 2)
            for i, at in enumerate(middle_steps):
                q = jnp.where(between & (g == at), i, q)
            return q, (q >= 0) & (q < items) & (g >= 2) & (between | (lax.rem(g, 2) == 1))

        def after(g):
            for at, tick in ticks.items():
                pl.when(g == at)(lambda tick=tick: tick_add(*tick))
            last = g - 1 - (n - 1) * (CHUNKS + 1)
            pl.when(last >= 0)(lambda: finish(last))
            q, due_now = item_of(g)

            @pl.when(due_now)
            def _():
                s, jj = item_place(q)
                for copy in item_copies(q):
                    copy.wait()

                def tile(i, _):
                    a = columns(i)
                    g_up[a] += tn(left[:, a], middle[...])
                    db = gathered[s, pl.ds(2 * jj, 2), :, a].reshape(2 * rows, TILE)
                    g_down[a] += tn(db, right[...])
                    return 0

                lax.fori_loop(0, c // TILE, tile, 0)

            @pl.when(g == 2 * items + 2)
            def _():
                give(g_up, left, out_up, stored.at[2])
                swaps[0].start()

            @pl.when(g == 2 * items + 3)
            def _():
                give(g_down, right, out_down, stored.at[3])
                swaps[1].start()

        core = dp_bit(0)

        def result(j):
            return pltpu.make_async_copy(total, out.at[j], stored.at[5])

        def finish(j):
            pl.when(j > 0)(lambda: result(j - 1).wait())
            own_sum(n, d, j, partial, travel, total)
            result(j).start()

        def rows_at(i):
            return pl.ds(pl.multiple_of(i * piece, piece), piece)

        def give(source, stage, target, sem):
            def one(i, _):
                stage[pl.ds(0, piece)] = source[rows_at(2 * i + 1 - core)].astype(BF)
                copy = pltpu.make_async_copy(stage.at[pl.ds(0, piece)], target.at[i], sem)
                copy.start()
                copy.wait()
                return 0

            lax.fori_loop(0, devices // 2, one, 0)

        def keep_sums():
            sets = ((g_up, left, got_up, g_up_out, 2), (g_down, right, got_down, g_down_out, 3))

            def loads(i):
                return [
                    pltpu.make_async_copy(got.at[i], stage.at[pl.ds(0, piece)], stored.at[sem])
                    for _, stage, got, _, sem in sets
                ]

            def one(i, _):
                for load in loads(i):
                    load.start()
                saves = []
                for load, (source, stage, _, target, sem) in zip(loads(i), sets):
                    load.wait()
                    here = stage.at[pl.ds(0, piece)]
                    here[...] = (source[rows_at(2 * i + core)] + here[...].astype(F32)).astype(BF)
                    saves.append(pltpu.make_async_copy(here, target.at[i], stored.at[sem]))
                    saves[-1].start()
                for save in saves:
                    save.wait()
                return 0

            lax.fori_loop(0, devices // 2, one, 0)

        swaps = [
            pltpu.make_async_remote_copy(
                src_ref=src, dst_ref=dst, send_sem=core_send.at[i], recv_sem=core_recv.at[i],
                device_id={"dp": dp_mate(0)}, device_id_type=MESH,
            )
            for i, (src, dst) in enumerate(((out_up, got_up), (out_down, got_down)))
        ]
        def clear(i, _):
            some = pl.ds(pl.multiple_of(i * TILE, TILE), TILE)
            g_up[some] = jnp.zeros((TILE, h), F32)
            g_down[some] = jnp.zeros((TILE, h), F32)
            return 0

        def begin_all():
            begin()
            lax.fori_loop(0, c // TILE, clear, 0)

        chain_exchange(
            n, CHUNKS, 1, gathered, partial, travel, sems, own_chunk, prepare, arrived, compute,
            [dp_mate(b) for b in range(steps + 1)], begin_all, turn, after, True,
        )
        keep = pltpu.make_async_copy(gathered.at[d], d_own, stored.at[0])
        keep.start()
        result(CHUNKS - 1).wait()
        keep.wait()
        if not ticks:
            for plan in plans:
                pass_on(steps - 1, plan)
        for swap in swaps:
            swap.wait()
        keep_sums()

    whole = pl.BlockSpec(memory_space=pl.ANY)
    local = pl.BlockSpec(memory_space=pltpu.VMEM)
    dma = pltpu.SemaphoreType.DMA
    out, d_own, g_up, g_down, _, _, _, _, _, sums, *_ = pl.pallas_call(
        kernel,
        out_shape=(
            jax.ShapeDtypeStruct((CHUNKS, rows, c), F32),
            jax.ShapeDtypeStruct((CHUNKS, rows, c), BF),
            *[jax.ShapeDtypeStruct((devices // 2, piece, h), BF)] * 6,
            jax.ShapeDtypeStruct((n, CHUNKS // 2, 2 * rows, h), BF),
            jax.ShapeDtypeStruct((2, 1, 1, split, g_cols), BF),
            *extras,
        ),
        in_specs=[local] * 4 + [whole] * 3 + [local] * 2 + [whole] * 2,
        out_specs=(whole,) * (10 + 2 * each),
        scratch_shapes=chunk_buffers(n, rows, c, BF)
        + [
            pltpu.VMEM((rows, h), BF), pltpu.VMEM((rows, h), BF),
            pltpu.VMEM((2 * rows, c), BF), pltpu.VMEM((2 * rows, h), BF), pltpu.VMEM((2 * rows, h), BF),
            pltpu.VMEM((c, h), F32), pltpu.VMEM((c, h), F32),
            pltpu.VMEM((rows, c), F32), pltpu.VMEM((c // LANES, pairs_here * cols, LANES), F32),
            pltpu.VMEM((2, 4, split, plans[0].block), BF),
            dma((2,)), dma((2,)), dma((6,)), dma((3, 4)),
        ]
        + plans[0].semaphores() + plans[1].semaphores()
        + chain_sems(n, CHUNKS),
        compiler_params=pltpu.CompilerParams(
            collective_id=1, has_side_effects=True, vmem_limit_bytes=62 * MIB
        ),
        cost_estimate=pl.CostEstimate(
            flops=8 * n * t * c * h, bytes_accessed=8 * n * t * c, transcendentals=0
        ),
    )(
        cot, d_pooled.reshape(CHUNKS, pairs_here * half, c), share.reshape(CHUNKS, pairs_here * half, 1),
        mask.reshape(CHUNKS, rows, 1), *(v.reshape(n, CHUNKS // 2, 2 * rows, -1) for v in (x_all, act_all)),
        slope_all, up_t, down_t,
        grads.reshape(pairs // 2, 2, g_rows, g_cols), grads.reshape(2, pairs // 2, g_rows, g_cols),
    )
    return (
        out.reshape(cot.shape), d_own.reshape(cot.shape), [g_up, g_down],
        sums.reshape(g_rows, g_cols),
    )


def frame(dst, src):
    rows, cols, _ = src.shape
    dst[:, :EDGE] = jnp.zeros((rows, EDGE, LANES), F32)
    dst[:, EDGE + cols:] = jnp.zeros((rows, EDGE, LANES), F32)
    dst[:, EDGE:EDGE + cols] = src[...].astype(F32)


def correlate(out, framed, taps, size, flip, group, first=0, last=None, every=1):
    rows, cols, _ = out.shape
    reach = size // 2
    def some(k, _):
        r = first + k * every
        acc = jnp.zeros((group, cols, LANES), F32)
        for a in range(size):
            for b in range(size):
                tap = (size - 1 - a) * size + size - 1 - b if flip else a * size + b
                acc = acc + framed[pl.ds(r * group + a, group), pl.ds(EDGE - reach + b, cols), :] * taps[tap]
        out[pl.ds(r * group, group)] = acc
        return 0
    lax.fori_loop(0, (rows // group if last is None else last) - first if every == 1 else 2, some, 0)


def conv_forward(x, w, size, n):
    rows, cols, c = x.shape
    reach = size // 2

    def kernel(x_ref, w_ref, out, bordered, framed, sent, got, own):
        d = lax.axis_index("mp")
        has_up, has_down = d > 0, d < n - 1
        barrier = pltpu.get_barrier_semaphore()

        @pl.when(has_up)
        def _():
            pl.semaphore_signal(barrier, inc=1, device_id={"mp": d - 1}, device_id_type=MESH)

        @pl.when(has_down)
        def _():
            pl.semaphore_signal(barrier, inc=1, device_id={"mp": d + 1}, device_id_type=MESH)

        keep = pltpu.make_async_copy(x_ref, bordered.at[pl.ds(reach, rows)], own)
        keep.start()
        pl.semaphore_wait(barrier, has_up.astype(jnp.int32) + has_down.astype(jnp.int32))
        up = pltpu.make_async_remote_copy(
            src_ref=x_ref.at[pl.ds(0, reach)], dst_ref=bordered.at[pl.ds(reach + rows, reach)],
            send_sem=sent.at[0], recv_sem=got.at[0], device_id={"mp": d - 1}, device_id_type=MESH,
        )
        down = pltpu.make_async_remote_copy(
            src_ref=x_ref.at[pl.ds(rows - reach, reach)], dst_ref=bordered.at[pl.ds(0, reach)],
            send_sem=sent.at[1], recv_sem=got.at[1], device_id={"mp": d + 1}, device_id_type=MESH,
        )
        nothing = jnp.zeros((reach, cols, c), BF)

        @pl.when(has_up)
        def _():
            up.start()

        @pl.when(has_down)
        def _():
            down.start()

        @pl.when(d == 0)
        def _():
            bordered[:reach] = nothing

        @pl.when(d == n - 1)
        def _():
            bordered[reach + rows :] = nothing

        groups = rows // reach

        def inner(i, _):
            lanes = pl.ds(pl.multiple_of(i * LANES, LANES), LANES)
            frame(framed.at[pl.ds(reach, rows)], x_ref.at[:, :, lanes])
            correlate(out.at[:, :, lanes], framed, w_ref.at[:, :, lanes], size, False, reach, 1, groups - 1)
            return 0

        lax.fori_loop(0, c // LANES, inner, 0)
        keep.wait()

        @pl.when(has_up)
        def _():
            down.wait_recv()

        @pl.when(has_down)
        def _():
            up.wait_recv()

        def block(i, _):
            lanes = pl.ds(pl.multiple_of(i * LANES, LANES), LANES)
            frame(framed, bordered.at[:, :, lanes])
            correlate(out.at[:, :, lanes], framed, w_ref.at[:, :, lanes], size, False, reach, 0, None, groups - 1)
            return 0

        lax.fori_loop(0, c // LANES, block, 0)

        @pl.when(has_up)
        def _():
            up.wait_send()

        @pl.when(has_down)
        def _():
            down.wait_send()

    local = pl.BlockSpec(memory_space=pltpu.VMEM)
    dma = pltpu.SemaphoreType.DMA
    return pl.pallas_call(
        kernel,
        out_shape=(
            jax.ShapeDtypeStruct((rows, cols, c), F32),
            jax.ShapeDtypeStruct((rows + 2 * reach, cols, c), BF),
        ),
        in_specs=[local, local],
        out_specs=(local, local),
        scratch_shapes=[pltpu.VMEM((rows + 2 * reach, cols + 2 * EDGE, LANES), F32), dma((2,)), dma((2,)), dma],
        compiler_params=pltpu.CompilerParams(
            collective_id=5, has_side_effects=True, vmem_limit_bytes=40 * MIB
        ),
    )(x, w)


def conv_backward(d_normed, conv_out, gain, mask, bordered, d_map, w, low_gains, size, grads, devices, n):
    rows, cols, c = conv_out.shape
    reach = size // 2
    high = rows + 2 * reach
    group = 4 if rows % 4 == 0 else 1
    bits = range(1, devices.bit_length() - 1)
    steps = len(bits)
    shape = grads[0].shape
    plans = [Halving(bits, [last] * steps, shape, shape[2]) for last in (True, False)]
    each = 2 * steps
    blocks = c // LANES
    taps = size * size
    count = taps + 1 + low_gains.shape[0]
    small = -(-count // devices)
    first_due = blocks + blocks // 3
    begins = {first_due + blocks // 2 * p // (steps - 1): p for p in range(steps - 1)}
    ends = {mark + 1: p for mark, p in begins.items()}
    rounds = {blocks + 10 * blocks // 12: 1}

    def kernel(
        dn, co, gain_ref, mask_ref, w_ref, low_ref, b_hbm, dm_hbm, g0, g1, out, g_all, *rest
    ):
        extra, rest = rest[: 2 * each], rest[2 * each :]
        around, x_around, d_here, dframed, xframed, g_own, here, level, addend, sent, got, own, add_sem = rest[:13]
        ar, halving_sems = rest[13:19], rest[19:]
        plans[0].bind(g0, extra[:each], halving_sems[0], halving_sems[1])
        plans[1].bind(g1, extra[each:], halving_sems[2], halving_sems[3])
        me, d = lax.axis_index("dp"), lax.axis_index("mp")
        has_up, has_down = d > 0, d < n - 1
        barrier = pltpu.get_barrier_semaphore()

        def greet(k, _):
            pl.semaphore_signal(
                barrier, inc=1, device_id={"dp": lax.rem(me + k, devices)}, device_id_type=MESH
            )
            return 0

        lax.fori_loop(1, devices, greet, 0)
        for k in range(1, n):
            pl.semaphore_signal(barrier, inc=1, device_id={"mp": lax.rem(d + k, n)}, device_id_type=MESH)
        load_x = pltpu.make_async_copy(b_hbm, x_around, own.at[0])
        load_d = pltpu.make_async_copy(dm_hbm, d_here, own.at[1])
        load_x.start()
        load_d.start()

        def halving_loads(p, i):
            plan, count = plans[i], plans[i].got[p].shape[0]
            some = pl.ds(0, count)
            return [
                pltpu.make_async_copy(plan.part(p, True), addend.at[0, i, some], add_sem.at[0, i]),
                pltpu.make_async_copy(plan.got[p], addend.at[1, i, some], add_sem.at[1, i]),
            ]

        def halving_save(p, i, k):
            plan = plans[i]
            ways = plan.split(plan.got[p].shape[0], p + 1)
            target = plan.now[p + 1].at[k // ways[1], k % ways[1]]
            return pltpu.make_async_copy(addend.at[0, i, k], target, add_sem.at[2 + i, k])

        def halving_begin(p):
            for i, plan in enumerate(plans):
                plan.copy(p).wait()
                for load in halving_loads(p, i):
                    load.start()

        def halving_end(p):
            for i, plan in enumerate(plans):
                for load in halving_loads(p, i):
                    load.wait()
                for k in range(plan.got[p].shape[0]):
                    addend[0, i, k] = (addend[0, i, k].astype(F32) + addend[1, i, k].astype(F32)).astype(BF)
                    halving_save(p, i, k).start()
            for i, plan in enumerate(plans):
                for k in range(plan.got[p].shape[0]):
                    halving_save(p, i, k).wait()
            if p + 1 < steps:
                for plan in plans:
                    plan.start(p + 1)

        def keep(row, lanes, value):
            g_own[row // small, row % small : row % small + 1, lanes] = value

        pl.semaphore_wait(barrier, devices + n - 2)
        for plan in plans:
            plan.start(0)
        g_own[...] = jnp.zeros(g_own.shape, F32)

        def norm(r, total):
            cells = mask_ref[r]
            back, part = normalise_back(co[r] * cells, gain_ref[...], dn[r])
            around[reach + r] = (back * cells).astype(BF)
            return total + part

        keep(taps, slice(None), lax.fori_loop(0, rows, norm, jnp.zeros((1, c), F32)))
        for i in range(low_gains.shape[0]):
            keep(taps + 1 + i, slice(None), low_ref[i : i + 1])
        up = pltpu.make_async_remote_copy(
            src_ref=around.at[pl.ds(reach, reach)], dst_ref=around.at[pl.ds(reach + rows, reach)],
            send_sem=sent.at[0], recv_sem=got.at[0], device_id={"mp": d - 1}, device_id_type=MESH,
        )
        down = pltpu.make_async_remote_copy(
            src_ref=around.at[pl.ds(rows, reach)], dst_ref=around.at[pl.ds(0, reach)],
            send_sem=sent.at[1], recv_sem=got.at[1], device_id={"mp": d + 1}, device_id_type=MESH,
        )
        nothing = jnp.zeros((reach, cols, c), BF)

        @pl.when(has_up)
        def _():
            up.start()

        @pl.when(has_down)
        def _():
            down.start()

        @pl.when(d == 0)
        def _():
            around[:reach] = nothing

        @pl.when(d == n - 1)
        def _():
            around[reach + rows :] = nothing

        load_x.wait()

        def lanes_of(i):
            return pl.ds(pl.multiple_of(i * LANES, LANES), LANES)

        def kernel_block(i, _):
            lanes = lanes_of(i)
            frame(dframed.at[pl.ds(reach, rows)], around.at[pl.ds(reach, rows), :, lanes])
            frame(xframed, x_around.at[:, :, lanes])
            for a in range(size):
                def some(r, accs):
                    dv = dframed[pl.ds(reach + r * group, group), EDGE : EDGE + cols]
                    new = []
                    for b in range(size):
                        prod = dv * xframed[pl.ds(r * group + a, group), pl.ds(EDGE - reach + b, cols), :]
                        new.append(accs[b] + jnp.sum(prod.reshape(-1, 8, LANES), axis=0))
                    return tuple(new)

                accs = lax.fori_loop(
                    0, rows // group, some, tuple(jnp.zeros((8, LANES), F32) for _ in range(size))
                )
                for b in range(size):
                    keep(a * size + b, lanes, jnp.sum(accs[b], axis=0, keepdims=True))
            return 0

        def input_block(i, _):
            lanes = lanes_of(i)
            frame(dframed, around.at[:, :, lanes])
            correlate(out.at[:, :, lanes], dframed, w_ref.at[:, :, lanes], size, True, group)
            for r in range(rows):
                out[r, :, lanes] = (out[r, :, lanes] + d_here[r, :, lanes].astype(F32)) * mask_ref[r]
            return 0

        def spread(k):
            peer = lax.rem(me + k, devices)
            return pltpu.make_async_remote_copy(
                src_ref=g_own.at[peer], dst_ref=here.at[me], send_sem=ar[0].at[k], recv_sem=ar[1].at[k],
                device_id={"dp": peer}, device_id_type=MESH,
            )

        def across(k):
            return pltpu.make_async_remote_copy(
                src_ref=level.at[d], dst_ref=level.at[d], send_sem=ar[2].at[k], recv_sem=ar[3].at[k],
                device_id={"mp": lax.rem(d + k, n)}, device_id_type=MESH,
            )

        def tell(k):
            return pltpu.make_async_remote_copy(
                src_ref=g_all.at[me], dst_ref=g_all.at[me], send_sem=ar[4].at[k], recv_sem=ar[5].at[k],
                device_id={"dp": lax.rem(me + k, devices)}, device_id_type=MESH,
            )

        def all_of(length, make, act):
            def one(k, _):
                act(make(k))
                return 0

            lax.fori_loop(1, length, one, 0)

        def sum_round(p):
            if p == 0:
                here[me] = g_own[me]
                all_of(devices, spread, lambda x: x.start())
            elif p == 1:
                all_of(devices, spread, lambda x: x.wait())
                level[d] = jnp.sum(here[...], axis=0)
                all_of(n, across, lambda x: x.start())
            elif p == 2:
                all_of(n, across, lambda x: x.wait())
                g_all[me] = jnp.sum(level[...], axis=0)
                all_of(devices, tell, lambda x: x.start())
            else:
                all_of(devices, tell, lambda x: x.wait())

        marks = sorted(set(begins) | set(ends) | set(rounds) | {blocks, 2 * blocks})
        at = 0
        for mark in marks:
            if at < blocks:
                lax.fori_loop(at, min(mark, blocks), kernel_block, 0)
            else:
                lax.fori_loop(at - blocks, mark - blocks, input_block, 0)
            at = mark
            if mark in ends:
                halving_end(ends[mark])
            if mark in begins:
                halving_begin(begins[mark])
            if mark == first_due:
                sum_round(0)
            if mark == blocks:
                load_d.wait()

                @pl.when(has_up)
                def _():
                    down.wait_recv()

                @pl.when(has_down)
                def _():
                    up.wait_recv()
            if mark in rounds:
                sum_round(rounds[mark])
        sum_round(2)
        halving_begin(steps - 1)
        halving_end(steps - 1)
        sum_round(3)

        @pl.when(has_up)
        def _():
            up.wait_send()

        @pl.when(has_down)
        def _():
            down.wait_send()

    whole = pl.BlockSpec(memory_space=pl.ANY)
    local = pl.BlockSpec(memory_space=pltpu.VMEM)
    vm, dma = pltpu.VMEM, pltpu.SemaphoreType.DMA
    d_in, g_all, *extra = pl.pallas_call(
        kernel,
        out_shape=(
            jax.ShapeDtypeStruct((rows, cols, c), F32),
            jax.ShapeDtypeStruct((devices, small, c), F32),
            *plans[0].buffers(),
            *plans[1].buffers(),
        ),
        in_specs=[local] * 6 + [whole] * 4,
        out_specs=(local,) * 2 + (whole,) * (2 * each),
        scratch_shapes=[
            vm((high, cols, c), BF), vm((high, cols, c), BF), vm((rows, cols, c), BF),
            vm((high, cols + 2 * EDGE, LANES), F32), vm((high, cols + 2 * EDGE, LANES), F32),
            vm((devices, small, c), F32), vm((devices, small, c), F32), vm((n, small, c), F32),
            vm((2, 2, shape[0] // 2) + shape[1:], BF),
            dma((2,)), dma((2,)), dma((2,)), dma((4, max(2, shape[0] // 2))),
            dma((devices,)), dma((devices,)), dma((n,)), dma((n,)), dma((devices,)), dma((devices,)),
        ]
        + plans[0].semaphores() + plans[1].semaphores(),
        compiler_params=pltpu.CompilerParams(
            collective_id=3, has_side_effects=True, vmem_limit_bytes=50 * MIB
        ),
        cost_estimate=pl.CostEstimate(flops=6 * 10**10, bytes_accessed=10**8, transcendentals=0),
    )(
        d_normed, conv_out, gain, mask, w, low_gains, bordered, d_map,
        grads[0].reshape((shape[0] // 2, 2) + shape[1:]), grads[1].reshape((2, shape[0] // 2) + shape[1:]),
    )
    sums = g_all.reshape(devices * small, c)[:count]
    return d_in, sums, [extra[each - 1].reshape(shape[1:]), extra[2 * each - 1].reshape(shape[1:])]


GATE, OUT, HIGH_A, HIGH_B, QUERY, KEY, VALUE, PROJ = range(8)
L_LOW, L_DF, L_POOL_A, L_POOL_B, L_FIRST, L_DA, L_SECOND, L_COT = range(8)
R_DGATE, R_MERGE, R_DHIGH, R_DQ, R_DK, R_DV, R_ATT, R_DUP, R_ACT = range(9)


def nn(a, b):
    return jnp.dot(a, b, preferred_element_type=F32)


def nt(a, b):
    return lax.dot_general(a, b, (((1,), (1,)), ((), ())), preferred_element_type=F32)


def tn(a, b):
    return lax.dot_general(a, b, (((0,), (0,)), ((), ())), preferred_element_type=F32)


def normalise(x, gain):
    centred = x - jnp.mean(x, -1, keepdims=True)
    rate = lax.rsqrt(jnp.mean(centred * centred, -1, keepdims=True) + 1e-06)
    return centred * rate * gain


def normalise_back(x, gain, d):
    centred = x - jnp.mean(x, -1, keepdims=True)
    rate = lax.rsqrt(jnp.mean(centred * centred, -1, keepdims=True) + 1e-06)
    hat = centred * rate
    dg = d * gain
    back = rate * (dg - jnp.mean(dg, -1, keepdims=True) - hat * jnp.mean(dg * hat, -1, keepdims=True))
    return back, jnp.sum(d * hat, axis=0, keepdims=True)


def low_stage(low, pooled, cot, gain1, gain2, packed, n, devices, cid):
    t, dim = low.shape
    every = n * t
    width = dim // n
    heads = width // HEAD
    groups = width // LANES
    pairs = devices // 2
    rows = dim // devices
    half = dim // 2
    ff = 4 * dim
    natural = rows % LANES == 0
    high_rows = pooled.shape[1] // devices

    def place_of(k):
        return (k % 2) * half + k // 2 * rows

    def in_order(ref):
        if not natural:
            return ref[...]
        order = sorted(range(devices), key=place_of)
        return jnp.concatenate([ref[:, k * rows : (k + 1) * rows] for k in order], axis=1)

    scale = HEAD ** (-0.5)

    def kernel(
        low_ref, pooled_ref, cot_ref, gain1_ref, gain2_ref, w_hbm,
        low_out, d_low, d_pooled, g_ln1, g_ln2, grads,
        wv, lhs, lhs2, rhs, gate, high, merged, resid, d_res, slope, mixed, heads_in, att_all, d_att, d_mixed,
        d_heads, probs, d_scores, stage, left, w_sem, q_send, q_got, a_send, a_got, b_send, b_got, c_send, c_got, own_sem,
        l_send, l_got, r_send, r_got, stage_sem,
    ):
        d = lax.axis_index("mp")
        dp = lax.axis_index("dp")
        core = lax.rem(dp, 2)
        mate = dp + 1 - 2 * core
        barrier = pltpu.get_barrier_semaphore()
        for k in range(1, n):
            pl.semaphore_signal(barrier, inc=1, device_id={"mp": lax.rem(d + k, n)}, device_id_type=MESH)
        pl.semaphore_signal(barrier, inc=1, device_id={"dp": mate}, device_id_type=MESH)

        def w_copy(w, k):
            c, z = k // n, lax.rem(k, n)
            wide, base, at = w_place(w)
            src = w_hbm.at[:, c, z, :, pl.ds(base, wide)]
            dst = wv.at[c, :, :, pl.ds(pl.multiple_of(at + z * wide, wide), wide)]
            return pltpu.make_async_copy(src, dst, w_sem.at[w, k])

        def w_place(w):
            if w < 8:
                return width, w * width, w * dim
            return ff // n, 8 * width + (w - 8) * ff // n, 8 * dim + (w - 8) * ff

        def w_each(w, act):
            def one(k, _):
                act(w_copy(w, k))
                return 0

            lax.fori_loop(0, 2 * n, one, 0)

        for w in range(10):
            w_each(w, lambda copy: copy.start())

        def w_wait(*which):
            for w in which:
                w_each(w, lambda copy: copy.wait())

        def w_cols(at, size):
            return wv[:, :, :, pl.ds(at, size)].reshape(dim, size)

        def forward(x, first, count, put):
            def one(i, _):
                put(pl.multiple_of(i * TILE, TILE), nn(x, w_cols(pl.multiple_of(first * dim + i * TILE, TILE), TILE)))
                return 0
            lax.fori_loop(0, count * dim // TILE, one, 0)

        def backward(get, first, count, dst, fresh):
            def one(i, _):
                for c in range(2):
                    part = wv[c, :, :, pl.ds(pl.multiple_of((first + i) * dim, dim), dim)].reshape(half, dim)
                    y = nt(get(pl.multiple_of(i * dim, dim)), part)
                    cols = slice(c * half, (c + 1) * half)
                    if fresh and count == 1:
                        dst[:, cols] = y
                    else:
                        dst[:, cols] += y
                return 0
            if fresh and count > 1:
                dst[...] = jnp.zeros(dst.shape, F32)
            if count == 1:
                one(0, 0)
            else:
                lax.fori_loop(0, count, one, 0)

        def r_cols(block, count=1):
            return pl.ds(block * dim, count * dim)

        def r_at(block):
            return block * dim if block <= R_DUP else block * dim + 3 * dim

        def r_copy(block):
            cols = pl.ds(r_at(block), dim if block < R_DUP else ff)
            return pltpu.make_async_remote_copy(
                src_ref=rhs.at[0, :, cols], dst_ref=rhs.at[1, :, cols], send_sem=r_send.at[block],
                recv_sem=r_got.at[block], device_id={"dp": mate}, device_id_type=MESH)

        def l_copy(i):
            return pltpu.make_async_remote_copy(
                src_ref=lhs.at[i, :, pl.ds(pl.multiple_of((1 - core) * half, half), half)], dst_ref=lhs2.at[i],
                send_sem=l_send.at[i], recv_sem=l_got.at[i], device_id={"dp": mate}, device_id_type=MESH)

        stored = []
        turned = [None]

        def put_natural(dst, value):
            if natural:
                for k in range(devices):
                    dst[:, k * rows : (k + 1) * rows] = value[:, place_of(k) : place_of(k) + rows]
            else:
                dst[...] = value

        def grad(i, block, at, count, shared=False):
            if not shared:
                r_copy(block).wait_recv()
            if turned[0] != i:
                left[0] = lhs[i, :, pl.ds(pl.multiple_of(core * half, half), half)].T
                left[1] = lhs2[i].T
                turned[0] = i

            wide, base, first = w_place(at if at < 8 else 8 + (at - 8) * dim // ff)
            piece = min(TILE, wide)

            def out_copies(slot, k):
                out = []
                for q in range(TILE // piece):
                    z, col = divmod(at * dim - first + k * TILE + q * piece, wide)
                    out.append(
                        pltpu.make_async_copy(
                            stage.at[slot, :, :, pl.ds(q * piece, piece)],
                            grads.at[:, pl.ds(z * rows, rows), pl.ds(base + col, piece)],
                            stage_sem.at[slot, q],
                        )
                    )
                return out

            for k in range(count * dim // TILE):
                slot = len(stored) % 2
                if len(stored) >= 2:
                    wait(stored[-2])
                cols = pl.ds(r_at(block) + k * TILE, TILE)
                y = nn(left[0], rhs[0, :, cols]) + nn(left[1], rhs[1, :, cols])
                stage[slot] = y.astype(BF).reshape(pairs, rows, TILE)
                stored.append(out_copies(slot, k))
                start(stored[-1])

        def to_heads(k, src, dst, send, got):
            out = []
            for step in range(1, n):
                peer = lax.rem(d + step, n)
                out.append(pltpu.make_async_remote_copy(
                    src_ref=src.at[:, pl.ds(pl.multiple_of(peer * width, width), width)],
                    dst_ref=dst.at[pl.ds(pl.multiple_of(d * t, t), t)],
                    send_sem=send.at[k, step], recv_sem=got.at[k, step], device_id={"mp": peer}, device_id_type=MESH))
            out.append(pltpu.make_async_copy(
                src.at[:, pl.ds(pl.multiple_of(d * width, width), width)], dst.at[pl.ds(pl.multiple_of(d * t, t), t)], own_sem.at[k]))
            return out

        def to_tokens(k, src, dst, send, got, group):
            out = []
            slot = k * groups + group
            lanes = pl.ds(group * LANES, LANES)
            there = pl.ds(pl.multiple_of(d * width + group * LANES, LANES), LANES)
            for step in range(1, n):
                peer = lax.rem(d + step, n)
                out.append(pltpu.make_async_remote_copy(
                    src_ref=src.at[pl.ds(pl.multiple_of(peer * t, t), t), lanes], dst_ref=dst.at[:, there],
                    send_sem=send.at[slot, step], recv_sem=got.at[slot, step], device_id={"mp": peer}, device_id_type=MESH))
            out.append(pltpu.make_async_copy(
                src.at[pl.ds(pl.multiple_of(d * t, t), t), lanes], dst.at[:, there], own_sem.at[slot]))
            return out

        def start(copies):
            for c in copies:
                c.start()

        def wait(copies):
            for c in copies:
                c.wait()

        gain1_here, gain2_here = in_order(gain1_ref), in_order(gain2_ref)
        if natural:
            for i, ref in ((L_LOW, low_ref), (L_COT, cot_ref)):
                for k in range(devices):
                    lhs[i, :, place_of(k) : place_of(k) + rows] = ref[:, k * rows : (k + 1) * rows]
            for k in range(devices):
                own = slice(place_of(k), place_of(k) + rows)
                lhs[L_POOL_A, :, own] = pooled_ref[:, k * high_rows : k * high_rows + rows].astype(BF)
                more = pooled_ref[:, k * high_rows + rows : (k + 1) * high_rows].astype(BF)
                lhs[L_POOL_B, :, own] = jnp.concatenate([more, jnp.zeros((t, 2 * rows - high_rows), BF)], axis=1)
        else:
            lhs[L_LOW] = low_ref[...]
            lhs[L_COT] = cot_ref[...]
            lhs[L_POOL_A] = pooled_ref[:, :dim].astype(BF)
            lhs[L_POOL_B] = pooled_ref[:, dim:].astype(BF)
        acc = d_low
        w_wait(GATE)

        def put_gate(at, y):
            gate[:, pl.ds(at, TILE)] = 1.0 / (1.0 + jnp.exp(-y))
        forward(lhs[L_LOW], GATE, 1, put_gate)
        w_wait(HIGH_A, HIGH_B, OUT)

        def put_high(at, y):
            high[:, pl.ds(at, TILE)] = y
        forward(lhs[L_POOL_A], HIGH_A, 1, put_high)

        def put_merging(at, y):
            cols = pl.ds(at, TILE)
            total = high[:, cols] + y
            high[:, cols] = total
            rhs[0, :, pl.ds(R_MERGE * dim + at, TILE)] = (total * gate[:, cols]).astype(BF)
        forward(lhs[L_POOL_B], HIGH_B, 1, put_merging)
        backward(lambda at: rhs[0, :, r_cols(R_MERGE)], OUT, 1, merged, True)
        merged[...] += lhs[L_LOW].astype(F32)
        lhs[L_FIRST] = normalise(merged[...], gain1_here).astype(BF)

        w_wait(QUERY, KEY, VALUE, PROJ)
        pl.semaphore_wait(barrier, n)
        for i in (L_LOW, L_POOL_A, L_POOL_B, L_COT, L_FIRST):
            l_copy(i).start()
        r_copy(R_MERGE).start()
        out_q = []
        for k in range(3):
            def put_mixed(at, y):
                mixed[k, :, pl.ds(at, TILE)] = y.astype(BF)
            forward(lhs[L_FIRST], QUERY + k, 1, put_mixed)
            copies = to_heads(k, mixed.at[k], heads_in.at[k], q_send, q_got)
            start(copies)
            out_q.append(copies)
        wait(out_q[0] + out_q[1])

        for h in range(heads):
            lanes = slice(h * HEAD, (h + 1) * HEAD)

            def rows_of(b, _):
                some = pl.ds(pl.multiple_of(b * t, t), t)
                s = nt(heads_in[0, some, lanes], heads_in[1, :, lanes]) * scale
                e = jnp.exp(s - jnp.max(s, -1, keepdims=True))
                p = (e * (1.0 / jnp.sum(e, -1, keepdims=True))).astype(BF)
                probs[h, some] = p
                return 0
            lax.fori_loop(0, n, rows_of, 0)
        wait(out_q[2])
        out_a = []
        for h in range(heads):
            lanes = slice(h * HEAD, (h + 1) * HEAD)

            def attend(b, _):
                some = pl.ds(pl.multiple_of(b * t, t), t)
                att_all[some, lanes] = nn(probs[h, some], heads_in[2, :, lanes]).astype(BF)
                return 0
            lax.fori_loop(0, n, attend, 0)
            if (h + 1) * HEAD % LANES == 0:
                copies = to_tokens(0, att_all, rhs.at[0, :, r_cols(R_ATT)], a_send, a_got, h * HEAD // LANES)
                start(copies)
                out_a += copies
        wait(out_a)
        r_copy(R_ATT).start()
        backward(lambda at: rhs[0, :, r_cols(R_ATT)], PROJ, 1, resid, True)
        resid[...] += merged[...]
        lhs[L_SECOND] = normalise(resid[...], gain2_here).astype(BF)
        l_copy(L_SECOND).start()

        w_wait(8)

        def put_up(at, y):
            value, rate = gelu_parts(y)
            rhs[0, :, pl.ds(r_at(R_ACT) + at, TILE)] = value.astype(BF)
            slope[:, pl.ds(at, TILE)] = rate.astype(BF)
        forward(lhs[L_SECOND], 8, 4, put_up)
        r_copy(R_ACT).start()
        w_wait(9)
        backward(lambda at: rhs[0, :, pl.ds(r_at(R_ACT) + at, dim)], 12, 4, acc, True)
        put_natural(low_out, resid[...] + acc[...])

        def put_d_up(at, y):
            rhs[0, :, pl.ds(r_at(R_DUP) + at, TILE)] = (y * slope[:, pl.ds(at, TILE)].astype(F32)).astype(BF)
        forward(lhs[L_COT], 12, 4, put_d_up)
        r_copy(R_DUP).start()
        backward(lambda at: rhs[0, :, pl.ds(r_at(R_DUP) + at, dim)], 8, 4, acc, True)
        back, g = normalise_back(resid[...], gain2_here, acc[...])
        put_natural(g_ln2, g)
        d_res[...] = lhs[L_COT].astype(F32) + back
        lhs[L_DA] = d_res[...].astype(BF)
        l_copy(L_DA).start()

        def put_d_att(at, y):
            mixed[0, :, pl.ds(at, TILE)] = y.astype(BF)
        forward(lhs[L_DA], PROJ, 1, put_d_att)
        out_b = to_heads(0, mixed.at[0], d_att, b_send, b_got)
        start(out_b)
        l_copy(L_COT).wait_recv()
        grad(L_COT, R_ACT, 12, 4)
        wait(out_b)
        out_c = []

        def send_back(k, h):
            if (h + 1) * HEAD % LANES == 0:
                copies = to_tokens(k, d_heads.at[k], rhs.at[0, :, r_cols(R_DQ + k)], c_send, c_got, h * HEAD // LANES)
                start(copies)
                out_c.extend(copies)

        for h in range(heads):
            lanes = slice(h * HEAD, (h + 1) * HEAD)
            d_heads[2, :, lanes] = tn(probs[h], d_att[:, lanes]).astype(BF)
            send_back(2, h)
        for h in range(heads):
            lanes = slice(h * HEAD, (h + 1) * HEAD)

            def rows_of(b, _):
                some = pl.ds(pl.multiple_of(b * t, t), t)
                p = probs[h, some].astype(F32)
                dp_ = nt(d_att[some, lanes], heads_in[2, :, lanes])
                ds = (p * (dp_ - jnp.sum(dp_ * p, -1, keepdims=True)) * scale).astype(BF)
                d_scores[some] = ds
                d_heads[0, some, lanes] = nn(ds, heads_in[1, :, lanes]).astype(BF)
                return 0
            lax.fori_loop(0, n, rows_of, 0)
            d_heads[1, :, lanes] = tn(d_scores[...], heads_in[0, :, lanes]).astype(BF)
            send_back(0, h)
            send_back(1, h)
        l_copy(L_SECOND).wait_recv()
        grad(L_SECOND, R_DUP, 8, 4)
        l_copy(L_DA).wait_recv()
        grad(L_DA, R_ATT, PROJ, 1)
        wait(out_c)
        for k in range(3):
            r_copy(R_DQ + k).start()
        backward(lambda at: rhs[0, :, pl.ds(R_DQ * dim + at, dim)], QUERY, 3, acc, True)
        back, g = normalise_back(merged[...], gain1_here, acc[...])
        put_natural(g_ln1, g)
        d_res[...] += back
        lhs[L_DF] = d_res[...].astype(BF)
        l_copy(L_DF).start()

        def put_d_gate(at, y):
            cols = pl.ds(at, TILE)
            gv = gate[:, cols]
            part = y * gv
            rhs[0, :, pl.ds(R_DHIGH * dim + at, TILE)] = part.astype(BF)
            rhs[0, :, pl.ds(R_DGATE * dim + at, TILE)] = (part * high[:, cols] * (1.0 - gv)).astype(BF)
        forward(lhs[L_DF], OUT, 1, put_d_gate)
        r_copy(R_DHIGH).start()
        r_copy(R_DGATE).start()
        backward(lambda at: rhs[0, :, r_cols(R_DHIGH)], HIGH_A, 1, gate, True)
        backward(lambda at: rhs[0, :, r_cols(R_DHIGH)], HIGH_B, 1, high, True)
        if natural:
            for k in range(devices):
                at = place_of(k)
                d_pooled[:, k * high_rows : k * high_rows + rows] = gate[:, at : at + rows]
                d_pooled[:, k * high_rows + rows : (k + 1) * high_rows] = high[:, at : at + high_rows - rows]
        else:
            d_pooled[:, :dim] = gate[...]
            d_pooled[:, dim:] = high[...]
        backward(lambda at: rhs[0, :, r_cols(R_DGATE)], GATE, 1, acc, True)
        put_natural(d_low, d_res[...] + acc[...])
        l_copy(L_FIRST).wait_recv()
        for k in range(3):
            grad(L_FIRST, R_DQ + k, QUERY + k, 1)
        l_copy(L_DF).wait_recv()
        grad(L_DF, R_MERGE, OUT, 1)
        l_copy(L_POOL_A).wait_recv()
        grad(L_POOL_A, R_DHIGH, HIGH_A, 1)
        l_copy(L_POOL_B).wait_recv()
        grad(L_POOL_B, R_DHIGH, HIGH_B, 1, shared=True)
        l_copy(L_LOW).wait_recv()
        grad(L_LOW, R_DGATE, GATE, 1)
        wait(stored[-2])
        wait(stored[-1])
        for i in range(8):
            l_copy(i).wait_send()
        for b in range(9):
            r_copy(b).wait_send()

    whole = pl.BlockSpec(memory_space=pl.ANY)
    local = pl.BlockSpec(memory_space=pltpu.VMEM)
    vm, dma = pltpu.VMEM, pltpu.SemaphoreType.DMA
    tok = jax.ShapeDtypeStruct((t, dim), F32)
    one = jax.ShapeDtypeStruct((1, dim), F32)
    return pl.pallas_call(
        kernel,
        out_shape=(tok, tok, jax.ShapeDtypeStruct(pooled.shape, F32), one, one, jax.ShapeDtypeStruct((pairs, n * rows, 16 * width), BF)),
        in_specs=[local] * 5 + [whole],
        out_specs=(local,) * 5 + (whole,),
        scratch_shapes=[
            vm((2, pairs, rows, 16 * dim), BF), vm((8, t, dim), BF), vm((8, t, half), BF), vm((2, t, 15 * dim), BF),
            vm((t, dim), F32), vm((t, dim), F32), vm((t, dim), F32), vm((t, dim), F32), vm((t, dim), F32),
            vm((t, ff), BF), vm((3, t, dim), BF), vm((3, every, width), BF), vm((every, width), BF), vm((every, width), BF),
            vm((1, 8, 128), BF), vm((3, every, width), BF), vm((heads, every, every), BF), vm((every, every), BF),
            vm((2, pairs, rows, TILE), BF), vm((2, half, t), BF),
            dma((10, 2 * n)), dma((3, n)), dma((3, n)), dma((groups, n)), dma((groups, n)), dma((1, n)), dma((1, n)),
            dma((3 * groups, n)), dma((3 * groups, n)), dma((3 * groups,)), dma((8,)), dma((8,)), dma((9,)), dma((9,)), dma((2, 2)),
        ],
        compiler_params=pltpu.CompilerParams(collective_id=cid, has_side_effects=True, vmem_limit_bytes=62 * MIB),
        cost_estimate=pl.CostEstimate(flops=14 * 10**9, bytes_accessed=70 * 10**6, transcendentals=10**7),
    )(low, pooled, cot, gain1, gain2, packed.reshape(pairs, 2, n, rows, 16 * width))
def low_outputs(own, widths, high_rows):
    share = own.shape[0]
    width, wide = widths[0], widths[-1]

    def kernel(x, gate, high, out, qkv, proj, up, down):
        def part(i, size=width):
            at = sum(widths[:i])
            return x[:, at : at + size].astype(F32)

        gate[...] = part(0)
        out[...] = part(1).T
        high[:share] = part(2)
        high[share:] = part(3)[: high_rows - share]
        for k in range(3):
            qkv[k] = part(4 + k)
        proj[...] = part(7).T
        up[...] = part(8, wide)
        down[...] = part(9, wide).T

    local = pl.BlockSpec(memory_space=pltpu.VMEM)
    shapes = [
        (share, width), (high_rows, width), (width, share), (3, share, width), (width, share), (share, wide), (wide, share),
    ]
    return pl.pallas_call(
        kernel,
        out_shape=[jax.ShapeDtypeStruct(s, F32) for s in shapes],
        in_specs=[local],
        out_specs=[local] * 7,
        compiler_params=pltpu.CompilerParams(vmem_limit_bytes=32 * MIB),
    )(own)


def map_outputs(g_up, g_down, others):
    count = len(others)

    def kernel(up, down, *rest):
        sources, o_up, o_down = rest[:count], rest[count], rest[count + 1]
        targets, held, sems = rest[count + 2 : 2 * count + 2], rest[2 * count + 2 : -1], rest[-1]
        loads = [pltpu.make_async_copy(a, b, sems.at[0, i]) for i, (a, b) in enumerate(zip(sources, held))]
        saves = [pltpu.make_async_copy(a, b, sems.at[1, i]) for i, (a, b) in enumerate(zip(held, targets))]
        for load in loads:
            load.start()
        o_up[...] = up[...].astype(F32)
        o_down[...] = down[...].astype(F32)
        for load, save in zip(loads, saves):
            load.wait()
            save.start()
        for save in saves:
            save.wait()

    whole = pl.BlockSpec(memory_space=pl.ANY)
    local = pl.BlockSpec(memory_space=pltpu.VMEM)
    return pl.pallas_call(
        kernel,
        out_shape=[jax.ShapeDtypeStruct(x.shape, F32) for x in (g_up, g_down, *others)],
        in_specs=[local] * 2 + [whole] * count,
        out_specs=[local] * 2 + [whole] * count,
        scratch_shapes=[pltpu.VMEM(o.shape, o.dtype) for o in others] + [pltpu.SemaphoreType.DMA((2, count))],
        compiler_params=pltpu.CompilerParams(vmem_limit_bytes=60 * MIB),
        cost_estimate=pl.CostEstimate(flops=10**9, bytes_accessed=24 * 10**6, transcendentals=0),
    )(g_up, g_down, *others)


def pack_weights(ad_gate, ad_out, ad_high, w_qkv, w_proj, w_up, w_down, devices):
    dim, width = ad_gate.shape
    share, high_rows, wide = dim // devices, ad_high.shape[0] // devices, w_up.shape[1]
    rest = high_rows - share

    def kernel(gate, out, high, qkv, proj, up, down, packed, side, side_wide, sems):
        me = lax.axis_index("dp")
        mine = pl.ds(pl.multiple_of(me * share, share), share)
        lanes = mine

        def at(i, size=width):
            return packed.at[:, pl.ds(i * width, size)]

        straight = [(gate.at[mine], at(0)), (up.at[mine], at(8, wide))]
        straight += [(qkv.at[k, mine], at(4 + k)) for k in range(3)]
        straight.append((high.at[pl.ds(pl.multiple_of(me * high_rows, rest), share)], at(2)))
        straight.append((high.at[pl.ds(pl.multiple_of(me * high_rows + share, rest), rest)], at(3).at[pl.ds(0, rest)]))
        straight += [(out.at[:, lanes], side.at[0]), (proj.at[:, lanes], side.at[1]), (down.at[:, lanes], side_wide)]
        copies = [pltpu.make_async_copy(a, b, sems.at[i]) for i, (a, b) in enumerate(straight)]
        for copy in copies:
            copy.start()
        packed[rest:, 3 * width : 4 * width] = jnp.zeros((share - rest, width), BF)
        for copy in copies:
            copy.wait()
        packed[:, width : 2 * width] = side[0].T
        packed[:, 7 * width : 8 * width] = side[1].T
        packed[:, 8 * width + wide :] = side_wide[...].T

    whole = pl.BlockSpec(memory_space=pl.ANY)
    return pl.pallas_call(
        kernel,
        out_shape=jax.ShapeDtypeStruct((share, 8 * width + 2 * wide), BF),
        in_specs=[whole] * 7,
        out_specs=pl.BlockSpec(memory_space=pltpu.VMEM),
        scratch_shapes=[
            pltpu.VMEM((2, width, share), BF), pltpu.VMEM((wide, share), BF), pltpu.SemaphoreType.DMA((10,)),
        ],
        compiler_params=pltpu.CompilerParams(vmem_limit_bytes=60 * MIB),
    )(ad_gate, ad_out, ad_high, w_qkv, w_proj, w_up, w_down)


def rows_first(x):
    return with_layout_constraint(x, Layout(major_to_minor=tuple(range(x.ndim))))


def own_part(w, axis):
    length = w.shape[axis] // lax.axis_size("dp")
    return lax.dynamic_slice_in_dim(w, lax.axis_index("dp") * length, length, axis)


def fold(w, rows):
    return w[:rows], jnp.pad(w[rows:], ((0, 2 * rows - w.shape[0]), (0, 0)))


def core_first(x, devices):
    shape = x.shape
    return x.reshape(shape[:-1] + (devices // 2, 2, -1)).swapaxes(-3, -2).reshape(shape)


def core_last(x, devices):
    shape = x.shape
    return x.reshape(shape[:-1] + (2, devices // 2, -1)).swapaxes(-3, -2).reshape(shape)


def layer_norm(values, gain):
    centre = jnp.mean(values, -1, keepdims=True)
    centred = values - centre
    variance = jnp.mean(centred * centred, -1, keepdims=True)
    return centred * lax.rsqrt(variance + 1e-06) * gain


def per_device(
    hr_in,
    low_in,
    valid,
    conv_w,
    hr_gain,
    cn_up,
    cn_down,
    ad_gate,
    ad_high,
    ad_out,
    ln1_gain,
    w_qkv,
    w_proj,
    ln2_gain,
    w_up,
    w_down,
    cot_low,
    cot_hr,
):
    _, row_count, col_count, chan_count = hr_in.shape
    devices, shards = lax.axis_size("dp"), lax.axis_size("mp")
    dims = low_in.shape[2]
    share = dims // devices
    qkv = own_part(w_qkv, 1)
    low_weights = (ad_gate, ad_out, ad_high, w_qkv, w_proj, w_up, w_down)
    pieces = [
        own_part(ad_gate, 0), own_part(ad_out, 1).T, *fold(own_part(ad_high, 0), share),
        qkv[0], qkv[1], qkv[2], own_part(w_proj, 1).T, own_part(w_up, 0), own_part(w_down, 1).T,
    ]
    if share % LANES:
        packed = rows_first(jnp.concatenate(pieces, axis=1))
    else:
        packed = pack_weights(*low_weights, devices)
    packed = rows_first(lax.all_gather(packed, "mp", axis=0, tiled=True))
    plane_mask = valid[0].astype(F32)
    cell_mask = plane_mask[..., None]
    masked = hr_in[0] * valid[0].astype(BF)[..., None]
    half_rows, half_cols = (row_count // 2, col_count // 2)
    counts = plane_mask.reshape(half_rows, 2, half_cols, 2).sum(axis=(1, 3))
    shares = 1.0 / jnp.maximum(counts, 1.0)
    size = conv_w.shape[0]
    taps = conv_w.astype(F32).reshape(size * size, 1, chan_count)
    conv_out, bordered = conv_forward(masked, taps, size, shards)
    hr_gainf = hr_gain.astype(F32)
    normed = layer_norm(conv_out * cell_mask, hr_gainf).astype(BF)
    mask_chunks, share_chunks = plane_mask.reshape(CHUNKS, -1, 1), shares.reshape(CHUNKS, -1, 1)
    normed, packed, mask_chunks, share_chunks = lax.optimization_barrier((normed, packed, mask_chunks, share_chunks))
    packed = rows_first(lax.all_gather(packed, "dp", axis=0, tiled=True))
    hr_out, pooled, normed_all, hidden_act, hidden_slope, up_t, down_t = big_forward(
        normed.reshape(row_count * col_count, chan_count), cn_up, cn_down, masked, mask_chunks, share_chunks, shards
    )
    hr_out = hr_out.reshape(hr_in.shape)
    tokens = half_rows * half_cols
    low_ins, gains = [low_in[0], pooled, cot_low[0]], [ln1_gain.astype(F32)[None], ln2_gain.astype(F32)[None]]
    if share % LANES:
        by_share = pooled.reshape(tokens, devices, -1)
        pool_a = by_share[:, :, :share].reshape(tokens, dims)
        pool_b = by_share[:, :, share:]
        pool_b = jnp.pad(pool_b, ((0, 0), (0, 0), (0, share - pool_b.shape[2]))).reshape(tokens, dims)
        low_ins = [core_first(low_in[0], devices), None, core_first(cot_low[0], devices)]
        low_ins[1] = jnp.concatenate([core_first(pool_a, devices), core_first(pool_b, devices)], axis=1)
        gains = [core_first(g, devices) for g in gains]
    low_out, d_low_in, d_pooled, g_ln1, g_ln2, low_grads = low_stage(*low_ins, *gains, packed, shards, devices, 2)
    if share % LANES:
        low_out, d_low_in = core_last(low_out, devices), core_last(d_low_in, devices)
        g_ln1, g_ln2 = core_last(g_ln1, devices), core_last(g_ln2, devices)
        d_pooled = jnp.concatenate(
            [
                core_last(d_pooled[:, :dims], devices).reshape(tokens, devices, share),
                core_last(d_pooled[:, dims:], devices).reshape(tokens, devices, share)[:, :, : by_share.shape[2] - share],
            ],
            axis=2,
        ).reshape(tokens, chan_count)
    low_out, d_low_in, g_ln1, g_ln2 = low_out[None], d_low_in[None], g_ln1[0], g_ln2[0]
    d_normed, d_map, cn_grads, low_sums = big_backward(
        cot_hr[0], d_pooled, share_chunks, mask_chunks, normed_all, hidden_act, hidden_slope,
        up_t, down_t, low_grads, shards, devices,
    )
    low_sums = rows_first(low_sums.reshape(shards, share, -1))
    low_sums = rows_first(lax.psum_scatter(low_sums, "mp", scatter_dimension=0))
    low_gains = jnp.pad(jnp.stack([g_ln1, g_ln2]), ((0, 0), (0, chan_count - dims)))
    d_hr_in, small_sums, (g_cn_up, g_cn_down) = conv_backward(
        d_normed, conv_out, hr_gainf[None], cell_mask, bordered, d_map, taps, low_gains, size, cn_grads, devices, shards
    )
    d_hr_in = d_hr_in[None]
    g_conv = small_sums[: size * size].reshape(conv_w.shape)
    g_hr_gain, g_ln1, g_ln2 = small_sums[size * size], small_sums[-2, :dims], small_sums[-1, :dims]
    g_cn_up, g_cn_down, low_out, hr_out, d_low_in, d_hr_in = map_outputs(
        g_cn_up, g_cn_down, (low_out, hr_out, d_low_in, d_hr_in)
    )
    g_ad_gate, g_ad_high, g_ad_out, g_qkv, g_proj, g_up, g_down = low_outputs(
        low_sums.reshape(share, -1), [p.shape[1] for p in pieces], ad_high.shape[0] // devices
    )
    g_cn_down = g_cn_down.T
    return (
        low_out,
        hr_out,
        d_low_in,
        d_hr_in,
        g_conv,
        g_hr_gain,
        g_cn_up,
        g_cn_down,
        g_ad_gate,
        g_ad_high,
        g_ad_out,
        g_ln1,
        g_qkv,
        g_proj,
        g_ln2,
        g_up,
        g_down,
    )


def solution(mesh):
    return jax.shard_map(
        per_device,
        mesh=mesh,
        in_specs=(
            P("dp", "mp", None, None),
            P("dp", "mp", None),
            P("dp", "mp", None),
            P(),
            P(),
            P(None, "mp"),
            P("mp", None),
            P(None, "mp"),
            P(None, "mp"),
            P("mp", None),
            P(),
            P(None, None, "mp"),
            P("mp", None),
            P(),
            P(None, "mp"),
            P("mp", None),
            P("dp", "mp", None),
            P("dp", "mp", None, None),
        ),
        out_specs=(
            P("dp", "mp", None),
            P("dp", "mp", None, None),
            P("dp", "mp", None),
            P("dp", "mp", None, None),
            P(),
            P(),
            P("dp", "mp"),
            P("mp", "dp"),
            P("dp", "mp"),
            P("dp", "mp"),
            P("mp", "dp"),
            P(),
            P(None, "dp", "mp"),
            P("mp", "dp"),
            P(),
            P("dp", "mp"),
            P("mp", "dp"),
        ),
        check_vma=False,
    )
```

```python
import jax
import jax.numpy as jnp
from jax import lax
from jax.experimental.layout import Layout, with_layout_constraint
from jax.experimental import pallas as pl
from jax.experimental.pallas import tpu as pltpu
from jax.sharding import PartitionSpec as P

HEAD = 64
LANES = 128
EDGE = 8
CHUNKS = 6
TILE = 512
MIB = 1024 * 1024
MESH = pl.DeviceIdType.MESH
BF = jnp.bfloat16
F32 = jnp.float32

def gelu_parts(x):
    c = 0.7978845608028654
    x2 = x * x
    t = jnp.tanh(c * x * (1.0 + 0.044715 * x2))
    half = 0.5 * (1.0 + t)
    slope = half + 0.5 * x * (1.0 - t * t) * (c * (1.0 + 3 * 0.044715 * x2))
    return x * half, slope


def gelu(x):
    c = 0.7978845608028654
    t = jnp.tanh(c * x * (1.0 + 0.044715 * (x * x)))
    return 0.5 * x * (1.0 + t)


def dp_bit(position):
    return lax.rem(lax.axis_index("dp") // 2**position, 2)


def dp_mate(position):
    return lax.axis_index("dp") + 2**position * (1 - 2 * dp_bit(position))


class Halving:
    def __init__(self, bits, lasts, shape, block):
        self.lasts, self.shape, self.block = lasts, shape, block
        left = list(bits)
        self.bits = [left.pop(0 if last else -1) for last in lasts]

    def split(self, count, p):
        if count == 1:
            return (1, 1)
        return (count // 2, 2) if self.lasts[p] else (2, count // 2)

    def buffers(self):
        count, rows, cols = self.shape
        got, held = [], []
        for p in range(len(self.bits)):
            count //= 2
            got.append(jax.ShapeDtypeStruct((count, rows, cols), BF))
            held.append(jax.ShapeDtypeStruct(self.split(count, p + 1) + (rows, cols), BF))
        return got + held

    def semaphores(self):
        return [pltpu.SemaphoreType.DMA((len(self.bits),))] * 2

    def bind(self, first, buffers, send, recv):
        steps = len(self.bits)
        self.now = [first] + list(buffers[steps:])
        self.got, self.send, self.recv = buffers[:steps], send, recv

    def part(self, p, mine):
        bit = dp_bit(self.bits[p])
        index = bit if mine else 1 - bit
        return self.now[p].at[:, index] if self.lasts[p] else self.now[p].at[index]

    def copy(self, p):
        return pltpu.make_async_remote_copy(
            src_ref=self.part(p, False), dst_ref=self.got[p], send_sem=self.send.at[p], recv_sem=self.recv.at[p],
            device_id={"dp": dp_mate(self.bits[p])}, device_id_type=MESH,
        )

    def start(self, p):
        self.copy(p).start()

    def finish(self, p, wait=True):
        if wait:
            self.copy(p).wait()
        count, rows, cols = self.got[p].shape
        ways = self.split(count, p + 1)

        def add(a, b, out):
            out[...] = (a[...].astype(F32) + b[...].astype(F32)).astype(BF).reshape(out.shape)

        flat = pl.BlockSpec((1, rows, self.block), lambda k, c: (k, 0, c))
        paired = pl.BlockSpec((1, 1, rows, self.block), lambda k, c: (k // ways[1], lax.rem(k, ways[1]), 0, c))
        pltpu.emit_pipeline(add, grid=(count, cols // self.block), in_specs=[flat, flat], out_specs=[paired])(
            self.part(p, True), self.got[p], self.now[p + 1]
        )


def chain_exchange(
    n, chunks, lag, gathered, partial, travel, sems, own_chunk, prepare, arrived, compute, mates=(), begin=None, turn=None, after=None, early=False
):
    ag_send, ag_recv, rs_send, rs_recv = sems
    d = lax.axis_index("mp")
    has_left, has_right = d > 0, d < n - 1

    barrier = pltpu.get_barrier_semaphore()

    @pl.when(has_left)
    def _():
        pl.semaphore_signal(barrier, inc=1, device_id={"mp": d - 1}, device_id_type=MESH)

    @pl.when(has_right)
    def _():
        pl.semaphore_signal(barrier, inc=1, device_id={"mp": d + 1}, device_id_type=MESH)

    for mate in mates:
        pl.semaphore_signal(barrier, inc=1, device_id={"dp": mate}, device_id_type=MESH)

    own_chunk(0)
    pl.semaphore_wait(barrier, has_left.astype(jnp.int32) + has_right.astype(jnp.int32) + len(mates))
    if begin is not None:
        begin()

    def ag(way, s, j):
        return pltpu.make_async_remote_copy(
            src_ref=gathered.at[s, j], dst_ref=gathered.at[s, j],
            send_sem=ag_send.at[way, s, j], recv_sem=ag_recv.at[s, j],
            device_id={"mp": d + 1 - 2 * way}, device_id_type=MESH,
        )

    def rs(way, s, j):
        there = d + 1 - 2 * way
        slot = jnp.where((s == there) & (way == 0), n, s)
        return pltpu.make_async_remote_copy(
            src_ref=travel.at[s, j], dst_ref=travel.at[slot, j],
            send_sem=rs_send.at[s, j], recv_sem=rs_recv.at[slot, j],
            device_id={"mp": there}, device_id_type=MESH,
        )

    def rs_wait(slot, j):
        pltpu.make_async_copy(travel.at[slot, j], travel.at[slot, j], rs_recv.at[slot, j]).wait()

    def first(j, _):
        @pl.when(j > 0)
        def _():
            own_chunk(j)

        @pl.when(has_right)
        def _():
            ag(0, d, j).start()

        @pl.when(has_left)
        def _():
            ag(1, d, j).start()

        return 0

    lax.fori_loop(0, chunks, first, 0)

    def flow(way, q):
        ql = jnp.clip(q, 0, n * chunks - 1)
        s, jj = ql // chunks, lax.rem(ql, chunks)
        if way == 1:
            s = n - 1 - s
        ahead = (s > d) if way == 0 else (s < d)
        source = has_left if way == 0 else has_right

        @pl.when((q >= 0) & (q < n * chunks) & (ahead | ((s == d) & source)))
        def _():
            @pl.when(source)
            def _():
                rs_wait(jnp.where(s == d, n, s) if way == 0 else s, jj)

            @pl.when(ahead & source)
            def _():
                travel[s, jj] = (partial[s, jj].astype(F32) + travel[s, jj].astype(F32)).astype(BF)

            @pl.when(ahead & jnp.logical_not(source))
            def _():
                travel[s, jj] = partial[s, jj].astype(BF)

            @pl.when(ahead)
            def _():
                rs(way, s, jj).start()

    def block_of(k, way):
        s = d - k + 2 * k * way
        return s, (s >= 0) & (s < n) & ((k > 0) | (way == 0))

    def receive(k, way, s, j):
        @pl.when(k > 0)
        def _():
            pltpu.make_async_copy(gathered.at[s, j], gathered.at[s, j], ag_recv.at[s, j]).wait()

            @pl.when((way == 0) & has_right)
            def _():
                ag(0, s, j).start()

            @pl.when((way == 1) & has_left)
            def _():
                ag(1, s, j).start()

        arrived(s, j)

    wait_one = 1 if early else 0

    def step(g, _):
        k, j = g // chunks, lax.rem(g, chunks)

        def sides(act):
            @pl.when(g < n * chunks)
            def _():
                def side(way, _):
                    s, ok = block_of(k, way)
                    pl.when(ok)(lambda: act(way, s))
                    return 0

                lax.fori_loop(0, 2, side, 0)

        def flows():
            flow(1, g - wait_one - (n - 1 - d) * lag)
            flow(0, g - wait_one - d * lag)

        if turn is not None:
            turn(g)
        if early:
            sides(lambda way, s: receive(k, way, s, j))
            flows()

            def later(way, s):
                prepare(way, s, j)
                compute(way, s, j)

            sides(later)
        else:
            def work(way, s):
                prepare(way, s, j)
                receive(k, way, s, j)
                compute(way, s, j)

            sides(work)
            flows()
        if after is not None:
            after(g)
        return 0

    lax.fori_loop(0, n * chunks + (n - 1) * lag + wait_one, step, 0)

    def drain(i, _):
        s, j = i // chunks, lax.rem(i, chunks)

        @pl.when(has_right & (s <= d))
        def _():
            ag(0, s, j).wait_send()

        @pl.when(has_left & (s >= d))
        def _():
            ag(1, s, j).wait_send()

        @pl.when(s < d)
        def _():
            rs(1, s, j).wait_send()

        @pl.when(s > d)
        def _():
            rs(0, s, j).wait_send()

        return 0

    lax.fori_loop(0, n * chunks, drain, 0)


def own_sum(n, d, j, partial, travel, total):
    total[...] = partial[d, j].astype(F32)

    @pl.when(d > 0)
    def _():
        total[...] += travel[n, j].astype(F32)

    @pl.when(d < n - 1)
    def _():
        total[...] += travel[d, j].astype(F32)


def chain_sems(n, chunks):
    dma = pltpu.SemaphoreType.DMA
    return [dma((2, n, chunks)), dma((n, chunks)), dma((n, chunks)), dma((n + 1, chunks))]


def chunk_buffers(n, rows, c, kept):
    return [
        pltpu.VMEM((n, CHUNKS, rows, c), BF),
        pltpu.VMEM((n, CHUNKS, rows, c), kept),
        pltpu.VMEM((n + 1, CHUNKS, rows, c), BF),
    ]


def columns(i):
    return pl.ds(pl.multiple_of(i * TILE, TILE), TILE)


def drain_copies(n, copy):
    def one(i, _):
        copy(i // CHUNKS, lax.rem(i, CHUNKS)).wait()
        return 0

    lax.fori_loop(0, n * CHUNKS, one, 0)


def big_forward(x, w_up, w_down, residual, mask, share, n):
    t, c = x.shape
    h = w_up.shape[1]
    rows = t // CHUNKS
    cols = residual.shape[1]
    half = cols // 2
    pairs = rows // cols // 2

    def kernel(
        x_ref, wu, wd, res, mask_ref, share_ref, out, pooled, x_all, act_all, slope_all, wu_t, wd_t,
        gathered, partial, travel, act, slope, total, folded, turned, copied, stored, load_sem, *sems
    ):
        d = lax.axis_index("mp")
        load = pltpu.make_async_copy(x_ref, gathered.at[d], load_sem)

        def own_chunk(j):
            if isinstance(j, int):
                load.start()
                load.wait()

        def x_copy(s, j):
            return pltpu.make_async_copy(gathered.at[s, j], x_all.at[s, j], copied.at[s, j])

        def prepare(way, s, j):
            pass

        def arrived(s, j):
            x_copy(s, j).start()

        def compute(way, s, j):
            block = gathered.at[s, j]

            def up(i, _):
                pre = jnp.dot(block[...], wu[:, columns(i)], preferred_element_type=F32)
                value, rate = gelu_parts(pre)
                act[:, columns(i)] = value.astype(BF)
                slope[:, columns(i)] = rate.astype(BF)
                return 0

            lax.fori_loop(0, h // TILE, up, 0)
            keep_act = pltpu.make_async_copy(act, act_all.at[s, j], stored.at[0])
            keep_slope = pltpu.make_async_copy(slope, slope_all.at[s, j], stored.at[1])
            keep_act.start()
            keep_slope.start()

            def down(i, _):
                partial[s, j, :, columns(i)] = jnp.dot(
                    act[...], wd[:, columns(i)], preferred_element_type=F32
                )
                return 0

            lax.fori_loop(0, c // TILE, down, 0)
            keep_act.wait()
            keep_slope.wait()

        def finish(j):
            pl.when(j > 0)(lambda: put(j - 1).wait())
            own_sum(n, d, j, partial, travel, total)
            values = (res[pl.ds(j * 2 * pairs, 2 * pairs)].reshape(rows, c).astype(F32) + total[...]) * mask_ref[j]
            partial[d, j] = values
            put(j).start()
            both = values.reshape(pairs, 2, cols, c)
            summed = (both[:, 0] + both[:, 1]).reshape(pairs * cols, c)
            for b in range(c // LANES):
                lanes = slice(b * LANES, (b + 1) * LANES)
                folded[b] = summed[:, lanes]
                every = folded[b, pl.ds(0, pairs * half, 2), :] + folded[b, pl.ds(1, pairs * half, 2), :]
                pooled[j, :, lanes] = every * share_ref[j]

        def put(j):
            return pltpu.make_async_copy(partial.at[d, j], out.at[j], load_sem)

        def after(g):
            last = g - (n - 1) * (CHUNKS + 1)
            pl.when(last >= 0)(lambda: finish(last))
            for i, (w, target, size) in enumerate(((wu, wu_t, h), (wd, wd_t, c))):
                late = g - n * CHUNKS // 2

                @pl.when((late >= 0) & (late < size // LANES))
                def _():
                    some = pl.ds(pl.multiple_of(late * LANES, LANES), LANES)
                    turned[i, :, pl.ds(0, w.shape[0])] = w[:, some].T
                    copy = pltpu.make_async_copy(turned.at[i, :, pl.ds(0, w.shape[0])], target.at[some], stored.at[i])
                    copy.start()
                    copy.wait()

        chain_exchange(
            n, CHUNKS, 1, gathered, partial, travel, sems, own_chunk, prepare, arrived, compute, after=after
        )

        put(CHUNKS - 1).wait()
        drain_copies(n, x_copy)

    whole = pl.BlockSpec(memory_space=pl.ANY)
    local = pl.BlockSpec(memory_space=pltpu.VMEM)
    out, pooled, x_all, act_all, slope_all, wu_t, wd_t = pl.pallas_call(
        kernel,
        out_shape=(
            jax.ShapeDtypeStruct((CHUNKS, rows, c), F32),
            jax.ShapeDtypeStruct((CHUNKS, pairs * half, c), F32),
            jax.ShapeDtypeStruct((n, CHUNKS, rows, c), BF),
            jax.ShapeDtypeStruct((n, CHUNKS, rows, h), BF),
            jax.ShapeDtypeStruct((n, CHUNKS, rows, h), BF),
            jax.ShapeDtypeStruct((h, c), BF),
            jax.ShapeDtypeStruct((c, h), BF),
        ),
        in_specs=[whole, local, local, local, local, local],
        out_specs=(whole, local, whole, whole, whole, whole, whole),
        scratch_shapes=chunk_buffers(n, rows, c, F32)
        + [pltpu.VMEM((rows, h), BF)] * 2
        + [pltpu.VMEM((rows, c), F32), pltpu.VMEM((c // LANES, pairs * cols, LANES), F32), pltpu.VMEM((2, LANES, max(c, h)), BF)]
        + [pltpu.SemaphoreType.DMA((n, CHUNKS)), pltpu.SemaphoreType.DMA((2,)), pltpu.SemaphoreType.DMA]
        + chain_sems(n, CHUNKS),
        compiler_params=pltpu.CompilerParams(
            collective_id=0, has_side_effects=True, vmem_limit_bytes=60 * MIB
        ),
        cost_estimate=pl.CostEstimate(
            flops=4 * n * t * c * h, bytes_accessed=8 * n * t * c, transcendentals=n * t * h
        ),
    )(
        x.reshape(CHUNKS, rows, c), w_up, w_down, residual,
        mask.reshape(CHUNKS, rows, 1), share.reshape(CHUNKS, pairs * half, 1),
    )
    return (
        out.reshape(t, c),
        pooled.reshape(t // 4, c),
        x_all,
        act_all,
        slope_all,
        wu_t,
        wd_t,
    )


def big_backward(cot, d_pooled, share, mask, x_all, act_all, slope_all, up_t, down_t, grads, n, devices):
    _, cols, c = cot.shape
    t = cot.shape[0] * cols
    h = up_t.shape[0]
    rows = t // CHUNKS
    half = cols // 2
    pairs_here = rows // cols // 2
    piece = c // devices
    items = n * CHUNKS // 2
    pairs, g_rows, g_cols = grads.shape
    bits = range(1, devices.bit_length() - 1)
    split = g_rows // 2
    steps = len(bits)
    plans = [Halving(bits, [last] * steps, (pairs, split, g_cols), min(g_cols, 1024)) for last in (True, False)]
    extras = [b for plan in plans for b in plan.buffers()[:-1]]
    each = 2 * steps - 1

    def kernel(
        cot_ref, pool_ref, share_ref, mask_ref, x_hbm, act_hbm, slopes, wu, wd, g_first, g_second,
        out, d_own, g_up_out, g_down_out, out_up, out_down, got_up, got_down, h_all, *rest
    ):
        sums, extra, rest = rest[0], rest[1 : 1 + 2 * each], rest[1 + 2 * each :]
        gathered, partial, travel, slope, grad, left, right, middle, g_up, g_down, total, spread_rows, addend = rest[:13]
        core_send, core_recv, stored, add_sem, send0, recv0, send1, recv1 = rest[13:21]
        sems = rest[21:]
        d = lax.axis_index("mp")
        plans[0].bind(g_first.at[:, :, pl.ds(0, split)], extra[:each] + (sums.at[0],), send0, recv0)
        plans[1].bind(g_second.at[:, :, pl.ds(split, split)], extra[each:] + (sums.at[1],), send1, recv1)

        def begin():
            for plan in plans:
                plan.start(0)

        def pass_on(p, plan):
            plan.finish(p)
            if p + 1 < steps:
                plan.start(p + 1)

        first_due = 2 * CHUNKS + 4
        ticks = {}
        if steps == 2:
            for p, start in ((0, first_due), (1, n * CHUNKS + n - 2)):
                tiles = [
                    (plan, k, q)
                    for plan in plans
                    for k in range(plan.got[p].shape[0])
                    for q in range(g_cols // plan.block)
                ]
                for m in range(0, len(tiles), 4):
                    ticks[start + m // 4] = (p, m == 0, m + 4 >= len(tiles), tiles[m : m + 4])

        def tile_copy(which, p, i, plan, k, q):
            lanes = pl.ds(q * plan.block, plan.block)
            if which == 0:
                source, target = plan.part(p, True).at[k, :, lanes], addend.at[0, i]
            elif which == 1:
                source, target = plan.got[p].at[k, :, lanes], addend.at[1, i]
            else:
                ways = plan.split(plan.got[p].shape[0], p + 1)
                source, target = addend.at[0, i], plan.now[p + 1].at[k // ways[1], k % ways[1], :, lanes]
            return pltpu.make_async_copy(source, target, add_sem.at[which, i])

        def tick_begin(p, fresh, final, tiles):
            if fresh:
                for plan in plans:
                    plan.copy(p).wait()
            for i, tile in enumerate(tiles):
                for which in range(2):
                    tile_copy(which, p, i, *tile).start()

        def tick_add(p, fresh, final, tiles):
            for i, tile in enumerate(tiles):
                for which in range(2):
                    tile_copy(which, p, i, *tile).wait()
                addend[0, i] = (addend[0, i].astype(F32) + addend[1, i].astype(F32)).astype(BF)
                tile_copy(2, p, i, *tile).start()
            for i, tile in enumerate(tiles):
                tile_copy(2, p, i, *tile).wait()
            if final and p + 1 < steps:
                for plan in plans:
                    plan.start(p + 1)

        all_steps = n * CHUNKS + n
        due = [all_steps * 9 * (2**steps - 2 ** (steps - 1 - p)) // (10 * (2**steps - 1)) // 2 * 2 for p in range(steps)]

        def turn(g):
            if ticks:
                for at, tick in ticks.items():
                    pl.when(g == at)(lambda tick=tick: tick_begin(*tick))
            else:
                for p in range(steps - 1):
                    for i, plan in enumerate(plans):
                        pl.when(g == due[p] + 2 * i)(lambda p=p, plan=plan: pass_on(p, plan))

            q, due_now = item_of(g)

            @pl.when(due_now)
            def _():
                for copy in item_copies(q):
                    copy.start()

        def own_chunk(j):
            part = pool_ref[j] * share_ref[j]
            here = cot_ref.at[pl.ds(j * 2 * pairs_here, 2 * pairs_here)]
            for b in range(c // LANES):
                lanes = slice(b * LANES, (b + 1) * LANES)
                spread_rows[b, pl.ds(0, pairs_here * half, 2), :] = part[:, lanes]
                spread_rows[b, pl.ds(1, pairs_here * half, 2), :] = part[:, lanes]
                block = jnp.broadcast_to(
                    spread_rows[b].reshape(pairs_here, 1, cols, LANES), (pairs_here, 2, cols, LANES)
                ).reshape(rows, LANES)
                cell = here[:, :, lanes].reshape(rows, LANES).astype(F32)
                gathered[d, j, :, lanes] = ((cell + block) * mask_ref[j]).astype(BF)

        def slope_copy(s, j):
            return pltpu.make_async_copy(slopes.at[s, j], slope, stored.at[0])

        def prepare(way, s, j):
            slope_copy(s, j).start()

        def arrived(s, j):
            pass

        def compute(way, s, j):
            block = gathered.at[s, j]
            slope_copy(s, j).wait()

            def up(i, _):
                back = nn(block[...], wd[:, columns(i)])
                grad[:, columns(i)] = (back * slope[:, columns(i)].astype(F32)).astype(BF)
                return 0

            lax.fori_loop(0, h // TILE, up, 0)
            half_pair = pl.ds(pl.multiple_of(lax.rem(j, 2) * rows, rows), rows)
            keep = pltpu.make_async_copy(grad, h_all.at[s, j // 2, half_pair], stored.at[1])
            keep.start()

            def down(i, _):
                partial[s, j, :, columns(i)] = nn(grad[...], wu[:, columns(i)]).astype(BF)
                return 0

            lax.fori_loop(0, c // TILE, down, 0)
            keep.wait()

        def item_place(q):
            s, jj, base = d, q, CHUNKS // 2
            for k in range(1, n):
                to_left, to_right = d - k >= 0, d + k < n
                two = to_left & to_right
                r = q - base
                here = (r >= 0) & (to_left | to_right)
                s = jnp.where(here, jnp.where(to_left & (jnp.logical_not(two) | (lax.rem(r, 2) == 0)), d - k, d + k), s)
                jj = jnp.where(here, jnp.where(two, r // 2, r), jj)
                base = base + (CHUNKS // 2) * (to_left.astype(jnp.int32) + to_right.astype(jnp.int32))
            return s, jj

        def item_copies(q):
            s, jj = item_place(q)
            return (
                pltpu.make_async_copy(x_hbm.at[s, jj], left, stored.at[2]),
                pltpu.make_async_copy(act_hbm.at[s, jj], right, stored.at[3]),
                pltpu.make_async_copy(h_all.at[s, jj], middle, stored.at[4]),
            )

        between = (d > 0) & (d < n - 1)
        middle_steps = [n * CHUNKS - items + i for i in range(items)]
        if n == 4 and CHUNKS == 6:
            middle_steps = [2, 4, 12, 13, 14, 15, 17, 19, 20, 21, 22, 23]

        def item_of(g):
            q = jnp.where(between, -1, (g - 3) // 2)
            for i, at in enumerate(middle_steps):
                q = jnp.where(between & (g == at), i, q)
            return q, (q >= 0) & (q < items) & (g >= 2) & (between | (lax.rem(g, 2) == 1))

        def after(g):
            for at, tick in ticks.items():
                pl.when(g == at)(lambda tick=tick: tick_add(*tick))
            last = g - 1 - (n - 1) * (CHUNKS + 1)
            pl.when(last >= 0)(lambda: finish(last))
            q, due_now = item_of(g)

            @pl.when(due_now)
            def _():
                s, jj = item_place(q)
                for copy in item_copies(q):
                    copy.wait()

                def tile(i, _):
                    a = columns(i)
                    g_up[a] += tn(left[:, a], middle[...])
                    db = gathered[s, pl.ds(2 * jj, 2), :, a].reshape(2 * rows, TILE)
                    g_down[a] += tn(db, right[...])
                    return 0

                lax.fori_loop(0, c // TILE, tile, 0)

            @pl.when(g == 2 * items + 2)
            def _():
                give(g_up, left, out_up, stored.at[2])
                swaps[0].start()

            @pl.when(g == 2 * items + 3)
            def _():
                give(g_down, right, out_down, stored.at[3])
                swaps[1].start()

        core = dp_bit(0)

        def result(j):
            return pltpu.make_async_copy(total, out.at[j], stored.at[5])

        def finish(j):
            pl.when(j > 0)(lambda: result(j - 1).wait())
            own_sum(n, d, j, partial, travel, total)
            result(j).start()

        def rows_at(i):
            return pl.ds(pl.multiple_of(i * piece, piece), piece)

        def give(source, stage, target, sem):
            def one(i, _):
                stage[pl.ds(0, piece)] = source[rows_at(2 * i + 1 - core)].astype(BF)
                copy = pltpu.make_async_copy(stage.at[pl.ds(0, piece)], target.at[i], sem)
                copy.start()
                copy.wait()
                return 0

            lax.fori_loop(0, devices // 2, one, 0)

        def keep_sums():
            sets = ((g_up, left, got_up, g_up_out, 2), (g_down, right, got_down, g_down_out, 3))

            def loads(i):
                return [
                    pltpu.make_async_copy(got.at[i], stage.at[pl.ds(0, piece)], stored.at[sem])
                    for _, stage, got, _, sem in sets
                ]

            def one(i, _):
                for load in loads(i):
                    load.start()
                saves = []
                for load, (source, stage, _, target, sem) in zip(loads(i), sets):
                    load.wait()
                    here = stage.at[pl.ds(0, piece)]
                    here[...] = (source[rows_at(2 * i + core)] + here[...].astype(F32)).astype(BF)
                    saves.append(pltpu.make_async_copy(here, target.at[i], stored.at[sem]))
                    saves[-1].start()
                for save in saves:
                    save.wait()
                return 0

            lax.fori_loop(0, devices // 2, one, 0)

        swaps = [
            pltpu.make_async_remote_copy(
                src_ref=src, dst_ref=dst, send_sem=core_send.at[i], recv_sem=core_recv.at[i],
                device_id={"dp": dp_mate(0)}, device_id_type=MESH,
            )
            for i, (src, dst) in enumerate(((out_up, got_up), (out_down, got_down)))
        ]
        def clear(i, _):
            some = pl.ds(pl.multiple_of(i * TILE, TILE), TILE)
            g_up[some] = jnp.zeros((TILE, h), F32)
            g_down[some] = jnp.zeros((TILE, h), F32)
            return 0

        def begin_all():
            begin()
            lax.fori_loop(0, c // TILE, clear, 0)

        chain_exchange(
            n, CHUNKS, 1, gathered, partial, travel, sems, own_chunk, prepare, arrived, compute,
            [dp_mate(b) for b in range(steps + 1)], begin_all, turn, after, True,
        )
        keep = pltpu.make_async_copy(gathered.at[d], d_own, stored.at[0])
        keep.start()
        result(CHUNKS - 1).wait()
        keep.wait()
        if not ticks:
            for plan in plans:
                pass_on(steps - 1, plan)
        for swap in swaps:
            swap.wait()
        keep_sums()

    whole = pl.BlockSpec(memory_space=pl.ANY)
    local = pl.BlockSpec(memory_space=pltpu.VMEM)
    dma = pltpu.SemaphoreType.DMA
    out, d_own, g_up, g_down, _, _, _, _, _, sums, *_ = pl.pallas_call(
        kernel,
        out_shape=(
            jax.ShapeDtypeStruct((CHUNKS, rows, c), F32),
            jax.ShapeDtypeStruct((CHUNKS, rows, c), BF),
            *[jax.ShapeDtypeStruct((devices // 2, piece, h), BF)] * 6,
            jax.ShapeDtypeStruct((n, CHUNKS // 2, 2 * rows, h), BF),
            jax.ShapeDtypeStruct((2, 1, 1, split, g_cols), BF),
            *extras,
        ),
        in_specs=[local] * 4 + [whole] * 3 + [local] * 2 + [whole] * 2,
        out_specs=(whole,) * (10 + 2 * each),
        scratch_shapes=chunk_buffers(n, rows, c, BF)
        + [
            pltpu.VMEM((rows, h), BF), pltpu.VMEM((rows, h), BF),
            pltpu.VMEM((2 * rows, c), BF), pltpu.VMEM((2 * rows, h), BF), pltpu.VMEM((2 * rows, h), BF),
            pltpu.VMEM((c, h), F32), pltpu.VMEM((c, h), F32),
            pltpu.VMEM((rows, c), F32), pltpu.VMEM((c // LANES, pairs_here * cols, LANES), F32),
            pltpu.VMEM((2, 4, split, plans[0].block), BF),
            dma((2,)), dma((2,)), dma((6,)), dma((3, 4)),
        ]
        + plans[0].semaphores() + plans[1].semaphores()
        + chain_sems(n, CHUNKS),
        compiler_params=pltpu.CompilerParams(
            collective_id=1, has_side_effects=True, vmem_limit_bytes=62 * MIB
        ),
        cost_estimate=pl.CostEstimate(
            flops=8 * n * t * c * h, bytes_accessed=8 * n * t * c, transcendentals=0
        ),
    )(
        cot, d_pooled.reshape(CHUNKS, pairs_here * half, c), share.reshape(CHUNKS, pairs_here * half, 1),
        mask.reshape(CHUNKS, rows, 1), *(v.reshape(n, CHUNKS // 2, 2 * rows, -1) for v in (x_all, act_all)),
        slope_all, up_t, down_t,
        grads.reshape(pairs // 2, 2, g_rows, g_cols), grads.reshape(2, pairs // 2, g_rows, g_cols),
    )
    return (
        out.reshape(cot.shape), d_own.reshape(cot.shape), [g_up, g_down],
        sums.reshape(g_rows, g_cols),
    )


def frame(dst, src):
    rows, cols, _ = src.shape
    dst[:, :EDGE] = jnp.zeros((rows, EDGE, LANES), F32)
    dst[:, EDGE + cols:] = jnp.zeros((rows, EDGE, LANES), F32)
    dst[:, EDGE:EDGE + cols] = src[...].astype(F32)


def correlate(out, framed, taps, size, flip, group, first=0, last=None, every=1):
    rows, cols, _ = out.shape
    reach = size // 2
    def some(k, _):
        r = first + k * every
        acc = jnp.zeros((group, cols, LANES), F32)
        for a in range(size):
            for b in range(size):
                tap = (size - 1 - a) * size + size - 1 - b if flip else a * size + b
                acc = acc + framed[pl.ds(r * group + a, group), pl.ds(EDGE - reach + b, cols), :] * taps[tap]
        out[pl.ds(r * group, group)] = acc
        return 0
    lax.fori_loop(0, (rows // group if last is None else last) - first if every == 1 else 2, some, 0)


def conv_forward(x, w, size, n):
    rows, cols, c = x.shape
    reach = size // 2

    def kernel(x_ref, w_ref, out, bordered, framed, sent, got, own):
        d = lax.axis_index("mp")
        has_up, has_down = d > 0, d < n - 1
        barrier = pltpu.get_barrier_semaphore()

        @pl.when(has_up)
        def _():
            pl.semaphore_signal(barrier, inc=1, device_id={"mp": d - 1}, device_id_type=MESH)

        @pl.when(has_down)
        def _():
            pl.semaphore_signal(barrier, inc=1, device_id={"mp": d + 1}, device_id_type=MESH)

        keep = pltpu.make_async_copy(x_ref, bordered.at[pl.ds(reach, rows)], own)
        keep.start()
        pl.semaphore_wait(barrier, has_up.astype(jnp.int32) + has_down.astype(jnp.int32))
        up = pltpu.make_async_remote_copy(
            src_ref=x_ref.at[pl.ds(0, reach)], dst_ref=bordered.at[pl.ds(reach + rows, reach)],
            send_sem=sent.at[0], recv_sem=got.at[0], device_id={"mp": d - 1}, device_id_type=MESH,
        )
        down = pltpu.make_async_remote_copy(
            src_ref=x_ref.at[pl.ds(rows - reach, reach)], dst_ref=bordered.at[pl.ds(0, reach)],
            send_sem=sent.at[1], recv_sem=got.at[1], device_id={"mp": d + 1}, device_id_type=MESH,
        )
        nothing = jnp.zeros((reach, cols, c), BF)

        @pl.when(has_up)
        def _():
            up.start()

        @pl.when(has_down)
        def _():
            down.start()

        @pl.when(d == 0)
        def _():
            bordered[:reach] = nothing

        @pl.when(d == n - 1)
        def _():
            bordered[reach + rows :] = nothing

        groups = rows // reach

        def inner(i, _):
            lanes = pl.ds(pl.multiple_of(i * LANES, LANES), LANES)
            frame(framed.at[pl.ds(reach, rows)], x_ref.at[:, :, lanes])
            correlate(out.at[:, :, lanes], framed, w_ref.at[:, :, lanes], size, False, reach, 1, groups - 1)
            return 0

        lax.fori_loop(0, c // LANES, inner, 0)
        keep.wait()

        @pl.when(has_up)
        def _():
            down.wait_recv()

        @pl.when(has_down)
        def _():
            up.wait_recv()

        def block(i, _):
            lanes = pl.ds(pl.multiple_of(i * LANES, LANES), LANES)
            frame(framed, bordered.at[:, :, lanes])
            correlate(out.at[:, :, lanes], framed, w_ref.at[:, :, lanes], size, False, reach, 0, None, groups - 1)
            return 0

        lax.fori_loop(0, c // LANES, block, 0)

        @pl.when(has_up)
        def _():
            up.wait_send()

        @pl.when(has_down)
        def _():
            down.wait_send()

    local = pl.BlockSpec(memory_space=pltpu.VMEM)
    dma = pltpu.SemaphoreType.DMA
    return pl.pallas_call(
        kernel,
        out_shape=(
            jax.ShapeDtypeStruct((rows, cols, c), F32),
            jax.ShapeDtypeStruct((rows + 2 * reach, cols, c), BF),
        ),
        in_specs=[local, local],
        out_specs=(local, local),
        scratch_shapes=[pltpu.VMEM((rows + 2 * reach, cols + 2 * EDGE, LANES), F32), dma((2,)), dma((2,)), dma],
        compiler_params=pltpu.CompilerParams(
            collective_id=5, has_side_effects=True, vmem_limit_bytes=40 * MIB
        ),
    )(x, w)


def conv_backward(d_normed, conv_out, gain, mask, bordered, d_map, w, low_gains, size, grads, devices, n):
    rows, cols, c = conv_out.shape
    reach = size // 2
    high = rows + 2 * reach
    group = 4 if rows % 4 == 0 else 1
    bits = range(1, devices.bit_length() - 1)
    steps = len(bits)
    shape = grads[0].shape
    plans = [Halving(bits, [last] * steps, shape, shape[2]) for last in (True, False)]
    each = 2 * steps
    blocks = c // LANES
    taps = size * size
    count = taps + 1 + low_gains.shape[0]
    small = -(-count // devices)
    first_due = blocks + blocks // 3
    begins = {first_due + blocks // 2 * p // (steps - 1): p for p in range(steps - 1)}
    ends = {mark + 1: p for mark, p in begins.items()}
    rounds = {blocks + 10 * blocks // 12: 1}

    def kernel(
        dn, co, gain_ref, mask_ref, w_ref, low_ref, b_hbm, dm_hbm, g0, g1, out, g_all, *rest
    ):
        extra, rest = rest[: 2 * each], rest[2 * each :]
        around, x_around, d_here, dframed, xframed, g_own, here, level, addend, sent, got, own, add_sem = rest[:13]
        ar, halving_sems = rest[13:19], rest[19:]
        plans[0].bind(g0, extra[:each], halving_sems[0], halving_sems[1])
        plans[1].bind(g1, extra[each:], halving_sems[2], halving_sems[3])
        me, d = lax.axis_index("dp"), lax.axis_index("mp")
        has_up, has_down = d > 0, d < n - 1
        barrier = pltpu.get_barrier_semaphore()

        def greet(k, _):
            pl.semaphore_signal(
                barrier, inc=1, device_id={"dp": lax.rem(me + k, devices)}, device_id_type=MESH
            )
            return 0

        lax.fori_loop(1, devices, greet, 0)
        for k in range(1, n):
            pl.semaphore_signal(barrier, inc=1, device_id={"mp": lax.rem(d + k, n)}, device_id_type=MESH)
        load_x = pltpu.make_async_copy(b_hbm, x_around, own.at[0])
        load_d = pltpu.make_async_copy(dm_hbm, d_here, own.at[1])
        load_x.start()
        load_d.start()

        def halving_loads(p, i):
            plan, count = plans[i], plans[i].got[p].shape[0]
            some = pl.ds(0, count)
            return [
                pltpu.make_async_copy(plan.part(p, True), addend.at[0, i, some], add_sem.at[0, i]),
                pltpu.make_async_copy(plan.got[p], addend.at[1, i, some], add_sem.at[1, i]),
            ]

        def halving_save(p, i, k):
            plan = plans[i]
            ways = plan.split(plan.got[p].shape[0], p + 1)
            target = plan.now[p + 1].at[k // ways[1], k % ways[1]]
            return pltpu.make_async_copy(addend.at[0, i, k], target, add_sem.at[2 + i, k])

        def halving_begin(p):
            for i, plan in enumerate(plans):
                plan.copy(p).wait()
                for load in halving_loads(p, i):
                    load.start()

        def halving_end(p):
            for i, plan in enumerate(plans):
                for load in halving_loads(p, i):
                    load.wait()
                for k in range(plan.got[p].shape[0]):
                    addend[0, i, k] = (addend[0, i, k].astype(F32) + addend[1, i, k].astype(F32)).astype(BF)
                    halving_save(p, i, k).start()
            for i, plan in enumerate(plans):
                for k in range(plan.got[p].shape[0]):
                    halving_save(p, i, k).wait()
            if p + 1 < steps:
                for plan in plans:
                    plan.start(p + 1)

        def keep(row, lanes, value):
            g_own[row // small, row % small : row % small + 1, lanes] = value

        pl.semaphore_wait(barrier, devices + n - 2)
        for plan in plans:
            plan.start(0)
        g_own[...] = jnp.zeros(g_own.shape, F32)

        def norm(r, total):
            cells = mask_ref[r]
            back, part = normalise_back(co[r] * cells, gain_ref[...], dn[r])
            around[reach + r] = (back * cells).astype(BF)
            return total + part

        keep(taps, slice(None), lax.fori_loop(0, rows, norm, jnp.zeros((1, c), F32)))
        for i in range(low_gains.shape[0]):
            keep(taps + 1 + i, slice(None), low_ref[i : i + 1])
        up = pltpu.make_async_remote_copy(
            src_ref=around.at[pl.ds(reach, reach)], dst_ref=around.at[pl.ds(reach + rows, reach)],
            send_sem=sent.at[0], recv_sem=got.at[0], device_id={"mp": d - 1}, device_id_type=MESH,
        )
        down = pltpu.make_async_remote_copy(
            src_ref=around.at[pl.ds(rows, reach)], dst_ref=around.at[pl.ds(0, reach)],
            send_sem=sent.at[1], recv_sem=got.at[1], device_id={"mp": d + 1}, device_id_type=MESH,
        )
        nothing = jnp.zeros((reach, cols, c), BF)

        @pl.when(has_up)
        def _():
            up.start()

        @pl.when(has_down)
        def _():
            down.start()

        @pl.when(d == 0)
        def _():
            around[:reach] = nothing

        @pl.when(d == n - 1)
        def _():
            around[reach + rows :] = nothing

        load_x.wait()

        def lanes_of(i):
            return pl.ds(pl.multiple_of(i * LANES, LANES), LANES)

        def kernel_block(i, _):
            lanes = lanes_of(i)
            frame(dframed.at[pl.ds(reach, rows)], around.at[pl.ds(reach, rows), :, lanes])
            frame(xframed, x_around.at[:, :, lanes])
            for a in range(size):
                def some(r, accs):
                    dv = dframed[pl.ds(reach + r * group, group), EDGE : EDGE + cols]
                    new = []
                    for b in range(size):
                        prod = dv * xframed[pl.ds(r * group + a, group), pl.ds(EDGE - reach + b, cols), :]
                        new.append(accs[b] + jnp.sum(prod.reshape(-1, 8, LANES), axis=0))
                    return tuple(new)

                accs = lax.fori_loop(
                    0, rows // group, some, tuple(jnp.zeros((8, LANES), F32) for _ in range(size))
                )
                for b in range(size):
                    keep(a * size + b, lanes, jnp.sum(accs[b], axis=0, keepdims=True))
            return 0

        def input_block(i, _):
            lanes = lanes_of(i)
            frame(dframed, around.at[:, :, lanes])
            correlate(out.at[:, :, lanes], dframed, w_ref.at[:, :, lanes], size, True, group)
            for r in range(rows):
                out[r, :, lanes] = (out[r, :, lanes] + d_here[r, :, lanes].astype(F32)) * mask_ref[r]
            return 0

        def spread(k):
            peer = lax.rem(me + k, devices)
            return pltpu.make_async_remote_copy(
                src_ref=g_own.at[peer], dst_ref=here.at[me], send_sem=ar[0].at[k], recv_sem=ar[1].at[k],
                device_id={"dp": peer}, device_id_type=MESH,
            )

        def across(k):
            return pltpu.make_async_remote_copy(
                src_ref=level.at[d], dst_ref=level.at[d], send_sem=ar[2].at[k], recv_sem=ar[3].at[k],
                device_id={"mp": lax.rem(d + k, n)}, device_id_type=MESH,
            )

        def tell(k):
            return pltpu.make_async_remote_copy(
                src_ref=g_all.at[me], dst_ref=g_all.at[me], send_sem=ar[4].at[k], recv_sem=ar[5].at[k],
                device_id={"dp": lax.rem(me + k, devices)}, device_id_type=MESH,
            )

        def all_of(length, make, act):
            def one(k, _):
                act(make(k))
                return 0

            lax.fori_loop(1, length, one, 0)

        def sum_round(p):
            if p == 0:
                here[me] = g_own[me]
                all_of(devices, spread, lambda x: x.start())
            elif p == 1:
                all_of(devices, spread, lambda x: x.wait())
                level[d] = jnp.sum(here[...], axis=0)
                all_of(n, across, lambda x: x.start())
            elif p == 2:
                all_of(n, across, lambda x: x.wait())
                g_all[me] = jnp.sum(level[...], axis=0)
                all_of(devices, tell, lambda x: x.start())
            else:
                all_of(devices, tell, lambda x: x.wait())

        marks = sorted(set(begins) | set(ends) | set(rounds) | {blocks, 2 * blocks})
        at = 0
        for mark in marks:
            if at < blocks:
                lax.fori_loop(at, min(mark, blocks), kernel_block, 0)
            else:
                lax.fori_loop(at - blocks, mark - blocks, input_block, 0)
            at = mark
            if mark in ends:
                halving_end(ends[mark])
            if mark in begins:
                halving_begin(begins[mark])
            if mark == first_due:
                sum_round(0)
            if mark == blocks:
                load_d.wait()

                @pl.when(has_up)
                def _():
                    down.wait_recv()

                @pl.when(has_down)
                def _():
                    up.wait_recv()
            if mark in rounds:
                sum_round(rounds[mark])
        sum_round(2)
        halving_begin(steps - 1)
        halving_end(steps - 1)
        sum_round(3)

        @pl.when(has_up)
        def _():
            up.wait_send()

        @pl.when(has_down)
        def _():
            down.wait_send()

    whole = pl.BlockSpec(memory_space=pl.ANY)
    local = pl.BlockSpec(memory_space=pltpu.VMEM)
    vm, dma = pltpu.VMEM, pltpu.SemaphoreType.DMA
    d_in, g_all, *extra = pl.pallas_call(
        kernel,
        out_shape=(
            jax.ShapeDtypeStruct((rows, cols, c), F32),
            jax.ShapeDtypeStruct((devices, small, c), F32),
            *plans[0].buffers(),
            *plans[1].buffers(),
        ),
        in_specs=[local] * 6 + [whole] * 4,
        out_specs=(local,) * 2 + (whole,) * (2 * each),
        scratch_shapes=[
            vm((high, cols, c), BF), vm((high, cols, c), BF), vm((rows, cols, c), BF),
            vm((high, cols + 2 * EDGE, LANES), F32), vm((high, cols + 2 * EDGE, LANES), F32),
            vm((devices, small, c), F32), vm((devices, small, c), F32), vm((n, small, c), F32),
            vm((2, 2, shape[0] // 2) + shape[1:], BF),
            dma((2,)), dma((2,)), dma((2,)), dma((4, max(2, shape[0] // 2))),
            dma((devices,)), dma((devices,)), dma((n,)), dma((n,)), dma((devices,)), dma((devices,)),
        ]
        + plans[0].semaphores() + plans[1].semaphores(),
        compiler_params=pltpu.CompilerParams(
            collective_id=3, has_side_effects=True, vmem_limit_bytes=50 * MIB
        ),
        cost_estimate=pl.CostEstimate(flops=6 * 10**10, bytes_accessed=10**8, transcendentals=0),
    )(
        d_normed, conv_out, gain, mask, w, low_gains, bordered, d_map,
        grads[0].reshape((shape[0] // 2, 2) + shape[1:]), grads[1].reshape((2, shape[0] // 2) + shape[1:]),
    )
    sums = g_all.reshape(devices * small, c)[:count]
    return d_in, sums, [extra[each - 1].reshape(shape[1:]), extra[2 * each - 1].reshape(shape[1:])]


GATE, OUT, HIGH_A, HIGH_B, QUERY, KEY, VALUE, PROJ = range(8)
L_LOW, L_DF, L_POOL_A, L_POOL_B, L_FIRST, L_DA, L_SECOND, L_COT = range(8)
R_DGATE, R_MERGE, R_DHIGH, R_DQ, R_DK, R_DV, R_ATT, R_DUP, R_ACT = range(9)


def nn(a, b):
    return jnp.dot(a, b, preferred_element_type=F32)


def nt(a, b):
    return lax.dot_general(a, b, (((1,), (1,)), ((), ())), preferred_element_type=F32)


def tn(a, b):
    return lax.dot_general(a, b, (((0,), (0,)), ((), ())), preferred_element_type=F32)


def normalise(x, gain):
    centred = x - jnp.mean(x, -1, keepdims=True)
    rate = lax.rsqrt(jnp.mean(centred * centred, -1, keepdims=True) + 1e-06)
    return centred * rate * gain


def normalise_back(x, gain, d):
    centred = x - jnp.mean(x, -1, keepdims=True)
    rate = lax.rsqrt(jnp.mean(centred * centred, -1, keepdims=True) + 1e-06)
    hat = centred * rate
    dg = d * gain
    back = rate * (dg - jnp.mean(dg, -1, keepdims=True) - hat * jnp.mean(dg * hat, -1, keepdims=True))
    return back, jnp.sum(d * hat, axis=0, keepdims=True)


def low_stage(low, pooled, cot, gain1, gain2, packed, n, devices, cid):
    t, dim = low.shape
    every = n * t
    width = dim // n
    heads = width // HEAD
    groups = width // LANES
    pairs = devices // 2
    rows = dim // devices
    half = dim // 2
    ff = 4 * dim
    natural = rows % LANES == 0
    high_rows = pooled.shape[1] // devices

    def place_of(k):
        return (k % 2) * half + k // 2 * rows

    def in_order(ref):
        if not natural:
            return ref[...]
        order = sorted(range(devices), key=place_of)
        return jnp.concatenate([ref[:, k * rows : (k + 1) * rows] for k in order], axis=1)

    scale = HEAD ** (-0.5)

    def kernel(
        low_ref, pooled_ref, cot_ref, gain1_ref, gain2_ref, w_hbm,
        low_out, d_low, d_pooled, g_ln1, g_ln2, grads,
        wv, lhs, lhs2, rhs, gate, high, merged, resid, d_res, slope, mixed, heads_in, att_all, d_att, d_mixed,
        d_heads, probs, d_scores, stage, left, w_sem, q_send, q_got, a_send, a_got, b_send, b_got, c_send, c_got, own_sem,
        l_send, l_got, r_send, r_got, stage_sem,
    ):
        d = lax.axis_index("mp")
        dp = lax.axis_index("dp")
        core = lax.rem(dp, 2)
        mate = dp + 1 - 2 * core
        barrier = pltpu.get_barrier_semaphore()
        for k in range(1, n):
            pl.semaphore_signal(barrier, inc=1, device_id={"mp": lax.rem(d + k, n)}, device_id_type=MESH)
        pl.semaphore_signal(barrier, inc=1, device_id={"dp": mate}, device_id_type=MESH)

        def w_copy(w, k):
            c, z = k // n, lax.rem(k, n)
            wide, base, at = w_place(w)
            src = w_hbm.at[:, c, z, :, pl.ds(base, wide)]
            dst = wv.at[c, :, :, pl.ds(pl.multiple_of(at + z * wide, wide), wide)]
            return pltpu.make_async_copy(src, dst, w_sem.at[w, k])

        def w_place(w):
            if w < 8:
                return width, w * width, w * dim
            return ff // n, 8 * width + (w - 8) * ff // n, 8 * dim + (w - 8) * ff

        def w_each(w, act):
            def one(k, _):
                act(w_copy(w, k))
                return 0

            lax.fori_loop(0, 2 * n, one, 0)

        for w in (GATE, HIGH_A, HIGH_B, OUT, QUERY, KEY, VALUE, PROJ):
            w_each(w, lambda copy: copy.start())

        def w_wait(*which):
            for w in which:
                w_each(w, lambda copy: copy.wait())

        def w_cols(at, size):
            return wv[:, :, :, pl.ds(at, size)].reshape(dim, size)

        def forward(x, first, count, put):
            def one(i, _):
                put(pl.multiple_of(i * TILE, TILE), nn(x, w_cols(pl.multiple_of(first * dim + i * TILE, TILE), TILE)))
                return 0
            lax.fori_loop(0, count * dim // TILE, one, 0)

        def backward(get, first, count, dst, fresh):
            def one(i, _):
                for c in range(2):
                    part = wv[c, :, :, pl.ds(pl.multiple_of((first + i) * dim, dim), dim)].reshape(half, dim)
                    y = nt(get(pl.multiple_of(i * dim, dim)), part)
                    cols = slice(c * half, (c + 1) * half)
                    if fresh and count == 1:
                        dst[:, cols] = y
                    else:
                        dst[:, cols] += y
                return 0
            if fresh and count > 1:
                dst[...] = jnp.zeros(dst.shape, F32)
            if count == 1:
                one(0, 0)
            else:
                lax.fori_loop(0, count, one, 0)

        def r_cols(block, count=1):
            return pl.ds(block * dim, count * dim)

        def r_at(block):
            return block * dim if block <= R_DUP else block * dim + 3 * dim

        def r_copy(block):
            cols = pl.ds(r_at(block), dim if block < R_DUP else ff)
            return pltpu.make_async_remote_copy(
                src_ref=rhs.at[0, :, cols], dst_ref=rhs.at[1, :, cols], send_sem=r_send.at[block],
                recv_sem=r_got.at[block], device_id={"dp": mate}, device_id_type=MESH)

        def l_copy(i):
            return pltpu.make_async_remote_copy(
                src_ref=lhs.at[i, :, pl.ds(pl.multiple_of((1 - core) * half, half), half)], dst_ref=lhs2.at[i],
                send_sem=l_send.at[i], recv_sem=l_got.at[i], device_id={"dp": mate}, device_id_type=MESH)

        stored = []
        turned = [None]

        def put_natural(dst, value):
            if natural:
                for k in range(devices):
                    dst[:, k * rows : (k + 1) * rows] = value[:, place_of(k) : place_of(k) + rows]
            else:
                dst[...] = value

        def grad(i, block, at, count, shared=False):
            if not shared:
                r_copy(block).wait_recv()
            if turned[0] != i:
                left[0] = lhs[i, :, pl.ds(pl.multiple_of(core * half, half), half)].T
                left[1] = lhs2[i].T
                turned[0] = i

            wide, base, first = w_place(at if at < 8 else 8 + (at - 8) * dim // ff)
            piece = min(TILE, wide)

            def out_copies(slot, k):
                out = []
                for q in range(TILE // piece):
                    z, col = divmod(at * dim - first + k * TILE + q * piece, wide)
                    out.append(
                        pltpu.make_async_copy(
                            stage.at[slot, :, :, pl.ds(q * piece, piece)],
                            grads.at[:, pl.ds(z * rows, rows), pl.ds(base + col, piece)],
                            stage_sem.at[slot, q],
                        )
                    )
                return out

            for k in range(count * dim // TILE):
                slot = len(stored) % 2
                if len(stored) >= 2:
                    wait(stored[-2])
                cols = pl.ds(r_at(block) + k * TILE, TILE)
                y = nn(left[0], rhs[0, :, cols]) + nn(left[1], rhs[1, :, cols])
                stage[slot] = y.astype(BF).reshape(pairs, rows, TILE)
                stored.append(out_copies(slot, k))
                start(stored[-1])

        def to_heads(k, src, dst, send, got):
            out = []
            for step in range(1, n):
                peer = lax.rem(d + step, n)
                out.append(pltpu.make_async_remote_copy(
                    src_ref=src.at[:, pl.ds(pl.multiple_of(peer * width, width), width)],
                    dst_ref=dst.at[pl.ds(pl.multiple_of(d * t, t), t)],
                    send_sem=send.at[k, step], recv_sem=got.at[k, step], device_id={"mp": peer}, device_id_type=MESH))
            out.append(pltpu.make_async_copy(
                src.at[:, pl.ds(pl.multiple_of(d * width, width), width)], dst.at[pl.ds(pl.multiple_of(d * t, t), t)], own_sem.at[k]))
            return out

        def to_tokens(k, src, dst, send, got, group):
            out = []
            slot = k * groups + group
            lanes = pl.ds(group * LANES, LANES)
            there = pl.ds(pl.multiple_of(d * width + group * LANES, LANES), LANES)
            for step in range(1, n):
                peer = lax.rem(d + step, n)
                out.append(pltpu.make_async_remote_copy(
                    src_ref=src.at[pl.ds(pl.multiple_of(peer * t, t), t), lanes], dst_ref=dst.at[:, there],
                    send_sem=send.at[slot, step], recv_sem=got.at[slot, step], device_id={"mp": peer}, device_id_type=MESH))
            out.append(pltpu.make_async_copy(
                src.at[pl.ds(pl.multiple_of(d * t, t), t), lanes], dst.at[:, there], own_sem.at[slot]))
            return out

        def start(copies):
            for c in copies:
                c.start()

        def wait(copies):
            for c in copies:
                c.wait()

        gain1_here, gain2_here = in_order(gain1_ref), in_order(gain2_ref)
        if natural:
            for i, ref in ((L_LOW, low_ref), (L_COT, cot_ref)):
                for k in range(devices):
                    lhs[i, :, place_of(k) : place_of(k) + rows] = ref[:, k * rows : (k + 1) * rows]
            for k in range(devices):
                own = slice(place_of(k), place_of(k) + rows)
                lhs[L_POOL_A, :, own] = pooled_ref[:, k * high_rows : k * high_rows + rows].astype(BF)
                more = pooled_ref[:, k * high_rows + rows : (k + 1) * high_rows].astype(BF)
                lhs[L_POOL_B, :, own] = jnp.concatenate([more, jnp.zeros((t, 2 * rows - high_rows), BF)], axis=1)
        else:
            lhs[L_LOW] = low_ref[...]
            lhs[L_COT] = cot_ref[...]
            lhs[L_POOL_A] = pooled_ref[:, :dim].astype(BF)
            lhs[L_POOL_B] = pooled_ref[:, dim:].astype(BF)
        acc = d_low
        w_wait(GATE)

        def put_gate(at, y):
            gate[:, pl.ds(at, TILE)] = 1.0 / (1.0 + jnp.exp(-y))
        forward(lhs[L_LOW], GATE, 1, put_gate)
        w_wait(HIGH_A, HIGH_B, OUT)
        for w in (8, 9):
            w_each(w, lambda copy: copy.start())

        def put_high(at, y):
            high[:, pl.ds(at, TILE)] = y
        forward(lhs[L_POOL_A], HIGH_A, 1, put_high)

        def put_merging(at, y):
            cols = pl.ds(at, TILE)
            total = high[:, cols] + y
            high[:, cols] = total
            rhs[0, :, pl.ds(R_MERGE * dim + at, TILE)] = (total * gate[:, cols]).astype(BF)
        forward(lhs[L_POOL_B], HIGH_B, 1, put_merging)
        backward(lambda at: rhs[0, :, r_cols(R_MERGE)], OUT, 1, merged, True)
        merged[...] += lhs[L_LOW].astype(F32)
        lhs[L_FIRST] = normalise(merged[...], gain1_here).astype(BF)

        w_wait(QUERY, KEY, VALUE, PROJ)
        pl.semaphore_wait(barrier, n)
        for i in (L_LOW, L_POOL_A, L_POOL_B, L_COT, L_FIRST):
            l_copy(i).start()
        r_copy(R_MERGE).start()
        out_q = []
        for k in range(3):
            def put_mixed(at, y):
                mixed[k, :, pl.ds(at, TILE)] = y.astype(BF)
            forward(lhs[L_FIRST], QUERY + k, 1, put_mixed)
            copies = to_heads(k, mixed.at[k], heads_in.at[k], q_send, q_got)
            start(copies)
            out_q.append(copies)
        wait(out_q[0] + out_q[1])

        for h in range(heads):
            lanes = slice(h * HEAD, (h + 1) * HEAD)

            def rows_of(b, _):
                some = pl.ds(pl.multiple_of(b * t, t), t)
                s = nt(heads_in[0, some, lanes], heads_in[1, :, lanes]) * scale
                e = jnp.exp(s - jnp.max(s, -1, keepdims=True))
                p = (e * (1.0 / jnp.sum(e, -1, keepdims=True))).astype(BF)
                probs[h, some] = p
                return 0
            lax.fori_loop(0, n, rows_of, 0)
        wait(out_q[2])
        out_a = []
        for h in range(heads):
            lanes = slice(h * HEAD, (h + 1) * HEAD)

            def attend(b, _):
                some = pl.ds(pl.multiple_of(b * t, t), t)
                att_all[some, lanes] = nn(probs[h, some], heads_in[2, :, lanes]).astype(BF)
                return 0
            lax.fori_loop(0, n, attend, 0)
            if (h + 1) * HEAD % LANES == 0:
                copies = to_tokens(0, att_all, rhs.at[0, :, r_cols(R_ATT)], a_send, a_got, h * HEAD // LANES)
                start(copies)
                out_a += copies
        wait(out_a)
        r_copy(R_ATT).start()
        backward(lambda at: rhs[0, :, r_cols(R_ATT)], PROJ, 1, resid, True)
        resid[...] += merged[...]
        lhs[L_SECOND] = normalise(resid[...], gain2_here).astype(BF)
        l_copy(L_SECOND).start()

        w_wait(8)

        def put_up(at, y):
            value, rate = gelu_parts(y)
            rhs[0, :, pl.ds(r_at(R_ACT) + at, TILE)] = value.astype(BF)
            slope[:, pl.ds(at, TILE)] = rate.astype(BF)
        forward(lhs[L_SECOND], 8, 4, put_up)
        r_copy(R_ACT).start()
        w_wait(9)
        backward(lambda at: rhs[0, :, pl.ds(r_at(R_ACT) + at, dim)], 12, 4, acc, True)
        put_natural(low_out, resid[...] + acc[...])

        def put_d_up(at, y):
            rhs[0, :, pl.ds(r_at(R_DUP) + at, TILE)] = (y * slope[:, pl.ds(at, TILE)].astype(F32)).astype(BF)
        forward(lhs[L_COT], 12, 4, put_d_up)
        r_copy(R_DUP).start()
        backward(lambda at: rhs[0, :, pl.ds(r_at(R_DUP) + at, dim)], 8, 4, acc, True)
        back, g = normalise_back(resid[...], gain2_here, acc[...])
        put_natural(g_ln2, g)
        d_res[...] = lhs[L_COT].astype(F32) + back
        lhs[L_DA] = d_res[...].astype(BF)
        l_copy(L_DA).start()

        def put_d_att(at, y):
            mixed[0, :, pl.ds(at, TILE)] = y.astype(BF)
        forward(lhs[L_DA], PROJ, 1, put_d_att)
        out_b = to_heads(0, mixed.at[0], d_att, b_send, b_got)
        start(out_b)
        l_copy(L_COT).wait_recv()
        grad(L_COT, R_ACT, 12, 4)
        wait(out_b)
        out_c = []

        def send_back(k, h):
            if (h + 1) * HEAD % LANES == 0:
                copies = to_tokens(k, d_heads.at[k], rhs.at[0, :, r_cols(R_DQ + k)], c_send, c_got, h * HEAD // LANES)
                start(copies)
                out_c.extend(copies)

        for h in range(heads):
            lanes = slice(h * HEAD, (h + 1) * HEAD)
            d_heads[2, :, lanes] = tn(probs[h], d_att[:, lanes]).astype(BF)
            send_back(2, h)
        for h in range(heads):
            lanes = slice(h * HEAD, (h + 1) * HEAD)

            def rows_of(b, _):
                some = pl.ds(pl.multiple_of(b * t, t), t)
                p = probs[h, some].astype(F32)
                dp_ = nt(d_att[some, lanes], heads_in[2, :, lanes])
                ds = (p * (dp_ - jnp.sum(dp_ * p, -1, keepdims=True)) * scale).astype(BF)
                d_scores[some] = ds
                d_heads[0, some, lanes] = nn(ds, heads_in[1, :, lanes]).astype(BF)
                return 0
            lax.fori_loop(0, n, rows_of, 0)
            d_heads[1, :, lanes] = tn(d_scores[...], heads_in[0, :, lanes]).astype(BF)
            send_back(0, h)
            send_back(1, h)
        l_copy(L_SECOND).wait_recv()
        grad(L_SECOND, R_DUP, 8, 4)
        l_copy(L_DA).wait_recv()
        grad(L_DA, R_ATT, PROJ, 1)
        wait(out_c)
        for k in range(3):
            r_copy(R_DQ + k).start()
        backward(lambda at: rhs[0, :, pl.ds(R_DQ * dim + at, dim)], QUERY, 3, acc, True)
        back, g = normalise_back(merged[...], gain1_here, acc[...])
        put_natural(g_ln1, g)
        d_res[...] += back
        lhs[L_DF] = d_res[...].astype(BF)
        l_copy(L_DF).start()

        def put_d_gate(at, y):
            cols = pl.ds(at, TILE)
            gv = gate[:, cols]
            part = y * gv
            rhs[0, :, pl.ds(R_DHIGH * dim + at, TILE)] = part.astype(BF)
            rhs[0, :, pl.ds(R_DGATE * dim + at, TILE)] = (part * high[:, cols] * (1.0 - gv)).astype(BF)
        forward(lhs[L_DF], OUT, 1, put_d_gate)
        r_copy(R_DHIGH).start()
        r_copy(R_DGATE).start()
        backward(lambda at: rhs[0, :, r_cols(R_DHIGH)], HIGH_A, 1, gate, True)
        backward(lambda at: rhs[0, :, r_cols(R_DHIGH)], HIGH_B, 1, high, True)
        if natural:
            for k in range(devices):
                at = place_of(k)
                d_pooled[:, k * high_rows : k * high_rows + rows] = gate[:, at : at + rows]
                d_pooled[:, k * high_rows + rows : (k + 1) * high_rows] = high[:, at : at + high_rows - rows]
        else:
            d_pooled[:, :dim] = gate[...]
            d_pooled[:, dim:] = high[...]
        backward(lambda at: rhs[0, :, r_cols(R_DGATE)], GATE, 1, acc, True)
        put_natural(d_low, d_res[...] + acc[...])
        l_copy(L_FIRST).wait_recv()
        for k in range(3):
            grad(L_FIRST, R_DQ + k, QUERY + k, 1)
        l_copy(L_DF).wait_recv()
        grad(L_DF, R_MERGE, OUT, 1)
        l_copy(L_POOL_A).wait_recv()
        grad(L_POOL_A, R_DHIGH, HIGH_A, 1)
        l_copy(L_POOL_B).wait_recv()
        grad(L_POOL_B, R_DHIGH, HIGH_B, 1, shared=True)
        l_copy(L_LOW).wait_recv()
        grad(L_LOW, R_DGATE, GATE, 1)
        wait(stored[-2])
        wait(stored[-1])
        for i in range(8):
            l_copy(i).wait_send()
        for b in range(9):
            r_copy(b).wait_send()

    whole = pl.BlockSpec(memory_space=pl.ANY)
    local = pl.BlockSpec(memory_space=pltpu.VMEM)
    vm, dma = pltpu.VMEM, pltpu.SemaphoreType.DMA
    tok = jax.ShapeDtypeStruct((t, dim), F32)
    one = jax.ShapeDtypeStruct((1, dim), F32)
    return pl.pallas_call(
        kernel,
        out_shape=(tok, tok, jax.ShapeDtypeStruct(pooled.shape, F32), one, one, jax.ShapeDtypeStruct((pairs, n * rows, 16 * width), BF)),
        in_specs=[local] * 5 + [whole],
        out_specs=(local,) * 5 + (whole,),
        scratch_shapes=[
            vm((2, pairs, rows, 16 * dim), BF), vm((8, t, dim), BF), vm((8, t, half), BF), vm((2, t, 15 * dim), BF),
            vm((t, dim), F32), vm((t, dim), F32), vm((t, dim), F32), vm((t, dim), F32), vm((t, dim), F32),
            vm((t, ff), BF), vm((3, t, dim), BF), vm((3, every, width), BF), vm((every, width), BF), vm((every, width), BF),
            vm((1, 8, 128), BF), vm((3, every, width), BF), vm((heads, every, every), BF), vm((every, every), BF),
            vm((2, pairs, rows, TILE), BF), vm((2, half, t), BF),
            dma((10, 2 * n)), dma((3, n)), dma((3, n)), dma((groups, n)), dma((groups, n)), dma((1, n)), dma((1, n)),
            dma((3 * groups, n)), dma((3 * groups, n)), dma((3 * groups,)), dma((8,)), dma((8,)), dma((9,)), dma((9,)), dma((2, 2)),
        ],
        compiler_params=pltpu.CompilerParams(collective_id=cid, has_side_effects=True, vmem_limit_bytes=62 * MIB),
        cost_estimate=pl.CostEstimate(flops=14 * 10**9, bytes_accessed=70 * 10**6, transcendentals=10**7),
    )(low, pooled, cot, gain1, gain2, packed.reshape(pairs, 2, n, rows, 16 * width))
def low_outputs(own, widths, high_rows):
    share = own.shape[0]
    width, wide = widths[0], widths[-1]

    def kernel(x, gate, high, out, qkv, proj, up, down):
        def part(i, size=width):
            at = sum(widths[:i])
            return x[:, at : at + size].astype(F32)

        gate[...] = part(0)
        out[...] = part(1).T
        high[:share] = part(2)
        high[share:] = part(3)[: high_rows - share]
        for k in range(3):
            qkv[k] = part(4 + k)
        proj[...] = part(7).T
        up[...] = part(8, wide)
        down[...] = part(9, wide).T

    local = pl.BlockSpec(memory_space=pltpu.VMEM)
    shapes = [
        (share, width), (high_rows, width), (width, share), (3, share, width), (width, share), (share, wide), (wide, share),
    ]
    return pl.pallas_call(
        kernel,
        out_shape=[jax.ShapeDtypeStruct(s, F32) for s in shapes],
        in_specs=[local],
        out_specs=[local] * 7,
        compiler_params=pltpu.CompilerParams(vmem_limit_bytes=32 * MIB),
    )(own)


def map_outputs(g_up, g_down, others):
    count = len(others)

    def kernel(up, down, *rest):
        sources, o_up, o_down = rest[:count], rest[count], rest[count + 1]
        targets, held, sems = rest[count + 2 : 2 * count + 2], rest[2 * count + 2 : -1], rest[-1]
        loads = [pltpu.make_async_copy(a, b, sems.at[0, i]) for i, (a, b) in enumerate(zip(sources, held))]
        saves = [pltpu.make_async_copy(a, b, sems.at[1, i]) for i, (a, b) in enumerate(zip(held, targets))]
        for load in loads:
            load.start()
        o_up[...] = up[...].astype(F32)
        o_down[...] = down[...].astype(F32)
        for load, save in zip(loads, saves):
            load.wait()
            save.start()
        for save in saves:
            save.wait()

    whole = pl.BlockSpec(memory_space=pl.ANY)
    local = pl.BlockSpec(memory_space=pltpu.VMEM)
    return pl.pallas_call(
        kernel,
        out_shape=[jax.ShapeDtypeStruct(x.shape, F32) for x in (g_up, g_down, *others)],
        in_specs=[local] * 2 + [whole] * count,
        out_specs=[local] * 2 + [whole] * count,
        scratch_shapes=[pltpu.VMEM(o.shape, o.dtype) for o in others] + [pltpu.SemaphoreType.DMA((2, count))],
        compiler_params=pltpu.CompilerParams(vmem_limit_bytes=60 * MIB),
        cost_estimate=pl.CostEstimate(flops=10**9, bytes_accessed=24 * 10**6, transcendentals=0),
    )(g_up, g_down, *others)


def pack_weights(ad_gate, ad_out, ad_high, w_qkv, w_proj, w_up, w_down, devices):
    dim, width = ad_gate.shape
    share, high_rows, wide = dim // devices, ad_high.shape[0] // devices, w_up.shape[1]
    rest = high_rows - share

    def kernel(gate, out, high, qkv, proj, up, down, packed, side, side_wide, sems):
        me = lax.axis_index("dp")
        mine = pl.ds(pl.multiple_of(me * share, share), share)
        lanes = mine

        def at(i, size=width):
            return packed.at[:, pl.ds(i * width, size)]

        straight = [(gate.at[mine], at(0)), (up.at[mine], at(8, wide))]
        straight += [(qkv.at[k, mine], at(4 + k)) for k in range(3)]
        straight.append((high.at[pl.ds(pl.multiple_of(me * high_rows, rest), share)], at(2)))
        straight.append((high.at[pl.ds(pl.multiple_of(me * high_rows + share, rest), rest)], at(3).at[pl.ds(0, rest)]))
        straight += [(out.at[:, lanes], side.at[0]), (proj.at[:, lanes], side.at[1]), (down.at[:, lanes], side_wide)]
        copies = [pltpu.make_async_copy(a, b, sems.at[i]) for i, (a, b) in enumerate(straight)]
        for copy in copies:
            copy.start()
        packed[rest:, 3 * width : 4 * width] = jnp.zeros((share - rest, width), BF)
        for copy in copies:
            copy.wait()
        packed[:, width : 2 * width] = side[0].T
        packed[:, 7 * width : 8 * width] = side[1].T
        packed[:, 8 * width + wide :] = side_wide[...].T

    whole = pl.BlockSpec(memory_space=pl.ANY)
    return pl.pallas_call(
        kernel,
        out_shape=jax.ShapeDtypeStruct((share, 8 * width + 2 * wide), BF),
        in_specs=[whole] * 7,
        out_specs=pl.BlockSpec(memory_space=pltpu.VMEM),
        scratch_shapes=[
            pltpu.VMEM((2, width, share), BF), pltpu.VMEM((wide, share), BF), pltpu.SemaphoreType.DMA((10,)),
        ],
        compiler_params=pltpu.CompilerParams(vmem_limit_bytes=60 * MIB),
    )(ad_gate, ad_out, ad_high, w_qkv, w_proj, w_up, w_down)


def rows_first(x):
    return with_layout_constraint(x, Layout(major_to_minor=tuple(range(x.ndim))))


def own_part(w, axis):
    length = w.shape[axis] // lax.axis_size("dp")
    return lax.dynamic_slice_in_dim(w, lax.axis_index("dp") * length, length, axis)


def fold(w, rows):
    return w[:rows], jnp.pad(w[rows:], ((0, 2 * rows - w.shape[0]), (0, 0)))


def core_first(x, devices):
    shape = x.shape
    return x.reshape(shape[:-1] + (devices // 2, 2, -1)).swapaxes(-3, -2).reshape(shape)


def core_last(x, devices):
    shape = x.shape
    return x.reshape(shape[:-1] + (2, devices // 2, -1)).swapaxes(-3, -2).reshape(shape)


def layer_norm(values, gain):
    centre = jnp.mean(values, -1, keepdims=True)
    centred = values - centre
    variance = jnp.mean(centred * centred, -1, keepdims=True)
    return centred * lax.rsqrt(variance + 1e-06) * gain


def per_device(
    hr_in,
    low_in,
    valid,
    conv_w,
    hr_gain,
    cn_up,
    cn_down,
    ad_gate,
    ad_high,
    ad_out,
    ln1_gain,
    w_qkv,
    w_proj,
    ln2_gain,
    w_up,
    w_down,
    cot_low,
    cot_hr,
):
    _, row_count, col_count, chan_count = hr_in.shape
    devices, shards = lax.axis_size("dp"), lax.axis_size("mp")
    dims = low_in.shape[2]
    share = dims // devices
    qkv = own_part(w_qkv, 1)
    low_weights = (ad_gate, ad_out, ad_high, w_qkv, w_proj, w_up, w_down)
    pieces = [
        own_part(ad_gate, 0), own_part(ad_out, 1).T, *fold(own_part(ad_high, 0), share),
        qkv[0], qkv[1], qkv[2], own_part(w_proj, 1).T, own_part(w_up, 0), own_part(w_down, 1).T,
    ]
    if share % LANES:
        packed = rows_first(jnp.concatenate(pieces, axis=1))
    else:
        packed = pack_weights(*low_weights, devices)
    packed = rows_first(lax.all_gather(packed, "mp", axis=0, tiled=True))
    plane_mask = valid[0].astype(F32)
    cell_mask = plane_mask[..., None]
    masked = hr_in[0] * valid[0].astype(BF)[..., None]
    half_rows, half_cols = (row_count // 2, col_count // 2)
    counts = plane_mask.reshape(half_rows, 2, half_cols, 2).sum(axis=(1, 3))
    shares = 1.0 / jnp.maximum(counts, 1.0)
    size = conv_w.shape[0]
    taps = conv_w.astype(F32).reshape(size * size, 1, chan_count)
    conv_out, bordered = conv_forward(masked, taps, size, shards)
    hr_gainf = hr_gain.astype(F32)
    normed = layer_norm(conv_out * cell_mask, hr_gainf).astype(BF)
    normed, packed = lax.optimization_barrier((normed, packed))
    packed = rows_first(lax.all_gather(packed, "dp", axis=0, tiled=True))
    hr_out, pooled, normed_all, hidden_act, hidden_slope, up_t, down_t = big_forward(
        normed.reshape(row_count * col_count, chan_count), cn_up, cn_down, masked, plane_mask, shares, shards
    )
    hr_out = hr_out.reshape(hr_in.shape)
    tokens = half_rows * half_cols
    low_ins, gains = [low_in[0], pooled, cot_low[0]], [ln1_gain.astype(F32)[None], ln2_gain.astype(F32)[None]]
    if share % LANES:
        by_share = pooled.reshape(tokens, devices, -1)
        pool_a = by_share[:, :, :share].reshape(tokens, dims)
        pool_b = by_share[:, :, share:]
        pool_b = jnp.pad(pool_b, ((0, 0), (0, 0), (0, share - pool_b.shape[2]))).reshape(tokens, dims)
        low_ins = [core_first(low_in[0], devices), None, core_first(cot_low[0], devices)]
        low_ins[1] = jnp.concatenate([core_first(pool_a, devices), core_first(pool_b, devices)], axis=1)
        gains = [core_first(g, devices) for g in gains]
    low_out, d_low_in, d_pooled, g_ln1, g_ln2, low_grads = low_stage(*low_ins, *gains, packed, shards, devices, 2)
    if share % LANES:
        low_out, d_low_in = core_last(low_out, devices), core_last(d_low_in, devices)
        g_ln1, g_ln2 = core_last(g_ln1, devices), core_last(g_ln2, devices)
        d_pooled = jnp.concatenate(
            [
                core_last(d_pooled[:, :dims], devices).reshape(tokens, devices, share),
                core_last(d_pooled[:, dims:], devices).reshape(tokens, devices, share)[:, :, : by_share.shape[2] - share],
            ],
            axis=2,
        ).reshape(tokens, chan_count)
    low_out, d_low_in, g_ln1, g_ln2 = low_out[None], d_low_in[None], g_ln1[0], g_ln2[0]
    d_normed, d_map, cn_grads, low_sums = big_backward(
        cot_hr[0], d_pooled, shares, plane_mask, normed_all, hidden_act, hidden_slope,
        up_t, down_t, low_grads, shards, devices,
    )
    low_sums = rows_first(low_sums.reshape(shards, share, -1))
    low_sums = rows_first(lax.psum_scatter(low_sums, "mp", scatter_dimension=0))
    low_gains = jnp.pad(jnp.stack([g_ln1, g_ln2]), ((0, 0), (0, chan_count - dims)))
    d_hr_in, small_sums, (g_cn_up, g_cn_down) = conv_backward(
        d_normed, conv_out, hr_gainf[None], cell_mask, bordered, d_map, taps, low_gains, size, cn_grads, devices, shards
    )
    d_hr_in = d_hr_in[None]
    g_conv = small_sums[: size * size].reshape(conv_w.shape)
    g_hr_gain, g_ln1, g_ln2 = small_sums[size * size], small_sums[-2, :dims], small_sums[-1, :dims]
    g_cn_up, g_cn_down, low_out, hr_out, d_low_in, d_hr_in = map_outputs(
        g_cn_up, g_cn_down, (low_out, hr_out, d_low_in, d_hr_in)
    )
    g_ad_gate, g_ad_high, g_ad_out, g_qkv, g_proj, g_up, g_down = low_outputs(
        low_sums.reshape(share, -1), [p.shape[1] for p in pieces], ad_high.shape[0] // devices
    )
    g_cn_down = g_cn_down.T
    return (
        low_out,
        hr_out,
        d_low_in,
        d_hr_in,
        g_conv,
        g_hr_gain,
        g_cn_up,
        g_cn_down,
        g_ad_gate,
        g_ad_high,
        g_ad_out,
        g_ln1,
        g_qkv,
        g_proj,
        g_ln2,
        g_up,
        g_down,
    )


def solution(mesh):
    return jax.shard_map(
        per_device,
        mesh=mesh,
        in_specs=(
            P("dp", "mp", None, None),
            P("dp", "mp", None),
            P("dp", "mp", None),
            P(),
            P(),
            P(None, "mp"),
            P("mp", None),
            P(None, "mp"),
            P(None, "mp"),
            P("mp", None),
            P(),
            P(None, None, "mp"),
            P("mp", None),
            P(),
            P(None, "mp"),
            P("mp", None),
            P("dp", "mp", None),
            P("dp", "mp", None, None),
        ),
        out_specs=(
            P("dp", "mp", None),
            P("dp", "mp", None, None),
            P("dp", "mp", None),
            P("dp", "mp", None, None),
            P(),
            P(),
            P("dp", "mp"),
            P("mp", "dp"),
            P("dp", "mp"),
            P("dp", "mp"),
            P("mp", "dp"),
            P(),
            P(None, "dp", "mp"),
            P("mp", "dp"),
            P(),
            P("dp", "mp"),
            P("mp", "dp"),
        ),
        check_vma=False,
    )
```

```python
import jax
import jax.numpy as jnp
from jax import lax
from jax.experimental.layout import Layout, with_layout_constraint
from jax.experimental import pallas as pl
from jax.experimental.pallas import tpu as pltpu
from jax.sharding import PartitionSpec as P

HEAD = 64
LANES = 128
EDGE = 8
CHUNKS = 6
TILE = 1536
LOW_TILE = 1024
GRAD_TILE = 512
MIB = 1024 * 1024
MESH = pl.DeviceIdType.MESH
BF = jnp.bfloat16
F32 = jnp.float32

def gelu_parts(x):
    c = 0.7978845608028654
    x2 = x * x
    t = jnp.tanh(c * x * (1.0 + 0.044715 * x2))
    half = 0.5 * (1.0 + t)
    slope = half + 0.5 * x * (1.0 - t * t) * (c * (1.0 + 3 * 0.044715 * x2))
    return x * half, slope


def gelu(x):
    c = 0.7978845608028654
    t = jnp.tanh(c * x * (1.0 + 0.044715 * (x * x)))
    return 0.5 * x * (1.0 + t)


def dp_bit(position):
    return lax.rem(lax.axis_index("dp") // 2**position, 2)


def dp_mate(position):
    return lax.axis_index("dp") + 2**position * (1 - 2 * dp_bit(position))


class Halving:
    def __init__(self, bits, lasts, shape, block):
        self.lasts, self.shape, self.block = lasts, shape, block
        left = list(bits)
        self.bits = [left.pop(0 if last else -1) for last in lasts]

    def split(self, count, p):
        if count == 1:
            return (1, 1)
        return (count // 2, 2) if self.lasts[p] else (2, count // 2)

    def buffers(self):
        count, rows, cols = self.shape
        got, held = [], []
        for p in range(len(self.bits)):
            count //= 2
            got.append(jax.ShapeDtypeStruct((count, rows, cols), BF))
            held.append(jax.ShapeDtypeStruct(self.split(count, p + 1) + (rows, cols), BF))
        return got + held

    def semaphores(self):
        return [pltpu.SemaphoreType.DMA((len(self.bits),))] * 2

    def bind(self, first, buffers, send, recv):
        steps = len(self.bits)
        self.now = [first] + list(buffers[steps:])
        self.got, self.send, self.recv = buffers[:steps], send, recv

    def part(self, p, mine):
        bit = dp_bit(self.bits[p])
        index = bit if mine else 1 - bit
        return self.now[p].at[:, index] if self.lasts[p] else self.now[p].at[index]

    def copy(self, p):
        return pltpu.make_async_remote_copy(
            src_ref=self.part(p, False), dst_ref=self.got[p], send_sem=self.send.at[p], recv_sem=self.recv.at[p],
            device_id={"dp": dp_mate(self.bits[p])}, device_id_type=MESH,
        )

    def start(self, p):
        self.copy(p).start()

    def finish(self, p, wait=True):
        if wait:
            self.copy(p).wait()
        count, rows, cols = self.got[p].shape
        ways = self.split(count, p + 1)

        def add(a, b, out):
            out[...] = (a[...].astype(F32) + b[...].astype(F32)).astype(BF).reshape(out.shape)

        flat = pl.BlockSpec((1, rows, self.block), lambda k, c: (k, 0, c))
        paired = pl.BlockSpec((1, 1, rows, self.block), lambda k, c: (k // ways[1], lax.rem(k, ways[1]), 0, c))
        pltpu.emit_pipeline(add, grid=(count, cols // self.block), in_specs=[flat, flat], out_specs=[paired])(
            self.part(p, True), self.got[p], self.now[p + 1]
        )


def chain_exchange(
    n, chunks, lag, gathered, partial, travel, sems, own_chunk, prepare, arrived, compute, mates=(), begin=None, turn=None, after=None, early=False
):
    ag_send, ag_recv, rs_send, rs_recv = sems
    d = lax.axis_index("mp")
    has_left, has_right = d > 0, d < n - 1

    barrier = pltpu.get_barrier_semaphore()

    @pl.when(has_left)
    def _():
        pl.semaphore_signal(barrier, inc=1, device_id={"mp": d - 1}, device_id_type=MESH)

    @pl.when(has_right)
    def _():
        pl.semaphore_signal(barrier, inc=1, device_id={"mp": d + 1}, device_id_type=MESH)

    for mate in mates:
        pl.semaphore_signal(barrier, inc=1, device_id={"dp": mate}, device_id_type=MESH)

    own_chunk(0)
    pl.semaphore_wait(barrier, has_left.astype(jnp.int32) + has_right.astype(jnp.int32) + len(mates))
    if begin is not None:
        begin()

    def ag(way, s, j):
        return pltpu.make_async_remote_copy(
            src_ref=gathered.at[s, j], dst_ref=gathered.at[s, j],
            send_sem=ag_send.at[way, s, j], recv_sem=ag_recv.at[s, j],
            device_id={"mp": d + 1 - 2 * way}, device_id_type=MESH,
        )

    def rs(way, s, j):
        there = d + 1 - 2 * way
        slot = jnp.where((s == there) & (way == 0), n, s)
        return pltpu.make_async_remote_copy(
            src_ref=travel.at[s, j], dst_ref=travel.at[slot, j],
            send_sem=rs_send.at[s, j], recv_sem=rs_recv.at[slot, j],
            device_id={"mp": there}, device_id_type=MESH,
        )

    def rs_wait(slot, j):
        pltpu.make_async_copy(travel.at[slot, j], travel.at[slot, j], rs_recv.at[slot, j]).wait()

    def first(j, _):
        @pl.when(j > 0)
        def _():
            own_chunk(j)

        @pl.when(has_right)
        def _():
            ag(0, d, j).start()

        @pl.when(has_left)
        def _():
            ag(1, d, j).start()

        return 0

    lax.fori_loop(0, chunks, first, 0)

    def flow(way, q):
        ql = jnp.clip(q, 0, n * chunks - 1)
        s, jj = ql // chunks, lax.rem(ql, chunks)
        if way == 1:
            s = n - 1 - s
        ahead = (s > d) if way == 0 else (s < d)
        source = has_left if way == 0 else has_right

        @pl.when((q >= 0) & (q < n * chunks) & (ahead | ((s == d) & source)))
        def _():
            @pl.when(source)
            def _():
                rs_wait(jnp.where(s == d, n, s) if way == 0 else s, jj)

            @pl.when(ahead & source)
            def _():
                travel[s, jj] = (partial[s, jj].astype(F32) + travel[s, jj].astype(F32)).astype(BF)

            @pl.when(ahead & jnp.logical_not(source))
            def _():
                travel[s, jj] = partial[s, jj].astype(BF)

            @pl.when(ahead)
            def _():
                rs(way, s, jj).start()

    def block_of(k, way):
        s = d - k + 2 * k * way
        return s, (s >= 0) & (s < n) & ((k > 0) | (way == 0))

    def receive(k, way, s, j):
        @pl.when(k > 0)
        def _():
            pltpu.make_async_copy(gathered.at[s, j], gathered.at[s, j], ag_recv.at[s, j]).wait()

            @pl.when((way == 0) & has_right)
            def _():
                ag(0, s, j).start()

            @pl.when((way == 1) & has_left)
            def _():
                ag(1, s, j).start()

        arrived(s, j)

    wait_one = 1 if early else 0

    def step(g, _):
        k, j = g // chunks, lax.rem(g, chunks)

        def sides(act):
            @pl.when(g < n * chunks)
            def _():
                def side(way, _):
                    s, ok = block_of(k, way)
                    pl.when(ok)(lambda: act(way, s))
                    return 0

                lax.fori_loop(0, 2, side, 0)

        def flows():
            flow(1, g - wait_one - (n - 1 - d) * lag)
            flow(0, g - wait_one - d * lag)

        if turn is not None:
            turn(g)
        if early:
            sides(lambda way, s: receive(k, way, s, j))
            flows()

            def later(way, s):
                prepare(way, s, j)
                compute(way, s, j)

            sides(later)
        else:
            def work(way, s):
                prepare(way, s, j)
                receive(k, way, s, j)
                compute(way, s, j)

            sides(work)
            flows()
        if after is not None:
            after(g)
        return 0

    lax.fori_loop(0, n * chunks + (n - 1) * lag + wait_one, step, 0)

    def drain(i, _):
        s, j = i // chunks, lax.rem(i, chunks)

        @pl.when(has_right & (s <= d))
        def _():
            ag(0, s, j).wait_send()

        @pl.when(has_left & (s >= d))
        def _():
            ag(1, s, j).wait_send()

        @pl.when(s < d)
        def _():
            rs(1, s, j).wait_send()

        @pl.when(s > d)
        def _():
            rs(0, s, j).wait_send()

        return 0

    lax.fori_loop(0, n * chunks, drain, 0)


def own_sum(n, d, j, partial, travel, total):
    total[...] = partial[d, j].astype(F32)

    @pl.when(d > 0)
    def _():
        total[...] += travel[n, j].astype(F32)

    @pl.when(d < n - 1)
    def _():
        total[...] += travel[d, j].astype(F32)


def chain_sems(n, chunks):
    dma = pltpu.SemaphoreType.DMA
    return [dma((2, n, chunks)), dma((n, chunks)), dma((n, chunks)), dma((n + 1, chunks))]


def chunk_buffers(n, rows, c, kept):
    return [
        pltpu.VMEM((n, CHUNKS, rows, c), BF),
        pltpu.VMEM((n, CHUNKS, rows, c), kept),
        pltpu.VMEM((n + 1, CHUNKS, rows, c), BF),
    ]


def columns(i):
    return pl.ds(pl.multiple_of(i * TILE, TILE), TILE)


def drain_copies(n, copy):
    def one(i, _):
        copy(i // CHUNKS, lax.rem(i, CHUNKS)).wait()
        return 0

    lax.fori_loop(0, n * CHUNKS, one, 0)


def big_forward(x, w_up, w_down, residual, mask, share, n):
    t, c = x.shape
    h = w_up.shape[1]
    rows = t // CHUNKS
    cols = residual.shape[1]
    half = cols // 2
    pairs = rows // cols // 2

    def kernel(
        x_ref, wu, wd, res, mask_ref, share_ref, out, pooled, x_all, act_all, slope_all, wu_t, wd_t,
        gathered, partial, travel, act, slope, total, folded, turned, copied, stored, load_sem, *sems
    ):
        d = lax.axis_index("mp")
        load = pltpu.make_async_copy(x_ref, gathered.at[d], load_sem)

        def own_chunk(j):
            if isinstance(j, int):
                load.start()
                load.wait()

        def x_copy(s, j):
            return pltpu.make_async_copy(gathered.at[s, j], x_all.at[s, j], copied.at[s, j])

        def prepare(way, s, j):
            pass

        def arrived(s, j):
            x_copy(s, j).start()

        def compute(way, s, j):
            block = gathered.at[s, j]

            def up(i, _):
                pre = jnp.dot(block[...], wu[:, columns(i)], preferred_element_type=F32)
                value, rate = gelu_parts(pre)
                act[:, columns(i)] = value.astype(BF)
                slope[:, columns(i)] = rate.astype(BF)
                return 0

            lax.fori_loop(0, h // TILE, up, 0)
            keep_act = pltpu.make_async_copy(act, act_all.at[s, j], stored.at[0])
            keep_slope = pltpu.make_async_copy(slope, slope_all.at[s, j], stored.at[1])
            keep_act.start()
            keep_slope.start()

            def down(i, _):
                partial[s, j, :, columns(i)] = jnp.dot(
                    act[...], wd[:, columns(i)], preferred_element_type=F32
                )
                return 0

            lax.fori_loop(0, c // TILE, down, 0)
            keep_act.wait()
            keep_slope.wait()

        def finish(j):
            pl.when(j > 0)(lambda: put(j - 1).wait())
            own_sum(n, d, j, partial, travel, total)
            values = (res[pl.ds(j * 2 * pairs, 2 * pairs)].reshape(rows, c).astype(F32) + total[...]) * mask_ref[j]
            partial[d, j] = values
            put(j).start()
            both = values.reshape(pairs, 2, cols, c)
            summed = (both[:, 0] + both[:, 1]).reshape(pairs * cols, c)
            for b in range(c // LANES):
                lanes = slice(b * LANES, (b + 1) * LANES)
                folded[b] = summed[:, lanes]
                every = folded[b, pl.ds(0, pairs * half, 2), :] + folded[b, pl.ds(1, pairs * half, 2), :]
                pooled[j, :, lanes] = every * share_ref[j]

        def put(j):
            return pltpu.make_async_copy(partial.at[d, j], out.at[j], load_sem)

        def after(g):
            last = g - (n - 1) * (CHUNKS + 1)
            pl.when(last >= 0)(lambda: finish(last))
            for i, (w, target, size) in enumerate(((wu, wu_t, h), (wd, wd_t, c))):
                late = g - n * CHUNKS // 2

                @pl.when((late >= 0) & (late < size // LANES))
                def _():
                    some = pl.ds(pl.multiple_of(late * LANES, LANES), LANES)
                    turned[i, :, pl.ds(0, w.shape[0])] = w[:, some].T
                    copy = pltpu.make_async_copy(turned.at[i, :, pl.ds(0, w.shape[0])], target.at[some], stored.at[i])
                    copy.start()
                    copy.wait()

        chain_exchange(
            n, CHUNKS, 1, gathered, partial, travel, sems, own_chunk, prepare, arrived, compute, after=after
        )

        put(CHUNKS - 1).wait()
        drain_copies(n, x_copy)

    whole = pl.BlockSpec(memory_space=pl.ANY)
    local = pl.BlockSpec(memory_space=pltpu.VMEM)
    out, pooled, x_all, act_all, slope_all, wu_t, wd_t = pl.pallas_call(
        kernel,
        out_shape=(
            jax.ShapeDtypeStruct((CHUNKS, rows, c), F32),
            jax.ShapeDtypeStruct((CHUNKS, pairs * half, c), F32),
            jax.ShapeDtypeStruct((n, CHUNKS, rows, c), BF),
            jax.ShapeDtypeStruct((n, CHUNKS, rows, h), BF),
            jax.ShapeDtypeStruct((n, CHUNKS, rows, h), BF),
            jax.ShapeDtypeStruct((h, c), BF),
            jax.ShapeDtypeStruct((c, h), BF),
        ),
        in_specs=[whole, local, local, local, local, local],
        out_specs=(whole, local, whole, whole, whole, whole, whole),
        scratch_shapes=chunk_buffers(n, rows, c, F32)
        + [pltpu.VMEM((rows, h), BF)] * 2
        + [pltpu.VMEM((rows, c), F32), pltpu.VMEM((c // LANES, pairs * cols, LANES), F32), pltpu.VMEM((2, LANES, max(c, h)), BF)]
        + [pltpu.SemaphoreType.DMA((n, CHUNKS)), pltpu.SemaphoreType.DMA((2,)), pltpu.SemaphoreType.DMA]
        + chain_sems(n, CHUNKS),
        compiler_params=pltpu.CompilerParams(
            collective_id=0, has_side_effects=True, vmem_limit_bytes=60 * MIB
        ),
        cost_estimate=pl.CostEstimate(
            flops=4 * n * t * c * h, bytes_accessed=8 * n * t * c, transcendentals=n * t * h
        ),
    )(
        x.reshape(CHUNKS, rows, c), w_up, w_down, residual,
        mask.reshape(CHUNKS, rows, 1), share.reshape(CHUNKS, pairs * half, 1),
    )
    return (
        out.reshape(t, c),
        pooled.reshape(t // 4, c),
        x_all,
        act_all,
        slope_all,
        wu_t,
        wd_t,
    )


def big_backward(cot, d_pooled, share, mask, x_all, act_all, slope_all, up_t, down_t, grads, n, devices):
    _, cols, c = cot.shape
    t = cot.shape[0] * cols
    h = up_t.shape[0]
    rows = t // CHUNKS
    half = cols // 2
    pairs_here = rows // cols // 2
    piece = c // devices
    items = n * CHUNKS // 2
    pairs, g_rows, g_cols = grads.shape
    bits = range(1, devices.bit_length() - 1)
    split = g_rows // 2
    steps = len(bits)
    plans = [Halving(bits, [last] * steps, (pairs, split, g_cols), min(g_cols, 1024)) for last in (True, False)]
    extras = [b for plan in plans for b in plan.buffers()[:-1]]
    each = 2 * steps - 1

    def kernel(
        cot_ref, pool_ref, share_ref, mask_ref, x_hbm, act_hbm, slopes, wu, wd, g_first, g_second,
        out, d_own, g_up_out, g_down_out, out_up, out_down, got_up, got_down, h_all, *rest
    ):
        sums, extra, rest = rest[0], rest[1 : 1 + 2 * each], rest[1 + 2 * each :]
        gathered, partial, travel, slope, grad, left, right, middle, g_up, g_down, total, spread_rows, addend = rest[:13]
        core_send, core_recv, stored, add_sem, send0, recv0, send1, recv1 = rest[13:21]
        sems = rest[21:]
        d = lax.axis_index("mp")
        plans[0].bind(g_first.at[:, :, pl.ds(0, split)], extra[:each] + (sums.at[0],), send0, recv0)
        plans[1].bind(g_second.at[:, :, pl.ds(split, split)], extra[each:] + (sums.at[1],), send1, recv1)

        def begin():
            for plan in plans:
                plan.start(0)

        def pass_on(p, plan):
            plan.finish(p)
            if p + 1 < steps:
                plan.start(p + 1)

        first_due = 2 * CHUNKS + 4
        ticks = {}
        if steps == 2:
            for p, start in ((0, first_due), (1, n * CHUNKS + n - 2)):
                tiles = [
                    (plan, k, q)
                    for plan in plans
                    for k in range(plan.got[p].shape[0])
                    for q in range(g_cols // plan.block)
                ]
                for m in range(0, len(tiles), 4):
                    ticks[start + m // 4] = (p, m == 0, m + 4 >= len(tiles), tiles[m : m + 4])

        def tile_copy(which, p, i, plan, k, q):
            lanes = pl.ds(q * plan.block, plan.block)
            if which == 0:
                source, target = plan.part(p, True).at[k, :, lanes], addend.at[0, i]
            elif which == 1:
                source, target = plan.got[p].at[k, :, lanes], addend.at[1, i]
            else:
                ways = plan.split(plan.got[p].shape[0], p + 1)
                source, target = addend.at[0, i], plan.now[p + 1].at[k // ways[1], k % ways[1], :, lanes]
            return pltpu.make_async_copy(source, target, add_sem.at[which, i])

        def tick_begin(p, fresh, final, tiles):
            if fresh:
                for plan in plans:
                    plan.copy(p).wait()
            for i, tile in enumerate(tiles):
                for which in range(2):
                    tile_copy(which, p, i, *tile).start()

        def tick_add(p, fresh, final, tiles):
            for i, tile in enumerate(tiles):
                for which in range(2):
                    tile_copy(which, p, i, *tile).wait()
                addend[0, i] = (addend[0, i].astype(F32) + addend[1, i].astype(F32)).astype(BF)
                tile_copy(2, p, i, *tile).start()
            for i, tile in enumerate(tiles):
                tile_copy(2, p, i, *tile).wait()
            if final and p + 1 < steps:
                for plan in plans:
                    plan.start(p + 1)

        all_steps = n * CHUNKS + n
        due = [all_steps * 9 * (2**steps - 2 ** (steps - 1 - p)) // (10 * (2**steps - 1)) // 2 * 2 for p in range(steps)]

        def turn(g):
            if ticks:
                for at, tick in ticks.items():
                    pl.when(g == at)(lambda tick=tick: tick_begin(*tick))
            else:
                for p in range(steps - 1):
                    for i, plan in enumerate(plans):
                        pl.when(g == due[p] + 2 * i)(lambda p=p, plan=plan: pass_on(p, plan))

            q, due_now = item_of(g)

            @pl.when(due_now)
            def _():
                for copy in item_copies(q):
                    copy.start()

        def own_chunk(j):
            part = pool_ref[j] * share_ref[j]
            here = cot_ref.at[pl.ds(j * 2 * pairs_here, 2 * pairs_here)]
            for b in range(c // LANES):
                lanes = slice(b * LANES, (b + 1) * LANES)
                spread_rows[b, pl.ds(0, pairs_here * half, 2), :] = part[:, lanes]
                spread_rows[b, pl.ds(1, pairs_here * half, 2), :] = part[:, lanes]
                block = jnp.broadcast_to(
                    spread_rows[b].reshape(pairs_here, 1, cols, LANES), (pairs_here, 2, cols, LANES)
                ).reshape(rows, LANES)
                cell = here[:, :, lanes].reshape(rows, LANES).astype(F32)
                gathered[d, j, :, lanes] = ((cell + block) * mask_ref[j]).astype(BF)

        def slope_copy(s, j):
            return pltpu.make_async_copy(slopes.at[s, j], slope, stored.at[0])

        def prepare(way, s, j):
            slope_copy(s, j).start()

        def arrived(s, j):
            pass

        def compute(way, s, j):
            block = gathered.at[s, j]
            slope_copy(s, j).wait()

            def up(i, _):
                back = nn(block[...], wd[:, columns(i)])
                grad[:, columns(i)] = (back * slope[:, columns(i)].astype(F32)).astype(BF)
                return 0

            lax.fori_loop(0, h // TILE, up, 0)
            half_pair = pl.ds(pl.multiple_of(lax.rem(j, 2) * rows, rows), rows)
            keep = pltpu.make_async_copy(grad, h_all.at[s, j // 2, half_pair], stored.at[1])
            keep.start()

            def down(i, _):
                partial[s, j, :, columns(i)] = nn(grad[...], wu[:, columns(i)]).astype(BF)
                return 0

            lax.fori_loop(0, c // TILE, down, 0)
            keep.wait()

        def item_place(q):
            s, jj, base = d, q, CHUNKS // 2
            for k in range(1, n):
                to_left, to_right = d - k >= 0, d + k < n
                two = to_left & to_right
                r = q - base
                here = (r >= 0) & (to_left | to_right)
                s = jnp.where(here, jnp.where(to_left & (jnp.logical_not(two) | (lax.rem(r, 2) == 0)), d - k, d + k), s)
                jj = jnp.where(here, jnp.where(two, r // 2, r), jj)
                base = base + (CHUNKS // 2) * (to_left.astype(jnp.int32) + to_right.astype(jnp.int32))
            return s, jj

        def item_copies(q):
            s, jj = item_place(q)
            return (
                pltpu.make_async_copy(x_hbm.at[s, jj], left, stored.at[2]),
                pltpu.make_async_copy(act_hbm.at[s, jj], right, stored.at[3]),
                pltpu.make_async_copy(h_all.at[s, jj], middle, stored.at[4]),
            )

        between = (d > 0) & (d < n - 1)
        middle_steps = [n * CHUNKS - items + i for i in range(items)]
        if n == 4 and CHUNKS == 6:
            middle_steps = [2, 4, 12, 13, 14, 15, 17, 19, 20, 21, 22, 23]

        def item_of(g):
            q = jnp.where(between, -1, (g - 3) // 2)
            for i, at in enumerate(middle_steps):
                q = jnp.where(between & (g == at), i, q)
            return q, (q >= 0) & (q < items) & (g >= 2) & (between | (lax.rem(g, 2) == 1))

        def after(g):
            for at, tick in ticks.items():
                pl.when(g == at)(lambda tick=tick: tick_add(*tick))
            last = g - 1 - (n - 1) * (CHUNKS + 1)
            pl.when(last >= 0)(lambda: finish(last))
            q, due_now = item_of(g)

            @pl.when(due_now)
            def _():
                s, jj = item_place(q)
                for copy in item_copies(q):
                    copy.wait()

                def tile(i, _):
                    a = columns(i)
                    g_up[a] += tn(left[:, a], middle[...])
                    db = gathered[s, pl.ds(2 * jj, 2), :, a].reshape(2 * rows, TILE)
                    g_down[a] += tn(db, right[...])
                    return 0

                lax.fori_loop(0, c // TILE, tile, 0)

            @pl.when(g == 2 * items + 2)
            def _():
                give(g_up, left, out_up, stored.at[2])
                swaps[0].start()

            @pl.when(g == 2 * items + 3)
            def _():
                give(g_down, right, out_down, stored.at[3])
                swaps[1].start()

        core = dp_bit(0)

        def result(j):
            return pltpu.make_async_copy(total, out.at[j], stored.at[5])

        def finish(j):
            pl.when(j > 0)(lambda: result(j - 1).wait())
            own_sum(n, d, j, partial, travel, total)
            result(j).start()

        def rows_at(i):
            return pl.ds(pl.multiple_of(i * piece, piece), piece)

        def give(source, stage, target, sem):
            def one(i, _):
                stage[pl.ds(0, piece)] = source[rows_at(2 * i + 1 - core)].astype(BF)
                copy = pltpu.make_async_copy(stage.at[pl.ds(0, piece)], target.at[i], sem)
                copy.start()
                copy.wait()
                return 0

            lax.fori_loop(0, devices // 2, one, 0)

        def keep_sums():
            sets = ((g_up, left, got_up, g_up_out, 2), (g_down, right, got_down, g_down_out, 3))

            def loads(i):
                return [
                    pltpu.make_async_copy(got.at[i], stage.at[pl.ds(0, piece)], stored.at[sem])
                    for _, stage, got, _, sem in sets
                ]

            def one(i, _):
                for load in loads(i):
                    load.start()
                saves = []
                for load, (source, stage, _, target, sem) in zip(loads(i), sets):
                    load.wait()
                    here = stage.at[pl.ds(0, piece)]
                    here[...] = (source[rows_at(2 * i + core)] + here[...].astype(F32)).astype(BF)
                    saves.append(pltpu.make_async_copy(here, target.at[i], stored.at[sem]))
                    saves[-1].start()
                for save in saves:
                    save.wait()
                return 0

            lax.fori_loop(0, devices // 2, one, 0)

        swaps = [
            pltpu.make_async_remote_copy(
                src_ref=src, dst_ref=dst, send_sem=core_send.at[i], recv_sem=core_recv.at[i],
                device_id={"dp": dp_mate(0)}, device_id_type=MESH,
            )
            for i, (src, dst) in enumerate(((out_up, got_up), (out_down, got_down)))
        ]
        def clear(i, _):
            some = pl.ds(pl.multiple_of(i * TILE, TILE), TILE)
            g_up[some] = jnp.zeros((TILE, h), F32)
            g_down[some] = jnp.zeros((TILE, h), F32)
            return 0

        def begin_all():
            begin()
            lax.fori_loop(0, c // TILE, clear, 0)

        chain_exchange(
            n, CHUNKS, 1, gathered, partial, travel, sems, own_chunk, prepare, arrived, compute,
            [dp_mate(b) for b in range(steps + 1)], begin_all, turn, after, True,
        )
        keep = pltpu.make_async_copy(gathered.at[d], d_own, stored.at[0])
        keep.start()
        result(CHUNKS - 1).wait()
        keep.wait()
        if not ticks:
            for plan in plans:
                pass_on(steps - 1, plan)
        for swap in swaps:
            swap.wait()
        keep_sums()

    whole = pl.BlockSpec(memory_space=pl.ANY)
    local = pl.BlockSpec(memory_space=pltpu.VMEM)
    dma = pltpu.SemaphoreType.DMA
    out, d_own, g_up, g_down, _, _, _, _, _, sums, *_ = pl.pallas_call(
        kernel,
        out_shape=(
            jax.ShapeDtypeStruct((CHUNKS, rows, c), F32),
            jax.ShapeDtypeStruct((CHUNKS, rows, c), BF),
            *[jax.ShapeDtypeStruct((devices // 2, piece, h), BF)] * 6,
            jax.ShapeDtypeStruct((n, CHUNKS // 2, 2 * rows, h), BF),
            jax.ShapeDtypeStruct((2, 1, 1, split, g_cols), BF),
            *extras,
        ),
        in_specs=[local] * 4 + [whole] * 3 + [local] * 2 + [whole] * 2,
        out_specs=(whole,) * (10 + 2 * each),
        scratch_shapes=chunk_buffers(n, rows, c, BF)
        + [
            pltpu.VMEM((rows, h), BF), pltpu.VMEM((rows, h), BF),
            pltpu.VMEM((2 * rows, c), BF), pltpu.VMEM((2 * rows, h), BF), pltpu.VMEM((2 * rows, h), BF),
            pltpu.VMEM((c, h), F32), pltpu.VMEM((c, h), F32),
            pltpu.VMEM((rows, c), F32), pltpu.VMEM((c // LANES, pairs_here * cols, LANES), F32),
            pltpu.VMEM((2, 4, split, plans[0].block), BF),
            dma((2,)), dma((2,)), dma((6,)), dma((3, 4)),
        ]
        + plans[0].semaphores() + plans[1].semaphores()
        + chain_sems(n, CHUNKS),
        compiler_params=pltpu.CompilerParams(
            collective_id=1, has_side_effects=True, vmem_limit_bytes=62 * MIB
        ),
        cost_estimate=pl.CostEstimate(
            flops=8 * n * t * c * h, bytes_accessed=8 * n * t * c, transcendentals=0
        ),
    )(
        cot, d_pooled.reshape(CHUNKS, pairs_here * half, c), share.reshape(CHUNKS, pairs_here * half, 1),
        mask.reshape(CHUNKS, rows, 1), *(v.reshape(n, CHUNKS // 2, 2 * rows, -1) for v in (x_all, act_all)),
        slope_all, up_t, down_t,
        grads.reshape(pairs // 2, 2, g_rows, g_cols), grads.reshape(2, pairs // 2, g_rows, g_cols),
    )
    return (
        out.reshape(cot.shape), d_own.reshape(cot.shape), [g_up, g_down],
        sums.reshape(g_rows, g_cols),
    )


def frame(dst, src):
    rows, cols, _ = src.shape
    dst[:, :EDGE] = jnp.zeros((rows, EDGE, LANES), F32)
    dst[:, EDGE + cols:] = jnp.zeros((rows, EDGE, LANES), F32)
    dst[:, EDGE:EDGE + cols] = src[...].astype(F32)


def correlate(out, framed, taps, size, flip, group, first=0, last=None, every=1):
    rows, cols, _ = out.shape
    reach = size // 2
    def some(k, _):
        r = first + k * every
        acc = jnp.zeros((group, cols, LANES), F32)
        for a in range(size):
            for b in range(size):
                tap = (size - 1 - a) * size + size - 1 - b if flip else a * size + b
                acc = acc + framed[pl.ds(r * group + a, group), pl.ds(EDGE - reach + b, cols), :] * taps[tap]
        out[pl.ds(r * group, group)] = acc
        return 0
    lax.fori_loop(0, (rows // group if last is None else last) - first if every == 1 else 2, some, 0)


def conv_forward(x, w, size, n):
    rows, cols, c = x.shape
    reach = size // 2

    def kernel(x_ref, w_ref, out, bordered, framed, sent, got, own):
        d = lax.axis_index("mp")
        has_up, has_down = d > 0, d < n - 1
        barrier = pltpu.get_barrier_semaphore()

        @pl.when(has_up)
        def _():
            pl.semaphore_signal(barrier, inc=1, device_id={"mp": d - 1}, device_id_type=MESH)

        @pl.when(has_down)
        def _():
            pl.semaphore_signal(barrier, inc=1, device_id={"mp": d + 1}, device_id_type=MESH)

        keep = pltpu.make_async_copy(x_ref, bordered.at[pl.ds(reach, rows)], own)
        keep.start()
        pl.semaphore_wait(barrier, has_up.astype(jnp.int32) + has_down.astype(jnp.int32))
        up = pltpu.make_async_remote_copy(
            src_ref=x_ref.at[pl.ds(0, reach)], dst_ref=bordered.at[pl.ds(reach + rows, reach)],
            send_sem=sent.at[0], recv_sem=got.at[0], device_id={"mp": d - 1}, device_id_type=MESH,
        )
        down = pltpu.make_async_remote_copy(
            src_ref=x_ref.at[pl.ds(rows - reach, reach)], dst_ref=bordered.at[pl.ds(0, reach)],
            send_sem=sent.at[1], recv_sem=got.at[1], device_id={"mp": d + 1}, device_id_type=MESH,
        )
        nothing = jnp.zeros((reach, cols, c), BF)

        @pl.when(has_up)
        def _():
            up.start()

        @pl.when(has_down)
        def _():
            down.start()

        @pl.when(d == 0)
        def _():
            bordered[:reach] = nothing

        @pl.when(d == n - 1)
        def _():
            bordered[reach + rows :] = nothing

        groups = rows // reach

        def inner(i, _):
            lanes = pl.ds(pl.multiple_of(i * LANES, LANES), LANES)
            frame(framed.at[pl.ds(reach, rows)], x_ref.at[:, :, lanes])
            correlate(out.at[:, :, lanes], framed, w_ref.at[:, :, lanes], size, False, reach, 1, groups - 1)
            return 0

        lax.fori_loop(0, c // LANES, inner, 0)
        keep.wait()

        @pl.when(has_up)
        def _():
            down.wait_recv()

        @pl.when(has_down)
        def _():
            up.wait_recv()

        def block(i, _):
            lanes = pl.ds(pl.multiple_of(i * LANES, LANES), LANES)
            frame(framed, bordered.at[:, :, lanes])
            correlate(out.at[:, :, lanes], framed, w_ref.at[:, :, lanes], size, False, reach, 0, None, groups - 1)
            return 0

        lax.fori_loop(0, c // LANES, block, 0)

        @pl.when(has_up)
        def _():
            up.wait_send()

        @pl.when(has_down)
        def _():
            down.wait_send()

    local = pl.BlockSpec(memory_space=pltpu.VMEM)
    dma = pltpu.SemaphoreType.DMA
    return pl.pallas_call(
        kernel,
        out_shape=(
            jax.ShapeDtypeStruct((rows, cols, c), F32),
            jax.ShapeDtypeStruct((rows + 2 * reach, cols, c), BF),
        ),
        in_specs=[local, local],
        out_specs=(local, local),
        scratch_shapes=[pltpu.VMEM((rows + 2 * reach, cols + 2 * EDGE, LANES), F32), dma((2,)), dma((2,)), dma],
        compiler_params=pltpu.CompilerParams(
            collective_id=5, has_side_effects=True, vmem_limit_bytes=40 * MIB
        ),
    )(x, w)


def conv_backward(d_normed, conv_out, gain, mask, bordered, d_map, w, low_gains, size, grads, devices, n):
    rows, cols, c = conv_out.shape
    reach = size // 2
    high = rows + 2 * reach
    group = 4 if rows % 4 == 0 else 1
    bits = range(1, devices.bit_length() - 1)
    steps = len(bits)
    shape = grads[0].shape
    plans = [Halving(bits, [last] * steps, shape, shape[2]) for last in (True, False)]
    each = 2 * steps
    blocks = c // LANES
    taps = size * size
    count = taps + 1 + low_gains.shape[0]
    small = -(-count // devices)
    first_due = blocks + blocks // 3
    begins = {first_due + blocks // 2 * p // (steps - 1): p for p in range(steps - 1)}
    ends = {mark + 1: p for mark, p in begins.items()}
    rounds = {blocks + 10 * blocks // 12: 1}

    def kernel(
        dn, co, gain_ref, mask_ref, w_ref, low_ref, b_hbm, dm_hbm, g0, g1, out, g_all, *rest
    ):
        extra, rest = rest[: 2 * each], rest[2 * each :]
        around, x_around, d_here, dframed, xframed, g_own, here, level, addend, sent, got, own, add_sem = rest[:13]
        ar, halving_sems = rest[13:19], rest[19:]
        plans[0].bind(g0, extra[:each], halving_sems[0], halving_sems[1])
        plans[1].bind(g1, extra[each:], halving_sems[2], halving_sems[3])
        me, d = lax.axis_index("dp"), lax.axis_index("mp")
        has_up, has_down = d > 0, d < n - 1
        barrier = pltpu.get_barrier_semaphore()

        def greet(k, _):
            pl.semaphore_signal(
                barrier, inc=1, device_id={"dp": lax.rem(me + k, devices)}, device_id_type=MESH
            )
            return 0

        lax.fori_loop(1, devices, greet, 0)
        for k in range(1, n):
            pl.semaphore_signal(barrier, inc=1, device_id={"mp": lax.rem(d + k, n)}, device_id_type=MESH)
        load_x = pltpu.make_async_copy(b_hbm, x_around, own.at[0])
        load_d = pltpu.make_async_copy(dm_hbm, d_here, own.at[1])
        load_x.start()
        load_d.start()

        def halving_loads(p, i):
            plan, count = plans[i], plans[i].got[p].shape[0]
            some = pl.ds(0, count)
            return [
                pltpu.make_async_copy(plan.part(p, True), addend.at[0, i, some], add_sem.at[0, i]),
                pltpu.make_async_copy(plan.got[p], addend.at[1, i, some], add_sem.at[1, i]),
            ]

        def halving_save(p, i, k):
            plan = plans[i]
            ways = plan.split(plan.got[p].shape[0], p + 1)
            target = plan.now[p + 1].at[k // ways[1], k % ways[1]]
            return pltpu.make_async_copy(addend.at[0, i, k], target, add_sem.at[2 + i, k])

        def halving_begin(p):
            for i, plan in enumerate(plans):
                plan.copy(p).wait()
                for load in halving_loads(p, i):
                    load.start()

        def halving_end(p):
            for i, plan in enumerate(plans):
                for load in halving_loads(p, i):
                    load.wait()
                for k in range(plan.got[p].shape[0]):
                    addend[0, i, k] = (addend[0, i, k].astype(F32) + addend[1, i, k].astype(F32)).astype(BF)
                    halving_save(p, i, k).start()
            for i, plan in enumerate(plans):
                for k in range(plan.got[p].shape[0]):
                    halving_save(p, i, k).wait()
            if p + 1 < steps:
                for plan in plans:
                    plan.start(p + 1)

        def keep(row, lanes, value):
            g_own[row // small, row % small : row % small + 1, lanes] = value

        pl.semaphore_wait(barrier, devices + n - 2)
        for plan in plans:
            plan.start(0)
        g_own[...] = jnp.zeros(g_own.shape, F32)

        def norm(r, total):
            cells = mask_ref[r]
            back, part = normalise_back(co[r] * cells, gain_ref[...], dn[r])
            around[reach + r] = (back * cells).astype(BF)
            return total + part

        keep(taps, slice(None), lax.fori_loop(0, rows, norm, jnp.zeros((1, c), F32)))
        for i in range(low_gains.shape[0]):
            keep(taps + 1 + i, slice(None), low_ref[i : i + 1])
        up = pltpu.make_async_remote_copy(
            src_ref=around.at[pl.ds(reach, reach)], dst_ref=around.at[pl.ds(reach + rows, reach)],
            send_sem=sent.at[0], recv_sem=got.at[0], device_id={"mp": d - 1}, device_id_type=MESH,
        )
        down = pltpu.make_async_remote_copy(
            src_ref=around.at[pl.ds(rows, reach)], dst_ref=around.at[pl.ds(0, reach)],
            send_sem=sent.at[1], recv_sem=got.at[1], device_id={"mp": d + 1}, device_id_type=MESH,
        )
        nothing = jnp.zeros((reach, cols, c), BF)

        @pl.when(has_up)
        def _():
            up.start()

        @pl.when(has_down)
        def _():
            down.start()

        @pl.when(d == 0)
        def _():
            around[:reach] = nothing

        @pl.when(d == n - 1)
        def _():
            around[reach + rows :] = nothing

        load_x.wait()

        def lanes_of(i):
            return pl.ds(pl.multiple_of(i * LANES, LANES), LANES)

        def kernel_block(i, _):
            lanes = lanes_of(i)
            frame(dframed.at[pl.ds(reach, rows)], around.at[pl.ds(reach, rows), :, lanes])
            frame(xframed, x_around.at[:, :, lanes])
            for a in range(size):
                def some(r, accs):
                    dv = dframed[pl.ds(reach + r * group, group), EDGE : EDGE + cols]
                    new = []
                    for b in range(size):
                        prod = dv * xframed[pl.ds(r * group + a, group), pl.ds(EDGE - reach + b, cols), :]
                        new.append(accs[b] + jnp.sum(prod.reshape(-1, 8, LANES), axis=0))
                    return tuple(new)

                accs = lax.fori_loop(
                    0, rows // group, some, tuple(jnp.zeros((8, LANES), F32) for _ in range(size))
                )
                for b in range(size):
                    keep(a * size + b, lanes, jnp.sum(accs[b], axis=0, keepdims=True))
            return 0

        def input_block(i, _):
            lanes = lanes_of(i)
            frame(dframed, around.at[:, :, lanes])
            correlate(out.at[:, :, lanes], dframed, w_ref.at[:, :, lanes], size, True, group)
            for r in range(rows):
                out[r, :, lanes] = (out[r, :, lanes] + d_here[r, :, lanes].astype(F32)) * mask_ref[r]
            return 0

        def spread(k):
            peer = lax.rem(me + k, devices)
            return pltpu.make_async_remote_copy(
                src_ref=g_own.at[peer], dst_ref=here.at[me], send_sem=ar[0].at[k], recv_sem=ar[1].at[k],
                device_id={"dp": peer}, device_id_type=MESH,
            )

        def across(k):
            return pltpu.make_async_remote_copy(
                src_ref=level.at[d], dst_ref=level.at[d], send_sem=ar[2].at[k], recv_sem=ar[3].at[k],
                device_id={"mp": lax.rem(d + k, n)}, device_id_type=MESH,
            )

        def tell(k):
            return pltpu.make_async_remote_copy(
                src_ref=g_all.at[me], dst_ref=g_all.at[me], send_sem=ar[4].at[k], recv_sem=ar[5].at[k],
                device_id={"dp": lax.rem(me + k, devices)}, device_id_type=MESH,
            )

        def all_of(length, make, act):
            def one(k, _):
                act(make(k))
                return 0

            lax.fori_loop(1, length, one, 0)

        def sum_round(p):
            if p == 0:
                here[me] = g_own[me]
                all_of(devices, spread, lambda x: x.start())
            elif p == 1:
                all_of(devices, spread, lambda x: x.wait())
                level[d] = jnp.sum(here[...], axis=0)
                all_of(n, across, lambda x: x.start())
            elif p == 2:
                all_of(n, across, lambda x: x.wait())
                g_all[me] = jnp.sum(level[...], axis=0)
                all_of(devices, tell, lambda x: x.start())
            else:
                all_of(devices, tell, lambda x: x.wait())

        marks = sorted(set(begins) | set(ends) | set(rounds) | {blocks, 2 * blocks})
        at = 0
        for mark in marks:
            if at < blocks:
                lax.fori_loop(at, min(mark, blocks), kernel_block, 0)
            else:
                lax.fori_loop(at - blocks, mark - blocks, input_block, 0)
            at = mark
            if mark in ends:
                halving_end(ends[mark])
            if mark in begins:
                halving_begin(begins[mark])
            if mark == first_due:
                sum_round(0)
            if mark == blocks:
                load_d.wait()

                @pl.when(has_up)
                def _():
                    down.wait_recv()

                @pl.when(has_down)
                def _():
                    up.wait_recv()
            if mark in rounds:
                sum_round(rounds[mark])
        sum_round(2)
        halving_begin(steps - 1)
        halving_end(steps - 1)
        sum_round(3)

        @pl.when(has_up)
        def _():
            up.wait_send()

        @pl.when(has_down)
        def _():
            down.wait_send()

    whole = pl.BlockSpec(memory_space=pl.ANY)
    local = pl.BlockSpec(memory_space=pltpu.VMEM)
    vm, dma = pltpu.VMEM, pltpu.SemaphoreType.DMA
    d_in, g_all, *extra = pl.pallas_call(
        kernel,
        out_shape=(
            jax.ShapeDtypeStruct((rows, cols, c), F32),
            jax.ShapeDtypeStruct((devices, small, c), F32),
            *plans[0].buffers(),
            *plans[1].buffers(),
        ),
        in_specs=[local] * 6 + [whole] * 4,
        out_specs=(local,) * 2 + (whole,) * (2 * each),
        scratch_shapes=[
            vm((high, cols, c), BF), vm((high, cols, c), BF), vm((rows, cols, c), BF),
            vm((high, cols + 2 * EDGE, LANES), F32), vm((high, cols + 2 * EDGE, LANES), F32),
            vm((devices, small, c), F32), vm((devices, small, c), F32), vm((n, small, c), F32),
            vm((2, 2, shape[0] // 2) + shape[1:], BF),
            dma((2,)), dma((2,)), dma((2,)), dma((4, max(2, shape[0] // 2))),
            dma((devices,)), dma((devices,)), dma((n,)), dma((n,)), dma((devices,)), dma((devices,)),
        ]
        + plans[0].semaphores() + plans[1].semaphores(),
        compiler_params=pltpu.CompilerParams(
            collective_id=3, has_side_effects=True, vmem_limit_bytes=50 * MIB
        ),
        cost_estimate=pl.CostEstimate(flops=6 * 10**10, bytes_accessed=10**8, transcendentals=0),
    )(
        d_normed, conv_out, gain, mask, w, low_gains, bordered, d_map,
        grads[0].reshape((shape[0] // 2, 2) + shape[1:]), grads[1].reshape((2, shape[0] // 2) + shape[1:]),
    )
    sums = g_all.reshape(devices * small, c)[:count]
    return d_in, sums, [extra[each - 1].reshape(shape[1:]), extra[2 * each - 1].reshape(shape[1:])]


GATE, OUT, HIGH_A, HIGH_B, QUERY, KEY, VALUE, PROJ = range(8)
L_LOW, L_DF, L_POOL_A, L_POOL_B, L_FIRST, L_DA, L_SECOND, L_COT = range(8)
R_DGATE, R_MERGE, R_DHIGH, R_DQ, R_DK, R_DV, R_ATT, R_DUP, R_ACT = range(9)


def nn(a, b):
    return jnp.dot(a, b, preferred_element_type=F32)


def nt(a, b):
    return lax.dot_general(a, b, (((1,), (1,)), ((), ())), preferred_element_type=F32)


def tn(a, b):
    return lax.dot_general(a, b, (((0,), (0,)), ((), ())), preferred_element_type=F32)


def normalise(x, gain):
    centred = x - jnp.mean(x, -1, keepdims=True)
    rate = lax.rsqrt(jnp.mean(centred * centred, -1, keepdims=True) + 1e-06)
    return centred * rate * gain


def normalise_back(x, gain, d):
    centred = x - jnp.mean(x, -1, keepdims=True)
    rate = lax.rsqrt(jnp.mean(centred * centred, -1, keepdims=True) + 1e-06)
    hat = centred * rate
    dg = d * gain
    back = rate * (dg - jnp.mean(dg, -1, keepdims=True) - hat * jnp.mean(dg * hat, -1, keepdims=True))
    return back, jnp.sum(d * hat, axis=0, keepdims=True)


def low_stage(low, pooled, cot, gain1, gain2, packed, n, devices, cid):
    t, dim = low.shape
    every = n * t
    width = dim // n
    heads = width // HEAD
    groups = width // LANES
    pairs = devices // 2
    rows = dim // devices
    half = dim // 2
    ff = 4 * dim
    natural = rows % LANES == 0
    high_rows = pooled.shape[1] // devices

    def place_of(k):
        return (k % 2) * half + k // 2 * rows

    def in_order(ref):
        if not natural:
            return ref[...]
        order = sorted(range(devices), key=place_of)
        return jnp.concatenate([ref[:, k * rows : (k + 1) * rows] for k in order], axis=1)

    scale = HEAD ** (-0.5)

    def kernel(
        low_ref, pooled_ref, cot_ref, gain1_ref, gain2_ref, w_hbm,
        low_out, d_low, d_pooled, g_ln1, g_ln2, grads,
        wv, lhs, lhs2, rhs, gate, high, merged, resid, d_res, slope, mixed, heads_in, att_all, d_att, d_mixed,
        d_heads, probs, d_scores, stage, left, w_sem, q_send, q_got, a_send, a_got, b_send, b_got, c_send, c_got, own_sem,
        l_send, l_got, r_send, r_got, stage_sem,
    ):
        d = lax.axis_index("mp")
        dp = lax.axis_index("dp")
        core = lax.rem(dp, 2)
        mate = dp + 1 - 2 * core
        barrier = pltpu.get_barrier_semaphore()
        for k in range(1, n):
            pl.semaphore_signal(barrier, inc=1, device_id={"mp": lax.rem(d + k, n)}, device_id_type=MESH)
        pl.semaphore_signal(barrier, inc=1, device_id={"dp": mate}, device_id_type=MESH)

        def w_copy(w, k):
            c, z = k // n, lax.rem(k, n)
            wide, base, at = w_place(w)
            src = w_hbm.at[:, c, z, :, pl.ds(base, wide)]
            dst = wv.at[c, :, :, pl.ds(pl.multiple_of(at + z * wide, wide), wide)]
            return pltpu.make_async_copy(src, dst, w_sem.at[w, k])

        def w_place(w):
            if w < 8:
                return width, w * width, w * dim
            return ff // n, 8 * width + (w - 8) * ff // n, 8 * dim + (w - 8) * ff

        def w_each(w, act):
            def one(k, _):
                act(w_copy(w, k))
                return 0

            lax.fori_loop(0, 2 * n, one, 0)

        for w in (GATE, HIGH_A, HIGH_B, OUT, QUERY, KEY, VALUE, PROJ):
            w_each(w, lambda copy: copy.start())

        def w_wait(*which):
            for w in which:
                w_each(w, lambda copy: copy.wait())

        def w_cols(at, size):
            return wv[:, :, :, pl.ds(at, size)].reshape(dim, size)

        def forward(x, first, count, put):
            def one(i, _):
                put(pl.multiple_of(i * LOW_TILE, LOW_TILE), nn(x, w_cols(pl.multiple_of(first * dim + i * LOW_TILE, LOW_TILE), LOW_TILE)))
                return 0
            lax.fori_loop(0, count * dim // LOW_TILE, one, 0)

        def backward(get, first, count, dst, fresh):
            def one(i, _):
                for c in range(2):
                    part = wv[c, :, :, pl.ds(pl.multiple_of((first + i) * dim, dim), dim)].reshape(half, dim)
                    y = nt(get(pl.multiple_of(i * dim, dim)), part)
                    cols = slice(c * half, (c + 1) * half)
                    if fresh and count == 1:
                        dst[:, cols] = y
                    else:
                        dst[:, cols] += y
                return 0
            if fresh and count > 1:
                dst[...] = jnp.zeros(dst.shape, F32)
            if count == 1:
                one(0, 0)
            else:
                lax.fori_loop(0, count, one, 0)

        def r_cols(block, count=1):
            return pl.ds(block * dim, count * dim)

        def r_at(block):
            return block * dim if block <= R_DUP else block * dim + 3 * dim

        def r_copy(block):
            cols = pl.ds(r_at(block), dim if block < R_DUP else ff)
            return pltpu.make_async_remote_copy(
                src_ref=rhs.at[0, :, cols], dst_ref=rhs.at[1, :, cols], send_sem=r_send.at[block],
                recv_sem=r_got.at[block], device_id={"dp": mate}, device_id_type=MESH)

        def l_copy(i):
            return pltpu.make_async_remote_copy(
                src_ref=lhs.at[i, :, pl.ds(pl.multiple_of((1 - core) * half, half), half)], dst_ref=lhs2.at[i],
                send_sem=l_send.at[i], recv_sem=l_got.at[i], device_id={"dp": mate}, device_id_type=MESH)

        stored = []
        turned = [None]

        def put_natural(dst, value):
            if natural:
                for k in range(devices):
                    dst[:, k * rows : (k + 1) * rows] = value[:, place_of(k) : place_of(k) + rows]
            else:
                dst[...] = value

        def grad(i, block, at, count, shared=False):
            if not shared:
                r_copy(block).wait_recv()
            if turned[0] != i:
                left[0] = lhs[i, :, pl.ds(pl.multiple_of(core * half, half), half)].T
                left[1] = lhs2[i].T
                turned[0] = i

            wide, base, first = w_place(at if at < 8 else 8 + (at - 8) * dim // ff)
            piece = min(GRAD_TILE, wide)

            def out_copies(slot, k):
                out = []
                for q in range(GRAD_TILE // piece):
                    z, col = divmod(at * dim - first + k * GRAD_TILE + q * piece, wide)
                    out.append(
                        pltpu.make_async_copy(
                            stage.at[slot, :, :, pl.ds(q * piece, piece)],
                            grads.at[:, pl.ds(z * rows, rows), pl.ds(base + col, piece)],
                            stage_sem.at[slot, q],
                        )
                    )
                return out

            for k in range(count * dim // GRAD_TILE):
                slot = len(stored) % 2
                if len(stored) >= 2:
                    wait(stored[-2])
                cols = pl.ds(r_at(block) + k * GRAD_TILE, GRAD_TILE)
                y = nn(left[0], rhs[0, :, cols]) + nn(left[1], rhs[1, :, cols])
                stage[slot] = y.astype(BF).reshape(pairs, rows, GRAD_TILE)
                stored.append(out_copies(slot, k))
                start(stored[-1])

        def to_heads(k, src, dst, send, got):
            out = []
            for step in range(1, n):
                peer = lax.rem(d + step, n)
                out.append(pltpu.make_async_remote_copy(
                    src_ref=src.at[:, pl.ds(pl.multiple_of(peer * width, width), width)],
                    dst_ref=dst.at[pl.ds(pl.multiple_of(d * t, t), t)],
                    send_sem=send.at[k, step], recv_sem=got.at[k, step], device_id={"mp": peer}, device_id_type=MESH))
            out.append(pltpu.make_async_copy(
                src.at[:, pl.ds(pl.multiple_of(d * width, width), width)], dst.at[pl.ds(pl.multiple_of(d * t, t), t)], own_sem.at[k]))
            return out

        def to_tokens(k, src, dst, send, got, group):
            out = []
            slot = k * groups + group
            lanes = pl.ds(group * LANES, LANES)
            there = pl.ds(pl.multiple_of(d * width + group * LANES, LANES), LANES)
            for step in range(1, n):
                peer = lax.rem(d + step, n)
                out.append(pltpu.make_async_remote_copy(
                    src_ref=src.at[pl.ds(pl.multiple_of(peer * t, t), t), lanes], dst_ref=dst.at[:, there],
                    send_sem=send.at[slot, step], recv_sem=got.at[slot, step], device_id={"mp": peer}, device_id_type=MESH))
            out.append(pltpu.make_async_copy(
                src.at[pl.ds(pl.multiple_of(d * t, t), t), lanes], dst.at[:, there], own_sem.at[slot]))
            return out

        def start(copies):
            for c in copies:
                c.start()

        def wait(copies):
            for c in copies:
                c.wait()

        gain1_here, gain2_here = in_order(gain1_ref), in_order(gain2_ref)
        if natural:
            for i, ref in ((L_LOW, low_ref), (L_COT, cot_ref)):
                for k in range(devices):
                    lhs[i, :, place_of(k) : place_of(k) + rows] = ref[:, k * rows : (k + 1) * rows]
            for k in range(devices):
                own = slice(place_of(k), place_of(k) + rows)
                lhs[L_POOL_A, :, own] = pooled_ref[:, k * high_rows : k * high_rows + rows].astype(BF)
                more = pooled_ref[:, k * high_rows + rows : (k + 1) * high_rows].astype(BF)
                lhs[L_POOL_B, :, own] = jnp.concatenate([more, jnp.zeros((t, 2 * rows - high_rows), BF)], axis=1)
        else:
            lhs[L_LOW] = low_ref[...]
            lhs[L_COT] = cot_ref[...]
            lhs[L_POOL_A] = pooled_ref[:, :dim].astype(BF)
            lhs[L_POOL_B] = pooled_ref[:, dim:].astype(BF)
        acc = d_low
        w_wait(GATE)

        def put_gate(at, y):
            gate[:, pl.ds(at, LOW_TILE)] = 1.0 / (1.0 + jnp.exp(-y))
        forward(lhs[L_LOW], GATE, 1, put_gate)
        w_wait(HIGH_A, HIGH_B, OUT)
        for w in (8, 9):
            w_each(w, lambda copy: copy.start())

        def put_high(at, y):
            high[:, pl.ds(at, LOW_TILE)] = y
        forward(lhs[L_POOL_A], HIGH_A, 1, put_high)

        def put_merging(at, y):
            cols = pl.ds(at, LOW_TILE)
            total = high[:, cols] + y
            high[:, cols] = total
            rhs[0, :, pl.ds(R_MERGE * dim + at, LOW_TILE)] = (total * gate[:, cols]).astype(BF)
        forward(lhs[L_POOL_B], HIGH_B, 1, put_merging)
        backward(lambda at: rhs[0, :, r_cols(R_MERGE)], OUT, 1, merged, True)
        merged[...] += lhs[L_LOW].astype(F32)
        lhs[L_FIRST] = normalise(merged[...], gain1_here).astype(BF)

        w_wait(QUERY, KEY, VALUE, PROJ)
        pl.semaphore_wait(barrier, n)
        for i in (L_LOW, L_POOL_A, L_POOL_B, L_COT, L_FIRST):
            l_copy(i).start()
        r_copy(R_MERGE).start()
        out_q = []
        for k in range(3):
            def put_mixed(at, y):
                mixed[k, :, pl.ds(at, LOW_TILE)] = y.astype(BF)
            forward(lhs[L_FIRST], QUERY + k, 1, put_mixed)
            copies = to_heads(k, mixed.at[k], heads_in.at[k], q_send, q_got)
            start(copies)
            out_q.append(copies)
        wait(out_q[0] + out_q[1])

        for h in range(heads):
            lanes = slice(h * HEAD, (h + 1) * HEAD)

            def rows_of(b, _):
                some = pl.ds(pl.multiple_of(b * t, t), t)
                s = nt(heads_in[0, some, lanes], heads_in[1, :, lanes]) * scale
                e = jnp.exp(s - jnp.max(s, -1, keepdims=True))
                p = (e * (1.0 / jnp.sum(e, -1, keepdims=True))).astype(BF)
                probs[h, some] = p
                return 0
            lax.fori_loop(0, n, rows_of, 0)
        wait(out_q[2])
        out_a = []
        for h in range(heads):
            lanes = slice(h * HEAD, (h + 1) * HEAD)

            def attend(b, _):
                some = pl.ds(pl.multiple_of(b * t, t), t)
                att_all[some, lanes] = nn(probs[h, some], heads_in[2, :, lanes]).astype(BF)
                return 0
            lax.fori_loop(0, n, attend, 0)
            if (h + 1) * HEAD % LANES == 0:
                copies = to_tokens(0, att_all, rhs.at[0, :, r_cols(R_ATT)], a_send, a_got, h * HEAD // LANES)
                start(copies)
                out_a += copies
        wait(out_a)
        r_copy(R_ATT).start()
        backward(lambda at: rhs[0, :, r_cols(R_ATT)], PROJ, 1, resid, True)
        resid[...] += merged[...]
        lhs[L_SECOND] = normalise(resid[...], gain2_here).astype(BF)
        l_copy(L_SECOND).start()

        w_wait(8)

        def put_up(at, y):
            value, rate = gelu_parts(y)
            rhs[0, :, pl.ds(r_at(R_ACT) + at, LOW_TILE)] = value.astype(BF)
            slope[:, pl.ds(at, LOW_TILE)] = rate.astype(BF)
        forward(lhs[L_SECOND], 8, 4, put_up)
        r_copy(R_ACT).start()
        w_wait(9)
        backward(lambda at: rhs[0, :, pl.ds(r_at(R_ACT) + at, dim)], 12, 4, acc, True)
        put_natural(low_out, resid[...] + acc[...])

        def put_d_up(at, y):
            rhs[0, :, pl.ds(r_at(R_DUP) + at, LOW_TILE)] = (y * slope[:, pl.ds(at, LOW_TILE)].astype(F32)).astype(BF)
        forward(lhs[L_COT], 12, 4, put_d_up)
        r_copy(R_DUP).start()
        backward(lambda at: rhs[0, :, pl.ds(r_at(R_DUP) + at, dim)], 8, 4, acc, True)
        back, g = normalise_back(resid[...], gain2_here, acc[...])
        put_natural(g_ln2, g)
        d_res[...] = lhs[L_COT].astype(F32) + back
        lhs[L_DA] = d_res[...].astype(BF)
        l_copy(L_DA).start()

        def put_d_att(at, y):
            mixed[0, :, pl.ds(at, LOW_TILE)] = y.astype(BF)
        forward(lhs[L_DA], PROJ, 1, put_d_att)
        out_b = to_heads(0, mixed.at[0], d_att, b_send, b_got)
        start(out_b)
        l_copy(L_COT).wait_recv()
        grad(L_COT, R_ACT, 12, 4)
        wait(out_b)
        out_c = []

        def send_back(k, h):
            if (h + 1) * HEAD % LANES == 0:
                copies = to_tokens(k, d_heads.at[k], rhs.at[0, :, r_cols(R_DQ + k)], c_send, c_got, h * HEAD // LANES)
                start(copies)
                out_c.extend(copies)

        for h in range(heads):
            lanes = slice(h * HEAD, (h + 1) * HEAD)
            d_heads[2, :, lanes] = tn(probs[h], d_att[:, lanes]).astype(BF)
            send_back(2, h)
        for h in range(heads):
            lanes = slice(h * HEAD, (h + 1) * HEAD)

            def rows_of(b, _):
                some = pl.ds(pl.multiple_of(b * t, t), t)
                p = probs[h, some].astype(F32)
                dp_ = nt(d_att[some, lanes], heads_in[2, :, lanes])
                ds = (p * (dp_ - jnp.sum(dp_ * p, -1, keepdims=True)) * scale).astype(BF)
                d_scores[some] = ds
                d_heads[0, some, lanes] = nn(ds, heads_in[1, :, lanes]).astype(BF)
                return 0
            lax.fori_loop(0, n, rows_of, 0)
            d_heads[1, :, lanes] = tn(d_scores[...], heads_in[0, :, lanes]).astype(BF)
            send_back(0, h)
            send_back(1, h)
        l_copy(L_SECOND).wait_recv()
        grad(L_SECOND, R_DUP, 8, 4)
        l_copy(L_DA).wait_recv()
        grad(L_DA, R_ATT, PROJ, 1)
        wait(out_c)
        for k in range(3):
            r_copy(R_DQ + k).start()
        backward(lambda at: rhs[0, :, pl.ds(R_DQ * dim + at, dim)], QUERY, 3, acc, True)
        back, g = normalise_back(merged[...], gain1_here, acc[...])
        put_natural(g_ln1, g)
        d_res[...] += back
        lhs[L_DF] = d_res[...].astype(BF)
        l_copy(L_DF).start()

        def put_d_gate(at, y):
            cols = pl.ds(at, LOW_TILE)
            gv = gate[:, cols]
            part = y * gv
            rhs[0, :, pl.ds(R_DHIGH * dim + at, LOW_TILE)] = part.astype(BF)
            rhs[0, :, pl.ds(R_DGATE * dim + at, LOW_TILE)] = (part * high[:, cols] * (1.0 - gv)).astype(BF)
        forward(lhs[L_DF], OUT, 1, put_d_gate)
        r_copy(R_DHIGH).start()
        r_copy(R_DGATE).start()
        backward(lambda at: rhs[0, :, r_cols(R_DHIGH)], HIGH_A, 1, gate, True)
        backward(lambda at: rhs[0, :, r_cols(R_DHIGH)], HIGH_B, 1, high, True)
        if natural:
            for k in range(devices):
                at = place_of(k)
                d_pooled[:, k * high_rows : k * high_rows + rows] = gate[:, at : at + rows]
                d_pooled[:, k * high_rows + rows : (k + 1) * high_rows] = high[:, at : at + high_rows - rows]
        else:
            d_pooled[:, :dim] = gate[...]
            d_pooled[:, dim:] = high[...]
        backward(lambda at: rhs[0, :, r_cols(R_DGATE)], GATE, 1, acc, True)
        put_natural(d_low, d_res[...] + acc[...])
        l_copy(L_FIRST).wait_recv()
        for k in range(3):
            grad(L_FIRST, R_DQ + k, QUERY + k, 1)
        l_copy(L_DF).wait_recv()
        grad(L_DF, R_MERGE, OUT, 1)
        l_copy(L_POOL_A).wait_recv()
        grad(L_POOL_A, R_DHIGH, HIGH_A, 1)
        l_copy(L_POOL_B).wait_recv()
        grad(L_POOL_B, R_DHIGH, HIGH_B, 1, shared=True)
        l_copy(L_LOW).wait_recv()
        grad(L_LOW, R_DGATE, GATE, 1)
        wait(stored[-2])
        wait(stored[-1])
        for i in range(8):
            l_copy(i).wait_send()
        for b in range(9):
            r_copy(b).wait_send()

    whole = pl.BlockSpec(memory_space=pl.ANY)
    local = pl.BlockSpec(memory_space=pltpu.VMEM)
    vm, dma = pltpu.VMEM, pltpu.SemaphoreType.DMA
    tok = jax.ShapeDtypeStruct((t, dim), F32)
    one = jax.ShapeDtypeStruct((1, dim), F32)
    return pl.pallas_call(
        kernel,
        out_shape=(tok, tok, jax.ShapeDtypeStruct(pooled.shape, F32), one, one, jax.ShapeDtypeStruct((pairs, n * rows, 16 * width), BF)),
        in_specs=[local] * 5 + [whole],
        out_specs=(local,) * 5 + (whole,),
        scratch_shapes=[
            vm((2, pairs, rows, 16 * dim), BF), vm((8, t, dim), BF), vm((8, t, half), BF), vm((2, t, 15 * dim), BF),
            vm((t, dim), F32), vm((t, dim), F32), vm((t, dim), F32), vm((t, dim), F32), vm((t, dim), F32),
            vm((t, ff), BF), vm((3, t, dim), BF), vm((3, every, width), BF), vm((every, width), BF), vm((every, width), BF),
            vm((1, 8, 128), BF), vm((3, every, width), BF), vm((heads, every, every), BF), vm((every, every), BF),
            vm((2, pairs, rows, GRAD_TILE), BF), vm((2, half, t), BF),
            dma((10, 2 * n)), dma((3, n)), dma((3, n)), dma((groups, n)), dma((groups, n)), dma((1, n)), dma((1, n)),
            dma((3 * groups, n)), dma((3 * groups, n)), dma((3 * groups,)), dma((8,)), dma((8,)), dma((9,)), dma((9,)), dma((2, 2)),
        ],
        compiler_params=pltpu.CompilerParams(collective_id=cid, has_side_effects=True, vmem_limit_bytes=62 * MIB),
        cost_estimate=pl.CostEstimate(flops=14 * 10**9, bytes_accessed=70 * 10**6, transcendentals=10**7),
    )(low, pooled, cot, gain1, gain2, packed.reshape(pairs, 2, n, rows, 16 * width))
def low_outputs(own, widths, high_rows):
    share = own.shape[0]
    width, wide = widths[0], widths[-1]

    def kernel(x, gate, high, out, qkv, proj, up, down):
        def part(i, size=width):
            at = sum(widths[:i])
            return x[:, at : at + size].astype(F32)

        gate[...] = part(0)
        out[...] = part(1).T
        high[:share] = part(2)
        high[share:] = part(3)[: high_rows - share]
        for k in range(3):
            qkv[k] = part(4 + k)
        proj[...] = part(7).T
        up[...] = part(8, wide)
        down[...] = part(9, wide).T

    local = pl.BlockSpec(memory_space=pltpu.VMEM)
    shapes = [
        (share, width), (high_rows, width), (width, share), (3, share, width), (width, share), (share, wide), (wide, share),
    ]
    return pl.pallas_call(
        kernel,
        out_shape=[jax.ShapeDtypeStruct(s, F32) for s in shapes],
        in_specs=[local],
        out_specs=[local] * 7,
        compiler_params=pltpu.CompilerParams(vmem_limit_bytes=32 * MIB),
    )(own)


def map_outputs(g_up, g_down, others):
    count = len(others)

    def kernel(up, down, *rest):
        sources, o_up, o_down = rest[:count], rest[count], rest[count + 1]
        targets, held, sems = rest[count + 2 : 2 * count + 2], rest[2 * count + 2 : -1], rest[-1]
        loads = [pltpu.make_async_copy(a, b, sems.at[0, i]) for i, (a, b) in enumerate(zip(sources, held))]
        saves = [pltpu.make_async_copy(a, b, sems.at[1, i]) for i, (a, b) in enumerate(zip(held, targets))]
        for load in loads:
            load.start()
        o_up[...] = up[...].astype(F32)
        o_down[...] = down[...].astype(F32)
        for load, save in zip(loads, saves):
            load.wait()
            save.start()
        for save in saves:
            save.wait()

    whole = pl.BlockSpec(memory_space=pl.ANY)
    local = pl.BlockSpec(memory_space=pltpu.VMEM)
    return pl.pallas_call(
        kernel,
        out_shape=[jax.ShapeDtypeStruct(x.shape, F32) for x in (g_up, g_down, *others)],
        in_specs=[local] * 2 + [whole] * count,
        out_specs=[local] * 2 + [whole] * count,
        scratch_shapes=[pltpu.VMEM(o.shape, o.dtype) for o in others] + [pltpu.SemaphoreType.DMA((2, count))],
        compiler_params=pltpu.CompilerParams(vmem_limit_bytes=60 * MIB),
        cost_estimate=pl.CostEstimate(flops=10**9, bytes_accessed=24 * 10**6, transcendentals=0),
    )(g_up, g_down, *others)


def pack_weights(ad_gate, ad_out, ad_high, w_qkv, w_proj, w_up, w_down, devices):
    dim, width = ad_gate.shape
    share, high_rows, wide = dim // devices, ad_high.shape[0] // devices, w_up.shape[1]
    rest = high_rows - share

    def kernel(gate, out, high, qkv, proj, up, down, packed, side, side_wide, sems):
        me = lax.axis_index("dp")
        mine = pl.ds(pl.multiple_of(me * share, share), share)
        lanes = mine

        def at(i, size=width):
            return packed.at[:, pl.ds(i * width, size)]

        straight = [(gate.at[mine], at(0)), (up.at[mine], at(8, wide))]
        straight += [(qkv.at[k, mine], at(4 + k)) for k in range(3)]
        straight.append((high.at[pl.ds(pl.multiple_of(me * high_rows, rest), share)], at(2)))
        straight.append((high.at[pl.ds(pl.multiple_of(me * high_rows + share, rest), rest)], at(3).at[pl.ds(0, rest)]))
        straight += [(out.at[:, lanes], side.at[0]), (proj.at[:, lanes], side.at[1]), (down.at[:, lanes], side_wide)]
        copies = [pltpu.make_async_copy(a, b, sems.at[i]) for i, (a, b) in enumerate(straight)]
        for copy in copies:
            copy.start()
        packed[rest:, 3 * width : 4 * width] = jnp.zeros((share - rest, width), BF)
        for copy in copies:
            copy.wait()
        packed[:, width : 2 * width] = side[0].T
        packed[:, 7 * width : 8 * width] = side[1].T
        packed[:, 8 * width + wide :] = side_wide[...].T

    whole = pl.BlockSpec(memory_space=pl.ANY)
    return pl.pallas_call(
        kernel,
        out_shape=jax.ShapeDtypeStruct((share, 8 * width + 2 * wide), BF),
        in_specs=[whole] * 7,
        out_specs=pl.BlockSpec(memory_space=pltpu.VMEM),
        scratch_shapes=[
            pltpu.VMEM((2, width, share), BF), pltpu.VMEM((wide, share), BF), pltpu.SemaphoreType.DMA((10,)),
        ],
        compiler_params=pltpu.CompilerParams(vmem_limit_bytes=60 * MIB),
    )(ad_gate, ad_out, ad_high, w_qkv, w_proj, w_up, w_down)


def rows_first(x):
    return with_layout_constraint(x, Layout(major_to_minor=tuple(range(x.ndim))))


def own_part(w, axis):
    length = w.shape[axis] // lax.axis_size("dp")
    return lax.dynamic_slice_in_dim(w, lax.axis_index("dp") * length, length, axis)


def fold(w, rows):
    return w[:rows], jnp.pad(w[rows:], ((0, 2 * rows - w.shape[0]), (0, 0)))


def core_first(x, devices):
    shape = x.shape
    return x.reshape(shape[:-1] + (devices // 2, 2, -1)).swapaxes(-3, -2).reshape(shape)


def core_last(x, devices):
    shape = x.shape
    return x.reshape(shape[:-1] + (2, devices // 2, -1)).swapaxes(-3, -2).reshape(shape)


def layer_norm(values, gain):
    centre = jnp.mean(values, -1, keepdims=True)
    centred = values - centre
    variance = jnp.mean(centred * centred, -1, keepdims=True)
    return centred * lax.rsqrt(variance + 1e-06) * gain


def per_device(
    hr_in,
    low_in,
    valid,
    conv_w,
    hr_gain,
    cn_up,
    cn_down,
    ad_gate,
    ad_high,
    ad_out,
    ln1_gain,
    w_qkv,
    w_proj,
    ln2_gain,
    w_up,
    w_down,
    cot_low,
    cot_hr,
):
    _, row_count, col_count, chan_count = hr_in.shape
    devices, shards = lax.axis_size("dp"), lax.axis_size("mp")
    dims = low_in.shape[2]
    share = dims // devices
    qkv = own_part(w_qkv, 1)
    low_weights = (ad_gate, ad_out, ad_high, w_qkv, w_proj, w_up, w_down)
    pieces = [
        own_part(ad_gate, 0), own_part(ad_out, 1).T, *fold(own_part(ad_high, 0), share),
        qkv[0], qkv[1], qkv[2], own_part(w_proj, 1).T, own_part(w_up, 0), own_part(w_down, 1).T,
    ]
    if share % LANES:
        packed = rows_first(jnp.concatenate(pieces, axis=1))
    else:
        packed = pack_weights(*low_weights, devices)
    packed = rows_first(lax.all_gather(packed, "mp", axis=0, tiled=True))
    plane_mask = valid[0].astype(F32)
    cell_mask = plane_mask[..., None]
    masked = hr_in[0] * valid[0].astype(BF)[..., None]
    half_rows, half_cols = (row_count // 2, col_count // 2)
    counts = plane_mask.reshape(half_rows, 2, half_cols, 2).sum(axis=(1, 3))
    shares = 1.0 / jnp.maximum(counts, 1.0)
    size = conv_w.shape[0]
    taps = conv_w.astype(F32).reshape(size * size, 1, chan_count)
    conv_out, bordered = conv_forward(masked, taps, size, shards)
    hr_gainf = hr_gain.astype(F32)
    normed = layer_norm(conv_out * cell_mask, hr_gainf).astype(BF)
    normed, packed = lax.optimization_barrier((normed, packed))
    packed = rows_first(lax.all_gather(packed, "dp", axis=0, tiled=True))
    hr_out, pooled, normed_all, hidden_act, hidden_slope, up_t, down_t = big_forward(
        normed.reshape(row_count * col_count, chan_count), cn_up, cn_down, masked, plane_mask, shares, shards
    )
    hr_out = hr_out.reshape(hr_in.shape)
    tokens = half_rows * half_cols
    low_ins, gains = [low_in[0], pooled, cot_low[0]], [ln1_gain.astype(F32)[None], ln2_gain.astype(F32)[None]]
    if share % LANES:
        by_share = pooled.reshape(tokens, devices, -1)
        pool_a = by_share[:, :, :share].reshape(tokens, dims)
        pool_b = by_share[:, :, share:]
        pool_b = jnp.pad(pool_b, ((0, 0), (0, 0), (0, share - pool_b.shape[2]))).reshape(tokens, dims)
        low_ins = [core_first(low_in[0], devices), None, core_first(cot_low[0], devices)]
        low_ins[1] = jnp.concatenate([core_first(pool_a, devices), core_first(pool_b, devices)], axis=1)
        gains = [core_first(g, devices) for g in gains]
    low_out, d_low_in, d_pooled, g_ln1, g_ln2, low_grads = low_stage(*low_ins, *gains, packed, shards, devices, 2)
    if share % LANES:
        low_out, d_low_in = core_last(low_out, devices), core_last(d_low_in, devices)
        g_ln1, g_ln2 = core_last(g_ln1, devices), core_last(g_ln2, devices)
        d_pooled = jnp.concatenate(
            [
                core_last(d_pooled[:, :dims], devices).reshape(tokens, devices, share),
                core_last(d_pooled[:, dims:], devices).reshape(tokens, devices, share)[:, :, : by_share.shape[2] - share],
            ],
            axis=2,
        ).reshape(tokens, chan_count)
    low_out, d_low_in, g_ln1, g_ln2 = low_out[None], d_low_in[None], g_ln1[0], g_ln2[0]
    d_normed, d_map, cn_grads, low_sums = big_backward(
        cot_hr[0], d_pooled, shares, plane_mask, normed_all, hidden_act, hidden_slope,
        up_t, down_t, low_grads, shards, devices,
    )
    low_sums = rows_first(low_sums.reshape(shards, share, -1))
    low_sums = rows_first(lax.psum_scatter(low_sums, "mp", scatter_dimension=0))
    low_gains = jnp.pad(jnp.stack([g_ln1, g_ln2]), ((0, 0), (0, chan_count - dims)))
    d_hr_in, small_sums, (g_cn_up, g_cn_down) = conv_backward(
        d_normed, conv_out, hr_gainf[None], cell_mask, bordered, d_map, taps, low_gains, size, cn_grads, devices, shards
    )
    d_hr_in = d_hr_in[None]
    g_conv = small_sums[: size * size].reshape(conv_w.shape)
    g_hr_gain, g_ln1, g_ln2 = small_sums[size * size], small_sums[-2, :dims], small_sums[-1, :dims]
    g_cn_up, g_cn_down, low_out, hr_out, d_low_in, d_hr_in = map_outputs(
        g_cn_up, g_cn_down, (low_out, hr_out, d_low_in, d_hr_in)
    )
    g_ad_gate, g_ad_high, g_ad_out, g_qkv, g_proj, g_up, g_down = low_outputs(
        low_sums.reshape(share, -1), [p.shape[1] for p in pieces], ad_high.shape[0] // devices
    )
    g_cn_down = g_cn_down.T
    return (
        low_out,
        hr_out,
        d_low_in,
        d_hr_in,
        g_conv,
        g_hr_gain,
        g_cn_up,
        g_cn_down,
        g_ad_gate,
        g_ad_high,
        g_ad_out,
        g_ln1,
        g_qkv,
        g_proj,
        g_ln2,
        g_up,
        g_down,
    )


def solution(mesh):
    return jax.shard_map(
        per_device,
        mesh=mesh,
        in_specs=(
            P("dp", "mp", None, None),
            P("dp", "mp", None),
            P("dp", "mp", None),
            P(),
            P(),
            P(None, "mp"),
            P("mp", None),
            P(None, "mp"),
            P(None, "mp"),
            P("mp", None),
            P(),
            P(None, None, "mp"),
            P("mp", None),
            P(),
            P(None, "mp"),
            P("mp", None),
            P("dp", "mp", None),
            P("dp", "mp", None, None),
        ),
        out_specs=(
            P("dp", "mp", None),
            P("dp", "mp", None, None),
            P("dp", "mp", None),
            P("dp", "mp", None, None),
            P(),
            P(),
            P("dp", "mp"),
            P("mp", "dp"),
            P("dp", "mp"),
            P("dp", "mp"),
            P("mp", "dp"),
            P(),
            P(None, "dp", "mp"),
            P("mp", "dp"),
            P(),
            P("dp", "mp"),
            P("mp", "dp"),
        ),
        check_vma=False,
    )
```

```python
import jax
import jax.numpy as jnp
from jax import lax
from jax.experimental.layout import Layout, with_layout_constraint
from jax.experimental import pallas as pl
from jax.experimental.pallas import tpu as pltpu
from jax.sharding import PartitionSpec as P

HEAD = 64
LANES = 128
EDGE = 8
CHUNKS = 6
TILE = 1536
LOW_TILE = 1024
GRAD_TILE = 512
MIB = 1024 * 1024
MESH = pl.DeviceIdType.MESH
BF = jnp.bfloat16
F32 = jnp.float32

def gelu_parts(x):
    c = 0.7978845608028654
    x2 = x * x
    t = jnp.tanh(c * x * (1.0 + 0.044715 * x2))
    half = 0.5 * (1.0 + t)
    slope = half + 0.5 * x * (1.0 - t * t) * (c * (1.0 + 3 * 0.044715 * x2))
    return x * half, slope


def gelu(x):
    c = 0.7978845608028654
    t = jnp.tanh(c * x * (1.0 + 0.044715 * (x * x)))
    return 0.5 * x * (1.0 + t)


def dp_bit(position):
    return lax.rem(lax.axis_index("dp") // 2**position, 2)


def dp_mate(position):
    return lax.axis_index("dp") + 2**position * (1 - 2 * dp_bit(position))


class Halving:
    def __init__(self, bits, lasts, shape, block):
        self.lasts, self.shape, self.block = lasts, shape, block
        left = list(bits)
        self.bits = [left.pop(0 if last else -1) for last in lasts]

    def split(self, count, p):
        if count == 1:
            return (1, 1)
        return (count // 2, 2) if self.lasts[p] else (2, count // 2)

    def buffers(self):
        count, rows, cols = self.shape
        got, held = [], []
        for p in range(len(self.bits)):
            count //= 2
            got.append(jax.ShapeDtypeStruct((count, rows, cols), BF))
            held.append(jax.ShapeDtypeStruct(self.split(count, p + 1) + (rows, cols), BF))
        return got + held

    def semaphores(self):
        return [pltpu.SemaphoreType.DMA((len(self.bits),))] * 2

    def bind(self, first, buffers, send, recv):
        steps = len(self.bits)
        self.now = [first] + list(buffers[steps:])
        self.got, self.send, self.recv = buffers[:steps], send, recv

    def part(self, p, mine):
        bit = dp_bit(self.bits[p])
        index = bit if mine else 1 - bit
        return self.now[p].at[:, index] if self.lasts[p] else self.now[p].at[index]

    def copy(self, p):
        return pltpu.make_async_remote_copy(
            src_ref=self.part(p, False), dst_ref=self.got[p], send_sem=self.send.at[p], recv_sem=self.recv.at[p],
            device_id={"dp": dp_mate(self.bits[p])}, device_id_type=MESH,
        )

    def start(self, p):
        self.copy(p).start()

    def finish(self, p, wait=True):
        if wait:
            self.copy(p).wait()
        count, rows, cols = self.got[p].shape
        ways = self.split(count, p + 1)

        def add(a, b, out):
            out[...] = (a[...].astype(F32) + b[...].astype(F32)).astype(BF).reshape(out.shape)

        flat = pl.BlockSpec((1, rows, self.block), lambda k, c: (k, 0, c))
        paired = pl.BlockSpec((1, 1, rows, self.block), lambda k, c: (k // ways[1], lax.rem(k, ways[1]), 0, c))
        pltpu.emit_pipeline(add, grid=(count, cols // self.block), in_specs=[flat, flat], out_specs=[paired])(
            self.part(p, True), self.got[p], self.now[p + 1]
        )


def chain_exchange(
    n, chunks, lag, gathered, partial, travel, sems, own_chunk, prepare, arrived, compute, mates=(), begin=None, turn=None, after=None, early=False
):
    ag_send, ag_recv, rs_send, rs_recv = sems
    d = lax.axis_index("mp")
    has_left, has_right = d > 0, d < n - 1

    barrier = pltpu.get_barrier_semaphore()

    @pl.when(has_left)
    def _():
        pl.semaphore_signal(barrier, inc=1, device_id={"mp": d - 1}, device_id_type=MESH)

    @pl.when(has_right)
    def _():
        pl.semaphore_signal(barrier, inc=1, device_id={"mp": d + 1}, device_id_type=MESH)

    for mate in mates:
        pl.semaphore_signal(barrier, inc=1, device_id={"dp": mate}, device_id_type=MESH)

    own_chunk(0)
    pl.semaphore_wait(barrier, has_left.astype(jnp.int32) + has_right.astype(jnp.int32) + len(mates))
    if begin is not None:
        begin()

    def ag(way, s, j):
        return pltpu.make_async_remote_copy(
            src_ref=gathered.at[s, j], dst_ref=gathered.at[s, j],
            send_sem=ag_send.at[way, s, j], recv_sem=ag_recv.at[s, j],
            device_id={"mp": d + 1 - 2 * way}, device_id_type=MESH,
        )

    def rs(way, s, j):
        there = d + 1 - 2 * way
        slot = jnp.where((s == there) & (way == 0), n, s)
        return pltpu.make_async_remote_copy(
            src_ref=travel.at[s, j], dst_ref=travel.at[slot, j],
            send_sem=rs_send.at[s, j], recv_sem=rs_recv.at[slot, j],
            device_id={"mp": there}, device_id_type=MESH,
        )

    def rs_wait(slot, j):
        pltpu.make_async_copy(travel.at[slot, j], travel.at[slot, j], rs_recv.at[slot, j]).wait()

    def first(j, _):
        @pl.when(j > 0)
        def _():
            own_chunk(j)

        @pl.when(has_right)
        def _():
            ag(0, d, j).start()

        @pl.when(has_left)
        def _():
            ag(1, d, j).start()

        return 0

    lax.fori_loop(0, chunks, first, 0)

    def flow(way, q):
        ql = jnp.clip(q, 0, n * chunks - 1)
        s, jj = ql // chunks, lax.rem(ql, chunks)
        if way == 1:
            s = n - 1 - s
        ahead = (s > d) if way == 0 else (s < d)
        source = has_left if way == 0 else has_right

        @pl.when((q >= 0) & (q < n * chunks) & (ahead | ((s == d) & source)))
        def _():
            @pl.when(source)
            def _():
                rs_wait(jnp.where(s == d, n, s) if way == 0 else s, jj)

            @pl.when(ahead & source)
            def _():
                travel[s, jj] = (partial[s, jj].astype(F32) + travel[s, jj].astype(F32)).astype(BF)

            @pl.when(ahead & jnp.logical_not(source))
            def _():
                travel[s, jj] = partial[s, jj].astype(BF)

            @pl.when(ahead)
            def _():
                rs(way, s, jj).start()

    def block_of(k, way):
        s = d - k + 2 * k * way
        return s, (s >= 0) & (s < n) & ((k > 0) | (way == 0))

    def receive(k, way, s, j):
        @pl.when(k > 0)
        def _():
            pltpu.make_async_copy(gathered.at[s, j], gathered.at[s, j], ag_recv.at[s, j]).wait()

            @pl.when((way == 0) & has_right)
            def _():
                ag(0, s, j).start()

            @pl.when((way == 1) & has_left)
            def _():
                ag(1, s, j).start()

        arrived(s, j)

    wait_one = 1 if early else 0

    def step(g, _):
        k, j = g // chunks, lax.rem(g, chunks)

        def sides(act):
            @pl.when(g < n * chunks)
            def _():
                def side(way, _):
                    s, ok = block_of(k, way)
                    pl.when(ok)(lambda: act(way, s))
                    return 0

                lax.fori_loop(0, 2, side, 0)

        def flows():
            flow(1, g - wait_one - (n - 1 - d) * lag)
            flow(0, g - wait_one - d * lag)

        if turn is not None:
            turn(g)
        if early:
            sides(lambda way, s: receive(k, way, s, j))
            flows()

            def later(way, s):
                prepare(way, s, j)
                compute(way, s, j)

            sides(later)
        else:
            def work(way, s):
                prepare(way, s, j)
                receive(k, way, s, j)
                compute(way, s, j)

            sides(work)
            flows()
        if after is not None:
            after(g)
        return 0

    lax.fori_loop(0, n * chunks + (n - 1) * lag + wait_one, step, 0)

    def drain(i, _):
        s, j = i // chunks, lax.rem(i, chunks)

        @pl.when(has_right & (s <= d))
        def _():
            ag(0, s, j).wait_send()

        @pl.when(has_left & (s >= d))
        def _():
            ag(1, s, j).wait_send()

        @pl.when(s < d)
        def _():
            rs(1, s, j).wait_send()

        @pl.when(s > d)
        def _():
            rs(0, s, j).wait_send()

        return 0

    lax.fori_loop(0, n * chunks, drain, 0)


def own_sum(n, d, j, partial, travel, total):
    total[...] = partial[d, j].astype(F32)

    @pl.when(d > 0)
    def _():
        total[...] += travel[n, j].astype(F32)

    @pl.when(d < n - 1)
    def _():
        total[...] += travel[d, j].astype(F32)


def chain_sems(n, chunks):
    dma = pltpu.SemaphoreType.DMA
    return [dma((2, n, chunks)), dma((n, chunks)), dma((n, chunks)), dma((n + 1, chunks))]


def chunk_buffers(n, rows, c, kept):
    return [
        pltpu.VMEM((n, CHUNKS, rows, c), BF),
        pltpu.VMEM((n, CHUNKS, rows, c), kept),
        pltpu.VMEM((n + 1, CHUNKS, rows, c), BF),
    ]


def columns(i):
    return pl.ds(pl.multiple_of(i * TILE, TILE), TILE)


def drain_copies(n, copy):
    def one(i, _):
        copy(i // CHUNKS, lax.rem(i, CHUNKS)).wait()
        return 0

    lax.fori_loop(0, n * CHUNKS, one, 0)


def big_forward(x, w_up, w_down, residual, mask, share, n):
    t, c = x.shape
    h = w_up.shape[1]
    rows = t // CHUNKS
    cols = residual.shape[1]
    half = cols // 2
    pairs = rows // cols // 2

    def kernel(
        x_ref, wu, wd, res, mask_ref, share_ref, out, pooled, x_all, act_all, slope_all, wu_t, wd_t,
        gathered, partial, travel, act, slope, total, folded, turned, copied, stored, load_sem, *sems
    ):
        d = lax.axis_index("mp")
        load = pltpu.make_async_copy(x_ref, gathered.at[d], load_sem)

        def own_chunk(j):
            if isinstance(j, int):
                load.start()
                load.wait()

        def x_copy(s, j):
            return pltpu.make_async_copy(gathered.at[s, j], x_all.at[s, j], copied.at[s, j])

        def prepare(way, s, j):
            pass

        def arrived(s, j):
            x_copy(s, j).start()

        def compute(way, s, j):
            block = gathered.at[s, j]

            def up(i, _):
                pre = jnp.dot(block[...], wu[:, columns(i)], preferred_element_type=F32)
                value, rate = gelu_parts(pre)
                act[:, columns(i)] = value.astype(BF)
                slope[:, columns(i)] = rate.astype(BF)
                return 0

            lax.fori_loop(0, h // TILE, up, 0)
            keep_act = pltpu.make_async_copy(act, act_all.at[s, j], stored.at[0])
            keep_slope = pltpu.make_async_copy(slope, slope_all.at[s, j], stored.at[1])
            keep_act.start()
            keep_slope.start()

            def down(i, _):
                partial[s, j, :, columns(i)] = jnp.dot(
                    act[...], wd[:, columns(i)], preferred_element_type=F32
                )
                return 0

            lax.fori_loop(0, c // TILE, down, 0)
            keep_act.wait()
            keep_slope.wait()

        def finish(j):
            pl.when(j > 0)(lambda: put(j - 1).wait())
            own_sum(n, d, j, partial, travel, total)
            values = (res[pl.ds(j * 2 * pairs, 2 * pairs)].reshape(rows, c).astype(F32) + total[...]) * mask_ref[j]
            partial[d, j] = values
            put(j).start()
            both = values.reshape(pairs, 2, cols, c)
            summed = (both[:, 0] + both[:, 1]).reshape(pairs * cols, c)
            for b in range(c // LANES):
                lanes = slice(b * LANES, (b + 1) * LANES)
                folded[b] = summed[:, lanes]
                every = folded[b, pl.ds(0, pairs * half, 2), :] + folded[b, pl.ds(1, pairs * half, 2), :]
                pooled[j, :, lanes] = every * share_ref[j]

        def put(j):
            return pltpu.make_async_copy(partial.at[d, j], out.at[j], load_sem)

        def after(g):
            last = g - (n - 1) * (CHUNKS + 1)
            pl.when(last >= 0)(lambda: finish(last))
            for i, (w, target, size) in enumerate(((wu, wu_t, h), (wd, wd_t, c))):
                late = g - n * CHUNKS // 2

                @pl.when((late >= 0) & (late < size // LANES))
                def _():
                    some = pl.ds(pl.multiple_of(late * LANES, LANES), LANES)
                    turned[i, :, pl.ds(0, w.shape[0])] = w[:, some].T
                    copy = pltpu.make_async_copy(turned.at[i, :, pl.ds(0, w.shape[0])], target.at[some], stored.at[i])
                    copy.start()
                    copy.wait()

        chain_exchange(
            n, CHUNKS, 1, gathered, partial, travel, sems, own_chunk, prepare, arrived, compute, after=after
        )

        put(CHUNKS - 1).wait()
        drain_copies(n, x_copy)

    whole = pl.BlockSpec(memory_space=pl.ANY)
    local = pl.BlockSpec(memory_space=pltpu.VMEM)
    out, pooled, x_all, act_all, slope_all, wu_t, wd_t = pl.pallas_call(
        kernel,
        out_shape=(
            jax.ShapeDtypeStruct((CHUNKS, rows, c), F32),
            jax.ShapeDtypeStruct((CHUNKS, pairs * half, c), F32),
            jax.ShapeDtypeStruct((n, CHUNKS, rows, c), BF),
            jax.ShapeDtypeStruct((n, CHUNKS, rows, h), BF),
            jax.ShapeDtypeStruct((n, CHUNKS, rows, h), BF),
            jax.ShapeDtypeStruct((h, c), BF),
            jax.ShapeDtypeStruct((c, h), BF),
        ),
        in_specs=[whole, local, local, local, local, local],
        out_specs=(whole, local, whole, whole, whole, whole, whole),
        scratch_shapes=chunk_buffers(n, rows, c, F32)
        + [pltpu.VMEM((rows, h), BF)] * 2
        + [pltpu.VMEM((rows, c), F32), pltpu.VMEM((c // LANES, pairs * cols, LANES), F32), pltpu.VMEM((2, LANES, max(c, h)), BF)]
        + [pltpu.SemaphoreType.DMA((n, CHUNKS)), pltpu.SemaphoreType.DMA((2,)), pltpu.SemaphoreType.DMA]
        + chain_sems(n, CHUNKS),
        compiler_params=pltpu.CompilerParams(
            collective_id=0, has_side_effects=True, vmem_limit_bytes=60 * MIB
        ),
        cost_estimate=pl.CostEstimate(
            flops=4 * n * t * c * h, bytes_accessed=8 * n * t * c, transcendentals=n * t * h
        ),
    )(
        x.reshape(CHUNKS, rows, c), w_up, w_down, residual,
        mask.reshape(CHUNKS, rows, 1), share.reshape(CHUNKS, pairs * half, 1),
    )
    return (
        out.reshape(t, c),
        pooled.reshape(t // 4, c),
        x_all,
        act_all,
        slope_all,
        wu_t,
        wd_t,
    )


def big_backward(cot, d_pooled, share, mask, x_all, act_all, slope_all, up_t, down_t, grads, n, devices):
    _, cols, c = cot.shape
    t = cot.shape[0] * cols
    h = up_t.shape[0]
    rows = t // CHUNKS
    half = cols // 2
    pairs_here = rows // cols // 2
    piece = c // devices
    items = n * CHUNKS // 2
    pairs, g_rows, g_cols = grads.shape
    bits = range(1, devices.bit_length() - 1)
    split = g_rows // 2
    steps = len(bits)
    plans = [Halving(bits, [last] * steps, (pairs, split, g_cols), min(g_cols, 1024)) for last in (True, False)]
    extras = [b for plan in plans for b in plan.buffers()[:-1]]
    each = 2 * steps - 1

    def kernel(
        cot_ref, pool_ref, share_ref, mask_ref, x_hbm, act_hbm, slopes, wu, wd, g_first, g_second,
        out, d_own, g_up_out, g_down_out, out_up, out_down, got_up, got_down, h_all, *rest
    ):
        sums, extra, rest = rest[0], rest[1 : 1 + 2 * each], rest[1 + 2 * each :]
        gathered, partial, travel, slope, grad, left, right, middle, g_up, g_down, total, spread_rows, addend = rest[:13]
        core_send, core_recv, stored, add_sem, send0, recv0, send1, recv1 = rest[13:21]
        sems = rest[21:]
        d = lax.axis_index("mp")
        plans[0].bind(g_first.at[:, :, pl.ds(0, split)], extra[:each] + (sums.at[0],), send0, recv0)
        plans[1].bind(g_second.at[:, :, pl.ds(split, split)], extra[each:] + (sums.at[1],), send1, recv1)

        def begin():
            for plan in plans:
                plan.start(0)

        def pass_on(p, plan):
            plan.finish(p)
            if p + 1 < steps:
                plan.start(p + 1)

        first_due = 2 * CHUNKS + 4
        ticks = {}
        if steps == 2:
            for p, start in ((0, first_due), (1, n * CHUNKS + n - 2)):
                tiles = [
                    (plan, k, q)
                    for plan in plans
                    for k in range(plan.got[p].shape[0])
                    for q in range(g_cols // plan.block)
                ]
                for m in range(0, len(tiles), 4):
                    ticks[start + m // 4] = (p, m == 0, m + 4 >= len(tiles), tiles[m : m + 4])

        def tile_copy(which, p, i, plan, k, q):
            lanes = pl.ds(q * plan.block, plan.block)
            if which == 0:
                source, target = plan.part(p, True).at[k, :, lanes], addend.at[0, i]
            elif which == 1:
                source, target = plan.got[p].at[k, :, lanes], addend.at[1, i]
            else:
                ways = plan.split(plan.got[p].shape[0], p + 1)
                source, target = addend.at[0, i], plan.now[p + 1].at[k // ways[1], k % ways[1], :, lanes]
            return pltpu.make_async_copy(source, target, add_sem.at[which, i])

        def tick_begin(p, fresh, final, tiles):
            if fresh:
                for plan in plans:
                    plan.copy(p).wait()
            for i, tile in enumerate(tiles):
                for which in range(2):
                    tile_copy(which, p, i, *tile).start()

        def tick_add(p, fresh, final, tiles):
            for i, tile in enumerate(tiles):
                for which in range(2):
                    tile_copy(which, p, i, *tile).wait()
                addend[0, i] = (addend[0, i].astype(F32) + addend[1, i].astype(F32)).astype(BF)
                tile_copy(2, p, i, *tile).start()
            for i, tile in enumerate(tiles):
                tile_copy(2, p, i, *tile).wait()
            if final and p + 1 < steps:
                for plan in plans:
                    plan.start(p + 1)

        all_steps = n * CHUNKS + n
        due = [all_steps * 9 * (2**steps - 2 ** (steps - 1 - p)) // (10 * (2**steps - 1)) // 2 * 2 for p in range(steps)]

        def turn(g):
            if ticks:
                for at, tick in ticks.items():
                    pl.when(g == at)(lambda tick=tick: tick_begin(*tick))
            else:
                for p in range(steps - 1):
                    for i, plan in enumerate(plans):
                        pl.when(g == due[p] + 2 * i)(lambda p=p, plan=plan: pass_on(p, plan))

            q, due_now = item_of(g)

            @pl.when(due_now)
            def _():
                for copy in item_copies(q):
                    copy.start()

        def own_chunk(j):
            part = pool_ref[j] * share_ref[j]
            here = cot_ref.at[pl.ds(j * 2 * pairs_here, 2 * pairs_here)]
            for b in range(c // LANES):
                lanes = slice(b * LANES, (b + 1) * LANES)
                spread_rows[b, pl.ds(0, pairs_here * half, 2), :] = part[:, lanes]
                spread_rows[b, pl.ds(1, pairs_here * half, 2), :] = part[:, lanes]
                block = jnp.broadcast_to(
                    spread_rows[b].reshape(pairs_here, 1, cols, LANES), (pairs_here, 2, cols, LANES)
                ).reshape(rows, LANES)
                cell = here[:, :, lanes].reshape(rows, LANES).astype(F32)
                gathered[d, j, :, lanes] = ((cell + block) * mask_ref[j]).astype(BF)

        def slope_copy(s, j):
            return pltpu.make_async_copy(slopes.at[s, j], slope, stored.at[0])

        def prepare(way, s, j):
            slope_copy(s, j).start()

        def arrived(s, j):
            pass

        def compute(way, s, j):
            block = gathered.at[s, j]
            slope_copy(s, j).wait()

            def up(i, _):
                back = nn(block[...], wd[:, columns(i)])
                grad[:, columns(i)] = (back * slope[:, columns(i)].astype(F32)).astype(BF)
                return 0

            lax.fori_loop(0, h // TILE, up, 0)
            half_pair = pl.ds(pl.multiple_of(lax.rem(j, 2) * rows, rows), rows)
            keep = pltpu.make_async_copy(grad, h_all.at[s, j // 2, half_pair], stored.at[1])
            keep.start()

            def down(i, _):
                partial[s, j, :, columns(i)] = nn(grad[...], wu[:, columns(i)]).astype(BF)
                return 0

            lax.fori_loop(0, c // TILE, down, 0)
            keep.wait()

        def item_place(q):
            s, jj, base = d, q, CHUNKS // 2
            for k in range(1, n):
                to_left, to_right = d - k >= 0, d + k < n
                two = to_left & to_right
                r = q - base
                here = (r >= 0) & (to_left | to_right)
                s = jnp.where(here, jnp.where(to_left & (jnp.logical_not(two) | (lax.rem(r, 2) == 0)), d - k, d + k), s)
                jj = jnp.where(here, jnp.where(two, r // 2, r), jj)
                base = base + (CHUNKS // 2) * (to_left.astype(jnp.int32) + to_right.astype(jnp.int32))
            return s, jj

        def item_copies(q):
            s, jj = item_place(q)
            return (
                pltpu.make_async_copy(x_hbm.at[s, jj], left, stored.at[2]),
                pltpu.make_async_copy(act_hbm.at[s, jj], right, stored.at[3]),
                pltpu.make_async_copy(h_all.at[s, jj], middle, stored.at[4]),
            )

        between = (d > 0) & (d < n - 1)
        middle_steps = [n * CHUNKS - items + i for i in range(items)]
        if n == 4 and CHUNKS == 6:
            middle_steps = [2, 4, 12, 13, 14, 15, 17, 19, 20, 21, 22, 23]

        def item_of(g):
            q = jnp.where(between, -1, (g - 2) // 2)
            for i, at in enumerate(middle_steps):
                q = jnp.where(between & (g == at), i, q)
            return q, (q >= 0) & (q < items) & (g >= 2) & (between | (lax.rem(g, 2) == 0))

        def after(g):
            for at, tick in ticks.items():
                pl.when(g == at)(lambda tick=tick: tick_add(*tick))
            last = g - 1 - (n - 1) * (CHUNKS + 1)
            pl.when(last >= 0)(lambda: finish(last))
            q, due_now = item_of(g)

            @pl.when(due_now)
            def _():
                s, jj = item_place(q)
                for copy in item_copies(q):
                    copy.wait()

                def tile(i, _):
                    a = columns(i)
                    g_up[a] += tn(left[:, a], middle[...])
                    db = gathered[s, pl.ds(2 * jj, 2), :, a].reshape(2 * rows, TILE)
                    g_down[a] += tn(db, right[...])
                    return 0

                lax.fori_loop(0, c // TILE, tile, 0)

            @pl.when(g == 2 * items + 1)
            def _():
                give(g_up, left, out_up, stored.at[2])
                swaps[0].start()

            @pl.when(g == 2 * items + 2)
            def _():
                give(g_down, right, out_down, stored.at[3])
                swaps[1].start()

        core = dp_bit(0)

        def result(j):
            return pltpu.make_async_copy(total, out.at[j], stored.at[5])

        def finish(j):
            pl.when(j > 0)(lambda: result(j - 1).wait())
            own_sum(n, d, j, partial, travel, total)
            result(j).start()

        def rows_at(i):
            return pl.ds(pl.multiple_of(i * piece, piece), piece)

        def give(source, stage, target, sem):
            def one(i, _):
                stage[pl.ds(0, piece)] = source[rows_at(2 * i + 1 - core)].astype(BF)
                copy = pltpu.make_async_copy(stage.at[pl.ds(0, piece)], target.at[i], sem)
                copy.start()
                copy.wait()
                return 0

            lax.fori_loop(0, devices // 2, one, 0)

        def keep_sums():
            sets = ((g_up, left, got_up, g_up_out, 2), (g_down, right, got_down, g_down_out, 3))

            def loads(i):
                return [
                    pltpu.make_async_copy(got.at[i], stage.at[pl.ds(0, piece)], stored.at[sem])
                    for _, stage, got, _, sem in sets
                ]

            def one(i, _):
                for load in loads(i):
                    load.start()
                saves = []
                for load, (source, stage, _, target, sem) in zip(loads(i), sets):
                    load.wait()
                    here = stage.at[pl.ds(0, piece)]
                    here[...] = (source[rows_at(2 * i + core)] + here[...].astype(F32)).astype(BF)
                    saves.append(pltpu.make_async_copy(here, target.at[i], stored.at[sem]))
                    saves[-1].start()
                for save in saves:
                    save.wait()
                return 0

            lax.fori_loop(0, devices // 2, one, 0)

        swaps = [
            pltpu.make_async_remote_copy(
                src_ref=src, dst_ref=dst, send_sem=core_send.at[i], recv_sem=core_recv.at[i],
                device_id={"dp": dp_mate(0)}, device_id_type=MESH,
            )
            for i, (src, dst) in enumerate(((out_up, got_up), (out_down, got_down)))
        ]
        def clear(i, _):
            some = pl.ds(pl.multiple_of(i * TILE, TILE), TILE)
            g_up[some] = jnp.zeros((TILE, h), F32)
            g_down[some] = jnp.zeros((TILE, h), F32)
            return 0

        def begin_all():
            begin()
            lax.fori_loop(0, c // TILE, clear, 0)

        chain_exchange(
            n, CHUNKS, 1, gathered, partial, travel, sems, own_chunk, prepare, arrived, compute,
            [dp_mate(b) for b in range(steps + 1)], begin_all, turn, after, True,
        )
        keep = pltpu.make_async_copy(gathered.at[d], d_own, stored.at[0])
        keep.start()
        result(CHUNKS - 1).wait()
        keep.wait()
        if not ticks:
            for plan in plans:
                pass_on(steps - 1, plan)
        for swap in swaps:
            swap.wait()
        keep_sums()

    whole = pl.BlockSpec(memory_space=pl.ANY)
    local = pl.BlockSpec(memory_space=pltpu.VMEM)
    dma = pltpu.SemaphoreType.DMA
    out, d_own, g_up, g_down, _, _, _, _, _, sums, *_ = pl.pallas_call(
        kernel,
        out_shape=(
            jax.ShapeDtypeStruct((CHUNKS, rows, c), F32),
            jax.ShapeDtypeStruct((CHUNKS, rows, c), BF),
            *[jax.ShapeDtypeStruct((devices // 2, piece, h), BF)] * 6,
            jax.ShapeDtypeStruct((n, CHUNKS // 2, 2 * rows, h), BF),
            jax.ShapeDtypeStruct((2, 1, 1, split, g_cols), BF),
            *extras,
        ),
        in_specs=[local] * 4 + [whole] * 3 + [local] * 2 + [whole] * 2,
        out_specs=(whole,) * (10 + 2 * each),
        scratch_shapes=chunk_buffers(n, rows, c, BF)
        + [
            pltpu.VMEM((rows, h), BF), pltpu.VMEM((rows, h), BF),
            pltpu.VMEM((2 * rows, c), BF), pltpu.VMEM((2 * rows, h), BF), pltpu.VMEM((2 * rows, h), BF),
            pltpu.VMEM((c, h), F32), pltpu.VMEM((c, h), F32),
            pltpu.VMEM((rows, c), F32), pltpu.VMEM((c // LANES, pairs_here * cols, LANES), F32),
            pltpu.VMEM((2, 4, split, plans[0].block), BF),
            dma((2,)), dma((2,)), dma((6,)), dma((3, 4)),
        ]
        + plans[0].semaphores() + plans[1].semaphores()
        + chain_sems(n, CHUNKS),
        compiler_params=pltpu.CompilerParams(
            collective_id=1, has_side_effects=True, vmem_limit_bytes=62 * MIB
        ),
        cost_estimate=pl.CostEstimate(
            flops=8 * n * t * c * h, bytes_accessed=8 * n * t * c, transcendentals=0
        ),
    )(
        cot, d_pooled.reshape(CHUNKS, pairs_here * half, c), share.reshape(CHUNKS, pairs_here * half, 1),
        mask.reshape(CHUNKS, rows, 1), *(v.reshape(n, CHUNKS // 2, 2 * rows, -1) for v in (x_all, act_all)),
        slope_all, up_t, down_t,
        grads.reshape(pairs // 2, 2, g_rows, g_cols), grads.reshape(2, pairs // 2, g_rows, g_cols),
    )
    return (
        out.reshape(cot.shape), d_own.reshape(cot.shape), [g_up, g_down],
        sums.reshape(g_rows, g_cols),
    )


def frame(dst, src):
    rows, cols, _ = src.shape
    dst[:, :EDGE] = jnp.zeros((rows, EDGE, LANES), F32)
    dst[:, EDGE + cols:] = jnp.zeros((rows, EDGE, LANES), F32)
    dst[:, EDGE:EDGE + cols] = src[...].astype(F32)


def correlate(out, framed, taps, size, flip, group, first=0, last=None, every=1):
    rows, cols, _ = out.shape
    reach = size // 2
    def some(k, _):
        r = first + k * every
        acc = jnp.zeros((group, cols, LANES), F32)
        for a in range(size):
            for b in range(size):
                tap = (size - 1 - a) * size + size - 1 - b if flip else a * size + b
                acc = acc + framed[pl.ds(r * group + a, group), pl.ds(EDGE - reach + b, cols), :] * taps[tap]
        out[pl.ds(r * group, group)] = acc
        return 0
    lax.fori_loop(0, (rows // group if last is None else last) - first if every == 1 else 2, some, 0)


def conv_forward(x, w, size, n):
    rows, cols, c = x.shape
    reach = size // 2

    def kernel(x_ref, w_ref, out, bordered, framed, sent, got, own):
        d = lax.axis_index("mp")
        has_up, has_down = d > 0, d < n - 1
        barrier = pltpu.get_barrier_semaphore()

        @pl.when(has_up)
        def _():
            pl.semaphore_signal(barrier, inc=1, device_id={"mp": d - 1}, device_id_type=MESH)

        @pl.when(has_down)
        def _():
            pl.semaphore_signal(barrier, inc=1, device_id={"mp": d + 1}, device_id_type=MESH)

        keep = pltpu.make_async_copy(x_ref, bordered.at[pl.ds(reach, rows)], own)
        keep.start()
        pl.semaphore_wait(barrier, has_up.astype(jnp.int32) + has_down.astype(jnp.int32))
        up = pltpu.make_async_remote_copy(
            src_ref=x_ref.at[pl.ds(0, reach)], dst_ref=bordered.at[pl.ds(reach + rows, reach)],
            send_sem=sent.at[0], recv_sem=got.at[0], device_id={"mp": d - 1}, device_id_type=MESH,
        )
        down = pltpu.make_async_remote_copy(
            src_ref=x_ref.at[pl.ds(rows - reach, reach)], dst_ref=bordered.at[pl.ds(0, reach)],
            send_sem=sent.at[1], recv_sem=got.at[1], device_id={"mp": d + 1}, device_id_type=MESH,
        )
        nothing = jnp.zeros((reach, cols, c), BF)

        @pl.when(has_up)
        def _():
            up.start()

        @pl.when(has_down)
        def _():
            down.start()

        @pl.when(d == 0)
        def _():
            bordered[:reach] = nothing

        @pl.when(d == n - 1)
        def _():
            bordered[reach + rows :] = nothing

        groups = rows // reach

        def inner(i, _):
            lanes = pl.ds(pl.multiple_of(i * LANES, LANES), LANES)
            frame(framed.at[pl.ds(reach, rows)], x_ref.at[:, :, lanes])
            correlate(out.at[:, :, lanes], framed, w_ref.at[:, :, lanes], size, False, reach, 1, groups - 1)
            return 0

        lax.fori_loop(0, c // LANES, inner, 0)
        keep.wait()

        @pl.when(has_up)
        def _():
            down.wait_recv()

        @pl.when(has_down)
        def _():
            up.wait_recv()

        def block(i, _):
            lanes = pl.ds(pl.multiple_of(i * LANES, LANES), LANES)
            frame(framed, bordered.at[:, :, lanes])
            correlate(out.at[:, :, lanes], framed, w_ref.at[:, :, lanes], size, False, reach, 0, None, groups - 1)
            return 0

        lax.fori_loop(0, c // LANES, block, 0)

        @pl.when(has_up)
        def _():
            up.wait_send()

        @pl.when(has_down)
        def _():
            down.wait_send()

    local = pl.BlockSpec(memory_space=pltpu.VMEM)
    dma = pltpu.SemaphoreType.DMA
    return pl.pallas_call(
        kernel,
        out_shape=(
            jax.ShapeDtypeStruct((rows, cols, c), F32),
            jax.ShapeDtypeStruct((rows + 2 * reach, cols, c), BF),
        ),
        in_specs=[local, local],
        out_specs=(local, local),
        scratch_shapes=[pltpu.VMEM((rows + 2 * reach, cols + 2 * EDGE, LANES), F32), dma((2,)), dma((2,)), dma],
        compiler_params=pltpu.CompilerParams(
            collective_id=5, has_side_effects=True, vmem_limit_bytes=40 * MIB
        ),
    )(x, w)


def conv_backward(d_normed, conv_out, gain, mask, bordered, d_map, w, low_gains, size, grads, devices, n):
    rows, cols, c = conv_out.shape
    reach = size // 2
    high = rows + 2 * reach
    group = 4 if rows % 4 == 0 else 1
    bits = range(1, devices.bit_length() - 1)
    steps = len(bits)
    shape = grads[0].shape
    plans = [Halving(bits, [last] * steps, shape, shape[2]) for last in (True, False)]
    each = 2 * steps
    blocks = c // LANES
    taps = size * size
    count = taps + 1 + low_gains.shape[0]
    small = -(-count // devices)
    first_due = blocks + blocks // 3
    begins = {first_due + blocks // 2 * p // (steps - 1): p for p in range(steps - 1)}
    ends = {mark + 1: p for mark, p in begins.items()}
    rounds = {blocks + 10 * blocks // 12: 1}

    def kernel(
        dn, co, gain_ref, mask_ref, w_ref, low_ref, b_hbm, dm_hbm, g0, g1, out, g_all, *rest
    ):
        extra, rest = rest[: 2 * each], rest[2 * each :]
        around, x_around, d_here, dframed, xframed, g_own, here, level, addend, sent, got, own, add_sem = rest[:13]
        ar, halving_sems = rest[13:19], rest[19:]
        plans[0].bind(g0, extra[:each], halving_sems[0], halving_sems[1])
        plans[1].bind(g1, extra[each:], halving_sems[2], halving_sems[3])
        me, d = lax.axis_index("dp"), lax.axis_index("mp")
        has_up, has_down = d > 0, d < n - 1
        barrier = pltpu.get_barrier_semaphore()

        def greet(k, _):
            pl.semaphore_signal(
                barrier, inc=1, device_id={"dp": lax.rem(me + k, devices)}, device_id_type=MESH
            )
            return 0

        lax.fori_loop(1, devices, greet, 0)
        for k in range(1, n):
            pl.semaphore_signal(barrier, inc=1, device_id={"mp": lax.rem(d + k, n)}, device_id_type=MESH)
        load_x = pltpu.make_async_copy(b_hbm, x_around, own.at[0])
        load_d = pltpu.make_async_copy(dm_hbm, d_here, own.at[1])
        load_x.start()
        load_d.start()

        def halving_loads(p, i):
            plan, count = plans[i], plans[i].got[p].shape[0]
            some = pl.ds(0, count)
            return [
                pltpu.make_async_copy(plan.part(p, True), addend.at[0, i, some], add_sem.at[0, i]),
                pltpu.make_async_copy(plan.got[p], addend.at[1, i, some], add_sem.at[1, i]),
            ]

        def halving_save(p, i, k):
            plan = plans[i]
            ways = plan.split(plan.got[p].shape[0], p + 1)
            target = plan.now[p + 1].at[k // ways[1], k % ways[1]]
            return pltpu.make_async_copy(addend.at[0, i, k], target, add_sem.at[2 + i, k])

        def halving_begin(p):
            for i, plan in enumerate(plans):
                plan.copy(p).wait()
                for load in halving_loads(p, i):
                    load.start()

        def halving_end(p):
            for i, plan in enumerate(plans):
                for load in halving_loads(p, i):
                    load.wait()
                for k in range(plan.got[p].shape[0]):
                    addend[0, i, k] = (addend[0, i, k].astype(F32) + addend[1, i, k].astype(F32)).astype(BF)
                    halving_save(p, i, k).start()
            for i, plan in enumerate(plans):
                for k in range(plan.got[p].shape[0]):
                    halving_save(p, i, k).wait()
            if p + 1 < steps:
                for plan in plans:
                    plan.start(p + 1)

        def keep(row, lanes, value):
            g_own[row // small, row % small : row % small + 1, lanes] = value

        pl.semaphore_wait(barrier, devices + n - 2)
        for plan in plans:
            plan.start(0)
        g_own[...] = jnp.zeros(g_own.shape, F32)

        def norm(r, total):
            cells = mask_ref[r]
            back, part = normalise_back(co[r] * cells, gain_ref[...], dn[r])
            around[reach + r] = (back * cells).astype(BF)
            return total + part

        keep(taps, slice(None), lax.fori_loop(0, rows, norm, jnp.zeros((1, c), F32)))
        for i in range(low_gains.shape[0]):
            keep(taps + 1 + i, slice(None), low_ref[i : i + 1])
        up = pltpu.make_async_remote_copy(
            src_ref=around.at[pl.ds(reach, reach)], dst_ref=around.at[pl.ds(reach + rows, reach)],
            send_sem=sent.at[0], recv_sem=got.at[0], device_id={"mp": d - 1}, device_id_type=MESH,
        )
        down = pltpu.make_async_remote_copy(
            src_ref=around.at[pl.ds(rows, reach)], dst_ref=around.at[pl.ds(0, reach)],
            send_sem=sent.at[1], recv_sem=got.at[1], device_id={"mp": d + 1}, device_id_type=MESH,
        )
        nothing = jnp.zeros((reach, cols, c), BF)

        @pl.when(has_up)
        def _():
            up.start()

        @pl.when(has_down)
        def _():
            down.start()

        @pl.when(d == 0)
        def _():
            around[:reach] = nothing

        @pl.when(d == n - 1)
        def _():
            around[reach + rows :] = nothing

        load_x.wait()

        def lanes_of(i):
            return pl.ds(pl.multiple_of(i * LANES, LANES), LANES)

        def kernel_block(i, _):
            lanes = lanes_of(i)
            frame(dframed.at[pl.ds(reach, rows)], around.at[pl.ds(reach, rows), :, lanes])
            frame(xframed, x_around.at[:, :, lanes])
            for a in range(size):
                def some(r, accs):
                    dv = dframed[pl.ds(reach + r * group, group), EDGE : EDGE + cols]
                    new = []
                    for b in range(size):
                        prod = dv * xframed[pl.ds(r * group + a, group), pl.ds(EDGE - reach + b, cols), :]
                        new.append(accs[b] + jnp.sum(prod.reshape(-1, 8, LANES), axis=0))
                    return tuple(new)

                accs = lax.fori_loop(
                    0, rows // group, some, tuple(jnp.zeros((8, LANES), F32) for _ in range(size))
                )
                for b in range(size):
                    keep(a * size + b, lanes, jnp.sum(accs[b], axis=0, keepdims=True))
            return 0

        def input_block(i, _):
            lanes = lanes_of(i)
            frame(dframed, around.at[:, :, lanes])
            correlate(out.at[:, :, lanes], dframed, w_ref.at[:, :, lanes], size, True, group)
            for r in range(rows):
                out[r, :, lanes] = (out[r, :, lanes] + d_here[r, :, lanes].astype(F32)) * mask_ref[r]
            return 0

        def spread(k):
            peer = lax.rem(me + k, devices)
            return pltpu.make_async_remote_copy(
                src_ref=g_own.at[peer], dst_ref=here.at[me], send_sem=ar[0].at[k], recv_sem=ar[1].at[k],
                device_id={"dp": peer}, device_id_type=MESH,
            )

        def across(k):
            return pltpu.make_async_remote_copy(
                src_ref=level.at[d], dst_ref=level.at[d], send_sem=ar[2].at[k], recv_sem=ar[3].at[k],
                device_id={"mp": lax.rem(d + k, n)}, device_id_type=MESH,
            )

        def tell(k):
            return pltpu.make_async_remote_copy(
                src_ref=g_all.at[me], dst_ref=g_all.at[me], send_sem=ar[4].at[k], recv_sem=ar[5].at[k],
                device_id={"dp": lax.rem(me + k, devices)}, device_id_type=MESH,
            )

        def all_of(length, make, act):
            def one(k, _):
                act(make(k))
                return 0

            lax.fori_loop(1, length, one, 0)

        def sum_round(p):
            if p == 0:
                here[me] = g_own[me]
                all_of(devices, spread, lambda x: x.start())
            elif p == 1:
                all_of(devices, spread, lambda x: x.wait())
                level[d] = jnp.sum(here[...], axis=0)
                all_of(n, across, lambda x: x.start())
            elif p == 2:
                all_of(n, across, lambda x: x.wait())
                g_all[me] = jnp.sum(level[...], axis=0)
                all_of(devices, tell, lambda x: x.start())
            else:
                all_of(devices, tell, lambda x: x.wait())

        marks = sorted(set(begins) | set(ends) | set(rounds) | {blocks, 2 * blocks})
        at = 0
        for mark in marks:
            if at < blocks:
                lax.fori_loop(at, min(mark, blocks), kernel_block, 0)
            else:
                lax.fori_loop(at - blocks, mark - blocks, input_block, 0)
            at = mark
            if mark in ends:
                halving_end(ends[mark])
            if mark in begins:
                halving_begin(begins[mark])
            if mark == first_due:
                sum_round(0)
            if mark == blocks:
                load_d.wait()

                @pl.when(has_up)
                def _():
                    down.wait_recv()

                @pl.when(has_down)
                def _():
                    up.wait_recv()
            if mark in rounds:
                sum_round(rounds[mark])
        sum_round(2)
        halving_begin(steps - 1)
        halving_end(steps - 1)
        sum_round(3)

        @pl.when(has_up)
        def _():
            up.wait_send()

        @pl.when(has_down)
        def _():
            down.wait_send()

    whole = pl.BlockSpec(memory_space=pl.ANY)
    local = pl.BlockSpec(memory_space=pltpu.VMEM)
    vm, dma = pltpu.VMEM, pltpu.SemaphoreType.DMA
    d_in, g_all, *extra = pl.pallas_call(
        kernel,
        out_shape=(
            jax.ShapeDtypeStruct((rows, cols, c), F32),
            jax.ShapeDtypeStruct((devices, small, c), F32),
            *plans[0].buffers(),
            *plans[1].buffers(),
        ),
        in_specs=[local] * 6 + [whole] * 4,
        out_specs=(local,) * 2 + (whole,) * (2 * each),
        scratch_shapes=[
            vm((high, cols, c), BF), vm((high, cols, c), BF), vm((rows, cols, c), BF),
            vm((high, cols + 2 * EDGE, LANES), F32), vm((high, cols + 2 * EDGE, LANES), F32),
            vm((devices, small, c), F32), vm((devices, small, c), F32), vm((n, small, c), F32),
            vm((2, 2, shape[0] // 2) + shape[1:], BF),
            dma((2,)), dma((2,)), dma((2,)), dma((4, max(2, shape[0] // 2))),
            dma((devices,)), dma((devices,)), dma((n,)), dma((n,)), dma((devices,)), dma((devices,)),
        ]
        + plans[0].semaphores() + plans[1].semaphores(),
        compiler_params=pltpu.CompilerParams(
            collective_id=3, has_side_effects=True, vmem_limit_bytes=50 * MIB
        ),
        cost_estimate=pl.CostEstimate(flops=6 * 10**10, bytes_accessed=10**8, transcendentals=0),
    )(
        d_normed, conv_out, gain, mask, w, low_gains, bordered, d_map,
        grads[0].reshape((shape[0] // 2, 2) + shape[1:]), grads[1].reshape((2, shape[0] // 2) + shape[1:]),
    )
    sums = g_all.reshape(devices * small, c)[:count]
    return d_in, sums, [extra[each - 1].reshape(shape[1:]), extra[2 * each - 1].reshape(shape[1:])]


GATE, OUT, HIGH_A, HIGH_B, QUERY, KEY, VALUE, PROJ = range(8)
L_LOW, L_DF, L_POOL_A, L_POOL_B, L_FIRST, L_DA, L_SECOND, L_COT = range(8)
R_DGATE, R_MERGE, R_DHIGH, R_DQ, R_DK, R_DV, R_ATT, R_DUP, R_ACT = range(9)


def nn(a, b):
    return jnp.dot(a, b, preferred_element_type=F32)


def nt(a, b):
    return lax.dot_general(a, b, (((1,), (1,)), ((), ())), preferred_element_type=F32)


def tn(a, b):
    return lax.dot_general(a, b, (((0,), (0,)), ((), ())), preferred_element_type=F32)


def normalise(x, gain):
    centred = x - jnp.mean(x, -1, keepdims=True)
    rate = lax.rsqrt(jnp.mean(centred * centred, -1, keepdims=True) + 1e-06)
    return centred * rate * gain


def normalise_back(x, gain, d):
    centred = x - jnp.mean(x, -1, keepdims=True)
    rate = lax.rsqrt(jnp.mean(centred * centred, -1, keepdims=True) + 1e-06)
    hat = centred * rate
    dg = d * gain
    back = rate * (dg - jnp.mean(dg, -1, keepdims=True) - hat * jnp.mean(dg * hat, -1, keepdims=True))
    return back, jnp.sum(d * hat, axis=0, keepdims=True)


def low_stage(low, pooled, cot, gain1, gain2, packed, n, devices, cid):
    t, dim = low.shape
    every = n * t
    width = dim // n
    heads = width // HEAD
    groups = width // LANES
    pairs = devices // 2
    rows = dim // devices
    half = dim // 2
    ff = 4 * dim
    natural = rows % LANES == 0
    high_rows = pooled.shape[1] // devices

    def place_of(k):
        return (k % 2) * half + k // 2 * rows

    def in_order(ref):
        if not natural:
            return ref[...]
        order = sorted(range(devices), key=place_of)
        return jnp.concatenate([ref[:, k * rows : (k + 1) * rows] for k in order], axis=1)

    scale = HEAD ** (-0.5)

    def kernel(
        low_ref, pooled_ref, cot_ref, gain1_ref, gain2_ref, w_hbm,
        low_out, d_low, d_pooled, g_ln1, g_ln2, grads,
        wv, lhs, lhs2, rhs, gate, high, merged, resid, d_res, slope, mixed, heads_in, att_all, d_att, d_mixed,
        d_heads, probs, d_scores, stage, left, w_sem, q_send, q_got, a_send, a_got, b_send, b_got, c_send, c_got, own_sem,
        l_send, l_got, r_send, r_got, stage_sem,
    ):
        d = lax.axis_index("mp")
        dp = lax.axis_index("dp")
        core = lax.rem(dp, 2)
        mate = dp + 1 - 2 * core
        barrier = pltpu.get_barrier_semaphore()
        for k in range(1, n):
            pl.semaphore_signal(barrier, inc=1, device_id={"mp": lax.rem(d + k, n)}, device_id_type=MESH)
        pl.semaphore_signal(barrier, inc=1, device_id={"dp": mate}, device_id_type=MESH)

        def w_copy(w, k):
            c, z = k // n, lax.rem(k, n)
            wide, base, at = w_place(w)
            src = w_hbm.at[:, c, z, :, pl.ds(base, wide)]
            dst = wv.at[c, :, :, pl.ds(pl.multiple_of(at + z * wide, wide), wide)]
            return pltpu.make_async_copy(src, dst, w_sem.at[w, k])

        def w_place(w):
            if w < 8:
                return width, w * width, w * dim
            return ff // n, 8 * width + (w - 8) * ff // n, 8 * dim + (w - 8) * ff

        def w_each(w, act):
            def one(k, _):
                act(w_copy(w, k))
                return 0

            lax.fori_loop(0, 2 * n, one, 0)

        for w in (GATE, HIGH_A, HIGH_B, OUT, QUERY, KEY, VALUE, PROJ):
            w_each(w, lambda copy: copy.start())

        def w_wait(*which):
            for w in which:
                w_each(w, lambda copy: copy.wait())

        def w_cols(at, size):
            return wv[:, :, :, pl.ds(at, size)].reshape(dim, size)

        def forward(x, first, count, put):
            def one(i, _):
                put(pl.multiple_of(i * LOW_TILE, LOW_TILE), nn(x, w_cols(pl.multiple_of(first * dim + i * LOW_TILE, LOW_TILE), LOW_TILE)))
                return 0
            lax.fori_loop(0, count * dim // LOW_TILE, one, 0)

        def backward(get, first, count, dst, fresh):
            def one(i, _):
                for c in range(2):
                    part = wv[c, :, :, pl.ds(pl.multiple_of((first + i) * dim, dim), dim)].reshape(half, dim)
                    y = nt(get(pl.multiple_of(i * dim, dim)), part)
                    cols = slice(c * half, (c + 1) * half)
                    if fresh and count == 1:
                        dst[:, cols] = y
                    else:
                        dst[:, cols] += y
                return 0
            if fresh and count > 1:
                dst[...] = jnp.zeros(dst.shape, F32)
            if count == 1:
                one(0, 0)
            else:
                lax.fori_loop(0, count, one, 0)

        def r_cols(block, count=1):
            return pl.ds(block * dim, count * dim)

        def r_at(block):
            return block * dim if block <= R_DUP else block * dim + 3 * dim

        def r_copy(block):
            cols = pl.ds(r_at(block), dim if block < R_DUP else ff)
            return pltpu.make_async_remote_copy(
                src_ref=rhs.at[0, :, cols], dst_ref=rhs.at[1, :, cols], send_sem=r_send.at[block],
                recv_sem=r_got.at[block], device_id={"dp": mate}, device_id_type=MESH)

        def l_copy(i):
            return pltpu.make_async_remote_copy(
                src_ref=lhs.at[i, :, pl.ds(pl.multiple_of((1 - core) * half, half), half)], dst_ref=lhs2.at[i],
                send_sem=l_send.at[i], recv_sem=l_got.at[i], device_id={"dp": mate}, device_id_type=MESH)

        stored = []
        turned = [None]

        def put_natural(dst, value):
            if natural:
                for k in range(devices):
                    dst[:, k * rows : (k + 1) * rows] = value[:, place_of(k) : place_of(k) + rows]
            else:
                dst[...] = value

        def grad(i, block, at, count, shared=False):
            if not shared:
                r_copy(block).wait_recv()
            if turned[0] != i:
                left[0] = lhs[i, :, pl.ds(pl.multiple_of(core * half, half), half)].T
                left[1] = lhs2[i].T
                turned[0] = i

            wide, base, first = w_place(at if at < 8 else 8 + (at - 8) * dim // ff)
            piece = min(GRAD_TILE, wide)

            def out_copies(slot, k):
                out = []
                for q in range(GRAD_TILE // piece):
                    z, col = divmod(at * dim - first + k * GRAD_TILE + q * piece, wide)
                    out.append(
                        pltpu.make_async_copy(
                            stage.at[slot, :, :, pl.ds(q * piece, piece)],
                            grads.at[:, pl.ds(z * rows, rows), pl.ds(base + col, piece)],
                            stage_sem.at[slot, q],
                        )
                    )
                return out

            for k in range(count * dim // GRAD_TILE):
                slot = len(stored) % 2
                if len(stored) >= 2:
                    wait(stored[-2])
                cols = pl.ds(r_at(block) + k * GRAD_TILE, GRAD_TILE)
                y = nn(left[0], rhs[0, :, cols]) + nn(left[1], rhs[1, :, cols])
                stage[slot] = y.astype(BF).reshape(pairs, rows, GRAD_TILE)
                stored.append(out_copies(slot, k))
                start(stored[-1])

        def to_heads(k, src, dst, send, got):
            out = []
            for step in range(1, n):
                peer = lax.rem(d + step, n)
                out.append(pltpu.make_async_remote_copy(
                    src_ref=src.at[:, pl.ds(pl.multiple_of(peer * width, width), width)],
                    dst_ref=dst.at[pl.ds(pl.multiple_of(d * t, t), t)],
                    send_sem=send.at[k, step], recv_sem=got.at[k, step], device_id={"mp": peer}, device_id_type=MESH))
            out.append(pltpu.make_async_copy(
                src.at[:, pl.ds(pl.multiple_of(d * width, width), width)], dst.at[pl.ds(pl.multiple_of(d * t, t), t)], own_sem.at[k]))
            return out

        def to_tokens(k, src, dst, send, got, group):
            out = []
            slot = k * groups + group
            lanes = pl.ds(group * LANES, LANES)
            there = pl.ds(pl.multiple_of(d * width + group * LANES, LANES), LANES)
            for step in range(1, n):
                peer = lax.rem(d + step, n)
                out.append(pltpu.make_async_remote_copy(
                    src_ref=src.at[pl.ds(pl.multiple_of(peer * t, t), t), lanes], dst_ref=dst.at[:, there],
                    send_sem=send.at[slot, step], recv_sem=got.at[slot, step], device_id={"mp": peer}, device_id_type=MESH))
            out.append(pltpu.make_async_copy(
                src.at[pl.ds(pl.multiple_of(d * t, t), t), lanes], dst.at[:, there], own_sem.at[slot]))
            return out

        def start(copies):
            for c in copies:
                c.start()

        def wait(copies):
            for c in copies:
                c.wait()

        gain1_here, gain2_here = in_order(gain1_ref), in_order(gain2_ref)
        if natural:
            for i, ref in ((L_LOW, low_ref), (L_COT, cot_ref)):
                for k in range(devices):
                    lhs[i, :, place_of(k) : place_of(k) + rows] = ref[:, k * rows : (k + 1) * rows]
            for k in range(devices):
                own = slice(place_of(k), place_of(k) + rows)
                lhs[L_POOL_A, :, own] = pooled_ref[:, k * high_rows : k * high_rows + rows].astype(BF)
                more = pooled_ref[:, k * high_rows + rows : (k + 1) * high_rows].astype(BF)
                lhs[L_POOL_B, :, own] = jnp.concatenate([more, jnp.zeros((t, 2 * rows - high_rows), BF)], axis=1)
        else:
            lhs[L_LOW] = low_ref[...]
            lhs[L_COT] = cot_ref[...]
            lhs[L_POOL_A] = pooled_ref[:, :dim].astype(BF)
            lhs[L_POOL_B] = pooled_ref[:, dim:].astype(BF)
        acc = d_low
        w_wait(GATE)

        def put_gate(at, y):
            gate[:, pl.ds(at, LOW_TILE)] = 1.0 / (1.0 + jnp.exp(-y))
        forward(lhs[L_LOW], GATE, 1, put_gate)
        w_wait(HIGH_A, HIGH_B, OUT)
        for w in (8, 9):
            w_each(w, lambda copy: copy.start())

        def put_high(at, y):
            high[:, pl.ds(at, LOW_TILE)] = y
        forward(lhs[L_POOL_A], HIGH_A, 1, put_high)

        def put_merging(at, y):
            cols = pl.ds(at, LOW_TILE)
            total = high[:, cols] + y
            high[:, cols] = total
            rhs[0, :, pl.ds(R_MERGE * dim + at, LOW_TILE)] = (total * gate[:, cols]).astype(BF)
        forward(lhs[L_POOL_B], HIGH_B, 1, put_merging)
        backward(lambda at: rhs[0, :, r_cols(R_MERGE)], OUT, 1, merged, True)
        merged[...] += lhs[L_LOW].astype(F32)
        lhs[L_FIRST] = normalise(merged[...], gain1_here).astype(BF)

        w_wait(QUERY, KEY, VALUE, PROJ)
        pl.semaphore_wait(barrier, n)
        for i in (L_LOW, L_POOL_A, L_POOL_B, L_COT, L_FIRST):
            l_copy(i).start()
        r_copy(R_MERGE).start()
        out_q = []
        for k in range(3):
            def put_mixed(at, y):
                mixed[k, :, pl.ds(at, LOW_TILE)] = y.astype(BF)
            forward(lhs[L_FIRST], QUERY + k, 1, put_mixed)
            copies = to_heads(k, mixed.at[k], heads_in.at[k], q_send, q_got)
            start(copies)
            out_q.append(copies)
        wait(out_q[0] + out_q[1])

        for h in range(heads):
            lanes = slice(h * HEAD, (h + 1) * HEAD)

            def rows_of(b, _):
                some = pl.ds(pl.multiple_of(b * t, t), t)
                s = nt(heads_in[0, some, lanes], heads_in[1, :, lanes]) * scale
                e = jnp.exp(s - jnp.max(s, -1, keepdims=True))
                p = (e * (1.0 / jnp.sum(e, -1, keepdims=True))).astype(BF)
                probs[h, some] = p
                return 0
            lax.fori_loop(0, n, rows_of, 0)
        wait(out_q[2])
        out_a = []
        for h in range(heads):
            lanes = slice(h * HEAD, (h + 1) * HEAD)

            def attend(b, _):
                some = pl.ds(pl.multiple_of(b * t, t), t)
                att_all[some, lanes] = nn(probs[h, some], heads_in[2, :, lanes]).astype(BF)
                return 0
            lax.fori_loop(0, n, attend, 0)
            if (h + 1) * HEAD % LANES == 0:
                copies = to_tokens(0, att_all, rhs.at[0, :, r_cols(R_ATT)], a_send, a_got, h * HEAD // LANES)
                start(copies)
                out_a += copies
        wait(out_a)
        r_copy(R_ATT).start()
        backward(lambda at: rhs[0, :, r_cols(R_ATT)], PROJ, 1, resid, True)
        resid[...] += merged[...]
        lhs[L_SECOND] = normalise(resid[...], gain2_here).astype(BF)
        l_copy(L_SECOND).start()

        w_wait(8)

        def put_up(at, y):
            value, rate = gelu_parts(y)
            rhs[0, :, pl.ds(r_at(R_ACT) + at, LOW_TILE)] = value.astype(BF)
            slope[:, pl.ds(at, LOW_TILE)] = rate.astype(BF)
        forward(lhs[L_SECOND], 8, 4, put_up)
        r_copy(R_ACT).start()
        w_wait(9)
        backward(lambda at: rhs[0, :, pl.ds(r_at(R_ACT) + at, dim)], 12, 4, acc, True)
        put_natural(low_out, resid[...] + acc[...])

        def put_d_up(at, y):
            rhs[0, :, pl.ds(r_at(R_DUP) + at, LOW_TILE)] = (y * slope[:, pl.ds(at, LOW_TILE)].astype(F32)).astype(BF)
        forward(lhs[L_COT], 12, 4, put_d_up)
        r_copy(R_DUP).start()
        backward(lambda at: rhs[0, :, pl.ds(r_at(R_DUP) + at, dim)], 8, 4, acc, True)
        back, g = normalise_back(resid[...], gain2_here, acc[...])
        put_natural(g_ln2, g)
        d_res[...] = lhs[L_COT].astype(F32) + back
        lhs[L_DA] = d_res[...].astype(BF)
        l_copy(L_DA).start()

        def put_d_att(at, y):
            mixed[0, :, pl.ds(at, LOW_TILE)] = y.astype(BF)
        forward(lhs[L_DA], PROJ, 1, put_d_att)
        out_b = to_heads(0, mixed.at[0], d_att, b_send, b_got)
        start(out_b)
        l_copy(L_COT).wait_recv()
        grad(L_COT, R_ACT, 12, 4)
        wait(out_b)
        out_c = []

        def send_back(k, h):
            if (h + 1) * HEAD % LANES == 0:
                copies = to_tokens(k, d_heads.at[k], rhs.at[0, :, r_cols(R_DQ + k)], c_send, c_got, h * HEAD // LANES)
                start(copies)
                out_c.extend(copies)

        for h in range(heads):
            lanes = slice(h * HEAD, (h + 1) * HEAD)
            d_heads[2, :, lanes] = tn(probs[h], d_att[:, lanes]).astype(BF)
            send_back(2, h)
        for h in range(heads):
            lanes = slice(h * HEAD, (h + 1) * HEAD)

            def rows_of(b, _):
                some = pl.ds(pl.multiple_of(b * t, t), t)
                p = probs[h, some].astype(F32)
                dp_ = nt(d_att[some, lanes], heads_in[2, :, lanes])
                ds = (p * (dp_ - jnp.sum(dp_ * p, -1, keepdims=True)) * scale).astype(BF)
                d_scores[some] = ds
                d_heads[0, some, lanes] = nn(ds, heads_in[1, :, lanes]).astype(BF)
                return 0
            lax.fori_loop(0, n, rows_of, 0)
            d_heads[1, :, lanes] = tn(d_scores[...], heads_in[0, :, lanes]).astype(BF)
            send_back(0, h)
            send_back(1, h)
        l_copy(L_SECOND).wait_recv()
        grad(L_SECOND, R_DUP, 8, 4)
        l_copy(L_DA).wait_recv()
        grad(L_DA, R_ATT, PROJ, 1)
        wait(out_c)
        for k in range(3):
            r_copy(R_DQ + k).start()
        backward(lambda at: rhs[0, :, pl.ds(R_DQ * dim + at, dim)], QUERY, 3, acc, True)
        back, g = normalise_back(merged[...], gain1_here, acc[...])
        put_natural(g_ln1, g)
        d_res[...] += back
        lhs[L_DF] = d_res[...].astype(BF)
        l_copy(L_DF).start()

        def put_d_gate(at, y):
            cols = pl.ds(at, LOW_TILE)
            gv = gate[:, cols]
            part = y * gv
            rhs[0, :, pl.ds(R_DHIGH * dim + at, LOW_TILE)] = part.astype(BF)
            rhs[0, :, pl.ds(R_DGATE * dim + at, LOW_TILE)] = (part * high[:, cols] * (1.0 - gv)).astype(BF)
        forward(lhs[L_DF], OUT, 1, put_d_gate)
        r_copy(R_DHIGH).start()
        r_copy(R_DGATE).start()
        backward(lambda at: rhs[0, :, r_cols(R_DHIGH)], HIGH_A, 1, gate, True)
        backward(lambda at: rhs[0, :, r_cols(R_DHIGH)], HIGH_B, 1, high, True)
        if natural:
            for k in range(devices):
                at = place_of(k)
                d_pooled[:, k * high_rows : k * high_rows + rows] = gate[:, at : at + rows]
                d_pooled[:, k * high_rows + rows : (k + 1) * high_rows] = high[:, at : at + high_rows - rows]
        else:
            d_pooled[:, :dim] = gate[...]
            d_pooled[:, dim:] = high[...]
        backward(lambda at: rhs[0, :, r_cols(R_DGATE)], GATE, 1, acc, True)
        put_natural(d_low, d_res[...] + acc[...])
        l_copy(L_FIRST).wait_recv()
        for k in range(3):
            grad(L_FIRST, R_DQ + k, QUERY + k, 1)
        l_copy(L_DF).wait_recv()
        grad(L_DF, R_MERGE, OUT, 1)
        l_copy(L_POOL_A).wait_recv()
        grad(L_POOL_A, R_DHIGH, HIGH_A, 1)
        l_copy(L_POOL_B).wait_recv()
        grad(L_POOL_B, R_DHIGH, HIGH_B, 1, shared=True)
        l_copy(L_LOW).wait_recv()
        grad(L_LOW, R_DGATE, GATE, 1)
        wait(stored[-2])
        wait(stored[-1])
        for i in range(8):
            l_copy(i).wait_send()
        for b in range(9):
            r_copy(b).wait_send()

    whole = pl.BlockSpec(memory_space=pl.ANY)
    local = pl.BlockSpec(memory_space=pltpu.VMEM)
    vm, dma = pltpu.VMEM, pltpu.SemaphoreType.DMA
    tok = jax.ShapeDtypeStruct((t, dim), F32)
    one = jax.ShapeDtypeStruct((1, dim), F32)
    return pl.pallas_call(
        kernel,
        out_shape=(tok, tok, jax.ShapeDtypeStruct(pooled.shape, F32), one, one, jax.ShapeDtypeStruct((pairs, n * rows, 16 * width), BF)),
        in_specs=[local] * 5 + [whole],
        out_specs=(local,) * 5 + (whole,),
        scratch_shapes=[
            vm((2, pairs, rows, 16 * dim), BF), vm((8, t, dim), BF), vm((8, t, half), BF), vm((2, t, 15 * dim), BF),
            vm((t, dim), F32), vm((t, dim), F32), vm((t, dim), F32), vm((t, dim), F32), vm((t, dim), F32),
            vm((t, ff), BF), vm((3, t, dim), BF), vm((3, every, width), BF), vm((every, width), BF), vm((every, width), BF),
            vm((1, 8, 128), BF), vm((3, every, width), BF), vm((heads, every, every), BF), vm((every, every), BF),
            vm((2, pairs, rows, GRAD_TILE), BF), vm((2, half, t), BF),
            dma((10, 2 * n)), dma((3, n)), dma((3, n)), dma((groups, n)), dma((groups, n)), dma((1, n)), dma((1, n)),
            dma((3 * groups, n)), dma((3 * groups, n)), dma((3 * groups,)), dma((8,)), dma((8,)), dma((9,)), dma((9,)), dma((2, 2)),
        ],
        compiler_params=pltpu.CompilerParams(collective_id=cid, has_side_effects=True, vmem_limit_bytes=62 * MIB),
        cost_estimate=pl.CostEstimate(flops=14 * 10**9, bytes_accessed=70 * 10**6, transcendentals=10**7),
    )(low, pooled, cot, gain1, gain2, packed.reshape(pairs, 2, n, rows, 16 * width))
def low_outputs(own, widths, high_rows):
    share = own.shape[0]
    width, wide = widths[0], widths[-1]

    def kernel(x, gate, high, out, qkv, proj, up, down):
        def part(i, size=width):
            at = sum(widths[:i])
            return x[:, at : at + size].astype(F32)

        gate[...] = part(0)
        out[...] = part(1).T
        high[:share] = part(2)
        high[share:] = part(3)[: high_rows - share]
        for k in range(3):
            qkv[k] = part(4 + k)
        proj[...] = part(7).T
        up[...] = part(8, wide)
        down[...] = part(9, wide).T

    local = pl.BlockSpec(memory_space=pltpu.VMEM)
    shapes = [
        (share, width), (high_rows, width), (width, share), (3, share, width), (width, share), (share, wide), (wide, share),
    ]
    return pl.pallas_call(
        kernel,
        out_shape=[jax.ShapeDtypeStruct(s, F32) for s in shapes],
        in_specs=[local],
        out_specs=[local] * 7,
        compiler_params=pltpu.CompilerParams(vmem_limit_bytes=32 * MIB),
    )(own)


def map_outputs(g_up, g_down, others):
    count = len(others)

    def kernel(up, down, *rest):
        sources, o_up, o_down = rest[:count], rest[count], rest[count + 1]
        targets, held, sems = rest[count + 2 : 2 * count + 2], rest[2 * count + 2 : -1], rest[-1]
        loads = [pltpu.make_async_copy(a, b, sems.at[0, i]) for i, (a, b) in enumerate(zip(sources, held))]
        saves = [pltpu.make_async_copy(a, b, sems.at[1, i]) for i, (a, b) in enumerate(zip(held, targets))]
        for load in loads:
            load.start()
        o_up[...] = up[...].astype(F32)
        o_down[...] = down[...].astype(F32)
        for load, save in zip(loads, saves):
            load.wait()
            save.start()
        for save in saves:
            save.wait()

    whole = pl.BlockSpec(memory_space=pl.ANY)
    local = pl.BlockSpec(memory_space=pltpu.VMEM)
    return pl.pallas_call(
        kernel,
        out_shape=[jax.ShapeDtypeStruct(x.shape, F32) for x in (g_up, g_down, *others)],
        in_specs=[local] * 2 + [whole] * count,
        out_specs=[local] * 2 + [whole] * count,
        scratch_shapes=[pltpu.VMEM(o.shape, o.dtype) for o in others] + [pltpu.SemaphoreType.DMA((2, count))],
        compiler_params=pltpu.CompilerParams(vmem_limit_bytes=60 * MIB),
        cost_estimate=pl.CostEstimate(flops=10**9, bytes_accessed=24 * 10**6, transcendentals=0),
    )(g_up, g_down, *others)


def pack_weights(ad_gate, ad_out, ad_high, w_qkv, w_proj, w_up, w_down, devices):
    dim, width = ad_gate.shape
    share, high_rows, wide = dim // devices, ad_high.shape[0] // devices, w_up.shape[1]
    rest = high_rows - share

    def kernel(gate, out, high, qkv, proj, up, down, packed, side, side_wide, sems):
        me = lax.axis_index("dp")
        mine = pl.ds(pl.multiple_of(me * share, share), share)
        lanes = mine

        def at(i, size=width):
            return packed.at[:, pl.ds(i * width, size)]

        straight = [(gate.at[mine], at(0)), (up.at[mine], at(8, wide))]
        straight += [(qkv.at[k, mine], at(4 + k)) for k in range(3)]
        straight.append((high.at[pl.ds(pl.multiple_of(me * high_rows, rest), share)], at(2)))
        straight.append((high.at[pl.ds(pl.multiple_of(me * high_rows + share, rest), rest)], at(3).at[pl.ds(0, rest)]))
        straight += [(out.at[:, lanes], side.at[0]), (proj.at[:, lanes], side.at[1]), (down.at[:, lanes], side_wide)]
        copies = [pltpu.make_async_copy(a, b, sems.at[i]) for i, (a, b) in enumerate(straight)]
        for copy in copies:
            copy.start()
        packed[rest:, 3 * width : 4 * width] = jnp.zeros((share - rest, width), BF)
        for copy in copies:
            copy.wait()
        packed[:, width : 2 * width] = side[0].T
        packed[:, 7 * width : 8 * width] = side[1].T
        packed[:, 8 * width + wide :] = side_wide[...].T

    whole = pl.BlockSpec(memory_space=pl.ANY)
    return pl.pallas_call(
        kernel,
        out_shape=jax.ShapeDtypeStruct((share, 8 * width + 2 * wide), BF),
        in_specs=[whole] * 7,
        out_specs=pl.BlockSpec(memory_space=pltpu.VMEM),
        scratch_shapes=[
            pltpu.VMEM((2, width, share), BF), pltpu.VMEM((wide, share), BF), pltpu.SemaphoreType.DMA((10,)),
        ],
        compiler_params=pltpu.CompilerParams(vmem_limit_bytes=60 * MIB),
    )(ad_gate, ad_out, ad_high, w_qkv, w_proj, w_up, w_down)


def rows_first(x):
    return with_layout_constraint(x, Layout(major_to_minor=tuple(range(x.ndim))))


def own_part(w, axis):
    length = w.shape[axis] // lax.axis_size("dp")
    return lax.dynamic_slice_in_dim(w, lax.axis_index("dp") * length, length, axis)


def fold(w, rows):
    return w[:rows], jnp.pad(w[rows:], ((0, 2 * rows - w.shape[0]), (0, 0)))


def core_first(x, devices):
    shape = x.shape
    return x.reshape(shape[:-1] + (devices // 2, 2, -1)).swapaxes(-3, -2).reshape(shape)


def core_last(x, devices):
    shape = x.shape
    return x.reshape(shape[:-1] + (2, devices // 2, -1)).swapaxes(-3, -2).reshape(shape)


def layer_norm(values, gain):
    centre = jnp.mean(values, -1, keepdims=True)
    centred = values - centre
    variance = jnp.mean(centred * centred, -1, keepdims=True)
    return centred * lax.rsqrt(variance + 1e-06) * gain


def per_device(
    hr_in,
    low_in,
    valid,
    conv_w,
    hr_gain,
    cn_up,
    cn_down,
    ad_gate,
    ad_high,
    ad_out,
    ln1_gain,
    w_qkv,
    w_proj,
    ln2_gain,
    w_up,
    w_down,
    cot_low,
    cot_hr,
):
    _, row_count, col_count, chan_count = hr_in.shape
    devices, shards = lax.axis_size("dp"), lax.axis_size("mp")
    dims = low_in.shape[2]
    share = dims // devices
    qkv = own_part(w_qkv, 1)
    low_weights = (ad_gate, ad_out, ad_high, w_qkv, w_proj, w_up, w_down)
    pieces = [
        own_part(ad_gate, 0), own_part(ad_out, 1).T, *fold(own_part(ad_high, 0), share),
        qkv[0], qkv[1], qkv[2], own_part(w_proj, 1).T, own_part(w_up, 0), own_part(w_down, 1).T,
    ]
    if share % LANES:
        packed = rows_first(jnp.concatenate(pieces, axis=1))
    else:
        packed = pack_weights(*low_weights, devices)
    packed = rows_first(lax.all_gather(packed, "mp", axis=0, tiled=True))
    plane_mask = valid[0].astype(F32)
    cell_mask = plane_mask[..., None]
    masked = hr_in[0] * valid[0].astype(BF)[..., None]
    half_rows, half_cols = (row_count // 2, col_count // 2)
    counts = plane_mask.reshape(half_rows, 2, half_cols, 2).sum(axis=(1, 3))
    shares = 1.0 / jnp.maximum(counts, 1.0)
    size = conv_w.shape[0]
    taps = conv_w.astype(F32).reshape(size * size, 1, chan_count)
    conv_out, bordered = conv_forward(masked, taps, size, shards)
    hr_gainf = hr_gain.astype(F32)
    normed = layer_norm(conv_out * cell_mask, hr_gainf).astype(BF)
    normed, packed = lax.optimization_barrier((normed, packed))
    packed = rows_first(lax.all_gather(packed, "dp", axis=0, tiled=True))
    hr_out, pooled, normed_all, hidden_act, hidden_slope, up_t, down_t = big_forward(
        normed.reshape(row_count * col_count, chan_count), cn_up, cn_down, masked, cell_mask, shares, shards
    )
    hr_out = hr_out.reshape(hr_in.shape)
    tokens = half_rows * half_cols
    low_ins, gains = [low_in[0], pooled, cot_low[0]], [ln1_gain.astype(F32)[None], ln2_gain.astype(F32)[None]]
    if share % LANES:
        by_share = pooled.reshape(tokens, devices, -1)
        pool_a = by_share[:, :, :share].reshape(tokens, dims)
        pool_b = by_share[:, :, share:]
        pool_b = jnp.pad(pool_b, ((0, 0), (0, 0), (0, share - pool_b.shape[2]))).reshape(tokens, dims)
        low_ins = [core_first(low_in[0], devices), None, core_first(cot_low[0], devices)]
        low_ins[1] = jnp.concatenate([core_first(pool_a, devices), core_first(pool_b, devices)], axis=1)
        gains = [core_first(g, devices) for g in gains]
    low_out, d_low_in, d_pooled, g_ln1, g_ln2, low_grads = low_stage(*low_ins, *gains, packed, shards, devices, 2)
    if share % LANES:
        low_out, d_low_in = core_last(low_out, devices), core_last(d_low_in, devices)
        g_ln1, g_ln2 = core_last(g_ln1, devices), core_last(g_ln2, devices)
        d_pooled = jnp.concatenate(
            [
                core_last(d_pooled[:, :dims], devices).reshape(tokens, devices, share),
                core_last(d_pooled[:, dims:], devices).reshape(tokens, devices, share)[:, :, : by_share.shape[2] - share],
            ],
            axis=2,
        ).reshape(tokens, chan_count)
    low_out, d_low_in, g_ln1, g_ln2 = low_out[None], d_low_in[None], g_ln1[0], g_ln2[0]
    d_normed, d_map, cn_grads, low_sums = big_backward(
        cot_hr[0], d_pooled, shares, cell_mask, normed_all, hidden_act, hidden_slope,
        up_t, down_t, low_grads, shards, devices,
    )
    low_sums = rows_first(low_sums.reshape(shards, share, -1))
    low_sums = rows_first(lax.psum_scatter(low_sums, "mp", scatter_dimension=0))
    low_gains = jnp.pad(jnp.stack([g_ln1, g_ln2]), ((0, 0), (0, chan_count - dims)))
    d_hr_in, small_sums, (g_cn_up, g_cn_down) = conv_backward(
        d_normed, conv_out, hr_gainf[None], cell_mask, bordered, d_map, taps, low_gains, size, cn_grads, devices, shards
    )
    d_hr_in = d_hr_in[None]
    g_conv = small_sums[: size * size].reshape(conv_w.shape)
    g_hr_gain, g_ln1, g_ln2 = small_sums[size * size], small_sums[-2, :dims], small_sums[-1, :dims]
    g_cn_up, g_cn_down, low_out, hr_out, d_low_in, d_hr_in = map_outputs(
        g_cn_up, g_cn_down, (low_out, hr_out, d_low_in, d_hr_in)
    )
    g_ad_gate, g_ad_high, g_ad_out, g_qkv, g_proj, g_up, g_down = low_outputs(
        low_sums.reshape(share, -1), [p.shape[1] for p in pieces], ad_high.shape[0] // devices
    )
    g_cn_down = g_cn_down.T
    return (
        low_out,
        hr_out,
        d_low_in,
        d_hr_in,
        g_conv,
        g_hr_gain,
        g_cn_up,
        g_cn_down,
        g_ad_gate,
        g_ad_high,
        g_ad_out,
        g_ln1,
        g_qkv,
        g_proj,
        g_ln2,
        g_up,
        g_down,
    )


def solution(mesh):
    return jax.shard_map(
        per_device,
        mesh=mesh,
        in_specs=(
            P("dp", "mp", None, None),
            P("dp", "mp", None),
            P("dp", "mp", None),
            P(),
            P(),
            P(None, "mp"),
            P("mp", None),
            P(None, "mp"),
            P(None, "mp"),
            P("mp", None),
            P(),
            P(None, None, "mp"),
            P("mp", None),
            P(),
            P(None, "mp"),
            P("mp", None),
            P("dp", "mp", None),
            P("dp", "mp", None, None),
        ),
        out_specs=(
            P("dp", "mp", None),
            P("dp", "mp", None, None),
            P("dp", "mp", None),
            P("dp", "mp", None, None),
            P(),
            P(),
            P("dp", "mp"),
            P("mp", "dp"),
            P("dp", "mp"),
            P("dp", "mp"),
            P("mp", "dp"),
            P(),
            P(None, "dp", "mp"),
            P("mp", "dp"),
            P(),
            P("dp", "mp"),
            P("mp", "dp"),
        ),
        check_vma=False,
    )
```

```python
import jax
import jax.numpy as jnp
from jax import lax
from jax.experimental.layout import Layout, with_layout_constraint
from jax.experimental import pallas as pl
from jax.experimental.pallas import tpu as pltpu
from jax.sharding import PartitionSpec as P

HEAD = 64
LANES = 128
EDGE = 8
CHUNKS = 6
TILE = 1536
LOW_TILE = 1024
GRAD_TILE = 512
MIB = 1024 * 1024
MESH = pl.DeviceIdType.MESH
BF = jnp.bfloat16
F32 = jnp.float32

def gelu_parts(x):
    c = 0.7978845608028654
    x2 = x * x
    t = jnp.tanh(c * x * (1.0 + 0.044715 * x2))
    half = 0.5 * (1.0 + t)
    slope = half + 0.5 * x * (1.0 - t * t) * (c * (1.0 + 3 * 0.044715 * x2))
    return x * half, slope


def gelu(x):
    c = 0.7978845608028654
    t = jnp.tanh(c * x * (1.0 + 0.044715 * (x * x)))
    return 0.5 * x * (1.0 + t)


def dp_bit(position):
    return lax.rem(lax.axis_index("dp") // 2**position, 2)


def dp_mate(position):
    return lax.axis_index("dp") + 2**position * (1 - 2 * dp_bit(position))


class Halving:
    def __init__(self, bits, lasts, shape, block):
        self.lasts, self.shape, self.block = lasts, shape, block
        left = list(bits)
        self.bits = [left.pop(0 if last else -1) for last in lasts]

    def split(self, count, p):
        if count == 1:
            return (1, 1)
        return (count // 2, 2) if self.lasts[p] else (2, count // 2)

    def buffers(self):
        count, rows, cols = self.shape
        got, held = [], []
        for p in range(len(self.bits)):
            count //= 2
            got.append(jax.ShapeDtypeStruct((count, rows, cols), BF))
            held.append(jax.ShapeDtypeStruct(self.split(count, p + 1) + (rows, cols), BF))
        return got + held

    def semaphores(self):
        return [pltpu.SemaphoreType.DMA((len(self.bits),))] * 2

    def bind(self, first, buffers, send, recv):
        steps = len(self.bits)
        self.now = [first] + list(buffers[steps:])
        self.got, self.send, self.recv = buffers[:steps], send, recv

    def part(self, p, mine):
        bit = dp_bit(self.bits[p])
        index = bit if mine else 1 - bit
        return self.now[p].at[:, index] if self.lasts[p] else self.now[p].at[index]

    def copy(self, p):
        return pltpu.make_async_remote_copy(
            src_ref=self.part(p, False), dst_ref=self.got[p], send_sem=self.send.at[p], recv_sem=self.recv.at[p],
            device_id={"dp": dp_mate(self.bits[p])}, device_id_type=MESH,
        )

    def start(self, p):
        self.copy(p).start()

    def finish(self, p, wait=True):
        if wait:
            self.copy(p).wait()
        count, rows, cols = self.got[p].shape
        ways = self.split(count, p + 1)

        def add(a, b, out):
            out[...] = (a[...].astype(F32) + b[...].astype(F32)).astype(BF).reshape(out.shape)

        flat = pl.BlockSpec((1, rows, self.block), lambda k, c: (k, 0, c))
        paired = pl.BlockSpec((1, 1, rows, self.block), lambda k, c: (k // ways[1], lax.rem(k, ways[1]), 0, c))
        pltpu.emit_pipeline(add, grid=(count, cols // self.block), in_specs=[flat, flat], out_specs=[paired])(
            self.part(p, True), self.got[p], self.now[p + 1]
        )


def chain_exchange(
    n, chunks, lag, gathered, partial, travel, sems, own_chunk, prepare, arrived, compute, mates=(), begin=None, turn=None, after=None, early=False
):
    ag_send, ag_recv, rs_send, rs_recv = sems
    d = lax.axis_index("mp")
    has_left, has_right = d > 0, d < n - 1

    barrier = pltpu.get_barrier_semaphore()

    @pl.when(has_left)
    def _():
        pl.semaphore_signal(barrier, inc=1, device_id={"mp": d - 1}, device_id_type=MESH)

    @pl.when(has_right)
    def _():
        pl.semaphore_signal(barrier, inc=1, device_id={"mp": d + 1}, device_id_type=MESH)

    for mate in mates:
        pl.semaphore_signal(barrier, inc=1, device_id={"dp": mate}, device_id_type=MESH)

    own_chunk(0)
    pl.semaphore_wait(barrier, has_left.astype(jnp.int32) + has_right.astype(jnp.int32) + len(mates))
    if begin is not None:
        begin()

    def ag(way, s, j):
        return pltpu.make_async_remote_copy(
            src_ref=gathered.at[s, j], dst_ref=gathered.at[s, j],
            send_sem=ag_send.at[way, s, j], recv_sem=ag_recv.at[s, j],
            device_id={"mp": d + 1 - 2 * way}, device_id_type=MESH,
        )

    def rs(way, s, j):
        there = d + 1 - 2 * way
        slot = jnp.where((s == there) & (way == 0), n, s)
        return pltpu.make_async_remote_copy(
            src_ref=travel.at[s, j], dst_ref=travel.at[slot, j],
            send_sem=rs_send.at[s, j], recv_sem=rs_recv.at[slot, j],
            device_id={"mp": there}, device_id_type=MESH,
        )

    def rs_wait(slot, j):
        pltpu.make_async_copy(travel.at[slot, j], travel.at[slot, j], rs_recv.at[slot, j]).wait()

    def first(j, _):
        @pl.when(j > 0)
        def _():
            own_chunk(j)

        @pl.when(has_right)
        def _():
            ag(0, d, j).start()

        @pl.when(has_left)
        def _():
            ag(1, d, j).start()

        return 0

    lax.fori_loop(0, chunks, first, 0)

    def flow(way, q):
        ql = jnp.clip(q, 0, n * chunks - 1)
        s, jj = ql // chunks, lax.rem(ql, chunks)
        if way == 1:
            s = n - 1 - s
        ahead = (s > d) if way == 0 else (s < d)
        source = has_left if way == 0 else has_right

        @pl.when((q >= 0) & (q < n * chunks) & (ahead | ((s == d) & source)))
        def _():
            @pl.when(source)
            def _():
                rs_wait(jnp.where(s == d, n, s) if way == 0 else s, jj)

            @pl.when(ahead & source)
            def _():
                travel[s, jj] = (partial[s, jj].astype(F32) + travel[s, jj].astype(F32)).astype(BF)

            @pl.when(ahead & jnp.logical_not(source))
            def _():
                travel[s, jj] = partial[s, jj].astype(BF)

            @pl.when(ahead)
            def _():
                rs(way, s, jj).start()

    def block_of(k, way):
        s = d - k + 2 * k * way
        return s, (s >= 0) & (s < n) & ((k > 0) | (way == 0))

    def receive(k, way, s, j):
        @pl.when(k > 0)
        def _():
            pltpu.make_async_copy(gathered.at[s, j], gathered.at[s, j], ag_recv.at[s, j]).wait()

            @pl.when((way == 0) & has_right)
            def _():
                ag(0, s, j).start()

            @pl.when((way == 1) & has_left)
            def _():
                ag(1, s, j).start()

        arrived(s, j)

    wait_one = 1 if early else 0

    def step(g, _):
        k, j = g // chunks, lax.rem(g, chunks)

        def sides(act):
            @pl.when(g < n * chunks)
            def _():
                def side(way, _):
                    s, ok = block_of(k, way)
                    pl.when(ok)(lambda: act(way, s))
                    return 0

                lax.fori_loop(0, 2, side, 0)

        def flows():
            flow(1, g - wait_one - (n - 1 - d) * lag)
            flow(0, g - wait_one - d * lag)

        if turn is not None:
            turn(g)
        if early:
            sides(lambda way, s: receive(k, way, s, j))
            flows()

            def later(way, s):
                prepare(way, s, j)
                compute(way, s, j)

            sides(later)
        else:
            def work(way, s):
                prepare(way, s, j)
                receive(k, way, s, j)
                compute(way, s, j)

            sides(work)
            flows()
        if after is not None:
            after(g)
        return 0

    lax.fori_loop(0, n * chunks + (n - 1) * lag + wait_one, step, 0)

    def drain(i, _):
        s, j = i // chunks, lax.rem(i, chunks)

        @pl.when(has_right & (s <= d))
        def _():
            ag(0, s, j).wait_send()

        @pl.when(has_left & (s >= d))
        def _():
            ag(1, s, j).wait_send()

        @pl.when(s < d)
        def _():
            rs(1, s, j).wait_send()

        @pl.when(s > d)
        def _():
            rs(0, s, j).wait_send()

        return 0

    lax.fori_loop(0, n * chunks, drain, 0)


def own_sum(n, d, j, partial, travel, total):
    total[...] = partial[d, j].astype(F32)

    @pl.when(d > 0)
    def _():
        total[...] += travel[n, j].astype(F32)

    @pl.when(d < n - 1)
    def _():
        total[...] += travel[d, j].astype(F32)


def chain_sems(n, chunks):
    dma = pltpu.SemaphoreType.DMA
    return [dma((2, n, chunks)), dma((n, chunks)), dma((n, chunks)), dma((n + 1, chunks))]


def chunk_buffers(n, rows, c, kept):
    return [
        pltpu.VMEM((n, CHUNKS, rows, c), BF),
        pltpu.VMEM((n, CHUNKS, rows, c), kept),
        pltpu.VMEM((n + 1, CHUNKS, rows, c), BF),
    ]


def columns(i):
    return pl.ds(pl.multiple_of(i * TILE, TILE), TILE)


def drain_copies(n, copy):
    def one(i, _):
        copy(i // CHUNKS, lax.rem(i, CHUNKS)).wait()
        return 0

    lax.fori_loop(0, n * CHUNKS, one, 0)


def big_forward(x, w_up, w_down, residual, mask, share, n):
    t, c = x.shape
    h = w_up.shape[1]
    rows = t // CHUNKS
    cols = residual.shape[1]
    half = cols // 2
    pairs = rows // cols // 2

    def kernel(
        x_ref, wu, wd, res, mask_ref, share_ref, out, pooled, x_all, act_all, slope_all, wu_t, wd_t,
        gathered, partial, travel, act, slope, total, folded, turned, copied, stored, load_sem, *sems
    ):
        d = lax.axis_index("mp")
        load = pltpu.make_async_copy(x_ref, gathered.at[d], load_sem)

        def own_chunk(j):
            if isinstance(j, int):
                load.start()
                load.wait()

        def x_copy(s, j):
            return pltpu.make_async_copy(gathered.at[s, j], x_all.at[s, j], copied.at[s, j])

        def prepare(way, s, j):
            pass

        def arrived(s, j):
            x_copy(s, j).start()

        def compute(way, s, j):
            block = gathered.at[s, j]

            def up(i, _):
                pre = jnp.dot(block[...], wu[:, columns(i)], preferred_element_type=F32)
                value, rate = gelu_parts(pre)
                act[:, columns(i)] = value.astype(BF)
                slope[:, columns(i)] = rate.astype(BF)
                return 0

            lax.fori_loop(0, h // TILE, up, 0)
            keep_act = pltpu.make_async_copy(act, act_all.at[s, j], stored.at[0])
            keep_slope = pltpu.make_async_copy(slope, slope_all.at[s, j], stored.at[1])
            keep_act.start()
            keep_slope.start()

            def down(i, _):
                partial[s, j, :, columns(i)] = jnp.dot(
                    act[...], wd[:, columns(i)], preferred_element_type=F32
                )
                return 0

            lax.fori_loop(0, c // TILE, down, 0)
            keep_act.wait()
            keep_slope.wait()

        def finish(j):
            pl.when(j > 0)(lambda: put(j - 1).wait())
            own_sum(n, d, j, partial, travel, total)
            values = (res[pl.ds(j * 2 * pairs, 2 * pairs)].reshape(rows, c).astype(F32) + total[...]) * mask_ref[j]
            partial[d, j] = values
            put(j).start()
            both = values.reshape(pairs, 2, cols, c)
            summed = (both[:, 0] + both[:, 1]).reshape(pairs * cols, c)
            for b in range(c // LANES):
                lanes = slice(b * LANES, (b + 1) * LANES)
                folded[b] = summed[:, lanes]
                every = folded[b, pl.ds(0, pairs * half, 2), :] + folded[b, pl.ds(1, pairs * half, 2), :]
                pooled[j, :, lanes] = every * share_ref[j]

        def put(j):
            return pltpu.make_async_copy(partial.at[d, j], out.at[j], load_sem)

        def after(g):
            last = g - (n - 1) * (CHUNKS + 1)
            pl.when(last >= 0)(lambda: finish(last))
            for i, (w, target, size) in enumerate(((wu, wu_t, h), (wd, wd_t, c))):
                late = g - n * CHUNKS // 2

                @pl.when((late >= 0) & (late < size // LANES))
                def _():
                    some = pl.ds(pl.multiple_of(late * LANES, LANES), LANES)
                    turned[i, :, pl.ds(0, w.shape[0])] = w[:, some].T
                    copy = pltpu.make_async_copy(turned.at[i, :, pl.ds(0, w.shape[0])], target.at[some], stored.at[i])
                    copy.start()
                    copy.wait()

        chain_exchange(
            n, CHUNKS, 1, gathered, partial, travel, sems, own_chunk, prepare, arrived, compute, after=after
        )

        put(CHUNKS - 1).wait()
        drain_copies(n, x_copy)

    whole = pl.BlockSpec(memory_space=pl.ANY)
    local = pl.BlockSpec(memory_space=pltpu.VMEM)
    out, pooled, x_all, act_all, slope_all, wu_t, wd_t = pl.pallas_call(
        kernel,
        out_shape=(
            jax.ShapeDtypeStruct((CHUNKS, rows, c), F32),
            jax.ShapeDtypeStruct((CHUNKS, pairs * half, c), F32),
            jax.ShapeDtypeStruct((n, CHUNKS, rows, c), BF),
            jax.ShapeDtypeStruct((n, CHUNKS, rows, h), BF),
            jax.ShapeDtypeStruct((n, CHUNKS, rows, h), BF),
            jax.ShapeDtypeStruct((h, c), BF),
            jax.ShapeDtypeStruct((c, h), BF),
        ),
        in_specs=[whole, local, local, local, local, local],
        out_specs=(whole, local, whole, whole, whole, whole, whole),
        scratch_shapes=chunk_buffers(n, rows, c, F32)
        + [pltpu.VMEM((rows, h), BF)] * 2
        + [pltpu.VMEM((rows, c), F32), pltpu.VMEM((c // LANES, pairs * cols, LANES), F32), pltpu.VMEM((2, LANES, max(c, h)), BF)]
        + [pltpu.SemaphoreType.DMA((n, CHUNKS)), pltpu.SemaphoreType.DMA((2,)), pltpu.SemaphoreType.DMA]
        + chain_sems(n, CHUNKS),
        compiler_params=pltpu.CompilerParams(
            collective_id=0, has_side_effects=True, vmem_limit_bytes=60 * MIB
        ),
        cost_estimate=pl.CostEstimate(
            flops=4 * n * t * c * h, bytes_accessed=8 * n * t * c, transcendentals=n * t * h
        ),
    )(
        x.reshape(CHUNKS, rows, c), w_up, w_down, residual,
        mask.reshape(CHUNKS, rows, 1), share.reshape(CHUNKS, pairs * half, 1),
    )
    return (
        out.reshape(t, c),
        pooled.reshape(t // 4, c),
        x_all,
        act_all,
        slope_all,
        wu_t,
        wd_t,
    )


def big_backward(cot, d_pooled, share, mask, x_all, act_all, slope_all, up_t, down_t, grads, n, devices):
    _, cols, c = cot.shape
    t = cot.shape[0] * cols
    h = up_t.shape[0]
    rows = t // CHUNKS
    half = cols // 2
    pairs_here = rows // cols // 2
    piece = c // devices
    items = n * CHUNKS // 2
    pairs, g_rows, g_cols = grads.shape
    bits = range(1, devices.bit_length() - 1)
    split = g_rows // 2
    steps = len(bits)
    plans = [Halving(bits, [last] * steps, (pairs, split, g_cols), min(g_cols, 1024)) for last in (True, False)]
    extras = [b for plan in plans for b in plan.buffers()[:-1]]
    each = 2 * steps - 1

    def kernel(
        cot_ref, pool_ref, share_ref, mask_ref, x_hbm, act_hbm, slopes, wu, wd, g_first, g_second,
        out, d_own, g_up_out, g_down_out, out_up, out_down, got_up, got_down, h_all, *rest
    ):
        sums, extra, rest = rest[0], rest[1 : 1 + 2 * each], rest[1 + 2 * each :]
        gathered, partial, travel, slope, grad, left, right, middle, g_up, g_down, total, spread_rows, addend = rest[:13]
        core_send, core_recv, stored, add_sem, send0, recv0, send1, recv1 = rest[13:21]
        sems = rest[21:]
        d = lax.axis_index("mp")
        plans[0].bind(g_first.at[:, :, pl.ds(0, split)], extra[:each] + (sums.at[0],), send0, recv0)
        plans[1].bind(g_second.at[:, :, pl.ds(split, split)], extra[each:] + (sums.at[1],), send1, recv1)

        def begin():
            for plan in plans:
                plan.start(0)

        def pass_on(p, plan):
            plan.finish(p)
            if p + 1 < steps:
                plan.start(p + 1)

        first_due = 2 * CHUNKS + 4
        ticks = {}
        if steps == 2:
            for p, start in ((0, first_due), (1, n * CHUNKS + n - 2)):
                tiles = [
                    (plan, k, q)
                    for plan in plans
                    for k in range(plan.got[p].shape[0])
                    for q in range(g_cols // plan.block)
                ]
                for m in range(0, len(tiles), 4):
                    ticks[start + m // 4] = (p, m == 0, m + 4 >= len(tiles), tiles[m : m + 4])

        def tile_copy(which, p, i, plan, k, q):
            lanes = pl.ds(q * plan.block, plan.block)
            if which == 0:
                source, target = plan.part(p, True).at[k, :, lanes], addend.at[0, i]
            elif which == 1:
                source, target = plan.got[p].at[k, :, lanes], addend.at[1, i]
            else:
                ways = plan.split(plan.got[p].shape[0], p + 1)
                source, target = addend.at[0, i], plan.now[p + 1].at[k // ways[1], k % ways[1], :, lanes]
            return pltpu.make_async_copy(source, target, add_sem.at[which, i])

        def tick_begin(p, fresh, final, tiles):
            if fresh:
                for plan in plans:
                    plan.copy(p).wait()
            for i, tile in enumerate(tiles):
                for which in range(2):
                    tile_copy(which, p, i, *tile).start()

        def tick_add(p, fresh, final, tiles):
            for i, tile in enumerate(tiles):
                for which in range(2):
                    tile_copy(which, p, i, *tile).wait()
                addend[0, i] = (addend[0, i].astype(F32) + addend[1, i].astype(F32)).astype(BF)
                tile_copy(2, p, i, *tile).start()
            for i, tile in enumerate(tiles):
                tile_copy(2, p, i, *tile).wait()
            if final and p + 1 < steps:
                for plan in plans:
                    plan.start(p + 1)

        all_steps = n * CHUNKS + n
        due = [all_steps * 9 * (2**steps - 2 ** (steps - 1 - p)) // (10 * (2**steps - 1)) // 2 * 2 for p in range(steps)]

        def turn(g):
            if ticks:
                for at, tick in ticks.items():
                    pl.when(g == at)(lambda tick=tick: tick_begin(*tick))
            else:
                for p in range(steps - 1):
                    for i, plan in enumerate(plans):
                        pl.when(g == due[p] + 2 * i)(lambda p=p, plan=plan: pass_on(p, plan))

            q, due_now = item_of(g)

            @pl.when(due_now)
            def _():
                for copy in item_copies(q):
                    copy.start()

        def own_chunk(j):
            part = pool_ref[j] * share_ref[j]
            here = cot_ref.at[pl.ds(j * 2 * pairs_here, 2 * pairs_here)]
            for b in range(c // LANES):
                lanes = slice(b * LANES, (b + 1) * LANES)
                spread_rows[b, pl.ds(0, pairs_here * half, 2), :] = part[:, lanes]
                spread_rows[b, pl.ds(1, pairs_here * half, 2), :] = part[:, lanes]
                block = jnp.broadcast_to(
                    spread_rows[b].reshape(pairs_here, 1, cols, LANES), (pairs_here, 2, cols, LANES)
                ).reshape(rows, LANES)
                cell = here[:, :, lanes].reshape(rows, LANES).astype(F32)
                gathered[d, j, :, lanes] = ((cell + block) * mask_ref[j]).astype(BF)

        def slope_copy(s, j):
            return pltpu.make_async_copy(slopes.at[s, j], slope, stored.at[0])

        def prepare(way, s, j):
            slope_copy(s, j).start()

        def arrived(s, j):
            pass

        def compute(way, s, j):
            block = gathered.at[s, j]
            slope_copy(s, j).wait()

            def up(i, _):
                back = nn(block[...], wd[:, columns(i)])
                grad[:, columns(i)] = (back * slope[:, columns(i)].astype(F32)).astype(BF)
                return 0

            lax.fori_loop(0, h // TILE, up, 0)
            half_pair = pl.ds(pl.multiple_of(lax.rem(j, 2) * rows, rows), rows)
            keep = pltpu.make_async_copy(grad, h_all.at[s, j // 2, half_pair], stored.at[1])
            keep.start()

            def down(i, _):
                partial[s, j, :, columns(i)] = nn(grad[...], wu[:, columns(i)]).astype(BF)
                return 0

            lax.fori_loop(0, c // TILE, down, 0)
            keep.wait()

        def item_place(q):
            s, jj, base = d, q, CHUNKS // 2
            for k in range(1, n):
                to_left, to_right = d - k >= 0, d + k < n
                two = to_left & to_right
                r = q - base
                here = (r >= 0) & (to_left | to_right)
                s = jnp.where(here, jnp.where(to_left & (jnp.logical_not(two) | (lax.rem(r, 2) == 0)), d - k, d + k), s)
                jj = jnp.where(here, jnp.where(two, r // 2, r), jj)
                base = base + (CHUNKS // 2) * (to_left.astype(jnp.int32) + to_right.astype(jnp.int32))
            return s, jj

        def item_copies(q):
            s, jj = item_place(q)
            return (
                pltpu.make_async_copy(x_hbm.at[s, jj], left, stored.at[2]),
                pltpu.make_async_copy(act_hbm.at[s, jj], right, stored.at[3]),
                pltpu.make_async_copy(h_all.at[s, jj], middle, stored.at[4]),
            )

        between = (d > 0) & (d < n - 1)
        middle_steps = [n * CHUNKS - items + i for i in range(items)]
        if n == 4 and CHUNKS == 6:
            middle_steps = [2, 4, 12, 13, 14, 15, 17, 19, 20, 21, 22, 23]

        def item_of(g):
            q = jnp.where(between, -1, (g - 2) // 2)
            for i, at in enumerate(middle_steps):
                q = jnp.where(between & (g == at), i, q)
            return q, (q >= 0) & (q < items) & (g >= 2) & (between | (lax.rem(g, 2) == 0))

        def after(g):
            for at, tick in ticks.items():
                pl.when(g == at)(lambda tick=tick: tick_add(*tick))
            last = g - 1 - (n - 1) * (CHUNKS + 1)
            pl.when(last >= 0)(lambda: finish(last))
            q, due_now = item_of(g)

            @pl.when(due_now)
            def _():
                s, jj = item_place(q)
                for copy in item_copies(q):
                    copy.wait()

                def tile(i, _):
                    a = columns(i)
                    g_up[a] += tn(left[:, a], middle[...])
                    db = gathered[s, pl.ds(2 * jj, 2), :, a].reshape(2 * rows, TILE)
                    g_down[a] += tn(db, right[...])
                    return 0

                lax.fori_loop(0, c // TILE, tile, 0)

            @pl.when(g == 2 * items + 1)
            def _():
                give(g_up, left, out_up, stored.at[2])
                swaps[0].start()

            @pl.when(g == 2 * items + 2)
            def _():
                give(g_down, right, out_down, stored.at[3])
                swaps[1].start()

            @pl.when(g == 2 * items + 3)
            def _():
                keep_sums(0)

        core = dp_bit(0)

        def result(j):
            return pltpu.make_async_copy(total, out.at[j], stored.at[5])

        def finish(j):
            pl.when(j > 0)(lambda: result(j - 1).wait())
            own_sum(n, d, j, partial, travel, total)
            result(j).start()

        def rows_at(i):
            return pl.ds(pl.multiple_of(i * piece, piece), piece)

        def give(source, stage, target, sem):
            def one(i, _):
                stage[pl.ds(0, piece)] = source[rows_at(2 * i + 1 - core)].astype(BF)
                copy = pltpu.make_async_copy(stage.at[pl.ds(0, piece)], target.at[i], sem)
                copy.start()
                copy.wait()
                return 0

            lax.fori_loop(0, devices // 2, one, 0)

        def keep_sums(which):
            swaps[which].wait()
            sets = (((g_up, left, got_up, g_up_out, 2), (g_down, right, got_down, g_down_out, 3))[which],)

            def loads(i):
                return [
                    pltpu.make_async_copy(got.at[i], stage.at[pl.ds(0, piece)], stored.at[sem])
                    for _, stage, got, _, sem in sets
                ]

            def one(i, _):
                for load in loads(i):
                    load.start()
                saves = []
                for load, (source, stage, _, target, sem) in zip(loads(i), sets):
                    load.wait()
                    here = stage.at[pl.ds(0, piece)]
                    here[...] = (source[rows_at(2 * i + core)] + here[...].astype(F32)).astype(BF)
                    saves.append(pltpu.make_async_copy(here, target.at[i], stored.at[sem]))
                    saves[-1].start()
                for save in saves:
                    save.wait()
                return 0

            lax.fori_loop(0, devices // 2, one, 0)

        swaps = [
            pltpu.make_async_remote_copy(
                src_ref=src, dst_ref=dst, send_sem=core_send.at[i], recv_sem=core_recv.at[i],
                device_id={"dp": dp_mate(0)}, device_id_type=MESH,
            )
            for i, (src, dst) in enumerate(((out_up, got_up), (out_down, got_down)))
        ]
        def clear(i, _):
            some = pl.ds(pl.multiple_of(i * TILE, TILE), TILE)
            g_up[some] = jnp.zeros((TILE, h), F32)
            g_down[some] = jnp.zeros((TILE, h), F32)
            return 0

        def begin_all():
            begin()
            lax.fori_loop(0, c // TILE, clear, 0)

        chain_exchange(
            n, CHUNKS, 1, gathered, partial, travel, sems, own_chunk, prepare, arrived, compute,
            [dp_mate(b) for b in range(steps + 1)], begin_all, turn, after, True,
        )
        keep = pltpu.make_async_copy(gathered.at[d], d_own, stored.at[0])
        keep.start()
        result(CHUNKS - 1).wait()
        keep.wait()
        if not ticks:
            for plan in plans:
                pass_on(steps - 1, plan)
        keep_sums(1)

    whole = pl.BlockSpec(memory_space=pl.ANY)
    local = pl.BlockSpec(memory_space=pltpu.VMEM)
    dma = pltpu.SemaphoreType.DMA
    out, d_own, g_up, g_down, _, _, _, _, _, sums, *_ = pl.pallas_call(
        kernel,
        out_shape=(
            jax.ShapeDtypeStruct((CHUNKS, rows, c), F32),
            jax.ShapeDtypeStruct((CHUNKS, rows, c), BF),
            *[jax.ShapeDtypeStruct((devices // 2, piece, h), BF)] * 6,
            jax.ShapeDtypeStruct((n, CHUNKS // 2, 2 * rows, h), BF),
            jax.ShapeDtypeStruct((2, 1, 1, split, g_cols), BF),
            *extras,
        ),
        in_specs=[local] * 4 + [whole] * 3 + [local] * 2 + [whole] * 2,
        out_specs=(whole,) * (10 + 2 * each),
        scratch_shapes=chunk_buffers(n, rows, c, BF)
        + [
            pltpu.VMEM((rows, h), BF), pltpu.VMEM((rows, h), BF),
            pltpu.VMEM((2 * rows, c), BF), pltpu.VMEM((2 * rows, h), BF), pltpu.VMEM((2 * rows, h), BF),
            pltpu.VMEM((c, h), F32), pltpu.VMEM((c, h), F32),
            pltpu.VMEM((rows, c), F32), pltpu.VMEM((c // LANES, pairs_here * cols, LANES), F32),
            pltpu.VMEM((2, 4, split, plans[0].block), BF),
            dma((2,)), dma((2,)), dma((6,)), dma((3, 4)),
        ]
        + plans[0].semaphores() + plans[1].semaphores()
        + chain_sems(n, CHUNKS),
        compiler_params=pltpu.CompilerParams(
            collective_id=1, has_side_effects=True, vmem_limit_bytes=62 * MIB
        ),
        cost_estimate=pl.CostEstimate(
            flops=8 * n * t * c * h, bytes_accessed=8 * n * t * c, transcendentals=0
        ),
    )(
        cot, d_pooled.reshape(CHUNKS, pairs_here * half, c), share.reshape(CHUNKS, pairs_here * half, 1),
        mask.reshape(CHUNKS, rows, 1), *(v.reshape(n, CHUNKS // 2, 2 * rows, -1) for v in (x_all, act_all)),
        slope_all, up_t, down_t,
        grads.reshape(pairs // 2, 2, g_rows, g_cols), grads.reshape(2, pairs // 2, g_rows, g_cols),
    )
    return (
        out.reshape(cot.shape), d_own.reshape(cot.shape), [g_up, g_down],
        sums.reshape(g_rows, g_cols),
    )


def frame(dst, src):
    rows, cols, _ = src.shape
    dst[:, :EDGE] = jnp.zeros((rows, EDGE, LANES), F32)
    dst[:, EDGE + cols:] = jnp.zeros((rows, EDGE, LANES), F32)
    dst[:, EDGE:EDGE + cols] = src[...].astype(F32)


def correlate(out, framed, taps, size, flip, group, first=0, last=None, every=1):
    rows, cols, _ = out.shape
    reach = size // 2
    def some(k, _):
        r = first + k * every
        acc = jnp.zeros((group, cols, LANES), F32)
        for a in range(size):
            for b in range(size):
                tap = (size - 1 - a) * size + size - 1 - b if flip else a * size + b
                acc = acc + framed[pl.ds(r * group + a, group), pl.ds(EDGE - reach + b, cols), :] * taps[tap]
        out[pl.ds(r * group, group)] = acc
        return 0
    lax.fori_loop(0, (rows // group if last is None else last) - first if every == 1 else 2, some, 0)


def conv_forward(x, w, size, n):
    rows, cols, c = x.shape
    reach = size // 2

    def kernel(x_ref, w_ref, out, bordered, framed, sent, got, own):
        d = lax.axis_index("mp")
        has_up, has_down = d > 0, d < n - 1
        barrier = pltpu.get_barrier_semaphore()

        @pl.when(has_up)
        def _():
            pl.semaphore_signal(barrier, inc=1, device_id={"mp": d - 1}, device_id_type=MESH)

        @pl.when(has_down)
        def _():
            pl.semaphore_signal(barrier, inc=1, device_id={"mp": d + 1}, device_id_type=MESH)

        keep = pltpu.make_async_copy(x_ref, bordered.at[pl.ds(reach, rows)], own)
        keep.start()
        pl.semaphore_wait(barrier, has_up.astype(jnp.int32) + has_down.astype(jnp.int32))
        up = pltpu.make_async_remote_copy(
            src_ref=x_ref.at[pl.ds(0, reach)], dst_ref=bordered.at[pl.ds(reach + rows, reach)],
            send_sem=sent.at[0], recv_sem=got.at[0], device_id={"mp": d - 1}, device_id_type=MESH,
        )
        down = pltpu.make_async_remote_copy(
            src_ref=x_ref.at[pl.ds(rows - reach, reach)], dst_ref=bordered.at[pl.ds(0, reach)],
            send_sem=sent.at[1], recv_sem=got.at[1], device_id={"mp": d + 1}, device_id_type=MESH,
        )
        nothing = jnp.zeros((reach, cols, c), BF)

        @pl.when(has_up)
        def _():
            up.start()

        @pl.when(has_down)
        def _():
            down.start()

        @pl.when(d == 0)
        def _():
            bordered[:reach] = nothing

        @pl.when(d == n - 1)
        def _():
            bordered[reach + rows :] = nothing

        groups = rows // reach

        def inner(i, _):
            lanes = pl.ds(pl.multiple_of(i * LANES, LANES), LANES)
            frame(framed.at[pl.ds(reach, rows)], x_ref.at[:, :, lanes])
            correlate(out.at[:, :, lanes], framed, w_ref.at[:, :, lanes], size, False, reach, 1, groups - 1)
            return 0

        lax.fori_loop(0, c // LANES, inner, 0)
        keep.wait()

        @pl.when(has_up)
        def _():
            down.wait_recv()

        @pl.when(has_down)
        def _():
            up.wait_recv()

        def block(i, _):
            lanes = pl.ds(pl.multiple_of(i * LANES, LANES), LANES)
            frame(framed, bordered.at[:, :, lanes])
            correlate(out.at[:, :, lanes], framed, w_ref.at[:, :, lanes], size, False, reach, 0, None, groups - 1)
            return 0

        lax.fori_loop(0, c // LANES, block, 0)

        @pl.when(has_up)
        def _():
            up.wait_send()

        @pl.when(has_down)
        def _():
            down.wait_send()

    local = pl.BlockSpec(memory_space=pltpu.VMEM)
    dma = pltpu.SemaphoreType.DMA
    return pl.pallas_call(
        kernel,
        out_shape=(
            jax.ShapeDtypeStruct((rows, cols, c), F32),
            jax.ShapeDtypeStruct((rows + 2 * reach, cols, c), BF),
        ),
        in_specs=[local, local],
        out_specs=(local, local),
        scratch_shapes=[pltpu.VMEM((rows + 2 * reach, cols + 2 * EDGE, LANES), F32), dma((2,)), dma((2,)), dma],
        compiler_params=pltpu.CompilerParams(
            collective_id=5, has_side_effects=True, vmem_limit_bytes=40 * MIB
        ),
    )(x, w)


def conv_backward(d_normed, conv_out, gain, mask, bordered, d_map, w, low_gains, size, grads, devices, n):
    rows, cols, c = conv_out.shape
    reach = size // 2
    high = rows + 2 * reach
    group = 4 if rows % 4 == 0 else 1
    bits = range(1, devices.bit_length() - 1)
    steps = len(bits)
    shape = grads[0].shape
    plans = [Halving(bits, [last] * steps, shape, shape[2]) for last in (True, False)]
    each = 2 * steps
    blocks = c // LANES
    taps = size * size
    count = taps + 1 + low_gains.shape[0]
    small = -(-count // devices)
    first_due = blocks + blocks // 3
    begins = {first_due + blocks // 2 * p // (steps - 1): p for p in range(steps - 1)}
    ends = {mark + 1: p for mark, p in begins.items()}
    rounds = {blocks + 10 * blocks // 12: 1}

    def kernel(
        dn, co, gain_ref, mask_ref, w_ref, low_ref, b_hbm, dm_hbm, g0, g1, out, g_all, *rest
    ):
        extra, rest = rest[: 2 * each], rest[2 * each :]
        around, x_around, d_here, dframed, xframed, g_own, here, level, addend, sent, got, own, add_sem = rest[:13]
        ar, halving_sems = rest[13:19], rest[19:]
        plans[0].bind(g0, extra[:each], halving_sems[0], halving_sems[1])
        plans[1].bind(g1, extra[each:], halving_sems[2], halving_sems[3])
        me, d = lax.axis_index("dp"), lax.axis_index("mp")
        has_up, has_down = d > 0, d < n - 1
        barrier = pltpu.get_barrier_semaphore()

        def greet(k, _):
            pl.semaphore_signal(
                barrier, inc=1, device_id={"dp": lax.rem(me + k, devices)}, device_id_type=MESH
            )
            return 0

        lax.fori_loop(1, devices, greet, 0)
        for k in range(1, n):
            pl.semaphore_signal(barrier, inc=1, device_id={"mp": lax.rem(d + k, n)}, device_id_type=MESH)
        load_x = pltpu.make_async_copy(b_hbm, x_around, own.at[0])
        load_d = pltpu.make_async_copy(dm_hbm, d_here, own.at[1])
        load_x.start()
        load_d.start()

        def halving_loads(p, i):
            plan, count = plans[i], plans[i].got[p].shape[0]
            some = pl.ds(0, count)
            return [
                pltpu.make_async_copy(plan.part(p, True), addend.at[0, i, some], add_sem.at[0, i]),
                pltpu.make_async_copy(plan.got[p], addend.at[1, i, some], add_sem.at[1, i]),
            ]

        def halving_save(p, i, k):
            plan = plans[i]
            ways = plan.split(plan.got[p].shape[0], p + 1)
            target = plan.now[p + 1].at[k // ways[1], k % ways[1]]
            return pltpu.make_async_copy(addend.at[0, i, k], target, add_sem.at[2 + i, k])

        def halving_begin(p):
            for i, plan in enumerate(plans):
                plan.copy(p).wait()
                for load in halving_loads(p, i):
                    load.start()

        def halving_end(p):
            for i, plan in enumerate(plans):
                for load in halving_loads(p, i):
                    load.wait()
                for k in range(plan.got[p].shape[0]):
                    addend[0, i, k] = (addend[0, i, k].astype(F32) + addend[1, i, k].astype(F32)).astype(BF)
                    halving_save(p, i, k).start()
            for i, plan in enumerate(plans):
                for k in range(plan.got[p].shape[0]):
                    halving_save(p, i, k).wait()
            if p + 1 < steps:
                for plan in plans:
                    plan.start(p + 1)

        def keep(row, lanes, value):
            g_own[row // small, row % small : row % small + 1, lanes] = value

        pl.semaphore_wait(barrier, devices + n - 2)
        for plan in plans:
            plan.start(0)
        g_own[...] = jnp.zeros(g_own.shape, F32)

        def norm(r, total):
            cells = mask_ref[r]
            back, part = normalise_back(co[r] * cells, gain_ref[...], dn[r])
            around[reach + r] = (back * cells).astype(BF)
            return total + part

        keep(taps, slice(None), lax.fori_loop(0, rows, norm, jnp.zeros((1, c), F32)))
        for i in range(low_gains.shape[0]):
            keep(taps + 1 + i, slice(None), low_ref[i : i + 1])
        up = pltpu.make_async_remote_copy(
            src_ref=around.at[pl.ds(reach, reach)], dst_ref=around.at[pl.ds(reach + rows, reach)],
            send_sem=sent.at[0], recv_sem=got.at[0], device_id={"mp": d - 1}, device_id_type=MESH,
        )
        down = pltpu.make_async_remote_copy(
            src_ref=around.at[pl.ds(rows, reach)], dst_ref=around.at[pl.ds(0, reach)],
            send_sem=sent.at[1], recv_sem=got.at[1], device_id={"mp": d + 1}, device_id_type=MESH,
        )
        nothing = jnp.zeros((reach, cols, c), BF)

        @pl.when(has_up)
        def _():
            up.start()

        @pl.when(has_down)
        def _():
            down.start()

        @pl.when(d == 0)
        def _():
            around[:reach] = nothing

        @pl.when(d == n - 1)
        def _():
            around[reach + rows :] = nothing

        load_x.wait()

        def lanes_of(i):
            return pl.ds(pl.multiple_of(i * LANES, LANES), LANES)

        def kernel_block(i, _):
            lanes = lanes_of(i)
            frame(dframed.at[pl.ds(reach, rows)], around.at[pl.ds(reach, rows), :, lanes])
            frame(xframed, x_around.at[:, :, lanes])
            for a in range(size):
                def some(r, accs):
                    dv = dframed[pl.ds(reach + r * group, group), EDGE : EDGE + cols]
                    new = []
                    for b in range(size):
                        prod = dv * xframed[pl.ds(r * group + a, group), pl.ds(EDGE - reach + b, cols), :]
                        new.append(accs[b] + jnp.sum(prod.reshape(-1, 8, LANES), axis=0))
                    return tuple(new)

                accs = lax.fori_loop(
                    0, rows // group, some, tuple(jnp.zeros((8, LANES), F32) for _ in range(size))
                )
                for b in range(size):
                    keep(a * size + b, lanes, jnp.sum(accs[b], axis=0, keepdims=True))
            return 0

        def input_block(i, _):
            lanes = lanes_of(i)
            frame(dframed, around.at[:, :, lanes])
            correlate(out.at[:, :, lanes], dframed, w_ref.at[:, :, lanes], size, True, group)
            for r in range(rows):
                out[r, :, lanes] = (out[r, :, lanes] + d_here[r, :, lanes].astype(F32)) * mask_ref[r]
            return 0

        def spread(k):
            peer = lax.rem(me + k, devices)
            return pltpu.make_async_remote_copy(
                src_ref=g_own.at[peer], dst_ref=here.at[me], send_sem=ar[0].at[k], recv_sem=ar[1].at[k],
                device_id={"dp": peer}, device_id_type=MESH,
            )

        def across(k):
            return pltpu.make_async_remote_copy(
                src_ref=level.at[d], dst_ref=level.at[d], send_sem=ar[2].at[k], recv_sem=ar[3].at[k],
                device_id={"mp": lax.rem(d + k, n)}, device_id_type=MESH,
            )

        def tell(k):
            return pltpu.make_async_remote_copy(
                src_ref=g_all.at[me], dst_ref=g_all.at[me], send_sem=ar[4].at[k], recv_sem=ar[5].at[k],
                device_id={"dp": lax.rem(me + k, devices)}, device_id_type=MESH,
            )

        def all_of(length, make, act):
            def one(k, _):
                act(make(k))
                return 0

            lax.fori_loop(1, length, one, 0)

        def sum_round(p):
            if p == 0:
                here[me] = g_own[me]
                all_of(devices, spread, lambda x: x.start())
            elif p == 1:
                all_of(devices, spread, lambda x: x.wait())
                level[d] = jnp.sum(here[...], axis=0)
                all_of(n, across, lambda x: x.start())
            elif p == 2:
                all_of(n, across, lambda x: x.wait())
                g_all[me] = jnp.sum(level[...], axis=0)
                all_of(devices, tell, lambda x: x.start())
            else:
                all_of(devices, tell, lambda x: x.wait())

        marks = sorted(set(begins) | set(ends) | set(rounds) | {blocks, 2 * blocks})
        at = 0
        for mark in marks:
            if at < blocks:
                lax.fori_loop(at, min(mark, blocks), kernel_block, 0)
            else:
                lax.fori_loop(at - blocks, mark - blocks, input_block, 0)
            at = mark
            if mark in ends:
                halving_end(ends[mark])
            if mark in begins:
                halving_begin(begins[mark])
            if mark == first_due:
                sum_round(0)
            if mark == blocks:
                load_d.wait()

                @pl.when(has_up)
                def _():
                    down.wait_recv()

                @pl.when(has_down)
                def _():
                    up.wait_recv()
            if mark in rounds:
                sum_round(rounds[mark])
        sum_round(2)
        halving_begin(steps - 1)
        halving_end(steps - 1)
        sum_round(3)

        @pl.when(has_up)
        def _():
            up.wait_send()

        @pl.when(has_down)
        def _():
            down.wait_send()

    whole = pl.BlockSpec(memory_space=pl.ANY)
    local = pl.BlockSpec(memory_space=pltpu.VMEM)
    vm, dma = pltpu.VMEM, pltpu.SemaphoreType.DMA
    d_in, g_all, *extra = pl.pallas_call(
        kernel,
        out_shape=(
            jax.ShapeDtypeStruct((rows, cols, c), F32),
            jax.ShapeDtypeStruct((devices, small, c), F32),
            *plans[0].buffers(),
            *plans[1].buffers(),
        ),
        in_specs=[local] * 6 + [whole] * 4,
        out_specs=(local,) * 2 + (whole,) * (2 * each),
        scratch_shapes=[
            vm((high, cols, c), BF), vm((high, cols, c), BF), vm((rows, cols, c), BF),
            vm((high, cols + 2 * EDGE, LANES), F32), vm((high, cols + 2 * EDGE, LANES), F32),
            vm((devices, small, c), F32), vm((devices, small, c), F32), vm((n, small, c), F32),
            vm((2, 2, shape[0] // 2) + shape[1:], BF),
            dma((2,)), dma((2,)), dma((2,)), dma((4, max(2, shape[0] // 2))),
            dma((devices,)), dma((devices,)), dma((n,)), dma((n,)), dma((devices,)), dma((devices,)),
        ]
        + plans[0].semaphores() + plans[1].semaphores(),
        compiler_params=pltpu.CompilerParams(
            collective_id=3, has_side_effects=True, vmem_limit_bytes=50 * MIB
        ),
        cost_estimate=pl.CostEstimate(flops=6 * 10**10, bytes_accessed=10**8, transcendentals=0),
    )(
        d_normed, conv_out, gain, mask, w, low_gains, bordered, d_map,
        grads[0].reshape((shape[0] // 2, 2) + shape[1:]), grads[1].reshape((2, shape[0] // 2) + shape[1:]),
    )
    sums = g_all.reshape(devices * small, c)[:count]
    return d_in, sums, [extra[each - 1].reshape(shape[1:]), extra[2 * each - 1].reshape(shape[1:])]


GATE, OUT, HIGH_A, HIGH_B, QUERY, KEY, VALUE, PROJ = range(8)
L_LOW, L_DF, L_POOL_A, L_POOL_B, L_FIRST, L_DA, L_SECOND, L_COT = range(8)
R_DGATE, R_MERGE, R_DHIGH, R_DQ, R_DK, R_DV, R_ATT, R_DUP, R_ACT = range(9)


def nn(a, b):
    return jnp.dot(a, b, preferred_element_type=F32)


def nt(a, b):
    return lax.dot_general(a, b, (((1,), (1,)), ((), ())), preferred_element_type=F32)


def tn(a, b):
    return lax.dot_general(a, b, (((0,), (0,)), ((), ())), preferred_element_type=F32)


def normalise(x, gain):
    centred = x - jnp.mean(x, -1, keepdims=True)
    rate = lax.rsqrt(jnp.mean(centred * centred, -1, keepdims=True) + 1e-06)
    return centred * rate * gain


def normalise_back(x, gain, d):
    centred = x - jnp.mean(x, -1, keepdims=True)
    rate = lax.rsqrt(jnp.mean(centred * centred, -1, keepdims=True) + 1e-06)
    hat = centred * rate
    dg = d * gain
    back = rate * (dg - jnp.mean(dg, -1, keepdims=True) - hat * jnp.mean(dg * hat, -1, keepdims=True))
    return back, jnp.sum(d * hat, axis=0, keepdims=True)


def low_stage(low, pooled, cot, gain1, gain2, packed, n, devices, cid):
    t, dim = low.shape
    every = n * t
    width = dim // n
    heads = width // HEAD
    groups = width // LANES
    pairs = devices // 2
    rows = dim // devices
    half = dim // 2
    ff = 4 * dim
    natural = rows % LANES == 0
    high_rows = pooled.shape[1] // devices

    def place_of(k):
        return (k % 2) * half + k // 2 * rows

    def in_order(ref):
        if not natural:
            return ref[...]
        order = sorted(range(devices), key=place_of)
        return jnp.concatenate([ref[:, k * rows : (k + 1) * rows] for k in order], axis=1)

    scale = HEAD ** (-0.5)

    def kernel(
        low_ref, pooled_ref, cot_ref, gain1_ref, gain2_ref, w_hbm,
        low_out, d_low, d_pooled, g_ln1, g_ln2, grads,
        wv, lhs, lhs2, rhs, gate, high, merged, resid, d_res, slope, mixed, heads_in, att_all, d_att, d_mixed,
        d_heads, probs, d_scores, stage, left, w_sem, q_send, q_got, a_send, a_got, b_send, b_got, c_send, c_got, own_sem,
        l_send, l_got, r_send, r_got, stage_sem,
    ):
        d = lax.axis_index("mp")
        dp = lax.axis_index("dp")
        core = lax.rem(dp, 2)
        mate = dp + 1 - 2 * core
        barrier = pltpu.get_barrier_semaphore()
        for k in range(1, n):
            pl.semaphore_signal(barrier, inc=1, device_id={"mp": lax.rem(d + k, n)}, device_id_type=MESH)
        pl.semaphore_signal(barrier, inc=1, device_id={"dp": mate}, device_id_type=MESH)

        def w_copy(w, k):
            c, z = k // n, lax.rem(k, n)
            wide, base, at = w_place(w)
            src = w_hbm.at[:, c, z, :, pl.ds(base, wide)]
            dst = wv.at[c, :, :, pl.ds(pl.multiple_of(at + z * wide, wide), wide)]
            return pltpu.make_async_copy(src, dst, w_sem.at[w, k])

        def w_place(w):
            if w < 8:
                return width, w * width, w * dim
            return ff // n, 8 * width + (w - 8) * ff // n, 8 * dim + (w - 8) * ff

        def w_each(w, act):
            def one(k, _):
                act(w_copy(w, k))
                return 0

            lax.fori_loop(0, 2 * n, one, 0)

        for w in (GATE, HIGH_A, HIGH_B, OUT, QUERY, KEY, VALUE, PROJ):
            w_each(w, lambda copy: copy.start())

        def w_wait(*which):
            for w in which:
                w_each(w, lambda copy: copy.wait())

        def w_cols(at, size):
            return wv[:, :, :, pl.ds(at, size)].reshape(dim, size)

        def forward(x, first, count, put):
            def one(i, _):
                put(pl.multiple_of(i * LOW_TILE, LOW_TILE), nn(x, w_cols(pl.multiple_of(first * dim + i * LOW_TILE, LOW_TILE), LOW_TILE)))
                return 0
            lax.fori_loop(0, count * dim // LOW_TILE, one, 0)

        def backward(get, first, count, dst, fresh):
            def one(i, _):
                for c in range(2):
                    part = wv[c, :, :, pl.ds(pl.multiple_of((first + i) * dim, dim), dim)].reshape(half, dim)
                    y = nt(get(pl.multiple_of(i * dim, dim)), part)
                    cols = slice(c * half, (c + 1) * half)
                    if fresh and count == 1:
                        dst[:, cols] = y
                    else:
                        dst[:, cols] += y
                return 0
            if fresh and count > 1:
                dst[...] = jnp.zeros(dst.shape, F32)
            if count == 1:
                one(0, 0)
            else:
                lax.fori_loop(0, count, one, 0)

        def r_cols(block, count=1):
            return pl.ds(block * dim, count * dim)

        def r_at(block):
            return block * dim if block <= R_DUP else block * dim + 3 * dim

        def r_copy(block):
            cols = pl.ds(r_at(block), dim if block < R_DUP else ff)
            return pltpu.make_async_remote_copy(
                src_ref=rhs.at[0, :, cols], dst_ref=rhs.at[1, :, cols], send_sem=r_send.at[block],
                recv_sem=r_got.at[block], device_id={"dp": mate}, device_id_type=MESH)

        def l_copy(i):
            return pltpu.make_async_remote_copy(
                src_ref=lhs.at[i, :, pl.ds(pl.multiple_of((1 - core) * half, half), half)], dst_ref=lhs2.at[i],
                send_sem=l_send.at[i], recv_sem=l_got.at[i], device_id={"dp": mate}, device_id_type=MESH)

        stored = []
        turned = [None]

        def put_natural(dst, value):
            if natural:
                for k in range(devices):
                    dst[:, k * rows : (k + 1) * rows] = value[:, place_of(k) : place_of(k) + rows]
            else:
                dst[...] = value

        def grad(i, block, at, count, shared=False):
            if not shared:
                r_copy(block).wait_recv()
            if turned[0] != i:
                left[0] = lhs[i, :, pl.ds(pl.multiple_of(core * half, half), half)].T
                left[1] = lhs2[i].T
                turned[0] = i

            wide, base, first = w_place(at if at < 8 else 8 + (at - 8) * dim // ff)
            piece = min(GRAD_TILE, wide)

            def out_copies(slot, k):
                out = []
                for q in range(GRAD_TILE // piece):
                    z, col = divmod(at * dim - first + k * GRAD_TILE + q * piece, wide)
                    out.append(
                        pltpu.make_async_copy(
                            stage.at[slot, :, :, pl.ds(q * piece, piece)],
                            grads.at[:, pl.ds(z * rows, rows), pl.ds(base + col, piece)],
                            stage_sem.at[slot, q],
                        )
                    )
                return out

            for k in range(count * dim // GRAD_TILE):
                slot = len(stored) % 2
                if len(stored) >= 2:
                    wait(stored[-2])
                cols = pl.ds(r_at(block) + k * GRAD_TILE, GRAD_TILE)
                y = nn(left[0], rhs[0, :, cols]) + nn(left[1], rhs[1, :, cols])
                stage[slot] = y.astype(BF).reshape(pairs, rows, GRAD_TILE)
                stored.append(out_copies(slot, k))
                start(stored[-1])

        def to_heads(k, src, dst, send, got):
            out = []
            for step in range(1, n):
                peer = lax.rem(d + step, n)
                out.append(pltpu.make_async_remote_copy(
                    src_ref=src.at[:, pl.ds(pl.multiple_of(peer * width, width), width)],
                    dst_ref=dst.at[pl.ds(pl.multiple_of(d * t, t), t)],
                    send_sem=send.at[k, step], recv_sem=got.at[k, step], device_id={"mp": peer}, device_id_type=MESH))
            out.append(pltpu.make_async_copy(
                src.at[:, pl.ds(pl.multiple_of(d * width, width), width)], dst.at[pl.ds(pl.multiple_of(d * t, t), t)], own_sem.at[k]))
            return out

        def to_tokens(k, src, dst, send, got, group):
            out = []
            slot = k * groups + group
            lanes = pl.ds(group * LANES, LANES)
            there = pl.ds(pl.multiple_of(d * width + group * LANES, LANES), LANES)
            for step in range(1, n):
                peer = lax.rem(d + step, n)
                out.append(pltpu.make_async_remote_copy(
                    src_ref=src.at[pl.ds(pl.multiple_of(peer * t, t), t), lanes], dst_ref=dst.at[:, there],
                    send_sem=send.at[slot, step], recv_sem=got.at[slot, step], device_id={"mp": peer}, device_id_type=MESH))
            out.append(pltpu.make_async_copy(
                src.at[pl.ds(pl.multiple_of(d * t, t), t), lanes], dst.at[:, there], own_sem.at[slot]))
            return out

        def start(copies):
            for c in copies:
                c.start()

        def wait(copies):
            for c in copies:
                c.wait()

        gain1_here, gain2_here = in_order(gain1_ref), in_order(gain2_ref)
        if natural:
            for i, ref in ((L_LOW, low_ref), (L_COT, cot_ref)):
                for k in range(devices):
                    lhs[i, :, place_of(k) : place_of(k) + rows] = ref[:, k * rows : (k + 1) * rows]
            for k in range(devices):
                own = slice(place_of(k), place_of(k) + rows)
                lhs[L_POOL_A, :, own] = pooled_ref[:, k * high_rows : k * high_rows + rows].astype(BF)
                more = pooled_ref[:, k * high_rows + rows : (k + 1) * high_rows].astype(BF)
                lhs[L_POOL_B, :, own] = jnp.concatenate([more, jnp.zeros((t, 2 * rows - high_rows), BF)], axis=1)
        else:
            lhs[L_LOW] = low_ref[...]
            lhs[L_COT] = cot_ref[...]
            lhs[L_POOL_A] = pooled_ref[:, :dim].astype(BF)
            lhs[L_POOL_B] = pooled_ref[:, dim:].astype(BF)
        acc = d_low
        w_wait(GATE)

        def put_gate(at, y):
            gate[:, pl.ds(at, LOW_TILE)] = 1.0 / (1.0 + jnp.exp(-y))
        forward(lhs[L_LOW], GATE, 1, put_gate)
        w_wait(HIGH_A, HIGH_B, OUT)
        for w in (8, 9):
            w_each(w, lambda copy: copy.start())

        def put_high(at, y):
            high[:, pl.ds(at, LOW_TILE)] = y
        forward(lhs[L_POOL_A], HIGH_A, 1, put_high)

        def put_merging(at, y):
            cols = pl.ds(at, LOW_TILE)
            total = high[:, cols] + y
            high[:, cols] = total
            rhs[0, :, pl.ds(R_MERGE * dim + at, LOW_TILE)] = (total * gate[:, cols]).astype(BF)
        forward(lhs[L_POOL_B], HIGH_B, 1, put_merging)
        backward(lambda at: rhs[0, :, r_cols(R_MERGE)], OUT, 1, merged, True)
        merged[...] += lhs[L_LOW].astype(F32)
        lhs[L_FIRST] = normalise(merged[...], gain1_here).astype(BF)

        w_wait(QUERY, KEY, VALUE, PROJ)
        pl.semaphore_wait(barrier, n)
        for i in (L_LOW, L_POOL_A, L_POOL_B, L_COT, L_FIRST):
            l_copy(i).start()
        r_copy(R_MERGE).start()
        out_q = []
        for k in range(3):
            def put_mixed(at, y):
                mixed[k, :, pl.ds(at, LOW_TILE)] = y.astype(BF)
            forward(lhs[L_FIRST], QUERY + k, 1, put_mixed)
            copies = to_heads(k, mixed.at[k], heads_in.at[k], q_send, q_got)
            start(copies)
            out_q.append(copies)
        wait(out_q[0] + out_q[1])

        for h in range(heads):
            lanes = slice(h * HEAD, (h + 1) * HEAD)

            def rows_of(b, _):
                some = pl.ds(pl.multiple_of(b * t, t), t)
                s = nt(heads_in[0, some, lanes], heads_in[1, :, lanes]) * scale
                e = jnp.exp(s - jnp.max(s, -1, keepdims=True))
                p = (e * (1.0 / jnp.sum(e, -1, keepdims=True))).astype(BF)
                probs[h, some] = p
                return 0
            lax.fori_loop(0, n, rows_of, 0)
        wait(out_q[2])
        out_a = []
        for h in range(heads):
            lanes = slice(h * HEAD, (h + 1) * HEAD)

            def attend(b, _):
                some = pl.ds(pl.multiple_of(b * t, t), t)
                att_all[some, lanes] = nn(probs[h, some], heads_in[2, :, lanes]).astype(BF)
                return 0
            lax.fori_loop(0, n, attend, 0)
            if (h + 1) * HEAD % LANES == 0:
                copies = to_tokens(0, att_all, rhs.at[0, :, r_cols(R_ATT)], a_send, a_got, h * HEAD // LANES)
                start(copies)
                out_a += copies
        wait(out_a)
        r_copy(R_ATT).start()
        backward(lambda at: rhs[0, :, r_cols(R_ATT)], PROJ, 1, resid, True)
        resid[...] += merged[...]
        lhs[L_SECOND] = normalise(resid[...], gain2_here).astype(BF)
        l_copy(L_SECOND).start()

        w_wait(8)

        def put_up(at, y):
            value, rate = gelu_parts(y)
            rhs[0, :, pl.ds(r_at(R_ACT) + at, LOW_TILE)] = value.astype(BF)
            slope[:, pl.ds(at, LOW_TILE)] = rate.astype(BF)
        forward(lhs[L_SECOND], 8, 4, put_up)
        r_copy(R_ACT).start()
        w_wait(9)
        backward(lambda at: rhs[0, :, pl.ds(r_at(R_ACT) + at, dim)], 12, 4, acc, True)
        put_natural(low_out, resid[...] + acc[...])

        def put_d_up(at, y):
            rhs[0, :, pl.ds(r_at(R_DUP) + at, LOW_TILE)] = (y * slope[:, pl.ds(at, LOW_TILE)].astype(F32)).astype(BF)
        forward(lhs[L_COT], 12, 4, put_d_up)
        r_copy(R_DUP).start()
        backward(lambda at: rhs[0, :, pl.ds(r_at(R_DUP) + at, dim)], 8, 4, acc, True)
        back, g = normalise_back(resid[...], gain2_here, acc[...])
        put_natural(g_ln2, g)
        d_res[...] = lhs[L_COT].astype(F32) + back
        lhs[L_DA] = d_res[...].astype(BF)
        l_copy(L_DA).start()

        def put_d_att(at, y):
            mixed[0, :, pl.ds(at, LOW_TILE)] = y.astype(BF)
        forward(lhs[L_DA], PROJ, 1, put_d_att)
        out_b = to_heads(0, mixed.at[0], d_att, b_send, b_got)
        start(out_b)
        l_copy(L_COT).wait_recv()
        grad(L_COT, R_ACT, 12, 4)
        wait(out_b)
        out_c = []

        def send_back(k, h):
            if (h + 1) * HEAD % LANES == 0:
                copies = to_tokens(k, d_heads.at[k], rhs.at[0, :, r_cols(R_DQ + k)], c_send, c_got, h * HEAD // LANES)
                start(copies)
                out_c.extend(copies)

        for h in range(heads):
            lanes = slice(h * HEAD, (h + 1) * HEAD)
            d_heads[2, :, lanes] = tn(probs[h], d_att[:, lanes]).astype(BF)
            send_back(2, h)
        for h in range(heads):
            lanes = slice(h * HEAD, (h + 1) * HEAD)

            def rows_of(b, _):
                some = pl.ds(pl.multiple_of(b * t, t), t)
                p = probs[h, some].astype(F32)
                dp_ = nt(d_att[some, lanes], heads_in[2, :, lanes])
                ds = (p * (dp_ - jnp.sum(dp_ * p, -1, keepdims=True)) * scale).astype(BF)
                d_scores[some] = ds
                d_heads[0, some, lanes] = nn(ds, heads_in[1, :, lanes]).astype(BF)
                return 0
            lax.fori_loop(0, n, rows_of, 0)
            d_heads[1, :, lanes] = tn(d_scores[...], heads_in[0, :, lanes]).astype(BF)
            send_back(0, h)
            send_back(1, h)
        l_copy(L_SECOND).wait_recv()
        grad(L_SECOND, R_DUP, 8, 4)
        l_copy(L_DA).wait_recv()
        grad(L_DA, R_ATT, PROJ, 1)
        wait(out_c)
        for k in range(3):
            r_copy(R_DQ + k).start()
        backward(lambda at: rhs[0, :, pl.ds(R_DQ * dim + at, dim)], QUERY, 3, acc, True)
        back, g = normalise_back(merged[...], gain1_here, acc[...])
        put_natural(g_ln1, g)
        d_res[...] += back
        lhs[L_DF] = d_res[...].astype(BF)
        l_copy(L_DF).start()

        def put_d_gate(at, y):
            cols = pl.ds(at, LOW_TILE)
            gv = gate[:, cols]
            part = y * gv
            rhs[0, :, pl.ds(R_DHIGH * dim + at, LOW_TILE)] = part.astype(BF)
            rhs[0, :, pl.ds(R_DGATE * dim + at, LOW_TILE)] = (part * high[:, cols] * (1.0 - gv)).astype(BF)
        forward(lhs[L_DF], OUT, 1, put_d_gate)
        r_copy(R_DHIGH).start()
        r_copy(R_DGATE).start()
        backward(lambda at: rhs[0, :, r_cols(R_DHIGH)], HIGH_A, 1, gate, True)
        backward(lambda at: rhs[0, :, r_cols(R_DHIGH)], HIGH_B, 1, high, True)
        if natural:
            for k in range(devices):
                at = place_of(k)
                d_pooled[:, k * high_rows : k * high_rows + rows] = gate[:, at : at + rows]
                d_pooled[:, k * high_rows + rows : (k + 1) * high_rows] = high[:, at : at + high_rows - rows]
        else:
            d_pooled[:, :dim] = gate[...]
            d_pooled[:, dim:] = high[...]
        backward(lambda at: rhs[0, :, r_cols(R_DGATE)], GATE, 1, acc, True)
        put_natural(d_low, d_res[...] + acc[...])
        l_copy(L_FIRST).wait_recv()
        for k in range(3):
            grad(L_FIRST, R_DQ + k, QUERY + k, 1)
        l_copy(L_DF).wait_recv()
        grad(L_DF, R_MERGE, OUT, 1)
        l_copy(L_POOL_A).wait_recv()
        grad(L_POOL_A, R_DHIGH, HIGH_A, 1)
        l_copy(L_POOL_B).wait_recv()
        grad(L_POOL_B, R_DHIGH, HIGH_B, 1, shared=True)
        l_copy(L_LOW).wait_recv()
        grad(L_LOW, R_DGATE, GATE, 1)
        wait(stored[-2])
        wait(stored[-1])
        for i in range(8):
            l_copy(i).wait_send()
        for b in range(9):
            r_copy(b).wait_send()

    whole = pl.BlockSpec(memory_space=pl.ANY)
    local = pl.BlockSpec(memory_space=pltpu.VMEM)
    vm, dma = pltpu.VMEM, pltpu.SemaphoreType.DMA
    tok = jax.ShapeDtypeStruct((t, dim), F32)
    one = jax.ShapeDtypeStruct((1, dim), F32)
    return pl.pallas_call(
        kernel,
        out_shape=(tok, tok, jax.ShapeDtypeStruct(pooled.shape, F32), one, one, jax.ShapeDtypeStruct((pairs, n * rows, 16 * width), BF)),
        in_specs=[local] * 5 + [whole],
        out_specs=(local,) * 5 + (whole,),
        scratch_shapes=[
            vm((2, pairs, rows, 16 * dim), BF), vm((8, t, dim), BF), vm((8, t, half), BF), vm((2, t, 15 * dim), BF),
            vm((t, dim), F32), vm((t, dim), F32), vm((t, dim), F32), vm((t, dim), F32), vm((t, dim), F32),
            vm((t, ff), BF), vm((3, t, dim), BF), vm((3, every, width), BF), vm((every, width), BF), vm((every, width), BF),
            vm((1, 8, 128), BF), vm((3, every, width), BF), vm((heads, every, every), BF), vm((every, every), BF),
            vm((2, pairs, rows, GRAD_TILE), BF), vm((2, half, t), BF),
            dma((10, 2 * n)), dma((3, n)), dma((3, n)), dma((groups, n)), dma((groups, n)), dma((1, n)), dma((1, n)),
            dma((3 * groups, n)), dma((3 * groups, n)), dma((3 * groups,)), dma((8,)), dma((8,)), dma((9,)), dma((9,)), dma((2, 2)),
        ],
        compiler_params=pltpu.CompilerParams(collective_id=cid, has_side_effects=True, vmem_limit_bytes=62 * MIB),
        cost_estimate=pl.CostEstimate(flops=14 * 10**9, bytes_accessed=70 * 10**6, transcendentals=10**7),
    )(low, pooled, cot, gain1, gain2, packed.reshape(pairs, 2, n, rows, 16 * width))
def low_outputs(own, widths, high_rows):
    share = own.shape[0]
    width, wide = widths[0], widths[-1]

    def kernel(x, gate, high, out, qkv, proj, up, down):
        def part(i, size=width):
            at = sum(widths[:i])
            return x[:, at : at + size].astype(F32)

        gate[...] = part(0)
        out[...] = part(1).T
        high[:share] = part(2)
        high[share:] = part(3)[: high_rows - share]
        for k in range(3):
            qkv[k] = part(4 + k)
        proj[...] = part(7).T
        up[...] = part(8, wide)
        down[...] = part(9, wide).T

    local = pl.BlockSpec(memory_space=pltpu.VMEM)
    shapes = [
        (share, width), (high_rows, width), (width, share), (3, share, width), (width, share), (share, wide), (wide, share),
    ]
    return pl.pallas_call(
        kernel,
        out_shape=[jax.ShapeDtypeStruct(s, F32) for s in shapes],
        in_specs=[local],
        out_specs=[local] * 7,
        compiler_params=pltpu.CompilerParams(vmem_limit_bytes=32 * MIB),
    )(own)


def map_outputs(g_up, g_down, others):
    count = len(others)

    def kernel(up, down, *rest):
        sources, o_up, o_down = rest[:count], rest[count], rest[count + 1]
        targets, held, sems = rest[count + 2 : 2 * count + 2], rest[2 * count + 2 : -1], rest[-1]
        loads = [pltpu.make_async_copy(a, b, sems.at[0, i]) for i, (a, b) in enumerate(zip(sources, held))]
        saves = [pltpu.make_async_copy(a, b, sems.at[1, i]) for i, (a, b) in enumerate(zip(held, targets))]
        for load in loads:
            load.start()
        o_up[...] = up[...].astype(F32)
        o_down[...] = down[...].astype(F32)
        for load, save in zip(loads, saves):
            load.wait()
            save.start()
        for save in saves:
            save.wait()

    whole = pl.BlockSpec(memory_space=pl.ANY)
    local = pl.BlockSpec(memory_space=pltpu.VMEM)
    return pl.pallas_call(
        kernel,
        out_shape=[jax.ShapeDtypeStruct(x.shape, F32) for x in (g_up, g_down, *others)],
        in_specs=[local] * 2 + [whole] * count,
        out_specs=[local] * 2 + [whole] * count,
        scratch_shapes=[pltpu.VMEM(o.shape, o.dtype) for o in others] + [pltpu.SemaphoreType.DMA((2, count))],
        compiler_params=pltpu.CompilerParams(vmem_limit_bytes=60 * MIB),
        cost_estimate=pl.CostEstimate(flops=10**9, bytes_accessed=24 * 10**6, transcendentals=0),
    )(g_up, g_down, *others)


def pack_weights(ad_gate, ad_out, ad_high, w_qkv, w_proj, w_up, w_down, devices):
    dim, width = ad_gate.shape
    share, high_rows, wide = dim // devices, ad_high.shape[0] // devices, w_up.shape[1]
    rest = high_rows - share

    def kernel(gate, out, high, qkv, proj, up, down, packed, side, side_wide, sems):
        me = lax.axis_index("dp")
        mine = pl.ds(pl.multiple_of(me * share, share), share)
        lanes = mine

        def at(i, size=width):
            return packed.at[:, pl.ds(i * width, size)]

        straight = [(gate.at[mine], at(0)), (up.at[mine], at(8, wide))]
        straight += [(qkv.at[k, mine], at(4 + k)) for k in range(3)]
        straight.append((high.at[pl.ds(pl.multiple_of(me * high_rows, rest), share)], at(2)))
        straight.append((high.at[pl.ds(pl.multiple_of(me * high_rows + share, rest), rest)], at(3).at[pl.ds(0, rest)]))
        straight += [(out.at[:, lanes], side.at[0]), (proj.at[:, lanes], side.at[1]), (down.at[:, lanes], side_wide)]
        copies = [pltpu.make_async_copy(a, b, sems.at[i]) for i, (a, b) in enumerate(straight)]
        for copy in copies:
            copy.start()
        packed[rest:, 3 * width : 4 * width] = jnp.zeros((share - rest, width), BF)
        for copy in copies:
            copy.wait()
        packed[:, width : 2 * width] = side[0].T
        packed[:, 7 * width : 8 * width] = side[1].T
        packed[:, 8 * width + wide :] = side_wide[...].T

    whole = pl.BlockSpec(memory_space=pl.ANY)
    return pl.pallas_call(
        kernel,
        out_shape=jax.ShapeDtypeStruct((share, 8 * width + 2 * wide), BF),
        in_specs=[whole] * 7,
        out_specs=pl.BlockSpec(memory_space=pltpu.VMEM),
        scratch_shapes=[
            pltpu.VMEM((2, width, share), BF), pltpu.VMEM((wide, share), BF), pltpu.SemaphoreType.DMA((10,)),
        ],
        compiler_params=pltpu.CompilerParams(vmem_limit_bytes=60 * MIB),
    )(ad_gate, ad_out, ad_high, w_qkv, w_proj, w_up, w_down)


def rows_first(x):
    return with_layout_constraint(x, Layout(major_to_minor=tuple(range(x.ndim))))


def own_part(w, axis):
    length = w.shape[axis] // lax.axis_size("dp")
    return lax.dynamic_slice_in_dim(w, lax.axis_index("dp") * length, length, axis)


def fold(w, rows):
    return w[:rows], jnp.pad(w[rows:], ((0, 2 * rows - w.shape[0]), (0, 0)))


def core_first(x, devices):
    shape = x.shape
    return x.reshape(shape[:-1] + (devices // 2, 2, -1)).swapaxes(-3, -2).reshape(shape)


def core_last(x, devices):
    shape = x.shape
    return x.reshape(shape[:-1] + (2, devices // 2, -1)).swapaxes(-3, -2).reshape(shape)


def layer_norm(values, gain):
    centre = jnp.mean(values, -1, keepdims=True)
    centred = values - centre
    variance = jnp.mean(centred * centred, -1, keepdims=True)
    return centred * lax.rsqrt(variance + 1e-06) * gain


def per_device(
    hr_in,
    low_in,
    valid,
    conv_w,
    hr_gain,
    cn_up,
    cn_down,
    ad_gate,
    ad_high,
    ad_out,
    ln1_gain,
    w_qkv,
    w_proj,
    ln2_gain,
    w_up,
    w_down,
    cot_low,
    cot_hr,
):
    _, row_count, col_count, chan_count = hr_in.shape
    devices, shards = lax.axis_size("dp"), lax.axis_size("mp")
    dims = low_in.shape[2]
    share = dims // devices
    qkv = own_part(w_qkv, 1)
    low_weights = (ad_gate, ad_out, ad_high, w_qkv, w_proj, w_up, w_down)
    pieces = [
        own_part(ad_gate, 0), own_part(ad_out, 1).T, *fold(own_part(ad_high, 0), share),
        qkv[0], qkv[1], qkv[2], own_part(w_proj, 1).T, own_part(w_up, 0), own_part(w_down, 1).T,
    ]
    if share % LANES:
        packed = rows_first(jnp.concatenate(pieces, axis=1))
    else:
        packed = pack_weights(*low_weights, devices)
    packed = rows_first(lax.all_gather(packed, "mp", axis=0, tiled=True))
    plane_mask = valid[0].astype(F32)
    cell_mask = plane_mask[..., None]
    masked = hr_in[0] * valid[0].astype(BF)[..., None]
    half_rows, half_cols = (row_count // 2, col_count // 2)
    counts = plane_mask.reshape(half_rows, 2, half_cols, 2).sum(axis=(1, 3))
    shares = 1.0 / jnp.maximum(counts, 1.0)
    size = conv_w.shape[0]
    taps = conv_w.astype(F32).reshape(size * size, 1, chan_count)
    conv_out, bordered = conv_forward(masked, taps, size, shards)
    hr_gainf = hr_gain.astype(F32)
    normed = layer_norm(conv_out * cell_mask, hr_gainf).astype(BF)
    normed, packed = lax.optimization_barrier((normed, packed))
    packed = rows_first(lax.all_gather(packed, "dp", axis=0, tiled=True))
    hr_out, pooled, normed_all, hidden_act, hidden_slope, up_t, down_t = big_forward(
        normed.reshape(row_count * col_count, chan_count), cn_up, cn_down, masked, cell_mask, shares, shards
    )
    hr_out = hr_out.reshape(hr_in.shape)
    tokens = half_rows * half_cols
    low_ins, gains = [low_in[0], pooled, cot_low[0]], [ln1_gain.astype(F32)[None], ln2_gain.astype(F32)[None]]
    if share % LANES:
        by_share = pooled.reshape(tokens, devices, -1)
        pool_a = by_share[:, :, :share].reshape(tokens, dims)
        pool_b = by_share[:, :, share:]
        pool_b = jnp.pad(pool_b, ((0, 0), (0, 0), (0, share - pool_b.shape[2]))).reshape(tokens, dims)
        low_ins = [core_first(low_in[0], devices), None, core_first(cot_low[0], devices)]
        low_ins[1] = jnp.concatenate([core_first(pool_a, devices), core_first(pool_b, devices)], axis=1)
        gains = [core_first(g, devices) for g in gains]
    low_out, d_low_in, d_pooled, g_ln1, g_ln2, low_grads = low_stage(*low_ins, *gains, packed, shards, devices, 2)
    if share % LANES:
        low_out, d_low_in = core_last(low_out, devices), core_last(d_low_in, devices)
        g_ln1, g_ln2 = core_last(g_ln1, devices), core_last(g_ln2, devices)
        d_pooled = jnp.concatenate(
            [
                core_last(d_pooled[:, :dims], devices).reshape(tokens, devices, share),
                core_last(d_pooled[:, dims:], devices).reshape(tokens, devices, share)[:, :, : by_share.shape[2] - share],
            ],
            axis=2,
        ).reshape(tokens, chan_count)
    low_out, d_low_in, g_ln1, g_ln2 = low_out[None], d_low_in[None], g_ln1[0], g_ln2[0]
    d_normed, d_map, cn_grads, low_sums = big_backward(
        cot_hr[0], d_pooled, shares, cell_mask, normed_all, hidden_act, hidden_slope,
        up_t, down_t, low_grads, shards, devices,
    )
    low_sums = rows_first(low_sums.reshape(shards, share, -1))
    low_sums = rows_first(lax.psum_scatter(low_sums, "mp", scatter_dimension=0))
    low_gains = jnp.pad(jnp.stack([g_ln1, g_ln2]), ((0, 0), (0, chan_count - dims)))
    d_hr_in, small_sums, (g_cn_up, g_cn_down) = conv_backward(
        d_normed, conv_out, hr_gainf[None], cell_mask, bordered, d_map, taps, low_gains, size, cn_grads, devices, shards
    )
    d_hr_in = d_hr_in[None]
    g_conv = small_sums[: size * size].reshape(conv_w.shape)
    g_hr_gain, g_ln1, g_ln2 = small_sums[size * size], small_sums[-2, :dims], small_sums[-1, :dims]
    g_cn_up, g_cn_down, low_out, hr_out, d_low_in, d_hr_in = map_outputs(
        g_cn_up, g_cn_down, (low_out, hr_out, d_low_in, d_hr_in)
    )
    g_ad_gate, g_ad_high, g_ad_out, g_qkv, g_proj, g_up, g_down = low_outputs(
        low_sums.reshape(share, -1), [p.shape[1] for p in pieces], ad_high.shape[0] // devices
    )
    g_cn_down = g_cn_down.T
    return (
        low_out,
        hr_out,
        d_low_in,
        d_hr_in,
        g_conv,
        g_hr_gain,
        g_cn_up,
        g_cn_down,
        g_ad_gate,
        g_ad_high,
        g_ad_out,
        g_ln1,
        g_qkv,
        g_proj,
        g_ln2,
        g_up,
        g_down,
    )


def solution(mesh):
    return jax.shard_map(
        per_device,
        mesh=mesh,
        in_specs=(
            P("dp", "mp", None, None),
            P("dp", "mp", None),
            P("dp", "mp", None),
            P(),
            P(),
            P(None, "mp"),
            P("mp", None),
            P(None, "mp"),
            P(None, "mp"),
            P("mp", None),
            P(),
            P(None, None, "mp"),
            P("mp", None),
            P(),
            P(None, "mp"),
            P("mp", None),
            P("dp", "mp", None),
            P("dp", "mp", None, None),
        ),
        out_specs=(
            P("dp", "mp", None),
            P("dp", "mp", None, None),
            P("dp", "mp", None),
            P("dp", "mp", None, None),
            P(),
            P(),
            P("dp", "mp"),
            P("mp", "dp"),
            P("dp", "mp"),
            P("dp", "mp"),
            P("mp", "dp"),
            P(),
            P(None, "dp", "mp"),
            P("mp", "dp"),
            P(),
            P("dp", "mp"),
            P("mp", "dp"),
        ),
        check_vma=False,
    )
```
